32 devices in a mesh: dp: 8 (over z, y), tensor: 4 (over x, core).
Axes of the slice: x: 2, y: 2, z: 4, core: 2. Of those that a mesh axis runs over, the one named last changes fastest.
Arguments:
- tokens: bfloat16 [16384, 768], P('dp'), may hold values from -6 to 6
- lengths: int32 [16], P('dp'), may hold values from 256 to 1024, as said below
- span_starts: int32 [16, 64], P('dp'), may hold values from 0 to 1014, as said below
- query_weight: bfloat16 [768, 768], P(None, 'tensor'), may hold values from -0.3125 to 0.3125
- key_weight: bfloat16 [768, 768], P(None, 'tensor'), may hold values from -0.3125 to 0.3125
- value_weight: bfloat16 [768, 768], P(None, 'tensor'), may hold values from -0.21875 to 0.21875
- merge_weight: bfloat16 [768, 768], P('tensor'), may hold values from -0.75 to 0.75
- up_weight: bfloat16 [768, 3072], P(None, 'tensor'), may hold values from -0.21875 to 0.21875
- down_weight: bfloat16 [3072, 768], P('tensor'), may hold values from -0.15625 to 0.15625
- inner_gain: float32 [768], replicated, may hold values from 0.1 to 1.9
- inner_bias: float32 [768], replicated, may hold values from -3 to 3
- outer_gain: float32 [768], replicated, may hold values from 0.1 to 1.9
- outer_bias: float32 [768], replicated, may hold values from -3 to 3
- out_grad: bfloat16 [16384, 768], P('dp'), may hold values from -18 to 18
Outputs:
- layer_output: bfloat16 [16384, 768], P('dp')
- input_grad: bfloat16 [16384, 768], P('dp')
- query_grad: float32 [768, 768], P(None, 'tensor')
- key_grad: float32 [768, 768], P(None, 'tensor')
- value_grad: float32 [768, 768], P(None, 'tensor')
- merge_grad: float32 [768, 768], P('tensor')
- up_grad: float32 [768, 3072], P(None, 'tensor')
- down_grad: float32 [3072, 768], P('tensor')
- inner_gain_grad: float32 [768], replicated
- inner_bias_grad: float32 [768], replicated
- outer_gain_grad: float32 [768], replicated
- outer_bias_grad: float32 [768], replicated
The draws below stay inside these ranges and needn't reach their ends.
Inputs may be any that keep to these rules, and one draw needn't show every extreme that they name: `lengths`: live frames of each utterance; in every draw some utterance has all 1024 and some has 256. `span_starts`: every span of 10 frames ends within its utterance's live frames; spans may intersect.
All inputs are finite; a program needn't handle non-finite values.
Results may differ from the reference program's by a relative error of at most 0.024.
The reference program's roundings to bfloat16 on the way count: a program that leaves them out, or rounds other values in their place, can miss the bound.
Values may be sent and summed in bfloat16 or wider, within the bound.
No kernel may reach another device: no remote copies, remote signals or barrier semaphores. Data moves between devices by JAX's collectives and lax.ppermute only.
A program may use at most 192 MiB of HBM per device.

```python
import jax
import jax.numpy as jnp
from jax import lax

D = 768
HEADS = 12
HEAD_DIM = 64
FF = 3072
LEN = 1024
SPAN = 10
SPANS = 64
UTTERANCES = 16
TOKENS = 16384
N_TENSOR = 4


def shared_lengths(key):
    lower = LEN // 4
    drawn = jax.random.randint(key, (UTTERANCES,), lower, LEN + 1, dtype=jnp.int32)
    order = jax.random.permutation(jax.random.fold_in(key, 7), UTTERANCES)
    drawn = drawn.at[order[0]].set(LEN)
    drawn = drawn.at[order[1]].set(lower)
    return (drawn, order[0])


def draw_lengths(key, part):
    drawn, longest = shared_lengths(key)
    return drawn


def draw_span_starts(key, part):
    drawn, longest = shared_lengths(key)
    key = jax.random.fold_in(key, 2)
    starts = jax.random.randint(key, (UTTERANCES, SPANS), 0, (drawn - SPAN + 1)[:, None], dtype=jnp.int32)
    starts = starts.at[longest, 0].set(LEN - SPAN)
    starts = starts.at[longest, 1].set(0)
    return starts


def draw_out_grad(key, part):
    key = jax.random.fold_in(key, 3)
    place = jnp.arange(TOKENS, dtype=jnp.float32) / (TOKENS - 1)
    base = jax.random.truncated_normal(key, -6.0, 6.0, (TOKENS, D), jnp.float32)
    growth = 3.0 ** place
    return (base * growth[:, None]).astype(jnp.bfloat16)


def shard_levels(rng, extent, cuts, least, largest):
    factor_of = 1.0
    for position, blocks in cuts:
        steps = jax.random.uniform(jax.random.fold_in(jax.random.fold_in(rng, 6), position), (blocks,), jnp.float32, least / len(cuts), largest / len(cuts))
        factor_of = factor_of * jnp.repeat(jnp.exp(steps), extent[position] // blocks).reshape((-1,) + (1,) * (len(extent) - 1 - position))
    return factor_of


def gaussian(own_key, extent, width, bound, shards=(), held_as=jnp.bfloat16):
    array = width * jax.random.normal(own_key, extent, jnp.float32)
    if shards:
        array = array * shard_levels(own_key, extent, shards, -0.22, 0.18)
    return jnp.clip(array, -bound, bound).astype(held_as)


def setup_inputs(seed: int = 0) -> dict:
    streams_of = jax.random.split(jax.random.key(seed), 15)
    return {
        "tokens": gaussian(streams_of[0], (TOKENS, D), 1.0, 6.0, ((0, 8),)),
        "lengths": draw_lengths(jax.random.fold_in(streams_of[14], 71), 0),
        "span_starts": draw_span_starts(jax.random.fold_in(streams_of[14], 71), 0),
        "query_weight": gaussian(streams_of[3], (D, D), (D // 2) ** -0.5, 0.3125, ((1, 4),)),
        "key_weight": gaussian(streams_of[4], (D, D), (D // 2) ** -0.5, 0.3125, ((1, 4),)),
        "value_weight": gaussian(streams_of[5], (D, D), D ** -0.5, 0.21875, ((1, 4),)),
        "merge_weight": gaussian(streams_of[6], (D, D), (D // 12) ** -0.5, 0.75, ((0, 4),)),
        "up_weight": gaussian(streams_of[7], (D, FF), D ** -0.5, 0.21875, ((1, 4),)),
        "down_weight": gaussian(streams_of[8], (FF, D), (FF // 2) ** -0.5, 0.15625, ((0, 4),)),
        "inner_gain": jnp.clip(1.0 + 0.18 * jax.random.normal(streams_of[9], (D,), jnp.float32), 0.1, 1.9),
        "inner_bias": gaussian(streams_of[10], (D,), 0.5, 3.0, (), jnp.float32),
        "outer_gain": jnp.clip(1.0 + 0.18 * jax.random.normal(streams_of[11], (D,), jnp.float32), 0.1, 1.9),
        "outer_bias": gaussian(streams_of[12], (D,), 0.5, 3.0, (), jnp.float32),
        "out_grad": draw_out_grad(jax.random.fold_in(streams_of[14], 71), 0),
    }


@jax.custom_vjp
def low(v):
    return lax.optimization_barrier(v.astype(jnp.bfloat16)).astype(jnp.float32)

@jax.custom_vjp
def low_back(v):
    return v

def low_keep(v):
    return (low(v), None)

def low_pass(kept, grad):
    return (grad,)

def back_keep(v):
    return (v, None)

def back_low(kept, grad):
    return (low(grad),)
low.defvjp(low_keep, low_pass)
low_back.defvjp(back_keep, back_low)
highest = lax.Precision.HIGHEST

def layer_norm(values, gain, bias):
    average = lax.optimization_barrier(jnp.mean(values, axis=-1, keepdims=True))
    centred = values - average
    spread = lax.optimization_barrier(jnp.mean(centred * centred, axis=-1, keepdims=True))
    return centred * lax.rsqrt(spread + 1e-05) * gain + bias

def attend_block(query_block, keys, values, key_mask):
    scores = jnp.einsum('bhd,khd->hbk', query_block, keys, precision=highest) * HEAD_DIM ** (-0.5)
    scores = low_back(scores)
    scores = jnp.where(key_mask[None, None, :], scores, -1e+30)
    probs = low(jax.nn.softmax(scores, axis=-1))
    return jnp.einsum('hbk,khd->bhd', probs, values, precision=highest)

def attend(queries, keys, values, key_mask):
    block = min(512, LEN)

    def run_block(query_block):
        return attend_block(query_block, keys, values, key_mask)
    blocks = queries.reshape(LEN // block, block, HEADS, HEAD_DIM)
    return lax.map(jax.checkpoint(run_block), blocks).reshape(LEN, HEADS, HEAD_DIM)

def split_columns(weight):
    return weight.reshape(weight.shape[0], N_TENSOR, weight.shape[1] // N_TENSOR).transpose(1, 0, 2)

def split_rows(weight):
    return weight.reshape(N_TENSOR, weight.shape[0] // N_TENSOR, weight.shape[1])

def tiled(values):
    return low_back(jnp.broadcast_to(values[:, None, :], (values.shape[0], N_TENSOR, values.shape[1])))

def forward(frames, key_mask, query_weight, key_weight, value_weight, merge_weight, up_weight, down_weight, inner_gain, inner_bias, outer_gain, outer_bias):
    entry = tiled(frames)

    def project(weight):
        result = jnp.einsum('rtd,tdc->rtc', entry, split_columns(weight), precision=highest)
        return low_back(low(result)).reshape(LEN, HEADS, HEAD_DIM)
    attended = attend(project(query_weight), project(key_weight), project(value_weight), key_mask)
    attended = low_back(low(attended.reshape(LEN, N_TENSOR, D // N_TENSOR)))
    merge_parts = low(jnp.einsum('rtc,tce->rte', attended, split_rows(merge_weight), precision=highest))
    attn_branch = low_back(lax.optimization_barrier(jnp.sum(merge_parts, axis=1)))
    normed = layer_norm(frames + attn_branch, inner_gain, inner_bias)
    hidden_in = tiled(low(normed))
    pre_act = low_back(jnp.einsum('rtd,tdf->rtf', hidden_in, split_columns(up_weight), precision=highest))
    activated = low(jax.nn.gelu(pre_act, approximate=False))
    down_parts = low(jnp.einsum('rtf,tfe->rte', activated, split_rows(down_weight), precision=highest))
    ffn_branch = low_back(lax.optimization_barrier(jnp.sum(down_parts, axis=1)))
    return layer_norm(normed + ffn_branch, outer_gain, outer_bias)

def reference(tokens, lengths, span_starts, query_weight, key_weight, value_weight, merge_weight, up_weight, down_weight, inner_gain, inner_bias, outer_gain, outer_bias, out_grad):
    params = tuple((item.astype(jnp.float32) for item in (query_weight, key_weight, value_weight, merge_weight, up_weight, down_weight, inner_gain, inner_bias, outer_gain, outer_bias)))
    positions = jnp.arange(LEN)

    def one_utterance(totals, item):
        frames, length, starts, grad_rows = item
        key_mask = positions < length
        inside = (positions[None, :] >= starts[:, None]) & (positions[None, :] < starts[:, None] + SPAN)
        span_weight = jnp.any(inside, axis=0).astype(jnp.float32)

        def run_layer(frames_in, *weights):
            return forward(frames_in, key_mask, *weights)
        final, pullback = jax.vjp(run_layer, frames.astype(jnp.float32), *params)
        grads = pullback(grad_rows.astype(jnp.float32) * span_weight[:, None])
        totals = tuple((left + right for left, right in zip(totals, grads[1:])))
        return (totals, (final.astype(jnp.bfloat16), grads[0].astype(jnp.bfloat16)))
    start_totals = tuple((jnp.zeros_like(item) for item in params))
    totals, (outputs, entry_grads) = lax.scan(one_utterance, start_totals, (tokens.reshape(UTTERANCES, LEN, D), lengths, span_starts, out_grad.reshape(UTTERANCES, LEN, D)))
    return (outputs.reshape(TOKENS, D), entry_grads.reshape(TOKENS, D), totals[0], totals[1], totals[2], totals[3], totals[4], totals[5], totals[6], totals[7], totals[8], totals[9])
```

```python
import functools

import jax
import jax.numpy as jnp
from jax import lax
from jax.experimental import pallas as pl
from jax.experimental.pallas import tpu as pltpu
from jax.sharding import PartitionSpec as P

HEAD_DIM = 64
SPAN = 10
EPS = 1e-05
LOG2E = 1.4426950408889634
KB = 256
QB = 512
BF = jnp.bfloat16
F32 = jnp.float32
MIB = 1 << 20


def nn(a, b):
    return lax.dot_general(a, b, (((1,), (0,)), ((), ())), preferred_element_type=F32)


def nt(a, b):
    return lax.dot_general(a, b, (((1,), (1,)), ((), ())), preferred_element_type=F32)


def tn(a, b):
    return lax.dot_general(a, b, (((0,), (0,)), ((), ())), preferred_element_type=F32)


def params(limit):
    return pltpu.CompilerParams(vmem_limit_bytes=limit * MIB)


def lane_parts(block):
    left = block[:, :128]
    lane = lax.broadcasted_iota(jnp.int32, left.shape, 1)
    zero = jnp.zeros_like(left)
    return (
        jnp.where(lane < HEAD_DIM, left, zero),
        jnp.where(lane >= HEAD_DIM, left, zero),
        block[:, 128:],
    )


TILE = (0, 0, 1)


def forward_kernel(len_ref, q_ref, k_ref, v_ref, o_ref, o32_ref, lse_ref, s_ref):
    length = len_ref[0]
    blocks = lax.div(length + KB - 1, KB)
    parts = lane_parts(q_ref[...] * jnp.asarray(0.125, BF))
    width = q_ref.shape[0]

    def first(kb, highest):
        start = pl.multiple_of(kb * KB, KB)
        rows = pl.ds(start, KB)
        live = start + lax.broadcasted_iota(jnp.int32, (KB, width), 0) < length
        out = []
        for h in range(3):
            tile = pl.ds(128 * TILE[h], 128)
            s = nt(k_ref[rows, tile], parts[h])
            s = jnp.where(live, s, -1e30)
            s_ref[h, rows, :] = s
            out.append(jnp.maximum(highest[h], jnp.max(s, axis=0, keepdims=True)))
        return tuple(out)

    floor = jnp.full((1, width), -1e30, F32)
    highest = lax.fori_loop(0, blocks, first, (floor,) * 3)

    def second(kb, carry):
        rows = pl.ds(pl.multiple_of(kb * KB, KB), KB)
        out = []
        for h in range(3):
            total, result = carry[h]
            p = jnp.exp2((s_ref[h, rows, :] - highest[h]) * LOG2E)
            total = total + jnp.sum(p, axis=0, keepdims=True)
            v = v_ref[rows, pl.ds(128 * TILE[h], 128)]
            result = result + tn(v, p.astype(BF))
            out.append((total, result))
        return tuple(out)

    init = ((jnp.zeros((1, width), F32), jnp.zeros((128, width), F32)),) * 3
    done = lax.fori_loop(0, blocks, second, init)
    for h in range(3):
        total, result = done[h]
        lo = HEAD_DIM * (h % 2)
        o = result[lo : lo + HEAD_DIM] / total
        o_ref[pl.ds(h * HEAD_DIM, HEAD_DIM), :] = o.astype(BF)
        o32_ref[pl.ds(h * HEAD_DIM, HEAD_DIM), :] = o
        lse_ref[pl.ds(h, 1), :] = highest[h] * LOG2E + jnp.log2(total)


def attend_forward(length, qkv, u, frames):
    steps = frames // QB
    return pl.pallas_call(
        forward_kernel,
        grid=(steps,),
        in_specs=[
            pl.BlockSpec(memory_space=pltpu.SMEM),
            pl.BlockSpec((QB, 256), lambda i: (u * steps + i, 0)),
            pl.BlockSpec((frames, 256), lambda i: (u, 1)),
            pl.BlockSpec((frames, 256), lambda i: (u, 2)),
        ],
        out_specs=[
            pl.BlockSpec((192, QB), lambda i: (0, i)),
            pl.BlockSpec((192, QB), lambda i: (0, i)),
            pl.BlockSpec((8, QB), lambda i: (0, i)),
        ],
        out_shape=[
            jax.ShapeDtypeStruct((192, frames), BF),
            jax.ShapeDtypeStruct((192, frames), F32),
            jax.ShapeDtypeStruct((8, frames), F32),
        ],
        scratch_shapes=[pltpu.VMEM((3, frames, QB), F32)],
        compiler_params=params(32),
        cost_estimate=pl.CostEstimate(
            flops=3 * 4 * frames * frames * 256, bytes_accessed=4 * MIB, transcendentals=0
        ),
        name="attend_forward",
    )(length, qkv, qkv, qkv)


def backward_kernel(
    len_ref, q_ref, k_ref, v_ref, do_ref, o32_ref, lse_ref, dq_ref, dk_ref, dv_ref, kt_ref, dk_acc, dv_acc
):
    length = len_ref[0]
    blocks = lax.div(length + KB - 1, KB)
    step = pl.program_id(0)

    @pl.when(step == 0)
    def _():
        dk_acc[...] = jnp.zeros_like(dk_acc)
        dv_acc[...] = jnp.zeros_like(dv_acc)
        kt_ref[...] = jnp.transpose(k_ref[...])

    parts = lane_parts(q_ref[...] * jnp.asarray(0.125, BF))
    width = q_ref.shape[0]
    empty = jnp.zeros((HEAD_DIM, width), BF)
    head = [do_ref[pl.ds(h * HEAD_DIM, HEAD_DIM), :] for h in range(3)]
    grads = (
        jnp.concatenate([head[0], empty], axis=0),
        jnp.concatenate([empty, head[1]], axis=0),
        jnp.concatenate([head[2], empty], axis=0),
    )
    delta = [
        jnp.sum(
            head[h].astype(F32) * o32_ref[pl.ds(h * HEAD_DIM, HEAD_DIM), :], axis=0, keepdims=True
        )
        for h in range(3)
    ]
    lse = [lse_ref[pl.ds(h, 1), :] for h in range(3)]

    def body(kb, carry):
        start = pl.multiple_of(kb * KB, KB)
        rows = pl.ds(start, KB)
        live = start + lax.broadcasted_iota(jnp.int32, (KB, width), 0) < length
        out = []
        for h in range(3):
            tile = pl.ds(128 * TILE[h], 128)
            s = nt(k_ref[rows, tile], parts[h])
            s = jnp.where(live, s, -1e30)
            p = jnp.exp2(s * LOG2E - lse[h])
            dp = nn(v_ref[rows, tile], grads[h])
            ds = (p * (dp - delta[h])).astype(BF)
            dv_acc[rows, tile] += nt(p.astype(BF), grads[h])
            dk_acc[rows, tile] += nn(ds, parts[h])
            kt = kt_ref[pl.ds(h * HEAD_DIM, HEAD_DIM), rows]
            out.append(carry[h] + nn(kt, ds))
        return tuple(out)

    zero = jnp.zeros((HEAD_DIM, width), F32)
    done = lax.fori_loop(0, blocks, body, (zero,) * 3)
    full = jnp.concatenate(done + (zero,), axis=0) * 0.125
    dq_ref[...] = jnp.transpose(full).astype(BF)

    @pl.when(step == pl.num_programs(0) - 1)
    def _():
        dk_ref[...] = dk_acc[...].astype(BF)
        dv_ref[...] = dv_acc[...].astype(BF)


def attend_backward(length, qkv, grad, o32, lse, u, frames):
    steps = frames // QB
    return pl.pallas_call(
        backward_kernel,
        grid=(steps,),
        in_specs=[
            pl.BlockSpec(memory_space=pltpu.SMEM),
            pl.BlockSpec((QB, 256), lambda i: (u * steps + i, 0)),
            pl.BlockSpec((frames, 256), lambda i: (u, 1)),
            pl.BlockSpec((frames, 256), lambda i: (u, 2)),
            pl.BlockSpec((192, QB), lambda i: (0, i)),
            pl.BlockSpec((192, QB), lambda i: (0, i)),
            pl.BlockSpec((8, QB), lambda i: (0, i)),
        ],
        out_specs=[
            pl.BlockSpec((QB, 256), lambda i: (i, 0)),
            pl.BlockSpec((frames, 256), lambda i: (0, 0)),
            pl.BlockSpec((frames, 256), lambda i: (0, 0)),
        ],
        out_shape=[jax.ShapeDtypeStruct((frames, 256), BF)] * 3,
        scratch_shapes=[
            pltpu.VMEM((256, frames), BF),
            pltpu.VMEM((frames, 256), F32),
            pltpu.VMEM((frames, 256), F32),
        ],
        compiler_params=params(32),
        cost_estimate=pl.CostEstimate(
            flops=3 * 10 * frames * frames * 256, bytes_accessed=5 * MIB, transcendentals=0
        ),
        name="attend_backward",
    )(length, qkv, qkv, qkv, grad, o32, lse)


def normalise(values):
    average = jnp.mean(values, axis=-1, keepdims=True)
    centred = values - average
    spread = jnp.mean(centred * centred, axis=-1, keepdims=True)
    rstd = lax.rsqrt(spread + EPS)
    return centred * rstd, rstd


def merge_kernel(tok_ref, a0, a1, a2, a3, w0, w1, w2, w3, gain_ref, bias_ref, xhat_ref, rstd_ref, low_ref):
    branch = jnp.zeros(tok_ref.shape, F32)
    for a, w in ((a0, w0), (a1, w1), (a2, w2), (a3, w3)):
        branch = branch + tn(a[...], w[...]).astype(BF).astype(F32)
    xhat, rstd = normalise(tok_ref[...].astype(F32) + branch)
    xhat_ref[...] = xhat
    rstd_ref[...] = jnp.broadcast_to(rstd, rstd_ref.shape)
    low_ref[...] = (xhat * gain_ref[...] + bias_ref[...]).astype(BF)


def merge_forward(tok, att, weights, gain, bias):
    rows, d = tok.shape
    return pl.pallas_call(
        merge_kernel,
        out_shape=[
            jax.ShapeDtypeStruct((rows, d), F32),
            jax.ShapeDtypeStruct((rows, 128), F32),
            jax.ShapeDtypeStruct((rows, d), BF),
        ],
        compiler_params=params(32),
        cost_estimate=pl.CostEstimate(flops=2 * rows * d * d, bytes_accessed=7 * MIB, transcendentals=0),
        name="merge_forward",
    )(tok, *att, *weights, gain, bias)


def gelu_pair(v):
    e = jnp.exp2(v * v * (-0.5 * LOG2E))
    t = 1.0 / (1.0 + (0.3275911 * 0.7071067811865476) * jnp.abs(v))
    poly = t * (0.5 * 0.254829592 + t * (0.5 * -0.284496736 + t * (0.5 * 1.421413741 + t * (0.5 * -1.453152027 + t * (0.5 * 1.061405429)))))
    tail = poly * e
    phi_cap = jnp.where(v >= 0, 1.0 - tail, tail)
    return v * phi_cap, phi_cap + v * (e * 0.3989422804014327)


def up_down_kernel(x_ref, up_ref, down_ref, act_ref, slope_ref, part_ref, acc):
    step = pl.program_id(0)
    act, slope = gelu_pair(nn(x_ref[...], up_ref[...]))
    low = act.astype(BF)
    act_ref[...] = low
    slope_ref[...] = slope
    product = nn(low, down_ref[...])

    @pl.when(step == 0)
    def _():
        acc[...] = product

    @pl.when(step > 0)
    def _():
        acc[...] += product

    @pl.when(step == pl.num_programs(0) - 1)
    def _():
        part_ref[...] = acc[...].astype(BF)


HB = 256


def up_down(x, up, down):
    rows, d = x.shape
    hidden = up.shape[1]
    return pl.pallas_call(
        up_down_kernel,
        grid=(hidden // HB,),
        in_specs=[
            pl.BlockSpec((rows, d), lambda i: (0, 0)),
            pl.BlockSpec((d, HB), lambda i: (0, i)),
            pl.BlockSpec((HB, d), lambda i: (i, 0)),
        ],
        out_specs=[
            pl.BlockSpec((rows, HB), lambda i: (0, i)),
            pl.BlockSpec((rows, HB), lambda i: (0, i)),
            pl.BlockSpec((rows, d), lambda i: (0, 0)),
        ],
        out_shape=[
            jax.ShapeDtypeStruct((rows, hidden), BF),
            jax.ShapeDtypeStruct((rows, hidden), F32),
            jax.ShapeDtypeStruct((rows, d), BF),
        ],
        scratch_shapes=[pltpu.VMEM((rows, d), F32)],
        compiler_params=params(32),
        cost_estimate=pl.CostEstimate(flops=8 * rows * d * hidden, bytes_accessed=6 * MIB, transcendentals=0),
        name="up_down",
    )(x, up, down)


def outer_kernel(
    xhat_ref, p0, p1, p2, p3, grad_ref, weight_ref, ig_ref, ib_ref, og_ref, ob_ref, out_ref, sum_grad_ref, low_ref, small_ref
):
    branch = p0[...].astype(F32) + p1[...].astype(F32) + p2[...].astype(F32) + p3[...].astype(F32)
    normed = xhat_ref[...] * ig_ref[...] + ib_ref[...]
    xhat, rstd = normalise(normed + branch)
    out_ref[...] = (xhat * og_ref[...] + ob_ref[...]).astype(BF)
    cot = grad_ref[...].astype(F32) * weight_ref[...]
    small_ref[0:1, :] = jnp.sum(cot * xhat, axis=0, keepdims=True)
    small_ref[1:2, :] = jnp.sum(cot, axis=0, keepdims=True)
    gy = cot * og_ref[...]
    mean_gy = jnp.mean(gy, axis=-1, keepdims=True)
    mean_gx = jnp.mean(gy * xhat, axis=-1, keepdims=True)
    sum_grad = rstd * (gy - mean_gy - xhat * mean_gx)
    sum_grad_ref[...] = sum_grad
    low_ref[...] = sum_grad.astype(BF)


def outer_norm(xhat, parts, grad, weight, ig, ib, og, ob):
    rows, d = xhat.shape
    return pl.pallas_call(
        outer_kernel,
        out_shape=[
            jax.ShapeDtypeStruct((rows, d), BF),
            jax.ShapeDtypeStruct((rows, d), F32),
            jax.ShapeDtypeStruct((rows, d), BF),
            jax.ShapeDtypeStruct((2, d), F32),
        ],
        compiler_params=params(32),
        cost_estimate=pl.CostEstimate(flops=rows * d * 30, bytes_accessed=8 * MIB, transcendentals=0),
        name="outer_norm",
    )(xhat, *parts, grad, weight, ig, ib, og, ob)


def ffn_back_kernel(x_ref, g_ref, up_ref, down_ref, act_ref, slope_ref, part_ref, dup_ref, ddown_ref, acc):
    step = pl.program_id(0)
    g = g_ref[...]
    low = (nt(g, down_ref[...]) * slope_ref[...]).astype(BF)
    product = nt(low, up_ref[...])
    ddown_ref[...] = tn(act_ref[...], g).astype(BF)
    dup_ref[...] = tn(x_ref[...], low).astype(BF)

    @pl.when(step == 0)
    def _():
        acc[...] = product

    @pl.when(step > 0)
    def _():
        acc[...] += product

    @pl.when(step == pl.num_programs(0) - 1)
    def _():
        part_ref[...] = acc[...].astype(BF)


def ffn_back(x, g, up, down, act, slope):
    rows, d = x.shape
    hidden = up.shape[1]
    return pl.pallas_call(
        ffn_back_kernel,
        grid=(hidden // HB,),
        in_specs=[
            pl.BlockSpec((rows, d), lambda i: (0, 0)),
            pl.BlockSpec((rows, d), lambda i: (0, 0)),
            pl.BlockSpec((d, HB), lambda i: (0, i)),
            pl.BlockSpec((HB, d), lambda i: (i, 0)),
            pl.BlockSpec((rows, HB), lambda i: (0, i)),
            pl.BlockSpec((rows, HB), lambda i: (0, i)),
        ],
        out_specs=[
            pl.BlockSpec((rows, d), lambda i: (0, 0)),
            pl.BlockSpec((d, HB), lambda i: (0, i)),
            pl.BlockSpec((HB, d), lambda i: (i, 0)),
        ],
        out_shape=[
            jax.ShapeDtypeStruct((rows, d), BF),
            jax.ShapeDtypeStruct((d, hidden), BF),
            jax.ShapeDtypeStruct((hidden, d), BF),
        ],
        scratch_shapes=[pltpu.VMEM((rows, d), F32)],
        compiler_params=params(32),
        cost_estimate=pl.CostEstimate(flops=8 * rows * d * hidden, bytes_accessed=8 * MIB, transcendentals=0),
        name="ffn_back",
    )(x, g, up, down, act, slope)


def inner_kernel(
    sum_grad_ref, p0, p1, p2, p3, xhat_ref, rstd_ref, gain_ref, a0, a1, a2, a3, w0, w1, w2, w3,
    out_ref, g0, g1, g2, g3, m0, m1, m2, m3, small_ref,
):
    grad = sum_grad_ref[...] + (
        p0[...].astype(F32) + p1[...].astype(F32) + p2[...].astype(F32) + p3[...].astype(F32)
    )
    xhat = xhat_ref[...]
    small_ref[0:1, :] = jnp.sum(grad * xhat, axis=0, keepdims=True)
    small_ref[1:2, :] = jnp.sum(grad, axis=0, keepdims=True)
    gy = grad * gain_ref[...]
    mean_gy = jnp.mean(gy, axis=-1, keepdims=True)
    mean_gx = jnp.mean(gy * xhat, axis=-1, keepdims=True)
    inner = rstd_ref[:, 0:1] * (gy - mean_gy - xhat * mean_gx)
    out_ref[...] = inner
    low = inner.astype(BF)
    for g, m, a, w in ((g0, m0, a0, w0), (g1, m1, a1, w1), (g2, m2, a2, w2), (g3, m3, a3, w3)):
        g[...] = nt(w[...], low).astype(BF)
        m[...] = nn(a[...], low).astype(BF)


def inner_norm(sum_grad, parts, xhat, rstd, gain, att, weights):
    rows, d = xhat.shape
    return pl.pallas_call(
        inner_kernel,
        out_shape=[jax.ShapeDtypeStruct((rows, d), F32)]
        + [jax.ShapeDtypeStruct((192, rows), BF)] * 4
        + [jax.ShapeDtypeStruct((192, d), BF)] * 4
        + [jax.ShapeDtypeStruct((2, d), F32)],
        compiler_params=params(40),
        cost_estimate=pl.CostEstimate(flops=4 * rows * d * d, bytes_accessed=12 * MIB, transcendentals=0),
        name="inner_norm",
    )(sum_grad, *parts, xhat, rstd, gain, *att, *weights)


def local(groups, tokens, lengths, span_starts, wq, wk, wv, wm, wu, wd, ig, ib, og, ob, out_grad):
    rows, d = tokens.shape
    seqs = lengths.shape[0]
    frames = rows // seqs
    part = frames // 4
    t = lax.axis_index("tensor")
    y = lax.axis_index("dp") % 2

    def swap(value, bit):
        return lax.ppermute(value, "tensor", [(i, i ^ bit) for i in range(4)])

    def swap_dp(value):
        return lax.ppermute(value, "dp", [(i, i ^ 1) for i in range(groups)])

    def gather(own):
        half = own.shape[0] // 2
        mine = lax.dynamic_slice_in_dim(own, y * half, half, 0)
        first = swap(mine, 2)
        second = swap_dp(first)
        across = jnp.concatenate([first, second], axis=0)
        across = jnp.where(y == 0, across, jnp.concatenate([second, first], axis=0))
        return own, swap(own, 1), across, swap(across, 1)

    merge_w = gather(wm)
    up_w = gather(wu)
    down_w = gather(wd)

    pad = jnp.zeros((d, 256 - wq.shape[1]), BF)
    joint = jnp.concatenate([wq, pad, wk, pad, wv, pad], axis=1)
    qkv = nn(tokens, joint).astype(BF)
    each = [lengths[u : u + 1] for u in range(seqs)]
    fwd = [attend_forward(each[u], qkv, u, frames) for u in range(seqs)]

    def share(block, k):
        return lax.dynamic_slice_in_dim(block, (t ^ k) * part, part, 1)

    pieces = []
    for k in range(4):
        got = [share(fwd[u][0], k) for u in range(seqs)]
        if k:
            got = [swap(g, k) for g in got]
        pieces.append(got)
    att = [jnp.concatenate(got, axis=1) for got in pieces]

    def own_rows(array):
        cut = lax.dynamic_slice_in_dim(array.reshape(seqs, frames, -1), t * part, part, 1)
        return cut.reshape(seqs * part, -1)

    tok = own_rows(tokens)
    positions = t * part + jnp.arange(part)
    inside = (positions[None, None, :] >= span_starts[:, :, None]) & (
        positions[None, None, :] < span_starts[:, :, None] + SPAN
    )
    weight = jnp.any(inside, axis=1).astype(F32).reshape(seqs * part, 1)
    ig, ib, og, ob = (v.reshape(1, d) for v in (ig, ib, og, ob))

    xhat, rstd, normed_low = merge_forward(tok, att, merge_w, ig, ib)
    order = (0, 1, 2, 3)
    made = {k: up_down(normed_low, up_w[k], down_w[k]) for k in order}
    out_rows, sum_grad, g_low, outer_small = outer_norm(
        xhat, [made[k][2] for k in range(4)], own_rows(out_grad), weight, ig, ib, og, ob
    )

    def spread(block):
        whole = lax.all_gather(block.reshape(seqs, part, d), "tensor", axis=1, tiled=True)
        return whole.reshape(rows, d)

    layer_output = spread(out_rows)

    back = {}
    for k in (3, 2, 1, 0):
        back[k] = ffn_back(normed_low, g_low, up_w[k], down_w[k], made[k][0], made[k][1])

    def gather_sum(shares):
        near = (shares[0].astype(F32) + swap(shares[1], 1).astype(F32))
        far = (shares[2].astype(F32) + swap(shares[3], 1).astype(F32)).astype(BF)
        return (near + swap(far, 2).astype(F32)).astype(BF)

    down_sum = gather_sum([back[k][2] for k in range(4)])
    up_sum = gather_sum([back[k][1] for k in range(4)])
    ffn_sums = lax.psum((down_sum, up_sum), "dp")

    res = inner_norm(sum_grad, [back[k][0] for k in range(4)], xhat, rstd, ig, att, merge_w)
    inner_grad, att_grad, merge_grad, inner_small = res[0], res[1:5], res[5:9], res[9]

    got = [att_grad[0]] + [swap(att_grad[k], k) for k in (1, 2, 3)]
    grad = [jnp.zeros((192, frames), BF) for _ in range(seqs)]
    for u in range(seqs):
        for k in range(4):
            grad[u] = lax.dynamic_update_slice_in_dim(
                grad[u], got[k][:, u * part : (u + 1) * part], (t ^ k) * part, 1
            )

    small = jnp.concatenate([inner_small, outer_small], axis=0)
    small = small + swap(small, 1)
    small = small + swap(small, 2)
    merge_sum = gather_sum(merge_grad)

    bwd = [attend_backward(each[u], qkv, grad[u], fwd[u][1], fwd[u][2], u, frames) for u in range(seqs)]
    dq, dk, dv = (jnp.concatenate([bwd[u][i][:, :192] for u in range(seqs)], axis=0) for i in range(3))
    joint_grad = jnp.concatenate([dq, dk, dv], axis=1)
    qkv_grad = tn(tokens, joint_grad).astype(BF)
    tail = jnp.concatenate([qkv_grad.reshape(-1, d), merge_sum, small.astype(BF)], axis=0)
    ffn_sums, tail = lax.optimization_barrier((ffn_sums, tail))
    tail = lax.psum(tail, "dp")

    entry = nt(joint_grad, jnp.concatenate([wq, wk, wv], axis=1)).astype(BF).reshape(seqs, 4, part, d)

    def entry_block(k):
        return lax.dynamic_slice_in_dim(entry, t ^ k, 1, 1)[:, 0]

    one = jnp.stack([entry_block(1), entry_block(3)])
    one = swap(one, 1)
    far = (entry_block(2).astype(F32) + one[1].astype(F32)).astype(BF)
    near = entry_block(0).astype(F32) + one[0].astype(F32)
    total = near + swap(far, 2).astype(F32)
    input_rows = (inner_grad + total.reshape(seqs * part, d)).astype(BF)
    input_grad = spread(input_rows)

    split = d * wq.shape[1] * 3 // d
    qkv_sum = tail[:split].reshape(d, 3, wq.shape[1]).astype(F32)
    merge_sum = tail[split : split + wm.shape[0]].astype(F32)
    small = tail[split + wm.shape[0] :].astype(F32)
    return (
        layer_output,
        input_grad,
        qkv_sum[:, 0],
        qkv_sum[:, 1],
        qkv_sum[:, 2],
        merge_sum,
        ffn_sums[1].astype(F32),
        ffn_sums[0].astype(F32),
        small[0],
        small[1],
        small[2],
        small[3],
    )


def solution(mesh):
    in_specs = (
        P("dp", None),
        P("dp"),
        P("dp", None),
        P(None, "tensor"),
        P(None, "tensor"),
        P(None, "tensor"),
        P("tensor", None),
        P(None, "tensor"),
        P("tensor", None),
        P(),
        P(),
        P(),
        P(),
        P("dp", None),
    )
    out_specs = (
        P("dp", None),
        P("dp", None),
        P(None, "tensor"),
        P(None, "tensor"),
        P(None, "tensor"),
        P("tensor", None),
        P(None, "tensor"),
        P("tensor", None),
        P(),
        P(),
        P(),
        P(),
    )
    body = functools.partial(local, mesh.shape["dp"])
    return jax.shard_map(body, mesh=mesh, in_specs=in_specs, out_specs=out_specs, check_vma=False)
```

```python
import functools

import jax
import jax.numpy as jnp
from jax import lax
from jax.experimental import pallas as pl
from jax.experimental.pallas import tpu as pltpu
from jax.sharding import PartitionSpec as P

HEAD_DIM = 64
SPAN = 10
EPS = 1e-05
LOG2E = 1.4426950408889634
KB = 256
VMEM = 60
BF = jnp.bfloat16
F32 = jnp.float32
MIB = 1 << 20


def nn(a, b):
    return lax.dot_general(a, b, (((1,), (0,)), ((), ())), preferred_element_type=F32)


def nt(a, b):
    return lax.dot_general(a, b, (((1,), (1,)), ((), ())), preferred_element_type=F32)


def tn(a, b):
    return lax.dot_general(a, b, (((0,), (0,)), ((), ())), preferred_element_type=F32)


def params(limit):
    return pltpu.CompilerParams(vmem_limit_bytes=limit * MIB)


def cost(flops):
    return pl.CostEstimate(flops=flops, bytes_accessed=1024, transcendentals=0)


def project_kernel(x_ref, wq_ref, wk_ref, wv_ref, q_ref, k_ref, v_ref):
    x = x_ref[...]
    for w_ref, o_ref in ((wq_ref, q_ref), (wk_ref, k_ref), (wv_ref, v_ref)):
        o_ref[:, :192] = nn(x, w_ref[...]).astype(BF)
        o_ref[:, 192:] = jnp.zeros((x.shape[0], HEAD_DIM), BF)


def project(tokens, wq, wk, wv):
    rows, d = tokens.shape
    block = 512
    return pl.pallas_call(
        project_kernel,
        grid=(rows // block,),
        in_specs=[pl.BlockSpec((block, d), lambda i: (i, 0))]
        + [pl.BlockSpec((d, 192), lambda i: (0, 0))] * 3,
        out_specs=[pl.BlockSpec((block, 256), lambda i: (i, 0))] * 3,
        out_shape=[jax.ShapeDtypeStruct((rows, 256), BF)] * 3,
        compiler_params=params(VMEM),
        cost_estimate=cost(1000),
        name="project",
    )(tokens, wq, wk, wv)


def lane_parts(block):
    left = block[:, :128]
    lane = lax.broadcasted_iota(jnp.int32, left.shape, 1)
    zero = jnp.zeros_like(left)
    return (
        jnp.where(lane < HEAD_DIM, left, zero),
        jnp.where(lane >= HEAD_DIM, left, zero),
        block[:, 128:],
    )


TILE = (0, 0, 1)


def forward_kernel(meta_ref, q_ref, k_ref, v_ref, o0_ref, o1_ref, o2_ref, o3_ref, o32_ref, lse_ref, s_ref):
    length = meta_ref[1]
    step = pl.program_id(0)
    blocks = lax.div(length + KB - 1, KB)
    parts = lane_parts(q_ref[...] * jnp.asarray(0.125, BF))
    width = q_ref.shape[0]

    def first(kb, highest):
        start = pl.multiple_of(kb * KB, KB)
        rows = pl.ds(start, KB)
        live = start + lax.broadcasted_iota(jnp.int32, (KB, width), 0) < length
        out = []
        for h in range(3):
            tile = pl.ds(128 * TILE[h], 128)
            s = nt(k_ref[rows, tile], parts[h])
            s = jnp.where(live, s, -1e30)
            s_ref[h, rows, :] = s
            out.append(jnp.maximum(highest[h], jnp.max(s, axis=0, keepdims=True)))
        return tuple(out)

    floor = jnp.full((1, width), -1e30, F32)
    highest = lax.fori_loop(0, blocks, first, (floor,) * 3)

    def second(kb, carry):
        rows = pl.ds(pl.multiple_of(kb * KB, KB), KB)
        out = []
        for h in range(3):
            total, result = carry[h]
            p = jnp.exp2((s_ref[h, rows, :] - highest[h]) * LOG2E)
            total = total + jnp.sum(p, axis=0, keepdims=True)
            v = v_ref[rows, pl.ds(128 * TILE[h], 128)]
            result = result + tn(v, p.astype(BF))
            out.append((total, result))
        return tuple(out)

    init = ((jnp.zeros((1, width), F32), jnp.zeros((128, width), F32)),) * 3
    done = lax.fori_loop(0, blocks, second, init)
    outs = []
    for h in range(3):
        total, result = done[h]
        lo = HEAD_DIM * (h % 2)
        o = result[lo : lo + HEAD_DIM] / total
        o32_ref[0, pl.ds(h * HEAD_DIM, HEAD_DIM), :] = o
        lse_ref[0, pl.ds(h, 1), :] = highest[h] * LOG2E + jnp.log2(total)
        outs.append(o.astype(BF))
    whole = jnp.concatenate(outs, axis=0)
    for k, o_ref in enumerate((o0_ref, o1_ref, o2_ref, o3_ref)):

        @pl.when(step == k)
        def _():
            o_ref[...] = whole


def attend_forward(meta, q, k, v, u, frames):
    part = frames // 4
    return pl.pallas_call(
        forward_kernel,
        grid_spec=pltpu.PrefetchScalarGridSpec(
            num_scalar_prefetch=1,
            grid=(4,),
            in_specs=[
                pl.BlockSpec((part, 256), lambda i, m: (u * 4 + (i ^ m[0]), 0)),
                pl.BlockSpec((frames, 256), lambda i, m: (u, 0)),
                pl.BlockSpec((frames, 256), lambda i, m: (u, 0)),
            ],
            out_specs=[pl.BlockSpec((192, part), lambda i, m: (0, 0))] * 4
            + [
                pl.BlockSpec((1, 192, part), lambda i, m: (i, 0, 0)),
                pl.BlockSpec((1, 8, part), lambda i, m: (i, 0, 0)),
            ],
            scratch_shapes=[pltpu.VMEM((3, frames, part), F32)],
        ),
        out_shape=[jax.ShapeDtypeStruct((192, part), BF)] * 4
        + [
            jax.ShapeDtypeStruct((4, 192, part), F32),
            jax.ShapeDtypeStruct((4, 8, part), F32),
        ],
        compiler_params=params(VMEM),
        cost_estimate=cost(1000),
        name="attend_forward",
    )(meta, q, k, v)


def backward_kernel(
    meta_ref, q_ref, k_ref, v_ref, d0_ref, d1_ref, d2_ref, d3_ref, o32_ref, lse_ref,
    dq_ref, dk_ref, dv_ref, kt_ref, dk_acc, dv_acc, do_ref,
):
    length = meta_ref[1]
    blocks = lax.div(length + KB - 1, KB)
    step = pl.program_id(0)

    @pl.when(step == 0)
    def _():
        dk_acc[...] = jnp.zeros_like(dk_acc)
        dv_acc[...] = jnp.zeros_like(dv_acc)
        kt_ref[...] = jnp.transpose(k_ref[...])

    for k, d_ref in enumerate((d0_ref, d1_ref, d2_ref, d3_ref)):

        @pl.when(step == k)
        def _():
            do_ref[...] = d_ref[...]

    parts = lane_parts(q_ref[...] * jnp.asarray(0.125, BF))
    width = q_ref.shape[0]
    empty = jnp.zeros((HEAD_DIM, width), BF)
    head = [do_ref[pl.ds(h * HEAD_DIM, HEAD_DIM), :] for h in range(3)]
    grads = (
        jnp.concatenate([head[0], empty], axis=0),
        jnp.concatenate([empty, head[1]], axis=0),
        jnp.concatenate([head[2], empty], axis=0),
    )
    delta = [
        jnp.sum(
            head[h].astype(F32) * o32_ref[0, pl.ds(h * HEAD_DIM, HEAD_DIM), :], axis=0, keepdims=True
        )
        for h in range(3)
    ]
    lse = [lse_ref[0, pl.ds(h, 1), :] for h in range(3)]

    def body(kb, carry):
        start = pl.multiple_of(kb * KB, KB)
        rows = pl.ds(start, KB)
        live = start + lax.broadcasted_iota(jnp.int32, (KB, width), 0) < length
        out = []
        for h in range(3):
            tile = pl.ds(128 * TILE[h], 128)
            s = nt(k_ref[rows, tile], parts[h])
            s = jnp.where(live, s, -1e30)
            p = jnp.exp2(s * LOG2E - lse[h])
            dp = nn(v_ref[rows, tile], grads[h])
            ds = (p * (dp - delta[h])).astype(BF)
            dv_acc[rows, tile] += nt(p.astype(BF), grads[h])
            dk_acc[rows, tile] += nn(ds, parts[h])
            kt = kt_ref[pl.ds(h * HEAD_DIM, HEAD_DIM), rows]
            out.append(carry[h] + nn(kt, ds))
        return tuple(out)

    zero = jnp.zeros((HEAD_DIM, width), F32)
    done = lax.fori_loop(0, blocks, body, (zero,) * 3)
    full = jnp.concatenate(done + (zero,), axis=0) * 0.125
    dq_ref[...] = jnp.transpose(full).astype(BF)

    @pl.when(step == pl.num_programs(0) - 1)
    def _():
        dk_ref[...] = dk_acc[...].astype(BF)
        dv_ref[...] = dv_acc[...].astype(BF)


def attend_backward(meta, q, k, v, grads, o32, lse, u, frames):
    part = frames // 4
    return pl.pallas_call(
        backward_kernel,
        grid_spec=pltpu.PrefetchScalarGridSpec(
            num_scalar_prefetch=1,
            grid=(4,),
            in_specs=[
                pl.BlockSpec((part, 256), lambda i, m: (u * 4 + (i ^ m[0]), 0)),
                pl.BlockSpec((frames, 256), lambda i, m: (u, 0)),
                pl.BlockSpec((frames, 256), lambda i, m: (u, 0)),
            ]
            + [pl.BlockSpec((192, part), lambda i, m: (0, u))] * 4
            + [
                pl.BlockSpec((1, 192, part), lambda i, m: (i, 0, 0)),
                pl.BlockSpec((1, 8, part), lambda i, m: (i, 0, 0)),
            ],
            out_specs=[
                pl.BlockSpec((part, 256), lambda i, m: (i ^ m[0], 0)),
                pl.BlockSpec((frames, 256), lambda i, m: (0, 0)),
                pl.BlockSpec((frames, 256), lambda i, m: (0, 0)),
            ],
            scratch_shapes=[
                pltpu.VMEM((256, frames), BF),
                pltpu.VMEM((frames, 256), F32),
                pltpu.VMEM((frames, 256), F32),
                pltpu.VMEM((192, part), BF),
            ],
        ),
        out_shape=[jax.ShapeDtypeStruct((frames, 256), BF)] * 3,
        compiler_params=params(VMEM),
        cost_estimate=cost(1000),
        name="attend_backward",
    )(meta, q, k, v, *grads, o32, lse)


def entry_kernel(meta_ref, x_ref, dq_ref, dk_ref, dv_ref, wq_ref, wk_ref, wv_ref, before_ref, send_ref, keep_ref, sum_ref, acc):
    step = pl.program_id(0)
    x = x_ref[...]
    total = jnp.zeros(x.shape, F32)

    @pl.when(step == 0)
    def _():
        acc[...] = before_ref[...]

    for i, (g_ref, w_ref) in enumerate(((dq_ref, wq_ref), (dk_ref, wk_ref), (dv_ref, wv_ref))):
        g = g_ref[:, :192]
        total = total + nt(g, w_ref[...])
        acc[pl.ds(192 * i, 192), :] += tn(g, x)
    low = total.astype(BF)

    @pl.when(step < 2)
    def _():
        send_ref[0] = low

    @pl.when(step >= 2)
    def _():
        keep_ref[0] = low

    @pl.when(step == 3)
    def _():
        sum_ref[...] = acc[...].astype(sum_ref.dtype)


def entry_back(meta, tokens, grads, weights, before, u, frames, dtype):
    part = frames // 4
    d = tokens.shape[1]

    def block(i, m):
        return jnp.where(i < 2, 2 * i + 1, 2 * i - 4) ^ m[0]

    return pl.pallas_call(
        entry_kernel,
        grid_spec=pltpu.PrefetchScalarGridSpec(
            num_scalar_prefetch=1,
            grid=(4,),
            in_specs=[pl.BlockSpec((part, d), lambda i, m: (u * 4 + block(i, m), 0))]
            + [pl.BlockSpec((part, 256), lambda i, m: (block(i, m), 0))] * 3
            + [pl.BlockSpec((d, 192), lambda i, m: (0, 0))] * 3
            + [pl.BlockSpec((576, d), lambda i, m: (0, 0))],
            out_specs=[
                pl.BlockSpec((1, part, d), lambda i, m: (jnp.minimum(i, 1), 0, 0)),
                pl.BlockSpec((1, part, d), lambda i, m: (jnp.maximum(i - 2, 0), 0, 0)),
                pl.BlockSpec((576, d), lambda i, m: (0, 0)),
            ],
            scratch_shapes=[pltpu.VMEM((576, d), F32)],
        ),
        out_shape=[
            jax.ShapeDtypeStruct((2, part, d), BF),
            jax.ShapeDtypeStruct((2, part, d), BF),
            jax.ShapeDtypeStruct((576, d), dtype),
        ],
        compiler_params=params(VMEM),
        cost_estimate=cost(1000),
        name="entry_back",
    )(meta, tokens, *grads, *weights, before)


def place_kernel(meta_ref, r0_ref, r1_ref, r2_ref, r3_ref, o_ref):
    for k, r_ref in enumerate((r0_ref, r1_ref, r2_ref, r3_ref)):

        @pl.when(pl.program_id(1) == k)
        def _():
            o_ref[...] = r_ref[0]


def place(meta, blocks, seqs):
    part, d = blocks[0].shape[1:]
    return pl.pallas_call(
        place_kernel,
        grid_spec=pltpu.PrefetchScalarGridSpec(
            num_scalar_prefetch=1,
            grid=(seqs, 4),
            in_specs=[pl.BlockSpec((1, part, d), lambda u, k, m: (u, 0, 0))] * 4,
            out_specs=pl.BlockSpec((part, d), lambda u, k, m: (u * 4 + (k ^ m[0]), 0)),
        ),
        out_shape=jax.ShapeDtypeStruct((seqs * 4 * part, d), blocks[0].dtype),
        compiler_params=params(VMEM),
        cost_estimate=cost(1000),
        name="place",
    )(meta, *blocks)


def finish_kernel(sum_ref, q_ref, k_ref, v_ref):
    for i, o_ref in enumerate((q_ref, k_ref, v_ref)):
        o_ref[...] = jnp.transpose(sum_ref[pl.ds(192 * i, 192), :].astype(F32))


def finish(total):
    d = total.shape[1]
    return pl.pallas_call(
        finish_kernel,
        out_shape=[jax.ShapeDtypeStruct((d, 192), F32)] * 3,
        compiler_params=params(VMEM),
        cost_estimate=cost(1000),
        name="finish",
    )(total)


def normalise(values):
    average = jnp.mean(values, axis=-1, keepdims=True)
    centred = values - average
    spread = jnp.mean(centred * centred, axis=-1, keepdims=True)
    rstd = lax.rsqrt(spread + EPS)
    return centred * rstd, rstd


def merge_kernel(seqs, *refs):
    tok_ref = refs[0]
    att = refs[1 : 1 + 4 * seqs]
    weights = refs[1 + 4 * seqs : 5 + 4 * seqs]
    gain_ref, bias_ref, xhat_ref, rstd_ref, low_ref = refs[5 + 4 * seqs :]
    part = tok_ref.shape[0] // seqs
    for u in range(seqs):
        rows = pl.ds(u * part, part)
        branch = jnp.zeros((part, tok_ref.shape[1]), F32)
        for k in range(4):
            branch = branch + tn(att[u * 4 + k][...], weights[k][...]).astype(BF).astype(F32)
        xhat, rstd = normalise(tok_ref[rows, :].astype(F32) + branch)
        xhat_ref[rows, :] = xhat
        rstd_ref[rows, :] = jnp.broadcast_to(rstd, (part, rstd_ref.shape[1]))
        low_ref[rows, :] = (xhat * gain_ref[...] + bias_ref[...]).astype(BF)


def merge_forward(tok, att, weights, gain, bias):
    rows, d = tok.shape
    return pl.pallas_call(
        functools.partial(merge_kernel, len(att)),
        out_shape=[
            jax.ShapeDtypeStruct((rows, d), F32),
            jax.ShapeDtypeStruct((rows, 128), F32),
            jax.ShapeDtypeStruct((rows, d), BF),
        ],
        compiler_params=params(VMEM),
        cost_estimate=cost(1000),
        name="merge_forward",
    )(tok, *(a for each in att for a in each), *weights, gain, bias)


def gelu_pair(v):
    e = jnp.exp2(v * v * (-0.5 * LOG2E))
    t = 1.0 / (1.0 + (0.3275911 * 0.7071067811865476) * jnp.abs(v))
    poly = t * (0.5 * 0.254829592 + t * (0.5 * -0.284496736 + t * (0.5 * 1.421413741 + t * (0.5 * -1.453152027 + t * (0.5 * 1.061405429)))))
    tail = poly * e
    phi_cap = jnp.where(v >= 0, 1.0 - tail, tail)
    return v * phi_cap, phi_cap + v * (e * 0.3989422804014327)


def up_down_kernel(x_ref, up_ref, down_ref, act_ref, slope_ref, part_ref, acc):
    step = pl.program_id(0)
    act, slope = gelu_pair(nn(x_ref[...], up_ref[...]))
    low = act.astype(BF)
    act_ref[...] = low
    slope_ref[...] = slope
    product = nn(low, down_ref[...])

    @pl.when(step == 0)
    def _():
        acc[...] = product

    @pl.when(step > 0)
    def _():
        acc[...] += product

    @pl.when(step == pl.num_programs(0) - 1)
    def _():
        part_ref[...] = acc[...].astype(BF)


HB = 256


def up_down(x, up, down):
    rows, d = x.shape
    hidden = up.shape[1]
    return pl.pallas_call(
        up_down_kernel,
        grid=(hidden // HB,),
        in_specs=[
            pl.BlockSpec((rows, d), lambda i: (0, 0)),
            pl.BlockSpec((d, HB), lambda i: (0, i)),
            pl.BlockSpec((HB, d), lambda i: (i, 0)),
        ],
        out_specs=[
            pl.BlockSpec((rows, HB), lambda i: (0, i)),
            pl.BlockSpec((rows, HB), lambda i: (0, i)),
            pl.BlockSpec((rows, d), lambda i: (0, 0)),
        ],
        out_shape=[
            jax.ShapeDtypeStruct((rows, hidden), BF),
            jax.ShapeDtypeStruct((rows, hidden), F32),
            jax.ShapeDtypeStruct((rows, d), BF),
        ],
        scratch_shapes=[pltpu.VMEM((rows, d), F32)],
        compiler_params=params(VMEM),
        cost_estimate=cost(1000),
        name="up_down",
    )(x, up, down)


def outer_kernel(
    xhat_ref, p0, p1, p2, p3, grad_ref, weight_ref, ig_ref, ib_ref, og_ref, ob_ref, out_ref, sum_grad_ref, low_ref, small_ref
):
    branch = p0[...].astype(F32) + p1[...].astype(F32) + p2[...].astype(F32) + p3[...].astype(F32)
    normed = xhat_ref[...] * ig_ref[...] + ib_ref[...]
    xhat, rstd = normalise(normed + branch)
    out_ref[...] = (xhat * og_ref[...] + ob_ref[...]).astype(BF)
    cot = grad_ref[...].astype(F32) * weight_ref[...]
    small_ref[0:1, :] = jnp.sum(cot * xhat, axis=0, keepdims=True)
    small_ref[1:2, :] = jnp.sum(cot, axis=0, keepdims=True)
    gy = cot * og_ref[...]
    mean_gy = jnp.mean(gy, axis=-1, keepdims=True)
    mean_gx = jnp.mean(gy * xhat, axis=-1, keepdims=True)
    sum_grad = rstd * (gy - mean_gy - xhat * mean_gx)
    sum_grad_ref[...] = sum_grad
    low_ref[...] = sum_grad.astype(BF)


def outer_norm(xhat, parts, grad, weight, ig, ib, og, ob):
    rows, d = xhat.shape
    return pl.pallas_call(
        outer_kernel,
        out_shape=[
            jax.ShapeDtypeStruct((rows, d), BF),
            jax.ShapeDtypeStruct((rows, d), F32),
            jax.ShapeDtypeStruct((rows, d), BF),
            jax.ShapeDtypeStruct((2, d), F32),
        ],
        compiler_params=params(VMEM),
        cost_estimate=cost(1000),
        name="outer_norm",
    )(xhat, *parts, grad, weight, ig, ib, og, ob)


def ffn_back_kernel(x_ref, g_ref, up_ref, down_ref, act_ref, slope_ref, part_ref, dup_ref, ddown_ref, acc):
    step = pl.program_id(0)
    g = g_ref[...]
    low = (nt(g, down_ref[...]) * slope_ref[...]).astype(BF)
    product = nt(low, up_ref[...])
    ddown_ref[...] = tn(act_ref[...], g).astype(BF)
    dup_ref[...] = tn(x_ref[...], low).astype(BF)

    @pl.when(step == 0)
    def _():
        acc[...] = product

    @pl.when(step > 0)
    def _():
        acc[...] += product

    @pl.when(step == pl.num_programs(0) - 1)
    def _():
        part_ref[...] = acc[...].astype(BF)


def ffn_back(x, g, up, down, act, slope):
    rows, d = x.shape
    hidden = up.shape[1]
    return pl.pallas_call(
        ffn_back_kernel,
        grid=(hidden // HB,),
        in_specs=[
            pl.BlockSpec((rows, d), lambda i: (0, 0)),
            pl.BlockSpec((rows, d), lambda i: (0, 0)),
            pl.BlockSpec((d, HB), lambda i: (0, i)),
            pl.BlockSpec((HB, d), lambda i: (i, 0)),
            pl.BlockSpec((rows, HB), lambda i: (0, i)),
            pl.BlockSpec((rows, HB), lambda i: (0, i)),
        ],
        out_specs=[
            pl.BlockSpec((rows, d), lambda i: (0, 0)),
            pl.BlockSpec((d, HB), lambda i: (0, i)),
            pl.BlockSpec((HB, d), lambda i: (i, 0)),
        ],
        out_shape=[
            jax.ShapeDtypeStruct((rows, d), BF),
            jax.ShapeDtypeStruct((d, hidden), BF),
            jax.ShapeDtypeStruct((hidden, d), BF),
        ],
        scratch_shapes=[pltpu.VMEM((rows, d), F32)],
        compiler_params=params(VMEM),
        cost_estimate=cost(1000),
        name="ffn_back",
    )(x, g, up, down, act, slope)


def inner_kernel(seqs, sum_grad_ref, p0, p1, p2, p3, xhat_ref, rstd_ref, gain_ref, *refs):
    att = refs[: 4 * seqs]
    weights = refs[4 * seqs : 4 * seqs + 4]
    out_ref, g0, g1, g2, g3, m0, m1, m2, m3, small_ref = refs[4 * seqs + 4 :]
    part = out_ref.shape[0] // seqs
    grad = sum_grad_ref[...] + (
        p0[...].astype(F32) + p1[...].astype(F32) + p2[...].astype(F32) + p3[...].astype(F32)
    )
    xhat = xhat_ref[...]
    small_ref[0:1, :] = jnp.sum(grad * xhat, axis=0, keepdims=True)
    small_ref[1:2, :] = jnp.sum(grad, axis=0, keepdims=True)
    gy = grad * gain_ref[...]
    mean_gy = jnp.mean(gy, axis=-1, keepdims=True)
    mean_gx = jnp.mean(gy * xhat, axis=-1, keepdims=True)
    inner = rstd_ref[:, 0:1] * (gy - mean_gy - xhat * mean_gx)
    out_ref[...] = inner
    low = inner.astype(BF)
    for k, (g, m) in enumerate(((g0, m0), (g1, m1), (g2, m2), (g3, m3))):
        g[...] = nt(weights[k][...], low).astype(BF)
        m[...] = sum(nn(att[u * 4 + k][...], low[u * part : (u + 1) * part]) for u in range(seqs)).astype(BF)


def inner_norm(sum_grad, parts, xhat, rstd, gain, att, weights):
    rows, d = xhat.shape
    return pl.pallas_call(
        functools.partial(inner_kernel, len(att)),
        out_shape=[jax.ShapeDtypeStruct((rows, d), F32)]
        + [jax.ShapeDtypeStruct((192, rows), BF)] * 4
        + [jax.ShapeDtypeStruct((192, d), BF)] * 4
        + [jax.ShapeDtypeStruct((2, d), F32)],
        compiler_params=params(VMEM),
        cost_estimate=cost(1000),
        name="inner_norm",
    )(sum_grad, *parts, xhat, rstd, gain, *(a for each in att for a in each), *weights)


def local(groups, tokens, lengths, span_starts, wq, wk, wv, wm, wu, wd, ig, ib, og, ob, out_grad):
    rows, d = tokens.shape
    seqs = lengths.shape[0]
    frames = rows // seqs
    part = frames // 4
    t = lax.axis_index("tensor")
    place_dp = lax.axis_index("dp")
    bits = groups.bit_length() - 1
    y = place_dp % 2

    def swap(value, k):
        return lax.ppermute(value, "tensor", [(i, i ^ k) for i in range(4)])

    def swap_dp(value, b):
        return lax.ppermute(value, "dp", [(i, i ^ (1 << b)) for i in range(groups)])

    def add(a, b):
        return (a.astype(F32) + b.astype(F32)).astype(BF)

    def halve(array, b):
        half = array.shape[0] // 2
        bit = (place_dp >> b) & 1
        got = swap_dp(lax.dynamic_slice_in_dim(array, (1 - bit) * half, half, 0), b)
        return add(lax.dynamic_slice_in_dim(array, bit * half, half, 0), got)

    def double(array, b):
        got = swap_dp(array, b)
        bit = (place_dp >> b) & 1
        return jnp.concatenate([jnp.where(bit, got, array), jnp.where(bit, array, got)], axis=0)

    def sum_over(order, near, far=None):
        for b in order:
            if b == "x":
                near, far = add(near, swap(far, 2)), None
            else:
                near = halve(near, b)
                far = None if far is None else halve(far, b)
        for b in reversed([b for b in order if b != "x"]):
            near = double(near, b)
        return near

    def gather(own):
        half = own.shape[0] // 2
        mine = lax.dynamic_slice_in_dim(own, y * half, half, 0)
        first = swap(mine, 2)
        second = swap_dp(first, 0)
        across = jnp.concatenate([jnp.where(y, second, first), jnp.where(y, first, second)], axis=0)
        return own, swap(own, 1), across, swap(across, 1)

    merge_w = gather(wm)
    up_w = gather(wu)
    down_w = gather(wd)

    q, k, v = project(tokens, wq, wk, wv)
    meta = [jnp.stack([t, lengths[u]]) for u in range(seqs)]
    fwd = [attend_forward(meta[u], q, k, v, u, frames) for u in range(seqs)]
    att = [[fwd[u][0]] + [swap(fwd[u][j], j) for j in (1, 2, 3)] for u in range(seqs)]

    def own_rows(array):
        cut = lax.dynamic_slice_in_dim(array.reshape(seqs, frames, -1), t * part, part, 1)
        return cut.reshape(seqs * part, -1)

    tok = own_rows(tokens)
    positions = t * part + jnp.arange(part)
    inside = (positions[None, None, :] >= span_starts[:, :, None]) & (
        positions[None, None, :] < span_starts[:, :, None] + SPAN
    )
    weight = jnp.any(inside, axis=1).astype(F32).reshape(seqs * part, 1)
    ig, ib, og, ob = (vec.reshape(1, d) for vec in (ig, ib, og, ob))

    xhat, rstd, normed_low = merge_forward(tok, att, merge_w, ig, ib)
    made = {j: up_down(normed_low, up_w[j], down_w[j]) for j in range(4)}
    out_rows, sum_grad, g_low, outer_small = outer_norm(
        xhat, [made[j][2] for j in range(4)], own_rows(out_grad), weight, ig, ib, og, ob
    )
    whole = lax.all_gather(out_rows.reshape(seqs, part, d), "tensor", axis=1, tiled=True)
    layer_output = whole.reshape(rows, d)

    back = {j: ffn_back(normed_low, g_low, up_w[j], down_w[j], made[j][0], made[j][1]) for j in (3, 2, 1, 0)}
    res = inner_norm(sum_grad, [back[j][0] for j in range(4)], xhat, rstd, ig, att, merge_w)
    inner_grad, att_grad, merge_grad, inner_small = res[0], res[1:5], res[5:9], res[9]
    got = [att_grad[0]] + [swap(att_grad[j], j) for j in (1, 2, 3)]

    def chip_sums(shares):
        return add(shares[0], swap(shares[1], 1)), add(shares[2], swap(shares[3], 1))

    rest = list(range(2, bits))
    down_sum = sum_over([0, "x", 1] + rest, *chip_sums([back[j][2] for j in range(4)]))
    up_sum = sum_over([1, "x", 0] + rest, *chip_sums([back[j][1] for j in range(4)]))

    small = jnp.concatenate([inner_small, outer_small], axis=0)
    small = small + swap(small, 1)
    small = small + swap(small, 2)
    merge_near, merge_far = chip_sums(merge_grad)
    merge_near = add(merge_near, swap(merge_far, 2))
    merge_near = jnp.concatenate([merge_near, small.astype(BF), jnp.zeros((60, d), BF)], axis=0)
    merge_sum = sum_over([0, 1] + rest, merge_near)

    before = jnp.zeros((576, d), F32)
    entry = []
    for u in range(seqs):
        grads = attend_backward(meta[u], q, k, v, got, fwd[u][4], fwd[u][5], u, frames)
        last = u == seqs - 1
        entry.append(entry_back(meta[u], tokens, grads, (wq, wk, wv), before, u, frames, BF if last else F32))
        before = entry[-1][2]
    qkv_sum = sum_over([0, 1] + rest, before)

    ready = []
    for u in range(seqs):
        send, keep = entry[u][:2]
        one = swap(send, 1)
        far = swap(add(keep[1], one[1]), 2)
        total = keep[0].astype(F32) + one[0].astype(F32) + far.astype(F32)
        ready.append((inner_grad[u * part : (u + 1) * part] + total).astype(BF))
    ready = jnp.stack(ready)
    across = swap(ready, 2)
    input_grad = place(meta[0], (ready, swap(ready, 1), across, swap(across, 1)), seqs)

    query_grad, key_grad, value_grad = finish(qkv_sum)
    small = merge_sum[192:196].astype(F32)
    return (
        layer_output,
        input_grad,
        query_grad,
        key_grad,
        value_grad,
        merge_sum[:192].astype(F32),
        up_sum.astype(F32),
        down_sum.astype(F32),
        small[0],
        small[1],
        small[2],
        small[3],
    )


def solution(mesh):
    in_specs = (
        P("dp", None),
        P("dp"),
        P("dp", None),
        P(None, "tensor"),
        P(None, "tensor"),
        P(None, "tensor"),
        P("tensor", None),
        P(None, "tensor"),
        P("tensor", None),
        P(),
        P(),
        P(),
        P(),
        P("dp", None),
    )
    out_specs = (
        P("dp", None),
        P("dp", None),
        P(None, "tensor"),
        P(None, "tensor"),
        P(None, "tensor"),
        P("tensor", None),
        P(None, "tensor"),
        P("tensor", None),
        P(),
        P(),
        P(),
        P(),
    )
    body = functools.partial(local, mesh.shape["dp"])
    return jax.shard_map(body, mesh=mesh, in_specs=in_specs, out_specs=out_specs, check_vma=False)
```

```python
import functools

import jax
import jax.numpy as jnp
from jax import lax
from jax.experimental import pallas as pl
from jax.experimental.pallas import tpu as pltpu
from jax.sharding import PartitionSpec as P

HEAD_DIM = 64
SPAN = 10
EPS = 1e-05
LOG2E = 1.4426950408889634
KB = 256
VMEM = 32
BF = jnp.bfloat16
F32 = jnp.float32
MIB = 1 << 20


def nn(a, b):
    return lax.dot_general(a, b, (((1,), (0,)), ((), ())), preferred_element_type=F32)


def nt(a, b):
    return lax.dot_general(a, b, (((1,), (1,)), ((), ())), preferred_element_type=F32)


def tn(a, b):
    return lax.dot_general(a, b, (((0,), (0,)), ((), ())), preferred_element_type=F32)


def params(limit):
    return pltpu.CompilerParams(vmem_limit_bytes=limit * MIB)


def cost(flops):
    return pl.CostEstimate(flops=flops, bytes_accessed=1024, transcendentals=0)


def project_kernel(x_ref, wq_ref, wk_ref, wv_ref, q_ref, k_ref, v_ref):
    x = x_ref[...]
    for w_ref, o_ref in ((wq_ref, q_ref), (wk_ref, k_ref), (wv_ref, v_ref)):
        o_ref[:, :192] = nn(x, w_ref[...]).astype(BF)
        o_ref[:, 192:] = jnp.zeros((x.shape[0], HEAD_DIM), BF)


def project(tokens, wq, wk, wv):
    rows, d = tokens.shape
    block = 512
    return pl.pallas_call(
        project_kernel,
        grid=(rows // block,),
        in_specs=[pl.BlockSpec((block, d), lambda i: (i, 0))]
        + [pl.BlockSpec((d, 192), lambda i: (0, 0))] * 3,
        out_specs=[pl.BlockSpec((block, 256), lambda i: (i, 0))] * 3,
        out_shape=[jax.ShapeDtypeStruct((rows, 256), BF)] * 3,
        compiler_params=params(VMEM),
        cost_estimate=cost(1000),
        name="project",
    )(tokens, wq, wk, wv)


def lane_parts(block):
    left = block[:, :128]
    lane = lax.broadcasted_iota(jnp.int32, left.shape, 1)
    zero = jnp.zeros_like(left)
    return (
        jnp.where(lane < HEAD_DIM, left, zero),
        jnp.where(lane >= HEAD_DIM, left, zero),
        block[:, 128:],
    )


TILE = (0, 0, 1)


def call(kernel, name, grid, meta, args, in_specs, out_specs, out_shape, scratch=()):
    return pl.pallas_call(
        kernel,
        grid_spec=pltpu.PrefetchScalarGridSpec(
            num_scalar_prefetch=1,
            grid=grid,
            in_specs=in_specs,
            out_specs=out_specs,
            scratch_shapes=scratch,
        ),
        out_shape=out_shape,
        compiler_params=params(VMEM),
        cost_estimate=cost(1000),
        name=name,
    )(meta, *args)


def fixed(*shape):
    return pl.BlockSpec(shape, lambda *_: (0,) * len(shape))


def like(shape, dtype):
    return jax.ShapeDtypeStruct(shape, dtype)


def forward_kernel(meta_ref, q_ref, k_ref, v_ref, own_ref, other_ref, o32_ref, lse_ref, s_ref):
    length = meta_ref[1]
    step = pl.program_id(0)
    blocks = lax.div(length + KB - 1, KB)
    parts = lane_parts(q_ref[...] * jnp.asarray(0.125, BF))
    width = q_ref.shape[0]

    def first(kb, highest):
        start = pl.multiple_of(kb * KB, KB)
        rows = pl.ds(start, KB)
        live = start + lax.broadcasted_iota(jnp.int32, (KB, width), 0) < length
        out = []
        for h in range(3):
            tile = pl.ds(128 * TILE[h], 128)
            s = nt(k_ref[rows, tile], parts[h])
            s = jnp.where(live, s, -1e30)
            s_ref[h, rows, :] = s
            out.append(jnp.maximum(highest[h], jnp.max(s, axis=0, keepdims=True)))
        return tuple(out)

    floor = jnp.full((1, width), -1e30, F32)
    highest = lax.fori_loop(0, blocks, first, (floor,) * 3)

    def second(kb, carry):
        rows = pl.ds(pl.multiple_of(kb * KB, KB), KB)
        out = []
        for h in range(3):
            total, result = carry[h]
            p = jnp.exp2((s_ref[h, rows, :] - highest[h]) * LOG2E)
            total = total + jnp.sum(p, axis=0, keepdims=True)
            v = v_ref[rows, pl.ds(128 * TILE[h], 128)]
            result = result + tn(v, p.astype(BF))
            out.append((total, result))
        return tuple(out)

    init = ((jnp.zeros((1, width), F32), jnp.zeros((128, width), F32)),) * 3
    done = lax.fori_loop(0, blocks, second, init)
    outs = []
    for h in range(3):
        total, result = done[h]
        lo = HEAD_DIM * (h % 2)
        o = result[lo : lo + HEAD_DIM] / total
        o32_ref[0, pl.ds(h * HEAD_DIM, HEAD_DIM), :] = o
        lse_ref[0, pl.ds(h, 1), :] = highest[h] * LOG2E + jnp.log2(total)
        outs.append(o.astype(BF))
    whole = jnp.concatenate(outs, axis=0)
    for j, o_ref in enumerate((own_ref, other_ref)):

        @pl.when(step == j)
        def _():
            o_ref[...] = whole


def attend_forward(meta, q, k, v, u, frames):
    half = frames // 2
    return call(
        forward_kernel,
        "attend_forward",
        (2,),
        meta,
        (q, k, v),
        [
            pl.BlockSpec((half, 256), lambda i, m: (u * 2 + (i ^ m[0]), 0)),
            pl.BlockSpec((frames, 256), lambda i, m: (u, 0)),
            pl.BlockSpec((frames, 256), lambda i, m: (u, 0)),
        ],
        [
            fixed(192, half),
            fixed(192, half),
            pl.BlockSpec((1, 192, half), lambda i, m: (i, 0, 0)),
            pl.BlockSpec((1, 8, half), lambda i, m: (i, 0, 0)),
        ],
        [
            like((192, half), BF),
            like((192, half), BF),
            like((2, 192, half), F32),
            like((2, 8, half), F32),
        ],
        [pltpu.VMEM((3, frames, half), F32)],
    )


def backward_kernel(
    meta_ref, q_ref, k_ref, v_ref, d0_ref, d1_ref, o32_ref, lse_ref,
    dq_ref, dk_ref, dv_ref, kt_ref, dk_acc, dv_acc, do_ref,
):
    length = meta_ref[1]
    blocks = lax.div(length + KB - 1, KB)
    step = pl.program_id(0)

    @pl.when(step == 0)
    def _():
        dk_acc[...] = jnp.zeros_like(dk_acc)
        dv_acc[...] = jnp.zeros_like(dv_acc)
        kt_ref[...] = jnp.transpose(k_ref[...])
        do_ref[...] = d0_ref[...]

    @pl.when(step == 1)
    def _():
        do_ref[...] = d1_ref[...]

    parts = lane_parts(q_ref[...] * jnp.asarray(0.125, BF))
    width = q_ref.shape[0]
    empty = jnp.zeros((HEAD_DIM, width), BF)
    head = [do_ref[pl.ds(h * HEAD_DIM, HEAD_DIM), :] for h in range(3)]
    grads = (
        jnp.concatenate([head[0], empty], axis=0),
        jnp.concatenate([empty, head[1]], axis=0),
        jnp.concatenate([head[2], empty], axis=0),
    )
    delta = [
        jnp.sum(
            head[h].astype(F32) * o32_ref[0, pl.ds(h * HEAD_DIM, HEAD_DIM), :], axis=0, keepdims=True
        )
        for h in range(3)
    ]
    lse = [lse_ref[0, pl.ds(h, 1), :] for h in range(3)]

    def body(kb, carry):
        start = pl.multiple_of(kb * KB, KB)
        rows = pl.ds(start, KB)
        live = start + lax.broadcasted_iota(jnp.int32, (KB, width), 0) < length
        out = []
        for h in range(3):
            tile = pl.ds(128 * TILE[h], 128)
            s = nt(k_ref[rows, tile], parts[h])
            s = jnp.where(live, s, -1e30)
            p = jnp.exp2(s * LOG2E - lse[h])
            dp = nn(v_ref[rows, tile], grads[h])
            ds = (p * (dp - delta[h])).astype(BF)
            dv_acc[rows, tile] += nt(p.astype(BF), grads[h])
            dk_acc[rows, tile] += nn(ds, parts[h])
            kt = kt_ref[pl.ds(h * HEAD_DIM, HEAD_DIM), rows]
            out.append(carry[h] + nn(kt, ds))
        return tuple(out)

    zero = jnp.zeros((HEAD_DIM, width), F32)
    done = lax.fori_loop(0, blocks, body, (zero,) * 3)
    full = jnp.concatenate(done + (zero,), axis=0) * 0.125
    dq_ref[...] = jnp.transpose(full).astype(BF)

    @pl.when(step == 1)
    def _():
        dk_ref[...] = dk_acc[...].astype(BF)
        dv_ref[...] = dv_acc[...].astype(BF)


def attend_backward(meta, q, k, v, own, other, o32, lse, u, frames):
    half = frames // 2
    return call(
        backward_kernel,
        "attend_backward",
        (2,),
        meta,
        (q, k, v, own, other, o32, lse),
        [
            pl.BlockSpec((half, 256), lambda i, m: (u * 2 + (i ^ m[0]), 0)),
            pl.BlockSpec((frames, 256), lambda i, m: (u, 0)),
            pl.BlockSpec((frames, 256), lambda i, m: (u, 0)),
            fixed(192, half),
            fixed(192, half),
            pl.BlockSpec((1, 192, half), lambda i, m: (i, 0, 0)),
            pl.BlockSpec((1, 8, half), lambda i, m: (i, 0, 0)),
        ],
        [
            pl.BlockSpec((half, 256), lambda i, m: (i ^ m[0], 0)),
            fixed(frames, 256),
            fixed(frames, 256),
        ],
        [like((frames, 256), BF)] * 3,
        [
            pltpu.VMEM((256, frames), BF),
            pltpu.VMEM((frames, 256), F32),
            pltpu.VMEM((frames, 256), F32),
            pltpu.VMEM((192, half), BF),
        ],
    )


def entry_kernel(meta_ref, x_ref, dq_ref, dk_ref, dv_ref, wq_ref, wk_ref, wv_ref, *refs):
    before_ref = refs[0] if len(refs) == 5 else None
    send_ref, keep_ref, sum_ref, acc = refs[-4:]
    step = pl.program_id(0)
    x = x_ref[...]
    total = jnp.zeros(x.shape, F32)
    for i, (g_ref, w_ref) in enumerate(((dq_ref, wq_ref), (dk_ref, wk_ref), (dv_ref, wv_ref))):
        rows = pl.ds(192 * i, 192)
        g = g_ref[:, :192]
        total = total + nt(g, w_ref[...])
        product = tn(g, x)

        @pl.when(step == 0)
        def _():
            acc[rows, :] = product if before_ref is None else product + before_ref[rows, :]

        @pl.when(step == 1)
        def _():
            sum_ref[rows, :] = (product + acc[rows, :]).astype(sum_ref.dtype)

    low = total.astype(BF)

    @pl.when(step == 0)
    def _():
        send_ref[...] = low

    @pl.when(step == 1)
    def _():
        keep_ref[...] = low


def entry_back(meta, tokens, grads, weights, before, u, frames, dtype):
    half = frames // 2
    d = tokens.shape[1]
    return call(
        entry_kernel,
        "entry_back",
        (2,),
        meta,
        (tokens, *grads, *weights, *before),
        [pl.BlockSpec((half, d), lambda i, m: (u * 2 + (1 - i ^ m[0]), 0))]
        + [pl.BlockSpec((half, 256), lambda i, m: (1 - i ^ m[0], 0))] * 3
        + [fixed(d, 192)] * 3
        + [fixed(576, d)] * len(before),
        [fixed(half, d), fixed(half, d), fixed(576, d)],
        [like((half, d), BF), like((half, d), BF), like((576, d), dtype)],
        [pltpu.VMEM((576, d), F32)],
    )


def place_kernel(meta_ref, own_ref, other_ref, o_ref):
    for j, r_ref in enumerate((own_ref, other_ref)):

        @pl.when(pl.program_id(1) == j)
        def _():
            o_ref[...] = r_ref[0]


def place(meta, own, other):
    seqs, half, d = own.shape
    return call(
        place_kernel,
        "place",
        (seqs, 2),
        meta,
        (own, other),
        [pl.BlockSpec((1, half, d), lambda u, j, m: (u, 0, 0))] * 2,
        pl.BlockSpec((half, d), lambda u, j, m: (u * 2 + (j ^ m[0]), 0)),
        like((seqs * 2 * half, d), own.dtype),
    )


def finish_kernel(sum_ref, q_ref, k_ref, v_ref):
    for i, o_ref in enumerate((q_ref, k_ref, v_ref)):
        o_ref[...] = jnp.transpose(sum_ref[pl.ds(192 * i, 192), :].astype(F32))


def finish(total):
    d = total.shape[1]
    return pl.pallas_call(
        finish_kernel,
        out_shape=[like((d, 192), F32)] * 3,
        compiler_params=params(VMEM),
        cost_estimate=cost(1000),
        name="finish",
    )(total)


def normalise(values):
    average = jnp.mean(values, axis=-1, keepdims=True)
    centred = values - average
    spread = jnp.mean(centred * centred, axis=-1, keepdims=True)
    rstd = lax.rsqrt(spread + EPS)
    return centred * rstd, rstd


def merge_kernel(meta_ref, tok_ref, a0, a1, a2, a3, w0, w1, w2, w3, gain_ref, bias_ref, xhat_ref, rstd_ref, low_ref):
    branch = jnp.zeros(tok_ref.shape, F32)
    for a, w in ((a0, w0), (a1, w1), (a2, w2), (a3, w3)):
        branch = branch + tn(a[...], w[...]).astype(BF).astype(F32)
    xhat, rstd = normalise(tok_ref[...].astype(F32) + branch)
    xhat_ref[...] = xhat
    rstd_ref[...] = jnp.broadcast_to(rstd, rstd_ref.shape)
    low_ref[...] = (xhat * gain_ref[...] + bias_ref[...]).astype(BF)


def merge_forward(meta, tokens, att, weights, gain, bias, u):
    half = att[0].shape[1]
    d = tokens.shape[1]
    return call(
        merge_kernel,
        "merge_forward",
        (1,),
        meta,
        (tokens, *att, *weights, gain, bias),
        [pl.BlockSpec((half, d), lambda i, m: (u * 2 + m[0], 0))]
        + [fixed(192, half)] * 4
        + [fixed(192, d)] * 4
        + [fixed(1, d)] * 2,
        [fixed(half, d), fixed(half, 128), fixed(half, d)],
        [like((half, d), F32), like((half, 128), F32), like((half, d), BF)],
    )


def gelu_pair(v):
    e = jnp.exp2(v * v * (-0.5 * LOG2E))
    t = 1.0 / (1.0 + (0.3275911 * 0.7071067811865476) * jnp.abs(v))
    poly = t * (0.5 * 0.254829592 + t * (0.5 * -0.284496736 + t * (0.5 * 1.421413741 + t * (0.5 * -1.453152027 + t * (0.5 * 1.061405429)))))
    tail = poly * e
    phi_cap = jnp.where(v >= 0, 1.0 - tail, tail)
    return v * phi_cap, phi_cap + v * (e * 0.3989422804014327)


HB = 256


def group_sum(step, per, product, acc, total, sum_ref, low_ref):
    inner = step % per

    @pl.when(inner == 0)
    def _():
        acc[...] = product

    @pl.when(inner > 0)
    def _():
        acc[...] += product

    @pl.when(step == per - 1)
    def _():
        total[...] = acc[...].astype(BF).astype(F32)

    @pl.when(step == 2 * per - 1)
    def _():
        both = total[...] + acc[...].astype(BF).astype(F32)
        sum_ref[...] = both
        low_ref[...] = both.astype(BF)


def up_down_kernel(per, meta_ref, x_ref, ua_ref, ub_ref, da_ref, db_ref, act_ref, slope_ref, sum_ref, low_ref, acc, total):
    step = pl.program_id(0)
    first = step < per
    up = jnp.where(first, ua_ref[...], ub_ref[...])
    down = jnp.where(first, da_ref[...], db_ref[...])
    act, slope = gelu_pair(nn(x_ref[...], up))
    low = act.astype(BF)
    act_ref[...] = low
    slope_ref[...] = slope
    group_sum(step, per, nn(low, down), acc, total, sum_ref, low_ref)


def group_specs(d, per):
    return [
        pl.BlockSpec((d, HB), lambda i, m: (0, jnp.minimum(i, per - 1))),
        pl.BlockSpec((d, HB), lambda i, m: (0, jnp.maximum(i - per, 0))),
        pl.BlockSpec((HB, d), lambda i, m: (jnp.minimum(i, per - 1), 0)),
        pl.BlockSpec((HB, d), lambda i, m: (jnp.maximum(i - per, 0), 0)),
    ]


def up_down(meta, x, up, down):
    rows, d = x.shape
    per = up[0].shape[1] // HB
    return call(
        functools.partial(up_down_kernel, per),
        "up_down",
        (2 * per,),
        meta,
        (x, *up, *down),
        [fixed(rows, d)] + group_specs(d, per),
        [
            pl.BlockSpec((rows, HB), lambda i, m: (0, i)),
            pl.BlockSpec((rows, HB), lambda i, m: (0, i)),
            fixed(rows, d),
            fixed(rows, d),
        ],
        [
            like((rows, 2 * per * HB), BF),
            like((rows, 2 * per * HB), F32),
            like((rows, d), F32),
            like((rows, d), BF),
        ],
        [pltpu.VMEM((rows, d), F32)] * 2,
    )


def outer_kernel(
    meta_ref, xhat_ref, own_ref, far_ref, grad_ref, weight_ref, ig_ref, ib_ref, og_ref, ob_ref,
    out_ref, sum_grad_ref, low_ref, small_ref,
):
    branch = own_ref[...] + far_ref[...].astype(F32)
    normed = xhat_ref[...] * ig_ref[...] + ib_ref[...]
    xhat, rstd = normalise(normed + branch)
    out_ref[...] = (xhat * og_ref[...] + ob_ref[...]).astype(BF)
    cot = grad_ref[...].astype(F32) * weight_ref[...]
    small_ref[0:1, :] = jnp.sum(cot * xhat, axis=0, keepdims=True)
    small_ref[1:2, :] = jnp.sum(cot, axis=0, keepdims=True)
    gy = cot * og_ref[...]
    mean_gy = jnp.mean(gy, axis=-1, keepdims=True)
    mean_gx = jnp.mean(gy * xhat, axis=-1, keepdims=True)
    sum_grad = rstd * (gy - mean_gy - xhat * mean_gx)
    sum_grad_ref[...] = sum_grad
    low_ref[...] = sum_grad.astype(BF)


def outer_norm(meta, xhat, own, far, grad, weight, vectors, u):
    rows, d = xhat.shape
    return call(
        outer_kernel,
        "outer_norm",
        (1,),
        meta,
        (xhat, own, far, grad, weight, *vectors),
        [fixed(rows, d)] * 3
        + [pl.BlockSpec((rows, d), lambda i, m: (u * 2 + m[0], 0)), pl.BlockSpec((rows, 1), lambda i, m: (u * 2 + m[0], 0))]
        + [fixed(1, d)] * 4,
        [fixed(rows, d), fixed(rows, d), fixed(rows, d), fixed(2, d)],
        [like((rows, d), BF), like((rows, d), F32), like((rows, d), BF), like((2, d), F32)],
    )


def ffn_back_kernel(per, meta_ref, g_ref, ua_ref, ub_ref, da_ref, db_ref, slope_ref, pre_ref, sum_ref, low_ref, acc, total):
    step = pl.program_id(0)
    first = step < per
    up = jnp.where(first, ua_ref[...], ub_ref[...])
    down = jnp.where(first, da_ref[...], db_ref[...])
    low = (nt(g_ref[...], down) * slope_ref[...]).astype(BF)
    pre_ref[...] = low
    group_sum(step, per, nt(low, up), acc, total, sum_ref, low_ref)


def ffn_back(meta, g, up, down, slope):
    rows, d = g.shape
    per = up[0].shape[1] // HB
    return call(
        functools.partial(ffn_back_kernel, per),
        "ffn_back",
        (2 * per,),
        meta,
        (g, *up, *down, slope),
        [fixed(rows, d)] + group_specs(d, per) + [pl.BlockSpec((rows, HB), lambda i, m: (0, i))],
        [pl.BlockSpec((rows, HB), lambda i, m: (0, i)), fixed(rows, d), fixed(rows, d)],
        [like((rows, 2 * per * HB), BF), like((rows, d), F32), like((rows, d), BF)],
        [pltpu.VMEM((rows, d), F32)] * 2,
    )


def weight_kernel(seqs, meta_ref, *refs):
    acts, pres, gs, xs = (refs[i * seqs : (i + 1) * seqs] for i in range(4))
    dup_ref, ddown_ref = refs[4 * seqs :]
    dup_ref[...] = sum(tn(x[...], pre[...]) for x, pre in zip(xs, pres)).astype(BF)
    ddown_ref[...] = sum(tn(act[...], g[...]) for act, g in zip(acts, gs)).astype(BF)


def weight_grads(meta, acts, pres, gs, xs, group):
    seqs = len(acts)
    rows, d = xs[0].shape
    hidden = acts[0].shape[1] // 2
    per = hidden // HB
    block = pl.BlockSpec((rows, HB), lambda i, m: (0, group * per + i))
    return call(
        functools.partial(weight_kernel, seqs),
        "weight_grads",
        (per,),
        meta,
        (*acts, *pres, *gs, *xs),
        [block] * (2 * seqs) + [fixed(rows, d)] * (2 * seqs),
        [pl.BlockSpec((d, HB), lambda i, m: (0, i)), pl.BlockSpec((HB, d), lambda i, m: (i, 0))],
        [like((d, hidden), BF), like((hidden, d), BF)],
    )


def inner_kernel(meta_ref, sum_grad_ref, own_ref, far_ref, xhat_ref, rstd_ref, gain_ref, a0, a1, w0, w1, *refs):
    last = len(refs) == 11
    out_ref, g0, g1, m0, m1, small_ref = refs[-6:]
    grad = sum_grad_ref[...] + (own_ref[...] + far_ref[...].astype(F32))
    xhat = xhat_ref[...]
    gain_grad = jnp.sum(grad * xhat, axis=0, keepdims=True)
    bias_grad = jnp.sum(grad, axis=0, keepdims=True)
    gy = grad * gain_ref[...]
    mean_gy = jnp.mean(gy, axis=-1, keepdims=True)
    mean_gx = jnp.mean(gy * xhat, axis=-1, keepdims=True)
    inner = rstd_ref[:, 0:1] * (gy - mean_gy - xhat * mean_gx)
    out_ref[...] = inner
    low = inner.astype(BF)
    g0[...] = nt(w0[...], low).astype(BF)
    g1[...] = nt(w1[...], low).astype(BF)
    small = jnp.concatenate([gain_grad, bias_grad], axis=0)
    small_ref[...] = small
    if last:
        before0, before1, before_small, outer0, outer1 = refs[:5]
        below = jnp.concatenate(
            [small + before_small[...], outer0[...] + outer1[...], jnp.zeros((60, small.shape[1]), F32)], axis=0
        ).astype(BF)
        for m, a, before in ((m0, a0, before0), (m1, a1, before1)):
            m[:192, :] = (nn(a[...], low) + before[...]).astype(BF)
            m[192:, :] = below
    else:
        m0[...] = nn(a0[...], low)
        m1[...] = nn(a1[...], low)


def inner_norm(meta, sum_grad, own, far, xhat, rstd, gain, att, weights, before):
    rows, d = xhat.shape
    merge = like((256, d), BF) if before else like((192, d), F32)
    return call(
        inner_kernel,
        "inner_norm",
        (1,),
        meta,
        (sum_grad, own, far, xhat, rstd, gain, *att, *weights, *before),
        [fixed(rows, d)] * 4
        + [fixed(rows, 128), fixed(1, d)]
        + [fixed(192, rows)] * 2
        + [fixed(192, d)] * 2
        + ([fixed(192, d)] * 2 + [fixed(2, d)] * 3 if before else []),
        [fixed(rows, d), fixed(192, rows), fixed(192, rows), fixed(*merge.shape), fixed(*merge.shape), fixed(2, d)],
        [like((rows, d), F32), like((192, rows), BF), like((192, rows), BF), merge, merge, like((2, d), F32)],
    )


def local(groups, tokens, lengths, span_starts, wq, wk, wv, wm, wu, wd, ig, ib, og, ob, out_grad):
    rows, d = tokens.shape
    seqs = lengths.shape[0]
    frames = rows // seqs
    half = frames // 2
    core = lax.axis_index("tensor") % 2
    place_dp = lax.axis_index("dp")
    bits = groups.bit_length() - 1

    def swap(value, k):
        return lax.ppermute(value, "tensor", [(i, i ^ k) for i in range(4)])

    def swap_dp(value, k):
        return lax.ppermute(value, "dp", [(i, i ^ k) for i in range(groups)])

    def add(a, b):
        return (a.astype(F32) + b.astype(F32)).astype(BF)

    def cut(array, index, count):
        size = array.shape[0] // count
        return lax.dynamic_slice_in_dim(array, index * size, size, 0)

    def sum_over(array, stages):
        spots = []
        for low_bit, width in stages:
            count = 1 << width
            spot = (place_dp >> low_bit) & (count - 1)
            total = cut(array, spot, count).astype(F32)
            for j in range(1, count):
                total = total + swap_dp(cut(array, spot ^ j, count), j << low_bit).astype(F32)
            array = total.astype(BF)
            spots.append((spot, low_bit, count))
        for spot, low_bit, count in reversed(spots):
            pieces = [array] + [swap_dp(array, j << low_bit) for j in range(1, count)]
            size = array.shape[0]
            whole = jnp.zeros((size * count, d), BF)
            for j in range(count):
                whole = lax.dynamic_update_slice_in_dim(whole, pieces[j], (spot ^ j) * size, 0)
            array = whole
        return array

    metas = [jnp.stack([core, lengths[u]]) for u in range(seqs)]
    token = []

    def meta(u):
        value = metas[u]
        return lax.optimization_barrier((value, token[-1]))[0] if token else value

    def done(results):
        token.append(results[-1])
        return results

    merge_w = (wm, swap(wm, 1), swap(wm, 2), swap(wm, 3))
    up_w = (wu, swap(wu, 1))
    down_w = (wd, swap(wd, 1))
    positions = jnp.arange(frames)
    inside = (positions[None, None, :] >= span_starts[:, :, None]) & (
        positions[None, None, :] < span_starts[:, :, None] + SPAN
    )
    weight = jnp.any(inside, axis=1).astype(F32).reshape(rows, 1)
    ig, ib, og, ob = (vec.reshape(1, d) for vec in (ig, ib, og, ob))

    q, k, v = project(tokens, wq, wk, wv)
    fwd, att = [], []
    for u in range(seqs):
        fwd.append(done(attend_forward(meta(u), q, k, v, u, frames)))
        own, other = fwd[u][:2]
        att.append((own, swap(other, 1), swap(own, 2), swap(other, 3)))
    merged, ffn, far = [], [], []
    for u in range(seqs):
        merged.append(done(merge_forward(meta(u), tokens, att[u], merge_w, ig, ib, u)))
        ffn.append(done(up_down(meta(u), merged[u][2], up_w, down_w)))
        far.append(swap(ffn[u][3], 2))
    outer, back, far_grad = [], [], []
    for u in range(seqs):
        outer.append(done(outer_norm(meta(u), merged[u][0], ffn[u][2], far[u], out_grad, weight, (ig, ib, og, ob), u)))
        back.append(done(ffn_back(meta(u), outer[u][2], up_w, down_w, ffn[u][1])))
        far_grad.append(swap(back[u][2], 2))
    out_rows = jnp.stack([outer[u][0] for u in range(seqs)])
    out_other = swap(out_rows, 1)

    four = ([f[0] for f in ffn], [b[0] for b in back], [o[2] for o in outer], [m[2] for m in merged])
    up_other, down_other = done(weight_grads(meta(0), *four, 1))
    up_got, down_got = swap(up_other, 1), swap(down_other, 1)
    up_own, down_own = done(weight_grads(meta(0), *four, 0))
    up_sum = add(up_own, up_got)
    down_sum = add(down_own, down_got)
    up_sum = lax.psum(up_sum, "dp")

    inner, entry, before = [], [], ()
    total = ()
    for u in range(seqs):
        if u == seqs - 1:
            before = (inner[0][3], inner[0][4], inner[0][5], outer[0][3], outer[1][3])
        inner.append(
            done(inner_norm(meta(u), outer[u][1], back[u][1], far_grad[u], merged[u][0], merged[u][1], ig, att[u][:2], merge_w[:2], before))
        )
        other = swap(inner[u][2], 1)
        grads = done(attend_backward(meta(u), q, k, v, inner[u][1], other, fwd[u][2], fwd[u][3], u, frames))
        last = u == seqs - 1
        entry.append(done(entry_back(meta(u), tokens, grads, (wq, wk, wv), total, u, frames, BF if last else F32)))
        total = (entry[u][2],)
    merge_sum = add(inner[-1][3], swap(inner[-1][4], 1))
    rest = [(b, 2) for b in range(1, bits - 1, 2)] + ([(bits - 1, 1)] if bits % 2 == 0 else [])
    stages = [(0, 1)] + rest
    first = jnp.concatenate([down_sum, merge_sum], axis=0)
    first_sum = sum_over(first, stages)
    qkv_sum = sum_over(total[0], stages)

    ready = []
    for u in range(seqs):
        near = entry[u][1].astype(F32) + swap(entry[u][0], 1).astype(F32)
        ready.append((inner[u][0] + (near + swap(near.astype(BF), 2).astype(F32))).astype(BF))
    ready = jnp.stack(ready)
    layer_output = place(metas[0], out_rows, out_other)
    input_grad = place(metas[0], ready, swap(ready, 1))

    query_grad, key_grad, value_grad = finish(qkv_sum)
    hidden = down_sum.shape[0]
    small = first_sum[hidden + 192 : hidden + 196].astype(F32)
    return (
        layer_output,
        input_grad,
        query_grad,
        key_grad,
        value_grad,
        first_sum[hidden : hidden + 192].astype(F32),
        up_sum.astype(F32),
        first_sum[:hidden].astype(F32),
        small[0],
        small[1],
        small[2],
        small[3],
    )


def solution(mesh):
    in_specs = (
        P("dp", None),
        P("dp"),
        P("dp", None),
        P(None, "tensor"),
        P(None, "tensor"),
        P(None, "tensor"),
        P("tensor", None),
        P(None, "tensor"),
        P("tensor", None),
        P(),
        P(),
        P(),
        P(),
        P("dp", None),
    )
    out_specs = (
        P("dp", None),
        P("dp", None),
        P(None, "tensor"),
        P(None, "tensor"),
        P(None, "tensor"),
        P("tensor", None),
        P(None, "tensor"),
        P("tensor", None),
        P(),
        P(),
        P(),
        P(),
    )
    body = functools.partial(local, mesh.shape["dp"])
    return jax.shard_map(body, mesh=mesh, in_specs=in_specs, out_specs=out_specs, check_vma=False)
```

```python
import functools

import jax
import jax.numpy as jnp
from jax import lax
from jax.experimental import pallas as pl
from jax.experimental.pallas import tpu as pltpu
from jax.sharding import PartitionSpec as P

HEAD_DIM = 64
SPAN = 10
EPS = 1e-05
LOG2E = 1.4426950408889634
KB = 256
VMEM = 16
RB = 128
HB = 256
BF = jnp.bfloat16
F32 = jnp.float32
MIB = 1 << 20


def nn(a, b):
    return lax.dot_general(a, b, (((1,), (0,)), ((), ())), preferred_element_type=F32)


def nt(a, b):
    return lax.dot_general(a, b, (((1,), (1,)), ((), ())), preferred_element_type=F32)


def tn(a, b):
    return lax.dot_general(a, b, (((0,), (0,)), ((), ())), preferred_element_type=F32)


def params(limit):
    return pltpu.CompilerParams(vmem_limit_bytes=limit * MIB)


def cost(flops):
    return pl.CostEstimate(flops=flops, bytes_accessed=1024, transcendentals=0)


def project_kernel(x_ref, wq_ref, wk_ref, wv_ref, q_ref, k_ref, v_ref):
    x = x_ref[...]
    for w_ref, o_ref in ((wq_ref, q_ref), (wk_ref, k_ref), (wv_ref, v_ref)):
        o_ref[:, :192] = nt(x, w_ref[...]).astype(BF)
        o_ref[:, 192:] = jnp.zeros((x.shape[0], HEAD_DIM), BF)


def project(tokens, wq, wk, wv):
    rows, d = tokens.shape
    block = 512
    return pl.pallas_call(
        project_kernel,
        grid=(rows // block,),
        in_specs=[pl.BlockSpec((block, d), lambda i: (i, 0))]
        + [pl.BlockSpec((192, d), lambda i: (0, 0))] * 3,
        out_specs=[pl.BlockSpec((block, 256), lambda i: (i, 0))] * 3,
        out_shape=[jax.ShapeDtypeStruct((rows, 256), BF)] * 3,
        compiler_params=params(VMEM),
        cost_estimate=cost(1000),
        name="project",
    )(tokens, wq, wk, wv)


def lane_parts(block):
    left = block[:, :128]
    lane = lax.broadcasted_iota(jnp.int32, left.shape, 1)
    zero = jnp.zeros_like(left)
    return (
        jnp.where(lane < HEAD_DIM, left, zero),
        jnp.where(lane >= HEAD_DIM, left, zero),
        block[:, 128:],
    )


TILE = (0, 0, 1)


def call(kernel, name, grid, meta, args, in_specs, out_specs, out_shape, scratch=(), limit=VMEM):
    return pl.pallas_call(
        kernel,
        grid_spec=pltpu.PrefetchScalarGridSpec(
            num_scalar_prefetch=1,
            grid=grid,
            in_specs=in_specs,
            out_specs=out_specs,
            scratch_shapes=scratch,
        ),
        out_shape=out_shape,
        compiler_params=params(limit),
        cost_estimate=cost(1000),
        name=name,
    )(meta, *args)


def fixed(*shape):
    return pl.BlockSpec(shape, lambda *_: (0,) * len(shape))


def like(shape, dtype):
    return jax.ShapeDtypeStruct(shape, dtype)


def forward_kernel(u, meta_ref, q_ref, k_ref, v_ref, own_ref, other_ref, o32_ref, lse_ref, s_ref):
    length = meta_ref[1 + u]
    step = pl.program_id(0)
    blocks = lax.div(length + KB - 1, KB)
    parts = lane_parts(q_ref[...] * jnp.asarray(0.125, BF))
    width = q_ref.shape[0]

    def first(kb, highest):
        start = pl.multiple_of(kb * KB, KB)
        rows = pl.ds(start, KB)
        live = start + lax.broadcasted_iota(jnp.int32, (KB, width), 0) < length
        out = []
        for h in range(3):
            tile = pl.ds(128 * TILE[h], 128)
            s = nt(k_ref[rows, tile], parts[h])
            s = jnp.where(live, s, -1e30)
            s_ref[h, rows, :] = s
            out.append(jnp.maximum(highest[h], jnp.max(s, axis=0, keepdims=True)))
        return tuple(out)

    floor = jnp.full((1, width), -1e30, F32)
    highest = lax.fori_loop(0, blocks, first, (floor,) * 3)

    def second(kb, carry):
        rows = pl.ds(pl.multiple_of(kb * KB, KB), KB)
        out = []
        for h in range(3):
            total, result = carry[h]
            p = jnp.exp2((s_ref[h, rows, :] - highest[h]) * LOG2E)
            total = total + jnp.sum(p, axis=0, keepdims=True)
            v = v_ref[rows, pl.ds(128 * TILE[h], 128)]
            result = result + tn(v, p.astype(BF))
            out.append((total, result))
        return tuple(out)

    init = ((jnp.zeros((1, width), F32), jnp.zeros((128, width), F32)),) * 3
    done = lax.fori_loop(0, blocks, second, init)
    outs = []
    for h in range(3):
        total, result = done[h]
        lo = HEAD_DIM * (h % 2)
        o = result[lo : lo + HEAD_DIM] / total
        o32_ref[0, pl.ds(h * HEAD_DIM, HEAD_DIM), :] = o
        lse_ref[0, pl.ds(h, 1), :] = highest[h] * LOG2E + jnp.log2(total)
        outs.append(o.astype(BF))
    whole = jnp.concatenate(outs, axis=0)
    for j, o_ref in enumerate((own_ref, other_ref)):

        @pl.when(step == j)
        def _():
            o_ref[...] = whole


def attend_forward(meta, q, k, v, u, frames):
    half = frames // 2
    return call(
        functools.partial(forward_kernel, u),
        "attend_forward",
        (2,),
        meta,
        (q, k, v),
        [
            pl.BlockSpec((half, 256), lambda i, m: (u * 2 + (i ^ m[0]), 0)),
            pl.BlockSpec((frames, 256), lambda i, m: (u, 0)),
            pl.BlockSpec((frames, 256), lambda i, m: (u, 0)),
        ],
        [
            fixed(192, half),
            fixed(192, half),
            pl.BlockSpec((1, 192, half), lambda i, m: (i, 0, 0)),
            pl.BlockSpec((1, 8, half), lambda i, m: (i, 0, 0)),
        ],
        [
            like((192, half), BF),
            like((192, half), BF),
            like((2, 192, half), F32),
            like((2, 8, half), F32),
        ],
        [pltpu.VMEM((3, frames, half), F32)],
    )


def backward_kernel(
    u, meta_ref, q_ref, k_ref, v_ref, d0_ref, d1_ref, o32_ref, lse_ref,
    dq_ref, dk_ref, dv_ref, kt_ref, dk_acc, dv_acc, do_ref,
):
    length = meta_ref[1 + u]
    blocks = lax.div(length + KB - 1, KB)
    step = pl.program_id(0)

    @pl.when(step == 0)
    def _():
        dk_acc[...] = jnp.zeros_like(dk_acc)
        dv_acc[...] = jnp.zeros_like(dv_acc)
        kt_ref[...] = jnp.transpose(k_ref[...])
        do_ref[...] = d0_ref[...]

    @pl.when(step == 1)
    def _():
        do_ref[...] = d1_ref[...]

    parts = lane_parts(q_ref[...] * jnp.asarray(0.125, BF))
    width = q_ref.shape[0]
    empty = jnp.zeros((HEAD_DIM, width), BF)
    head = [do_ref[pl.ds(h * HEAD_DIM, HEAD_DIM), :] for h in range(3)]
    grads = (
        jnp.concatenate([head[0], empty], axis=0),
        jnp.concatenate([empty, head[1]], axis=0),
        jnp.concatenate([head[2], empty], axis=0),
    )
    delta = [
        jnp.sum(
            head[h].astype(F32) * o32_ref[0, pl.ds(h * HEAD_DIM, HEAD_DIM), :], axis=0, keepdims=True
        )
        for h in range(3)
    ]
    lse = [lse_ref[0, pl.ds(h, 1), :] for h in range(3)]

    def body(kb, carry):
        start = pl.multiple_of(kb * KB, KB)
        rows = pl.ds(start, KB)
        live = start + lax.broadcasted_iota(jnp.int32, (KB, width), 0) < length
        out = []
        for h in range(3):
            tile = pl.ds(128 * TILE[h], 128)
            s = nt(k_ref[rows, tile], parts[h])
            s = jnp.where(live, s, -1e30)
            p = jnp.exp2(s * LOG2E - lse[h])
            dp = nn(v_ref[rows, tile], grads[h])
            ds = (p * (dp - delta[h])).astype(BF)
            dv_acc[rows, tile] += nt(p.astype(BF), grads[h])
            dk_acc[rows, tile] += nn(ds, parts[h])
            kt = kt_ref[pl.ds(h * HEAD_DIM, HEAD_DIM), rows]
            out.append(carry[h] + nn(kt, ds))
        return tuple(out)

    zero = jnp.zeros((HEAD_DIM, width), F32)
    done = lax.fori_loop(0, blocks, body, (zero,) * 3)
    full = jnp.concatenate(done + (zero,), axis=0) * 0.125
    dq_ref[...] = jnp.transpose(full).astype(BF)

    @pl.when(step == 1)
    def _():
        dk_ref[...] = dk_acc[...].astype(BF)
        dv_ref[...] = dv_acc[...].astype(BF)


def attend_backward(meta, q, k, v, own, other, o32, lse, u, frames):
    half = frames // 2
    return call(
        functools.partial(backward_kernel, u),
        "attend_backward",
        (2,),
        meta,
        (q, k, v, own, other, o32, lse),
        [
            pl.BlockSpec((half, 256), lambda i, m: (u * 2 + (i ^ m[0]), 0)),
            pl.BlockSpec((frames, 256), lambda i, m: (u, 0)),
            pl.BlockSpec((frames, 256), lambda i, m: (u, 0)),
            fixed(192, half),
            fixed(192, half),
            pl.BlockSpec((1, 192, half), lambda i, m: (i, 0, 0)),
            pl.BlockSpec((1, 8, half), lambda i, m: (i, 0, 0)),
        ],
        [
            pl.BlockSpec((half, 256), lambda i, m: (i ^ m[0], 0)),
            fixed(frames, 256),
            fixed(frames, 256),
        ],
        [like((frames, 256), BF)] * 3,
        [
            pltpu.VMEM((256, frames), BF),
            pltpu.VMEM((frames, 256), F32),
            pltpu.VMEM((frames, 256), F32),
            pltpu.VMEM((192, half), BF),
        ],
    )


def entry_kernel(meta_ref, x_ref, dq_ref, dk_ref, dv_ref, wq_ref, wk_ref, wv_ref, *refs):
    before_ref = refs[0] if len(refs) == 5 else None
    send_ref, keep_ref, sum_ref, acc = refs[-4:]
    step = pl.program_id(0)
    x = x_ref[...]
    total = jnp.zeros(x.shape, F32)
    for i, (g_ref, w_ref) in enumerate(((dq_ref, wq_ref), (dk_ref, wk_ref), (dv_ref, wv_ref))):
        rows = pl.ds(192 * i, 192)
        g = g_ref[:, :192]
        total = total + nn(g, w_ref[...])
        product = tn(g, x)

        @pl.when(step == 0)
        def _():
            acc[rows, :] = product if before_ref is None else product + before_ref[rows, :]

        @pl.when(step == 1)
        def _():
            sum_ref[rows, :] = (product + acc[rows, :]).astype(sum_ref.dtype)

    low = total.astype(BF)

    @pl.when(step == 0)
    def _():
        send_ref[...] = low

    @pl.when(step == 1)
    def _():
        keep_ref[...] = low


def entry_back(meta, tokens, grads, weights, before, u, frames, dtype):
    half = frames // 2
    d = tokens.shape[1]
    return call(
        entry_kernel,
        "entry_back",
        (2,),
        meta,
        (tokens, *grads, *weights, *before),
        [pl.BlockSpec((half, d), lambda i, m: (u * 2 + (1 - i ^ m[0]), 0))]
        + [pl.BlockSpec((half, 256), lambda i, m: (1 - i ^ m[0], 0))] * 3
        + [fixed(192, d)] * 3
        + [fixed(576, d)] * len(before),
        [fixed(half, d), fixed(half, d), fixed(576, d)],
        [like((half, d), BF), like((half, d), BF), like((576, d), dtype)],
        [pltpu.VMEM((576, d), F32)],
    )


def place_kernel(meta_ref, own_ref, other_ref, o_ref):
    for j, r_ref in enumerate((own_ref, other_ref)):

        @pl.when(pl.program_id(1) == j)
        def _():
            o_ref[...] = r_ref[0]


def place(meta, own, other):
    seqs, half, d = own.shape
    return call(
        place_kernel,
        "place",
        (seqs, 2),
        meta,
        (own, other),
        [pl.BlockSpec((1, half, d), lambda u, j, m: (u, 0, 0))] * 2,
        pl.BlockSpec((half, d), lambda u, j, m: (u * 2 + (j ^ m[0]), 0)),
        like((seqs * 2 * half, d), own.dtype),
    )


def normalise(values):
    average = jnp.mean(values, axis=-1, keepdims=True)
    centred = values - average
    spread = jnp.mean(centred * centred, axis=-1, keepdims=True)
    rstd = lax.rsqrt(spread + EPS)
    return centred * rstd, rstd


def gelu_pair(v):
    e = jnp.exp2(v * v * (-0.5 * LOG2E))
    t = 1.0 / (1.0 + (0.3275911 * 0.7071067811865476) * jnp.abs(v))
    poly = t * (0.5 * 0.254829592 + t * (0.5 * -0.284496736 + t * (0.5 * 1.421413741 + t * (0.5 * -1.453152027 + t * (0.5 * 1.061405429)))))
    tail = poly * e
    phi_cap = jnp.where(v >= 0, 1.0 - tail, tail)
    return v * phi_cap, phi_cap + v * (e * 0.3989422804014327)


def ahead_kernel(
    meta_ref, tok_ref, a0, a1, a2, a3, w0, w1, w2, w3, ua_ref, ub_ref, da_ref, db_ref, vec_ref,
    xhat_ref, rstd_ref, low_ref, act_ref, slope_ref, own_ref, sent_ref,
):
    gain, bias = vec_ref[0:1, :], vec_ref[1:2, :]
    hidden = ua_ref.shape[1]
    for r in range(tok_ref.shape[0] // RB):
        rows = pl.ds(r * RB, RB)
        branch = jnp.zeros((RB, tok_ref.shape[1]), F32)
        for a, w in ((a0, w0), (a1, w1), (a2, w2), (a3, w3)):
            branch = branch + tn(a[:, rows], w[...]).astype(BF).astype(F32)
        xhat, rstd = normalise(tok_ref[rows, :].astype(F32) + branch)
        xhat_ref[rows, :] = xhat
        rstd_ref[rows, :] = jnp.broadcast_to(rstd, (RB, rstd_ref.shape[1]))
        normed = xhat * gain + bias
        low = normed.astype(BF)
        low_ref[rows, :] = low
        sent = jnp.zeros(normed.shape, F32)
        for g, (up, down) in enumerate(((ua_ref, da_ref), (ub_ref, db_ref))):
            acts = []
            for c in range(hidden // HB):
                act, slope = gelu_pair(nn(low, up[:, c * HB : (c + 1) * HB]))
                columns = pl.ds(g * hidden + c * HB, HB)
                acts.append(act.astype(BF))
                act_ref[rows, columns] = acts[-1]
                slope_ref[rows, columns] = slope.astype(BF)
            sent = sent + nn(jnp.concatenate(acts, axis=1), down[...]).astype(BF).astype(F32)
        own_ref[rows, :] = normed + sent
        sent_ref[rows, :] = sent.astype(BF)


def ahead(meta, tokens, att, merge_w, up, down, vectors, u):
    half = att[0].shape[1]
    d, hidden = up[0].shape
    return call(
        ahead_kernel,
        "ahead",
        (1,),
        meta,
        (tokens, *att, *merge_w, *up, *down, vectors),
        [pl.BlockSpec((half, d), lambda i, m: (u * 2 + m[0], 0))]
        + [fixed(192, half)] * 4
        + [fixed(192, d)] * 4
        + [fixed(d, hidden)] * 2
        + [fixed(hidden, d)] * 2
        + [fixed(4, d)],
        [fixed(half, d), fixed(half, 128), fixed(half, d), fixed(half, 2 * hidden), fixed(half, 2 * hidden), fixed(half, d), fixed(half, d)],
        [
            like((half, d), F32),
            like((half, 128), F32),
            like((half, d), BF),
            like((half, 2 * hidden), BF),
            like((half, 2 * hidden), BF),
            like((half, d), F32),
            like((half, d), BF),
        ],
    )


def astern_kernel(seqs, u, meta_ref, own_ref, far_ref, grad_ref, span_ref, ua_ref, ub_ref, da_ref, db_ref, slope_ref, vec_ref, *refs):
    last = u == seqs - 1
    before = refs[: 4 * seqs - 2] if last else ()
    out_ref, g_ref, pre_ref, back_ref, sent_ref, small_ref = refs[len(before) : len(before) + 6]
    gain, bias = vec_ref[2:3, :], vec_ref[3:4, :]
    half, d = own_ref.shape
    hidden = ua_ref.shape[1]
    starts = span_ref[u : u + 1, :]
    gain_grad = jnp.zeros(gain.shape, F32)
    bias_grad = jnp.zeros(gain.shape, F32)
    for r in range(half // RB):
        rows = pl.ds(r * RB, RB)
        xhat, rstd = normalise(own_ref[rows, :] + far_ref[rows, :].astype(F32))
        out_ref[rows, :] = (xhat * gain + bias).astype(BF)
        frame = meta_ref[0] * half + r * RB + lax.broadcasted_iota(jnp.int32, (RB, starts.shape[1]), 0)
        inside = (frame >= starts) & (frame < starts + SPAN)
        weight = jnp.max(jnp.where(inside, 1.0, 0.0), axis=1, keepdims=True)
        cot = grad_ref[rows, :].astype(F32) * weight
        gain_grad = gain_grad + jnp.sum(cot * xhat, axis=0, keepdims=True)
        bias_grad = bias_grad + jnp.sum(cot, axis=0, keepdims=True)
        gy = cot * gain
        mean_gy = jnp.mean(gy, axis=-1, keepdims=True)
        mean_gx = jnp.mean(gy * xhat, axis=-1, keepdims=True)
        sum_grad = rstd * (gy - mean_gy - xhat * mean_gx)
        low = sum_grad.astype(BF)
        g_ref[rows, :] = low
        sent = jnp.zeros(sum_grad.shape, F32)
        for g, (up, down) in enumerate(((ua_ref, da_ref), (ub_ref, db_ref))):
            pres = []
            for c in range(hidden // HB):
                columns = pl.ds(g * hidden + c * HB, HB)
                slope = slope_ref[rows, columns].astype(F32)
                pres.append((nt(low, down[c * HB : (c + 1) * HB, :]) * slope).astype(BF))
                pre_ref[rows, columns] = pres[-1]
            sent = sent + nt(jnp.concatenate(pres, axis=1), up[...]).astype(BF).astype(F32)
        back_ref[rows, :] = sum_grad + sent
        sent_ref[rows, :] = sent.astype(BF)
    small_ref[0:1, :] = gain_grad
    small_ref[1:2, :] = bias_grad
    if last:
        acts, xs = before[:seqs], before[seqs : 2 * seqs]
        pres = (*before[2 * seqs : 3 * seqs - 1], pre_ref)
        gs = (*before[3 * seqs - 1 :], g_ref)
        dups, ddowns = refs[-4:-2], refs[-2:]
        for g in range(2):
            for c in range(hidden // HB):
                columns = pl.ds(g * hidden + c * HB, HB)
                block = pl.ds(c * HB, HB)
                dups[g][:, block] = sum(tn(x[...], p[:, columns]) for x, p in zip(xs, pres)).astype(BF)
                ddowns[g][block, :] = sum(tn(a[:, columns], h[...]) for a, h in zip(acts, gs)).astype(BF)


def astern(meta, own, far, grad, spans, up, down, slope, vectors, u, seqs, before):
    half, d = own.shape
    hidden = up[0].shape[1]
    rows = fixed(half, d)
    wide = fixed(half, 2 * hidden)
    extra = [] if not before else [wide] * seqs + [rows] * seqs + [wide] * (seqs - 1) + [rows] * (seqs - 1)
    grads = [] if not before else [(d, hidden)] * 2 + [(hidden, d)] * 2
    return call(
        functools.partial(astern_kernel, seqs, u),
        "astern",
        (1,),
        meta,
        (own, far, grad, spans, *up, *down, slope, vectors, *before),
        [rows] * 2
        + [pl.BlockSpec((half, d), lambda i, m: (u * 2 + m[0], 0)), fixed(*spans.shape)]
        + [fixed(d, hidden)] * 2
        + [fixed(hidden, d)] * 2
        + [wide, fixed(4, d)]
        + extra,
        [rows, rows, wide, rows, rows, fixed(2, d)] + [fixed(*shape) for shape in grads],
        [
            like((half, d), BF),
            like((half, d), BF),
            like((half, 2 * hidden), BF),
            like((half, d), F32),
            like((half, d), BF),
            like((2, d), F32),
        ]
        + [like(shape, BF) for shape in grads],
        limit=32 if before else VMEM,
    )


def inner_kernel(meta_ref, own_ref, far_ref, xhat_ref, rstd_ref, vec_ref, a0, a1, w0, w1, *refs):
    last = len(refs) == 11
    out_ref, g0, g1, m0, m1, small_ref = refs[-6:]
    grad = own_ref[...] + far_ref[...].astype(F32)
    xhat = xhat_ref[...]
    gain_grad = jnp.sum(grad * xhat, axis=0, keepdims=True)
    bias_grad = jnp.sum(grad, axis=0, keepdims=True)
    gy = grad * vec_ref[0:1, :]
    mean_gy = jnp.mean(gy, axis=-1, keepdims=True)
    mean_gx = jnp.mean(gy * xhat, axis=-1, keepdims=True)
    inner = rstd_ref[:, 0:1] * (gy - mean_gy - xhat * mean_gx)
    out_ref[...] = inner
    low = inner.astype(BF)
    g0[...] = nt(w0[...], low).astype(BF)
    g1[...] = nt(w1[...], low).astype(BF)
    small = jnp.concatenate([gain_grad, bias_grad], axis=0)
    small_ref[...] = small
    if last:
        before0, before1, before_small, outer0, outer1 = refs[:5]
        below = jnp.concatenate(
            [small + before_small[...], outer0[...] + outer1[...], jnp.zeros((60, small.shape[1]), F32)], axis=0
        ).astype(BF)
        for m, a, before in ((m0, a0, before0), (m1, a1, before1)):
            m[:192, :] = (nn(a[...], low) + before[...]).astype(BF)
            m[192:, :] = below
    else:
        m0[...] = nn(a0[...], low)
        m1[...] = nn(a1[...], low)


def inner_norm(meta, own, far, xhat, rstd, vectors, att, weights, before):
    rows, d = xhat.shape
    merge = like((256, d), BF) if before else like((192, d), F32)
    return call(
        inner_kernel,
        "inner_norm",
        (1,),
        meta,
        (own, far, xhat, rstd, vectors, *att, *weights, *before),
        [fixed(rows, d)] * 3
        + [fixed(rows, 128), fixed(4, d)]
        + [fixed(192, rows)] * 2
        + [fixed(192, d)] * 2
        + ([fixed(192, d)] * 2 + [fixed(2, d)] * 3 if before else []),
        [fixed(rows, d), fixed(192, rows), fixed(192, rows), fixed(*merge.shape), fixed(*merge.shape), fixed(2, d)],
        [like((rows, d), F32), like((192, rows), BF), like((192, rows), BF), merge, merge, like((2, d), F32)],
    )


def local(groups, tokens, lengths, span_starts, wq, wk, wv, wm, wu, wd, ig, ib, og, ob, out_grad):
    rows, d = tokens.shape
    seqs = lengths.shape[0]
    frames = rows // seqs
    half = frames // 2
    core = lax.axis_index("tensor") % 2
    place_dp = lax.axis_index("dp")
    bits = groups.bit_length() - 1

    def swap(value, k):
        return lax.ppermute(value, "tensor", [(i, i ^ k) for i in range(4)])

    def swap_dp(value, k):
        return lax.ppermute(value, "dp", [(i, i ^ k) for i in range(groups)])

    def add(a, b):
        return (a.astype(F32) + b.astype(F32)).astype(BF)

    def cut(array, index, count):
        size = array.shape[0] // count
        return lax.dynamic_slice_in_dim(array, index * size, size, 0)

    def pieces_of(array, stage):
        low_bit, width = stage
        count = 1 << width
        spot = (place_dp >> low_bit) & (count - 1)
        got = [swap_dp(cut(array, spot ^ j, count), j << low_bit) for j in range(1, count)]
        return [cut(array, spot, count)] + got

    def add_up(pieces):
        return sum(piece.astype(F32) for piece in pieces).astype(BF)

    def scatter(array, stage):
        return add_up(pieces_of(array, stage))

    def collect(array, stage):
        low_bit, width = stage
        count = 1 << width
        spot = (place_dp >> low_bit) & (count - 1)
        size = array.shape[0]
        whole = jnp.zeros((size * count, d), BF)
        pieces = [array] + [swap_dp(array, j << low_bit) for j in range(1, count)]
        for j in range(count):
            whole = lax.dynamic_update_slice_in_dim(whole, pieces[j], (spot ^ j) * size, 0)
        return whole

    scalars = jnp.concatenate([core.reshape(1), lengths])
    token = []

    def meta():
        return lax.optimization_barrier((scalars, *token))[0] if token else scalars

    def done(results, *others):
        token[:] = [results[-1], *others]
        return results

    merge_w = (wm, swap(wm, 1), swap(wm, 2), swap(wm, 3))
    up_w = (wu, swap(wu, 1))
    down_w = (wd, swap(wd, 1))
    vectors = jnp.stack([ig, ib, og, ob])
    qkv_w = (wq.T, wk.T, wv.T)

    q, k, v = project(tokens, *qkv_w)
    fwd, att = [], []
    for u in range(seqs):
        fwd.append(done(attend_forward(meta(), q, k, v, u, frames), *merge_w[1:], up_w[1], down_w[1]))
        own, other = fwd[u][:2]
        att.append((own, swap(other, 1), swap(own, 2), swap(other, 3)))
    front, far = [], []
    for u in range(seqs):
        front.append(done(ahead(meta(), tokens, att[u], merge_w, up_w, down_w, vectors, u)))
        far.append(swap(front[u][6], 2))
    back, far_grad = [], []
    for u in range(seqs):
        before = ()
        if u == seqs - 1:
            before = (*(f[3] for f in front), *(f[2] for f in front), *(b[2] for b in back), *(b[1] for b in back))
        back.append(
            done(astern(meta(), front[u][5], far[u], out_grad, span_starts, up_w, down_w, front[u][4], vectors, u, seqs, before))
        )
        far_grad.append(swap(back[u][4], 2))
    up_own, up_other, down_own, down_other = back[-1][6:]
    up_sum, down_sum = add(up_own, swap(up_other, 1)), add(down_own, swap(down_other, 1))
    token.extend([up_sum, down_sum])
    up_sum, down_sum = lax.psum((up_sum, down_sum), "dp")

    def inner_step(u, before):
        res = done(inner_norm(meta(), back[u][3], far_grad[u], front[u][0], front[u][1], vectors, att[u][:2], merge_w[:2], before))
        return res, (res[1], swap(res[2], 1))

    def attend_step(u, grads):
        return done(attend_backward(meta(), q, k, v, *grads, fwd[u][2], fwd[u][3], u, frames))

    def entry_step(u, grads, before, dtype):
        return done(entry_back(meta(), tokens, grads, qkv_w, before, u, frames, dtype))


    stages = [(0, 1)] + [(b, 2) for b in range(1, bits - 1, 2)] + ([(bits - 1, 1)] if bits % 2 == 0 else [])
    inner, near, crossed, total = [], [], [], ()
    for u in range(seqs):
        last = u == seqs - 1
        if u == 0:
            res, grads = inner_step(0, ())
            inner.append(res)
        dqkv = attend_step(u, grads)
        if not last:
            before = ()
            if u + 1 == seqs - 1:
                before = (inner[0][3], inner[0][4], inner[0][5], back[0][5], back[1][5])
            res, grads = inner_step(u + 1, before)
            inner.append(res)
            if u + 1 == seqs - 1:
                merge_pieces = pieces_of(add(res[3], swap(res[4], 1)), stages[0])
        if last:
            merge_part = add_up(lax.optimization_barrier((*merge_pieces, dqkv[0]))[:-1])
            token.extend(crossed)
        res = entry_step(u, dqkv, total, BF if last else F32)
        total = (res[2],)
        got = swap(res[0], 1)
        near.append(res[1].astype(F32) + got.astype(F32))
        crossed.append(swap(near[u].astype(BF), 2))
        token.append(got)
    back_steps = [(collect, stage) for stage in reversed(stages)]
    steps = [(scatter, stage) for stage in stages] + back_steps
    merge_sum, qkv_sum = merge_part, total[0]
    for ahead_step, step in zip(steps[1:] + [None], steps):
        qkv_sum = step[0](qkv_sum, step[1])
        if ahead_step:
            merge_sum = ahead_step[0](merge_sum, ahead_step[1])
            merge_sum, qkv_sum = lax.optimization_barrier((merge_sum, qkv_sum))

    ready = []
    for u in range(seqs):
        ready.append((inner[u][0] + (near[u] + crossed[u].astype(F32))).astype(BF))
    ready = jnp.stack(ready)
    out_rows = jnp.stack([b[0] for b in back])
    layer_output = place(meta(), out_rows, swap(out_rows, 1))
    input_grad = place(scalars, ready, swap(ready, 1))

    small = merge_sum[192:196].astype(F32)
    query_grad, key_grad, value_grad = (qkv_sum[192 * i : 192 * (i + 1)].astype(F32).T for i in range(3))
    return (
        layer_output,
        input_grad,
        query_grad,
        key_grad,
        value_grad,
        merge_sum[:192].astype(F32),
        up_sum.astype(F32),
        down_sum.astype(F32),
        small[0],
        small[1],
        small[2],
        small[3],
    )


def solution(mesh):
    in_specs = (
        P("dp", None),
        P("dp"),
        P("dp", None),
        P(None, "tensor"),
        P(None, "tensor"),
        P(None, "tensor"),
        P("tensor", None),
        P(None, "tensor"),
        P("tensor", None),
        P(),
        P(),
        P(),
        P(),
        P("dp", None),
    )
    out_specs = (
        P("dp", None),
        P("dp", None),
        P(None, "tensor"),
        P(None, "tensor"),
        P(None, "tensor"),
        P("tensor", None),
        P(None, "tensor"),
        P("tensor", None),
        P(),
        P(),
        P(),
        P(),
    )
    body = functools.partial(local, mesh.shape["dp"])
    return jax.shard_map(body, mesh=mesh, in_specs=in_specs, out_specs=out_specs, check_vma=False)
```

```python
import functools

import jax
import jax.numpy as jnp
from jax import lax
from jax.experimental import pallas as pl
from jax.experimental.pallas import tpu as pltpu
from jax.sharding import PartitionSpec as P

HEAD_DIM = 64
SPAN = 10
EPS = 1e-05
LOG2E = 1.4426950408889634
KB = 256
VMEM = 16
RB = 128
HB = 256
BF = jnp.bfloat16
F32 = jnp.float32
MIB = 1 << 20


def nn(a, b):
    return lax.dot_general(a, b, (((1,), (0,)), ((), ())), preferred_element_type=F32)


def nt(a, b):
    return lax.dot_general(a, b, (((1,), (1,)), ((), ())), preferred_element_type=F32)


def tn(a, b):
    return lax.dot_general(a, b, (((0,), (0,)), ((), ())), preferred_element_type=F32)


def params(limit):
    return pltpu.CompilerParams(vmem_limit_bytes=limit * MIB)


def cost(micros):
    return pl.CostEstimate(flops=int(micros * 1.1e9), bytes_accessed=1024, transcendentals=0)


MICROS = {"attend_forward": 8, "attend_backward": 12, "entry_back": 5, "place": 3, "ahead": 9, "astern": 8, "inner_norm": 3}


def project_kernel(x_ref, wq_ref, wk_ref, wv_ref, q_ref, k_ref, v_ref):
    x = x_ref[...]
    for w_ref, o_ref in ((wq_ref, q_ref), (wk_ref, k_ref), (wv_ref, v_ref)):
        o_ref[:, :192] = nt(x, w_ref[...]).astype(BF)
        o_ref[:, 192:] = jnp.zeros((x.shape[0], HEAD_DIM), BF)


def project(tokens, wq, wk, wv):
    rows, d = tokens.shape
    block = 512
    return pl.pallas_call(
        project_kernel,
        grid=(rows // block,),
        in_specs=[pl.BlockSpec((block, d), lambda i: (i, 0))]
        + [pl.BlockSpec((192, d), lambda i: (0, 0))] * 3,
        out_specs=[pl.BlockSpec((block, 256), lambda i: (i, 0))] * 3,
        out_shape=[jax.ShapeDtypeStruct((rows, 256), BF)] * 3,
        compiler_params=params(VMEM),
        cost_estimate=cost(3),
        name="project",
    )(tokens, wq, wk, wv)


def lane_parts(block):
    left = block[:, :128]
    lane = lax.broadcasted_iota(jnp.int32, left.shape, 1)
    zero = jnp.zeros_like(left)
    return (
        jnp.where(lane < HEAD_DIM, left, zero),
        jnp.where(lane >= HEAD_DIM, left, zero),
        block[:, 128:],
    )


TILE = (0, 0, 1)


def call(kernel, name, grid, meta, args, in_specs, out_specs, out_shape, scratch=(), limit=VMEM):
    return pl.pallas_call(
        kernel,
        grid_spec=pltpu.PrefetchScalarGridSpec(
            num_scalar_prefetch=1,
            grid=grid,
            in_specs=in_specs,
            out_specs=out_specs,
            scratch_shapes=scratch,
        ),
        out_shape=out_shape,
        compiler_params=params(limit),
        cost_estimate=cost(MICROS[name]),
        name=name,
    )(meta, *args)


def fixed(*shape):
    return pl.BlockSpec(shape, lambda *_: (0,) * len(shape))


def like(shape, dtype):
    return jax.ShapeDtypeStruct(shape, dtype)


def forward_kernel(u, meta_ref, q_ref, k_ref, v_ref, own_ref, other_ref, o32_ref, lse_ref, s_ref):
    length = meta_ref[1 + u]
    step = pl.program_id(0)
    blocks = lax.div(length + KB - 1, KB)
    parts = lane_parts(q_ref[...] * jnp.asarray(0.125, BF))
    width = q_ref.shape[0]

    def first(kb, highest):
        start = pl.multiple_of(kb * KB, KB)
        rows = pl.ds(start, KB)
        live = start + lax.broadcasted_iota(jnp.int32, (KB, width), 0) < length
        out = []
        for h in range(3):
            tile = pl.ds(128 * TILE[h], 128)
            s = nt(k_ref[rows, tile], parts[h])
            s = jnp.where(live, s, -1e30)
            s_ref[h, rows, :] = s
            out.append(jnp.maximum(highest[h], jnp.max(s, axis=0, keepdims=True)))
        return tuple(out)

    floor = jnp.full((1, width), -1e30, F32)
    highest = lax.fori_loop(0, blocks, first, (floor,) * 3)

    def second(kb, carry):
        rows = pl.ds(pl.multiple_of(kb * KB, KB), KB)
        out = []
        for h in range(3):
            total, result = carry[h]
            p = jnp.exp2((s_ref[h, rows, :] - highest[h]) * LOG2E)
            total = total + jnp.sum(p, axis=0, keepdims=True)
            v = v_ref[rows, pl.ds(128 * TILE[h], 128)]
            result = result + tn(v, p.astype(BF))
            out.append((total, result))
        return tuple(out)

    init = ((jnp.zeros((1, width), F32), jnp.zeros((128, width), F32)),) * 3
    done = lax.fori_loop(0, blocks, second, init)
    outs = []
    for h in range(3):
        total, result = done[h]
        lo = HEAD_DIM * (h % 2)
        o = result[lo : lo + HEAD_DIM] / total
        o32_ref[0, pl.ds(h * HEAD_DIM, HEAD_DIM), :] = o
        lse_ref[0, pl.ds(h, 1), :] = highest[h] * LOG2E + jnp.log2(total)
        outs.append(o.astype(BF))
    whole = jnp.concatenate(outs, axis=0)
    for j, o_ref in enumerate((own_ref, other_ref)):

        @pl.when(step == j)
        def _():
            o_ref[...] = whole


def attend_forward(meta, q, k, v, u, frames):
    half = frames // 2
    return call(
        functools.partial(forward_kernel, u),
        "attend_forward",
        (2,),
        meta,
        (q, k, v),
        [
            pl.BlockSpec((half, 256), lambda i, m: (u * 2 + (i ^ m[0]), 0)),
            pl.BlockSpec((frames, 256), lambda i, m: (u, 0)),
            pl.BlockSpec((frames, 256), lambda i, m: (u, 0)),
        ],
        [
            fixed(192, half),
            fixed(192, half),
            pl.BlockSpec((1, 192, half), lambda i, m: (i, 0, 0)),
            pl.BlockSpec((1, 8, half), lambda i, m: (i, 0, 0)),
        ],
        [
            like((192, half), BF),
            like((192, half), BF),
            like((2, 192, half), F32),
            like((2, 8, half), F32),
        ],
        [pltpu.VMEM((3, frames, half), F32)],
    )


def backward_kernel(
    u, meta_ref, q_ref, k_ref, v_ref, d0_ref, d1_ref, o32_ref, lse_ref,
    dq_ref, dk_ref, dv_ref, kt_ref, dk_acc, dv_acc, do_ref,
):
    length = meta_ref[1 + u]
    blocks = lax.div(length + KB - 1, KB)
    step = pl.program_id(0)

    @pl.when(step == 0)
    def _():
        dk_acc[...] = jnp.zeros_like(dk_acc)
        dv_acc[...] = jnp.zeros_like(dv_acc)
        kt_ref[...] = jnp.transpose(k_ref[...])
        do_ref[...] = d0_ref[...]

    @pl.when(step == 1)
    def _():
        do_ref[...] = d1_ref[...]

    parts = lane_parts(q_ref[...] * jnp.asarray(0.125, BF))
    width = q_ref.shape[0]
    empty = jnp.zeros((HEAD_DIM, width), BF)
    head = [do_ref[pl.ds(h * HEAD_DIM, HEAD_DIM), :] for h in range(3)]
    grads = (
        jnp.concatenate([head[0], empty], axis=0),
        jnp.concatenate([empty, head[1]], axis=0),
        jnp.concatenate([head[2], empty], axis=0),
    )
    delta = [
        jnp.sum(
            head[h].astype(F32) * o32_ref[0, pl.ds(h * HEAD_DIM, HEAD_DIM), :], axis=0, keepdims=True
        )
        for h in range(3)
    ]
    lse = [lse_ref[0, pl.ds(h, 1), :] for h in range(3)]

    def body(kb, carry):
        start = pl.multiple_of(kb * KB, KB)
        rows = pl.ds(start, KB)
        live = start + lax.broadcasted_iota(jnp.int32, (KB, width), 0) < length
        out = []
        for h in range(3):
            tile = pl.ds(128 * TILE[h], 128)
            s = nt(k_ref[rows, tile], parts[h])
            s = jnp.where(live, s, -1e30)
            p = jnp.exp2(s * LOG2E - lse[h])
            dp = nn(v_ref[rows, tile], grads[h])
            ds = (p * (dp - delta[h])).astype(BF)
            dv_acc[rows, tile] += nt(p.astype(BF), grads[h])
            dk_acc[rows, tile] += nn(ds, parts[h])
            kt = kt_ref[pl.ds(h * HEAD_DIM, HEAD_DIM), rows]
            out.append(carry[h] + nn(kt, ds))
        return tuple(out)

    zero = jnp.zeros((HEAD_DIM, width), F32)
    done = lax.fori_loop(0, blocks, body, (zero,) * 3)
    full = jnp.concatenate(done + (zero,), axis=0) * 0.125
    dq_ref[...] = jnp.transpose(full).astype(BF)

    @pl.when(step == 1)
    def _():
        dk_ref[...] = dk_acc[...].astype(BF)
        dv_ref[...] = dv_acc[...].astype(BF)


def attend_backward(meta, q, k, v, own, other, o32, lse, u, frames):
    half = frames // 2
    return call(
        functools.partial(backward_kernel, u),
        "attend_backward",
        (2,),
        meta,
        (q, k, v, own, other, o32, lse),
        [
            pl.BlockSpec((half, 256), lambda i, m: (u * 2 + (i ^ m[0]), 0)),
            pl.BlockSpec((frames, 256), lambda i, m: (u, 0)),
            pl.BlockSpec((frames, 256), lambda i, m: (u, 0)),
            fixed(192, half),
            fixed(192, half),
            pl.BlockSpec((1, 192, half), lambda i, m: (i, 0, 0)),
            pl.BlockSpec((1, 8, half), lambda i, m: (i, 0, 0)),
        ],
        [
            pl.BlockSpec((half, 256), lambda i, m: (i ^ m[0], 0)),
            fixed(frames, 256),
            fixed(frames, 256),
        ],
        [like((frames, 256), BF)] * 3,
        [
            pltpu.VMEM((256, frames), BF),
            pltpu.VMEM((frames, 256), F32),
            pltpu.VMEM((frames, 256), F32),
            pltpu.VMEM((192, half), BF),
        ],
    )


def entry_kernel(meta_ref, x_ref, dq_ref, dk_ref, dv_ref, wq_ref, wk_ref, wv_ref, *refs):
    before_ref = refs[0] if len(refs) == 5 else None
    send_ref, keep_ref, sum_ref, acc = refs[-4:]
    step = pl.program_id(0)
    x = x_ref[...]
    total = jnp.zeros(x.shape, F32)
    for i, (g_ref, w_ref) in enumerate(((dq_ref, wq_ref), (dk_ref, wk_ref), (dv_ref, wv_ref))):
        rows = pl.ds(192 * i, 192)
        g = g_ref[:, :192]
        total = total + nn(g, w_ref[...])
        product = tn(g, x)

        @pl.when(step == 0)
        def _():
            acc[rows, :] = product if before_ref is None else product + before_ref[rows, :]

        @pl.when(step == 1)
        def _():
            sum_ref[rows, :] = (product + acc[rows, :]).astype(sum_ref.dtype)

    low = total.astype(BF)

    @pl.when(step == 0)
    def _():
        send_ref[...] = low

    @pl.when(step == 1)
    def _():
        keep_ref[...] = low


def entry_back(meta, tokens, grads, weights, before, u, frames, dtype):
    half = frames // 2
    d = tokens.shape[1]
    return call(
        entry_kernel,
        "entry_back",
        (2,),
        meta,
        (tokens, *grads, *weights, *before),
        [pl.BlockSpec((half, d), lambda i, m: (u * 2 + (1 - i ^ m[0]), 0))]
        + [pl.BlockSpec((half, 256), lambda i, m: (1 - i ^ m[0], 0))] * 3
        + [fixed(192, d)] * 3
        + [fixed(576, d)] * len(before),
        [fixed(half, d), fixed(half, d), fixed(576, d)],
        [like((half, d), BF), like((half, d), BF), like((576, d), dtype)],
        [pltpu.VMEM((576, d), F32)],
    )


def place_kernel(meta_ref, *refs):
    o_ref = refs[-1]
    for i, r_ref in enumerate(refs[:-1]):

        @pl.when(pl.program_id(0) == i)
        def _():
            o_ref[...] = r_ref[...]


def place(meta, own, other):
    half, d = own[0].shape
    count = 2 * len(own)
    return call(
        place_kernel,
        "place",
        (count,),
        meta,
        [block for pair in zip(own, other) for block in pair],
        [fixed(half, d)] * count,
        pl.BlockSpec((half, d), lambda i, m: (i ^ m[0], 0)),
        like((count * half, d), own[0].dtype),
    )


def normalise(values):
    average = jnp.mean(values, axis=-1, keepdims=True)
    centred = values - average
    spread = jnp.mean(centred * centred, axis=-1, keepdims=True)
    rstd = lax.rsqrt(spread + EPS)
    return centred * rstd, rstd


def gelu_pair(v):
    e = jnp.exp2(v * v * (-0.5 * LOG2E))
    t = 1.0 / (1.0 + (0.3275911 * 0.7071067811865476) * jnp.abs(v))
    poly = t * (0.5 * 0.254829592 + t * (0.5 * -0.284496736 + t * (0.5 * 1.421413741 + t * (0.5 * -1.453152027 + t * (0.5 * 1.061405429)))))
    tail = poly * e
    phi_cap = jnp.where(v >= 0, 1.0 - tail, tail)
    return v * phi_cap, phi_cap + v * (e * 0.3989422804014327)


def ahead_kernel(
    meta_ref, tok_ref, a0, a1, a2, a3, w0, w1, w2, w3, ua_ref, ub_ref, da_ref, db_ref, vec_ref,
    xhat_ref, rstd_ref, low_ref, act_ref, slope_ref, own_ref, sent_ref,
):
    gain, bias = vec_ref[0:1, :], vec_ref[1:2, :]
    hidden = ua_ref.shape[1]
    for r in range(tok_ref.shape[0] // RB):
        rows = pl.ds(r * RB, RB)
        branch = jnp.zeros((RB, tok_ref.shape[1]), F32)
        for a, w in ((a0, w0), (a1, w1), (a2, w2), (a3, w3)):
            branch = branch + tn(a[:, rows], w[...]).astype(BF).astype(F32)
        xhat, rstd = normalise(tok_ref[rows, :].astype(F32) + branch)
        xhat_ref[rows, :] = xhat
        rstd_ref[rows, :] = jnp.broadcast_to(rstd, (RB, rstd_ref.shape[1]))
        normed = xhat * gain + bias
        low = normed.astype(BF)
        low_ref[rows, :] = low
        sent = jnp.zeros(normed.shape, F32)
        for g, (up, down) in enumerate(((ua_ref, da_ref), (ub_ref, db_ref))):
            acts = []
            for c in range(hidden // HB):
                act, slope = gelu_pair(nn(low, up[:, c * HB : (c + 1) * HB]))
                columns = pl.ds(g * hidden + c * HB, HB)
                acts.append(act.astype(BF))
                act_ref[rows, columns] = acts[-1]
                slope_ref[rows, columns] = slope.astype(BF)
            sent = sent + nn(jnp.concatenate(acts, axis=1), down[...]).astype(BF).astype(F32)
        own_ref[rows, :] = normed + sent
        sent_ref[rows, :] = sent.astype(BF)


def ahead(meta, tokens, att, merge_w, up, down, vectors, u):
    half = att[0].shape[1]
    d, hidden = up[0].shape
    return call(
        ahead_kernel,
        "ahead",
        (1,),
        meta,
        (tokens, *att, *merge_w, *up, *down, vectors),
        [pl.BlockSpec((half, d), lambda i, m: (u * 2 + m[0], 0))]
        + [fixed(192, half)] * 4
        + [fixed(192, d)] * 4
        + [fixed(d, hidden)] * 2
        + [fixed(hidden, d)] * 2
        + [fixed(4, d)],
        [fixed(half, d), fixed(half, 128), fixed(half, d), fixed(half, 2 * hidden), fixed(half, 2 * hidden), fixed(half, d), fixed(half, d)],
        [
            like((half, d), F32),
            like((half, 128), F32),
            like((half, d), BF),
            like((half, 2 * hidden), BF),
            like((half, 2 * hidden), BF),
            like((half, d), F32),
            like((half, d), BF),
        ],
    )


def astern_kernel(seqs, u, meta_ref, own_ref, far_ref, grad_ref, span_ref, ua_ref, ub_ref, da_ref, db_ref, slope_ref, vec_ref, *refs):
    last = u == seqs - 1
    before = refs[: 4 * seqs - 2] if last else ()
    out_ref, g_ref, pre_ref, back_ref, sent_ref, small_ref = refs[len(before) : len(before) + 6]
    gain, bias = vec_ref[2:3, :], vec_ref[3:4, :]
    half, d = own_ref.shape
    hidden = ua_ref.shape[1]
    starts = span_ref[u : u + 1, :]
    gain_grad = jnp.zeros(gain.shape, F32)
    bias_grad = jnp.zeros(gain.shape, F32)
    for r in range(half // RB):
        rows = pl.ds(r * RB, RB)
        xhat, rstd = normalise(own_ref[rows, :] + far_ref[rows, :].astype(F32))
        out_ref[rows, :] = (xhat * gain + bias).astype(BF)
        frame = meta_ref[0] * half + r * RB + lax.broadcasted_iota(jnp.int32, (RB, starts.shape[1]), 0)
        inside = (frame >= starts) & (frame < starts + SPAN)
        weight = jnp.max(jnp.where(inside, 1.0, 0.0), axis=1, keepdims=True)
        cot = grad_ref[rows, :].astype(F32) * weight
        gain_grad = gain_grad + jnp.sum(cot * xhat, axis=0, keepdims=True)
        bias_grad = bias_grad + jnp.sum(cot, axis=0, keepdims=True)
        gy = cot * gain
        mean_gy = jnp.mean(gy, axis=-1, keepdims=True)
        mean_gx = jnp.mean(gy * xhat, axis=-1, keepdims=True)
        sum_grad = rstd * (gy - mean_gy - xhat * mean_gx)
        low = sum_grad.astype(BF)
        g_ref[rows, :] = low
        sent = jnp.zeros(sum_grad.shape, F32)
        for g, (up, down) in enumerate(((ua_ref, da_ref), (ub_ref, db_ref))):
            pres = []
            for c in range(hidden // HB):
                columns = pl.ds(g * hidden + c * HB, HB)
                slope = slope_ref[rows, columns].astype(F32)
                pres.append((nt(low, down[c * HB : (c + 1) * HB, :]) * slope).astype(BF))
                pre_ref[rows, columns] = pres[-1]
            sent = sent + nt(jnp.concatenate(pres, axis=1), up[...]).astype(BF).astype(F32)
        back_ref[rows, :] = sum_grad + sent
        sent_ref[rows, :] = sent.astype(BF)
    small_ref[0:1, :] = gain_grad
    small_ref[1:2, :] = bias_grad
    if last:
        acts, xs = before[:seqs], before[seqs : 2 * seqs]
        pres = (*before[2 * seqs : 3 * seqs - 1], pre_ref)
        gs = (*before[3 * seqs - 1 :], g_ref)
        dups, ddowns = refs[-4:-2], refs[-2:]
        for g in range(2):
            for c in range(hidden // HB):
                columns = pl.ds(g * hidden + c * HB, HB)
                block = pl.ds(c * HB, HB)
                dups[g][:, block] = sum(tn(x[...], p[:, columns]) for x, p in zip(xs, pres)).astype(BF)
                ddowns[g][block, :] = sum(tn(a[:, columns], h[...]) for a, h in zip(acts, gs)).astype(BF)


def astern(meta, own, far, grad, spans, up, down, slope, vectors, u, seqs, before):
    half, d = own.shape
    hidden = up[0].shape[1]
    rows = fixed(half, d)
    wide = fixed(half, 2 * hidden)
    extra = [] if not before else [wide] * seqs + [rows] * seqs + [wide] * (seqs - 1) + [rows] * (seqs - 1)
    grads = [] if not before else [(d, hidden)] * 2 + [(hidden, d)] * 2
    return call(
        functools.partial(astern_kernel, seqs, u),
        "astern",
        (1,),
        meta,
        (own, far, grad, spans, *up, *down, slope, vectors, *before),
        [rows] * 2
        + [pl.BlockSpec((half, d), lambda i, m: (u * 2 + m[0], 0)), fixed(*spans.shape)]
        + [fixed(d, hidden)] * 2
        + [fixed(hidden, d)] * 2
        + [wide, fixed(4, d)]
        + extra,
        [rows, rows, wide, rows, rows, fixed(2, d)] + [fixed(*shape) for shape in grads],
        [
            like((half, d), BF),
            like((half, d), BF),
            like((half, 2 * hidden), BF),
            like((half, d), F32),
            like((half, d), BF),
            like((2, d), F32),
        ]
        + [like(shape, BF) for shape in grads],
        limit=32 if before else VMEM,
    )


def inner_kernel(meta_ref, own_ref, far_ref, xhat_ref, rstd_ref, vec_ref, a0, a1, w0, w1, *refs):
    last = len(refs) == 11
    out_ref, g0, g1, m0, m1, small_ref = refs[-6:]
    grad = own_ref[...] + far_ref[...].astype(F32)
    xhat = xhat_ref[...]
    gain_grad = jnp.sum(grad * xhat, axis=0, keepdims=True)
    bias_grad = jnp.sum(grad, axis=0, keepdims=True)
    gy = grad * vec_ref[0:1, :]
    mean_gy = jnp.mean(gy, axis=-1, keepdims=True)
    mean_gx = jnp.mean(gy * xhat, axis=-1, keepdims=True)
    inner = rstd_ref[:, 0:1] * (gy - mean_gy - xhat * mean_gx)
    out_ref[...] = inner
    low = inner.astype(BF)
    g0[...] = nt(w0[...], low).astype(BF)
    g1[...] = nt(w1[...], low).astype(BF)
    small = jnp.concatenate([gain_grad, bias_grad], axis=0)
    small_ref[...] = small
    if last:
        before0, before1, before_small, outer0, outer1 = refs[:5]
        below = jnp.concatenate(
            [small + before_small[...], outer0[...] + outer1[...], jnp.zeros((60, small.shape[1]), F32)], axis=0
        ).astype(BF)
        for m, a, before in ((m0, a0, before0), (m1, a1, before1)):
            m[:192, :] = (nn(a[...], low) + before[...]).astype(BF)
            m[192:, :] = below
    else:
        m0[...] = nn(a0[...], low)
        m1[...] = nn(a1[...], low)


def inner_norm(meta, own, far, xhat, rstd, vectors, att, weights, before):
    rows, d = xhat.shape
    merge = like((256, d), BF) if before else like((192, d), F32)
    return call(
        inner_kernel,
        "inner_norm",
        (1,),
        meta,
        (own, far, xhat, rstd, vectors, *att, *weights, *before),
        [fixed(rows, d)] * 3
        + [fixed(rows, 128), fixed(4, d)]
        + [fixed(192, rows)] * 2
        + [fixed(192, d)] * 2
        + ([fixed(192, d)] * 2 + [fixed(2, d)] * 3 if before else []),
        [fixed(rows, d), fixed(192, rows), fixed(192, rows), fixed(*merge.shape), fixed(*merge.shape), fixed(2, d)],
        [like((rows, d), F32), like((192, rows), BF), like((192, rows), BF), merge, merge, like((2, d), F32)],
    )


def local(groups, tokens, lengths, span_starts, wq, wk, wv, wm, wu, wd, ig, ib, og, ob, out_grad):
    rows, d = tokens.shape
    seqs = lengths.shape[0]
    frames = rows // seqs
    half = frames // 2
    core = lax.axis_index("tensor") % 2
    place_dp = lax.axis_index("dp")
    bits = groups.bit_length() - 1

    def swap(value, k):
        return lax.ppermute(value, "tensor", [(i, i ^ k) for i in range(4)])

    def swap_dp(value, k):
        return lax.ppermute(value, "dp", [(i, i ^ k) for i in range(groups)])

    def add(a, b):
        return (a.astype(F32) + b.astype(F32)).astype(BF)

    def cut(array, index, count):
        size = array.shape[0] // count
        return lax.dynamic_slice_in_dim(array, index * size, size, 0)

    class Chain:
        def __init__(self, state, order):
            self.state = state
            self.steps = [(True, *stage) for stage in order] + [(False, *stage) for stage in reversed(order)]

        def start(self):
            if self.steps:
                scatter, low_bit, width = self.steps[0]
                count = 1 << width
                spot = (place_dp >> low_bit) & (count - 1)
                sent = [cut(self.state, spot ^ j, count) if scatter else self.state for j in range(1, count)]
                got = [swap_dp(piece, j << low_bit) for j, piece in enumerate(sent, 1)]
                self.pending = [cut(self.state, spot, count) if scatter else self.state] + got

        def finish(self, *after):
            if not self.steps:
                return
            scatter, low_bit, width = self.steps.pop(0)
            pieces = self.pending
            if after:
                pieces = lax.optimization_barrier((*pieces, *after))[: len(pieces)]
            count = 1 << width
            spot = (place_dp >> low_bit) & (count - 1)
            if scatter:
                self.state = sum(piece.astype(F32) for piece in pieces).astype(BF)
            elif count == 2:
                one, two = pieces
                self.state = jnp.concatenate([jnp.where(spot, two, one), jnp.where(spot, one, two)], axis=0)
            else:
                size = pieces[0].shape[0]
                whole = jnp.zeros((size * count, d), BF)
                for j in range(count):
                    whole = lax.dynamic_update_slice_in_dim(whole, pieces[j], (spot ^ j) * size, 0)
                self.state = whole

    scalars = jnp.concatenate([core.reshape(1), lengths])
    token = []

    def meta():
        return lax.optimization_barrier((scalars, *token))[0] if token else scalars

    def done(results, *others):
        token[:] = [results[0], *others]
        return results

    merge_w = (wm, swap(wm, 1), swap(wm, 2), swap(wm, 3))
    up_w = (wu, swap(wu, 1))
    down_w = (wd, swap(wd, 1))
    vectors = jnp.stack([ig, ib, og, ob])
    qkv_w = (wq.T, wk.T, wv.T)

    q, k, v = project(tokens, *qkv_w)
    fwd, att = [], []
    for u in range(seqs):
        fwd.append(done(attend_forward(meta(), q, k, v, u, frames), *merge_w[1:], up_w[1], down_w[1]))
        own, other = fwd[u][:2]
        att.append((own, swap(other, 1), swap(own, 2), swap(other, 3)))
    front, far = [], []
    for u in range(seqs):
        front.append(done(ahead(meta(), tokens, att[u], merge_w, up_w, down_w, vectors, u)))
        far.append(swap(front[u][6], 2))
    back, far_grad = [], []
    for u in range(seqs):
        before = ()
        if u == seqs - 1:
            before = (*(f[3] for f in front), *(f[2] for f in front), *(b[2] for b in back), *(b[1] for b in back))
        back.append(
            done(astern(meta(), front[u][5], far[u], out_grad, span_starts, up_w, down_w, front[u][4], vectors, u, seqs, before))
        )
        if u == 0:
            far_grad.append(swap(back[u][4], 2))

    def inner_step(u, before):
        res = done(inner_norm(meta(), back[u][3], far_grad[u], front[u][0], front[u][1], vectors, att[u][:2], merge_w[:2], before))
        return res, (res[1], swap(res[2], 1))

    def attend_step(u, grads):
        return done(attend_backward(meta(), q, k, v, *grads, fwd[u][2], fwd[u][3], u, frames))

    def entry_step(u, grads, before, dtype):
        return done(entry_back(meta(), tokens, grads, qkv_w, before, u, frames, dtype))


    pairs = [(b, 1) for b in range(bits)]
    stages = [(0, 1)] + [(b, 2) for b in range(1, bits - 1, 2)] + ([(bits - 1, 1)] if bits % 2 == 0 else [])
    inner, near, crossed, total, chains = [], [], [], (), []
    out_rows = [b[0] for b in back]
    out_other = [swap(r, 1) for r in out_rows]

    def advance(result):
        for chain in chains:
            chain.finish(result)
            token.append(chain.state)
            chain.start()

    for u in range(seqs):
        last = u == seqs - 1
        if u == 0:
            res, grads = inner_step(0, ())
            inner.append(res)
            later = lax.optimization_barrier((*back[-1][6:], back[-1][4], res[0]))
            up_own, up_other, down_own, down_other, sent = later[:5]
            far_grad.append(swap(sent, 2))
            chains.append(Chain(add(down_own, swap(down_other, 1)), pairs))
            chains.append(Chain(add(up_own, swap(up_other, 1)), pairs[1:2] + pairs[:1] + pairs[2:]))
            for chain in chains:
                token.append(chain.state)
                chain.start()
            token.extend(out_other)
        dqkv = attend_step(u, grads)
        advance(dqkv[0])
        if not last:
            before = ()
            if u + 1 == seqs - 1:
                before = (inner[0][3], inner[0][4], inner[0][5], back[0][5], back[1][5])
            res, grads = inner_step(u + 1, before)
            inner.append(res)
        else:
            token.extend(crossed)
        out = entry_step(u, dqkv, total, BF if last else F32)
        total = (out[2],)
        got = swap(out[0], 1)
        near.append(out[1].astype(F32) + got.astype(F32))
        crossed.append(swap(near[u].astype(BF), 2))
        token.append(got)
        if not last:
            advance(out[0])
            chains.append(Chain(add(res[3], swap(res[4], 1)), pairs))
            token.append(chains[-1].state)
            chains[-1].start()
    chains.append(Chain(total[0], stages))
    chains[-1].start()
    beside = {0: (got,), 1: (crossed[-1],)}
    rounds = 0
    while any(chain.steps for chain in chains):
        for chain in chains:
            chain.finish(total[0])
        states = tuple(chain.state for chain in chains)
        states = lax.optimization_barrier(states + beside.get(rounds, ()))[: len(chains)]
        for chain, state in zip(chains, states):
            chain.state = state
            chain.start()
        rounds += 1
    down_sum, up_sum, merge_sum, qkv_sum = (chain.state for chain in chains)

    ready = [(inner[u][0] + (near[u] + crossed[u].astype(F32))).astype(BF) for u in range(seqs)]
    layer_output = place(meta(), out_rows, out_other)
    input_grad = place(scalars, ready, [swap(r, 1) for r in ready])

    small = merge_sum[192:196].astype(F32)
    query_grad, key_grad, value_grad = (qkv_sum[192 * i : 192 * (i + 1)].astype(F32).T for i in range(3))
    return (
        layer_output,
        input_grad,
        query_grad,
        key_grad,
        value_grad,
        merge_sum[:192].astype(F32),
        up_sum.astype(F32),
        down_sum.astype(F32),
        small[0],
        small[1],
        small[2],
        small[3],
    )


def solution(mesh):
    in_specs = (
        P("dp", None),
        P("dp"),
        P("dp", None),
        P(None, "tensor"),
        P(None, "tensor"),
        P(None, "tensor"),
        P("tensor", None),
        P(None, "tensor"),
        P("tensor", None),
        P(),
        P(),
        P(),
        P(),
        P("dp", None),
    )
    out_specs = (
        P("dp", None),
        P("dp", None),
        P(None, "tensor"),
        P(None, "tensor"),
        P(None, "tensor"),
        P("tensor", None),
        P(None, "tensor"),
        P("tensor", None),
        P(),
        P(),
        P(),
        P(),
    )
    body = functools.partial(local, mesh.shape["dp"])
    return jax.shard_map(body, mesh=mesh, in_specs=in_specs, out_specs=out_specs, check_vma=False)
```

```python
import functools

import jax
import jax.numpy as jnp
from jax import lax
from jax.experimental import pallas as pl
from jax.experimental.pallas import tpu as pltpu
from jax.sharding import PartitionSpec as P

HEAD_DIM = 64
SPAN = 10
EPS = 1e-05
LOG2E = 1.4426950408889634
KB = 256
VMEM = 16
RB = 128
HB = 256
BF = jnp.bfloat16
F32 = jnp.float32
MIB = 1 << 20


def nn(a, b):
    return lax.dot_general(a, b, (((1,), (0,)), ((), ())), preferred_element_type=F32)


def nt(a, b):
    return lax.dot_general(a, b, (((1,), (1,)), ((), ())), preferred_element_type=F32)


def tn(a, b):
    return lax.dot_general(a, b, (((0,), (0,)), ((), ())), preferred_element_type=F32)


def params(limit):
    return pltpu.CompilerParams(vmem_limit_bytes=limit * MIB)


def cost(micros):
    return pl.CostEstimate(flops=int(micros * 1.1e9), bytes_accessed=1024, transcendentals=0)


MICROS = {"attend_forward": 8, "attend_backward": 12, "entry_back": 5, "place": 3, "ahead": 9, "astern": 10, "inner_norm": 3, "weight_grads": 5}


def project_kernel(x_ref, wq_ref, wk_ref, wv_ref, q_ref, k_ref, v_ref):
    x = x_ref[...]
    for w_ref, o_ref in ((wq_ref, q_ref), (wk_ref, k_ref), (wv_ref, v_ref)):
        o_ref[:, :192] = nt(x, w_ref[...]).astype(BF)
        o_ref[:, 192:] = jnp.zeros((x.shape[0], HEAD_DIM), BF)


def project(tokens, wq, wk, wv):
    rows, d = tokens.shape
    block = 512
    return pl.pallas_call(
        project_kernel,
        grid=(rows // block,),
        in_specs=[pl.BlockSpec((block, d), lambda i: (i, 0))]
        + [pl.BlockSpec((192, d), lambda i: (0, 0))] * 3,
        out_specs=[pl.BlockSpec((block, 256), lambda i: (i, 0))] * 3,
        out_shape=[jax.ShapeDtypeStruct((rows, 256), BF)] * 3,
        compiler_params=params(48),
        cost_estimate=cost(3),
        name="project",
    )(tokens, wq, wk, wv)


def lane_parts(block):
    left = block[:, :128]
    lane = lax.broadcasted_iota(jnp.int32, left.shape, 1)
    zero = jnp.zeros_like(left)
    return (
        jnp.where(lane < HEAD_DIM, left, zero),
        jnp.where(lane >= HEAD_DIM, left, zero),
        block[:, 128:],
    )


TILE = (0, 0, 1)


def call(kernel, name, grid, meta, args, in_specs, out_specs, out_shape, scratch=(), limit=VMEM):
    return pl.pallas_call(
        kernel,
        grid_spec=pltpu.PrefetchScalarGridSpec(
            num_scalar_prefetch=1,
            grid=grid,
            in_specs=in_specs,
            out_specs=out_specs,
            scratch_shapes=scratch,
        ),
        out_shape=out_shape,
        compiler_params=params(limit),
        cost_estimate=cost(MICROS[name]),
        name=name,
    )(meta, *args)


def fixed(*shape):
    return pl.BlockSpec(shape, lambda *_: (0,) * len(shape))


def like(shape, dtype):
    return jax.ShapeDtypeStruct(shape, dtype)


def forward_kernel(u, meta_ref, q_ref, k_ref, v_ref, own_ref, other_ref, o32_ref, lse_ref, s_ref):
    length = meta_ref[1 + u]
    step = pl.program_id(0)
    blocks = lax.div(length + KB - 1, KB)
    parts = lane_parts(q_ref[...] * jnp.asarray(0.125, BF))
    width = q_ref.shape[0]

    def first(kb, highest):
        start = pl.multiple_of(kb * KB, KB)
        rows = pl.ds(start, KB)
        live = start + lax.broadcasted_iota(jnp.int32, (KB, width), 0) < length
        out = []
        for h in range(3):
            tile = pl.ds(128 * TILE[h], 128)
            s = nt(k_ref[rows, tile], parts[h])
            s = jnp.where(live, s, -1e30)
            s_ref[h, rows, :] = s
            out.append(jnp.maximum(highest[h], jnp.max(s, axis=0, keepdims=True)))
        return tuple(out)

    floor = jnp.full((1, width), -1e30, F32)
    highest = lax.fori_loop(0, blocks, first, (floor,) * 3)

    def second(kb, carry):
        rows = pl.ds(pl.multiple_of(kb * KB, KB), KB)
        out = []
        for h in range(3):
            total, result = carry[h]
            p = jnp.exp2((s_ref[h, rows, :] - highest[h]) * LOG2E)
            total = total + jnp.sum(p, axis=0, keepdims=True)
            v = v_ref[rows, pl.ds(128 * TILE[h], 128)]
            result = result + tn(v, p.astype(BF))
            out.append((total, result))
        return tuple(out)

    init = ((jnp.zeros((1, width), F32), jnp.zeros((128, width), F32)),) * 3
    done = lax.fori_loop(0, blocks, second, init)
    outs = []
    for h in range(3):
        total, result = done[h]
        lo = HEAD_DIM * (h % 2)
        o = result[lo : lo + HEAD_DIM] / total
        o32_ref[0, pl.ds(h * HEAD_DIM, HEAD_DIM), :] = o
        lse_ref[0, pl.ds(h, 1), :] = highest[h] * LOG2E + jnp.log2(total)
        outs.append(o.astype(BF))
    whole = jnp.concatenate(outs, axis=0)
    for j, o_ref in enumerate((own_ref, other_ref)):

        @pl.when(step == j)
        def _():
            o_ref[...] = whole


def attend_forward(meta, q, k, v, u, frames):
    half = frames // 2
    return call(
        functools.partial(forward_kernel, u),
        "attend_forward",
        (2,),
        meta,
        (q, k, v),
        [
            pl.BlockSpec((half, 256), lambda i, m: (u * 2 + (i ^ m[0]), 0)),
            pl.BlockSpec((frames, 256), lambda i, m: (u, 0)),
            pl.BlockSpec((frames, 256), lambda i, m: (u, 0)),
        ],
        [
            fixed(192, half),
            fixed(192, half),
            pl.BlockSpec((1, 192, half), lambda i, m: (i, 0, 0)),
            pl.BlockSpec((1, 8, half), lambda i, m: (i, 0, 0)),
        ],
        [
            like((192, half), BF),
            like((192, half), BF),
            like((2, 192, half), F32),
            like((2, 8, half), F32),
        ],
        [pltpu.VMEM((3, frames, half), F32)],
    )


def backward_kernel(
    u, meta_ref, q_ref, k_ref, v_ref, d0_ref, d1_ref, o32_ref, lse_ref,
    dq_ref, dk_ref, dv_ref, kt_ref, dk_acc, dv_acc, do_ref,
):
    length = meta_ref[1 + u]
    blocks = lax.div(length + KB - 1, KB)
    step = pl.program_id(0)

    @pl.when(step == 0)
    def _():
        dk_acc[...] = jnp.zeros_like(dk_acc)
        dv_acc[...] = jnp.zeros_like(dv_acc)
        kt_ref[...] = jnp.transpose(k_ref[...])
        do_ref[...] = d0_ref[...]

    @pl.when(step == 1)
    def _():
        do_ref[...] = d1_ref[...]

    parts = lane_parts(q_ref[...] * jnp.asarray(0.125, BF))
    width = q_ref.shape[0]
    empty = jnp.zeros((HEAD_DIM, width), BF)
    head = [do_ref[pl.ds(h * HEAD_DIM, HEAD_DIM), :] for h in range(3)]
    grads = (
        jnp.concatenate([head[0], empty], axis=0),
        jnp.concatenate([empty, head[1]], axis=0),
        jnp.concatenate([head[2], empty], axis=0),
    )
    delta = [
        jnp.sum(
            head[h].astype(F32) * o32_ref[0, pl.ds(h * HEAD_DIM, HEAD_DIM), :], axis=0, keepdims=True
        )
        for h in range(3)
    ]
    lse = [lse_ref[0, pl.ds(h, 1), :] for h in range(3)]

    def body(kb, carry):
        start = pl.multiple_of(kb * KB, KB)
        rows = pl.ds(start, KB)
        live = start + lax.broadcasted_iota(jnp.int32, (KB, width), 0) < length
        out = []
        for h in range(3):
            tile = pl.ds(128 * TILE[h], 128)
            s = nt(k_ref[rows, tile], parts[h])
            s = jnp.where(live, s, -1e30)
            p = jnp.exp2(s * LOG2E - lse[h])
            dp = nn(v_ref[rows, tile], grads[h])
            ds = (p * (dp - delta[h])).astype(BF)
            dv_acc[rows, tile] += nt(p.astype(BF), grads[h])
            dk_acc[rows, tile] += nn(ds, parts[h])
            kt = kt_ref[pl.ds(h * HEAD_DIM, HEAD_DIM), rows]
            out.append(carry[h] + nn(kt, ds))
        return tuple(out)

    zero = jnp.zeros((HEAD_DIM, width), F32)
    done = lax.fori_loop(0, blocks, body, (zero,) * 3)
    full = jnp.concatenate(done + (zero,), axis=0) * 0.125
    dq_ref[...] = jnp.transpose(full).astype(BF)

    @pl.when(step == 1)
    def _():
        dk_ref[...] = dk_acc[...].astype(BF)
        dv_ref[...] = dv_acc[...].astype(BF)


def attend_backward(meta, q, k, v, own, other, o32, lse, u, frames):
    half = frames // 2
    return call(
        functools.partial(backward_kernel, u),
        "attend_backward",
        (2,),
        meta,
        (q, k, v, own, other, o32, lse),
        [
            pl.BlockSpec((half, 256), lambda i, m: (u * 2 + (i ^ m[0]), 0)),
            pl.BlockSpec((frames, 256), lambda i, m: (u, 0)),
            pl.BlockSpec((frames, 256), lambda i, m: (u, 0)),
            fixed(192, half),
            fixed(192, half),
            pl.BlockSpec((1, 192, half), lambda i, m: (i, 0, 0)),
            pl.BlockSpec((1, 8, half), lambda i, m: (i, 0, 0)),
        ],
        [
            pl.BlockSpec((half, 256), lambda i, m: (i ^ m[0], 0)),
            fixed(frames, 256),
            fixed(frames, 256),
        ],
        [like((frames, 256), BF)] * 3,
        [
            pltpu.VMEM((256, frames), BF),
            pltpu.VMEM((frames, 256), F32),
            pltpu.VMEM((frames, 256), F32),
            pltpu.VMEM((192, half), BF),
        ],
    )


def entry_kernel(meta_ref, x_ref, dq_ref, dk_ref, dv_ref, wq_ref, wk_ref, wv_ref, *refs):
    before_ref = refs[0] if len(refs) == 5 else None
    send_ref, keep_ref, sum_ref, acc = refs[-4:]
    step = pl.program_id(0)
    x = x_ref[...]
    total = jnp.zeros(x.shape, F32)
    for i, (g_ref, w_ref) in enumerate(((dq_ref, wq_ref), (dk_ref, wk_ref), (dv_ref, wv_ref))):
        rows = pl.ds(192 * i, 192)
        g = g_ref[:, :192]
        total = total + nn(g, w_ref[...])
        product = tn(g, x)

        @pl.when(step == 0)
        def _():
            acc[rows, :] = product if before_ref is None else product + before_ref[rows, :]

        @pl.when(step == 1)
        def _():
            sum_ref[rows, :] = (product + acc[rows, :]).astype(sum_ref.dtype)

    low = total.astype(BF)

    @pl.when(step == 0)
    def _():
        send_ref[...] = low

    @pl.when(step == 1)
    def _():
        keep_ref[...] = low


def entry_back(meta, tokens, grads, weights, before, u, frames, dtype):
    half = frames // 2
    d = tokens.shape[1]
    return call(
        entry_kernel,
        "entry_back",
        (2,),
        meta,
        (tokens, *grads, *weights, *before),
        [pl.BlockSpec((half, d), lambda i, m: (u * 2 + (1 - i ^ m[0]), 0))]
        + [pl.BlockSpec((half, 256), lambda i, m: (1 - i ^ m[0], 0))] * 3
        + [fixed(192, d)] * 3
        + [fixed(576, d)] * len(before),
        [fixed(half, d), fixed(half, d), fixed(576, d)],
        [like((half, d), BF), like((half, d), BF), like((576, d), dtype)],
        [pltpu.VMEM((576, d), F32)],
    )


def place_kernel(meta_ref, *refs):
    o_ref = refs[-1]
    for i, r_ref in enumerate(refs[:-1]):

        @pl.when(pl.program_id(0) == i)
        def _():
            o_ref[...] = r_ref[...]


def place(meta, own, other):
    half, d = own[0].shape
    count = 2 * len(own)
    return call(
        place_kernel,
        "place",
        (count,),
        meta,
        [block for pair in zip(own, other) for block in pair],
        [fixed(half, d)] * count,
        pl.BlockSpec((half, d), lambda i, m: (i ^ m[0], 0)),
        like((count * half, d), own[0].dtype),
    )


def normalise(values):
    average = jnp.mean(values, axis=-1, keepdims=True)
    centred = values - average
    spread = jnp.mean(centred * centred, axis=-1, keepdims=True)
    rstd = lax.rsqrt(spread + EPS)
    return centred * rstd, rstd


def gelu_pair(v):
    e = jnp.exp2(v * v * (-0.5 * LOG2E))
    t = 1.0 / (1.0 + (0.3275911 * 0.7071067811865476) * jnp.abs(v))
    poly = t * (0.5 * 0.254829592 + t * (0.5 * -0.284496736 + t * (0.5 * 1.421413741 + t * (0.5 * -1.453152027 + t * (0.5 * 1.061405429)))))
    tail = poly * e
    phi_cap = jnp.where(v >= 0, 1.0 - tail, tail)
    return v * phi_cap, phi_cap + v * (e * 0.3989422804014327)


def ahead_kernel(
    meta_ref, tok_ref, a0, a1, a2, a3, w0, w1, w2, w3, ua_ref, ub_ref, da_ref, db_ref, vec_ref,
    xhat_ref, rstd_ref, low_ref, act_ref, slope_ref, own_ref, sent_ref,
):
    gain, bias = vec_ref[0:1, :], vec_ref[1:2, :]
    hidden = ua_ref.shape[1]
    for r in range(tok_ref.shape[0] // RB):
        rows = pl.ds(r * RB, RB)
        branch = jnp.zeros((RB, tok_ref.shape[1]), F32)
        for a, w in ((a0, w0), (a1, w1), (a2, w2), (a3, w3)):
            branch = branch + tn(a[:, rows], w[...]).astype(BF).astype(F32)
        xhat, rstd = normalise(tok_ref[rows, :].astype(F32) + branch)
        xhat_ref[rows, :] = xhat
        rstd_ref[rows, :] = jnp.broadcast_to(rstd, (RB, rstd_ref.shape[1]))
        normed = xhat * gain + bias
        low = normed.astype(BF)
        low_ref[rows, :] = low
        sent = jnp.zeros(normed.shape, F32)
        for g, (up, down) in enumerate(((ua_ref, da_ref), (ub_ref, db_ref))):
            acts = []
            for c in range(hidden // HB):
                act, slope = gelu_pair(nn(low, up[:, c * HB : (c + 1) * HB]))
                columns = pl.ds(g * hidden + c * HB, HB)
                acts.append(act.astype(BF))
                act_ref[rows, columns] = acts[-1]
                slope_ref[rows, columns] = slope.astype(BF)
            sent = sent + nn(jnp.concatenate(acts, axis=1), down[...]).astype(BF).astype(F32)
        own_ref[rows, :] = normed + sent
        sent_ref[rows, :] = sent.astype(BF)


def ahead(meta, tokens, att, merge_w, up, down, vectors, u):
    half = att[0].shape[1]
    d, hidden = up[0].shape
    return call(
        ahead_kernel,
        "ahead",
        (1,),
        meta,
        (tokens, *att, *merge_w, *up, *down, vectors),
        [pl.BlockSpec((half, d), lambda i, m: (u * 2 + m[0], 0))]
        + [fixed(192, half)] * 4
        + [fixed(192, d)] * 4
        + [fixed(d, hidden)] * 2
        + [fixed(hidden, d)] * 2
        + [fixed(4, d)],
        [fixed(half, d), fixed(half, 128), fixed(half, d), fixed(half, 2 * hidden), fixed(half, 2 * hidden), fixed(half, d), fixed(half, d)],
        [
            like((half, d), F32),
            like((half, 128), F32),
            like((half, d), BF),
            like((half, 2 * hidden), BF),
            like((half, 2 * hidden), BF),
            like((half, d), F32),
            like((half, d), BF),
        ],
    )


def astern_kernel(u, meta_ref, own_ref, far_ref, grad_ref, span_ref, ua_ref, ub_ref, da_ref, db_ref, slope_ref, vec_ref, *refs):
    last = len(refs) > 6
    before = refs[: len(refs) - 10] if last else ()
    out_ref, g_ref, pre_ref, back_ref, sent_ref, small_ref = refs[len(before) : len(before) + 6]
    gain, bias = vec_ref[2:3, :], vec_ref[3:4, :]
    half, d = own_ref.shape
    hidden = ua_ref.shape[1]
    starts = span_ref[u : u + 1, :]
    gain_grad = jnp.zeros(gain.shape, F32)
    bias_grad = jnp.zeros(gain.shape, F32)
    for r in range(half // RB):
        rows = pl.ds(r * RB, RB)
        xhat, rstd = normalise(own_ref[rows, :] + far_ref[rows, :].astype(F32))
        out_ref[rows, :] = (xhat * gain + bias).astype(BF)
        frame = meta_ref[0] * half + r * RB + lax.broadcasted_iota(jnp.int32, (RB, starts.shape[1]), 0)
        inside = (frame >= starts) & (frame < starts + SPAN)
        weight = jnp.max(jnp.where(inside, 1.0, 0.0), axis=1, keepdims=True)
        cot = grad_ref[rows, :].astype(F32) * weight
        gain_grad = gain_grad + jnp.sum(cot * xhat, axis=0, keepdims=True)
        bias_grad = bias_grad + jnp.sum(cot, axis=0, keepdims=True)
        gy = cot * gain
        mean_gy = jnp.mean(gy, axis=-1, keepdims=True)
        mean_gx = jnp.mean(gy * xhat, axis=-1, keepdims=True)
        sum_grad = rstd * (gy - mean_gy - xhat * mean_gx)
        low = sum_grad.astype(BF)
        g_ref[rows, :] = low
        sent = jnp.zeros(sum_grad.shape, F32)
        for g, (up, down) in enumerate(((ua_ref, da_ref), (ub_ref, db_ref))):
            pres = []
            for c in range(hidden // HB):
                columns = pl.ds(g * hidden + c * HB, HB)
                slope = slope_ref[rows, columns].astype(F32)
                pres.append((nt(low, down[c * HB : (c + 1) * HB, :]) * slope).astype(BF))
                pre_ref[rows, columns] = pres[-1]
            sent = sent + nt(jnp.concatenate(pres, axis=1), up[...]).astype(BF).astype(F32)
        back_ref[rows, :] = sum_grad + sent
        sent_ref[rows, :] = sent.astype(BF)
    small_ref[0:1, :] = gain_grad
    small_ref[1:2, :] = bias_grad
    if last:
        x_ref, act_ref = before[:2]
        weight_sums(x_ref[...], g_ref[...], act_ref, pre_ref, before[2:], refs[-4:])


def astern(meta, own, far, grad, spans, up, down, slope, vectors, u, before):
    half, d = own.shape
    hidden = up[0].shape[1]
    rows = fixed(half, d)
    wide = fixed(half, 2 * hidden)
    grads = [] if not before else [(d, hidden)] * 2 + [(hidden, d)] * 2
    extra = [] if not before else [rows, wide] + [fixed(*shape) for shape in grads[: len(before) - 2]]
    return call(
        functools.partial(astern_kernel, u),
        "astern",
        (1,),
        meta,
        (own, far, grad, spans, *up, *down, slope, vectors, *before),
        [rows] * 2
        + [pl.BlockSpec((half, d), lambda i, m: (u * 2 + m[0], 0)), fixed(*spans.shape)]
        + [fixed(d, hidden)] * 2
        + [fixed(hidden, d)] * 2
        + [wide, fixed(4, d)]
        + extra,
        [rows, rows, wide, rows, rows, fixed(2, d)] + [fixed(*shape) for shape in grads],
        [
            like((half, d), BF),
            like((half, d), BF),
            like((half, 2 * hidden), BF),
            like((half, d), F32),
            like((half, d), BF),
            like((2, d), F32),
        ]
        + [like(shape, BF) for shape in grads],
        limit=28 if before else VMEM,
    )


def weight_kernel(meta_ref, x_ref, g_ref, act_ref, pre_ref, *refs):
    before, sums = refs[:-4], refs[-4:]
    weight_sums(x_ref[...], g_ref[...], act_ref, pre_ref, before, sums)


def weight_sums(x, g, act_ref, pre_ref, before, sums):
    hidden = act_ref.shape[1] // 2
    for i in range(2):
        for c in range(hidden // HB):
            columns = pl.ds(i * hidden + c * HB, HB)
            block = pl.ds(c * HB, HB)
            up = tn(x, pre_ref[:, columns])
            down = tn(act_ref[:, columns], g)
            if before:
                up = up + before[i][:, block].astype(F32)
                down = down + before[2 + i][block, :].astype(F32)
            sums[i][:, block] = up.astype(BF)
            sums[2 + i][block, :] = down.astype(BF)


def weight_grads(meta, x, g, act, pre, before):
    rows, d = x.shape
    hidden = act.shape[1] // 2
    shapes = [(d, hidden)] * 2 + [(hidden, d)] * 2
    return call(
        weight_kernel,
        "weight_grads",
        (1,),
        meta,
        (x, g, act, pre, *before),
        [fixed(rows, d)] * 2 + [fixed(rows, 2 * hidden)] * 2 + [fixed(*shape) for shape in shapes[: len(before)]],
        [fixed(*shape) for shape in shapes],
        [like(shape, BF) for shape in shapes],
        limit=24,
    )


def inner_kernel(meta_ref, own_ref, far_ref, xhat_ref, rstd_ref, vec_ref, a0, a1, w0, w1, *refs):
    last = len(refs) == 11
    out_ref, g0, g1, m0, m1, small_ref = refs[-6:]
    grad = own_ref[...] + far_ref[...].astype(F32)
    xhat = xhat_ref[...]
    gain_grad = jnp.sum(grad * xhat, axis=0, keepdims=True)
    bias_grad = jnp.sum(grad, axis=0, keepdims=True)
    gy = grad * vec_ref[0:1, :]
    mean_gy = jnp.mean(gy, axis=-1, keepdims=True)
    mean_gx = jnp.mean(gy * xhat, axis=-1, keepdims=True)
    inner = rstd_ref[:, 0:1] * (gy - mean_gy - xhat * mean_gx)
    out_ref[...] = inner
    low = inner.astype(BF)
    g0[...] = nt(w0[...], low).astype(BF)
    g1[...] = nt(w1[...], low).astype(BF)
    small = jnp.concatenate([gain_grad, bias_grad], axis=0)
    small_ref[...] = small
    if last:
        before0, before1, before_small, outer0, outer1 = refs[:5]
        below = jnp.concatenate(
            [small + before_small[...], outer0[...] + outer1[...], jnp.zeros((60, small.shape[1]), F32)], axis=0
        ).astype(BF)
        for m, a, before in ((m0, a0, before0), (m1, a1, before1)):
            m[:192, :] = (nn(a[...], low) + before[...]).astype(BF)
            m[192:, :] = below
    else:
        m0[...] = nn(a0[...], low)
        m1[...] = nn(a1[...], low)


def inner_norm(meta, own, far, xhat, rstd, vectors, att, weights, before):
    rows, d = xhat.shape
    merge = like((256, d), BF) if before else like((192, d), F32)
    return call(
        inner_kernel,
        "inner_norm",
        (1,),
        meta,
        (own, far, xhat, rstd, vectors, *att, *weights, *before),
        [fixed(rows, d)] * 3
        + [fixed(rows, 128), fixed(4, d)]
        + [fixed(192, rows)] * 2
        + [fixed(192, d)] * 2
        + ([fixed(192, d)] * 2 + [fixed(2, d)] * 3 if before else []),
        [fixed(rows, d), fixed(192, rows), fixed(192, rows), fixed(*merge.shape), fixed(*merge.shape), fixed(2, d)],
        [like((rows, d), F32), like((192, rows), BF), like((192, rows), BF), merge, merge, like((2, d), F32)],
    )


def local(groups, tokens, lengths, span_starts, wq, wk, wv, wm, wu, wd, ig, ib, og, ob, out_grad):
    rows, d = tokens.shape
    seqs = lengths.shape[0]
    frames = rows // seqs
    half = frames // 2
    core = lax.axis_index("tensor") % 2
    place_dp = lax.axis_index("dp")
    bits = groups.bit_length() - 1

    def swap(value, k):
        return lax.ppermute(value, "tensor", [(i, i ^ k) for i in range(4)])

    def swap_dp(value, k):
        return lax.ppermute(value, "dp", [(i, i ^ k) for i in range(groups)])

    def add(a, b):
        return (a.astype(F32) + b.astype(F32)).astype(BF)

    def cut(array, index, count):
        size = array.shape[0] // count
        return lax.dynamic_slice_in_dim(array, index * size, size, 0)

    def total(pieces):
        return sum(piece.astype(F32) for piece in pieces).astype(BF) if len(pieces) > 1 else pieces[0]

    class Chain:
        def __init__(self, parts, order):
            self.parts = parts
            self.steps = [(True, *stage) for stage in order] + [(False, *stage) for stage in reversed(order)]

        def start(self):
            if self.steps:
                scatter, low_bit, width = self.steps[0]
                count = 1 << width
                spot = (place_dp >> low_bit) & (count - 1)
                pick = lambda j: [cut(part, spot ^ j, count) if scatter else part for part in self.parts]
                got = [swap_dp(total(pick(j)), j << low_bit) for j in range(1, count)]
                self.pending = pick(0) + got

        def finish(self, *after):
            if not self.steps:
                return
            scatter, low_bit, width = self.steps.pop(0)
            pieces = self.pending
            if after:
                pieces = lax.optimization_barrier((*pieces, *after))[: len(pieces)]
            count = 1 << width
            spot = (place_dp >> low_bit) & (count - 1)
            if scatter:
                self.state = total(pieces)
            elif count == 2:
                one, two = pieces
                self.state = jnp.concatenate([jnp.where(spot, two, one), jnp.where(spot, one, two)], axis=0)
            else:
                size = pieces[0].shape[0]
                whole = jnp.zeros((size * count, d), BF)
                for j in range(count):
                    whole = lax.dynamic_update_slice_in_dim(whole, pieces[j], (spot ^ j) * size, 0)
                self.state = whole
            self.parts = (self.state,)

    scalars = jnp.concatenate([core.reshape(1), lengths])
    token = []

    def meta():
        return lax.optimization_barrier((scalars, *token))[0] if token else scalars

    def done(results, *others):
        token[:] = [results[0], *others]
        return results

    merge_w = (wm, swap(wm, 1), swap(wm, 2), swap(wm, 3))
    up_w = (wu, swap(wu, 1))
    down_w = (wd, swap(wd, 1))
    vectors = jnp.stack([ig, ib, og, ob])
    qkv_w = (wq.T, wk.T, wv.T)

    q, k, v = project(tokens, *qkv_w)
    fwd, att = [], []
    for u in range(seqs):
        fwd.append(done(attend_forward(meta(), q, k, v, u, frames), *merge_w[1:], up_w[1], down_w[1]))
        own, other = fwd[u][:2]
        att.append((own, swap(other, 1), swap(own, 2), swap(other, 3)))
    front, far = [], []
    for u in range(seqs):
        front.append(done(ahead(meta(), tokens, att[u], merge_w, up_w, down_w, vectors, u)))
        far.append(swap(front[u][6], 2))
    back, far_grad, sums = [], [], ()
    for u in range(seqs):
        before = (front[u][2], front[u][3], *sums) if u == seqs - 1 else ()
        back.append(
            done(astern(meta(), front[u][5], far[u], out_grad, span_starts, up_w, down_w, front[u][4], vectors, u, before))
        )
        if u < seqs - 1:
            far_grad.append(swap(back[u][4], 2))
            sums = done(weight_grads(meta(), front[u][2], back[u][1], front[u][3], back[u][2], sums))

    def inner_step(u, before):
        res = done(inner_norm(meta(), back[u][3], far_grad[u], front[u][0], front[u][1], vectors, att[u][:2], merge_w[:2], before))
        return res, (res[1], swap(res[2], 1))

    def attend_step(u, grads):
        return done(attend_backward(meta(), q, k, v, *grads, fwd[u][2], fwd[u][3], u, frames))

    def entry_step(u, grads, before, dtype):
        return done(entry_back(meta(), tokens, grads, qkv_w, before, u, frames, dtype))


    pairs = [(b, 1) for b in range(bits)]
    stages = [(0, 1)] + [(b, 2) for b in range(1, bits - 1, 2)] + ([(bits - 1, 1)] if bits % 2 == 0 else [])
    out_rows = [b[0] for b in back]
    out_other = [swap(r, 1) for r in out_rows]
    inner, near, crossed, so_far = [], [], [], ()
    ffn, chains = [], []

    def finish(group, *after):
        for chain in group:
            chain.finish(*after)
        return [chain.state for chain in group]

    def start(group):
        for chain in group:
            chain.start()

    def together(group, *others):
        values = lax.optimization_barrier((*(chain.state for chain in group), *others))
        for chain, value in zip(group, values):
            chain.state, chain.parts = value, (value,)
        return values[len(group) :]

    for u in range(seqs):
        last = u == seqs - 1
        if u == 0:
            up_own, up_other, down_own, down_other = lax.optimization_barrier((*back[-1][6:], far_grad[0]))[:4]
            ffn.append(Chain((down_own, swap(down_other, 1)), pairs))
            ffn.append(Chain((up_own, swap(up_other, 1)), pairs[1:2] + pairs[:1] + pairs[2:]))
            res, grads = inner_step(0, ())
            start(ffn)
            inner.append(res)
            far_grad.append(swap(lax.optimization_barrier((back[-1][4], res[0]))[0], 2))
            token.extend(out_other)
        dqkv = attend_step(u, grads)
        token.extend(finish(ffn + chains, dqkv[0]))
        start(ffn + chains)
        if not last:
            before = ()
            if u + 1 == seqs - 1:
                before = (inner[0][3], inner[0][4], inner[0][5], back[0][5], back[1][5])
            res, grads = inner_step(u + 1, before)
            inner.append(res)
            merge = Chain((res[3], swap(res[4], 1)), pairs)
            token.extend([grads[1], merge.parts[1]])
            merge.start()
        else:
            token.extend(crossed)
        out = entry_step(u, dqkv, so_far, BF if last else F32)
        so_far = (out[2],)
        got = swap(out[0], 1)
        if not last:
            chains.append(merge)
            finish(ffn + chains, out[0])
            (got,) = together(ffn + chains, got)
            start(ffn + chains)
            token.extend([chain.state for chain in ffn + chains])
            near.append(out[1].astype(F32) + got.astype(F32))
            crossed.append(swap(near[u].astype(BF), 2))
    qkv = Chain((so_far[0],), stages)
    qkv.start()
    finish(ffn + [merge], out[0])
    together(ffn + [merge])
    start(ffn + [merge])
    near.append(out[1].astype(F32) + got.astype(F32))
    chains = ffn + [merge, qkv]
    finish(chains)
    (arrived,) = together(chains, near[-1].astype(BF))
    crossed.append(swap(arrived, 2))
    start(chains)
    finish(chains)
    together(chains, crossed[-1])
    start(chains)
    while any(chain.steps for chain in chains):
        finish(chains)
        together(chains)
        start(chains)
    down_sum, up_sum, merge_sum, qkv_sum = (chain.state for chain in chains)

    ready = [(inner[u][0] + (near[u] + crossed[u].astype(F32))).astype(BF) for u in range(seqs)]
    layer_output = place(meta(), out_rows, out_other)
    input_grad = place(scalars, ready, [swap(r, 1) for r in ready])

    small = merge_sum[192:196].astype(F32)
    query_grad, key_grad, value_grad = (qkv_sum[192 * i : 192 * (i + 1)].astype(F32).T for i in range(3))
    return (
        layer_output,
        input_grad,
        query_grad,
        key_grad,
        value_grad,
        merge_sum[:192].astype(F32),
        up_sum.astype(F32),
        down_sum.astype(F32),
        small[0],
        small[1],
        small[2],
        small[3],
    )


def solution(mesh):
    in_specs = (
        P("dp", None),
        P("dp"),
        P("dp", None),
        P(None, "tensor"),
        P(None, "tensor"),
        P(None, "tensor"),
        P("tensor", None),
        P(None, "tensor"),
        P("tensor", None),
        P(),
        P(),
        P(),
        P(),
        P("dp", None),
    )
    out_specs = (
        P("dp", None),
        P("dp", None),
        P(None, "tensor"),
        P(None, "tensor"),
        P(None, "tensor"),
        P("tensor", None),
        P(None, "tensor"),
        P("tensor", None),
        P(),
        P(),
        P(),
        P(),
    )
    body = functools.partial(local, mesh.shape["dp"])
    return jax.shard_map(body, mesh=mesh, in_specs=in_specs, out_specs=out_specs, check_vma=False)
```

```python
import functools

import jax
import jax.numpy as jnp
from jax import lax
from jax.experimental import pallas as pl
from jax.experimental.pallas import tpu as pltpu
from jax.sharding import PartitionSpec as P

HEAD_DIM = 64
SPAN = 10
EPS = 1e-05
LOG2E = 1.4426950408889634
KB = 256
VMEM = 16
RB = 128
HB = 256
BF = jnp.bfloat16
F32 = jnp.float32
MIB = 1 << 20


def nn(a, b):
    return lax.dot_general(a, b, (((1,), (0,)), ((), ())), preferred_element_type=F32)


def nt(a, b):
    return lax.dot_general(a, b, (((1,), (1,)), ((), ())), preferred_element_type=F32)


def tn(a, b):
    return lax.dot_general(a, b, (((0,), (0,)), ((), ())), preferred_element_type=F32)


def params(limit):
    return pltpu.CompilerParams(vmem_limit_bytes=limit * MIB)


def cost(micros):
    return pl.CostEstimate(flops=int(micros * 1.1e9), bytes_accessed=1024, transcendentals=0)


MICROS = {"project": 3, "attend_forward": 8, "attend_backward": 12, "entry_back": 5, "place": 3, "ahead": 9, "astern": 10, "inner_norm": 3, "weight_grads": 5}


def lane_parts(block):
    left = block[:, :128]
    lane = lax.broadcasted_iota(jnp.int32, left.shape, 1)
    zero = jnp.zeros_like(left)
    return (
        jnp.where(lane < HEAD_DIM, left, zero),
        jnp.where(lane >= HEAD_DIM, left, zero),
        block[:, 128:],
    )


TILE = (0, 0, 1)


def call(kernel, name, grid, meta, args, in_specs, out_specs, out_shape, scratch=(), limit=VMEM, free=()):
    def place_input(i, value):
        large = value.size * value.dtype.itemsize > MIB // 4
        return pltpu.with_memory_space_constraint(value, pltpu.HBM) if large and i not in free else value

    def place_output(shape):
        large = shape.size * shape.dtype.itemsize > MIB // 4
        return pltpu.HBM(shape.shape, shape.dtype) if large else shape

    single = not isinstance(out_shape, list)
    return pl.pallas_call(
        kernel,
        grid_spec=pltpu.PrefetchScalarGridSpec(
            num_scalar_prefetch=1,
            grid=grid,
            in_specs=in_specs,
            out_specs=out_specs,
            scratch_shapes=scratch,
        ),
        out_shape=place_output(out_shape) if single else [place_output(shape) for shape in out_shape],
        compiler_params=params(limit),
        cost_estimate=cost(MICROS[name]),
        name=name,
    )(meta, *(place_input(i, value) for i, value in enumerate(args)))


def fixed(*shape):
    return pl.BlockSpec(shape, lambda *_: (0,) * len(shape))


def like(shape, dtype):
    return jax.ShapeDtypeStruct(shape, dtype)


def project_kernel(meta_ref, x_ref, wq_ref, wk_ref, wv_ref, q_ref, k_ref, v_ref):
    x = x_ref[...]
    for w_ref, o_ref in ((wq_ref, q_ref), (wk_ref, k_ref), (wv_ref, v_ref)):
        o_ref[:, :192] = nt(x, w_ref[...]).astype(BF)
        o_ref[:, 192:] = jnp.zeros((x.shape[0], HEAD_DIM), BF)


def project(meta, tokens, weights):
    rows, d = tokens.shape
    block = 512
    return call(
        project_kernel,
        "project",
        (rows // block,),
        meta,
        (tokens, *weights),
        [pl.BlockSpec((block, d), lambda i, m: (i, 0))] + [fixed(192, d)] * 3,
        [pl.BlockSpec((block, 256), lambda i, m: (i, 0))] * 3,
        [like((rows, 256), BF)] * 3,
    )


def forward_kernel(u, meta_ref, q_ref, k_ref, v_ref, own_ref, other_ref, lse_ref, s_ref):
    length = meta_ref[1 + u]
    step = pl.program_id(0)
    blocks = lax.div(length + KB - 1, KB)
    parts = lane_parts(q_ref[...] * jnp.asarray(0.125, BF))
    width = q_ref.shape[0]

    def first(kb, highest):
        start = pl.multiple_of(kb * KB, KB)
        rows = pl.ds(start, KB)
        live = start + lax.broadcasted_iota(jnp.int32, (KB, width), 0) < length
        out = []
        for h in range(3):
            tile = pl.ds(128 * TILE[h], 128)
            s = nt(k_ref[rows, tile], parts[h])
            s = jnp.where(live, s, -1e30)
            s_ref[h, rows, :] = s
            out.append(jnp.maximum(highest[h], jnp.max(s, axis=0, keepdims=True)))
        return tuple(out)

    floor = jnp.full((1, width), -1e30, F32)
    highest = lax.fori_loop(0, blocks, first, (floor,) * 3)

    def second(kb, carry):
        rows = pl.ds(pl.multiple_of(kb * KB, KB), KB)
        out = []
        for h in range(3):
            total, result = carry[h]
            p = jnp.exp2((s_ref[h, rows, :] - highest[h]) * LOG2E)
            total = total + jnp.sum(p, axis=0, keepdims=True)
            v = v_ref[rows, pl.ds(128 * TILE[h], 128)]
            result = result + tn(v, p.astype(BF))
            out.append((total, result))
        return tuple(out)

    init = ((jnp.zeros((1, width), F32), jnp.zeros((128, width), F32)),) * 3
    done = lax.fori_loop(0, blocks, second, init)
    outs = []
    for h in range(3):
        total, result = done[h]
        lo = HEAD_DIM * (h % 2)
        o = result[lo : lo + HEAD_DIM] / total
        lse_ref[0, pl.ds(h, 1), :] = highest[h] * LOG2E + jnp.log2(total)
        outs.append(o.astype(BF))
    whole = jnp.concatenate(outs, axis=0)
    for j, o_ref in enumerate((own_ref, other_ref)):

        @pl.when(step == j)
        def _():
            o_ref[...] = whole


def attend_forward(meta, q, k, v, u, frames):
    half = frames // 2
    return call(
        functools.partial(forward_kernel, u),
        "attend_forward",
        (2,),
        meta,
        (q, k, v),
        [
            pl.BlockSpec((half, 256), lambda i, m: (u * 2 + (i ^ m[0]), 0)),
            pl.BlockSpec((frames, 256), lambda i, m: (u, 0)),
            pl.BlockSpec((frames, 256), lambda i, m: (u, 0)),
        ],
        [
            fixed(192, half),
            fixed(192, half),
            pl.BlockSpec((1, 8, half), lambda i, m: (i, 0, 0)),
        ],
        [
            like((192, half), BF),
            like((192, half), BF),
            like((2, 8, half), F32),
        ],
        [pltpu.VMEM((3, frames, half), F32)],
    )


def backward_kernel(
    u, meta_ref, q_ref, k_ref, v_ref, d0_ref, d1_ref, o0_ref, o1_ref, lse_ref,
    dq_ref, dk_ref, dv_ref, kt_ref, dk_acc, dv_acc, do_ref, o_ref,
):
    length = meta_ref[1 + u]
    blocks = lax.div(length + KB - 1, KB)
    step = pl.program_id(0)

    @pl.when(step == 0)
    def _():
        dk_acc[...] = jnp.zeros_like(dk_acc)
        dv_acc[...] = jnp.zeros_like(dv_acc)
        kt_ref[...] = jnp.transpose(k_ref[...])
        do_ref[...] = d0_ref[...]
        o_ref[...] = o0_ref[...]

    @pl.when(step == 1)
    def _():
        do_ref[...] = d1_ref[...]
        o_ref[...] = o1_ref[...]

    parts = lane_parts(q_ref[...] * jnp.asarray(0.125, BF))
    width = q_ref.shape[0]
    empty = jnp.zeros((HEAD_DIM, width), BF)
    head = [do_ref[pl.ds(h * HEAD_DIM, HEAD_DIM), :] for h in range(3)]
    grads = (
        jnp.concatenate([head[0], empty], axis=0),
        jnp.concatenate([empty, head[1]], axis=0),
        jnp.concatenate([head[2], empty], axis=0),
    )
    delta = [
        jnp.sum(
            head[h].astype(F32) * o_ref[pl.ds(h * HEAD_DIM, HEAD_DIM), :].astype(F32), axis=0, keepdims=True
        )
        for h in range(3)
    ]
    lse = [lse_ref[0, pl.ds(h, 1), :] for h in range(3)]

    def body(kb, carry):
        start = pl.multiple_of(kb * KB, KB)
        rows = pl.ds(start, KB)
        live = start + lax.broadcasted_iota(jnp.int32, (KB, width), 0) < length
        out = []
        for h in range(3):
            tile = pl.ds(128 * TILE[h], 128)
            s = nt(k_ref[rows, tile], parts[h])
            s = jnp.where(live, s, -1e30)
            p = jnp.exp2(s * LOG2E - lse[h])
            dp = nn(v_ref[rows, tile], grads[h])
            ds = (p * (dp - delta[h])).astype(BF)
            dv_acc[rows, tile] += nt(p.astype(BF), grads[h])
            dk_acc[rows, tile] += nn(ds, parts[h])
            kt = kt_ref[pl.ds(h * HEAD_DIM, HEAD_DIM), rows]
            out.append(carry[h] + nn(kt, ds))
        return tuple(out)

    zero = jnp.zeros((HEAD_DIM, width), F32)
    done = lax.fori_loop(0, blocks, body, (zero,) * 3)
    full = jnp.concatenate(done + (zero,), axis=0) * 0.125
    dq_ref[...] = jnp.transpose(full).astype(BF)

    @pl.when(step == 1)
    def _():
        dk_ref[...] = dk_acc[...].astype(BF)
        dv_ref[...] = dv_acc[...].astype(BF)


def attend_backward(meta, q, k, v, grads, outs, lse, u, frames):
    half = frames // 2
    return call(
        functools.partial(backward_kernel, u),
        "attend_backward",
        (2,),
        meta,
        (q, k, v, *grads, *outs, lse),
        [
            pl.BlockSpec((half, 256), lambda i, m: (u * 2 + (i ^ m[0]), 0)),
            pl.BlockSpec((frames, 256), lambda i, m: (u, 0)),
            pl.BlockSpec((frames, 256), lambda i, m: (u, 0)),
            fixed(192, half),
            fixed(192, half),
            fixed(192, half),
            fixed(192, half),
            pl.BlockSpec((1, 8, half), lambda i, m: (i, 0, 0)),
        ],
        [
            pl.BlockSpec((half, 256), lambda i, m: (i ^ m[0], 0)),
            fixed(frames, 256),
            fixed(frames, 256),
        ],
        [like((frames, 256), BF)] * 3,
        [
            pltpu.VMEM((256, frames), BF),
            pltpu.VMEM((frames, 256), F32),
            pltpu.VMEM((frames, 256), F32),
            pltpu.VMEM((192, half), BF),
            pltpu.VMEM((192, half), BF),
        ],
    )


def entry_kernel(meta_ref, x_ref, dq_ref, dk_ref, dv_ref, wq_ref, wk_ref, wv_ref, *refs):
    before_ref = refs[0] if len(refs) == 5 else None
    send_ref, keep_ref, sum_ref, acc = refs[-4:]
    step = pl.program_id(0)
    x = x_ref[...]
    total = jnp.zeros(x.shape, F32)
    for i, (g_ref, w_ref) in enumerate(((dq_ref, wq_ref), (dk_ref, wk_ref), (dv_ref, wv_ref))):
        rows = pl.ds(192 * i, 192)
        g = g_ref[:, :192]
        total = total + nn(g, w_ref[...])
        product = tn(g, x)

        @pl.when(step == 0)
        def _():
            acc[rows, :] = product if before_ref is None else product + before_ref[rows, :]

        @pl.when(step == 1)
        def _():
            sum_ref[rows, :] = (product + acc[rows, :]).astype(sum_ref.dtype)

    low = total.astype(BF)

    @pl.when(step == 0)
    def _():
        send_ref[...] = low

    @pl.when(step == 1)
    def _():
        keep_ref[...] = low


def entry_back(meta, tokens, grads, weights, before, u, frames, dtype):
    half = frames // 2
    d = tokens.shape[1]
    return call(
        entry_kernel,
        "entry_back",
        (2,),
        meta,
        (tokens, *grads, *weights, *before),
        [pl.BlockSpec((half, d), lambda i, m: (u * 2 + (1 - i ^ m[0]), 0))]
        + [pl.BlockSpec((half, 256), lambda i, m: (1 - i ^ m[0], 0))] * 3
        + [fixed(192, d)] * 3
        + [fixed(576, d)] * len(before),
        [fixed(half, d), fixed(half, d), fixed(576, d)],
        [like((half, d), BF), like((half, d), BF), like((576, d), dtype)],
        [pltpu.VMEM((576, d), F32)],
    )


def place_kernel(meta_ref, *refs):
    o_ref = refs[-1]
    for i, r_ref in enumerate(refs[:-1]):

        @pl.when(pl.program_id(0) == i)
        def _():
            o_ref[...] = r_ref[...]


def place(meta, own, other):
    half, d = own[0].shape
    count = 2 * len(own)
    return call(
        place_kernel,
        "place",
        (count,),
        meta,
        [block for pair in zip(own, other) for block in pair],
        [fixed(half, d)] * count,
        pl.BlockSpec((half, d), lambda i, m: (i ^ m[0], 0)),
        like((count * half, d), own[0].dtype),
    )


def normalise(values):
    average = jnp.mean(values, axis=-1, keepdims=True)
    centred = values - average
    spread = jnp.mean(centred * centred, axis=-1, keepdims=True)
    rstd = lax.rsqrt(spread + EPS)
    return centred * rstd, rstd


def gelu_pair(v):
    e = jnp.exp2(v * v * (-0.5 * LOG2E))
    t = 1.0 / (1.0 + (0.3275911 * 0.7071067811865476) * jnp.abs(v))
    poly = t * (0.5 * 0.254829592 + t * (0.5 * -0.284496736 + t * (0.5 * 1.421413741 + t * (0.5 * -1.453152027 + t * (0.5 * 1.061405429)))))
    tail = poly * e
    phi_cap = jnp.where(v >= 0, 1.0 - tail, tail)
    return v * phi_cap, phi_cap + v * (e * 0.3989422804014327)


def ahead_kernel(
    meta_ref, tok_ref, a0, a1, a2, a3, w0, w1, w2, w3, ua_ref, ub_ref, da_ref, db_ref, vec_ref,
    xhat_ref, rstd_ref, low_ref, act_ref, slope_ref, own_ref, sent_ref,
):
    gain, bias = vec_ref[0:1, :], vec_ref[1:2, :]
    hidden = ua_ref.shape[1]
    branch = jnp.zeros(tok_ref.shape, F32)
    for a, w in ((a0, w0), (a1, w1), (a2, w2), (a3, w3)):
        branch = branch + tn(a[...], w[...]).astype(BF).astype(F32)
    xhat, rstd = normalise(tok_ref[...].astype(F32) + branch)
    xhat_ref[...] = xhat
    rstd_ref[...] = jnp.broadcast_to(rstd, rstd_ref.shape)
    normed = xhat * gain + bias
    low = normed.astype(BF)
    low_ref[...] = low
    sent = jnp.zeros(normed.shape, F32)
    for g, (up, down) in enumerate(((ua_ref, da_ref), (ub_ref, db_ref))):
        acts = []
        for c in range(hidden // HB):
            act, slope = gelu_pair(nn(low, up[:, c * HB : (c + 1) * HB]))
            columns = pl.ds(g * hidden + c * HB, HB)
            acts.append(act.astype(BF))
            act_ref[:, columns] = acts[-1]
            slope_ref[:, columns] = slope.astype(BF)
        sent = sent + nn(jnp.concatenate(acts, axis=1), down[...]).astype(BF).astype(F32)
    own_ref[...] = normed + sent
    sent_ref[...] = sent.astype(BF)


def rows_of(width):
    return pl.BlockSpec((RB, width), lambda i, m: (i, 0))


def ahead(meta, tokens, att, merge_w, up, down, vectors, u):
    half = att[0].shape[1]
    d, hidden = up[0].shape
    steps = half // RB
    return call(
        ahead_kernel,
        "ahead",
        (steps,),
        meta,
        (tokens, *att, *merge_w, *up, *down, vectors),
        [pl.BlockSpec((RB, d), lambda i, m: ((u * 2 + m[0]) * steps + i, 0))]
        + [pl.BlockSpec((192, RB), lambda i, m: (0, i))] * 4
        + [fixed(192, d)] * 4
        + [fixed(d, hidden)] * 2
        + [fixed(hidden, d)] * 2
        + [fixed(4, d)],
        [rows_of(d), rows_of(128), rows_of(d), rows_of(2 * hidden), rows_of(2 * hidden), rows_of(d), rows_of(d)],
        [
            like((half, d), F32),
            like((half, 128), F32),
            like((half, d), BF),
            like((half, 2 * hidden), BF),
            like((half, 2 * hidden), BF),
            like((half, d), F32),
            like((half, d), BF),
        ],
        limit=24,
        free=range(5, 13),
    )


def astern_kernel(u, meta_ref, own_ref, far_ref, grad_ref, span_ref, ua_ref, ub_ref, da_ref, db_ref, slope_ref, vec_ref, *refs):
    last = len(refs) > 7
    before = refs[: len(refs) - 12] if last else ()
    out_ref, g_ref, pre_ref, back_ref, sent_ref, small_ref = refs[len(before) : len(before) + 6]
    step = pl.program_id(0)
    gain, bias = vec_ref[2:3, :], vec_ref[3:4, :]
    hidden = ua_ref.shape[1]
    starts = span_ref[u : u + 1, :]
    xhat, rstd = normalise(own_ref[...] + far_ref[...].astype(F32))
    out_ref[...] = (xhat * gain + bias).astype(BF)
    first = (meta_ref[0] * pl.num_programs(0) + step) * RB
    frame = first + lax.broadcasted_iota(jnp.int32, (RB, starts.shape[1]), 0)
    inside = (frame >= starts) & (frame < starts + SPAN)
    weight = jnp.max(jnp.where(inside, 1.0, 0.0), axis=1, keepdims=True)
    cot = grad_ref[...].astype(F32) * weight
    gain_grad = jnp.sum(cot * xhat, axis=0, keepdims=True)
    bias_grad = jnp.sum(cot, axis=0, keepdims=True)
    gy = cot * gain
    mean_gy = jnp.mean(gy, axis=-1, keepdims=True)
    mean_gx = jnp.mean(gy * xhat, axis=-1, keepdims=True)
    sum_grad = rstd * (gy - mean_gy - xhat * mean_gx)
    low = sum_grad.astype(BF)
    g_ref[...] = low
    sent = jnp.zeros(sum_grad.shape, F32)
    pres = []
    for g, (up, down) in enumerate(((ua_ref, da_ref), (ub_ref, db_ref))):
        for c in range(hidden // HB):
            columns = pl.ds(g * hidden + c * HB, HB)
            slope = slope_ref[:, columns].astype(F32)
            pres.append((nt(low, down[c * HB : (c + 1) * HB, :]) * slope).astype(BF))
            pre_ref[:, columns] = pres[-1]
        group = jnp.concatenate(pres[g * (hidden // HB) :], axis=1)
        sent = sent + nt(group, up[...]).astype(BF).astype(F32)
    back_ref[...] = sum_grad + sent
    sent_ref[...] = sent.astype(BF)

    @pl.when(step == 0)
    def _():
        small_ref[0:1, :] = gain_grad
        small_ref[1:2, :] = bias_grad

    @pl.when(step > 0)
    def _():
        small_ref[0:1, :] += gain_grad
        small_ref[1:2, :] += bias_grad

    if last:
        x_ref, act_ref = before[:2]
        all_g, all_pre = refs[-2:]
        rows = pl.ds(pl.multiple_of(step * RB, RB), RB)
        all_g[rows, :] = low
        all_pre[rows, :] = jnp.concatenate(pres, axis=1)

        @pl.when(step == pl.num_programs(0) - 1)
        def _():
            weight_sums(x_ref[...], all_g[...], act_ref, all_pre, before[2:], refs[-6:-2])


def astern(meta, own, far, grad, spans, up, down, slope, vectors, u, before):
    half, d = own.shape
    hidden = up[0].shape[1]
    steps = half // RB
    wide = 2 * hidden
    grads = [] if not before else [(d, hidden)] * 2 + [(hidden, d)] * 2
    extra = [] if not before else [fixed(half, d), fixed(half, wide)] + [fixed(*shape) for shape in grads[: len(before) - 2]]
    return call(
        functools.partial(astern_kernel, u),
        "astern",
        (steps,),
        meta,
        (own, far, grad, spans, *up, *down, slope, vectors, *before),
        [rows_of(d), rows_of(d), pl.BlockSpec((RB, d), lambda i, m: ((u * 2 + m[0]) * steps + i, 0)), fixed(*spans.shape)]
        + [fixed(d, hidden)] * 2
        + [fixed(hidden, d)] * 2
        + [rows_of(wide), fixed(4, d)]
        + extra,
        [rows_of(d), rows_of(d), rows_of(wide), rows_of(d), rows_of(d), fixed(2, d)] + [fixed(*shape) for shape in grads],
        [
            like((half, d), BF),
            like((half, d), BF),
            like((half, wide), BF),
            like((half, d), F32),
            like((half, d), BF),
            like((2, d), F32),
        ]
        + [like(shape, BF) for shape in grads],
        [pltpu.VMEM((half, d), BF), pltpu.VMEM((half, wide), BF)] if before else [pltpu.VMEM((8, 128), F32)],
        limit=44 if before else 24,
        free=(4, 5, 6, 7, *range(12, 16)),
    )


def weight_sums(x, g, act_ref, pre_ref, before, sums):
    hidden = act_ref.shape[1] // 2
    for i in range(2):
        for c in range(hidden // HB):
            columns = pl.ds(i * hidden + c * HB, HB)
            block = pl.ds(c * HB, HB)
            up = tn(x, pre_ref[:, columns])
            down = tn(act_ref[:, columns], g)
            if before:
                up = up + before[i][:, block].astype(F32)
                down = down + before[2 + i][block, :].astype(F32)
            sums[i][:, block] = up.astype(BF)
            sums[2 + i][block, :] = down.astype(BF)


def weight_kernel(per, meta_ref, x_ref, g_ref, act_ref, pre_ref, *refs):
    step = pl.program_id(0)
    before, sums = refs[:-4], refs[-4:]
    up = tn(x_ref[...], pre_ref[...])
    down = tn(act_ref[...], g_ref[...])
    for i in range(2):

        @pl.when((step >= i * per) & (step < (i + 1) * per))
        def _():
            if before:
                sums[i][...] = (up + before[i][...].astype(F32)).astype(BF)
                sums[2 + i][...] = (down + before[2 + i][...].astype(F32)).astype(BF)
            else:
                sums[i][...] = up.astype(BF)
                sums[2 + i][...] = down.astype(BF)


def weight_grads(meta, x, g, act, pre, before):
    rows, d = x.shape
    hidden = act.shape[1] // 2
    per = hidden // HB

    def at(group, i):
        return jnp.minimum(i, per - 1) if group == 0 else jnp.maximum(i - per, 0)

    blocks = [pl.BlockSpec((d, HB), lambda i, m, g=g: (0, at(g, i))) for g in range(2)]
    blocks += [pl.BlockSpec((HB, d), lambda i, m, g=g: (at(g, i), 0)) for g in range(2)]
    return call(
        functools.partial(weight_kernel, per),
        "weight_grads",
        (2 * per,),
        meta,
        (x, g, act, pre, *before),
        [fixed(rows, d)] * 2 + [pl.BlockSpec((rows, HB), lambda i, m: (0, i))] * 2 + blocks[: len(before)],
        blocks,
        [like((d, hidden), BF)] * 2 + [like((hidden, d), BF)] * 2,
    )


def inner_kernel(meta_ref, own_ref, far_ref, xhat_ref, rstd_ref, vec_ref, a0, a1, w0, w1, *refs):
    last = len(refs) == 14
    out_ref, g0, g1, m0, m1, small_ref, acc0, acc1, acc_small = refs[-9:]
    step = pl.program_id(0)
    grad = own_ref[...] + far_ref[...].astype(F32)
    xhat = xhat_ref[...]
    gain_grad = jnp.sum(grad * xhat, axis=0, keepdims=True)
    bias_grad = jnp.sum(grad, axis=0, keepdims=True)
    gy = grad * vec_ref[0:1, :]
    mean_gy = jnp.mean(gy, axis=-1, keepdims=True)
    mean_gx = jnp.mean(gy * xhat, axis=-1, keepdims=True)
    inner = rstd_ref[:, 0:1] * (gy - mean_gy - xhat * mean_gx)
    out_ref[...] = inner
    low = inner.astype(BF)
    g0[...] = nt(w0[...], low).astype(BF)
    g1[...] = nt(w1[...], low).astype(BF)
    merge0, merge1 = nn(a0[...], low), nn(a1[...], low)

    @pl.when(step == 0)
    def _():
        if last:
            acc0[...] = merge0 + refs[0][...]
            acc1[...] = merge1 + refs[1][...]
            acc_small[0:1, :] = gain_grad + refs[2][0:1, :]
            acc_small[1:2, :] = bias_grad + refs[2][1:2, :]
        else:
            acc0[...] = merge0
            acc1[...] = merge1
            acc_small[0:1, :] = gain_grad
            acc_small[1:2, :] = bias_grad

    @pl.when(step > 0)
    def _():
        acc0[...] += merge0
        acc1[...] += merge1
        acc_small[0:1, :] += gain_grad
        acc_small[1:2, :] += bias_grad

    @pl.when(step == pl.num_programs(0) - 1)
    def _():
        small = acc_small[0:2, :]
        small_ref[...] = small
        if last:
            zeros = jnp.zeros((60, small.shape[1]), F32)
            below = jnp.concatenate([small, refs[3][...] + refs[4][...], zeros], axis=0).astype(BF)
            for m, acc in ((m0, acc0), (m1, acc1)):
                m[:192, :] = acc[...].astype(BF)
                m[192:, :] = below
        else:
            m0[...] = acc0[...]
            m1[...] = acc1[...]


def inner_norm(meta, own, far, xhat, rstd, vectors, att, weights, before):
    rows, d = xhat.shape
    merge = like((256, d), BF) if before else like((192, d), F32)
    lanes = pl.BlockSpec((192, RB), lambda i, m: (0, i))
    return call(
        inner_kernel,
        "inner_norm",
        (rows // RB,),
        meta,
        (own, far, xhat, rstd, vectors, *att, *weights, *before),
        [rows_of(d)] * 3
        + [rows_of(128), fixed(4, d)]
        + [lanes] * 2
        + [fixed(192, d)] * 2
        + ([fixed(192, d)] * 2 + [fixed(2, d)] * 3 if before else []),
        [rows_of(d), lanes, lanes, fixed(*merge.shape), fixed(*merge.shape), fixed(2, d)],
        [like((rows, d), F32), like((192, rows), BF), like((192, rows), BF), merge, merge, like((2, d), F32)],
        [pltpu.VMEM((192, d), F32)] * 2 + [pltpu.VMEM((8, d), F32)],
        free=(7, 8),
    )


def local(groups, tokens, lengths, span_starts, wq, wk, wv, wm, wu, wd, ig, ib, og, ob, out_grad):
    rows, d = tokens.shape
    seqs = lengths.shape[0]
    frames = rows // seqs
    half = frames // 2
    core = lax.axis_index("tensor") % 2
    place_dp = lax.axis_index("dp")
    bits = groups.bit_length() - 1

    def swap(value, k):
        return lax.ppermute(value, "tensor", [(i, i ^ k) for i in range(4)])

    def swap_dp(value, k):
        return lax.ppermute(value, "dp", [(i, i ^ k) for i in range(groups)])

    def add(a, b):
        return (a.astype(F32) + b.astype(F32)).astype(BF)

    def cut(array, index, count):
        size = array.shape[0] // count
        return lax.dynamic_slice_in_dim(array, index * size, size, 0)

    def total(pieces):
        return sum(piece.astype(F32) for piece in pieces).astype(BF) if len(pieces) > 1 else pieces[0]

    class Chain:
        def __init__(self, parts, order, back=None):
            self.parts = parts
            self.order = order
            self.held = list(order)
            self.steps = [(True, *stage) for stage in order] + [(False, *stage) for stage in back or reversed(order)]

        def start(self):
            if self.steps:
                scatter, low_bit, width = self.steps[0]
                count = 1 << width
                spot = (place_dp >> low_bit) & (count - 1)
                pick = lambda j: total([cut(part, spot ^ j, count) if scatter else part for part in self.parts])
                self.pending = [swap_dp(pick(j), j << low_bit) for j in range(1, count)]

        def finish(self, *after):
            if not self.steps:
                return
            scatter, low_bit, width = self.steps.pop(0)
            got = self.pending
            if after:
                got = list(lax.optimization_barrier((*got, *after))[: len(got)])
            count = 1 << width
            spot = (place_dp >> low_bit) & (count - 1)
            if scatter:
                self.state = total([cut(part, spot, count) for part in self.parts] + got)
                if all(step[0] is False for step in self.steps):
                    self.state = self.state.reshape((1,) * len(self.order) + self.state.shape)
            else:
                axis = self.order.index((low_bit, width))
                mine = self.parts[0]
                if count == 2:
                    halves = [jnp.where(spot, got[0], mine), jnp.where(spot, mine, got[0])]
                    self.state = jnp.concatenate(halves, axis=axis)
                else:
                    whole = jnp.zeros(mine.shape[:axis] + (count,) + mine.shape[axis + 1 :], BF)
                    for j, piece in enumerate([mine] + got):
                        whole = lax.dynamic_update_slice_in_dim(whole, piece, spot ^ j, axis)
                    self.state = whole
                if not self.steps:
                    self.state = self.state.reshape(-1, d)
            self.parts = (self.state,)

    scalars = jnp.concatenate([core.reshape(1), lengths])
    token = []

    def meta():
        return lax.optimization_barrier((scalars, *token))[0] if token else scalars

    def done(results, *others):
        token[:] = [results[0], *others]
        return results

    merge_w = (wm, swap(wm, 1), swap(wm, 2), swap(wm, 3))
    up_w = (wu, swap(wu, 1))
    down_w = (wd, swap(wd, 1))
    vectors = jnp.stack([ig, ib, og, ob])
    qkv_w = (wq.T, wk.T, wv.T)

    q, k, v = project(scalars, tokens, qkv_w)
    fwd, att = [], []
    for u in range(seqs):
        fwd.append(done(attend_forward(meta(), q, k, v, u, frames), *merge_w[1:], up_w[1], down_w[1]))
        own, other = fwd[u][:2]
        att.append((own, swap(other, 1), swap(own, 2), swap(other, 3)))
    front, far = [], []
    for u in range(seqs):
        front.append(done(ahead(meta(), tokens, att[u], merge_w, up_w, down_w, vectors, u)))
        far.append(swap(front[u][6], 2))
    back, far_grad, sums = [], [], ()
    for u in range(seqs):
        before = (front[u][2], front[u][3], *sums) if u == seqs - 1 else ()
        back.append(
            done(astern(meta(), front[u][5], far[u], out_grad, span_starts, up_w, down_w, front[u][4], vectors, u, before))
        )
        if u < seqs - 1:
            far_grad.append(swap(back[u][4], 2))
            sums = done(weight_grads(meta(), front[u][2], back[u][1], front[u][3], back[u][2], sums))

    def inner_step(u, before):
        res = done(inner_norm(meta(), back[u][3], far_grad[u], front[u][0], front[u][1], vectors, att[u][:2], merge_w[:2], before))
        return res, (res[1], swap(res[2], 1))

    def attend_step(u, grads):
        return done(attend_backward(meta(), q, k, v, grads, fwd[u][:2], fwd[u][2], u, frames))

    def entry_step(u, grads, before, dtype):
        return done(entry_back(meta(), tokens, grads, qkv_w, before, u, frames, dtype))


    pairs = [(b, 1) for b in range(bits)]
    stages = [(0, 1)] + [(b, 2) for b in range(1, bits - 1, 2)] + ([(bits - 1, 1)] if bits % 2 == 0 else [])
    out_rows = [b[0] for b in back]
    out_other = [swap(r, 1) for r in out_rows]
    inner, near, crossed, so_far = [], [], [], ()
    ffn, chains = [], []

    def finish(group, *after):
        for chain in group:
            chain.finish(*after)
        return [chain.state for chain in group]

    def start(group):
        for chain in group:
            chain.start()

    def together(group, *others):
        values = lax.optimization_barrier((*(chain.state for chain in group), *others))
        for chain, value in zip(group, values):
            chain.state, chain.parts = value, (value,)
        return values[len(group) :]

    for u in range(seqs):
        last = u == seqs - 1
        if u == 0:
            up_own, up_other, down_own, down_other = lax.optimization_barrier((*back[-1][6:], far_grad[0]))[:4]
            ffn.append(Chain((down_own, swap(down_other, 1)), pairs))
            ffn.append(Chain((up_own, swap(up_other, 1)), pairs[1:2] + pairs[:1] + pairs[2:], pairs[::-1]))
            res, grads = inner_step(0, ())
            start(ffn)
            inner.append(res)
            far_grad.append(swap(lax.optimization_barrier((back[-1][4], res[0]))[0], 2))
            token.extend(out_other)
        dqkv = attend_step(u, grads)
        token.extend(finish(ffn + chains, dqkv[0]))
        start(ffn + chains)
        if not last:
            before = ()
            if u + 1 == seqs - 1:
                before = (inner[0][3], inner[0][4], inner[0][5], back[0][5], back[1][5])
            res, grads = inner_step(u + 1, before)
            inner.append(res)
            merge = Chain((res[3], swap(res[4], 1)), pairs)
            token.extend([grads[1], merge.parts[1]])
            merge.start()
        else:
            token.extend(crossed)
        out = entry_step(u, dqkv, so_far, BF if last else F32)
        so_far = (out[2],)
        got = swap(out[0], 1)
        if not last:
            chains.append(merge)
            finish(ffn + chains, out[0])
            (got,) = together(ffn + chains, got)
            start(ffn + chains)
            token.extend([chain.state for chain in ffn + chains])
            near.append(out[1].astype(F32) + got.astype(F32))
            crossed.append(swap(near[u].astype(BF), 2))
    qkv = Chain((so_far[0],), stages)
    qkv.start()
    finish(ffn + [merge], out[0])
    together(ffn + [merge])
    start(ffn + [merge])
    near.append(out[1].astype(F32) + got.astype(F32))
    chains = ffn + [merge, qkv]
    finish(chains)
    (arrived,) = together(chains, near[-1].astype(BF))
    crossed.append(swap(arrived, 2))
    start(chains)
    finish(chains)
    together(chains, crossed[-1])
    start(chains)
    while any(chain.steps for chain in chains):
        finish(chains)
        together(chains)
        start(chains)
    down_sum, up_sum, merge_sum, qkv_sum = (chain.state for chain in chains)

    ready = [(inner[u][0] + (near[u] + crossed[u].astype(F32))).astype(BF) for u in range(seqs)]
    layer_output = place(meta(), out_rows, out_other)
    input_grad = place(scalars, ready, [swap(r, 1) for r in ready])

    small = merge_sum[192:196].astype(F32)
    query_grad, key_grad, value_grad = (qkv_sum[192 * i : 192 * (i + 1)].astype(F32).T for i in range(3))
    return (
        layer_output,
        input_grad,
        query_grad,
        key_grad,
        value_grad,
        merge_sum[:192].astype(F32),
        up_sum.astype(F32),
        down_sum.astype(F32),
        small[0],
        small[1],
        small[2],
        small[3],
    )


def solution(mesh):
    in_specs = (
        P("dp", None),
        P("dp"),
        P("dp", None),
        P(None, "tensor"),
        P(None, "tensor"),
        P(None, "tensor"),
        P("tensor", None),
        P(None, "tensor"),
        P("tensor", None),
        P(),
        P(),
        P(),
        P(),
        P("dp", None),
    )
    out_specs = (
        P("dp", None),
        P("dp", None),
        P(None, "tensor"),
        P(None, "tensor"),
        P(None, "tensor"),
        P("tensor", None),
        P(None, "tensor"),
        P("tensor", None),
        P(),
        P(),
        P(),
        P(),
    )
    body = functools.partial(local, mesh.shape["dp"])
    return jax.shard_map(body, mesh=mesh, in_specs=in_specs, out_specs=out_specs, check_vma=False)
```

```python
import functools

import jax
import jax.numpy as jnp
from jax import lax
from jax.experimental import pallas as pl
from jax.experimental.pallas import tpu as pltpu
from jax.sharding import PartitionSpec as P

HEAD_DIM = 64
SPAN = 10
EPS = 1e-05
LOG2E = 1.4426950408889634
KB = 256
VMEM = 16
RB = 128
HB = 256
BF = jnp.bfloat16
F32 = jnp.float32
MIB = 1 << 20


def nn(a, b):
    return lax.dot_general(a, b, (((1,), (0,)), ((), ())), preferred_element_type=F32)


def nt(a, b):
    return lax.dot_general(a, b, (((1,), (1,)), ((), ())), preferred_element_type=F32)


def tn(a, b):
    return lax.dot_general(a, b, (((0,), (0,)), ((), ())), preferred_element_type=F32)


def params(limit):
    return pltpu.CompilerParams(vmem_limit_bytes=limit * MIB)


def cost(micros):
    return pl.CostEstimate(flops=int(micros * 1.1e9), bytes_accessed=1024, transcendentals=0)


MICROS = {"project": 3, "attend_forward": 8, "attend_backward": 12, "entry_back": 5, "place": 3, "ahead": 9, "astern": 10, "inner_norm": 3, "weight_grads": 5}


def lane_parts(block):
    left = block[:, :128]
    lane = lax.broadcasted_iota(jnp.int32, left.shape, 1)
    zero = jnp.zeros_like(left)
    return (
        jnp.where(lane < HEAD_DIM, left, zero),
        jnp.where(lane >= HEAD_DIM, left, zero),
        block[:, 128:],
    )


TILE = (0, 0, 1)


def call(kernel, name, grid, meta, args, in_specs, out_specs, out_shape, scratch=(), limit=VMEM, hold=(), out=()):
    args = list(args)
    for i in hold:
        space = pltpu.VMEM if i >= 0 else pltpu.HBM
        spot = i if i >= 0 else -1 - i
        args[spot] = pltpu.with_memory_space_constraint(args[spot], space)
    if isinstance(out_shape, list):
        out_shape = [pltpu.VMEM(o.shape, o.dtype) if i in out else o for i, o in enumerate(out_shape)]
    return pl.pallas_call(
        kernel,
        grid_spec=pltpu.PrefetchScalarGridSpec(
            num_scalar_prefetch=1,
            grid=grid,
            in_specs=in_specs,
            out_specs=out_specs,
            scratch_shapes=scratch,
        ),
        out_shape=out_shape,
        compiler_params=params(limit),
        cost_estimate=cost(MICROS[name]),
        name=name,
    )(meta, *args)


def fixed(*shape):
    return pl.BlockSpec(shape, lambda *_: (0,) * len(shape))


def like(shape, dtype):
    return jax.ShapeDtypeStruct(shape, dtype)


def project_kernel(meta_ref, x_ref, wq_ref, wk_ref, wv_ref, q_ref, k_ref, v_ref):
    x = x_ref[...]
    for w_ref, o_ref in ((wq_ref, q_ref), (wk_ref, k_ref), (wv_ref, v_ref)):
        o_ref[:, :192] = nt(x, w_ref[...]).astype(BF)
        o_ref[:, 192:] = jnp.zeros((x.shape[0], HEAD_DIM), BF)


def project(meta, tokens, weights):
    rows, d = tokens.shape
    block = 256
    return call(
        project_kernel,
        "project",
        (rows // block,),
        meta,
        (tokens, *weights),
        [pl.BlockSpec((block, d), lambda i, m: (i, 0))] + [fixed(192, d)] * 3,
        [pl.BlockSpec((block, 256), lambda i, m: (i, 0))] * 3,
        [like((rows, 256), BF)] * 3,
        hold=(-1, -2, -3, -4),
        out=(0, 1, 2),
    )


def forward_kernel(u, meta_ref, q_ref, k_ref, v_ref, own_ref, other_ref, lse_ref, s_ref):
    length = meta_ref[1 + u]
    step = pl.program_id(0)
    blocks = lax.div(length + KB - 1, KB)
    parts = lane_parts(q_ref[...] * jnp.asarray(0.125, BF))
    width = q_ref.shape[0]

    def first(kb, highest):
        start = pl.multiple_of(kb * KB, KB)
        rows = pl.ds(start, KB)
        live = start + lax.broadcasted_iota(jnp.int32, (KB, width), 0) < length
        out = []
        for h in range(3):
            tile = pl.ds(128 * TILE[h], 128)
            s = nt(k_ref[rows, tile], parts[h])
            s = jnp.where(live, s, -1e30)
            s_ref[h, rows, :] = s
            out.append(jnp.maximum(highest[h], jnp.max(s, axis=0, keepdims=True)))
        return tuple(out)

    floor = jnp.full((1, width), -1e30, F32)
    highest = lax.fori_loop(0, blocks, first, (floor,) * 3)

    def second(kb, carry):
        rows = pl.ds(pl.multiple_of(kb * KB, KB), KB)
        out = []
        for h in range(3):
            total, result = carry[h]
            p = jnp.exp2((s_ref[h, rows, :] - highest[h]) * LOG2E)
            total = total + jnp.sum(p, axis=0, keepdims=True)
            v = v_ref[rows, pl.ds(128 * TILE[h], 128)]
            result = result + tn(v, p.astype(BF))
            out.append((total, result))
        return tuple(out)

    init = ((jnp.zeros((1, width), F32), jnp.zeros((128, width), F32)),) * 3
    done = lax.fori_loop(0, blocks, second, init)
    outs = []
    for h in range(3):
        total, result = done[h]
        lo = HEAD_DIM * (h % 2)
        o = result[lo : lo + HEAD_DIM] / total
        lse_ref[0, pl.ds(h, 1), :] = highest[h] * LOG2E + jnp.log2(total)
        outs.append(o.astype(BF))
    whole = jnp.concatenate(outs, axis=0)
    for j, o_ref in enumerate((own_ref, other_ref)):

        @pl.when(step == j)
        def _():
            o_ref[...] = whole


def attend_forward(meta, q, k, v, u, frames):
    half = frames // 2
    return call(
        functools.partial(forward_kernel, u),
        "attend_forward",
        (2,),
        meta,
        (q, k, v),
        [
            pl.BlockSpec((half, 256), lambda i, m: (u * 2 + (i ^ m[0]), 0)),
            pl.BlockSpec((frames, 256), lambda i, m: (u, 0)),
            pl.BlockSpec((frames, 256), lambda i, m: (u, 0)),
        ],
        [
            fixed(192, half),
            fixed(192, half),
            pl.BlockSpec((1, 8, half), lambda i, m: (i, 0, 0)),
        ],
        [
            like((192, half), BF),
            like((192, half), BF),
            like((2, 8, half), F32),
        ],
        [pltpu.VMEM((3, frames, half), F32)],
        hold=(0, 1, 2),
        out=(2,),
    )


def backward_kernel(
    u, meta_ref, q_ref, k_ref, v_ref, d0_ref, d1_ref, o0_ref, o1_ref, lse_ref,
    dq_ref, dk_ref, dv_ref, kt_ref, dk_acc, dv_acc, do_ref, o_ref,
):
    length = meta_ref[1 + u]
    blocks = lax.div(length + KB - 1, KB)
    step = pl.program_id(0)

    @pl.when(step == 0)
    def _():
        dk_acc[...] = jnp.zeros_like(dk_acc)
        dv_acc[...] = jnp.zeros_like(dv_acc)
        kt_ref[...] = jnp.transpose(k_ref[...])
        do_ref[...] = d0_ref[...]
        o_ref[...] = o0_ref[...]

    @pl.when(step == 1)
    def _():
        do_ref[...] = d1_ref[...]
        o_ref[...] = o1_ref[...]

    parts = lane_parts(q_ref[...] * jnp.asarray(0.125, BF))
    width = q_ref.shape[0]
    empty = jnp.zeros((HEAD_DIM, width), BF)
    head = [do_ref[pl.ds(h * HEAD_DIM, HEAD_DIM), :] for h in range(3)]
    grads = (
        jnp.concatenate([head[0], empty], axis=0),
        jnp.concatenate([empty, head[1]], axis=0),
        jnp.concatenate([head[2], empty], axis=0),
    )
    delta = [
        jnp.sum(
            head[h].astype(F32) * o_ref[pl.ds(h * HEAD_DIM, HEAD_DIM), :].astype(F32), axis=0, keepdims=True
        )
        for h in range(3)
    ]
    lse = [lse_ref[0, pl.ds(h, 1), :] for h in range(3)]

    def body(kb, carry):
        start = pl.multiple_of(kb * KB, KB)
        rows = pl.ds(start, KB)
        live = start + lax.broadcasted_iota(jnp.int32, (KB, width), 0) < length
        out = []
        for h in range(3):
            tile = pl.ds(128 * TILE[h], 128)
            s = nt(k_ref[rows, tile], parts[h])
            s = jnp.where(live, s, -1e30)
            p = jnp.exp2(s * LOG2E - lse[h])
            dp = nn(v_ref[rows, tile], grads[h])
            ds = (p * (dp - delta[h])).astype(BF)
            dv_acc[rows, tile] += nt(p.astype(BF), grads[h])
            dk_acc[rows, tile] += nn(ds, parts[h])
            kt = kt_ref[pl.ds(h * HEAD_DIM, HEAD_DIM), rows]
            out.append(carry[h] + nn(kt, ds))
        return tuple(out)

    zero = jnp.zeros((HEAD_DIM, width), F32)
    done = lax.fori_loop(0, blocks, body, (zero,) * 3)
    full = jnp.concatenate(done + (zero,), axis=0) * 0.125
    dq_ref[...] = jnp.transpose(full).astype(BF)

    @pl.when(step == 1)
    def _():
        dk_ref[...] = dk_acc[...].astype(BF)
        dv_ref[...] = dv_acc[...].astype(BF)


def attend_backward(meta, q, k, v, grads, outs, lse, u, frames):
    half = frames // 2
    return call(
        functools.partial(backward_kernel, u),
        "attend_backward",
        (2,),
        meta,
        (q, k, v, *grads, *outs, lse),
        [
            pl.BlockSpec((half, 256), lambda i, m: (u * 2 + (i ^ m[0]), 0)),
            pl.BlockSpec((frames, 256), lambda i, m: (u, 0)),
            pl.BlockSpec((frames, 256), lambda i, m: (u, 0)),
            fixed(192, half),
            fixed(192, half),
            fixed(192, half),
            fixed(192, half),
            pl.BlockSpec((1, 8, half), lambda i, m: (i, 0, 0)),
        ],
        [
            pl.BlockSpec((half, 256), lambda i, m: (i ^ m[0], 0)),
            fixed(frames, 256),
            fixed(frames, 256),
        ],
        [like((frames, 256), BF)] * 3,
        [
            pltpu.VMEM((256, frames), BF),
            pltpu.VMEM((frames, 256), F32),
            pltpu.VMEM((frames, 256), F32),
            pltpu.VMEM((192, half), BF),
            pltpu.VMEM((192, half), BF),
        ],
        hold=(0, 1, 2, 7),
        out=(0, 1, 2),
    )


def entry_kernel(meta_ref, x_ref, dq_ref, dk_ref, dv_ref, wq_ref, wk_ref, wv_ref, *refs):
    before_ref = refs[0] if len(refs) == 5 else None
    send_ref, keep_ref, sum_ref, acc = refs[-4:]
    step = pl.program_id(0)
    x = x_ref[...]
    total = jnp.zeros(x.shape, F32)
    for i, (g_ref, w_ref) in enumerate(((dq_ref, wq_ref), (dk_ref, wk_ref), (dv_ref, wv_ref))):
        rows = pl.ds(192 * i, 192)
        g = g_ref[:, :192]
        total = total + nn(g, w_ref[...])
        product = tn(g, x)

        @pl.when(step == 0)
        def _():
            acc[rows, :] = product if before_ref is None else product + before_ref[rows, :]

        @pl.when(step == 1)
        def _():
            sum_ref[rows, :] = (product + acc[rows, :]).astype(sum_ref.dtype)

    low = total.astype(BF)

    @pl.when(step == 0)
    def _():
        send_ref[...] = low

    @pl.when(step == 1)
    def _():
        keep_ref[...] = low


def entry_back(meta, tokens, grads, weights, before, u, frames, dtype):
    half = frames // 2
    d = tokens.shape[1]
    return call(
        entry_kernel,
        "entry_back",
        (2,),
        meta,
        (tokens, *grads, *weights, *before),
        [pl.BlockSpec((half, d), lambda i, m: (u * 2 + (1 - i ^ m[0]), 0))]
        + [pl.BlockSpec((half, 256), lambda i, m: (1 - i ^ m[0], 0))] * 3
        + [fixed(192, d)] * 3
        + [fixed(576, d)] * len(before),
        [fixed(half, d), fixed(half, d), fixed(576, d)],
        [like((half, d), BF), like((half, d), BF), like((576, d), dtype)],
        [pltpu.VMEM((576, d), F32)],
        hold=(-1, 1, 2, 3, -5, -6, -7),
    )


def place_kernel(meta_ref, *refs):
    o_ref = refs[-1]
    for i, r_ref in enumerate(refs[:-1]):

        @pl.when(pl.program_id(0) == i)
        def _():
            o_ref[...] = r_ref[...]


def place(meta, own, other):
    half, d = own[0].shape
    count = 2 * len(own)
    return call(
        place_kernel,
        "place",
        (count,),
        meta,
        [block for pair in zip(own, other) for block in pair],
        [fixed(half, d)] * count,
        pl.BlockSpec((half, d), lambda i, m: (i ^ m[0], 0)),
        like((count * half, d), own[0].dtype),
    )


def normalise(values):
    average = jnp.mean(values, axis=-1, keepdims=True)
    centred = values - average
    spread = jnp.mean(centred * centred, axis=-1, keepdims=True)
    rstd = lax.rsqrt(spread + EPS)
    return centred * rstd, rstd


def gelu_pair(v):
    e = jnp.exp2(v * v * (-0.5 * LOG2E))
    t = 1.0 / (1.0 + (0.3275911 * 0.7071067811865476) * jnp.abs(v))
    poly = t * (0.5 * 0.254829592 + t * (0.5 * -0.284496736 + t * (0.5 * 1.421413741 + t * (0.5 * -1.453152027 + t * (0.5 * 1.061405429)))))
    tail = poly * e
    phi_cap = jnp.where(v >= 0, 1.0 - tail, tail)
    return v * phi_cap, phi_cap + v * (e * 0.3989422804014327)


def ahead_kernel(
    meta_ref, tok_ref, a0, a1, a2, a3, w0, w1, w2, w3, ua_ref, ub_ref, da_ref, db_ref, vec_ref,
    xhat_ref, rstd_ref, low_ref, act_ref, slope_ref, own_ref, sent_ref,
):
    gain, bias = vec_ref[0:1, :], vec_ref[1:2, :]
    hidden = ua_ref.shape[1]
    for r in range(tok_ref.shape[0] // RB):
        rows = pl.ds(r * RB, RB)
        branch = jnp.zeros((RB, tok_ref.shape[1]), F32)
        for a, w in ((a0, w0), (a1, w1), (a2, w2), (a3, w3)):
            branch = branch + tn(a[:, rows], w[...]).astype(BF).astype(F32)
        xhat, rstd = normalise(tok_ref[rows, :].astype(F32) + branch)
        xhat_ref[rows, :] = xhat
        rstd_ref[rows, :] = jnp.broadcast_to(rstd, (RB, rstd_ref.shape[1]))
        normed = xhat * gain + bias
        low = normed.astype(BF)
        low_ref[rows, :] = low
        sent = jnp.zeros(normed.shape, F32)
        for g, (up, down) in enumerate(((ua_ref, da_ref), (ub_ref, db_ref))):
            acts = []
            for c in range(hidden // HB):
                act, slope = gelu_pair(nn(low, up[:, c * HB : (c + 1) * HB]))
                columns = pl.ds(g * hidden + c * HB, HB)
                acts.append(act.astype(BF))
                act_ref[rows, columns] = acts[-1]
                slope_ref[rows, columns] = slope.astype(BF)
            sent = sent + nn(jnp.concatenate(acts, axis=1), down[...]).astype(BF).astype(F32)
        own_ref[rows, :] = normed + sent
        sent_ref[rows, :] = sent.astype(BF)


def ahead(meta, tokens, att, merge_w, up, down, vectors, u):
    half = att[0].shape[1]
    d, hidden = up[0].shape
    return call(
        ahead_kernel,
        "ahead",
        (1,),
        meta,
        (tokens, *att, *merge_w, *up, *down, vectors),
        [pl.BlockSpec((half, d), lambda i, m: (u * 2 + m[0], 0))]
        + [fixed(192, half)] * 4
        + [fixed(192, d)] * 4
        + [fixed(d, hidden)] * 2
        + [fixed(hidden, d)] * 2
        + [fixed(4, d)],
        [fixed(half, d), fixed(half, 128), fixed(half, d), fixed(half, 2 * hidden), fixed(half, 2 * hidden), fixed(half, d), fixed(half, d)],
        [
            like((half, d), F32),
            like((half, 128), F32),
            like((half, d), BF),
            like((half, 2 * hidden), BF),
            like((half, 2 * hidden), BF),
            like((half, d), F32),
            like((half, d), BF),
        ],
        hold=(-1,),
        out=(0, 1, 2, 3, 4, 5),
    )


def astern_kernel(u, meta_ref, own_ref, far_ref, grad_ref, span_ref, ua_ref, ub_ref, da_ref, db_ref, slope_ref, vec_ref, *refs):
    last = len(refs) > 6
    before = refs[: len(refs) - 10] if last else ()
    out_ref, g_ref, pre_ref, back_ref, sent_ref, small_ref = refs[len(before) : len(before) + 6]
    gain, bias = vec_ref[2:3, :], vec_ref[3:4, :]
    half, d = own_ref.shape
    hidden = ua_ref.shape[1]
    starts = span_ref[u : u + 1, :]
    gain_grad = jnp.zeros(gain.shape, F32)
    bias_grad = jnp.zeros(gain.shape, F32)
    for r in range(half // RB):
        rows = pl.ds(r * RB, RB)
        xhat, rstd = normalise(own_ref[rows, :] + far_ref[rows, :].astype(F32))
        out_ref[rows, :] = (xhat * gain + bias).astype(BF)
        frame = meta_ref[0] * half + r * RB + lax.broadcasted_iota(jnp.int32, (RB, starts.shape[1]), 0)
        inside = (frame >= starts) & (frame < starts + SPAN)
        weight = jnp.max(jnp.where(inside, 1.0, 0.0), axis=1, keepdims=True)
        cot = grad_ref[rows, :].astype(F32) * weight
        gain_grad = gain_grad + jnp.sum(cot * xhat, axis=0, keepdims=True)
        bias_grad = bias_grad + jnp.sum(cot, axis=0, keepdims=True)
        gy = cot * gain
        mean_gy = jnp.mean(gy, axis=-1, keepdims=True)
        mean_gx = jnp.mean(gy * xhat, axis=-1, keepdims=True)
        sum_grad = rstd * (gy - mean_gy - xhat * mean_gx)
        low = sum_grad.astype(BF)
        g_ref[rows, :] = low
        sent = jnp.zeros(sum_grad.shape, F32)
        for g, (up, down) in enumerate(((ua_ref, da_ref), (ub_ref, db_ref))):
            pres = []
            for c in range(hidden // HB):
                columns = pl.ds(g * hidden + c * HB, HB)
                slope = slope_ref[rows, columns].astype(F32)
                pres.append((nt(low, down[c * HB : (c + 1) * HB, :]) * slope).astype(BF))
                pre_ref[rows, columns] = pres[-1]
            sent = sent + nt(jnp.concatenate(pres, axis=1), up[...]).astype(BF).astype(F32)
        back_ref[rows, :] = sum_grad + sent
        sent_ref[rows, :] = sent.astype(BF)
    small_ref[0:1, :] = gain_grad
    small_ref[1:2, :] = bias_grad
    if last:
        x_ref, act_ref = before[:2]
        weight_sums(x_ref[...], g_ref[...], act_ref, pre_ref, before[2:], refs[-4:])


def astern(meta, own, far, grad, spans, up, down, slope, vectors, u, before):
    half, d = own.shape
    hidden = up[0].shape[1]
    rows = fixed(half, d)
    wide = fixed(half, 2 * hidden)
    grads = [] if not before else [(d, hidden)] * 2 + [(hidden, d)] * 2
    extra = [] if not before else [rows, wide] + [fixed(*shape) for shape in grads[: len(before) - 2]]
    return call(
        functools.partial(astern_kernel, u),
        "astern",
        (1,),
        meta,
        (own, far, grad, spans, *up, *down, slope, vectors, *before),
        [rows] * 2
        + [pl.BlockSpec((half, d), lambda i, m: (u * 2 + m[0], 0)), fixed(*spans.shape)]
        + [fixed(d, hidden)] * 2
        + [fixed(hidden, d)] * 2
        + [wide, fixed(4, d)]
        + extra,
        [rows, rows, wide, rows, rows, fixed(2, d)] + [fixed(*shape) for shape in grads],
        [
            like((half, d), BF),
            like((half, d), BF),
            like((half, 2 * hidden), BF),
            like((half, d), F32),
            like((half, d), BF),
            like((2, d), F32),
        ]
        + [like(shape, BF) for shape in grads],
        limit=24 if before else VMEM,
        hold=(0, -3, 8, *range(10, 10 + len(before))),
        out=(3,) if before else (1, 2, 3),
    )


def weight_kernel(meta_ref, x_ref, g_ref, act_ref, pre_ref, *refs):
    before, sums = refs[:-4], refs[-4:]
    weight_sums(x_ref[...], g_ref[...], act_ref, pre_ref, before, sums)


def weight_sums(x, g, act_ref, pre_ref, before, sums):
    hidden = act_ref.shape[1] // 2
    for i in range(2):
        for c in range(hidden // HB):
            columns = pl.ds(i * hidden + c * HB, HB)
            block = pl.ds(c * HB, HB)
            up = tn(x, pre_ref[:, columns])
            down = tn(act_ref[:, columns], g)
            if before:
                up = up + before[i][:, block].astype(F32)
                down = down + before[2 + i][block, :].astype(F32)
            sums[i][:, block] = up.astype(BF)
            sums[2 + i][block, :] = down.astype(BF)


def weight_grads(meta, x, g, act, pre, before):
    rows, d = x.shape
    hidden = act.shape[1] // 2
    shapes = [(d, hidden)] * 2 + [(hidden, d)] * 2
    return call(
        weight_kernel,
        "weight_grads",
        (1,),
        meta,
        (x, g, act, pre, *before),
        [fixed(rows, d)] * 2 + [fixed(rows, 2 * hidden)] * 2 + [fixed(*shape) for shape in shapes[: len(before)]],
        [fixed(*shape) for shape in shapes],
        [like(shape, BF) for shape in shapes],
        hold=(0, 1, 2, 3),
        out=(0, 1, 2, 3),
    )


def inner_kernel(meta_ref, own_ref, far_ref, xhat_ref, rstd_ref, vec_ref, a0, a1, w0, w1, *refs):
    last = len(refs) == 11
    out_ref, g0, g1, m0, m1, small_ref = refs[-6:]
    grad = own_ref[...] + far_ref[...].astype(F32)
    xhat = xhat_ref[...]
    gain_grad = jnp.sum(grad * xhat, axis=0, keepdims=True)
    bias_grad = jnp.sum(grad, axis=0, keepdims=True)
    gy = grad * vec_ref[0:1, :]
    mean_gy = jnp.mean(gy, axis=-1, keepdims=True)
    mean_gx = jnp.mean(gy * xhat, axis=-1, keepdims=True)
    inner = rstd_ref[:, 0:1] * (gy - mean_gy - xhat * mean_gx)
    out_ref[...] = inner
    low = inner.astype(BF)
    g0[...] = nt(w0[...], low).astype(BF)
    g1[...] = nt(w1[...], low).astype(BF)
    small = jnp.concatenate([gain_grad, bias_grad], axis=0)
    small_ref[...] = small
    if last:
        before0, before1, before_small, outer0, outer1 = refs[:5]
        below = jnp.concatenate(
            [small + before_small[...], outer0[...] + outer1[...], jnp.zeros((60, small.shape[1]), F32)], axis=0
        ).astype(BF)
        for m, a, before in ((m0, a0, before0), (m1, a1, before1)):
            m[:192, :] = (nn(a[...], low) + before[...]).astype(BF)
            m[192:, :] = below
    else:
        m0[...] = nn(a0[...], low)
        m1[...] = nn(a1[...], low)


def inner_norm(meta, own, far, xhat, rstd, vectors, att, weights, before):
    rows, d = xhat.shape
    merge = like((256, d), BF) if before else like((192, d), F32)
    return call(
        inner_kernel,
        "inner_norm",
        (1,),
        meta,
        (own, far, xhat, rstd, vectors, *att, *weights, *before),
        [fixed(rows, d)] * 3
        + [fixed(rows, 128), fixed(4, d)]
        + [fixed(192, rows)] * 2
        + [fixed(192, d)] * 2
        + ([fixed(192, d)] * 2 + [fixed(2, d)] * 3 if before else []),
        [fixed(rows, d), fixed(192, rows), fixed(192, rows), fixed(*merge.shape), fixed(*merge.shape), fixed(2, d)],
        [like((rows, d), F32), like((192, rows), BF), like((192, rows), BF), merge, merge, like((2, d), F32)],
        hold=(0, 2, 3),
    )


def local(groups, tokens, lengths, span_starts, wq, wk, wv, wm, wu, wd, ig, ib, og, ob, out_grad):
    rows, d = tokens.shape
    seqs = lengths.shape[0]
    frames = rows // seqs
    half = frames // 2
    core = lax.axis_index("tensor") % 2
    place_dp = lax.axis_index("dp")
    bits = groups.bit_length() - 1

    def swap(value, k):
        return lax.ppermute(value, "tensor", [(i, i ^ k) for i in range(4)])

    def swap_dp(value, k):
        return lax.ppermute(value, "dp", [(i, i ^ k) for i in range(groups)])

    def add(a, b):
        return (a.astype(F32) + b.astype(F32)).astype(BF)

    def cut(array, index, count):
        size = array.shape[0] // count
        return lax.dynamic_slice_in_dim(array, index * size, size, 0)

    def total(pieces):
        return sum(piece.astype(F32) for piece in pieces).astype(BF) if len(pieces) > 1 else pieces[0]

    class Chain:
        def __init__(self, parts, order, back=None):
            self.parts = parts
            self.order = order
            self.held = list(order)
            self.steps = [(True, *stage) for stage in order] + [(False, *stage) for stage in back or reversed(order)]

        def start(self):
            if self.steps:
                scatter, low_bit, width = self.steps[0]
                count = 1 << width
                spot = (place_dp >> low_bit) & (count - 1)
                pick = lambda j: total([cut(part, spot ^ j, count) if scatter else part for part in self.parts])
                self.pending = [swap_dp(pick(j), j << low_bit) for j in range(1, count)]

        def finish(self, *after):
            if not self.steps:
                return
            scatter, low_bit, width = self.steps.pop(0)
            got = self.pending
            if after:
                got = list(lax.optimization_barrier((*got, *after))[: len(got)])
            count = 1 << width
            spot = (place_dp >> low_bit) & (count - 1)
            if scatter:
                self.state = total([cut(part, spot, count) for part in self.parts] + got)
                if all(step[0] is False for step in self.steps):
                    self.state = self.state.reshape((1,) * len(self.order) + self.state.shape)
            else:
                axis = self.order.index((low_bit, width))
                mine = self.parts[0]
                if count == 2:
                    halves = [jnp.where(spot, got[0], mine), jnp.where(spot, mine, got[0])]
                    self.state = jnp.concatenate(halves, axis=axis)
                else:
                    whole = jnp.zeros(mine.shape[:axis] + (count,) + mine.shape[axis + 1 :], BF)
                    for j, piece in enumerate([mine] + got):
                        whole = lax.dynamic_update_slice_in_dim(whole, piece, spot ^ j, axis)
                    self.state = whole
                if not self.steps:
                    self.state = self.state.reshape(-1, d)
            self.parts = (self.state,)

    scalars = jnp.concatenate([core.reshape(1), lengths])
    token = []

    def meta():
        return lax.optimization_barrier((scalars, *token))[0] if token else scalars

    def done(results, *others):
        token[:] = [results[0], *others]
        return results

    merge_w = (wm, swap(wm, 1), swap(wm, 2), swap(wm, 3))
    up_w = (wu, swap(wu, 1))
    down_w = (wd, swap(wd, 1))
    vectors = jnp.stack([ig, ib, og, ob])
    qkv_w = (wq.T, wk.T, wv.T)

    q, k, v = project(scalars, tokens, qkv_w)
    fwd, att = [], []
    for u in range(seqs):
        fwd.append(done(attend_forward(meta(), q, k, v, u, frames), *merge_w[1:], up_w[1], down_w[1]))
        own, other = fwd[u][:2]
        att.append((own, swap(other, 1), swap(own, 2), swap(other, 3)))
    front, far = [], []
    for u in range(seqs):
        front.append(done(ahead(meta(), tokens, att[u], merge_w, up_w, down_w, vectors, u)))
        far.append(swap(front[u][6], 2))
    back, far_grad, sums = [], [], ()
    for u in range(seqs):
        before = (front[u][2], front[u][3], *sums) if u == seqs - 1 else ()
        back.append(
            done(astern(meta(), front[u][5], far[u], out_grad, span_starts, up_w, down_w, front[u][4], vectors, u, before))
        )
        if u < seqs - 1:
            far_grad.append(swap(back[u][4], 2))
            sums = done(weight_grads(meta(), front[u][2], back[u][1], front[u][3], back[u][2], sums))

    def inner_step(u, before):
        res = done(inner_norm(meta(), back[u][3], far_grad[u], front[u][0], front[u][1], vectors, att[u][:2], merge_w[:2], before))
        return res, (res[1], swap(res[2], 1))

    def attend_step(u, grads):
        return done(attend_backward(meta(), q, k, v, grads, fwd[u][:2], fwd[u][2], u, frames))

    def entry_step(u, grads, before, dtype):
        return done(entry_back(meta(), tokens, grads, qkv_w, before, u, frames, dtype))


    pairs = [(b, 1) for b in range(bits)]
    stages = [(0, 1)] + [(b, 2) for b in range(1, bits - 1, 2)] + ([(bits - 1, 1)] if bits % 2 == 0 else [])
    out_rows = [b[0] for b in back]
    out_other = [swap(r, 1) for r in out_rows]
    inner, near, crossed, so_far = [], [], [], ()
    ffn, chains = [], []

    def finish(group, *after):
        for chain in group:
            chain.finish(*after)
        return [chain.state for chain in group]

    def start(group):
        for chain in group:
            chain.start()

    def together(group, *others):
        values = lax.optimization_barrier((*(chain.state for chain in group), *others))
        for chain, value in zip(group, values):
            chain.state, chain.parts = value, (value,)
        return values[len(group) :]

    for u in range(seqs):
        last = u == seqs - 1
        if u == 0:
            up_own, up_other, down_own, down_other = lax.optimization_barrier((*back[-1][6:], far_grad[0]))[:4]
            ffn.append(Chain((down_own, swap(down_other, 1)), pairs))
            ffn.append(Chain((up_own, swap(up_other, 1)), pairs[1:2] + pairs[:1] + pairs[2:], pairs[::-1]))
            res, grads = inner_step(0, ())
            start(ffn)
            inner.append(res)
            far_grad.append(swap(lax.optimization_barrier((back[-1][4], res[0]))[0], 2))
            token.extend(out_other)
        dqkv = attend_step(u, grads)
        token.extend(finish(ffn + chains, dqkv[0]))
        start(ffn + chains)
        if not last:
            before = ()
            if u + 1 == seqs - 1:
                before = (inner[0][3], inner[0][4], inner[0][5], back[0][5], back[1][5])
            res, grads = inner_step(u + 1, before)
            inner.append(res)
            merge = Chain((res[3], swap(res[4], 1)), pairs)
            token.extend([grads[1], merge.parts[1]])
            merge.start()
        else:
            token.extend(crossed)
        out = entry_step(u, dqkv, so_far, BF if last else F32)
        so_far = (out[2],)
        got = swap(out[0], 1)
        if not last:
            chains.append(merge)
            finish(ffn + chains, out[0])
            (got,) = together(ffn + chains, got)
            start(ffn + chains)
            token.extend([chain.state for chain in ffn + chains])
            near.append(out[1].astype(F32) + got.astype(F32))
            crossed.append(swap(near[u].astype(BF), 2))
    qkv = Chain((so_far[0],), stages)
    qkv.start()
    finish(ffn + [merge], out[0])
    together(ffn + [merge])
    start(ffn + [merge])
    near.append(out[1].astype(F32) + got.astype(F32))
    chains = ffn + [merge, qkv]
    finish(chains)
    (arrived,) = together(chains, near[-1].astype(BF))
    crossed.append(swap(arrived, 2))
    start(chains)
    finish(chains)
    together(chains, crossed[-1])
    start(chains)
    while any(chain.steps for chain in chains):
        finish(chains)
        together(chains)
        start(chains)
    down_sum, up_sum, merge_sum, qkv_sum = (chain.state for chain in chains)

    ready = [(inner[u][0] + (near[u] + crossed[u].astype(F32))).astype(BF) for u in range(seqs)]
    layer_output = place(meta(), out_rows, out_other)
    input_grad = place(scalars, ready, [swap(r, 1) for r in ready])

    small = merge_sum[192:196].astype(F32)
    query_grad, key_grad, value_grad = (qkv_sum[192 * i : 192 * (i + 1)].astype(F32).T for i in range(3))
    return (
        layer_output,
        input_grad,
        query_grad,
        key_grad,
        value_grad,
        merge_sum[:192].astype(F32),
        up_sum.astype(F32),
        down_sum.astype(F32),
        small[0],
        small[1],
        small[2],
        small[3],
    )


def solution(mesh):
    in_specs = (
        P("dp", None),
        P("dp"),
        P("dp", None),
        P(None, "tensor"),
        P(None, "tensor"),
        P(None, "tensor"),
        P("tensor", None),
        P(None, "tensor"),
        P("tensor", None),
        P(),
        P(),
        P(),
        P(),
        P("dp", None),
    )
    out_specs = (
        P("dp", None),
        P("dp", None),
        P(None, "tensor"),
        P(None, "tensor"),
        P(None, "tensor"),
        P("tensor", None),
        P(None, "tensor"),
        P("tensor", None),
        P(),
        P(),
        P(),
        P(),
    )
    body = functools.partial(local, mesh.shape["dp"])
    return jax.shard_map(body, mesh=mesh, in_specs=in_specs, out_specs=out_specs, check_vma=False)
```

```python
import functools

import jax
import jax.numpy as jnp
from jax import lax
from jax.experimental import pallas as pl
from jax.experimental.pallas import tpu as pltpu
from jax.sharding import PartitionSpec as P

HEAD_DIM = 64
SPAN = 10
EPS = 1e-05
LOG2E = 1.4426950408889634
KB = 256
VMEM = 16
RB = 128
HB = 256
BF = jnp.bfloat16
F32 = jnp.float32
MIB = 1 << 20


def nn(a, b):
    return lax.dot_general(a, b, (((1,), (0,)), ((), ())), preferred_element_type=F32)


def nt(a, b):
    return lax.dot_general(a, b, (((1,), (1,)), ((), ())), preferred_element_type=F32)


def tn(a, b):
    return lax.dot_general(a, b, (((0,), (0,)), ((), ())), preferred_element_type=F32)


def params(limit):
    return pltpu.CompilerParams(vmem_limit_bytes=limit * MIB)


def cost(micros):
    return pl.CostEstimate(flops=int(micros * 1.1e9), bytes_accessed=1024, transcendentals=0)


MICROS = {"project": 3, "attend_forward": 8, "attend_backward": 12, "entry_back": 5, "place": 3, "ahead": 9, "astern": 10, "inner_norm": 3, "weight_grads": 5}


def lane_parts(block):
    left = block[:, :128]
    lane = lax.broadcasted_iota(jnp.int32, left.shape, 1)
    zero = jnp.zeros_like(left)
    return (
        jnp.where(lane < HEAD_DIM, left, zero),
        jnp.where(lane >= HEAD_DIM, left, zero),
        block[:, 128:],
    )


TILE = (0, 0, 1)


def call(kernel, name, grid, meta, args, in_specs, out_specs, out_shape, scratch=(), limit=VMEM, hold=(), out=()):
    args = list(args)
    for i in hold:
        space = pltpu.VMEM if i >= 0 else pltpu.HBM
        spot = i if i >= 0 else -1 - i
        args[spot] = pltpu.with_memory_space_constraint(args[spot], space)
    if isinstance(out_shape, list):
        out_shape = [pltpu.VMEM(o.shape, o.dtype) if i in out else o for i, o in enumerate(out_shape)]
    return pl.pallas_call(
        kernel,
        grid_spec=pltpu.PrefetchScalarGridSpec(
            num_scalar_prefetch=1,
            grid=grid,
            in_specs=in_specs,
            out_specs=out_specs,
            scratch_shapes=scratch,
        ),
        out_shape=out_shape,
        compiler_params=params(limit),
        cost_estimate=cost(MICROS[name]),
        name=name,
    )(meta, *args)


def fixed(*shape):
    return pl.BlockSpec(shape, lambda *_: (0,) * len(shape))


def like(shape, dtype):
    return jax.ShapeDtypeStruct(shape, dtype)


def project_kernel(meta_ref, x_ref, wq_ref, wk_ref, wv_ref, q_ref, k_ref, v_ref):
    x = x_ref[...]
    for w_ref, o_ref in ((wq_ref, q_ref), (wk_ref, k_ref), (wv_ref, v_ref)):
        o_ref[:, :192] = nt(x, w_ref[...]).astype(BF)
        o_ref[:, 192:] = jnp.zeros((x.shape[0], HEAD_DIM), BF)


def project(meta, tokens, weights):
    rows, d = tokens.shape
    block = 256
    return call(
        project_kernel,
        "project",
        (rows // block,),
        meta,
        (tokens, *weights),
        [pl.BlockSpec((block, d), lambda i, m: (i, 0))] + [fixed(192, d)] * 3,
        [pl.BlockSpec((block, 256), lambda i, m: (i, 0))] * 3,
        [like((rows, 256), BF)] * 3,
        hold=(-1, -2, -3, -4),
        out=(0, 1, 2),
    )


def forward_kernel(u, meta_ref, q_ref, k_ref, v_ref, own_ref, other_ref, lse_ref, s_ref):
    length = meta_ref[1 + u]
    step = pl.program_id(0)
    blocks = lax.div(length + KB - 1, KB)
    parts = lane_parts(q_ref[...] * jnp.asarray(0.125, BF))
    width = q_ref.shape[0]

    def first(kb, highest):
        start = pl.multiple_of(kb * KB, KB)
        rows = pl.ds(start, KB)
        live = start + lax.broadcasted_iota(jnp.int32, (KB, width), 0) < length
        out = []
        for h in range(3):
            tile = pl.ds(128 * TILE[h], 128)
            s = nt(k_ref[rows, tile], parts[h])
            s = jnp.where(live, s, -1e30)
            s_ref[h, rows, :] = s
            out.append(jnp.maximum(highest[h], jnp.max(s, axis=0, keepdims=True)))
        return tuple(out)

    floor = jnp.full((1, width), -1e30, F32)
    highest = lax.fori_loop(0, blocks, first, (floor,) * 3)

    def second(kb, carry):
        rows = pl.ds(pl.multiple_of(kb * KB, KB), KB)
        out = []
        for h in range(3):
            total, result = carry[h]
            p = jnp.exp2((s_ref[h, rows, :] - highest[h]) * LOG2E)
            total = total + jnp.sum(p, axis=0, keepdims=True)
            v = v_ref[rows, pl.ds(128 * TILE[h], 128)]
            result = result + tn(v, p.astype(BF))
            out.append((total, result))
        return tuple(out)

    init = ((jnp.zeros((1, width), F32), jnp.zeros((128, width), F32)),) * 3
    done = lax.fori_loop(0, blocks, second, init)
    outs = []
    for h in range(3):
        total, result = done[h]
        lo = HEAD_DIM * (h % 2)
        o = result[lo : lo + HEAD_DIM] / total
        lse_ref[0, pl.ds(h, 1), :] = highest[h] * LOG2E + jnp.log2(total)
        outs.append(o.astype(BF))
    whole = jnp.concatenate(outs, axis=0)
    for j, o_ref in enumerate((own_ref, other_ref)):

        @pl.when(step == j)
        def _():
            o_ref[...] = whole


def attend_forward(meta, q, k, v, u, frames):
    half = frames // 2
    return call(
        functools.partial(forward_kernel, u),
        "attend_forward",
        (2,),
        meta,
        (q, k, v),
        [
            pl.BlockSpec((half, 256), lambda i, m: (u * 2 + (i ^ m[0]), 0)),
            pl.BlockSpec((frames, 256), lambda i, m: (u, 0)),
            pl.BlockSpec((frames, 256), lambda i, m: (u, 0)),
        ],
        [
            fixed(192, half),
            fixed(192, half),
            pl.BlockSpec((1, 8, half), lambda i, m: (i, 0, 0)),
        ],
        [
            like((192, half), BF),
            like((192, half), BF),
            like((2, 8, half), F32),
        ],
        [pltpu.VMEM((3, frames, half), F32)],
        hold=(0, 1, 2),
        out=(2,),
    )


def backward_kernel(
    u, meta_ref, q_ref, k_ref, v_ref, d0_ref, d1_ref, o0_ref, o1_ref, lse_ref,
    dq_ref, dk_ref, dv_ref, kt_ref, dk_acc, dv_acc, do_ref, o_ref,
):
    length = meta_ref[1 + u]
    blocks = lax.div(length + KB - 1, KB)
    step = pl.program_id(0)

    @pl.when(step == 0)
    def _():
        dk_acc[...] = jnp.zeros_like(dk_acc)
        dv_acc[...] = jnp.zeros_like(dv_acc)
        kt_ref[...] = jnp.transpose(k_ref[...])
        do_ref[...] = d0_ref[...]
        o_ref[...] = o0_ref[...]

    @pl.when(step == 1)
    def _():
        do_ref[...] = d1_ref[...]
        o_ref[...] = o1_ref[...]

    parts = lane_parts(q_ref[...] * jnp.asarray(0.125, BF))
    width = q_ref.shape[0]
    empty = jnp.zeros((HEAD_DIM, width), BF)
    head = [do_ref[pl.ds(h * HEAD_DIM, HEAD_DIM), :] for h in range(3)]
    grads = (
        jnp.concatenate([head[0], empty], axis=0),
        jnp.concatenate([empty, head[1]], axis=0),
        jnp.concatenate([head[2], empty], axis=0),
    )
    delta = [
        jnp.sum(
            head[h].astype(F32) * o_ref[pl.ds(h * HEAD_DIM, HEAD_DIM), :].astype(F32), axis=0, keepdims=True
        )
        for h in range(3)
    ]
    lse = [lse_ref[0, pl.ds(h, 1), :] for h in range(3)]

    def body(kb, carry):
        start = pl.multiple_of(kb * KB, KB)
        rows = pl.ds(start, KB)
        live = start + lax.broadcasted_iota(jnp.int32, (KB, width), 0) < length
        out = []
        for h in range(3):
            tile = pl.ds(128 * TILE[h], 128)
            s = nt(k_ref[rows, tile], parts[h])
            s = jnp.where(live, s, -1e30)
            p = jnp.exp2(s * LOG2E - lse[h])
            dp = nn(v_ref[rows, tile], grads[h])
            ds = (p * (dp - delta[h])).astype(BF)
            dv_acc[rows, tile] += nt(p.astype(BF), grads[h])
            dk_acc[rows, tile] += nn(ds, parts[h])
            kt = kt_ref[pl.ds(h * HEAD_DIM, HEAD_DIM), rows]
            out.append(carry[h] + nn(kt, ds))
        return tuple(out)

    zero = jnp.zeros((HEAD_DIM, width), F32)
    done = lax.fori_loop(0, blocks, body, (zero,) * 3)
    full = jnp.concatenate(done + (zero,), axis=0) * 0.125
    dq_ref[...] = jnp.transpose(full).astype(BF)

    @pl.when(step == 1)
    def _():
        dk_ref[...] = dk_acc[...].astype(BF)
        dv_ref[...] = dv_acc[...].astype(BF)


def attend_backward(meta, q, k, v, grads, outs, lse, u, frames):
    half = frames // 2
    return call(
        functools.partial(backward_kernel, u),
        "attend_backward",
        (2,),
        meta,
        (q, k, v, *grads, *outs, lse),
        [
            pl.BlockSpec((half, 256), lambda i, m: (u * 2 + (i ^ m[0]), 0)),
            pl.BlockSpec((frames, 256), lambda i, m: (u, 0)),
            pl.BlockSpec((frames, 256), lambda i, m: (u, 0)),
            fixed(192, half),
            fixed(192, half),
            fixed(192, half),
            fixed(192, half),
            pl.BlockSpec((1, 8, half), lambda i, m: (i, 0, 0)),
        ],
        [
            pl.BlockSpec((half, 256), lambda i, m: (i ^ m[0], 0)),
            fixed(frames, 256),
            fixed(frames, 256),
        ],
        [like((frames, 256), BF)] * 3,
        [
            pltpu.VMEM((256, frames), BF),
            pltpu.VMEM((frames, 256), F32),
            pltpu.VMEM((frames, 256), F32),
            pltpu.VMEM((192, half), BF),
            pltpu.VMEM((192, half), BF),
        ],
        hold=(0, 1, 2, 7),
        out=(0, 1, 2),
    )


def entry_kernel(meta_ref, x_ref, dq_ref, dk_ref, dv_ref, wq_ref, wk_ref, wv_ref, *refs):
    before_ref = refs[0] if len(refs) == 5 else None
    send_ref, keep_ref, sum_ref, acc = refs[-4:]
    step = pl.program_id(0)
    x = x_ref[...]
    total = jnp.zeros(x.shape, F32)
    for i, (g_ref, w_ref) in enumerate(((dq_ref, wq_ref), (dk_ref, wk_ref), (dv_ref, wv_ref))):
        rows = pl.ds(192 * i, 192)
        g = g_ref[:, :192]
        total = total + nn(g, w_ref[...])
        product = tn(g, x)

        @pl.when(step == 0)
        def _():
            acc[rows, :] = product if before_ref is None else product + before_ref[rows, :]

        @pl.when(step == 1)
        def _():
            sum_ref[rows, :] = (product + acc[rows, :]).astype(sum_ref.dtype)

    low = total.astype(BF)

    @pl.when(step == 0)
    def _():
        send_ref[...] = low

    @pl.when(step == 1)
    def _():
        keep_ref[...] = low


def entry_back(meta, tokens, grads, weights, before, u, frames, dtype):
    half = frames // 2
    d = tokens.shape[1]
    return call(
        entry_kernel,
        "entry_back",
        (2,),
        meta,
        (tokens, *grads, *weights, *before),
        [pl.BlockSpec((half, d), lambda i, m: (u * 2 + (1 - i ^ m[0]), 0))]
        + [pl.BlockSpec((half, 256), lambda i, m: (1 - i ^ m[0], 0))] * 3
        + [fixed(192, d)] * 3
        + [fixed(576, d)] * len(before),
        [fixed(half, d), fixed(half, d), fixed(576, d)],
        [like((half, d), BF), like((half, d), BF), like((576, d), dtype)],
        [pltpu.VMEM((576, d), F32)],
        hold=(-1, 1, 2, 3, -5, -6, -7),
    )


def place_kernel(meta_ref, *refs):
    o_ref = refs[-1]
    for i, r_ref in enumerate(refs[:-1]):

        @pl.when(pl.program_id(0) == i)
        def _():
            o_ref[...] = r_ref[...]


def place(meta, own, other):
    half, d = own[0].shape
    count = 2 * len(own)
    return call(
        place_kernel,
        "place",
        (count,),
        meta,
        [block for pair in zip(own, other) for block in pair],
        [fixed(half, d)] * count,
        pl.BlockSpec((half, d), lambda i, m: (i ^ m[0], 0)),
        like((count * half, d), own[0].dtype),
    )


def normalise(values):
    average = jnp.mean(values, axis=-1, keepdims=True)
    centred = values - average
    spread = jnp.mean(centred * centred, axis=-1, keepdims=True)
    rstd = lax.rsqrt(spread + EPS)
    return centred * rstd, rstd


def gelu_pair(v):
    e = jnp.exp2(v * v * (-0.5 * LOG2E))
    t = 1.0 / (1.0 + (0.3275911 * 0.7071067811865476) * jnp.abs(v))
    poly = t * (0.5 * 0.254829592 + t * (0.5 * -0.284496736 + t * (0.5 * 1.421413741 + t * (0.5 * -1.453152027 + t * (0.5 * 1.061405429)))))
    tail = poly * e
    phi_cap = jnp.where(v >= 0, 1.0 - tail, tail)
    return v * phi_cap, phi_cap + v * (e * 0.3989422804014327)


def ahead_kernel(
    meta_ref, tok_ref, a0, a1, a2, a3, w0, w1, w2, w3, ua_ref, ub_ref, da_ref, db_ref, vec_ref,
    xhat_ref, rstd_ref, low_ref, act_ref, slope_ref, own_ref, sent_ref,
):
    gain, bias = vec_ref[0:1, :], vec_ref[1:2, :]
    hidden = ua_ref.shape[1]
    for r in range(tok_ref.shape[0] // RB):
        rows = pl.ds(r * RB, RB)
        branch = jnp.zeros((RB, tok_ref.shape[1]), F32)
        for a, w in ((a0, w0), (a1, w1), (a2, w2), (a3, w3)):
            branch = branch + tn(a[:, rows], w[...]).astype(BF).astype(F32)
        xhat, rstd = normalise(tok_ref[rows, :].astype(F32) + branch)
        xhat_ref[rows, :] = xhat
        rstd_ref[rows, :] = jnp.broadcast_to(rstd, (RB, rstd_ref.shape[1]))
        normed = xhat * gain + bias
        low = normed.astype(BF)
        low_ref[rows, :] = low
        sent = jnp.zeros(normed.shape, F32)
        for g, (up, down) in enumerate(((ua_ref, da_ref), (ub_ref, db_ref))):
            acts = []
            for c in range(hidden // HB):
                act, slope = gelu_pair(nn(low, up[:, c * HB : (c + 1) * HB]))
                columns = pl.ds(g * hidden + c * HB, HB)
                acts.append(act.astype(BF))
                act_ref[rows, columns] = acts[-1]
                slope_ref[rows, columns] = slope.astype(BF)
            sent = sent + nn(jnp.concatenate(acts, axis=1), down[...]).astype(BF).astype(F32)
        own_ref[rows, :] = normed + sent
        sent_ref[rows, :] = sent.astype(BF)


def ahead(meta, tokens, att, merge_w, up, down, vectors, u):
    half = att[0].shape[1]
    d, hidden = up[0].shape
    return call(
        ahead_kernel,
        "ahead",
        (1,),
        meta,
        (tokens, *att, *merge_w, *up, *down, vectors),
        [pl.BlockSpec((half, d), lambda i, m: (u * 2 + m[0], 0))]
        + [fixed(192, half)] * 4
        + [fixed(192, d)] * 4
        + [fixed(d, hidden)] * 2
        + [fixed(hidden, d)] * 2
        + [fixed(4, d)],
        [fixed(half, d), fixed(half, 128), fixed(half, d), fixed(half, 2 * hidden), fixed(half, 2 * hidden), fixed(half, d), fixed(half, d)],
        [
            like((half, d), F32),
            like((half, 128), F32),
            like((half, d), BF),
            like((half, 2 * hidden), BF),
            like((half, 2 * hidden), BF),
            like((half, d), F32),
            like((half, d), BF),
        ],
        hold=(-1,),
        out=(0, 1, 2, 3, 4, 5),
    )


def astern_kernel(u, meta_ref, own_ref, far_ref, grad_ref, span_ref, ua_ref, ub_ref, da_ref, db_ref, slope_ref, vec_ref, *refs):
    last = len(refs) > 6
    before = refs[: len(refs) - 10] if last else ()
    out_ref, g_ref, pre_ref, back_ref, sent_ref, small_ref = refs[len(before) : len(before) + 6]
    gain, bias = vec_ref[2:3, :], vec_ref[3:4, :]
    half, d = own_ref.shape
    hidden = ua_ref.shape[1]
    starts = span_ref[u : u + 1, :]
    gain_grad = jnp.zeros(gain.shape, F32)
    bias_grad = jnp.zeros(gain.shape, F32)
    for r in range(half // RB):
        rows = pl.ds(r * RB, RB)
        xhat, rstd = normalise(own_ref[rows, :] + far_ref[rows, :].astype(F32))
        out_ref[rows, :] = (xhat * gain + bias).astype(BF)
        frame = meta_ref[0] * half + r * RB + lax.broadcasted_iota(jnp.int32, (RB, starts.shape[1]), 0)
        inside = (frame >= starts) & (frame < starts + SPAN)
        weight = jnp.max(jnp.where(inside, 1.0, 0.0), axis=1, keepdims=True)
        cot = grad_ref[rows, :].astype(F32) * weight
        gain_grad = gain_grad + jnp.sum(cot * xhat, axis=0, keepdims=True)
        bias_grad = bias_grad + jnp.sum(cot, axis=0, keepdims=True)
        gy = cot * gain
        mean_gy = jnp.mean(gy, axis=-1, keepdims=True)
        mean_gx = jnp.mean(gy * xhat, axis=-1, keepdims=True)
        sum_grad = rstd * (gy - mean_gy - xhat * mean_gx)
        low = sum_grad.astype(BF)
        g_ref[rows, :] = low
        sent = jnp.zeros(sum_grad.shape, F32)
        for g, (up, down) in enumerate(((ua_ref, da_ref), (ub_ref, db_ref))):
            pres = []
            for c in range(hidden // HB):
                columns = pl.ds(g * hidden + c * HB, HB)
                slope = slope_ref[rows, columns].astype(F32)
                pres.append((nt(low, down[c * HB : (c + 1) * HB, :]) * slope).astype(BF))
                pre_ref[rows, columns] = pres[-1]
            sent = sent + nt(jnp.concatenate(pres, axis=1), up[...]).astype(BF).astype(F32)
        back_ref[rows, :] = sum_grad + sent
        sent_ref[rows, :] = sent.astype(BF)
    small_ref[0:1, :] = gain_grad
    small_ref[1:2, :] = bias_grad
    if last:
        x_ref, act_ref = before[:2]
        weight_sums(x_ref[...], g_ref[...], act_ref, pre_ref, before[2:], refs[-4:])


def astern(meta, own, far, grad, spans, up, down, slope, vectors, u, before):
    half, d = own.shape
    hidden = up[0].shape[1]
    rows = fixed(half, d)
    wide = fixed(half, 2 * hidden)
    grads = [] if not before else [(d, hidden)] * 2 + [(hidden, d)] * 2
    extra = [] if not before else [rows, wide] + [fixed(*shape) for shape in grads[: len(before) - 2]]
    return call(
        functools.partial(astern_kernel, u),
        "astern",
        (1,),
        meta,
        (own, far, grad, spans, *up, *down, slope, vectors, *before),
        [rows] * 2
        + [pl.BlockSpec((half, d), lambda i, m: (u * 2 + m[0], 0)), fixed(*spans.shape)]
        + [fixed(d, hidden)] * 2
        + [fixed(hidden, d)] * 2
        + [wide, fixed(4, d)]
        + extra,
        [rows, rows, wide, rows, rows, fixed(2, d)] + [fixed(*shape) for shape in grads],
        [
            like((half, d), BF),
            like((half, d), BF),
            like((half, 2 * hidden), BF),
            like((half, d), F32),
            like((half, d), BF),
            like((2, d), F32),
        ]
        + [like(shape, BF) for shape in grads],
        limit=24 if before else VMEM,
        hold=(0, -3, 8, *range(10, 10 + len(before))),
        out=(3,) if before else (1, 2, 3),
    )


def weight_kernel(meta_ref, x_ref, g_ref, act_ref, pre_ref, *refs):
    before, sums = refs[:-4], refs[-4:]
    weight_sums(x_ref[...], g_ref[...], act_ref, pre_ref, before, sums)


def weight_sums(x, g, act_ref, pre_ref, before, sums):
    hidden = act_ref.shape[1] // 2
    for i in range(2):
        for c in range(hidden // HB):
            columns = pl.ds(i * hidden + c * HB, HB)
            block = pl.ds(c * HB, HB)
            up = tn(x, pre_ref[:, columns])
            down = tn(act_ref[:, columns], g)
            if before:
                up = up + before[i][:, block].astype(F32)
                down = down + before[2 + i][block, :].astype(F32)
            sums[i][:, block] = up.astype(BF)
            sums[2 + i][block, :] = down.astype(BF)


def weight_grads(meta, x, g, act, pre, before):
    rows, d = x.shape
    hidden = act.shape[1] // 2
    shapes = [(d, hidden)] * 2 + [(hidden, d)] * 2
    return call(
        weight_kernel,
        "weight_grads",
        (1,),
        meta,
        (x, g, act, pre, *before),
        [fixed(rows, d)] * 2 + [fixed(rows, 2 * hidden)] * 2 + [fixed(*shape) for shape in shapes[: len(before)]],
        [fixed(*shape) for shape in shapes],
        [like(shape, BF) for shape in shapes],
        hold=(0, 1, 2, 3),
        out=(0, 1, 2, 3),
    )


def inner_kernel(meta_ref, own_ref, far_ref, xhat_ref, rstd_ref, vec_ref, a0, a1, w0, w1, *refs):
    last = len(refs) == 11
    out_ref, g0, g1, m0, m1, small_ref = refs[-6:]
    grad = own_ref[...] + far_ref[...].astype(F32)
    xhat = xhat_ref[...]
    gain_grad = jnp.sum(grad * xhat, axis=0, keepdims=True)
    bias_grad = jnp.sum(grad, axis=0, keepdims=True)
    gy = grad * vec_ref[0:1, :]
    mean_gy = jnp.mean(gy, axis=-1, keepdims=True)
    mean_gx = jnp.mean(gy * xhat, axis=-1, keepdims=True)
    inner = rstd_ref[:, 0:1] * (gy - mean_gy - xhat * mean_gx)
    out_ref[...] = inner
    low = inner.astype(BF)
    g0[...] = nt(w0[...], low).astype(BF)
    g1[...] = nt(w1[...], low).astype(BF)
    small = jnp.concatenate([gain_grad, bias_grad], axis=0)
    small_ref[...] = small
    if last:
        before0, before1, before_small, outer0, outer1 = refs[:5]
        below = jnp.concatenate(
            [small + before_small[...], outer0[...] + outer1[...], jnp.zeros((60, small.shape[1]), F32)], axis=0
        ).astype(BF)
        for m, a, before in ((m0, a0, before0), (m1, a1, before1)):
            m[:192, :] = (nn(a[...], low) + before[...]).astype(BF)
            m[192:, :] = below
    else:
        m0[...] = nn(a0[...], low)
        m1[...] = nn(a1[...], low)


def inner_norm(meta, own, far, xhat, rstd, vectors, att, weights, before):
    rows, d = xhat.shape
    merge = like((256, d), BF) if before else like((192, d), F32)
    return call(
        inner_kernel,
        "inner_norm",
        (1,),
        meta,
        (own, far, xhat, rstd, vectors, *att, *weights, *before),
        [fixed(rows, d)] * 3
        + [fixed(rows, 128), fixed(4, d)]
        + [fixed(192, rows)] * 2
        + [fixed(192, d)] * 2
        + ([fixed(192, d)] * 2 + [fixed(2, d)] * 3 if before else []),
        [fixed(rows, d), fixed(192, rows), fixed(192, rows), fixed(*merge.shape), fixed(*merge.shape), fixed(2, d)],
        [like((rows, d), F32), like((192, rows), BF), like((192, rows), BF), merge, merge, like((2, d), F32)],
        hold=(0, 2, 3),
    )


def local(groups, tokens, lengths, span_starts, wq, wk, wv, wm, wu, wd, ig, ib, og, ob, out_grad):
    rows, d = tokens.shape
    seqs = lengths.shape[0]
    frames = rows // seqs
    half = frames // 2
    core = lax.axis_index("tensor") % 2
    place_dp = lax.axis_index("dp")
    bits = groups.bit_length() - 1

    def swap(value, k):
        return lax.ppermute(value, "tensor", [(i, i ^ k) for i in range(4)])

    def swap_dp(value, k):
        return lax.ppermute(value, "dp", [(i, i ^ k) for i in range(groups)])

    def add(a, b):
        return (a.astype(F32) + b.astype(F32)).astype(BF)

    def cut(array, index, count):
        size = array.shape[0] // count
        return lax.dynamic_slice_in_dim(array, index * size, size, 0)

    def total(pieces):
        return sum(piece.astype(F32) for piece in pieces).astype(BF) if len(pieces) > 1 else pieces[0]

    class Chain:
        def __init__(self, parts, order, back=None):
            self.parts = parts
            self.order = order
            self.held = list(order)
            self.steps = [(True, *stage) for stage in order] + [(False, *stage) for stage in back or reversed(order)]

        def start(self):
            if self.steps:
                scatter, low_bit, width = self.steps[0]
                count = 1 << width
                spot = (place_dp >> low_bit) & (count - 1)
                pick = lambda j: total([cut(part, spot ^ j, count) if scatter else part for part in self.parts])
                self.pending = [swap_dp(pick(j), j << low_bit) for j in range(1, count)]

        def finish(self, *after):
            if not self.steps:
                return
            scatter, low_bit, width = self.steps.pop(0)
            got = self.pending
            if after:
                got = list(lax.optimization_barrier((*got, *after))[: len(got)])
            count = 1 << width
            spot = (place_dp >> low_bit) & (count - 1)
            if scatter:
                self.state = total([cut(part, spot, count) for part in self.parts] + got)
                if all(step[0] is False for step in self.steps):
                    self.state = self.state.reshape((1,) * len(self.order) + self.state.shape)
            else:
                axis = self.order.index((low_bit, width))
                mine = self.parts[0]
                if count == 2:
                    halves = [jnp.where(spot, got[0], mine), jnp.where(spot, mine, got[0])]
                    self.state = jnp.concatenate(halves, axis=axis)
                else:
                    whole = jnp.zeros(mine.shape[:axis] + (count,) + mine.shape[axis + 1 :], BF)
                    for j, piece in enumerate([mine] + got):
                        whole = lax.dynamic_update_slice_in_dim(whole, piece, spot ^ j, axis)
                    self.state = whole
                if not self.steps:
                    self.state = self.state.reshape(-1, d)
            self.parts = (self.state,)

    def sum_dp(value, turn):
        members = list(range(groups))
        return lax.psum(value, "dp", axis_index_groups=[members[turn:] + members[:turn]])

    scalars = jnp.concatenate([core.reshape(1), lengths])
    token = []

    def meta():
        return lax.optimization_barrier((scalars, *token))[0] if token else scalars

    def done(results, *others):
        token[:] = [results[0], *others]
        return results

    merge_w = (wm, swap(wm, 1), swap(wm, 2), swap(wm, 3))
    up_w = (wu, swap(wu, 1))
    down_w = (wd, swap(wd, 1))
    vectors = jnp.stack([ig, ib, og, ob])
    qkv_w = (wq.T, wk.T, wv.T)

    q, k, v = project(scalars, tokens, qkv_w)
    fwd, att = [], []
    for u in range(seqs):
        fwd.append(done(attend_forward(meta(), q, k, v, u, frames), *merge_w[1:], up_w[1], down_w[1]))
        own, other = fwd[u][:2]
        att.append((own, swap(other, 1), swap(own, 2), swap(other, 3)))
    front, far = [], []
    for u in range(seqs):
        front.append(done(ahead(meta(), tokens, att[u], merge_w, up_w, down_w, vectors, u)))
        far.append(swap(front[u][6], 2))
    back, far_grad, sums = [], [], ()
    for u in range(seqs):
        before = (front[u][2], front[u][3], *sums) if u == seqs - 1 else ()
        back.append(
            done(astern(meta(), front[u][5], far[u], out_grad, span_starts, up_w, down_w, front[u][4], vectors, u, before))
        )
        if u < seqs - 1:
            far_grad.append(swap(back[u][4], 2))
            sums = done(weight_grads(meta(), front[u][2], back[u][1], front[u][3], back[u][2], sums))

    def inner_step(u, before):
        res = done(inner_norm(meta(), back[u][3], far_grad[u], front[u][0], front[u][1], vectors, att[u][:2], merge_w[:2], before))
        return res, (res[1], swap(res[2], 1))

    def attend_step(u, grads):
        return done(attend_backward(meta(), q, k, v, grads, fwd[u][:2], fwd[u][2], u, frames))

    def entry_step(u, grads, before, dtype):
        return done(entry_back(meta(), tokens, grads, qkv_w, before, u, frames, dtype))


    stages = [(0, 1)] + [(b, 2) for b in range(1, bits - 1, 2)] + ([(bits - 1, 1)] if bits % 2 == 0 else [])
    out_rows = jnp.stack([b[0] for b in back])
    inner, near, crossed, so_far, entry, spare = [], [], [], (), [], []

    def together(group, *others):
        values = lax.optimization_barrier((*(chain.state for chain in group), *others))
        for chain, value in zip(group, values):
            chain.state, chain.parts = value, (value,)
        return values[len(group) :]

    for u in range(seqs):
        last = u == seqs - 1
        if u == 0:
            up_own, up_other, down_own, down_other = lax.optimization_barrier((*back[-1][6:], far_grad[0]))[:4]
            res, grads = inner_step(0, ())
            inner.append(res)
            far_grad.append(swap(lax.optimization_barrier((back[-1][4], res[0]))[0], 2))
            down_sum, up_sum = total((down_own, swap(down_other, 1))), total((up_own, swap(up_other, 1)))
            token.extend([down_sum, up_sum])
            down_sum, up_sum = sum_dp(down_sum, 0), sum_dp(up_sum, 1)
        dqkv = attend_step(u, grads)
        if not last:
            before = ()
            if u + 1 == seqs - 1:
                before = (inner[0][3], inner[0][4], inner[0][5], back[0][5], back[1][5])
            res, grads = inner_step(u + 1, before)
            inner.append(res)
        out = entry_step(u, dqkv, so_far, BF if last else F32)
        so_far = (out[2],)
        entry.append(out)
    qkv = Chain((so_far[0],), stages)
    qkv.start()
    merge_sum = sum_dp(lax.optimization_barrier((total((res[3], swap(res[4], 1))), entry[0][0]))[0], 2)
    for u in range(seqs):
        got = swap(entry[u][0], 1)
        near.append(entry[u][1].astype(F32) + got.astype(F32))
        crossed.append(swap(near[u].astype(BF), 2))
    chains = [qkv]
    while any(chain.steps for chain in chains):
        for chain in chains:
            chain.finish()
        if len(qkv.steps) == 1:
            down_sum, up_sum = together(chains, down_sum, up_sum)
        else:
            together(chains)
        for chain in chains:
            chain.start()
    qkv_sum = qkv.state
    merge_sum, qkv_sum = lax.optimization_barrier((merge_sum, qkv_sum))

    ready = [(inner[u][0] + (near[u] + crossed[u].astype(F32))).astype(BF) for u in range(seqs)]
    pairs = [[i, i + 1] for i in range(0, 4, 2)]
    layer_output = lax.all_gather(out_rows, "tensor", axis=1, tiled=True, axis_index_groups=pairs).reshape(rows, d)
    input_grad = place(scalars, ready, [swap(r, 1) for r in ready])

    small = merge_sum[192:196].astype(F32)
    query_grad, key_grad, value_grad = (qkv_sum[192 * i : 192 * (i + 1)].astype(F32).T for i in range(3))
    return (
        layer_output,
        input_grad,
        query_grad,
        key_grad,
        value_grad,
        merge_sum[:192].astype(F32),
        up_sum.astype(F32),
        down_sum.astype(F32),
        small[0],
        small[1],
        small[2],
        small[3],
    )


def solution(mesh):
    in_specs = (
        P("dp", None),
        P("dp"),
        P("dp", None),
        P(None, "tensor"),
        P(None, "tensor"),
        P(None, "tensor"),
        P("tensor", None),
        P(None, "tensor"),
        P("tensor", None),
        P(),
        P(),
        P(),
        P(),
        P("dp", None),
    )
    out_specs = (
        P("dp", None),
        P("dp", None),
        P(None, "tensor"),
        P(None, "tensor"),
        P(None, "tensor"),
        P("tensor", None),
        P(None, "tensor"),
        P("tensor", None),
        P(),
        P(),
        P(),
        P(),
    )
    body = functools.partial(local, mesh.shape["dp"])
    return jax.shard_map(body, mesh=mesh, in_specs=in_specs, out_specs=out_specs, check_vma=False)
```

```python
import functools

import jax
import jax.numpy as jnp
from jax import lax
from jax.experimental import pallas as pl
from jax.experimental.pallas import tpu as pltpu
from jax.sharding import PartitionSpec as P

HEAD_DIM = 64
SPAN = 10
EPS = 1e-05
LOG2E = 1.4426950408889634
KB = 256
VMEM = 10
RB = 128
HB = 256
BF = jnp.bfloat16
F32 = jnp.float32
MIB = 1 << 20


def nn(a, b):
    return lax.dot_general(a, b, (((1,), (0,)), ((), ())), preferred_element_type=F32)


def nt(a, b):
    return lax.dot_general(a, b, (((1,), (1,)), ((), ())), preferred_element_type=F32)


def tn(a, b):
    return lax.dot_general(a, b, (((0,), (0,)), ((), ())), preferred_element_type=F32)


def params(limit):
    return pltpu.CompilerParams(vmem_limit_bytes=limit * MIB)


def cost(micros):
    return pl.CostEstimate(flops=int(micros * 1.1e9), bytes_accessed=1024, transcendentals=0)


MICROS = {"project": 3, "attend_forward": 8, "attend_backward": 12, "entry_back": 5, "place": 3, "ahead": 9, "astern": 10, "inner_norm": 3, "weight_grads": 5}


def lane_parts(block):
    left = block[:, :128]
    lane = lax.broadcasted_iota(jnp.int32, left.shape, 1)
    zero = jnp.zeros_like(left)
    return (
        jnp.where(lane < HEAD_DIM, left, zero),
        jnp.where(lane >= HEAD_DIM, left, zero),
        block[:, 128:],
    )


TILE = (0, 0, 1)


def call(kernel, name, grid, meta, args, in_specs, out_specs, out_shape, scratch=(), limit=VMEM, hold=(), out=()):
    args = list(args)
    for i in hold:
        space = pltpu.VMEM if i >= 0 else pltpu.HBM
        spot = i if i >= 0 else -1 - i
        args[spot] = pltpu.with_memory_space_constraint(args[spot], space)
    if isinstance(out_shape, list):
        out_shape = [pltpu.VMEM(o.shape, o.dtype) if i in out else o for i, o in enumerate(out_shape)]
    return pl.pallas_call(
        kernel,
        grid_spec=pltpu.PrefetchScalarGridSpec(
            num_scalar_prefetch=1,
            grid=grid,
            in_specs=in_specs,
            out_specs=out_specs,
            scratch_shapes=scratch,
        ),
        out_shape=out_shape,
        compiler_params=params(limit),
        cost_estimate=cost(MICROS[name]),
        name=name,
    )(meta, *args)


def fixed(*shape):
    return pl.BlockSpec(shape, lambda *_: (0,) * len(shape))


def like(shape, dtype):
    return jax.ShapeDtypeStruct(shape, dtype)


def project_kernel(meta_ref, x_ref, wq_ref, wk_ref, wv_ref, q_ref, k_ref, v_ref):
    x = x_ref[...]
    for w_ref, o_ref in ((wq_ref, q_ref), (wk_ref, k_ref), (wv_ref, v_ref)):
        o_ref[:, :192] = nt(x, w_ref[...]).astype(BF)
        o_ref[:, 192:] = jnp.zeros((x.shape[0], HEAD_DIM), BF)


def project(meta, tokens, weights):
    rows, d = tokens.shape
    block = 256
    return call(
        project_kernel,
        "project",
        (rows // block,),
        meta,
        (tokens, *weights),
        [pl.BlockSpec((block, d), lambda i, m: (i, 0))] + [fixed(192, d)] * 3,
        [pl.BlockSpec((block, 256), lambda i, m: (i, 0))] * 3,
        [like((rows, 256), BF)] * 3,
        hold=(-1, -2, -3, -4),
        out=(0, 1, 2),
    )


def forward_kernel(u, meta_ref, q_ref, k_ref, v_ref, own_ref, other_ref, lse_ref, s_ref):
    length = meta_ref[1 + u]
    step = pl.program_id(0)
    blocks = lax.div(length + KB - 1, KB)
    parts = lane_parts(q_ref[...] * jnp.asarray(0.125, BF))
    width = q_ref.shape[0]

    def first(kb, highest):
        start = pl.multiple_of(kb * KB, KB)
        rows = pl.ds(start, KB)
        live = start + lax.broadcasted_iota(jnp.int32, (KB, width), 0) < length
        out = []
        for h in range(3):
            tile = pl.ds(128 * TILE[h], 128)
            s = nt(k_ref[rows, tile], parts[h])
            s = jnp.where(live, s, -1e30)
            s_ref[h, rows, :] = s
            out.append(jnp.maximum(highest[h], jnp.max(s, axis=0, keepdims=True)))
        return tuple(out)

    floor = jnp.full((1, width), -1e30, F32)
    highest = lax.fori_loop(0, blocks, first, (floor,) * 3)

    def second(kb, carry):
        rows = pl.ds(pl.multiple_of(kb * KB, KB), KB)
        out = []
        for h in range(3):
            total, result = carry[h]
            p = jnp.exp2((s_ref[h, rows, :] - highest[h]) * LOG2E)
            total = total + jnp.sum(p, axis=0, keepdims=True)
            v = v_ref[rows, pl.ds(128 * TILE[h], 128)]
            result = result + tn(v, p.astype(BF))
            out.append((total, result))
        return tuple(out)

    init = ((jnp.zeros((1, width), F32), jnp.zeros((128, width), F32)),) * 3
    done = lax.fori_loop(0, blocks, second, init)
    outs = []
    for h in range(3):
        total, result = done[h]
        lo = HEAD_DIM * (h % 2)
        o = result[lo : lo + HEAD_DIM] / total
        lse_ref[0, pl.ds(h, 1), :] = highest[h] * LOG2E + jnp.log2(total)
        outs.append(o.astype(BF))
    whole = jnp.concatenate(outs, axis=0)
    for j, o_ref in enumerate((own_ref, other_ref)):

        @pl.when(step == j)
        def _():
            o_ref[...] = whole


def attend_forward(meta, q, k, v, u, frames):
    half = frames // 2
    return call(
        functools.partial(forward_kernel, u),
        "attend_forward",
        (2,),
        meta,
        (q, k, v),
        [
            pl.BlockSpec((half, 256), lambda i, m: (u * 2 + (i ^ m[0]), 0)),
            pl.BlockSpec((frames, 256), lambda i, m: (u, 0)),
            pl.BlockSpec((frames, 256), lambda i, m: (u, 0)),
        ],
        [
            fixed(192, half),
            fixed(192, half),
            pl.BlockSpec((1, 8, half), lambda i, m: (i, 0, 0)),
        ],
        [
            like((192, half), BF),
            like((192, half), BF),
            like((2, 8, half), F32),
        ],
        [pltpu.VMEM((3, frames, half), F32)],
        hold=(0, 1, 2),
        out=(2,),
    )


def backward_kernel(
    u, meta_ref, q_ref, k_ref, v_ref, d0_ref, d1_ref, o0_ref, o1_ref, lse_ref,
    dq_ref, dk_ref, dv_ref, kt_ref, dk_acc, dv_acc, do_ref, o_ref,
):
    length = meta_ref[1 + u]
    blocks = lax.div(length + KB - 1, KB)
    step = pl.program_id(0)

    @pl.when(step == 0)
    def _():
        dk_acc[...] = jnp.zeros_like(dk_acc)
        dv_acc[...] = jnp.zeros_like(dv_acc)
        kt_ref[...] = jnp.transpose(k_ref[...])
        do_ref[...] = d0_ref[...]
        o_ref[...] = o0_ref[...]

    @pl.when(step == 1)
    def _():
        do_ref[...] = d1_ref[...]
        o_ref[...] = o1_ref[...]

    parts = lane_parts(q_ref[...] * jnp.asarray(0.125, BF))
    width = q_ref.shape[0]
    empty = jnp.zeros((HEAD_DIM, width), BF)
    head = [do_ref[pl.ds(h * HEAD_DIM, HEAD_DIM), :] for h in range(3)]
    grads = (
        jnp.concatenate([head[0], empty], axis=0),
        jnp.concatenate([empty, head[1]], axis=0),
        jnp.concatenate([head[2], empty], axis=0),
    )
    delta = [
        jnp.sum(
            head[h].astype(F32) * o_ref[pl.ds(h * HEAD_DIM, HEAD_DIM), :].astype(F32), axis=0, keepdims=True
        )
        for h in range(3)
    ]
    lse = [lse_ref[0, pl.ds(h, 1), :] for h in range(3)]

    def body(kb, carry):
        start = pl.multiple_of(kb * KB, KB)
        rows = pl.ds(start, KB)
        live = start + lax.broadcasted_iota(jnp.int32, (KB, width), 0) < length
        out = []
        for h in range(3):
            tile = pl.ds(128 * TILE[h], 128)
            s = nt(k_ref[rows, tile], parts[h])
            s = jnp.where(live, s, -1e30)
            p = jnp.exp2(s * LOG2E - lse[h])
            dp = nn(v_ref[rows, tile], grads[h])
            ds = (p * (dp - delta[h])).astype(BF)
            dv_acc[rows, tile] += nt(p.astype(BF), grads[h])
            dk_acc[rows, tile] += nn(ds, parts[h])
            kt = kt_ref[pl.ds(h * HEAD_DIM, HEAD_DIM), rows]
            out.append(carry[h] + nn(kt, ds))
        return tuple(out)

    zero = jnp.zeros((HEAD_DIM, width), F32)
    done = lax.fori_loop(0, blocks, body, (zero,) * 3)
    full = jnp.concatenate(done + (zero,), axis=0) * 0.125
    dq_ref[...] = jnp.transpose(full).astype(BF)

    @pl.when(step == 1)
    def _():
        dk_ref[...] = dk_acc[...].astype(BF)
        dv_ref[...] = dv_acc[...].astype(BF)


def attend_backward(meta, q, k, v, grads, outs, lse, u, frames):
    half = frames // 2
    return call(
        functools.partial(backward_kernel, u),
        "attend_backward",
        (2,),
        meta,
        (q, k, v, *grads, *outs, lse),
        [
            pl.BlockSpec((half, 256), lambda i, m: (u * 2 + (i ^ m[0]), 0)),
            pl.BlockSpec((frames, 256), lambda i, m: (u, 0)),
            pl.BlockSpec((frames, 256), lambda i, m: (u, 0)),
            fixed(192, half),
            fixed(192, half),
            fixed(192, half),
            fixed(192, half),
            pl.BlockSpec((1, 8, half), lambda i, m: (i, 0, 0)),
        ],
        [
            pl.BlockSpec((half, 256), lambda i, m: (i ^ m[0], 0)),
            fixed(frames, 256),
            fixed(frames, 256),
        ],
        [like((frames, 256), BF)] * 3,
        [
            pltpu.VMEM((256, frames), BF),
            pltpu.VMEM((frames, 256), F32),
            pltpu.VMEM((frames, 256), F32),
            pltpu.VMEM((192, half), BF),
            pltpu.VMEM((192, half), BF),
        ],
        hold=(0, 1, 2, 7),
        out=(0, 1, 2),
    )


def entry_kernel(meta_ref, x_ref, dq_ref, dk_ref, dv_ref, wq_ref, wk_ref, wv_ref, *refs):
    before_ref = refs[0] if len(refs) == 5 else None
    send_ref, keep_ref, sum_ref, acc = refs[-4:]
    step = pl.program_id(0)
    x = x_ref[...]
    total = jnp.zeros(x.shape, F32)
    for i, (g_ref, w_ref) in enumerate(((dq_ref, wq_ref), (dk_ref, wk_ref), (dv_ref, wv_ref))):
        rows = pl.ds(192 * i, 192)
        g = g_ref[:, :192]
        total = total + nn(g, w_ref[...])
        product = tn(g, x)

        @pl.when(step == 0)
        def _():
            acc[rows, :] = product if before_ref is None else product + before_ref[rows, :]

        @pl.when(step == 1)
        def _():
            sum_ref[rows, :] = (product + acc[rows, :]).astype(sum_ref.dtype)

    low = total.astype(BF)

    @pl.when(step == 0)
    def _():
        send_ref[...] = low

    @pl.when(step == 1)
    def _():
        keep_ref[...] = low


def entry_back(meta, tokens, grads, weights, before, u, frames, dtype):
    half = frames // 2
    d = tokens.shape[1]
    return call(
        entry_kernel,
        "entry_back",
        (2,),
        meta,
        (tokens, *grads, *weights, *before),
        [pl.BlockSpec((half, d), lambda i, m: (u * 2 + (1 - i ^ m[0]), 0))]
        + [pl.BlockSpec((half, 256), lambda i, m: (1 - i ^ m[0], 0))] * 3
        + [fixed(192, d)] * 3
        + [fixed(576, d)] * len(before),
        [fixed(half, d), fixed(half, d), fixed(576, d)],
        [like((half, d), BF), like((half, d), BF), like((576, d), dtype)],
        [pltpu.VMEM((576, d), F32)],
        hold=(-1, 1, 2, 3, -5, -6, -7),
    )


def place_kernel(meta_ref, *refs):
    o_ref = refs[-1]
    for i, r_ref in enumerate(refs[:-1]):

        @pl.when(pl.program_id(0) == i)
        def _():
            o_ref[...] = r_ref[...]


def place(meta, own, other):
    half, d = own[0].shape
    count = 2 * len(own)
    return call(
        place_kernel,
        "place",
        (count,),
        meta,
        [block for pair in zip(own, other) for block in pair],
        [fixed(half, d)] * count,
        pl.BlockSpec((half, d), lambda i, m: (i ^ m[0], 0)),
        like((count * half, d), own[0].dtype),
    )


def normalise(values):
    average = jnp.mean(values, axis=-1, keepdims=True)
    centred = values - average
    spread = jnp.mean(centred * centred, axis=-1, keepdims=True)
    rstd = lax.rsqrt(spread + EPS)
    return centred * rstd, rstd


def gelu_pair(v):
    e = jnp.exp2(v * v * (-0.5 * LOG2E))
    t = 1.0 / (1.0 + (0.3275911 * 0.7071067811865476) * jnp.abs(v))
    poly = t * (0.5 * 0.254829592 + t * (0.5 * -0.284496736 + t * (0.5 * 1.421413741 + t * (0.5 * -1.453152027 + t * (0.5 * 1.061405429)))))
    tail = poly * e
    phi_cap = jnp.where(v >= 0, 1.0 - tail, tail)
    return v * phi_cap, phi_cap + v * (e * 0.3989422804014327)


def ahead_kernel(
    meta_ref, tok_ref, a0, a1, a2, a3, w0, w1, w2, w3, ua_ref, ub_ref, da_ref, db_ref, vec_ref,
    xhat_ref, rstd_ref, low_ref, act_ref, slope_ref, own_ref, sent_ref,
):
    gain, bias = vec_ref[0:1, :], vec_ref[1:2, :]
    hidden = ua_ref.shape[1]
    for r in range(tok_ref.shape[0] // RB):
        rows = pl.ds(r * RB, RB)
        branch = jnp.zeros((RB, tok_ref.shape[1]), F32)
        for a, w in ((a0, w0), (a1, w1), (a2, w2), (a3, w3)):
            branch = branch + tn(a[:, rows], w[...]).astype(BF).astype(F32)
        xhat, rstd = normalise(tok_ref[rows, :].astype(F32) + branch)
        xhat_ref[rows, :] = xhat
        rstd_ref[rows, :] = jnp.broadcast_to(rstd, (RB, rstd_ref.shape[1]))
        normed = xhat * gain + bias
        low = normed.astype(BF)
        low_ref[rows, :] = low
        sent = jnp.zeros(normed.shape, F32)
        for g, (up, down) in enumerate(((ua_ref, da_ref), (ub_ref, db_ref))):
            acts = []
            for c in range(hidden // HB):
                act, slope = gelu_pair(nn(low, up[:, c * HB : (c + 1) * HB]))
                columns = pl.ds(g * hidden + c * HB, HB)
                acts.append(act.astype(BF))
                act_ref[rows, columns] = acts[-1]
                slope_ref[rows, columns] = slope.astype(BF)
            sent = sent + nn(jnp.concatenate(acts, axis=1), down[...]).astype(BF).astype(F32)
        own_ref[rows, :] = normed + sent
        sent_ref[rows, :] = sent.astype(BF)


def ahead(meta, tokens, att, merge_w, up, down, vectors, u):
    half = att[0].shape[1]
    d, hidden = up[0].shape
    return call(
        ahead_kernel,
        "ahead",
        (1,),
        meta,
        (tokens, *att, *merge_w, *up, *down, vectors),
        [pl.BlockSpec((half, d), lambda i, m: (u * 2 + m[0], 0))]
        + [fixed(192, half)] * 4
        + [fixed(192, d)] * 4
        + [fixed(d, hidden)] * 2
        + [fixed(hidden, d)] * 2
        + [fixed(4, d)],
        [fixed(half, d), fixed(half, 128), fixed(half, d), fixed(half, 2 * hidden), fixed(half, 2 * hidden), fixed(half, d), fixed(half, d)],
        [
            like((half, d), F32),
            like((half, 128), F32),
            like((half, d), BF),
            like((half, 2 * hidden), BF),
            like((half, 2 * hidden), BF),
            like((half, d), F32),
            like((half, d), BF),
        ],
        hold=(-1,),
        out=(0, 1, 2, 3, 4, 5),
    )


def astern_kernel(u, meta_ref, own_ref, far_ref, grad_ref, span_ref, ua_ref, ub_ref, da_ref, db_ref, slope_ref, vec_ref, *refs):
    last = len(refs) > 6
    before = refs[: len(refs) - 10] if last else ()
    out_ref, g_ref, pre_ref, back_ref, sent_ref, small_ref = refs[len(before) : len(before) + 6]
    gain, bias = vec_ref[2:3, :], vec_ref[3:4, :]
    half, d = own_ref.shape
    hidden = ua_ref.shape[1]
    starts = span_ref[u : u + 1, :]
    gain_grad = jnp.zeros(gain.shape, F32)
    bias_grad = jnp.zeros(gain.shape, F32)
    for r in range(half // RB):
        rows = pl.ds(r * RB, RB)
        xhat, rstd = normalise(own_ref[rows, :] + far_ref[rows, :].astype(F32))
        out_ref[rows, :] = (xhat * gain + bias).astype(BF)
        frame = meta_ref[0] * half + r * RB + lax.broadcasted_iota(jnp.int32, (RB, starts.shape[1]), 0)
        inside = (frame >= starts) & (frame < starts + SPAN)
        weight = jnp.max(jnp.where(inside, 1.0, 0.0), axis=1, keepdims=True)
        cot = grad_ref[rows, :].astype(F32) * weight
        gain_grad = gain_grad + jnp.sum(cot * xhat, axis=0, keepdims=True)
        bias_grad = bias_grad + jnp.sum(cot, axis=0, keepdims=True)
        gy = cot * gain
        mean_gy = jnp.mean(gy, axis=-1, keepdims=True)
        mean_gx = jnp.mean(gy * xhat, axis=-1, keepdims=True)
        sum_grad = rstd * (gy - mean_gy - xhat * mean_gx)
        low = sum_grad.astype(BF)
        g_ref[rows, :] = low
        sent = jnp.zeros(sum_grad.shape, F32)
        for g, (up, down) in enumerate(((ua_ref, da_ref), (ub_ref, db_ref))):
            pres = []
            for c in range(hidden // HB):
                columns = pl.ds(g * hidden + c * HB, HB)
                slope = slope_ref[rows, columns].astype(F32)
                pres.append((nt(low, down[c * HB : (c + 1) * HB, :]) * slope).astype(BF))
                pre_ref[rows, columns] = pres[-1]
            sent = sent + nt(jnp.concatenate(pres, axis=1), up[...]).astype(BF).astype(F32)
        back_ref[rows, :] = sum_grad + sent
        sent_ref[rows, :] = sent.astype(BF)
    small_ref[0:1, :] = gain_grad
    small_ref[1:2, :] = bias_grad
    if last:
        x_ref, act_ref = before[:2]
        weight_sums(x_ref[...], g_ref[...], act_ref, pre_ref, before[2:], refs[-4:])


def astern(meta, own, far, grad, spans, up, down, slope, vectors, u, before):
    half, d = own.shape
    hidden = up[0].shape[1]
    rows = fixed(half, d)
    wide = fixed(half, 2 * hidden)
    grads = [] if not before else [(d, hidden)] * 2 + [(hidden, d)] * 2
    extra = [] if not before else [rows, wide] + [fixed(*shape) for shape in grads[: len(before) - 2]]
    return call(
        functools.partial(astern_kernel, u),
        "astern",
        (1,),
        meta,
        (own, far, grad, spans, *up, *down, slope, vectors, *before),
        [rows] * 2
        + [pl.BlockSpec((half, d), lambda i, m: (u * 2 + m[0], 0)), fixed(*spans.shape)]
        + [fixed(d, hidden)] * 2
        + [fixed(hidden, d)] * 2
        + [wide, fixed(4, d)]
        + extra,
        [rows, rows, wide, rows, rows, fixed(2, d)] + [fixed(*shape) for shape in grads],
        [
            like((half, d), BF),
            like((half, d), BF),
            like((half, 2 * hidden), BF),
            like((half, d), F32),
            like((half, d), BF),
            like((2, d), F32),
        ]
        + [like(shape, BF) for shape in grads],
        limit=12 if before else VMEM,
        hold=(0, -3, 8, *range(10, 10 + len(before))),
        out=(3,) if before else (1, 2, 3),
    )


def weight_kernel(meta_ref, x_ref, g_ref, act_ref, pre_ref, *refs):
    before, sums = refs[:-4], refs[-4:]
    weight_sums(x_ref[...], g_ref[...], act_ref, pre_ref, before, sums)


def weight_sums(x, g, act_ref, pre_ref, before, sums):
    hidden = act_ref.shape[1] // 2
    for i in range(2):
        for c in range(hidden // HB):
            columns = pl.ds(i * hidden + c * HB, HB)
            block = pl.ds(c * HB, HB)
            up = tn(x, pre_ref[:, columns])
            down = tn(act_ref[:, columns], g)
            if before:
                up = up + before[i][:, block].astype(F32)
                down = down + before[2 + i][block, :].astype(F32)
            sums[i][:, block] = up.astype(BF)
            sums[2 + i][block, :] = down.astype(BF)


def weight_grads(meta, x, g, act, pre, before):
    rows, d = x.shape
    hidden = act.shape[1] // 2
    shapes = [(d, hidden)] * 2 + [(hidden, d)] * 2
    return call(
        weight_kernel,
        "weight_grads",
        (1,),
        meta,
        (x, g, act, pre, *before),
        [fixed(rows, d)] * 2 + [fixed(rows, 2 * hidden)] * 2 + [fixed(*shape) for shape in shapes[: len(before)]],
        [fixed(*shape) for shape in shapes],
        [like(shape, BF) for shape in shapes],
        hold=(0, 1, 2, 3),
        out=(0, 1, 2, 3),
    )


def inner_kernel(meta_ref, own_ref, far_ref, xhat_ref, rstd_ref, vec_ref, a0, a1, w0, w1, *refs):
    last = len(refs) == 11
    out_ref, g0, g1, m0, m1, small_ref = refs[-6:]
    grad = own_ref[...] + far_ref[...].astype(F32)
    xhat = xhat_ref[...]
    gain_grad = jnp.sum(grad * xhat, axis=0, keepdims=True)
    bias_grad = jnp.sum(grad, axis=0, keepdims=True)
    gy = grad * vec_ref[0:1, :]
    mean_gy = jnp.mean(gy, axis=-1, keepdims=True)
    mean_gx = jnp.mean(gy * xhat, axis=-1, keepdims=True)
    inner = rstd_ref[:, 0:1] * (gy - mean_gy - xhat * mean_gx)
    out_ref[...] = inner
    low = inner.astype(BF)
    g0[...] = nt(w0[...], low).astype(BF)
    g1[...] = nt(w1[...], low).astype(BF)
    small = jnp.concatenate([gain_grad, bias_grad], axis=0)
    small_ref[...] = small
    if last:
        before0, before1, before_small, outer0, outer1 = refs[:5]
        below = jnp.concatenate(
            [small + before_small[...], outer0[...] + outer1[...], jnp.zeros((60, small.shape[1]), F32)], axis=0
        ).astype(BF)
        for m, a, before in ((m0, a0, before0), (m1, a1, before1)):
            m[:192, :] = (nn(a[...], low) + before[...]).astype(BF)
            m[192:, :] = below
    else:
        m0[...] = nn(a0[...], low)
        m1[...] = nn(a1[...], low)


def inner_norm(meta, own, far, xhat, rstd, vectors, att, weights, before):
    rows, d = xhat.shape
    merge = like((256, d), BF) if before else like((192, d), F32)
    return call(
        inner_kernel,
        "inner_norm",
        (1,),
        meta,
        (own, far, xhat, rstd, vectors, *att, *weights, *before),
        [fixed(rows, d)] * 3
        + [fixed(rows, 128), fixed(4, d)]
        + [fixed(192, rows)] * 2
        + [fixed(192, d)] * 2
        + ([fixed(192, d)] * 2 + [fixed(2, d)] * 3 if before else []),
        [fixed(rows, d), fixed(192, rows), fixed(192, rows), fixed(*merge.shape), fixed(*merge.shape), fixed(2, d)],
        [like((rows, d), F32), like((192, rows), BF), like((192, rows), BF), merge, merge, like((2, d), F32)],
        hold=(0, 2, 3),
    )


def local(groups, tokens, lengths, span_starts, wq, wk, wv, wm, wu, wd, ig, ib, og, ob, out_grad):
    rows, d = tokens.shape
    seqs = lengths.shape[0]
    frames = rows // seqs
    half = frames // 2
    core = lax.axis_index("tensor") % 2
    place_dp = lax.axis_index("dp")
    bits = groups.bit_length() - 1

    def swap(value, k):
        return lax.ppermute(value, "tensor", [(i, i ^ k) for i in range(4)])

    def swap_dp(value, k):
        return lax.ppermute(value, "dp", [(i, i ^ k) for i in range(groups)])

    def add(a, b):
        return (a.astype(F32) + b.astype(F32)).astype(BF)

    def cut(array, index, count):
        size = array.shape[0] // count
        return lax.dynamic_slice_in_dim(array, index * size, size, 0)

    def total(pieces):
        return sum(piece.astype(F32) for piece in pieces).astype(BF) if len(pieces) > 1 else pieces[0]

    class Chain:
        def __init__(self, parts, order, back=None):
            self.parts = parts
            self.order = order
            self.held = list(order)
            self.steps = [(True, *stage) for stage in order] + [(False, *stage) for stage in back or reversed(order)]

        def start(self):
            if self.steps:
                scatter, low_bit, width = self.steps[0]
                count = 1 << width
                spot = (place_dp >> low_bit) & (count - 1)
                pick = lambda j: total([cut(part, spot ^ j, count) if scatter else part for part in self.parts])
                self.pending = [swap_dp(pick(j), j << low_bit) for j in range(1, count)]

        def finish(self, *after):
            if not self.steps:
                return
            scatter, low_bit, width = self.steps.pop(0)
            got = self.pending
            if after:
                got = list(lax.optimization_barrier((*got, *after))[: len(got)])
            count = 1 << width
            spot = (place_dp >> low_bit) & (count - 1)
            if scatter:
                self.state = total([cut(part, spot, count) for part in self.parts] + got)
                if all(step[0] is False for step in self.steps):
                    self.state = self.state.reshape((1,) * len(self.order) + self.state.shape)
            else:
                axis = self.order.index((low_bit, width))
                mine = self.parts[0]
                if count == 2:
                    halves = [jnp.where(spot, got[0], mine), jnp.where(spot, mine, got[0])]
                    self.state = jnp.concatenate(halves, axis=axis)
                else:
                    whole = jnp.zeros(mine.shape[:axis] + (count,) + mine.shape[axis + 1 :], BF)
                    for j, piece in enumerate([mine] + got):
                        whole = lax.dynamic_update_slice_in_dim(whole, piece, spot ^ j, axis)
                    self.state = whole
                if not self.steps:
                    self.state = self.state.reshape(-1, d)
            self.parts = (self.state,)

    scalars = jnp.concatenate([core.reshape(1), lengths])
    token = []

    def meta():
        return lax.optimization_barrier((scalars, *token))[0] if token else scalars

    def done(results, *others):
        token[:] = [results[0], *others]
        return results

    merge_w = (wm, swap(wm, 1), swap(wm, 2), swap(wm, 3))
    up_w = (wu, swap(wu, 1))
    down_w = (wd, swap(wd, 1))
    vectors = jnp.stack([ig, ib, og, ob])
    qkv_w = (wq.T, wk.T, wv.T)

    q, k, v = project(scalars, tokens, qkv_w)
    fwd, att = [], []
    for u in range(seqs):
        fwd.append(done(attend_forward(meta(), q, k, v, u, frames), *merge_w[1:], up_w[1], down_w[1]))
        own, other = fwd[u][:2]
        att.append((own, swap(other, 1), swap(own, 2), swap(other, 3)))
    front, far = [], []
    for u in range(seqs):
        front.append(done(ahead(meta(), tokens, att[u], merge_w, up_w, down_w, vectors, u)))
        far.append(swap(front[u][6], 2))
    back, far_grad, sums = [], [], ()
    for u in range(seqs):
        before = (front[u][2], front[u][3], *sums) if u == seqs - 1 else ()
        back.append(
            done(astern(meta(), front[u][5], far[u], out_grad, span_starts, up_w, down_w, front[u][4], vectors, u, before))
        )
        if u < seqs - 1:
            far_grad.append(swap(back[u][4], 2))
            sums = done(weight_grads(meta(), front[u][2], back[u][1], front[u][3], back[u][2], sums))

    def inner_step(u, before):
        res = done(inner_norm(meta(), back[u][3], far_grad[u], front[u][0], front[u][1], vectors, att[u][:2], merge_w[:2], before))
        return res, (res[1], swap(res[2], 1))

    def attend_step(u, grads):
        return done(attend_backward(meta(), q, k, v, grads, fwd[u][:2], fwd[u][2], u, frames))

    def entry_step(u, grads, before, dtype):
        return done(entry_back(meta(), tokens, grads, qkv_w, before, u, frames, dtype))


    stages = [(0, 1)] + [(b, 2) for b in range(1, bits - 1, 2)] + ([(bits - 1, 1)] if bits % 2 == 0 else [])
    inner, near, crossed, so_far, entry, spare = [], [], [], (), [], []

    def together(group, *others):
        values = lax.optimization_barrier((*(chain.state for chain in group), *others))
        for chain, value in zip(group, values):
            chain.state, chain.parts = value, (value,)
        return values[len(group) :]

    for u in range(seqs):
        last = u == seqs - 1
        if u == 0:
            up_own, up_other, down_own, down_other = lax.optimization_barrier((*back[-1][6:], far_grad[0]))[:4]
            res, grads = inner_step(0, ())
            inner.append(res)
            far_grad.append(swap(lax.optimization_barrier((back[-1][4], res[0]))[0], 2))
            down_sum, up_sum = total((down_own, swap(down_other, 1))), total((up_own, swap(up_other, 1)))
            token.extend([down_sum, up_sum])
            down_sum, up_sum = lax.psum((down_sum, up_sum), "dp")
        dqkv = attend_step(u, grads)
        if not last:
            before = ()
            if u + 1 == seqs - 1:
                before = (inner[0][3], inner[0][4], inner[0][5], back[0][5], back[1][5])
            res, grads = inner_step(u + 1, before)
            inner.append(res)
        out = entry_step(u, dqkv, so_far, BF if last else F32)
        so_far = (out[2],)
        entry.append(out)
    qkv = Chain((so_far[0],), stages)
    merge = Chain((res[3], swap(lax.optimization_barrier((res[4], entry[0][0]))[0], 1)), stages[1:] + stages[:1])
    for u in range(seqs):
        got = swap(entry[u][0], 1)
        near.append(entry[u][1].astype(F32) + got.astype(F32))
        crossed.append(swap(near[u].astype(BF), 2))
    chains = [qkv, merge]
    for chain in chains:
        chain.start()
    while any(chain.steps for chain in chains):
        for chain in chains:
            chain.finish()
        together(chains)
        for chain in chains:
            chain.start()
    merge_sum, qkv_sum = merge.state, qkv.state

    pairs = [[i, i + 1] for i in range(0, 4, 2)]

    def both_cores(blocks):
        whole = lax.all_gather(jnp.stack(blocks), "tensor", axis=1, tiled=True, axis_index_groups=pairs)
        return whole.reshape(rows, d)

    down_sum, up_sum = down_sum.astype(F32), up_sum.astype(F32)
    layer_output = both_cores(list(lax.optimization_barrier((*(b[0] for b in back), inner[0][0]))[:seqs]))
    layer_output, down_sum, up_sum = lax.optimization_barrier((layer_output, down_sum, up_sum))
    input_grad = both_cores([(inner[u][0] + (near[u] + crossed[u].astype(F32))).astype(BF) for u in range(seqs)])

    small = merge_sum[192:196].astype(F32)
    query_grad, key_grad, value_grad = (qkv_sum[192 * i : 192 * (i + 1)].astype(F32).T for i in range(3))
    return (
        layer_output,
        input_grad,
        query_grad,
        key_grad,
        value_grad,
        merge_sum[:192].astype(F32),
        up_sum,
        down_sum,
        small[0],
        small[1],
        small[2],
        small[3],
    )


def solution(mesh):
    in_specs = (
        P("dp", None),
        P("dp"),
        P("dp", None),
        P(None, "tensor"),
        P(None, "tensor"),
        P(None, "tensor"),
        P("tensor", None),
        P(None, "tensor"),
        P("tensor", None),
        P(),
        P(),
        P(),
        P(),
        P("dp", None),
    )
    out_specs = (
        P("dp", None),
        P("dp", None),
        P(None, "tensor"),
        P(None, "tensor"),
        P(None, "tensor"),
        P("tensor", None),
        P(None, "tensor"),
        P("tensor", None),
        P(),
        P(),
        P(),
        P(),
    )
    body = functools.partial(local, mesh.shape["dp"])
    return jax.shard_map(body, mesh=mesh, in_specs=in_specs, out_specs=out_specs, check_vma=False)
```

```python
import functools

import jax
import jax.numpy as jnp
from jax import lax
from jax.experimental import pallas as pl
from jax.experimental.pallas import tpu as pltpu
from jax.sharding import PartitionSpec as P

HEAD_DIM = 64
SPAN = 10
EPS = 1e-05
LOG2E = 1.4426950408889634
KB = 256
VMEM = 10
RB = 128
HB = 256
BF = jnp.bfloat16
F32 = jnp.float32
MIB = 1 << 20


def nn(a, b):
    return lax.dot_general(a, b, (((1,), (0,)), ((), ())), preferred_element_type=F32)


def nt(a, b):
    return lax.dot_general(a, b, (((1,), (1,)), ((), ())), preferred_element_type=F32)


def tn(a, b):
    return lax.dot_general(a, b, (((0,), (0,)), ((), ())), preferred_element_type=F32)


def params(limit):
    return pltpu.CompilerParams(vmem_limit_bytes=limit * MIB)


def cost(micros):
    return pl.CostEstimate(flops=int(micros * 1.1e9), bytes_accessed=1024, transcendentals=0)


MICROS = {"project": 3, "attend_forward": 8, "attend_backward": 12, "entry_back": 5, "place": 3, "ahead": 9, "astern": 10, "inner_norm": 3, "weight_grads": 5}


def lane_parts(block):
    left = block[:, :128]
    lane = lax.broadcasted_iota(jnp.int32, left.shape, 1)
    zero = jnp.zeros_like(left)
    return (
        jnp.where(lane < HEAD_DIM, left, zero),
        jnp.where(lane >= HEAD_DIM, left, zero),
        block[:, 128:],
    )


TILE = (0, 0, 1)


def call(kernel, name, grid, meta, args, in_specs, out_specs, out_shape, scratch=(), limit=VMEM, hold=(), out=()):
    args = list(args)
    for i in hold:
        space = pltpu.VMEM if i >= 0 else pltpu.HBM
        spot = i if i >= 0 else -1 - i
        args[spot] = pltpu.with_memory_space_constraint(args[spot], space)
    if isinstance(out_shape, list):
        out_shape = [pltpu.VMEM(o.shape, o.dtype) if i in out else o for i, o in enumerate(out_shape)]
    return pl.pallas_call(
        kernel,
        grid_spec=pltpu.PrefetchScalarGridSpec(
            num_scalar_prefetch=1,
            grid=grid,
            in_specs=in_specs,
            out_specs=out_specs,
            scratch_shapes=scratch,
        ),
        out_shape=out_shape,
        compiler_params=params(limit),
        cost_estimate=cost(MICROS[name]),
        name=name,
    )(meta, *args)


def fixed(*shape):
    return pl.BlockSpec(shape, lambda *_: (0,) * len(shape))


def like(shape, dtype):
    return jax.ShapeDtypeStruct(shape, dtype)


def project_kernel(meta_ref, x_ref, wq_ref, wk_ref, wv_ref, q_ref, k_ref, v_ref):
    x = x_ref[...]
    for w_ref, o_ref in ((wq_ref, q_ref), (wk_ref, k_ref), (wv_ref, v_ref)):
        o_ref[:, :192] = nt(x, w_ref[...]).astype(BF)
        o_ref[:, 192:] = jnp.zeros((x.shape[0], HEAD_DIM), BF)


def project(meta, tokens, weights):
    rows, d = tokens.shape
    block = 256
    return call(
        project_kernel,
        "project",
        (rows // block,),
        meta,
        (tokens, *weights),
        [pl.BlockSpec((block, d), lambda i, m: (i, 0))] + [fixed(192, d)] * 3,
        [pl.BlockSpec((block, 256), lambda i, m: (i, 0))] * 3,
        [like((rows, 256), BF)] * 3,
        hold=(-1, -2, -3, -4),
        out=(0, 1, 2),
    )


def forward_kernel(u, meta_ref, q_ref, k_ref, v_ref, own_ref, other_ref, lse_ref, s_ref):
    length = meta_ref[1 + u]
    step = pl.program_id(0)
    blocks = lax.div(length + KB - 1, KB)
    parts = lane_parts(q_ref[...] * jnp.asarray(0.125, BF))
    width = q_ref.shape[0]

    def first(kb, highest):
        start = pl.multiple_of(kb * KB, KB)
        rows = pl.ds(start, KB)
        live = start + lax.broadcasted_iota(jnp.int32, (KB, width), 0) < length
        out = []
        for h in range(3):
            tile = pl.ds(128 * TILE[h], 128)
            s = nt(k_ref[rows, tile], parts[h])
            s = jnp.where(live, s, -1e30)
            s_ref[h, rows, :] = s
            out.append(jnp.maximum(highest[h], jnp.max(s, axis=0, keepdims=True)))
        return tuple(out)

    floor = jnp.full((1, width), -1e30, F32)
    highest = lax.fori_loop(0, blocks, first, (floor,) * 3)

    def second(kb, carry):
        rows = pl.ds(pl.multiple_of(kb * KB, KB), KB)
        out = []
        for h in range(3):
            total, result = carry[h]
            p = jnp.exp2((s_ref[h, rows, :] - highest[h]) * LOG2E)
            total = total + jnp.sum(p, axis=0, keepdims=True)
            v = v_ref[rows, pl.ds(128 * TILE[h], 128)]
            result = result + tn(v, p.astype(BF))
            out.append((total, result))
        return tuple(out)

    init = ((jnp.zeros((1, width), F32), jnp.zeros((128, width), F32)),) * 3
    done = lax.fori_loop(0, blocks, second, init)
    outs = []
    for h in range(3):
        total, result = done[h]
        lo = HEAD_DIM * (h % 2)
        o = result[lo : lo + HEAD_DIM] / total
        lse_ref[0, pl.ds(h, 1), :] = highest[h] * LOG2E + jnp.log2(total)
        outs.append(o.astype(BF))
    whole = jnp.concatenate(outs, axis=0)
    for j, o_ref in enumerate((own_ref, other_ref)):

        @pl.when(step == j)
        def _():
            o_ref[...] = whole


def attend_forward(meta, q, k, v, u, frames):
    half = frames // 2
    return call(
        functools.partial(forward_kernel, u),
        "attend_forward",
        (2,),
        meta,
        (q, k, v),
        [
            pl.BlockSpec((half, 256), lambda i, m: (u * 2 + (i ^ m[0]), 0)),
            pl.BlockSpec((frames, 256), lambda i, m: (u, 0)),
            pl.BlockSpec((frames, 256), lambda i, m: (u, 0)),
        ],
        [
            fixed(192, half),
            fixed(192, half),
            pl.BlockSpec((1, 8, half), lambda i, m: (i, 0, 0)),
        ],
        [
            like((192, half), BF),
            like((192, half), BF),
            like((2, 8, half), F32),
        ],
        [pltpu.VMEM((3, frames, half), F32)],
        hold=(0, 1, 2),
        out=(2,),
    )


def backward_kernel(
    u, meta_ref, q_ref, k_ref, v_ref, d0_ref, d1_ref, o0_ref, o1_ref, lse_ref,
    dq_ref, dk_ref, dv_ref, kt_ref, dk_acc, dv_acc, do_ref, o_ref,
):
    length = meta_ref[1 + u]
    blocks = lax.div(length + KB - 1, KB)
    step = pl.program_id(0)

    @pl.when(step == 0)
    def _():
        dk_acc[...] = jnp.zeros_like(dk_acc)
        dv_acc[...] = jnp.zeros_like(dv_acc)
        kt_ref[...] = jnp.transpose(k_ref[...])
        do_ref[...] = d0_ref[...]
        o_ref[...] = o0_ref[...]

    @pl.when(step == 1)
    def _():
        do_ref[...] = d1_ref[...]
        o_ref[...] = o1_ref[...]

    parts = lane_parts(q_ref[...] * jnp.asarray(0.125, BF))
    width = q_ref.shape[0]
    empty = jnp.zeros((HEAD_DIM, width), BF)
    head = [do_ref[pl.ds(h * HEAD_DIM, HEAD_DIM), :] for h in range(3)]
    grads = (
        jnp.concatenate([head[0], empty], axis=0),
        jnp.concatenate([empty, head[1]], axis=0),
        jnp.concatenate([head[2], empty], axis=0),
    )
    delta = [
        jnp.sum(
            head[h].astype(F32) * o_ref[pl.ds(h * HEAD_DIM, HEAD_DIM), :].astype(F32), axis=0, keepdims=True
        )
        for h in range(3)
    ]
    lse = [lse_ref[0, pl.ds(h, 1), :] for h in range(3)]

    def body(kb, carry):
        start = pl.multiple_of(kb * KB, KB)
        rows = pl.ds(start, KB)
        live = start + lax.broadcasted_iota(jnp.int32, (KB, width), 0) < length
        out = []
        for h in range(3):
            tile = pl.ds(128 * TILE[h], 128)
            s = nt(k_ref[rows, tile], parts[h])
            s = jnp.where(live, s, -1e30)
            p = jnp.exp2(s * LOG2E - lse[h])
            dp = nn(v_ref[rows, tile], grads[h])
            ds = (p * (dp - delta[h])).astype(BF)
            dv_acc[rows, tile] += nt(p.astype(BF), grads[h])
            dk_acc[rows, tile] += nn(ds, parts[h])
            kt = kt_ref[pl.ds(h * HEAD_DIM, HEAD_DIM), rows]
            out.append(carry[h] + nn(kt, ds))
        return tuple(out)

    zero = jnp.zeros((HEAD_DIM, width), F32)
    done = lax.fori_loop(0, blocks, body, (zero,) * 3)
    full = jnp.concatenate(done + (zero,), axis=0) * 0.125
    dq_ref[...] = jnp.transpose(full).astype(BF)

    @pl.when(step == 1)
    def _():
        dk_ref[...] = dk_acc[...].astype(BF)
        dv_ref[...] = dv_acc[...].astype(BF)


def attend_backward(meta, q, k, v, grads, outs, lse, u, frames):
    half = frames // 2
    return call(
        functools.partial(backward_kernel, u),
        "attend_backward",
        (2,),
        meta,
        (q, k, v, *grads, *outs, lse),
        [
            pl.BlockSpec((half, 256), lambda i, m: (u * 2 + (i ^ m[0]), 0)),
            pl.BlockSpec((frames, 256), lambda i, m: (u, 0)),
            pl.BlockSpec((frames, 256), lambda i, m: (u, 0)),
            fixed(192, half),
            fixed(192, half),
            fixed(192, half),
            fixed(192, half),
            pl.BlockSpec((1, 8, half), lambda i, m: (i, 0, 0)),
        ],
        [
            pl.BlockSpec((half, 256), lambda i, m: (i ^ m[0], 0)),
            fixed(frames, 256),
            fixed(frames, 256),
        ],
        [like((frames, 256), BF)] * 3,
        [
            pltpu.VMEM((256, frames), BF),
            pltpu.VMEM((frames, 256), F32),
            pltpu.VMEM((frames, 256), F32),
            pltpu.VMEM((192, half), BF),
            pltpu.VMEM((192, half), BF),
        ],
        hold=(-1, -2, -3, 7),
        out=(0, 1, 2),
    )


def entry_kernel(meta_ref, x_ref, dq_ref, dk_ref, dv_ref, wq_ref, wk_ref, wv_ref, *refs):
    last = len(refs) == 7
    before_ref = refs[0] if last else None
    send_ref, keep_ref, sum_ref, acc = refs[-4:]
    step = pl.program_id(0)
    x = x_ref[...]
    total = jnp.zeros(x.shape, F32)
    for i, (g_ref, w_ref) in enumerate(((dq_ref, wq_ref), (dk_ref, wk_ref), (dv_ref, wv_ref))):
        rows = pl.ds(192 * i, 192)
        g = g_ref[:, :192]
        total = total + nn(g, w_ref[...])
        product = tn(g, x)

        @pl.when(step == 0)
        def _():
            acc[rows, :] = product if before_ref is None else product + before_ref[rows, :]

        @pl.when(step == 1)
        def _():
            sum_ref[rows, :] = (product + acc[rows, :]).astype(sum_ref.dtype)

    low = total.astype(BF)

    @pl.when(step == 0)
    def _():
        send_ref[...] = low
        if last:
            merged = refs[1][...].astype(F32) + refs[2][...].astype(F32)
            sum_ref[576:, :] = merged.astype(sum_ref.dtype)

    @pl.when(step == 1)
    def _():
        keep_ref[...] = low


def entry_back(meta, tokens, grads, weights, before, u, frames):
    half = frames // 2
    d = tokens.shape[1]
    rows, dtype = (832, BF) if before else (576, F32)
    return call(
        entry_kernel,
        "entry_back",
        (2,),
        meta,
        (tokens, *grads, *weights, *before),
        [pl.BlockSpec((half, d), lambda i, m: (u * 2 + (1 - i ^ m[0]), 0))]
        + [pl.BlockSpec((half, 256), lambda i, m: (1 - i ^ m[0], 0))] * 3
        + [fixed(192, d)] * 3
        + [fixed(*value.shape) for value in before],
        [fixed(half, d), fixed(half, d), fixed(rows, d)],
        [like((half, d), BF), like((half, d), BF), like((rows, d), dtype)],
        [pltpu.VMEM((576, d), F32)],
        hold=(-1, 1, 2, 3, -5, -6, -7),
    )


def place_kernel(meta_ref, *refs):
    o_ref = refs[-1]
    for i, r_ref in enumerate(refs[:-1]):

        @pl.when(pl.program_id(0) == i)
        def _():
            o_ref[...] = r_ref[...]


def place(meta, own, other):
    half, d = own[0].shape
    count = 2 * len(own)
    return call(
        place_kernel,
        "place",
        (count,),
        meta,
        [block for pair in zip(own, other) for block in pair],
        [fixed(half, d)] * count,
        pl.BlockSpec((half, d), lambda i, m: (i ^ m[0], 0)),
        like((count * half, d), own[0].dtype),
    )


def normalise(values):
    average = jnp.mean(values, axis=-1, keepdims=True)
    centred = values - average
    spread = jnp.mean(centred * centred, axis=-1, keepdims=True)
    rstd = lax.rsqrt(spread + EPS)
    return centred * rstd, rstd


def gelu_pair(v):
    e = jnp.exp2(v * v * (-0.5 * LOG2E))
    t = 1.0 / (1.0 + (0.3275911 * 0.7071067811865476) * jnp.abs(v))
    poly = t * (0.5 * 0.254829592 + t * (0.5 * -0.284496736 + t * (0.5 * 1.421413741 + t * (0.5 * -1.453152027 + t * (0.5 * 1.061405429)))))
    tail = poly * e
    phi_cap = jnp.where(v >= 0, 1.0 - tail, tail)
    return v * phi_cap, phi_cap + v * (e * 0.3989422804014327)


def ahead_kernel(
    meta_ref, tok_ref, a0, a1, a2, a3, w0, w1, w2, w3, ua_ref, ub_ref, da_ref, db_ref, vec_ref,
    xhat_ref, rstd_ref, low_ref, act_ref, slope_ref, own_ref, sent_ref,
):
    gain, bias = vec_ref[0:1, :], vec_ref[1:2, :]
    hidden = ua_ref.shape[1]
    for r in range(tok_ref.shape[0] // RB):
        rows = pl.ds(r * RB, RB)
        branch = jnp.zeros((RB, tok_ref.shape[1]), F32)
        for a, w in ((a0, w0), (a1, w1), (a2, w2), (a3, w3)):
            branch = branch + tn(a[:, rows], w[...]).astype(BF).astype(F32)
        xhat, rstd = normalise(tok_ref[rows, :].astype(F32) + branch)
        xhat_ref[rows, :] = xhat
        rstd_ref[rows, :] = jnp.broadcast_to(rstd, (RB, rstd_ref.shape[1]))
        normed = xhat * gain + bias
        low = normed.astype(BF)
        low_ref[rows, :] = low
        sent = jnp.zeros(normed.shape, F32)
        for g, (up, down) in enumerate(((ua_ref, da_ref), (ub_ref, db_ref))):
            acts = []
            for c in range(hidden // HB):
                act, slope = gelu_pair(nn(low, up[:, c * HB : (c + 1) * HB]))
                columns = pl.ds(g * hidden + c * HB, HB)
                acts.append(act.astype(BF))
                act_ref[rows, columns] = acts[-1]
                slope_ref[rows, columns] = slope.astype(BF)
            sent = sent + nn(jnp.concatenate(acts, axis=1), down[...]).astype(BF).astype(F32)
        own_ref[rows, :] = normed + sent
        sent_ref[rows, :] = sent.astype(BF)


def ahead(meta, tokens, att, merge_w, up, down, vectors, u):
    half = att[0].shape[1]
    d, hidden = up[0].shape
    return call(
        ahead_kernel,
        "ahead",
        (1,),
        meta,
        (tokens, *att, *merge_w, *up, *down, vectors),
        [pl.BlockSpec((half, d), lambda i, m: (u * 2 + m[0], 0))]
        + [fixed(192, half)] * 4
        + [fixed(192, d)] * 4
        + [fixed(d, hidden)] * 2
        + [fixed(hidden, d)] * 2
        + [fixed(4, d)],
        [fixed(half, d), fixed(half, 128), fixed(half, d), fixed(half, 2 * hidden), fixed(half, 2 * hidden), fixed(half, d), fixed(half, d)],
        [
            like((half, d), F32),
            like((half, 128), F32),
            like((half, d), BF),
            like((half, 2 * hidden), BF),
            like((half, 2 * hidden), BF),
            like((half, d), F32),
            like((half, d), BF),
        ],
        hold=(-1,),
        out=(0, 1, 2, 3, 4, 5),
    )


def astern_kernel(u, meta_ref, own_ref, far_ref, grad_ref, span_ref, ua_ref, ub_ref, da_ref, db_ref, slope_ref, vec_ref, *refs):
    last = len(refs) > 6
    before = refs[: len(refs) - 10] if last else ()
    out_ref, g_ref, pre_ref, back_ref, sent_ref, small_ref = refs[len(before) : len(before) + 6]
    gain, bias = vec_ref[2:3, :], vec_ref[3:4, :]
    half, d = own_ref.shape
    hidden = ua_ref.shape[1]
    starts = span_ref[u : u + 1, :]
    gain_grad = jnp.zeros(gain.shape, F32)
    bias_grad = jnp.zeros(gain.shape, F32)
    for r in range(half // RB):
        rows = pl.ds(r * RB, RB)
        xhat, rstd = normalise(own_ref[rows, :] + far_ref[rows, :].astype(F32))
        out_ref[rows, :] = (xhat * gain + bias).astype(BF)
        frame = meta_ref[0] * half + r * RB + lax.broadcasted_iota(jnp.int32, (RB, starts.shape[1]), 0)
        inside = (frame >= starts) & (frame < starts + SPAN)
        weight = jnp.max(jnp.where(inside, 1.0, 0.0), axis=1, keepdims=True)
        cot = grad_ref[rows, :].astype(F32) * weight
        gain_grad = gain_grad + jnp.sum(cot * xhat, axis=0, keepdims=True)
        bias_grad = bias_grad + jnp.sum(cot, axis=0, keepdims=True)
        gy = cot * gain
        mean_gy = jnp.mean(gy, axis=-1, keepdims=True)
        mean_gx = jnp.mean(gy * xhat, axis=-1, keepdims=True)
        sum_grad = rstd * (gy - mean_gy - xhat * mean_gx)
        low = sum_grad.astype(BF)
        g_ref[rows, :] = low
        sent = jnp.zeros(sum_grad.shape, F32)
        for g, (up, down) in enumerate(((ua_ref, da_ref), (ub_ref, db_ref))):
            pres = []
            for c in range(hidden // HB):
                columns = pl.ds(g * hidden + c * HB, HB)
                slope = slope_ref[rows, columns].astype(F32)
                pres.append((nt(low, down[c * HB : (c + 1) * HB, :]) * slope).astype(BF))
                pre_ref[rows, columns] = pres[-1]
            sent = sent + nt(jnp.concatenate(pres, axis=1), up[...]).astype(BF).astype(F32)
        back_ref[rows, :] = sum_grad + sent
        sent_ref[rows, :] = sent.astype(BF)
    small_ref[0:1, :] = gain_grad
    small_ref[1:2, :] = bias_grad
    if last:
        x_ref, act_ref = before[:2]
        weight_sums(x_ref[...], g_ref[...], act_ref, pre_ref, before[2:], refs[-4:])


def astern(meta, own, far, grad, spans, up, down, slope, vectors, u, before):
    half, d = own.shape
    hidden = up[0].shape[1]
    rows = fixed(half, d)
    wide = fixed(half, 2 * hidden)
    grads = [] if not before else [(d, hidden)] * 2 + [(hidden, d)] * 2
    extra = [] if not before else [rows, wide] + [fixed(*shape) for shape in grads[: len(before) - 2]]
    return call(
        functools.partial(astern_kernel, u),
        "astern",
        (1,),
        meta,
        (own, far, grad, spans, *up, *down, slope, vectors, *before),
        [rows] * 2
        + [pl.BlockSpec((half, d), lambda i, m: (u * 2 + m[0], 0)), fixed(*spans.shape)]
        + [fixed(d, hidden)] * 2
        + [fixed(hidden, d)] * 2
        + [wide, fixed(4, d)]
        + extra,
        [rows, rows, wide, rows, rows, fixed(2, d)] + [fixed(*shape) for shape in grads],
        [
            like((half, d), BF),
            like((half, d), BF),
            like((half, 2 * hidden), BF),
            like((half, d), F32),
            like((half, d), BF),
            like((2, d), F32),
        ]
        + [like(shape, BF) for shape in grads],
        limit=12 if before else VMEM,
        hold=(0, -3, 8, *range(10, 10 + len(before))),
        out=(3,) if before else (1, 2, 3),
    )


def weight_kernel(meta_ref, x_ref, g_ref, act_ref, pre_ref, *refs):
    before, sums = refs[:-4], refs[-4:]
    weight_sums(x_ref[...], g_ref[...], act_ref, pre_ref, before, sums)


def weight_sums(x, g, act_ref, pre_ref, before, sums):
    hidden = act_ref.shape[1] // 2
    for i in range(2):
        for c in range(hidden // HB):
            columns = pl.ds(i * hidden + c * HB, HB)
            block = pl.ds(c * HB, HB)
            up = tn(x, pre_ref[:, columns])
            down = tn(act_ref[:, columns], g)
            if before:
                up = up + before[i][:, block].astype(F32)
                down = down + before[2 + i][block, :].astype(F32)
            sums[i][:, block] = up.astype(BF)
            sums[2 + i][block, :] = down.astype(BF)


def weight_grads(meta, x, g, act, pre, before):
    rows, d = x.shape
    hidden = act.shape[1] // 2
    shapes = [(d, hidden)] * 2 + [(hidden, d)] * 2
    return call(
        weight_kernel,
        "weight_grads",
        (1,),
        meta,
        (x, g, act, pre, *before),
        [fixed(rows, d)] * 2 + [fixed(rows, 2 * hidden)] * 2 + [fixed(*shape) for shape in shapes[: len(before)]],
        [fixed(*shape) for shape in shapes],
        [like(shape, BF) for shape in shapes],
        hold=(0, 1, 2, 3),
        out=(0, 1, 2, 3),
    )


def inner_kernel(meta_ref, own_ref, far_ref, xhat_ref, rstd_ref, vec_ref, a0, a1, w0, w1, *refs):
    last = len(refs) == 11
    out_ref, g0, g1, m0, m1, small_ref = refs[-6:]
    grad = own_ref[...] + far_ref[...].astype(F32)
    xhat = xhat_ref[...]
    gain_grad = jnp.sum(grad * xhat, axis=0, keepdims=True)
    bias_grad = jnp.sum(grad, axis=0, keepdims=True)
    gy = grad * vec_ref[0:1, :]
    mean_gy = jnp.mean(gy, axis=-1, keepdims=True)
    mean_gx = jnp.mean(gy * xhat, axis=-1, keepdims=True)
    inner = rstd_ref[:, 0:1] * (gy - mean_gy - xhat * mean_gx)
    out_ref[...] = inner
    low = inner.astype(BF)
    g0[...] = nt(w0[...], low).astype(BF)
    g1[...] = nt(w1[...], low).astype(BF)
    small = jnp.concatenate([gain_grad, bias_grad], axis=0)
    small_ref[...] = small
    if last:
        before0, before1, before_small, outer0, outer1 = refs[:5]
        below = jnp.concatenate(
            [small + before_small[...], outer0[...] + outer1[...], jnp.zeros((60, small.shape[1]), F32)], axis=0
        ).astype(BF)
        for m, a, before in ((m0, a0, before0), (m1, a1, before1)):
            m[:192, :] = (nn(a[...], low) + before[...]).astype(BF)
            m[192:, :] = below
    else:
        m0[...] = nn(a0[...], low)
        m1[...] = nn(a1[...], low)


def inner_norm(meta, own, far, xhat, rstd, vectors, att, weights, before):
    rows, d = xhat.shape
    merge = like((256, d), BF) if before else like((192, d), F32)
    return call(
        inner_kernel,
        "inner_norm",
        (1,),
        meta,
        (own, far, xhat, rstd, vectors, *att, *weights, *before),
        [fixed(rows, d)] * 3
        + [fixed(rows, 128), fixed(4, d)]
        + [fixed(192, rows)] * 2
        + [fixed(192, d)] * 2
        + ([fixed(192, d)] * 2 + [fixed(2, d)] * 3 if before else []),
        [fixed(rows, d), fixed(192, rows), fixed(192, rows), fixed(*merge.shape), fixed(*merge.shape), fixed(2, d)],
        [like((rows, d), F32), like((192, rows), BF), like((192, rows), BF), merge, merge, like((2, d), F32)],
        hold=(0, 2, 3),
    )


def local(groups, tokens, lengths, span_starts, wq, wk, wv, wm, wu, wd, ig, ib, og, ob, out_grad):
    rows, d = tokens.shape
    seqs = lengths.shape[0]
    frames = rows // seqs
    half = frames // 2
    core = lax.axis_index("tensor") % 2
    place_dp = lax.axis_index("dp")
    bits = groups.bit_length() - 1

    def swap(value, k):
        return lax.ppermute(value, "tensor", [(i, i ^ k) for i in range(4)])

    def swap_dp(value, k):
        return lax.ppermute(value, "dp", [(i, i ^ k) for i in range(groups)])

    def add(a, b):
        return (a.astype(F32) + b.astype(F32)).astype(BF)

    def total(pieces):
        return sum(piece.astype(F32) for piece in pieces).astype(BF) if len(pieces) > 1 else pieces[0]

    stages = [(0, 1)] + [(b, 2) for b in range(1, bits - 1, 2)] + ([(bits - 1, 1)] if bits % 2 == 0 else [])

    class Scatter:
        def __init__(self, parts, turned):
            shape = [1 << width for _, width in reversed(stages)]
            self.parts = [part.reshape(*shape, -1, d) for part in parts]
            self.turned = turned
            self.steps = list(enumerate(stages))

        def cut(self, j):
            k, (low_bit, width) = self.steps[0]
            flip = (1 << width) - 1 if self.turned else 0
            spot = ((place_dp >> low_bit) & ((1 << width) - 1)) ^ flip ^ j
            return [lax.dynamic_slice_in_dim(part, spot, 1, len(stages) - 1 - k) for part in self.parts]

        def start(self):
            if self.steps:
                low_bit, width = self.steps[0][1]
                self.pending = [swap_dp(total(self.cut(j)), j << low_bit) for j in range(1, 1 << width)]

        def finish(self, *after):
            if self.steps:
                got = self.pending
                if after:
                    got = list(lax.optimization_barrier((*got, *after))[: len(got)])
                self.parts = [total(self.cut(0) + got)]
                self.steps.pop(0)

        def gather(self):
            members = list(range(groups))[:: -1 if self.turned else 1]
            block = self.parts[0].reshape(-1, d)
            return lax.all_gather(block, "dp", axis=0, tiled=True, axis_index_groups=[members])

    scalars = jnp.concatenate([core.reshape(1), lengths])
    token = []

    def meta():
        return lax.optimization_barrier((scalars, *token))[0] if token else scalars

    def done(results, *others):
        token[:] = [results[0], *others]
        return results

    merge_w = (wm, swap(wm, 1), swap(wm, 2), swap(wm, 3))
    up_w = (wu, swap(wu, 1))
    down_w = (wd, swap(wd, 1))
    vectors = jnp.stack([ig, ib, og, ob])
    qkv_w = (wq.T, wk.T, wv.T)

    q, k, v = project(scalars, tokens, qkv_w)
    fwd, att = [], []
    for u in range(seqs):
        fwd.append(done(attend_forward(meta(), q, k, v, u, frames), *merge_w[1:], up_w[1], down_w[1]))
        own, other = fwd[u][:2]
        att.append((own, swap(other, 1), swap(own, 2), swap(other, 3)))
    front, far = [], []
    for u in range(seqs):
        front.append(done(ahead(meta(), tokens, att[u], merge_w, up_w, down_w, vectors, u)))
        far.append(swap(front[u][6], 2))
    back, far_grad, sums = [], [], ()
    for u in range(seqs):
        before = (front[u][2], front[u][3], *sums) if u == seqs - 1 else ()
        back.append(
            done(astern(meta(), front[u][5], far[u], out_grad, span_starts, up_w, down_w, front[u][4], vectors, u, before))
        )
        if u < seqs - 1:
            far_grad.append(swap(back[u][4], 2))
            sums = done(weight_grads(meta(), front[u][2], back[u][1], front[u][3], back[u][2], sums))

    def inner_step(u, before):
        res = done(inner_norm(meta(), back[u][3], far_grad[u], front[u][0], front[u][1], vectors, att[u][:2], merge_w[:2], before))
        return res, (res[1], swap(res[2], 1))

    def attend_step(u, grads):
        return done(attend_backward(meta(), q, k, v, grads, fwd[u][:2], fwd[u][2], u, frames))

    def entry_step(u, grads, before):
        return done(entry_back(meta(), tokens, grads, qkv_w, before, u, frames))


    inner, entry, so_far = [], [], ()
    for u in range(seqs):
        last = u == seqs - 1
        if u == 0:
            up_own, up_other, down_own, down_other = lax.optimization_barrier((*back[-1][6:], far_grad[0]))[:4]
            res, grads = inner_step(0, ())
            inner.append(res)
            far_grad.append(swap(lax.optimization_barrier((back[-1][4], res[0]))[0], 2))
            up_sum = total((up_own, swap(up_other, 1)))
            token.append(up_sum)
            up_sum = lax.psum(up_sum, "dp")
            down = Scatter((down_own, swap(down_other, 1)), False)
            down.start()
        dqkv = attend_step(u, grads)
        if not last:
            before = ()
            if u + 1 == seqs - 1:
                before = (inner[0][3], inner[0][4], inner[0][5], back[0][5], back[1][5])
            res, grads = inner_step(u + 1, before)
            inner.append(res)
            down.finish(res[0])
            down.start()
            token.append(down.parts[0])
        else:
            down.finish(dqkv[0])
            token.append(down.parts[0])
            down.start()
        out = entry_step(u, dqkv, so_far)
        if not last:
            merge_got = swap(lax.optimization_barrier((res[4], out[0]))[0], 1)
            so_far = (out[2], res[3], merge_got)
        entry.append(out)
    qkv = Scatter((out[2],), True)
    qkv.start()

    ready = []
    for u in range(seqs):
        got = swap(entry[u][0], 1)
        crossed = swap(total((entry[u][1], got)), 2)
        rest = entry[u][1].astype(F32) + got.astype(F32) + crossed.astype(F32)
        ready.append((inner[u][0] + rest).astype(BF))
    while qkv.steps or down.steps:
        for scatter in (qkv, down):
            scatter.finish()
            scatter.start()

    up_sum = up_sum.astype(F32)
    pairs = [[i, i + 1] for i in range(0, 4, 2)]
    out_rows = lax.optimization_barrier((*(b[0] for b in back), inner[0][0]))[:seqs]
    layer_output = lax.all_gather(jnp.stack(out_rows), "tensor", axis=1, tiled=True, axis_index_groups=pairs)
    layer_output, up_sum = lax.optimization_barrier((layer_output.reshape(rows, d), up_sum))
    down_sum = down.gather()
    layer_output, down_sum = lax.optimization_barrier((layer_output, down_sum))
    joint = qkv.gather()
    down_sum, joint = lax.optimization_barrier((down_sum, joint))
    input_grad = place(scalars, ready, [swap(r, 1) for r in ready])
    qkv_sum, merge_sum = joint[:576], joint[576:]
    small = merge_sum[192:196].astype(F32)
    query_grad, key_grad, value_grad = (qkv_sum[192 * i : 192 * (i + 1)].astype(F32).T for i in range(3))
    return (
        layer_output,
        input_grad,
        query_grad,
        key_grad,
        value_grad,
        merge_sum[:192].astype(F32),
        up_sum,
        down_sum.astype(F32),
        small[0],
        small[1],
        small[2],
        small[3],
    )


def solution(mesh):
    in_specs = (
        P("dp", None),
        P("dp"),
        P("dp", None),
        P(None, "tensor"),
        P(None, "tensor"),
        P(None, "tensor"),
        P("tensor", None),
        P(None, "tensor"),
        P("tensor", None),
        P(),
        P(),
        P(),
        P(),
        P("dp", None),
    )
    out_specs = (
        P("dp", None),
        P("dp", None),
        P(None, "tensor"),
        P(None, "tensor"),
        P(None, "tensor"),
        P("tensor", None),
        P(None, "tensor"),
        P("tensor", None),
        P(),
        P(),
        P(),
        P(),
    )
    body = functools.partial(local, mesh.shape["dp"])
    return jax.shard_map(body, mesh=mesh, in_specs=in_specs, out_specs=out_specs, check_vma=False)
```

```python
import functools

import jax
import jax.numpy as jnp
from jax import lax
from jax.experimental import pallas as pl
from jax.experimental.pallas import tpu as pltpu
from jax.sharding import PartitionSpec as P

HEAD_DIM = 64
SPAN = 10
EPS = 1e-05
LOG2E = 1.4426950408889634
KB = 256
VMEM = 10
RB = 128
HB = 256
BF = jnp.bfloat16
F32 = jnp.float32
MIB = 1 << 20


def nn(a, b):
    return lax.dot_general(a, b, (((1,), (0,)), ((), ())), preferred_element_type=F32)


def nt(a, b):
    return lax.dot_general(a, b, (((1,), (1,)), ((), ())), preferred_element_type=F32)


def tn(a, b):
    return lax.dot_general(a, b, (((0,), (0,)), ((), ())), preferred_element_type=F32)


def params(limit):
    return pltpu.CompilerParams(vmem_limit_bytes=limit * MIB)


def cost(micros):
    return pl.CostEstimate(flops=int(micros * 1.1e9), bytes_accessed=1024, transcendentals=0)


MICROS = {"project": 3, "attend_forward": 8, "attend_backward": 12, "entry_back": 5, "place": 3, "ahead": 9, "astern": 10, "inner_norm": 3, "weight_grads": 5}


def lane_parts(block):
    left = block[:, :128]
    lane = lax.broadcasted_iota(jnp.int32, left.shape, 1)
    zero = jnp.zeros_like(left)
    return (
        jnp.where(lane < HEAD_DIM, left, zero),
        jnp.where(lane >= HEAD_DIM, left, zero),
        block[:, 128:],
    )


TILE = (0, 0, 1)


def call(kernel, name, grid, meta, args, in_specs, out_specs, out_shape, scratch=(), limit=VMEM, hold=(), out=()):
    args = list(args)
    for i in hold:
        space = pltpu.VMEM if i >= 0 else pltpu.HBM
        spot = i if i >= 0 else -1 - i
        args[spot] = pltpu.with_memory_space_constraint(args[spot], space)
    if isinstance(out_shape, list):
        out_shape = [pltpu.VMEM(o.shape, o.dtype) if i in out else o for i, o in enumerate(out_shape)]
    return pl.pallas_call(
        kernel,
        grid_spec=pltpu.PrefetchScalarGridSpec(
            num_scalar_prefetch=1,
            grid=grid,
            in_specs=in_specs,
            out_specs=out_specs,
            scratch_shapes=scratch,
        ),
        out_shape=out_shape,
        compiler_params=params(limit),
        cost_estimate=cost(MICROS[name]),
        name=name,
    )(meta, *args)


def fixed(*shape):
    return pl.BlockSpec(shape, lambda *_: (0,) * len(shape))


def like(shape, dtype):
    return jax.ShapeDtypeStruct(shape, dtype)


def project_kernel(meta_ref, x_ref, wq_ref, wk_ref, wv_ref, q_ref, k_ref, v_ref):
    x = x_ref[...]
    for w_ref, o_ref in ((wq_ref, q_ref), (wk_ref, k_ref), (wv_ref, v_ref)):
        o_ref[:, :192] = nt(x, w_ref[...]).astype(BF)
        o_ref[:, 192:] = jnp.zeros((x.shape[0], HEAD_DIM), BF)


def project(meta, tokens, weights, u, frames):
    rows, d = frames, tokens.shape[1]
    block = 256
    return call(
        project_kernel,
        "project",
        (rows // block,),
        meta,
        (tokens, *weights),
        [pl.BlockSpec((block, d), lambda i, m: (u * (rows // block) + i, 0))] + [fixed(192, d)] * 3,
        [pl.BlockSpec((block, 256), lambda i, m: (i, 0))] * 3,
        [like((rows, 256), BF)] * 3,
        hold=(-1, -2, -3, -4),
        out=(0, 1, 2),
    )


def forward_kernel(u, meta_ref, q_ref, k_ref, v_ref, own_ref, other_ref, lse_ref, s_ref):
    length = meta_ref[1 + u]
    step = pl.program_id(0)
    blocks = lax.div(length + KB - 1, KB)
    parts = lane_parts(q_ref[...] * jnp.asarray(0.125, BF))
    width = q_ref.shape[0]

    def first(kb, highest):
        start = pl.multiple_of(kb * KB, KB)
        rows = pl.ds(start, KB)
        live = start + lax.broadcasted_iota(jnp.int32, (KB, width), 0) < length
        out = []
        for h in range(3):
            tile = pl.ds(128 * TILE[h], 128)
            s = nt(k_ref[rows, tile], parts[h])
            s = jnp.where(live, s, -1e30)
            s_ref[h, rows, :] = s
            out.append(jnp.maximum(highest[h], jnp.max(s, axis=0, keepdims=True)))
        return tuple(out)

    floor = jnp.full((1, width), -1e30, F32)
    highest = lax.fori_loop(0, blocks, first, (floor,) * 3)

    def second(kb, carry):
        rows = pl.ds(pl.multiple_of(kb * KB, KB), KB)
        out = []
        for h in range(3):
            total, result = carry[h]
            p = jnp.exp2((s_ref[h, rows, :] - highest[h]) * LOG2E)
            total = total + jnp.sum(p, axis=0, keepdims=True)
            v = v_ref[rows, pl.ds(128 * TILE[h], 128)]
            result = result + tn(v, p.astype(BF))
            out.append((total, result))
        return tuple(out)

    init = ((jnp.zeros((1, width), F32), jnp.zeros((128, width), F32)),) * 3
    done = lax.fori_loop(0, blocks, second, init)
    outs = []
    for h in range(3):
        total, result = done[h]
        lo = HEAD_DIM * (h % 2)
        o = result[lo : lo + HEAD_DIM] / total
        lse_ref[0, pl.ds(h, 1), :] = highest[h] * LOG2E + jnp.log2(total)
        outs.append(o.astype(BF))
    whole = jnp.concatenate(outs, axis=0)
    for j, o_ref in enumerate((own_ref, other_ref)):

        @pl.when(step == j)
        def _():
            o_ref[...] = whole


def attend_forward(meta, q, k, v, u, frames):
    half = frames // 2
    return call(
        functools.partial(forward_kernel, u),
        "attend_forward",
        (2,),
        meta,
        (q, k, v),
        [
            pl.BlockSpec((half, 256), lambda i, m: (i ^ m[0], 0)),
            fixed(frames, 256),
            fixed(frames, 256),
        ],
        [
            fixed(192, half),
            fixed(192, half),
            pl.BlockSpec((1, 8, half), lambda i, m: (i, 0, 0)),
        ],
        [
            like((192, half), BF),
            like((192, half), BF),
            like((2, 8, half), F32),
        ],
        [pltpu.VMEM((3, frames, half), F32)],
        hold=(0, 1, 2),
        out=(2,),
    )


def backward_kernel(
    u, meta_ref, q_ref, k_ref, v_ref, d0_ref, d1_ref, o0_ref, o1_ref, lse_ref,
    dq_ref, dk_ref, dv_ref, kt_ref, dk_acc, dv_acc, do_ref, o_ref,
):
    length = meta_ref[1 + u]
    blocks = lax.div(length + KB - 1, KB)
    step = pl.program_id(0)

    @pl.when(step == 0)
    def _():
        dk_acc[...] = jnp.zeros_like(dk_acc)
        dv_acc[...] = jnp.zeros_like(dv_acc)
        kt_ref[...] = jnp.transpose(k_ref[...])
        do_ref[...] = d0_ref[...]
        o_ref[...] = o0_ref[...]

    @pl.when(step == 1)
    def _():
        do_ref[...] = d1_ref[...]
        o_ref[...] = o1_ref[...]

    parts = lane_parts(q_ref[...] * jnp.asarray(0.125, BF))
    width = q_ref.shape[0]
    empty = jnp.zeros((HEAD_DIM, width), BF)
    head = [do_ref[pl.ds(h * HEAD_DIM, HEAD_DIM), :] for h in range(3)]
    grads = (
        jnp.concatenate([head[0], empty], axis=0),
        jnp.concatenate([empty, head[1]], axis=0),
        jnp.concatenate([head[2], empty], axis=0),
    )
    delta = [
        jnp.sum(
            head[h].astype(F32) * o_ref[pl.ds(h * HEAD_DIM, HEAD_DIM), :].astype(F32), axis=0, keepdims=True
        )
        for h in range(3)
    ]
    lse = [lse_ref[0, pl.ds(h, 1), :] for h in range(3)]

    def body(kb, carry):
        start = pl.multiple_of(kb * KB, KB)
        rows = pl.ds(start, KB)
        live = start + lax.broadcasted_iota(jnp.int32, (KB, width), 0) < length
        out = []
        for h in range(3):
            tile = pl.ds(128 * TILE[h], 128)
            s = nt(k_ref[rows, tile], parts[h])
            s = jnp.where(live, s, -1e30)
            p = jnp.exp2(s * LOG2E - lse[h])
            dp = nn(v_ref[rows, tile], grads[h])
            ds = (p * (dp - delta[h])).astype(BF)
            dv_acc[rows, tile] += nt(p.astype(BF), grads[h])
            dk_acc[rows, tile] += nn(ds, parts[h])
            kt = kt_ref[pl.ds(h * HEAD_DIM, HEAD_DIM), rows]
            out.append(carry[h] + nn(kt, ds))
        return tuple(out)

    zero = jnp.zeros((HEAD_DIM, width), F32)
    done = lax.fori_loop(0, blocks, body, (zero,) * 3)
    full = jnp.concatenate(done + (zero,), axis=0) * 0.125
    dq_ref[...] = jnp.transpose(full).astype(BF)

    @pl.when(step == 1)
    def _():
        dk_ref[...] = dk_acc[...].astype(BF)
        dv_ref[...] = dv_acc[...].astype(BF)


def attend_backward(meta, q, k, v, grads, outs, lse, u, frames):
    half = frames // 2
    return call(
        functools.partial(backward_kernel, u),
        "attend_backward",
        (2,),
        meta,
        (q, k, v, *grads, *outs, lse),
        [
            pl.BlockSpec((half, 256), lambda i, m: (i ^ m[0], 0)),
            fixed(frames, 256),
            fixed(frames, 256),
            fixed(192, half),
            fixed(192, half),
            fixed(192, half),
            fixed(192, half),
            pl.BlockSpec((1, 8, half), lambda i, m: (i, 0, 0)),
        ],
        [
            pl.BlockSpec((half, 256), lambda i, m: (i ^ m[0], 0)),
            fixed(frames, 256),
            fixed(frames, 256),
        ],
        [like((frames, 256), BF)] * 3,
        [
            pltpu.VMEM((256, frames), BF),
            pltpu.VMEM((frames, 256), F32),
            pltpu.VMEM((frames, 256), F32),
            pltpu.VMEM((192, half), BF),
            pltpu.VMEM((192, half), BF),
        ],
        hold=(-1, -2, -3, 7),
        out=(0, 1, 2),
    )


def entry_kernel(meta_ref, x_ref, dq_ref, dk_ref, dv_ref, wq_ref, wk_ref, wv_ref, *refs):
    last = len(refs) == 7
    before_ref = refs[0] if last else None
    send_ref, keep_ref, sum_ref, acc = refs[-4:]
    step = pl.program_id(0)
    x = x_ref[...]
    total = jnp.zeros(x.shape, F32)
    for i, (g_ref, w_ref) in enumerate(((dq_ref, wq_ref), (dk_ref, wk_ref), (dv_ref, wv_ref))):
        rows = pl.ds(192 * i, 192)
        g = g_ref[:, :192]
        total = total + nn(g, w_ref[...])
        product = tn(g, x)

        @pl.when(step == 0)
        def _():
            acc[rows, :] = product if before_ref is None else product + before_ref[rows, :]

        @pl.when(step == 1)
        def _():
            sum_ref[rows, :] = (product + acc[rows, :]).astype(sum_ref.dtype)

    low = total.astype(BF)

    @pl.when(step == 0)
    def _():
        send_ref[...] = low
        if last:
            merged = refs[1][...].astype(F32) + refs[2][...].astype(F32)
            sum_ref[576:, :] = merged.astype(sum_ref.dtype)

    @pl.when(step == 1)
    def _():
        keep_ref[...] = low


def entry_back(meta, tokens, grads, weights, before, u, frames):
    half = frames // 2
    d = tokens.shape[1]
    rows, dtype = (832, BF) if before else (576, F32)
    return call(
        entry_kernel,
        "entry_back",
        (2,),
        meta,
        (tokens, *grads, *weights, *before),
        [pl.BlockSpec((half, d), lambda i, m: (u * 2 + (1 - i ^ m[0]), 0))]
        + [pl.BlockSpec((half, 256), lambda i, m: (1 - i ^ m[0], 0))] * 3
        + [fixed(192, d)] * 3
        + [fixed(*value.shape) for value in before],
        [fixed(half, d), fixed(half, d), fixed(rows, d)],
        [like((half, d), BF), like((half, d), BF), like((rows, d), dtype)],
        [pltpu.VMEM((576, d), F32)],
        hold=(-1, 1, 2, 3, -5, -6, -7),
    )


def place_kernel(meta_ref, *refs):
    o_ref = refs[-1]
    for i, r_ref in enumerate(refs[:-1]):

        @pl.when(pl.program_id(0) == i)
        def _():
            o_ref[...] = r_ref[...]


def place(meta, own, other):
    half, d = own[0].shape
    count = 2 * len(own)
    return call(
        place_kernel,
        "place",
        (count,),
        meta,
        [block for pair in zip(own, other) for block in pair],
        [fixed(half, d)] * count,
        pl.BlockSpec((half, d), lambda i, m: (i ^ m[0], 0)),
        like((count * half, d), own[0].dtype),
    )


def normalise(values):
    average = jnp.mean(values, axis=-1, keepdims=True)
    centred = values - average
    spread = jnp.mean(centred * centred, axis=-1, keepdims=True)
    rstd = lax.rsqrt(spread + EPS)
    return centred * rstd, rstd


def gelu_pair(v):
    e = jnp.exp2(v * v * (-0.5 * LOG2E))
    t = 1.0 / (1.0 + (0.3275911 * 0.7071067811865476) * jnp.abs(v))
    poly = t * (0.5 * 0.254829592 + t * (0.5 * -0.284496736 + t * (0.5 * 1.421413741 + t * (0.5 * -1.453152027 + t * (0.5 * 1.061405429)))))
    tail = poly * e
    phi_cap = jnp.where(v >= 0, 1.0 - tail, tail)
    return v * phi_cap, phi_cap + v * (e * 0.3989422804014327)


def ahead_kernel(
    meta_ref, tok_ref, a0, a1, a2, a3, w0, w1, w2, w3, ua_ref, ub_ref, da_ref, db_ref, vec_ref,
    xhat_ref, rstd_ref, low_ref, act_ref, slope_ref, own_ref, sent_ref,
):
    gain, bias = vec_ref[0:1, :], vec_ref[1:2, :]
    hidden = ua_ref.shape[1]
    for r in range(tok_ref.shape[0] // RB):
        rows = pl.ds(r * RB, RB)
        branch = jnp.zeros((RB, tok_ref.shape[1]), F32)
        for a, w in ((a0, w0), (a1, w1), (a2, w2), (a3, w3)):
            branch = branch + tn(a[:, rows], w[...]).astype(BF).astype(F32)
        xhat, rstd = normalise(tok_ref[rows, :].astype(F32) + branch)
        xhat_ref[rows, :] = xhat
        rstd_ref[rows, :] = jnp.broadcast_to(rstd, (RB, rstd_ref.shape[1]))
        normed = xhat * gain + bias
        low = normed.astype(BF)
        low_ref[rows, :] = low
        sent = jnp.zeros(normed.shape, F32)
        for g, (up, down) in enumerate(((ua_ref, da_ref), (ub_ref, db_ref))):
            acts = []
            for c in range(hidden // HB):
                act, slope = gelu_pair(nn(low, up[:, c * HB : (c + 1) * HB]))
                columns = pl.ds(g * hidden + c * HB, HB)
                acts.append(act.astype(BF))
                act_ref[rows, columns] = acts[-1]
                slope_ref[rows, columns] = slope.astype(BF)
            sent = sent + nn(jnp.concatenate(acts, axis=1), down[...]).astype(BF).astype(F32)
        own_ref[rows, :] = normed + sent
        sent_ref[rows, :] = sent.astype(BF)


def ahead(meta, tokens, att, merge_w, up, down, vectors, u):
    half = att[0].shape[1]
    d, hidden = up[0].shape
    return call(
        ahead_kernel,
        "ahead",
        (1,),
        meta,
        (tokens, *att, *merge_w, *up, *down, vectors),
        [pl.BlockSpec((half, d), lambda i, m: (u * 2 + m[0], 0))]
        + [fixed(192, half)] * 4
        + [fixed(192, d)] * 4
        + [fixed(d, hidden)] * 2
        + [fixed(hidden, d)] * 2
        + [fixed(4, d)],
        [fixed(half, d), fixed(half, 128), fixed(half, d), fixed(half, 2 * hidden), fixed(half, 2 * hidden), fixed(half, d), fixed(half, d)],
        [
            like((half, d), F32),
            like((half, 128), F32),
            like((half, d), BF),
            like((half, 2 * hidden), BF),
            like((half, 2 * hidden), BF),
            like((half, d), F32),
            like((half, d), BF),
        ],
        hold=(-1,),
        out=(0, 1, 2, 3, 4, 5),
    )


def astern_kernel(u, meta_ref, own_ref, far_ref, grad_ref, span_ref, ua_ref, ub_ref, da_ref, db_ref, slope_ref, vec_ref, *refs):
    last = len(refs) > 6
    before = refs[: len(refs) - 10] if last else ()
    out_ref, g_ref, pre_ref, back_ref, sent_ref, small_ref = refs[len(before) : len(before) + 6]
    gain, bias = vec_ref[2:3, :], vec_ref[3:4, :]
    half, d = own_ref.shape
    hidden = ua_ref.shape[1]
    starts = span_ref[u : u + 1, :]
    gain_grad = jnp.zeros(gain.shape, F32)
    bias_grad = jnp.zeros(gain.shape, F32)
    for r in range(half // RB):
        rows = pl.ds(r * RB, RB)
        xhat, rstd = normalise(own_ref[rows, :] + far_ref[rows, :].astype(F32))
        out_ref[rows, :] = (xhat * gain + bias).astype(BF)
        frame = meta_ref[0] * half + r * RB + lax.broadcasted_iota(jnp.int32, (RB, starts.shape[1]), 0)
        inside = (frame >= starts) & (frame < starts + SPAN)
        weight = jnp.max(jnp.where(inside, 1.0, 0.0), axis=1, keepdims=True)
        cot = grad_ref[rows, :].astype(F32) * weight
        gain_grad = gain_grad + jnp.sum(cot * xhat, axis=0, keepdims=True)
        bias_grad = bias_grad + jnp.sum(cot, axis=0, keepdims=True)
        gy = cot * gain
        mean_gy = jnp.mean(gy, axis=-1, keepdims=True)
        mean_gx = jnp.mean(gy * xhat, axis=-1, keepdims=True)
        sum_grad = rstd * (gy - mean_gy - xhat * mean_gx)
        low = sum_grad.astype(BF)
        g_ref[rows, :] = low
        sent = jnp.zeros(sum_grad.shape, F32)
        for g, (up, down) in enumerate(((ua_ref, da_ref), (ub_ref, db_ref))):
            pres = []
            for c in range(hidden // HB):
                columns = pl.ds(g * hidden + c * HB, HB)
                slope = slope_ref[rows, columns].astype(F32)
                pres.append((nt(low, down[c * HB : (c + 1) * HB, :]) * slope).astype(BF))
                pre_ref[rows, columns] = pres[-1]
            sent = sent + nt(jnp.concatenate(pres, axis=1), up[...]).astype(BF).astype(F32)
        back_ref[rows, :] = sum_grad + sent
        sent_ref[rows, :] = sent.astype(BF)
    small_ref[0:1, :] = gain_grad
    small_ref[1:2, :] = bias_grad
    if last:
        x_ref, act_ref = before[:2]
        weight_sums(x_ref[...], g_ref[...], act_ref, pre_ref, before[2:], refs[-4:])


def astern(meta, own, far, grad, spans, up, down, slope, vectors, u, before):
    half, d = own.shape
    hidden = up[0].shape[1]
    rows = fixed(half, d)
    wide = fixed(half, 2 * hidden)
    grads = [] if not before else [(d, hidden)] * 2 + [(hidden, d)] * 2
    extra = [] if not before else [rows, wide] + [fixed(*shape) for shape in grads[: len(before) - 2]]
    return call(
        functools.partial(astern_kernel, u),
        "astern",
        (1,),
        meta,
        (own, far, grad, spans, *up, *down, slope, vectors, *before),
        [rows] * 2
        + [pl.BlockSpec((half, d), lambda i, m: (u * 2 + m[0], 0)), fixed(*spans.shape)]
        + [fixed(d, hidden)] * 2
        + [fixed(hidden, d)] * 2
        + [wide, fixed(4, d)]
        + extra,
        [rows, rows, wide, rows, rows, fixed(2, d)] + [fixed(*shape) for shape in grads],
        [
            like((half, d), BF),
            like((half, d), BF),
            like((half, 2 * hidden), BF),
            like((half, d), F32),
            like((half, d), BF),
            like((2, d), F32),
        ]
        + [like(shape, BF) for shape in grads],
        limit=12 if before else VMEM,
        hold=(0, -3, 8, *range(10, 10 + len(before))),
        out=(3,) if before else (1, 2, 3),
    )


def weight_kernel(meta_ref, x_ref, g_ref, act_ref, pre_ref, *refs):
    before, sums = refs[:-4], refs[-4:]
    weight_sums(x_ref[...], g_ref[...], act_ref, pre_ref, before, sums)


def weight_sums(x, g, act_ref, pre_ref, before, sums):
    hidden = act_ref.shape[1] // 2
    for i in range(2):
        for c in range(hidden // HB):
            columns = pl.ds(i * hidden + c * HB, HB)
            block = pl.ds(c * HB, HB)
            up = tn(x, pre_ref[:, columns])
            down = tn(act_ref[:, columns], g)
            if before:
                up = up + before[i][:, block].astype(F32)
                down = down + before[2 + i][block, :].astype(F32)
            sums[i][:, block] = up.astype(BF)
            sums[2 + i][block, :] = down.astype(BF)


def weight_grads(meta, x, g, act, pre, before):
    rows, d = x.shape
    hidden = act.shape[1] // 2
    shapes = [(d, hidden)] * 2 + [(hidden, d)] * 2
    return call(
        weight_kernel,
        "weight_grads",
        (1,),
        meta,
        (x, g, act, pre, *before),
        [fixed(rows, d)] * 2 + [fixed(rows, 2 * hidden)] * 2 + [fixed(*shape) for shape in shapes[: len(before)]],
        [fixed(*shape) for shape in shapes],
        [like(shape, BF) for shape in shapes],
        hold=(0, 1, 2, 3),
        out=(0, 1, 2, 3),
    )


def inner_kernel(meta_ref, own_ref, far_ref, xhat_ref, rstd_ref, vec_ref, a0, a1, w0, w1, *refs):
    last, cuts = len(refs) == 11, len(refs) == 14
    if cuts:
        for i in range(2):
            here, there, send, keep = refs[2 * i], refs[2 * i + 1], refs[-4 + 2 * i], refs[-3 + 2 * i]
            half = send.shape[0]
            bit = meta_ref[meta_ref.shape[0] - 2 + i]
            for part, j in ((send, 1 - bit), (keep, bit)):
                rows = pl.ds(pl.multiple_of(j * half, 128), half)
                part[...] = (here[rows, :].astype(F32) + there[rows, :].astype(F32)).astype(BF)
        refs = refs[4:-4]
    out_ref, g0, g1, m0, m1, small_ref = refs[-6:]
    grad = own_ref[...] + far_ref[...].astype(F32)
    xhat = xhat_ref[...]
    gain_grad = jnp.sum(grad * xhat, axis=0, keepdims=True)
    bias_grad = jnp.sum(grad, axis=0, keepdims=True)
    gy = grad * vec_ref[0:1, :]
    mean_gy = jnp.mean(gy, axis=-1, keepdims=True)
    mean_gx = jnp.mean(gy * xhat, axis=-1, keepdims=True)
    inner = rstd_ref[:, 0:1] * (gy - mean_gy - xhat * mean_gx)
    out_ref[...] = inner
    low = inner.astype(BF)
    g0[...] = nt(w0[...], low).astype(BF)
    g1[...] = nt(w1[...], low).astype(BF)
    small = jnp.concatenate([gain_grad, bias_grad], axis=0)
    small_ref[...] = small
    if last:
        before0, before1, before_small, outer0, outer1 = refs[:5]
        below = jnp.concatenate(
            [small + before_small[...], outer0[...] + outer1[...], jnp.zeros((60, small.shape[1]), F32)], axis=0
        ).astype(BF)
        for m, a, before in ((m0, a0, before0), (m1, a1, before1)):
            m[:192, :] = (nn(a[...], low) + before[...]).astype(BF)
            m[192:, :] = below
    else:
        m0[...] = nn(a0[...], low)
        m1[...] = nn(a1[...], low)


def inner_norm(meta, own, far, xhat, rstd, vectors, att, weights, before=(), sums=()):
    rows, d = xhat.shape
    merge = like((256, d), BF) if before else like((192, d), F32)
    half = like((sums[0].shape[0] // 2, d), BF) if sums else None
    return call(
        inner_kernel,
        "inner_norm",
        (1,),
        meta,
        (own, far, xhat, rstd, vectors, *att, *weights, *before, *sums),
        [fixed(rows, d)] * 3
        + [fixed(rows, 128), fixed(4, d)]
        + [fixed(192, rows)] * 2
        + [fixed(192, d)] * 2
        + ([fixed(192, d)] * 2 + [fixed(2, d)] * 3 if before else [])
        + [fixed(*value.shape) for value in sums],
        [fixed(rows, d), fixed(192, rows), fixed(192, rows), fixed(*merge.shape), fixed(*merge.shape), fixed(2, d)]
        + ([fixed(*half.shape)] * 4 if sums else []),
        [like((rows, d), F32), like((192, rows), BF), like((192, rows), BF), merge, merge, like((2, d), F32)]
        + ([half] * 4 if sums else []),
        hold=(0, 2, 3),
        limit=20 if sums else VMEM,
    )


def local(groups, tokens, lengths, span_starts, wq, wk, wv, wm, wu, wd, ig, ib, og, ob, out_grad):
    rows, d = tokens.shape
    seqs = lengths.shape[0]
    frames = rows // seqs
    half = frames // 2
    core = lax.axis_index("tensor") % 2
    place_dp = lax.axis_index("dp")
    bits = groups.bit_length() - 1

    def swap(value, k):
        return lax.ppermute(value, "tensor", [(i, i ^ k) for i in range(4)])

    def swap_dp(value, k):
        return lax.ppermute(value, "dp", [(i, i ^ k) for i in range(groups)])

    def add(a, b):
        return (a.astype(F32) + b.astype(F32)).astype(BF)

    def total(pieces):
        return sum(piece.astype(F32) for piece in pieces).astype(BF) if len(pieces) > 1 else pieces[0]

    pairs = [(b, 1) for b in range(bits)]
    stages = [(0, 1)] + [(b, 2) for b in range(1, bits - 1, 2)] + ([(bits - 1, 1)] if bits % 2 == 0 else [])
    orders = (pairs, pairs[1:2] + pairs[:1] + pairs[2:])

    def spot_of(stage):
        return (place_dp >> stage[0]) & ((1 << stage[1]) - 1)

    class Chain:
        def __init__(self, parts, order, back=None, halves=None):
            self.parts = parts
            self.halves = halves
            self.order = order
            self.steps = [(True, stage) for stage in order] + [(False, stage) for stage in back or reversed(order)]

        def cut(self, stage, j):
            count = 1 << stage[1]
            size = self.parts[0].shape[0] // count
            return [lax.dynamic_slice_in_dim(p, (spot_of(stage) ^ j) * size, size, 0) for p in self.parts]

        def start(self):
            if self.steps:
                scatter, stage = self.steps[0]
                others = range(1, 1 << stage[1])
                if self.halves:
                    sent = [self.halves[0]]
                else:
                    sent = [total(self.cut(stage, j)) if scatter else self.parts[0] for j in others]
                self.pending = [swap_dp(piece, j << stage[0]) for j, piece in zip(others, sent)]

        def finish(self, *after):
            if not self.steps:
                return
            scatter, stage = self.steps.pop(0)
            got = self.pending
            if after:
                got = list(lax.optimization_barrier((*got, *after))[: len(got)])
            if scatter:
                state = total(([self.halves[1]] if self.halves else self.cut(stage, 0)) + got)
                self.halves = None
                if not self.steps[0][0]:
                    state = state.reshape((1,) * len(self.order) + state.shape)
            else:
                axis = self.order.index(stage)
                spot = spot_of(stage)
                mine = self.parts[0]
                if len(got) == 1:
                    laid = [jnp.where(spot, got[0], mine), jnp.where(spot, mine, got[0])]
                    state = jnp.concatenate(laid, axis=axis)
                else:
                    state = jnp.zeros(mine.shape[:axis] + (1 + len(got),) + mine.shape[axis + 1 :], BF)
                    for j, piece in enumerate([mine] + got):
                        state = lax.dynamic_update_slice_in_dim(state, piece, spot ^ j, axis)
                if not self.steps:
                    state = state.reshape(-1, d)
            self.parts = [state]

    def finish(group, *after):
        for chain in group:
            chain.finish(*after)

    def start(group):
        for chain in group:
            chain.start()

    def together(group):
        for chain, value in zip(group, lax.optimization_barrier(tuple(chain.parts[0] for chain in group))):
            chain.parts = [value]

    scalars = jnp.concatenate([core.reshape(1), lengths, *(spot_of(order[0]).reshape(1) for order in orders)])
    token = []

    def meta():
        return lax.optimization_barrier((scalars, *token))[0] if token else scalars

    def done(results, *others):
        token[:] = [results[0], *others]
        return results

    merge_w = (wm, swap(wm, 1), swap(wm, 2), swap(wm, 3))
    up_w = (wu, swap(wu, 1))
    down_w = (wd, swap(wd, 1))
    vectors = jnp.stack([ig, ib, og, ob])
    qkv_w = (wq.T, wk.T, wv.T)

    fwd, att, front, far = [], [], [], []
    qkv_of = [done(project(scalars, tokens, qkv_w, 0, frames))]
    for u in range(seqs):
        fwd.append(done(attend_forward(meta(), *qkv_of[u], u, frames), *(merge_w[1:] if u == 0 else ())))
        own, other = fwd[u][:2]
        att.append((own, swap(other, 1), swap(own, 2), swap(other, 3)))
        if u + 1 < seqs:
            qkv_of.append(done(project(meta(), tokens, qkv_w, u + 1, frames), up_w[1], down_w[1]))
    for u in range(seqs):
        front.append(done(ahead(meta(), tokens, att[u], merge_w, up_w, down_w, vectors, u)))
        far.append(swap(front[u][6], 2))
    back, far_grad, sums = [], [], ()
    for u in range(seqs):
        before = (front[u][2], front[u][3], *sums) if u == seqs - 1 else ()
        back.append(
            done(astern(meta(), front[u][5], far[u], out_grad, span_starts, up_w, down_w, front[u][4], vectors, u, before))
        )
        if u < seqs - 1:
            far_grad.append(swap(back[u][4], 2))
            sums = done(weight_grads(meta(), front[u][2], back[u][1], front[u][3], back[u][2], sums))

    def inner_step(u, **more):
        res = done(inner_norm(meta(), back[u][3], far_grad[u], front[u][0], front[u][1], vectors, att[u][:2], merge_w[:2], **more))
        return res, (res[1], swap(res[2], 1))

    def attend_step(u, grads):
        return done(attend_backward(meta(), *qkv_of[u], grads, fwd[u][:2], fwd[u][2], u, frames))

    def entry_step(u, grads, before):
        return done(entry_back(meta(), tokens, grads, qkv_w, before, u, frames))


    inner, entry, so_far = [], [], ()
    for u in range(seqs):
        last = u == seqs - 1
        if u == 0:
            up_own, up_other, down_own, down_other = lax.optimization_barrier((*back[-1][6:], far_grad[0]))[:4]
            sums = (down_own, swap(down_other, 1), up_own, swap(up_other, 1))
            res, grads = inner_step(0, sums=sums)
            inner.append(res)
            far_grad.append(swap(lax.optimization_barrier((back[-1][4], res[0]))[0], 2))
            ffn = [Chain(None, order, None, res[6 + 2 * i : 8 + 2 * i]) for i, order in enumerate(orders)]
            start(ffn)
        dqkv = attend_step(u, grads)
        finish(ffn, dqkv[0])
        token.extend(chain.parts[0] for chain in ffn)
        start(ffn)
        if not last:
            before = ()
            if u + 1 == seqs - 1:
                before = (inner[0][3], inner[0][4], inner[0][5], back[0][5], back[1][5])
            res, grads = inner_step(u + 1, before=before)
            inner.append(res)
        out = entry_step(u, dqkv, so_far)
        entry.append(out)
        if not last:
            merge_got = swap(lax.optimization_barrier((res[4], out[0]))[0], 1)
            so_far = (out[2], res[3], merge_got)
            finish(ffn, out[0])
            token.extend(chain.parts[0] for chain in ffn)
            start(ffn)
    qkv = Chain([out[2]], stages)
    qkv.start()

    ready = []
    for u in range(seqs):
        got = swap(entry[u][0], 1)
        crossed = swap(total((entry[u][1], got)), 2)
        rest = entry[u][1].astype(F32) + got.astype(F32) + crossed.astype(F32)
        ready.append((inner[u][0] + rest).astype(BF))

    first, second = ffn
    finish(ffn, got)
    for group, sending in (((qkv,), (qkv, first, second)), ((qkv, first, second), (qkv, first)), ((qkv, first), (qkv, second))):
        finish(group)
        together([qkv, first, second])
        start(sending)
    finish([qkv, second])
    while qkv.steps or first.steps or second.steps:
        start([qkv, first, second])
        finish([qkv, first, second])
        together([qkv, first, second])
    down_sum, up_sum, joint = (chain.parts[0] for chain in ffn + [qkv])
    chips = [[i, i + 1] for i in range(0, 4, 2)]
    out_rows = lax.optimization_barrier((*(b[0] for b in back), inner[0][0]))[:seqs]
    layer_output = lax.all_gather(jnp.stack(out_rows), "tensor", axis=1, tiled=True, axis_index_groups=chips)
    layer_output = layer_output.reshape(rows, d)
    input_grad = place(scalars, ready, [swap(r, 1) for r in ready])
    qkv_sum, merge_sum = joint[:576], joint[576:]
    small = merge_sum[192:196].astype(F32)
    query_grad, key_grad, value_grad = (qkv_sum[192 * i : 192 * (i + 1)].astype(F32).T for i in range(3))
    return (
        layer_output,
        input_grad,
        query_grad,
        key_grad,
        value_grad,
        merge_sum[:192].astype(F32),
        up_sum.astype(F32),
        down_sum.astype(F32),
        small[0],
        small[1],
        small[2],
        small[3],
    )


def solution(mesh):
    in_specs = (
        P("dp", None),
        P("dp"),
        P("dp", None),
        P(None, "tensor"),
        P(None, "tensor"),
        P(None, "tensor"),
        P("tensor", None),
        P(None, "tensor"),
        P("tensor", None),
        P(),
        P(),
        P(),
        P(),
        P("dp", None),
    )
    out_specs = (
        P("dp", None),
        P("dp", None),
        P(None, "tensor"),
        P(None, "tensor"),
        P(None, "tensor"),
        P("tensor", None),
        P(None, "tensor"),
        P("tensor", None),
        P(),
        P(),
        P(),
        P(),
    )
    body = functools.partial(local, mesh.shape["dp"])
    return jax.shard_map(body, mesh=mesh, in_specs=in_specs, out_specs=out_specs, check_vma=False)
```

```python
import functools

import jax
import jax.numpy as jnp
from jax import lax
from jax.experimental import pallas as pl
from jax.experimental.pallas import tpu as pltpu
from jax.sharding import PartitionSpec as P

HEAD_DIM = 64
SPAN = 10
EPS = 1e-05
LOG2E = 1.4426950408889634
KB = 256
VMEM = 12
RB = 128
HB = 256
BF = jnp.bfloat16
F32 = jnp.float32
MIB = 1 << 20


def nn(a, b):
    return lax.dot_general(a, b, (((1,), (0,)), ((), ())), preferred_element_type=F32)


def nt(a, b):
    return lax.dot_general(a, b, (((1,), (1,)), ((), ())), preferred_element_type=F32)


def tn(a, b):
    return lax.dot_general(a, b, (((0,), (0,)), ((), ())), preferred_element_type=F32)


def params(limit):
    return pltpu.CompilerParams(vmem_limit_bytes=limit * MIB)


def cost(micros):
    return pl.CostEstimate(flops=int(micros * 1.1e9), bytes_accessed=1024, transcendentals=0)


MICROS = {"project": 3, "attend_forward": 8, "attend_backward": 12, "entry_back": 5, "place": 3, "ahead": 9, "astern": 10, "inner_norm": 3, "weight_grads": 4, "fold": 2}


def lane_parts(block):
    left = block[:, :128]
    lane = lax.broadcasted_iota(jnp.int32, left.shape, 1)
    zero = jnp.zeros_like(left)
    return (
        jnp.where(lane < HEAD_DIM, left, zero),
        jnp.where(lane >= HEAD_DIM, left, zero),
        block[:, 128:],
    )


TILE = (0, 0, 1)


def call(kernel, name, grid, meta, args, in_specs, out_specs, out_shape, scratch=(), limit=VMEM, hold=(), far=(), out=(), out_far=()):
    def place_input(i, value):
        space = pltpu.VMEM if i in hold else pltpu.HBM if i in far else None
        return value if space is None else pltpu.with_memory_space_constraint(value, space)

    def place_output(i, value):
        space = pltpu.VMEM if i in out else pltpu.HBM if i in out_far else None
        return value if space is None else space(value.shape, value.dtype)

    single = not isinstance(out_shape, list)
    return pl.pallas_call(
        kernel,
        grid_spec=pltpu.PrefetchScalarGridSpec(
            num_scalar_prefetch=1,
            grid=grid,
            in_specs=in_specs,
            out_specs=out_specs,
            scratch_shapes=scratch,
        ),
        out_shape=place_output(0, out_shape) if single else [place_output(i, o) for i, o in enumerate(out_shape)],
        compiler_params=params(limit),
        cost_estimate=cost(MICROS[name]),
        name=name,
    )(meta, *(place_input(i, value) for i, value in enumerate(args)))


def fixed(*shape):
    return pl.BlockSpec(shape, lambda *_: (0,) * len(shape))


def like(shape, dtype):
    return jax.ShapeDtypeStruct(shape, dtype)


def project_kernel(meta_ref, x_ref, wq_ref, wk_ref, wv_ref, q_ref, k_ref, v_ref):
    x = x_ref[...]
    for w_ref, o_ref in ((wq_ref, q_ref), (wk_ref, k_ref), (wv_ref, v_ref)):
        o_ref[:, :192] = nt(x, w_ref[...]).astype(BF)
        o_ref[:, 192:] = jnp.zeros((x.shape[0], HEAD_DIM), BF)


def project(meta, tokens, weights, u, frames):
    rows, d = frames, tokens.shape[1]
    block = 256
    return call(
        project_kernel,
        "project",
        (rows // block,),
        meta,
        (tokens, *weights),
        [pl.BlockSpec((block, d), lambda i, m: (u * (rows // block) + i, 0))] + [fixed(192, d)] * 3,
        [pl.BlockSpec((block, 256), lambda i, m: (i, 0))] * 3,
        [like((rows, 256), BF)] * 3,
        far=range(4),
        out=(0, 1, 2),
    )


def forward_kernel(u, meta_ref, q_ref, k_ref, v_ref, own_ref, other_ref, lse_ref, s_ref):
    length = meta_ref[1 + u]
    step = pl.program_id(0)
    blocks = lax.div(length + KB - 1, KB)
    parts = lane_parts(q_ref[...] * jnp.asarray(0.125, BF))
    width = q_ref.shape[0]

    def first(kb, highest):
        start = pl.multiple_of(kb * KB, KB)
        rows = pl.ds(start, KB)
        live = start + lax.broadcasted_iota(jnp.int32, (KB, width), 0) < length
        out = []
        for h in range(3):
            tile = pl.ds(128 * TILE[h], 128)
            s = nt(k_ref[rows, tile], parts[h])
            s = jnp.where(live, s, -1e30)
            s_ref[h, rows, :] = s
            out.append(jnp.maximum(highest[h], jnp.max(s, axis=0, keepdims=True)))
        return tuple(out)

    floor = jnp.full((1, width), -1e30, F32)
    highest = lax.fori_loop(0, blocks, first, (floor,) * 3)

    def second(kb, carry):
        rows = pl.ds(pl.multiple_of(kb * KB, KB), KB)
        out = []
        for h in range(3):
            total, result = carry[h]
            p = jnp.exp2((s_ref[h, rows, :] - highest[h]) * LOG2E)
            total = total + jnp.sum(p, axis=0, keepdims=True)
            v = v_ref[rows, pl.ds(128 * TILE[h], 128)]
            result = result + tn(v, p.astype(BF))
            out.append((total, result))
        return tuple(out)

    init = ((jnp.zeros((1, width), F32), jnp.zeros((128, width), F32)),) * 3
    done = lax.fori_loop(0, blocks, second, init)
    outs = []
    for h in range(3):
        total, result = done[h]
        lo = HEAD_DIM * (h % 2)
        o = result[lo : lo + HEAD_DIM] / total
        lse_ref[0, pl.ds(h, 1), :] = highest[h] * LOG2E + jnp.log2(total)
        outs.append(o.astype(BF))
    whole = jnp.concatenate(outs, axis=0)
    for j, o_ref in enumerate((own_ref, other_ref)):

        @pl.when(step == j)
        def _():
            o_ref[...] = whole


def attend_forward(meta, q, k, v, u, frames):
    half = frames // 2
    return call(
        functools.partial(forward_kernel, u),
        "attend_forward",
        (2,),
        meta,
        (q, k, v),
        [
            pl.BlockSpec((half, 256), lambda i, m: (i ^ m[0], 0)),
            fixed(frames, 256),
            fixed(frames, 256),
        ],
        [
            fixed(192, half),
            fixed(192, half),
            pl.BlockSpec((1, 8, half), lambda i, m: (i, 0, 0)),
        ],
        [
            like((192, half), BF),
            like((192, half), BF),
            like((2, 8, half), F32),
        ],
        [pltpu.VMEM((3, frames, half), F32)],
        hold=(0, 1, 2),
    )


def backward_kernel(
    u, meta_ref, q_ref, k_ref, v_ref, d0_ref, d1_ref, o0_ref, o1_ref, lse_ref,
    dq_ref, dk_ref, dv_ref, kt_ref, dk_acc, dv_acc, do_ref, o_ref,
):
    length = meta_ref[1 + u]
    blocks = lax.div(length + KB - 1, KB)
    step = pl.program_id(0)

    @pl.when(step == 0)
    def _():
        dk_acc[...] = jnp.zeros_like(dk_acc)
        dv_acc[...] = jnp.zeros_like(dv_acc)
        kt_ref[...] = jnp.transpose(k_ref[...])
        do_ref[...] = d0_ref[...]
        o_ref[...] = o0_ref[...]

    @pl.when(step == 1)
    def _():
        do_ref[...] = d1_ref[...]
        o_ref[...] = o1_ref[...]

    parts = lane_parts(q_ref[...] * jnp.asarray(0.125, BF))
    width = q_ref.shape[0]
    empty = jnp.zeros((HEAD_DIM, width), BF)
    head = [do_ref[pl.ds(h * HEAD_DIM, HEAD_DIM), :] for h in range(3)]
    grads = (
        jnp.concatenate([head[0], empty], axis=0),
        jnp.concatenate([empty, head[1]], axis=0),
        jnp.concatenate([head[2], empty], axis=0),
    )
    delta = [
        jnp.sum(
            head[h].astype(F32) * o_ref[pl.ds(h * HEAD_DIM, HEAD_DIM), :].astype(F32), axis=0, keepdims=True
        )
        for h in range(3)
    ]
    lse = [lse_ref[0, pl.ds(h, 1), :] for h in range(3)]

    def body(kb, carry):
        start = pl.multiple_of(kb * KB, KB)
        rows = pl.ds(start, KB)
        live = start + lax.broadcasted_iota(jnp.int32, (KB, width), 0) < length
        out = []
        for h in range(3):
            tile = pl.ds(128 * TILE[h], 128)
            s = nt(k_ref[rows, tile], parts[h])
            s = jnp.where(live, s, -1e30)
            p = jnp.exp2(s * LOG2E - lse[h])
            dp = nn(v_ref[rows, tile], grads[h])
            ds = (p * (dp - delta[h])).astype(BF)
            dv_acc[rows, tile] += nt(p.astype(BF), grads[h])
            dk_acc[rows, tile] += nn(ds, parts[h])
            kt = kt_ref[pl.ds(h * HEAD_DIM, HEAD_DIM), rows]
            out.append(carry[h] + nn(kt, ds))
        return tuple(out)

    zero = jnp.zeros((HEAD_DIM, width), F32)
    done = lax.fori_loop(0, blocks, body, (zero,) * 3)
    full = jnp.concatenate(done + (zero,), axis=0) * 0.125
    dq_ref[...] = jnp.transpose(full).astype(BF)

    @pl.when(step == 1)
    def _():
        dk_ref[...] = dk_acc[...].astype(BF)
        dv_ref[...] = dv_acc[...].astype(BF)


def attend_backward(meta, q, k, v, grads, outs, lse, u, frames):
    half = frames // 2
    return call(
        functools.partial(backward_kernel, u),
        "attend_backward",
        (2,),
        meta,
        (q, k, v, *grads, *outs, lse),
        [
            pl.BlockSpec((half, 256), lambda i, m: (i ^ m[0], 0)),
            fixed(frames, 256),
            fixed(frames, 256),
            fixed(192, half),
            fixed(192, half),
            fixed(192, half),
            fixed(192, half),
            pl.BlockSpec((1, 8, half), lambda i, m: (i, 0, 0)),
        ],
        [
            pl.BlockSpec((half, 256), lambda i, m: (i ^ m[0], 0)),
            fixed(frames, 256),
            fixed(frames, 256),
        ],
        [like((frames, 256), BF)] * 3,
        [
            pltpu.VMEM((256, frames), BF),
            pltpu.VMEM((frames, 256), F32),
            pltpu.VMEM((frames, 256), F32),
            pltpu.VMEM((192, half), BF),
            pltpu.VMEM((192, half), BF),
        ],
        hold=(3,),
        far=(0, 1, 2),
        out=(0, 1, 2),
    )


def entry_kernel(meta_ref, x_ref, dq_ref, dk_ref, dv_ref, wq_ref, wk_ref, wv_ref, *refs):
    last = len(refs) == 7
    before_ref = refs[0] if last else None
    send_ref, keep_ref, sum_ref, acc = refs[-4:]
    step = pl.program_id(0)
    x = x_ref[...]
    total = jnp.zeros(x.shape, F32)
    for i, (g_ref, w_ref) in enumerate(((dq_ref, wq_ref), (dk_ref, wk_ref), (dv_ref, wv_ref))):
        rows = pl.ds(192 * i, 192)
        g = g_ref[:, :192]
        total = total + nn(g, w_ref[...])
        product = tn(g, x)

        @pl.when(step == 0)
        def _():
            acc[rows, :] = product if before_ref is None else product + before_ref[rows, :]

        @pl.when(step == 1)
        def _():
            sum_ref[rows, :] = (product + acc[rows, :]).astype(sum_ref.dtype)

    low = total.astype(BF)

    @pl.when(step == 0)
    def _():
        send_ref[...] = low
        if last:
            merged = refs[1][...].astype(F32) + refs[2][...].astype(F32)
            sum_ref[576:, :] = merged.astype(sum_ref.dtype)

    @pl.when(step == 1)
    def _():
        keep_ref[...] = low


def entry_back(meta, tokens, grads, weights, before, u, frames):
    half = frames // 2
    d = tokens.shape[1]
    rows, dtype = (832, BF) if before else (576, F32)
    return call(
        entry_kernel,
        "entry_back",
        (2,),
        meta,
        (tokens, *grads, *weights, *before),
        [pl.BlockSpec((half, d), lambda i, m: (u * 2 + (1 - i ^ m[0]), 0))]
        + [pl.BlockSpec((half, 256), lambda i, m: (1 - i ^ m[0], 0))] * 3
        + [fixed(192, d)] * 3
        + [fixed(*value.shape) for value in before],
        [fixed(half, d), fixed(half, d), fixed(rows, d)],
        [like((half, d), BF), like((half, d), BF), like((rows, d), dtype)],
        [pltpu.VMEM((576, d), F32)],
        hold=(1, 2, 3),
        far=(0, 4, 5, 6),
    )


def place_kernel(meta_ref, *refs):
    o_ref = refs[-1]
    for i, r_ref in enumerate(refs[:-1]):

        @pl.when(pl.program_id(0) == i)
        def _():
            o_ref[...] = r_ref[...]


def place(meta, own, other):
    half, d = own[0].shape
    count = 2 * len(own)
    return call(
        place_kernel,
        "place",
        (count,),
        meta,
        [block for pair in zip(own, other) for block in pair],
        [fixed(half, d)] * count,
        pl.BlockSpec((half, d), lambda i, m: (i ^ m[0], 0)),
        like((count * half, d), own[0].dtype),
    )


def normalise(values):
    average = jnp.mean(values, axis=-1, keepdims=True)
    centred = values - average
    spread = jnp.mean(centred * centred, axis=-1, keepdims=True)
    rstd = lax.rsqrt(spread + EPS)
    return centred * rstd, rstd


def gelu_pair(v):
    e = jnp.exp2(v * v * (-0.5 * LOG2E))
    t = 1.0 / (1.0 + (0.3275911 * 0.7071067811865476) * jnp.abs(v))
    poly = t * (0.5 * 0.254829592 + t * (0.5 * -0.284496736 + t * (0.5 * 1.421413741 + t * (0.5 * -1.453152027 + t * (0.5 * 1.061405429)))))
    tail = poly * e
    phi_cap = jnp.where(v >= 0, 1.0 - tail, tail)
    return v * phi_cap, phi_cap + v * (e * 0.3989422804014327)


def ahead_kernel(
    meta_ref, tok_ref, a0, a1, a2, a3, w0, w1, w2, w3, ua_ref, ub_ref, da_ref, db_ref, vec_ref,
    xhat_ref, rstd_ref, low_ref, act_ref, slope_ref, own_ref, sent_ref,
):
    gain, bias = vec_ref[0:1, :], vec_ref[1:2, :]
    hidden = ua_ref.shape[1]
    for r in range(tok_ref.shape[0] // RB):
        rows = pl.ds(r * RB, RB)
        branch = jnp.zeros((RB, tok_ref.shape[1]), F32)
        for a, w in ((a0, w0), (a1, w1), (a2, w2), (a3, w3)):
            branch = branch + tn(a[:, rows], w[...]).astype(BF).astype(F32)
        xhat, rstd = normalise(tok_ref[rows, :].astype(F32) + branch)
        xhat_ref[rows, :] = xhat
        rstd_ref[rows, :] = jnp.broadcast_to(rstd, (RB, rstd_ref.shape[1]))
        normed = xhat * gain + bias
        low = normed.astype(BF)
        low_ref[rows, :] = low
        sent = jnp.zeros(normed.shape, F32)
        for g, (up, down) in enumerate(((ua_ref, da_ref), (ub_ref, db_ref))):
            acts = []
            for c in range(hidden // HB):
                act, slope = gelu_pair(nn(low, up[:, c * HB : (c + 1) * HB]))
                columns = pl.ds(g * hidden + c * HB, HB)
                acts.append(act.astype(BF))
                act_ref[rows, columns] = acts[-1]
                slope_ref[rows, columns] = slope.astype(BF)
            sent = sent + nn(jnp.concatenate(acts, axis=1), down[...]).astype(BF).astype(F32)
        own_ref[rows, :] = normed + sent
        sent_ref[rows, :] = sent.astype(BF)


def ahead(meta, tokens, att, merge_w, up, down, vectors, u):
    half = att[0].shape[1]
    d, hidden = up[0].shape
    return call(
        ahead_kernel,
        "ahead",
        (1,),
        meta,
        (tokens, *att, *merge_w, *up, *down, vectors),
        [pl.BlockSpec((half, d), lambda i, m: (u * 2 + m[0], 0))]
        + [fixed(192, half)] * 4
        + [fixed(192, d)] * 4
        + [fixed(d, hidden)] * 2
        + [fixed(hidden, d)] * 2
        + [fixed(4, d)],
        [fixed(half, d), fixed(half, 128), fixed(half, d), fixed(half, 2 * hidden), fixed(half, 2 * hidden), fixed(half, d), fixed(half, d)],
        [
            like((half, d), F32),
            like((half, 128), F32),
            like((half, d), BF),
            like((half, 2 * hidden), BF),
            like((half, 2 * hidden), BF),
            like((half, d), F32),
            like((half, d), BF),
        ],
        far=(0,),
        out=(1, 2, 3, 4, 5),
        out_far=(0,),
    )


def astern_kernel(u, meta_ref, own_ref, far_ref, grad_ref, span_ref, ua_ref, ub_ref, da_ref, db_ref, slope_ref, vec_ref, *refs):
    last = len(refs) > 6
    before = refs[: len(refs) - 10] if last else ()
    out_ref, g_ref, pre_ref, back_ref, sent_ref, small_ref = refs[len(before) : len(before) + 6]
    gain, bias = vec_ref[2:3, :], vec_ref[3:4, :]
    half, d = own_ref.shape
    hidden = ua_ref.shape[1]
    starts = span_ref[u : u + 1, :]
    gain_grad = jnp.zeros(gain.shape, F32)
    bias_grad = jnp.zeros(gain.shape, F32)
    for r in range(half // RB):
        rows = pl.ds(r * RB, RB)
        xhat, rstd = normalise(own_ref[rows, :] + far_ref[rows, :].astype(F32))
        out_ref[rows, :] = (xhat * gain + bias).astype(BF)
        frame = meta_ref[0] * half + r * RB + lax.broadcasted_iota(jnp.int32, (RB, starts.shape[1]), 0)
        inside = (frame >= starts) & (frame < starts + SPAN)
        weight = jnp.max(jnp.where(inside, 1.0, 0.0), axis=1, keepdims=True)
        cot = grad_ref[rows, :].astype(F32) * weight
        gain_grad = gain_grad + jnp.sum(cot * xhat, axis=0, keepdims=True)
        bias_grad = bias_grad + jnp.sum(cot, axis=0, keepdims=True)
        gy = cot * gain
        mean_gy = jnp.mean(gy, axis=-1, keepdims=True)
        mean_gx = jnp.mean(gy * xhat, axis=-1, keepdims=True)
        sum_grad = rstd * (gy - mean_gy - xhat * mean_gx)
        low = sum_grad.astype(BF)
        g_ref[rows, :] = low
        sent = jnp.zeros(sum_grad.shape, F32)
        for g, (up, down) in enumerate(((ua_ref, da_ref), (ub_ref, db_ref))):
            pres = []
            for c in range(hidden // HB):
                columns = pl.ds(g * hidden + c * HB, HB)
                slope = slope_ref[rows, columns].astype(F32)
                pres.append((nt(low, down[c * HB : (c + 1) * HB, :]) * slope).astype(BF))
                pre_ref[rows, columns] = pres[-1]
            sent = sent + nt(jnp.concatenate(pres, axis=1), up[...]).astype(BF).astype(F32)
        back_ref[rows, :] = sum_grad + sent
        sent_ref[rows, :] = sent.astype(BF)
    small_ref[0:1, :] = gain_grad
    small_ref[1:2, :] = bias_grad
    if last:
        x_ref, act_ref = before[:2]
        weight_sums(x_ref[...], g_ref[...], act_ref, pre_ref, before[2:], refs[-4:])


def astern(meta, own, far, grad, spans, up, down, slope, vectors, u, before):
    half, d = own.shape
    hidden = up[0].shape[1]
    rows = fixed(half, d)
    wide = fixed(half, 2 * hidden)
    grads = [] if not before else [(d, hidden)] * 2 + [(hidden, d)] * 2
    extra = [] if not before else [rows, wide] + [fixed(*shape) for shape in grads[: len(before) - 2]]
    return call(
        functools.partial(astern_kernel, u),
        "astern",
        (1,),
        meta,
        (own, far, grad, spans, *up, *down, slope, vectors, *before),
        [rows] * 2
        + [pl.BlockSpec((half, d), lambda i, m: (u * 2 + m[0], 0)), fixed(*spans.shape)]
        + [fixed(d, hidden)] * 2
        + [fixed(hidden, d)] * 2
        + [wide, fixed(4, d)]
        + extra,
        [rows, rows, wide, rows, rows, fixed(2, d)] + [fixed(*shape) for shape in grads],
        [
            like((half, d), BF),
            like((half, d), BF),
            like((half, 2 * hidden), BF),
            like((half, d), F32),
            like((half, d), BF),
            like((2, d), F32),
        ]
        + [like(shape, BF) for shape in grads],
        limit=12 if before else VMEM,
        hold=(0, 8, *range(10, 10 + len(before))),
        far=(2,),
        out=(3,) if before else (1, 2, 3),
    )


def weight_kernel(meta_ref, x_ref, g_ref, act_ref, pre_ref, *refs):
    before, sums = refs[:-4], refs[-4:]
    weight_sums(x_ref[...], g_ref[...], act_ref, pre_ref, before, sums)


def weight_sums(x, g, act_ref, pre_ref, before, sums):
    hidden = act_ref.shape[1] // 2
    for i in range(2):
        for c in range(hidden // HB):
            columns = pl.ds(i * hidden + c * HB, HB)
            block = pl.ds(c * HB, HB)
            up = tn(x, pre_ref[:, columns])
            down = tn(act_ref[:, columns], g)
            if before:
                up = up + before[i][:, block].astype(F32)
                down = down + before[2 + i][block, :].astype(F32)
            sums[i][:, block] = up.astype(BF)
            sums[2 + i][block, :] = down.astype(BF)


def weight_grads(meta, x, g, act, pre, before):
    rows, d = x.shape
    hidden = act.shape[1] // 2
    shapes = [(d, hidden)] * 2 + [(hidden, d)] * 2
    return call(
        weight_kernel,
        "weight_grads",
        (1,),
        meta,
        (x, g, act, pre, *before),
        [fixed(rows, d)] * 2 + [fixed(rows, 2 * hidden)] * 2 + [fixed(*shape) for shape in shapes[: len(before)]],
        [fixed(*shape) for shape in shapes],
        [like(shape, BF) for shape in shapes],
        hold=(0, 1, 2, 3),
        out=(0, 1, 2, 3),
    )


def inner_kernel(meta_ref, own_ref, far_ref, xhat_ref, rstd_ref, vec_ref, a0, a1, w0, w1, *refs):
    last = len(refs) == 11
    out_ref, g0, g1, m0, m1, small_ref = refs[-6:]
    grad = own_ref[...] + far_ref[...].astype(F32)
    xhat = xhat_ref[...]
    gain_grad = jnp.sum(grad * xhat, axis=0, keepdims=True)
    bias_grad = jnp.sum(grad, axis=0, keepdims=True)
    gy = grad * vec_ref[0:1, :]
    mean_gy = jnp.mean(gy, axis=-1, keepdims=True)
    mean_gx = jnp.mean(gy * xhat, axis=-1, keepdims=True)
    inner = rstd_ref[:, 0:1] * (gy - mean_gy - xhat * mean_gx)
    out_ref[...] = inner
    low = inner.astype(BF)
    g0[...] = nt(w0[...], low).astype(BF)
    g1[...] = nt(w1[...], low).astype(BF)
    small = jnp.concatenate([gain_grad, bias_grad], axis=0)
    small_ref[...] = small
    if last:
        before0, before1, before_small, outer0, outer1 = refs[:5]
        below = jnp.concatenate(
            [small + before_small[...], outer0[...] + outer1[...], jnp.zeros((60, small.shape[1]), F32)], axis=0
        ).astype(BF)
        for m, a, before in ((m0, a0, before0), (m1, a1, before1)):
            m[:192, :] = (nn(a[...], low) + before[...]).astype(BF)
            m[192:, :] = below
    else:
        m0[...] = nn(a0[...], low)
        m1[...] = nn(a1[...], low)


def inner_norm(meta, own, far, xhat, rstd, vectors, att, weights, before):
    rows, d = xhat.shape
    merge = like((256, d), BF) if before else like((192, d), F32)
    return call(
        inner_kernel,
        "inner_norm",
        (1,),
        meta,
        (own, far, xhat, rstd, vectors, *att, *weights, *before),
        [fixed(rows, d)] * 3
        + [fixed(rows, 128), fixed(4, d)]
        + [fixed(192, rows)] * 2
        + [fixed(192, d)] * 2
        + ([fixed(192, d)] * 2 + [fixed(2, d)] * 3 if before else []),
        [fixed(rows, d), fixed(192, rows), fixed(192, rows), fixed(*merge.shape), fixed(*merge.shape), fixed(2, d)],
        [like((rows, d), F32), like((192, rows), BF), like((192, rows), BF), merge, merge, like((2, d), F32)],
        hold=(0, 3, 9, 10) if before else (0, 3),
        far=(2,),
        out=(1,) if before else (1, 3, 4),
        out_far=(0,),
    )


def fold_kernel(bits, meta_ref, *refs):
    for i in range(2):
        here, there = refs[2 * i : 2 * i + 2]
        if bits:
            send, keep = refs[4 + 2 * i : 6 + 2 * i]
            half = send.shape[0]
            bit = meta_ref[bits[i]]
            for part, j in ((send, 1 - bit), (keep, bit)):
                rows = pl.ds(pl.multiple_of(j * half, 16), half)
                part[...] = (here[rows, :].astype(F32) + there[rows, :].astype(F32)).astype(BF)
        else:
            refs[4 + i][...] = (here[...].astype(F32) + there[...].astype(F32)).astype(BF)


def fold(meta, pairs, bits, hold=()):
    args = [value for pair in pairs for value in pair]
    rows, d = args[0].shape
    shapes = [like((rows // 2, d), BF)] * 4 if bits else [like((rows, d), BF)] * 2
    return call(
        functools.partial(fold_kernel, bits),
        "fold",
        (1,),
        meta,
        args,
        [fixed(rows, d)] * 4,
        [fixed(*shape.shape) for shape in shapes],
        shapes,
        hold=hold,
    )


def local(groups, tokens, lengths, span_starts, wq, wk, wv, wm, wu, wd, ig, ib, og, ob, out_grad):
    rows, d = tokens.shape
    seqs = lengths.shape[0]
    frames = rows // seqs
    half = frames // 2
    core = lax.axis_index("tensor") % 2
    place_dp = lax.axis_index("dp")
    bits = groups.bit_length() - 1

    def swap(value, k):
        return lax.ppermute(value, "tensor", [(i, i ^ k) for i in range(4)])

    def swap_dp(value, k):
        return lax.ppermute(value, "dp", [(i, i ^ k) for i in range(groups)])

    def add(a, b):
        return (a.astype(F32) + b.astype(F32)).astype(BF)

    def total(pieces):
        return sum(piece.astype(F32) for piece in pieces).astype(BF) if len(pieces) > 1 else pieces[0]

    stages = [(0, 1)] + [(b, 2) for b in range(1, bits - 1, 2)] + ([(bits - 1, 1)] if bits % 2 == 0 else [])
    bit_orders = (list(range(bits)), [1, 0, *range(2, bits)])

    def spot_of(stage):
        return (place_dp >> stage[0]) & ((1 << stage[1]) - 1)

    class Chain:
        def __init__(self, part, order, cut_already=False):
            self.part = part.reshape((1,) * len(order) + part.shape) if cut_already else part
            self.order = order
            self.steps = [] if cut_already else [(True, stage) for stage in order]
            self.steps += [(False, stage) for stage in reversed(order)]

        def cut(self, stage, j):
            size = self.part.shape[0] >> stage[1]
            return lax.dynamic_slice_in_dim(self.part, (spot_of(stage) ^ j) * size, size, 0)

        def start(self):
            if self.steps:
                scatter, stage = self.steps[0]
                others = range(1, 1 << stage[1])
                self.pending = [swap_dp(self.cut(stage, j) if scatter else self.part, j << stage[0]) for j in others]

        def finish(self, *after):
            if not self.steps:
                return
            scatter, stage = self.steps.pop(0)
            got = self.pending
            if after:
                got = list(lax.optimization_barrier((*got, *after))[: len(got)])
            if scatter:
                state = total([self.cut(stage, 0)] + got)
                if not self.steps[0][0]:
                    state = state.reshape((1,) * len(self.order) + state.shape)
            else:
                axis = self.order.index(stage)
                spot = spot_of(stage)
                mine = self.part
                if len(got) == 1:
                    laid = [jnp.where(spot, got[0], mine), jnp.where(spot, mine, got[0])]
                    state = jnp.concatenate(laid, axis=axis)
                else:
                    state = jnp.zeros(mine.shape[:axis] + (1 + len(got),) + mine.shape[axis + 1 :], BF)
                    for j, piece in enumerate([mine] + got):
                        state = lax.dynamic_update_slice_in_dim(state, piece, spot ^ j, axis)
                if not self.steps:
                    state = state.reshape(-1, d)
            self.part = state

    def finish(group, *after):
        for chain in group:
            chain.finish(*after)

    def start(group):
        for chain in group:
            chain.start()

    def together(group):
        for chain, value in zip(group, lax.optimization_barrier(tuple(chain.part for chain in group))):
            chain.part = value

    all_bits = [((place_dp >> b) & 1).reshape(1) for b in range(bits)]
    scalars = jnp.concatenate([core.reshape(1), lengths, *all_bits])
    token = []

    def meta():
        return lax.optimization_barrier((scalars, *token))[0] if token else scalars

    def done(results, *others):
        token[:] = [results[0], *others]
        return results

    merge_w = (wm, swap(wm, 1), swap(wm, 2), swap(wm, 3))
    up_w = (wu, swap(wu, 1))
    down_w = (wd, swap(wd, 1))
    vectors = jnp.stack([ig, ib, og, ob])
    qkv_w = (wq.T, wk.T, wv.T)

    fwd, att, front, far = [], [], [], []
    qkv_of = [done(project(scalars, tokens, qkv_w, 0, frames))]
    for u in range(seqs):
        fwd.append(done(attend_forward(meta(), *qkv_of[u], u, frames), *(merge_w[1:] if u == 0 else ())))
        own, other = fwd[u][:2]
        att.append((own, swap(other, 1), swap(own, 2), swap(other, 3)))
        if u + 1 < seqs:
            qkv_of.append(done(project(meta(), tokens, qkv_w, u + 1, frames), up_w[1], down_w[1]))
    for u in range(seqs):
        front.append(done(ahead(meta(), tokens, att[u], merge_w, up_w, down_w, vectors, u)))
        far.append(swap(front[u][6], 2))
    back, far_grad, sums = [], [], ()
    for u in range(seqs):
        before = (front[u][2], front[u][3], *sums) if u == seqs - 1 else ()
        back.append(
            done(astern(meta(), front[u][5], far[u], out_grad, span_starts, up_w, down_w, front[u][4], vectors, u, before))
        )
        if u < seqs - 1:
            far_grad.append(swap(back[u][4], 2))
            sums = done(weight_grads(meta(), front[u][2], back[u][1], front[u][3], back[u][2], sums))

    def inner_step(u, before):
        res = done(inner_norm(meta(), back[u][3], far_grad[u], front[u][0], front[u][1], vectors, att[u][:2], merge_w[:2], before))
        return res, (res[1], swap(res[2], 1))

    def attend_step(u, grads):
        return done(attend_backward(meta(), *qkv_of[u], grads, fwd[u][:2], fwd[u][2], u, frames))

    def entry_step(u, grads, before):
        return done(entry_back(meta(), tokens, grads, qkv_w, before, u, frames))


    first_bit = 1 + seqs

    def scatter(step, pairs, after, hold=()):
        pairs = [tuple(lax.optimization_barrier((*pair, after))[:2]) for pair in pairs]
        if step == bits:
            return done(fold(meta(), pairs, (), hold))
        out = done(fold(meta(), pairs, tuple(first_bit + order[step] for order in bit_orders), hold))
        return [(out[2 * i + 1], swap_dp(out[2 * i], 1 << bit_orders[i][step])) for i in range(2)]

    inner, entry, so_far = [], [], ()
    for u in range(seqs):
        last = u == seqs - 1
        if u == 0:
            up_own, up_other, down_own, down_other = lax.optimization_barrier((*back[-1][6:], far_grad[0]))[:4]
            moving = [(down_own, swap(down_other, 1)), (up_own, swap(up_other, 1))]
            res, grads = inner_step(0, ())
            inner.append(res)
            far_grad.append(swap(lax.optimization_barrier((back[-1][4], res[0]))[0], 2))
            moving = scatter(0, moving, res[0], (0, 2))
        dqkv = attend_step(u, grads)
        moving = scatter(1 + 2 * u, moving, dqkv[0])
        if not last:
            before = ()
            if u + 1 == seqs - 1:
                before = (inner[0][3], inner[0][4], inner[0][5], back[0][5], back[1][5])
            res, grads = inner_step(u + 1, before)
            inner.append(res)
        else:
            for step in range(4, bits + 1):
                moving = scatter(step, moving, moving[0][0])
            first, second = (
                Chain(moving[i], [(b, 1) for b in order], True) for i, order in enumerate(bit_orders)
            )
            start([first, second])
        out = entry_step(u, dqkv, so_far)
        entry.append(out)
        if not last:
            merge_got = swap(lax.optimization_barrier((res[4], out[0]))[0], 1)
            so_far = (out[2], res[3], merge_got)
            moving = scatter(2, moving, out[0])
    qkv = Chain(out[2], stages)
    qkv.start()

    ready = []
    for u in range(seqs):
        got = swap(entry[u][0], 1)
        crossed = swap(total((entry[u][1], got)), 2)
        rest = entry[u][1].astype(F32) + got.astype(F32) + crossed.astype(F32)
        ready.append((inner[u][0] + rest).astype(BF))
    out_rows = [b[0] for b in back]
    layer_output = place(meta(), out_rows, [swap(r, 1) for r in out_rows])

    finish([first, second], got)
    for group, sending in (((qkv,), (qkv, first, second)), ((qkv, first, second), (qkv, first)), ((qkv, first), (qkv, second))):
        finish(group)
        together([qkv, first, second])
        start(sending)
    input_grad = place(scalars, ready, [swap(r, 1) for r in ready])
    finish([qkv, second], input_grad, layer_output)
    while qkv.steps or first.steps or second.steps:
        start([qkv, first, second])
        finish([qkv, first, second])
        together([qkv, first, second])
    down_sum, up_sum, joint = (chain.part for chain in (first, second, qkv))
    qkv_sum, merge_sum = joint[:576], joint[576:]
    small = merge_sum[192:196].astype(F32)
    query_grad, key_grad, value_grad = (qkv_sum[192 * i : 192 * (i + 1)].astype(F32).T for i in range(3))
    return (
        layer_output,
        input_grad,
        query_grad,
        key_grad,
        value_grad,
        merge_sum[:192].astype(F32),
        up_sum.astype(F32),
        down_sum.astype(F32),
        small[0],
        small[1],
        small[2],
        small[3],
    )


def solution(mesh):
    in_specs = (
        P("dp", None),
        P("dp"),
        P("dp", None),
        P(None, "tensor"),
        P(None, "tensor"),
        P(None, "tensor"),
        P("tensor", None),
        P(None, "tensor"),
        P("tensor", None),
        P(),
        P(),
        P(),
        P(),
        P("dp", None),
    )
    out_specs = (
        P("dp", None),
        P("dp", None),
        P(None, "tensor"),
        P(None, "tensor"),
        P(None, "tensor"),
        P("tensor", None),
        P(None, "tensor"),
        P("tensor", None),
        P(),
        P(),
        P(),
        P(),
    )
    body = functools.partial(local, mesh.shape["dp"])
    return jax.shard_map(body, mesh=mesh, in_specs=in_specs, out_specs=out_specs, check_vma=False)
```

```python
import functools

import jax
import jax.numpy as jnp
from jax import lax
from jax.experimental import pallas as pl
from jax.experimental.pallas import tpu as pltpu
from jax.sharding import PartitionSpec as P

HEAD_DIM = 64
SPAN = 10
EPS = 1e-05
LOG2E = 1.4426950408889634
KB = 256
VMEM = 12
RB = 128
HB = 256
BF = jnp.bfloat16
F32 = jnp.float32
MIB = 1 << 20


def nn(a, b):
    return lax.dot_general(a, b, (((1,), (0,)), ((), ())), preferred_element_type=F32)


def nt(a, b):
    return lax.dot_general(a, b, (((1,), (1,)), ((), ())), preferred_element_type=F32)


def tn(a, b):
    return lax.dot_general(a, b, (((0,), (0,)), ((), ())), preferred_element_type=F32)


def params(limit):
    return pltpu.CompilerParams(vmem_limit_bytes=limit * MIB)


def cost(micros):
    return pl.CostEstimate(flops=int(micros * 1.1e9), bytes_accessed=1024, transcendentals=0)


MICROS = {"project": 3, "attend_forward": 8, "attend_backward": 12, "entry_back": 5, "place": 3, "ahead": 9, "astern": 10, "inner_norm": 3, "weight_grads": 4, "fold": 2}


def lane_parts(block):
    left = block[:, :128]
    lane = lax.broadcasted_iota(jnp.int32, left.shape, 1)
    zero = jnp.zeros_like(left)
    return (
        jnp.where(lane < HEAD_DIM, left, zero),
        jnp.where(lane >= HEAD_DIM, left, zero),
        block[:, 128:],
    )


TILE = (0, 0, 1)


def call(kernel, name, grid, meta, args, in_specs, out_specs, out_shape, scratch=(), limit=VMEM, hold=(), far=(), out=(), out_far=()):
    def place_input(i, value):
        space = pltpu.VMEM if i in hold else pltpu.HBM if i in far else None
        return value if space is None else pltpu.with_memory_space_constraint(value, space)

    def place_output(i, value):
        space = pltpu.VMEM if i in out else pltpu.HBM if i in out_far else None
        return value if space is None else space(value.shape, value.dtype)

    single = not isinstance(out_shape, list)
    return pl.pallas_call(
        kernel,
        grid_spec=pltpu.PrefetchScalarGridSpec(
            num_scalar_prefetch=1,
            grid=grid,
            in_specs=in_specs,
            out_specs=out_specs,
            scratch_shapes=scratch,
        ),
        out_shape=place_output(0, out_shape) if single else [place_output(i, o) for i, o in enumerate(out_shape)],
        compiler_params=params(limit),
        cost_estimate=cost(MICROS[name]),
        name=name,
    )(meta, *(place_input(i, value) for i, value in enumerate(args)))


def fixed(*shape):
    return pl.BlockSpec(shape, lambda *_: (0,) * len(shape))


def like(shape, dtype):
    return jax.ShapeDtypeStruct(shape, dtype)


def project_kernel(meta_ref, x_ref, wq_ref, wk_ref, wv_ref, q_ref, k_ref, v_ref):
    x = x_ref[...]
    for w_ref, o_ref in ((wq_ref, q_ref), (wk_ref, k_ref), (wv_ref, v_ref)):
        o_ref[:, :192] = nt(x, w_ref[...]).astype(BF)
        o_ref[:, 192:] = jnp.zeros((x.shape[0], HEAD_DIM), BF)


def project(meta, tokens, weights, u, frames):
    rows, d = frames, tokens.shape[1]
    block = 256
    return call(
        project_kernel,
        "project",
        (rows // block,),
        meta,
        (tokens, *weights),
        [pl.BlockSpec((block, d), lambda i, m: (u * (rows // block) + i, 0))] + [fixed(192, d)] * 3,
        [pl.BlockSpec((block, 256), lambda i, m: (i, 0))] * 3,
        [like((rows, 256), BF)] * 3,
        far=range(4),
        out=(0, 1, 2),
    )


def forward_kernel(u, meta_ref, q_ref, k_ref, v_ref, own_ref, other_ref, lse_ref, s_ref):
    length = meta_ref[1 + u]
    step = pl.program_id(0)
    blocks = lax.div(length + KB - 1, KB)
    parts = lane_parts(q_ref[...] * jnp.asarray(0.125, BF))
    width = q_ref.shape[0]

    def first(kb, highest):
        start = pl.multiple_of(kb * KB, KB)
        rows = pl.ds(start, KB)
        live = start + lax.broadcasted_iota(jnp.int32, (KB, width), 0) < length
        out = []
        for h in range(3):
            tile = pl.ds(128 * TILE[h], 128)
            s = nt(k_ref[rows, tile], parts[h])
            s = jnp.where(live, s, -1e30)
            s_ref[h, rows, :] = s
            out.append(jnp.maximum(highest[h], jnp.max(s, axis=0, keepdims=True)))
        return tuple(out)

    floor = jnp.full((1, width), -1e30, F32)
    highest = lax.fori_loop(0, blocks, first, (floor,) * 3)

    def second(kb, carry):
        rows = pl.ds(pl.multiple_of(kb * KB, KB), KB)
        out = []
        for h in range(3):
            total, result = carry[h]
            p = jnp.exp2((s_ref[h, rows, :] - highest[h]) * LOG2E)
            total = total + jnp.sum(p, axis=0, keepdims=True)
            v = v_ref[rows, pl.ds(128 * TILE[h], 128)]
            result = result + tn(v, p.astype(BF))
            out.append((total, result))
        return tuple(out)

    init = ((jnp.zeros((1, width), F32), jnp.zeros((128, width), F32)),) * 3
    done = lax.fori_loop(0, blocks, second, init)
    outs = []
    for h in range(3):
        total, result = done[h]
        lo = HEAD_DIM * (h % 2)
        o = result[lo : lo + HEAD_DIM] / total
        lse_ref[0, pl.ds(h, 1), :] = highest[h] * LOG2E + jnp.log2(total)
        outs.append(o.astype(BF))
    whole = jnp.concatenate(outs, axis=0)
    for j, o_ref in enumerate((own_ref, other_ref)):

        @pl.when(step == j)
        def _():
            o_ref[...] = whole


def attend_forward(meta, q, k, v, u, frames):
    half = frames // 2
    return call(
        functools.partial(forward_kernel, u),
        "attend_forward",
        (2,),
        meta,
        (q, k, v),
        [
            pl.BlockSpec((half, 256), lambda i, m: (i ^ m[0], 0)),
            fixed(frames, 256),
            fixed(frames, 256),
        ],
        [
            fixed(192, half),
            fixed(192, half),
            pl.BlockSpec((1, 8, half), lambda i, m: (i, 0, 0)),
        ],
        [
            like((192, half), BF),
            like((192, half), BF),
            like((2, 8, half), F32),
        ],
        [pltpu.VMEM((3, frames, half), F32)],
        hold=(0, 1, 2),
    )


def backward_kernel(
    u, meta_ref, q_ref, k_ref, v_ref, d0_ref, d1_ref, o0_ref, o1_ref, lse_ref,
    dq_ref, dk_ref, dv_ref, kt_ref, dk_acc, dv_acc, do_ref, o_ref,
):
    length = meta_ref[1 + u]
    blocks = lax.div(length + KB - 1, KB)
    step = pl.program_id(0)

    @pl.when(step == 0)
    def _():
        dk_acc[...] = jnp.zeros_like(dk_acc)
        dv_acc[...] = jnp.zeros_like(dv_acc)
        kt_ref[...] = jnp.transpose(k_ref[...])
        do_ref[...] = d0_ref[...]
        o_ref[...] = o0_ref[...]

    @pl.when(step == 1)
    def _():
        do_ref[...] = d1_ref[...]
        o_ref[...] = o1_ref[...]

    parts = lane_parts(q_ref[...] * jnp.asarray(0.125, BF))
    width = q_ref.shape[0]
    empty = jnp.zeros((HEAD_DIM, width), BF)
    head = [do_ref[pl.ds(h * HEAD_DIM, HEAD_DIM), :] for h in range(3)]
    grads = (
        jnp.concatenate([head[0], empty], axis=0),
        jnp.concatenate([empty, head[1]], axis=0),
        jnp.concatenate([head[2], empty], axis=0),
    )
    delta = [
        jnp.sum(
            head[h].astype(F32) * o_ref[pl.ds(h * HEAD_DIM, HEAD_DIM), :].astype(F32), axis=0, keepdims=True
        )
        for h in range(3)
    ]
    lse = [lse_ref[0, pl.ds(h, 1), :] for h in range(3)]

    def body(kb, carry):
        start = pl.multiple_of(kb * KB, KB)
        rows = pl.ds(start, KB)
        live = start + lax.broadcasted_iota(jnp.int32, (KB, width), 0) < length
        out = []
        for h in range(3):
            tile = pl.ds(128 * TILE[h], 128)
            s = nt(k_ref[rows, tile], parts[h])
            s = jnp.where(live, s, -1e30)
            p = jnp.exp2(s * LOG2E - lse[h])
            dp = nn(v_ref[rows, tile], grads[h])
            ds = (p * (dp - delta[h])).astype(BF)
            dv_acc[rows, tile] += nt(p.astype(BF), grads[h])
            dk_acc[rows, tile] += nn(ds, parts[h])
            kt = kt_ref[pl.ds(h * HEAD_DIM, HEAD_DIM), rows]
            out.append(carry[h] + nn(kt, ds))
        return tuple(out)

    zero = jnp.zeros((HEAD_DIM, width), F32)
    done = lax.fori_loop(0, blocks, body, (zero,) * 3)
    full = jnp.concatenate(done + (zero,), axis=0) * 0.125
    dq_ref[...] = jnp.transpose(full).astype(BF)

    @pl.when(step == 1)
    def _():
        dk_ref[...] = dk_acc[...].astype(BF)
        dv_ref[...] = dv_acc[...].astype(BF)


def attend_backward(meta, q, k, v, grads, outs, lse, u, frames):
    half = frames // 2
    return call(
        functools.partial(backward_kernel, u),
        "attend_backward",
        (2,),
        meta,
        (q, k, v, *grads, *outs, lse),
        [
            pl.BlockSpec((half, 256), lambda i, m: (i ^ m[0], 0)),
            fixed(frames, 256),
            fixed(frames, 256),
            fixed(192, half),
            fixed(192, half),
            fixed(192, half),
            fixed(192, half),
            pl.BlockSpec((1, 8, half), lambda i, m: (i, 0, 0)),
        ],
        [
            pl.BlockSpec((half, 256), lambda i, m: (i ^ m[0], 0)),
            fixed(frames, 256),
            fixed(frames, 256),
        ],
        [like((frames, 256), BF)] * 3,
        [
            pltpu.VMEM((256, frames), BF),
            pltpu.VMEM((frames, 256), F32),
            pltpu.VMEM((frames, 256), F32),
            pltpu.VMEM((192, half), BF),
            pltpu.VMEM((192, half), BF),
        ],
        hold=(3,),
        far=(0, 1, 2),
        out=(0, 1, 2),
    )


def entry_kernel(meta_ref, x_ref, dq_ref, dk_ref, dv_ref, wq_ref, wk_ref, wv_ref, *refs):
    last = len(refs) == 7
    before_ref = refs[0] if last else None
    send_ref, keep_ref, sum_ref, acc = refs[-4:]
    step = pl.program_id(0)
    x = x_ref[...]
    total = jnp.zeros(x.shape, F32)
    for i, (g_ref, w_ref) in enumerate(((dq_ref, wq_ref), (dk_ref, wk_ref), (dv_ref, wv_ref))):
        rows = pl.ds(192 * i, 192)
        g = g_ref[:, :192]
        total = total + nn(g, w_ref[...])
        product = tn(g, x)

        @pl.when(step == 0)
        def _():
            acc[rows, :] = product if before_ref is None else product + before_ref[rows, :]

        @pl.when(step == 1)
        def _():
            sum_ref[rows, :] = (product + acc[rows, :]).astype(sum_ref.dtype)

    low = total.astype(BF)

    @pl.when(step == 0)
    def _():
        send_ref[...] = low
        if last:
            merged = refs[1][...].astype(F32) + refs[2][...].astype(F32)
            sum_ref[576:, :] = merged.astype(sum_ref.dtype)

    @pl.when(step == 1)
    def _():
        keep_ref[...] = low


def entry_back(meta, tokens, grads, weights, before, u, frames):
    half = frames // 2
    d = tokens.shape[1]
    rows, dtype = (832, BF) if before else (576, F32)
    return call(
        entry_kernel,
        "entry_back",
        (2,),
        meta,
        (tokens, *grads, *weights, *before),
        [pl.BlockSpec((half, d), lambda i, m: (u * 2 + (1 - i ^ m[0]), 0))]
        + [pl.BlockSpec((half, 256), lambda i, m: (1 - i ^ m[0], 0))] * 3
        + [fixed(192, d)] * 3
        + [fixed(*value.shape) for value in before],
        [fixed(half, d), fixed(half, d), fixed(rows, d)],
        [like((half, d), BF), like((half, d), BF), like((rows, d), dtype)],
        [pltpu.VMEM((576, d), F32)],
        hold=(1, 2, 3),
        far=(0, 4, 5, 6),
    )


def place_kernel(meta_ref, *refs):
    o_ref = refs[-1]
    for i, r_ref in enumerate(refs[:-1]):

        @pl.when(pl.program_id(0) == i)
        def _():
            o_ref[...] = r_ref[...]


def place(meta, own, other):
    half, d = own[0].shape
    count = 2 * len(own)
    return call(
        place_kernel,
        "place",
        (count,),
        meta,
        [block for pair in zip(own, other) for block in pair],
        [fixed(half, d)] * count,
        pl.BlockSpec((half, d), lambda i, m: (i ^ m[0], 0)),
        like((count * half, d), own[0].dtype),
    )


def normalise(values):
    average = jnp.mean(values, axis=-1, keepdims=True)
    centred = values - average
    spread = jnp.mean(centred * centred, axis=-1, keepdims=True)
    rstd = lax.rsqrt(spread + EPS)
    return centred * rstd, rstd


def gelu_pair(v):
    e = jnp.exp2(v * v * (-0.5 * LOG2E))
    t = 1.0 / (1.0 + (0.3275911 * 0.7071067811865476) * jnp.abs(v))
    poly = t * (0.5 * 0.254829592 + t * (0.5 * -0.284496736 + t * (0.5 * 1.421413741 + t * (0.5 * -1.453152027 + t * (0.5 * 1.061405429)))))
    tail = poly * e
    phi_cap = jnp.where(v >= 0, 1.0 - tail, tail)
    return v * phi_cap, phi_cap + v * (e * 0.3989422804014327)


def ahead_kernel(
    meta_ref, tok_ref, a0, a1, a2, a3, w0, w1, w2, w3, ua_ref, ub_ref, da_ref, db_ref, vec_ref,
    xhat_ref, rstd_ref, low_ref, act_ref, slope_ref, own_ref, sent_ref,
):
    gain, bias = vec_ref[0:1, :], vec_ref[1:2, :]
    hidden = ua_ref.shape[1]
    for r in range(tok_ref.shape[0] // RB):
        rows = pl.ds(r * RB, RB)
        branch = jnp.zeros((RB, tok_ref.shape[1]), F32)
        for a, w in ((a0, w0), (a1, w1), (a2, w2), (a3, w3)):
            branch = branch + tn(a[:, rows], w[...]).astype(BF).astype(F32)
        xhat, rstd = normalise(tok_ref[rows, :].astype(F32) + branch)
        xhat_ref[rows, :] = xhat
        rstd_ref[rows, :] = jnp.broadcast_to(rstd, (RB, rstd_ref.shape[1]))
        normed = xhat * gain + bias
        low = normed.astype(BF)
        low_ref[rows, :] = low
        sent = jnp.zeros(normed.shape, F32)
        for g, (up, down) in enumerate(((ua_ref, da_ref), (ub_ref, db_ref))):
            acts = []
            for c in range(hidden // HB):
                act, slope = gelu_pair(nn(low, up[:, c * HB : (c + 1) * HB]))
                columns = pl.ds(g * hidden + c * HB, HB)
                acts.append(act.astype(BF))
                act_ref[rows, columns] = acts[-1]
                slope_ref[rows, columns] = slope.astype(BF)
            sent = sent + nn(jnp.concatenate(acts, axis=1), down[...]).astype(BF).astype(F32)
        own_ref[rows, :] = normed + sent
        sent_ref[rows, :] = sent.astype(BF)


def ahead(meta, tokens, att, merge_w, up, down, vectors, u):
    half = att[0].shape[1]
    d, hidden = up[0].shape
    return call(
        ahead_kernel,
        "ahead",
        (1,),
        meta,
        (tokens, *att, *merge_w, *up, *down, vectors),
        [pl.BlockSpec((half, d), lambda i, m: (u * 2 + m[0], 0))]
        + [fixed(192, half)] * 4
        + [fixed(192, d)] * 4
        + [fixed(d, hidden)] * 2
        + [fixed(hidden, d)] * 2
        + [fixed(4, d)],
        [fixed(half, d), fixed(half, 128), fixed(half, d), fixed(half, 2 * hidden), fixed(half, 2 * hidden), fixed(half, d), fixed(half, d)],
        [
            like((half, d), F32),
            like((half, 128), F32),
            like((half, d), BF),
            like((half, 2 * hidden), BF),
            like((half, 2 * hidden), BF),
            like((half, d), F32),
            like((half, d), BF),
        ],
        far=(0,),
        out=(2, 3, 4, 5),
        out_far=(0, 1),
    )


def astern_kernel(u, meta_ref, own_ref, far_ref, grad_ref, span_ref, ua_ref, ub_ref, da_ref, db_ref, slope_ref, vec_ref, *refs):
    last = len(refs) > 6
    if last:
        before = refs[:-10]
        out_ref, back_ref, sent_ref, small_ref, *sums, g_ref, pre_ref = refs[-10:]
    else:
        out_ref, g_ref, pre_ref, back_ref, sent_ref, small_ref = refs
    gain, bias = vec_ref[2:3, :], vec_ref[3:4, :]
    half, d = own_ref.shape
    hidden = ua_ref.shape[1]
    starts = span_ref[u : u + 1, :]
    gain_grad = jnp.zeros(gain.shape, F32)
    bias_grad = jnp.zeros(gain.shape, F32)
    for r in range(half // RB):
        rows = pl.ds(r * RB, RB)
        xhat, rstd = normalise(own_ref[rows, :] + far_ref[rows, :].astype(F32))
        out_ref[rows, :] = (xhat * gain + bias).astype(BF)
        frame = meta_ref[0] * half + r * RB + lax.broadcasted_iota(jnp.int32, (RB, starts.shape[1]), 0)
        inside = (frame >= starts) & (frame < starts + SPAN)
        weight = jnp.max(jnp.where(inside, 1.0, 0.0), axis=1, keepdims=True)
        cot = grad_ref[rows, :].astype(F32) * weight
        gain_grad = gain_grad + jnp.sum(cot * xhat, axis=0, keepdims=True)
        bias_grad = bias_grad + jnp.sum(cot, axis=0, keepdims=True)
        gy = cot * gain
        mean_gy = jnp.mean(gy, axis=-1, keepdims=True)
        mean_gx = jnp.mean(gy * xhat, axis=-1, keepdims=True)
        sum_grad = rstd * (gy - mean_gy - xhat * mean_gx)
        low = sum_grad.astype(BF)
        g_ref[rows, :] = low
        sent = jnp.zeros(sum_grad.shape, F32)
        for g, (up, down) in enumerate(((ua_ref, da_ref), (ub_ref, db_ref))):
            pres = []
            for c in range(hidden // HB):
                columns = pl.ds(g * hidden + c * HB, HB)
                slope = slope_ref[rows, columns].astype(F32)
                pres.append((nt(low, down[c * HB : (c + 1) * HB, :]) * slope).astype(BF))
                pre_ref[rows, columns] = pres[-1]
            sent = sent + nt(jnp.concatenate(pres, axis=1), up[...]).astype(BF).astype(F32)
        back_ref[rows, :] = sum_grad + sent
        sent_ref[rows, :] = sent.astype(BF)
    small_ref[0:1, :] = gain_grad
    small_ref[1:2, :] = bias_grad
    if last:
        x_ref, act_ref = before[:2]
        weight_sums(x_ref[...], g_ref[...], act_ref, pre_ref, before[2:], sums)


def astern(meta, own, far, grad, spans, up, down, slope, vectors, u, before):
    half, d = own.shape
    hidden = up[0].shape[1]
    rows = fixed(half, d)
    wide = fixed(half, 2 * hidden)
    grads = [] if not before else [(d, hidden)] * 2 + [(hidden, d)] * 2
    extra = [] if not before else [rows, wide] + [fixed(*shape) for shape in grads[: len(before) - 2]]
    made = [like((half, d), BF), like((half, 2 * hidden), BF)]
    others = [like((half, d), F32), like((half, d), BF), like((2, d), F32)]
    shapes = [like((half, d), BF)] + ([] if before else made) + others + [like(shape, BF) for shape in grads]
    return call(
        functools.partial(astern_kernel, u),
        "astern",
        (1,),
        meta,
        (own, far, grad, spans, *up, *down, slope, vectors, *before),
        [rows] * 2
        + [pl.BlockSpec((half, d), lambda i, m: (u * 2 + m[0], 0)), fixed(*spans.shape)]
        + [fixed(d, hidden)] * 2
        + [fixed(hidden, d)] * 2
        + [wide, fixed(4, d)]
        + extra,
        [fixed(*shape.shape) for shape in shapes],
        shapes,
        [pltpu.VMEM(shape.shape, shape.dtype) for shape in made] if before else (),
        limit=20 if before else VMEM,
        hold=(0, 8, *range(10, 10 + len(before))),
        far=(2,),
        out=() if before else (1, 2),
        out_far=(0, 1) if before else (0, 3),
    )


def weight_kernel(meta_ref, x_ref, g_ref, act_ref, pre_ref, *refs):
    before, sums = refs[:-4], refs[-4:]
    weight_sums(x_ref[...], g_ref[...], act_ref, pre_ref, before, sums)


def weight_sums(x, g, act_ref, pre_ref, before, sums):
    hidden = act_ref.shape[1] // 2
    for i in range(2):
        for c in range(hidden // HB):
            columns = pl.ds(i * hidden + c * HB, HB)
            block = pl.ds(c * HB, HB)
            up = tn(x, pre_ref[:, columns])
            down = tn(act_ref[:, columns], g)
            if before:
                up = up + before[i][:, block].astype(F32)
                down = down + before[2 + i][block, :].astype(F32)
            sums[i][:, block] = up.astype(BF)
            sums[2 + i][block, :] = down.astype(BF)


def weight_grads(meta, x, g, act, pre, before):
    rows, d = x.shape
    hidden = act.shape[1] // 2
    shapes = [(d, hidden)] * 2 + [(hidden, d)] * 2
    return call(
        weight_kernel,
        "weight_grads",
        (1,),
        meta,
        (x, g, act, pre, *before),
        [fixed(rows, d)] * 2 + [fixed(rows, 2 * hidden)] * 2 + [fixed(*shape) for shape in shapes[: len(before)]],
        [fixed(*shape) for shape in shapes],
        [like(shape, BF) for shape in shapes],
        hold=(0, 1, 2, 3),
        out=(0, 1, 2, 3),
    )


def inner_kernel(meta_ref, own_ref, far_ref, xhat_ref, rstd_ref, vec_ref, a0, a1, w0, w1, *refs):
    last = len(refs) == 11
    out_ref, g0, g1, m0, m1, small_ref = refs[-6:]
    grad = own_ref[...] + far_ref[...].astype(F32)
    xhat = xhat_ref[...]
    gain_grad = jnp.sum(grad * xhat, axis=0, keepdims=True)
    bias_grad = jnp.sum(grad, axis=0, keepdims=True)
    gy = grad * vec_ref[0:1, :]
    mean_gy = jnp.mean(gy, axis=-1, keepdims=True)
    mean_gx = jnp.mean(gy * xhat, axis=-1, keepdims=True)
    inner = rstd_ref[:, 0:1] * (gy - mean_gy - xhat * mean_gx)
    out_ref[...] = inner
    low = inner.astype(BF)
    g0[...] = nt(w0[...], low).astype(BF)
    g1[...] = nt(w1[...], low).astype(BF)
    small = jnp.concatenate([gain_grad, bias_grad], axis=0)
    small_ref[...] = small
    if last:
        before0, before1, before_small, outer0, outer1 = refs[:5]
        below = jnp.concatenate(
            [small + before_small[...], outer0[...] + outer1[...], jnp.zeros((60, small.shape[1]), F32)], axis=0
        ).astype(BF)
        for m, a, before in ((m0, a0, before0), (m1, a1, before1)):
            m[:192, :] = (nn(a[...], low) + before[...]).astype(BF)
            m[192:, :] = below
    else:
        m0[...] = nn(a0[...], low)
        m1[...] = nn(a1[...], low)


def inner_norm(meta, own, far, xhat, rstd, vectors, att, weights, before):
    rows, d = xhat.shape
    merge = like((256, d), BF) if before else like((192, d), F32)
    return call(
        inner_kernel,
        "inner_norm",
        (1,),
        meta,
        (own, far, xhat, rstd, vectors, *att, *weights, *before),
        [fixed(rows, d)] * 3
        + [fixed(rows, 128), fixed(4, d)]
        + [fixed(192, rows)] * 2
        + [fixed(192, d)] * 2
        + ([fixed(192, d)] * 2 + [fixed(2, d)] * 3 if before else []),
        [fixed(rows, d), fixed(192, rows), fixed(192, rows), fixed(*merge.shape), fixed(*merge.shape), fixed(2, d)],
        [like((rows, d), F32), like((192, rows), BF), like((192, rows), BF), merge, merge, like((2, d), F32)],
        far=(0, 2, 3, 5, 6, 7, 8, *((9, 10) if before else ())),
        out=(1,),
        out_far=(0,) if before else (0, 3, 4),
    )


def fold_kernel(bits, meta_ref, *refs):
    for i in range(2):
        here, there = refs[2 * i : 2 * i + 2]
        if bits:
            send, keep = refs[4 + 2 * i : 6 + 2 * i]
            half = send.shape[0]
            bit = meta_ref[bits[i]]
            for part, j in ((send, 1 - bit), (keep, bit)):
                rows = pl.ds(pl.multiple_of(j * half, 16), half)
                part[...] = (here[rows, :].astype(F32) + there[rows, :].astype(F32)).astype(BF)
        else:
            refs[4 + i][...] = (here[...].astype(F32) + there[...].astype(F32)).astype(BF)


def fold(meta, pairs, bits, hold=()):
    args = [value for pair in pairs for value in pair]
    rows, d = args[0].shape
    shapes = [like((rows // 2, d), BF)] * 4 if bits else [like((rows, d), BF)] * 2
    return call(
        functools.partial(fold_kernel, bits),
        "fold",
        (1,),
        meta,
        args,
        [fixed(rows, d)] * 4,
        [fixed(*shape.shape) for shape in shapes],
        shapes,
        hold=hold,
    )


def local(groups, tokens, lengths, span_starts, wq, wk, wv, wm, wu, wd, ig, ib, og, ob, out_grad):
    rows, d = tokens.shape
    seqs = lengths.shape[0]
    frames = rows // seqs
    half = frames // 2
    core = lax.axis_index("tensor") % 2
    place_dp = lax.axis_index("dp")
    bits = groups.bit_length() - 1

    def swap(value, k):
        return lax.ppermute(value, "tensor", [(i, i ^ k) for i in range(4)])

    def swap_dp(value, k):
        return lax.ppermute(value, "dp", [(i, i ^ k) for i in range(groups)])

    def add(a, b):
        return (a.astype(F32) + b.astype(F32)).astype(BF)

    def total(pieces):
        return sum(piece.astype(F32) for piece in pieces).astype(BF) if len(pieces) > 1 else pieces[0]

    stages = [(0, 1)] + [(b, 2) for b in range(1, bits - 1, 2)] + ([(bits - 1, 1)] if bits % 2 == 0 else [])
    bit_orders = (list(range(bits)), [1, 0, *range(2, bits)])

    def spot_of(stage):
        return (place_dp >> stage[0]) & ((1 << stage[1]) - 1)

    class Chain:
        def __init__(self, part, order, cut_already=False):
            self.part = part.reshape((1,) * len(order) + part.shape) if cut_already else part
            self.order = order
            self.steps = [] if cut_already else [(True, stage) for stage in order]
            self.steps += [(False, stage) for stage in reversed(order)]

        def cut(self, stage, j):
            size = self.part.shape[0] >> stage[1]
            return lax.dynamic_slice_in_dim(self.part, (spot_of(stage) ^ j) * size, size, 0)

        def start(self):
            if self.steps:
                scatter, stage = self.steps[0]
                others = range(1, 1 << stage[1])
                self.pending = [swap_dp(self.cut(stage, j) if scatter else self.part, j << stage[0]) for j in others]

        def finish(self, *after):
            if not self.steps:
                return
            scatter, stage = self.steps.pop(0)
            got = self.pending
            if after:
                got = list(lax.optimization_barrier((*got, *after))[: len(got)])
            if scatter:
                state = total([self.cut(stage, 0)] + got)
                if not self.steps[0][0]:
                    state = state.reshape((1,) * len(self.order) + state.shape)
            else:
                axis = self.order.index(stage)
                spot = spot_of(stage)
                mine = self.part
                if len(got) == 1:
                    laid = [jnp.where(spot, got[0], mine), jnp.where(spot, mine, got[0])]
                    state = jnp.concatenate(laid, axis=axis)
                else:
                    state = jnp.zeros(mine.shape[:axis] + (1 + len(got),) + mine.shape[axis + 1 :], BF)
                    for j, piece in enumerate([mine] + got):
                        state = lax.dynamic_update_slice_in_dim(state, piece, spot ^ j, axis)
                if not self.steps:
                    state = state.reshape(-1, d)
            self.part = state

    def finish(group, *after):
        for chain in group:
            chain.finish(*after)

    def start(group):
        for chain in group:
            chain.start()

    def together(group):
        for chain, value in zip(group, lax.optimization_barrier(tuple(chain.part for chain in group))):
            chain.part = value

    all_bits = [((place_dp >> b) & 1).reshape(1) for b in range(bits)]
    scalars = jnp.concatenate([core.reshape(1), lengths, *all_bits])
    token = []

    def meta():
        return lax.optimization_barrier((scalars, *token))[0] if token else scalars

    def done(results, *others):
        token[:] = [results[0], *others]
        return results

    merge_w = (wm, swap(wm, 1), swap(wm, 2), swap(wm, 3))
    up_w = (wu, swap(wu, 1))
    down_w = (wd, swap(wd, 1))
    vectors = jnp.stack([ig, ib, og, ob])
    qkv_w = (wq.T, wk.T, wv.T)

    fwd, att, front, far = [], [], [], []
    qkv_of = [done(project(scalars, tokens, qkv_w, 0, frames))]
    for u in range(seqs):
        fwd.append(done(attend_forward(meta(), *qkv_of[u], u, frames), *(merge_w[1:] if u == 0 else ())))
        own, other = fwd[u][:2]
        att.append((own, swap(other, 1), swap(own, 2), swap(other, 3)))
        if u + 1 < seqs:
            qkv_of.append(done(project(meta(), tokens, qkv_w, u + 1, frames), up_w[1], down_w[1]))
    for u in range(seqs):
        front.append(done(ahead(meta(), tokens, att[u], merge_w, up_w, down_w, vectors, u)))
        far.append(swap(front[u][6], 2))
    out_rows, back, far_grad, smalls, sums = [], [], [], [], ()
    for u in range(seqs):
        last = u == seqs - 1
        before = (front[u][2], front[u][3], *sums) if last else ()
        res = done(astern(meta(), front[u][5], far[u], out_grad, span_starts, up_w, down_w, front[u][4], vectors, u, before))
        out_rows.append(res[0])
        back.append(res[1 if last else 3])
        smalls.append(res[3 if last else 5])
        if last:
            sent, sums = res[2], res[4:]
        else:
            far_grad.append(swap(res[4], 2))
            sums = done(weight_grads(meta(), front[u][2], res[1], front[u][3], res[2], sums))

    def inner_step(u, before):
        res = done(inner_norm(meta(), back[u], far_grad[u], front[u][0], front[u][1], vectors, att[u][:2], merge_w[:2], before))
        return res, (res[1], swap(res[2], 1))

    def attend_step(u, grads):
        return done(attend_backward(meta(), *qkv_of[u], grads, fwd[u][:2], fwd[u][2], u, frames))

    def entry_step(u, grads, before):
        return done(entry_back(meta(), tokens, grads, qkv_w, before, u, frames))


    first_bit = 1 + seqs

    def scatter(step, pairs, after, hold=()):
        pairs = [tuple(lax.optimization_barrier((*pair, after))[:2]) for pair in pairs]
        if step == bits:
            return done(fold(meta(), pairs, (), hold))
        out = done(fold(meta(), pairs, tuple(first_bit + order[step] for order in bit_orders), hold))
        return [(out[2 * i + 1], swap_dp(out[2 * i], 1 << bit_orders[i][step])) for i in range(2)]

    inner, entry, so_far, near, crossed = [], [], (), [], []
    out_other = [swap(r, 1) for r in out_rows]

    def exchange(out):
        got = swap(out[0], 1)
        near.append((out[1], got))
        crossed.append(swap(total(near[-1]), 2))
        return got

    for u in range(seqs):
        last = u == seqs - 1
        if u == 0:
            up_own, up_other, down_own, down_other = lax.optimization_barrier((*sums, far_grad[0]))[:4]
            moving = [(down_own, swap(down_other, 1)), (up_own, swap(up_other, 1))]
            res, grads = inner_step(0, ())
            inner.append(res)
            far_grad.append(swap(lax.optimization_barrier((sent, res[0]))[0], 2))
            moving = scatter(0, moving, res[0])
        dqkv = attend_step(u, grads)
        moving = scatter(1 + 2 * u, moving, dqkv[0])
        if not last:
            before = ()
            if u + 1 == seqs - 1:
                before = (inner[0][3], inner[0][4], inner[0][5], *smalls)
            res, grads = inner_step(u + 1, before)
            inner.append(res)
        else:
            for step in range(4, bits + 1):
                moving = scatter(step, moving, moving[0][0])
            first, second = (
                Chain(moving[i], [(b, 1) for b in order], True) for i, order in enumerate(bit_orders)
            )
            start([first, second])
            token.extend(out_other)
        out = entry_step(u, dqkv, so_far)
        entry.append(out)
        if not last:
            merge_got = swap(lax.optimization_barrier((res[4], out[0]))[0], 1)
            so_far = (out[2], res[3], merge_got)
            moving = scatter(2, moving, out[0])
            exchange(out)
    qkv = Chain(out[2], stages)
    qkv.start()

    got = exchange(out)
    layer_output = place(meta(), out_rows, out_other)

    finish([first, second], got)
    finish([qkv], crossed[0])
    together([qkv, first, second])
    start([qkv, first, second])
    finish([qkv, first, second], crossed[-1])
    together([qkv, first, second])
    start([qkv, first])
    ready = []
    for u in range(seqs):
        rest = near[u][0].astype(F32) + near[u][1].astype(F32) + crossed[u].astype(F32)
        ready.append((inner[u][0] + rest).astype(BF))
    input_grad = place(scalars, ready, [swap(r, 1) for r in ready])
    finish([qkv, first], layer_output)
    together([qkv, first, second])
    start([qkv, second])
    finish([qkv, second], input_grad)
    while qkv.steps or first.steps or second.steps:
        start([qkv, first, second])
        finish([qkv, first, second])
        together([qkv, first, second])
    down_sum, up_sum, joint = (chain.part for chain in (first, second, qkv))
    qkv_sum, merge_sum = joint[:576], joint[576:]
    small = merge_sum[192:196].astype(F32)
    query_grad, key_grad, value_grad = (qkv_sum[192 * i : 192 * (i + 1)].astype(F32).T for i in range(3))
    return (
        layer_output,
        input_grad,
        query_grad,
        key_grad,
        value_grad,
        merge_sum[:192].astype(F32),
        up_sum.astype(F32),
        down_sum.astype(F32),
        small[0],
        small[1],
        small[2],
        small[3],
    )


def solution(mesh):
    in_specs = (
        P("dp", None),
        P("dp"),
        P("dp", None),
        P(None, "tensor"),
        P(None, "tensor"),
        P(None, "tensor"),
        P("tensor", None),
        P(None, "tensor"),
        P("tensor", None),
        P(),
        P(),
        P(),
        P(),
        P("dp", None),
    )
    out_specs = (
        P("dp", None),
        P("dp", None),
        P(None, "tensor"),
        P(None, "tensor"),
        P(None, "tensor"),
        P("tensor", None),
        P(None, "tensor"),
        P("tensor", None),
        P(),
        P(),
        P(),
        P(),
    )
    body = functools.partial(local, mesh.shape["dp"])
    return jax.shard_map(body, mesh=mesh, in_specs=in_specs, out_specs=out_specs, check_vma=False)
```

```python
import functools

import jax
import jax.numpy as jnp
from jax import lax
from jax.experimental import pallas as pl
from jax.experimental.pallas import tpu as pltpu
from jax.sharding import PartitionSpec as P

HEAD_DIM = 64
SPAN = 10
EPS = 1e-05
LOG2E = 1.4426950408889634
KB = 512
VMEM = 12
RB = 128
HB = 256
BF = jnp.bfloat16
F32 = jnp.float32
MIB = 1 << 20


def nn(a, b):
    return lax.dot_general(a, b, (((1,), (0,)), ((), ())), preferred_element_type=F32)


def nt(a, b):
    return lax.dot_general(a, b, (((1,), (1,)), ((), ())), preferred_element_type=F32)


def tn(a, b):
    return lax.dot_general(a, b, (((0,), (0,)), ((), ())), preferred_element_type=F32)


def params(limit):
    return pltpu.CompilerParams(vmem_limit_bytes=limit * MIB)


def cost(micros):
    return pl.CostEstimate(flops=int(micros * 1.1e9), bytes_accessed=1024, transcendentals=0)


MICROS = {"project": 3, "attend_forward": 8, "attend_backward": 12, "entry_back": 5, "place": 3, "ahead": 9, "astern": 10, "inner_norm": 3, "weight_grads": 4, "fold": 2}


def lane_parts(block):
    left = block[:, :128]
    lane = lax.broadcasted_iota(jnp.int32, left.shape, 1)
    zero = jnp.zeros_like(left)
    return (
        jnp.where(lane < HEAD_DIM, left, zero),
        jnp.where(lane >= HEAD_DIM, left, zero),
        block[:, 128:],
    )


TILE = (0, 0, 1)


def call(kernel, name, grid, meta, args, in_specs, out_specs, out_shape, scratch=(), limit=VMEM, hold=(), far=(), out=(), out_far=()):
    def place_input(i, value):
        space = pltpu.VMEM if i in hold else pltpu.HBM if i in far else None
        return value if space is None else pltpu.with_memory_space_constraint(value, space)

    def place_output(i, value):
        space = pltpu.VMEM if i in out else pltpu.HBM if i in out_far else None
        return value if space is None else space(value.shape, value.dtype)

    single = not isinstance(out_shape, list)
    return pl.pallas_call(
        kernel,
        grid_spec=pltpu.PrefetchScalarGridSpec(
            num_scalar_prefetch=1,
            grid=grid,
            in_specs=in_specs,
            out_specs=out_specs,
            scratch_shapes=scratch,
        ),
        out_shape=place_output(0, out_shape) if single else [place_output(i, o) for i, o in enumerate(out_shape)],
        compiler_params=params(limit),
        cost_estimate=cost(MICROS[name]),
        name=name,
    )(meta, *(place_input(i, value) for i, value in enumerate(args)))


def fixed(*shape):
    return pl.BlockSpec(shape, lambda *_: (0,) * len(shape))


def like(shape, dtype):
    return jax.ShapeDtypeStruct(shape, dtype)


def project_kernel(meta_ref, x_ref, wq_ref, wk_ref, wv_ref, q_ref, k_ref, v_ref):
    x = x_ref[...]
    for w_ref, o_ref in ((wq_ref, q_ref), (wk_ref, k_ref), (wv_ref, v_ref)):
        o_ref[:, :192] = nt(x, w_ref[...]).astype(BF)
        o_ref[:, 192:] = jnp.zeros((x.shape[0], HEAD_DIM), BF)


def project(meta, tokens, weights, u, frames):
    rows, d = frames, tokens.shape[1]
    block = 256
    return call(
        project_kernel,
        "project",
        (rows // block,),
        meta,
        (tokens, *weights),
        [pl.BlockSpec((block, d), lambda i, m: (u * (rows // block) + i, 0))] + [fixed(192, d)] * 3,
        [pl.BlockSpec((block, 256), lambda i, m: (i, 0))] * 3,
        [like((rows, 256), BF)] * 3,
        far=range(4),
        out=(0, 1, 2),
    )


def forward_kernel(u, meta_ref, q_ref, k_ref, v_ref, own_ref, other_ref, lse_ref, s_ref):
    length = meta_ref[1 + u]
    step = pl.program_id(0)
    blocks = lax.div(length + KB - 1, KB)
    parts = lane_parts(q_ref[...] * jnp.asarray(0.125, BF))
    width = q_ref.shape[0]

    def first(kb, highest):
        start = pl.multiple_of(kb * KB, KB)
        rows = pl.ds(start, KB)
        live = start + lax.broadcasted_iota(jnp.int32, (KB, width), 0) < length
        out = []
        for h in range(3):
            tile = pl.ds(128 * TILE[h], 128)
            s = nt(k_ref[rows, tile], parts[h])
            s = jnp.where(live, s, -1e30)
            s_ref[h, rows, :] = s
            out.append(jnp.maximum(highest[h], jnp.max(s, axis=0, keepdims=True)))
        return tuple(out)

    floor = jnp.full((1, width), -1e30, F32)
    highest = lax.fori_loop(0, blocks, first, (floor,) * 3)

    def second(kb, carry):
        rows = pl.ds(pl.multiple_of(kb * KB, KB), KB)
        out = []
        for h in range(3):
            total, result = carry[h]
            p = jnp.exp2((s_ref[h, rows, :] - highest[h]) * LOG2E)
            total = total + jnp.sum(p, axis=0, keepdims=True)
            v = v_ref[rows, pl.ds(128 * TILE[h], 128)]
            result = result + tn(v, p.astype(BF))
            out.append((total, result))
        return tuple(out)

    init = ((jnp.zeros((1, width), F32), jnp.zeros((128, width), F32)),) * 3
    done = lax.fori_loop(0, blocks, second, init)
    outs = []
    for h in range(3):
        total, result = done[h]
        lo = HEAD_DIM * (h % 2)
        o = result[lo : lo + HEAD_DIM] / total
        lse_ref[0, pl.ds(h, 1), :] = highest[h] * LOG2E + jnp.log2(total)
        outs.append(o.astype(BF))
    whole = jnp.concatenate(outs, axis=0)
    for j, o_ref in enumerate((own_ref, other_ref)):

        @pl.when(step == j)
        def _():
            o_ref[...] = whole


def attend_forward(meta, q, k, v, u, frames):
    half = frames // 2
    return call(
        functools.partial(forward_kernel, u),
        "attend_forward",
        (2,),
        meta,
        (q, k, v),
        [
            pl.BlockSpec((half, 256), lambda i, m: (i ^ m[0], 0)),
            fixed(frames, 256),
            fixed(frames, 256),
        ],
        [
            fixed(192, half),
            fixed(192, half),
            pl.BlockSpec((1, 8, half), lambda i, m: (i, 0, 0)),
        ],
        [
            like((192, half), BF),
            like((192, half), BF),
            like((2, 8, half), F32),
        ],
        [pltpu.VMEM((3, frames, half), F32)],
        hold=(0, 1, 2),
    )


def backward_kernel(
    u, meta_ref, q_ref, k_ref, v_ref, d0_ref, d1_ref, o0_ref, o1_ref, lse_ref,
    dq_ref, dk_ref, dv_ref, kt_ref, dk_acc, dv_acc, do_ref, o_ref,
):
    length = meta_ref[1 + u]
    blocks = lax.div(length + KB - 1, KB)
    step = pl.program_id(0)

    @pl.when(step == 0)
    def _():
        dk_acc[...] = jnp.zeros_like(dk_acc)
        dv_acc[...] = jnp.zeros_like(dv_acc)
        kt_ref[...] = jnp.transpose(k_ref[...])
        do_ref[...] = d0_ref[...]
        o_ref[...] = o0_ref[...]

    @pl.when(step == 1)
    def _():
        do_ref[...] = d1_ref[...]
        o_ref[...] = o1_ref[...]

    parts = lane_parts(q_ref[...] * jnp.asarray(0.125, BF))
    width = q_ref.shape[0]
    empty = jnp.zeros((HEAD_DIM, width), BF)
    head = [do_ref[pl.ds(h * HEAD_DIM, HEAD_DIM), :] for h in range(3)]
    grads = (
        jnp.concatenate([head[0], empty], axis=0),
        jnp.concatenate([empty, head[1]], axis=0),
        jnp.concatenate([head[2], empty], axis=0),
    )
    delta = [
        jnp.sum(
            head[h].astype(F32) * o_ref[pl.ds(h * HEAD_DIM, HEAD_DIM), :].astype(F32), axis=0, keepdims=True
        )
        for h in range(3)
    ]
    lse = [lse_ref[0, pl.ds(h, 1), :] for h in range(3)]

    def body(kb, carry):
        start = pl.multiple_of(kb * KB, KB)
        rows = pl.ds(start, KB)
        live = start + lax.broadcasted_iota(jnp.int32, (KB, width), 0) < length
        out = []
        for h in range(3):
            tile = pl.ds(128 * TILE[h], 128)
            s = nt(k_ref[rows, tile], parts[h])
            s = jnp.where(live, s, -1e30)
            p = jnp.exp2(s * LOG2E - lse[h])
            dp = nn(v_ref[rows, tile], grads[h])
            ds = (p * (dp - delta[h])).astype(BF)
            dv_acc[rows, tile] += nt(p.astype(BF), grads[h])
            dk_acc[rows, tile] += nn(ds, parts[h])
            kt = kt_ref[pl.ds(h * HEAD_DIM, HEAD_DIM), rows]
            out.append(carry[h] + nn(kt, ds))
        return tuple(out)

    zero = jnp.zeros((HEAD_DIM, width), F32)
    done = lax.fori_loop(0, blocks, body, (zero,) * 3)
    full = jnp.concatenate(done + (zero,), axis=0) * 0.125
    dq_ref[...] = jnp.transpose(full).astype(BF)

    @pl.when(step == 1)
    def _():
        dk_ref[...] = dk_acc[...].astype(BF)
        dv_ref[...] = dv_acc[...].astype(BF)


def attend_backward(meta, q, k, v, grads, outs, lse, u, frames):
    half = frames // 2
    return call(
        functools.partial(backward_kernel, u),
        "attend_backward",
        (2,),
        meta,
        (q, k, v, *grads, *outs, lse),
        [
            pl.BlockSpec((half, 256), lambda i, m: (i ^ m[0], 0)),
            fixed(frames, 256),
            fixed(frames, 256),
            fixed(192, half),
            fixed(192, half),
            fixed(192, half),
            fixed(192, half),
            pl.BlockSpec((1, 8, half), lambda i, m: (i, 0, 0)),
        ],
        [
            pl.BlockSpec((half, 256), lambda i, m: (i ^ m[0], 0)),
            fixed(frames, 256),
            fixed(frames, 256),
        ],
        [like((frames, 256), BF)] * 3,
        [
            pltpu.VMEM((256, frames), BF),
            pltpu.VMEM((frames, 256), F32),
            pltpu.VMEM((frames, 256), F32),
            pltpu.VMEM((192, half), BF),
            pltpu.VMEM((192, half), BF),
        ],
        hold=(3,),
        far=(0, 1, 2),
        out=(0, 1, 2),
    )


def entry_kernel(meta_ref, x_ref, dq_ref, dk_ref, dv_ref, wq_ref, wk_ref, wv_ref, *refs):
    last = len(refs) == 7
    before_ref = refs[0] if last else None
    send_ref, keep_ref, sum_ref, acc = refs[-4:]
    step = pl.program_id(0)
    x = x_ref[...]
    total = jnp.zeros(x.shape, F32)
    for i, (g_ref, w_ref) in enumerate(((dq_ref, wq_ref), (dk_ref, wk_ref), (dv_ref, wv_ref))):
        rows = pl.ds(192 * i, 192)
        g = g_ref[:, :192]
        total = total + nn(g, w_ref[...])
        product = tn(g, x)

        @pl.when(step == 0)
        def _():
            acc[rows, :] = product if before_ref is None else product + before_ref[rows, :]

        @pl.when(step == 1)
        def _():
            sum_ref[rows, :] = (product + acc[rows, :]).astype(sum_ref.dtype)

    low = total.astype(BF)

    @pl.when(step == 0)
    def _():
        send_ref[...] = low
        if last:
            merged = refs[1][...].astype(F32) + refs[2][...].astype(F32)
            sum_ref[576:, :] = merged.astype(sum_ref.dtype)

    @pl.when(step == 1)
    def _():
        keep_ref[...] = low


def entry_back(meta, tokens, grads, weights, before, u, frames):
    half = frames // 2
    d = tokens.shape[1]
    rows, dtype = (832, BF) if before else (576, F32)
    return call(
        entry_kernel,
        "entry_back",
        (2,),
        meta,
        (tokens, *grads, *weights, *before),
        [pl.BlockSpec((half, d), lambda i, m: (u * 2 + (1 - i ^ m[0]), 0))]
        + [pl.BlockSpec((half, 256), lambda i, m: (1 - i ^ m[0], 0))] * 3
        + [fixed(192, d)] * 3
        + [fixed(*value.shape) for value in before],
        [fixed(half, d), fixed(half, d), fixed(rows, d)],
        [like((half, d), BF), like((half, d), BF), like((rows, d), dtype)],
        [pltpu.VMEM((576, d), F32)],
        hold=(1, 2, 3),
        far=(0, 4, 5, 6),
    )


def place_kernel(meta_ref, *refs):
    o_ref = refs[-1]
    for i, r_ref in enumerate(refs[:-1]):

        @pl.when(pl.program_id(0) == i)
        def _():
            o_ref[...] = r_ref[...]


def place(meta, own, other):
    half, d = own[0].shape
    count = 2 * len(own)
    return call(
        place_kernel,
        "place",
        (count,),
        meta,
        [block for pair in zip(own, other) for block in pair],
        [fixed(half, d)] * count,
        pl.BlockSpec((half, d), lambda i, m: (i ^ m[0], 0)),
        like((count * half, d), own[0].dtype),
    )


def normalise(values):
    average = jnp.mean(values, axis=-1, keepdims=True)
    centred = values - average
    spread = jnp.mean(centred * centred, axis=-1, keepdims=True)
    rstd = lax.rsqrt(spread + EPS)
    return centred * rstd, rstd


def gelu_pair(v):
    e = jnp.exp2(v * v * (-0.5 * LOG2E))
    t = 1.0 / (1.0 + (0.3275911 * 0.7071067811865476) * jnp.abs(v))
    poly = t * (0.5 * 0.254829592 + t * (0.5 * -0.284496736 + t * (0.5 * 1.421413741 + t * (0.5 * -1.453152027 + t * (0.5 * 1.061405429)))))
    tail = poly * e
    phi_cap = jnp.where(v >= 0, 1.0 - tail, tail)
    return v * phi_cap, phi_cap + v * (e * 0.3989422804014327)


def ahead_kernel(
    meta_ref, tok_ref, a0, a1, a2, a3, w0, w1, w2, w3, ua_ref, ub_ref, da_ref, db_ref, vec_ref,
    xhat_ref, rstd_ref, low_ref, act_ref, slope_ref, own_ref, *sent_refs,
):
    gain, bias = vec_ref[0:1, :], vec_ref[1:2, :]
    hidden = ua_ref.shape[1]
    count = tok_ref.shape[0] // RB
    for r in range(count):
        rows = pl.ds(r * RB, RB)
        branch = jnp.zeros((RB, tok_ref.shape[1]), F32)
        for a, w in ((a0, w0), (a1, w1), (a2, w2), (a3, w3)):
            branch = branch + tn(a[:, rows], w[...]).astype(BF).astype(F32)
        xhat, rstd = normalise(tok_ref[rows, :].astype(F32) + branch)
        xhat_ref[rows, :] = xhat
        rstd_ref[rows, :] = jnp.broadcast_to(rstd, (RB, rstd_ref.shape[1]))
        normed = xhat * gain + bias
        low = normed.astype(BF)
        low_ref[rows, :] = low
        sent = jnp.zeros(normed.shape, F32)
        for g, (up, down) in enumerate(((ua_ref, da_ref), (ub_ref, db_ref))):
            acts = []
            for c in range(hidden // HB):
                act, slope = gelu_pair(nn(low, up[:, c * HB : (c + 1) * HB]))
                columns = pl.ds(g * hidden + c * HB, HB)
                acts.append(act.astype(BF))
                act_ref[rows, columns] = acts[-1]
                slope_ref[rows, columns] = slope.astype(BF)
            sent = sent + nn(jnp.concatenate(acts, axis=1), down[...]).astype(BF).astype(F32)
        own_ref[rows, :] = normed + sent
        per = count // len(sent_refs)
        sent_refs[r // per][pl.ds(r % per * RB, RB), :] = sent.astype(BF)


def ahead(meta, tokens, att, merge_w, up, down, vectors, u, cuts):
    half = att[0].shape[1]
    d, hidden = up[0].shape
    return call(
        ahead_kernel,
        "ahead",
        (1,),
        meta,
        (tokens, *att, *merge_w, *up, *down, vectors),
        [pl.BlockSpec((half, d), lambda i, m: (u * 2 + m[0], 0))]
        + [fixed(192, half)] * 4
        + [fixed(192, d)] * 4
        + [fixed(d, hidden)] * 2
        + [fixed(hidden, d)] * 2
        + [fixed(4, d)],
        [fixed(half, d), fixed(half, 128), fixed(half, d), fixed(half, 2 * hidden), fixed(half, 2 * hidden), fixed(half, d)]
        + [fixed(half // cuts, d)] * cuts,
        [
            like((half, d), F32),
            like((half, 128), F32),
            like((half, d), BF),
            like((half, 2 * hidden), BF),
            like((half, 2 * hidden), BF),
            like((half, d), F32),
        ]
        + [like((half // cuts, d), BF)] * cuts,
        far=(0,),
        out=(2, 3, 4, 5),
        out_far=(0, 1),
    )


def astern_kernel(u, cuts, meta_ref, own_ref, *refs):
    far_refs = refs[:cuts]
    grad_ref, span_ref, ua_ref, ub_ref, da_ref, db_ref, slope_ref, vec_ref, *refs = refs[cuts:]
    last = len(refs) > 6
    if last:
        before = refs[:-10]
        out_ref, back_ref, sent_ref, small_ref, *sums, g_ref, pre_ref = refs[-10:]
    else:
        out_ref, g_ref, pre_ref, back_ref, sent_ref, small_ref = refs
    gain, bias = vec_ref[2:3, :], vec_ref[3:4, :]
    half, d = own_ref.shape
    hidden = ua_ref.shape[1]
    starts = span_ref[u : u + 1, :]
    gain_grad = jnp.zeros(gain.shape, F32)
    bias_grad = jnp.zeros(gain.shape, F32)
    for r in range(half // RB):
        rows = pl.ds(r * RB, RB)
        per = half // RB // cuts
        far = far_refs[r // per][pl.ds(r % per * RB, RB), :].astype(F32)
        xhat, rstd = normalise(own_ref[rows, :] + far)
        out_ref[rows, :] = (xhat * gain + bias).astype(BF)
        frame = meta_ref[0] * half + r * RB + lax.broadcasted_iota(jnp.int32, (RB, starts.shape[1]), 0)
        inside = (frame >= starts) & (frame < starts + SPAN)
        weight = jnp.max(jnp.where(inside, 1.0, 0.0), axis=1, keepdims=True)
        cot = grad_ref[rows, :].astype(F32) * weight
        gain_grad = gain_grad + jnp.sum(cot * xhat, axis=0, keepdims=True)
        bias_grad = bias_grad + jnp.sum(cot, axis=0, keepdims=True)
        gy = cot * gain
        mean_gy = jnp.mean(gy, axis=-1, keepdims=True)
        mean_gx = jnp.mean(gy * xhat, axis=-1, keepdims=True)
        sum_grad = rstd * (gy - mean_gy - xhat * mean_gx)
        low = sum_grad.astype(BF)
        g_ref[rows, :] = low
        sent = jnp.zeros(sum_grad.shape, F32)
        for g, (up, down) in enumerate(((ua_ref, da_ref), (ub_ref, db_ref))):
            pres = []
            for c in range(hidden // HB):
                columns = pl.ds(g * hidden + c * HB, HB)
                slope = slope_ref[rows, columns].astype(F32)
                pres.append((nt(low, down[c * HB : (c + 1) * HB, :]) * slope).astype(BF))
                pre_ref[rows, columns] = pres[-1]
            sent = sent + nt(jnp.concatenate(pres, axis=1), up[...]).astype(BF).astype(F32)
        back_ref[rows, :] = sum_grad + sent
        sent_ref[rows, :] = sent.astype(BF)
    small_ref[0:1, :] = gain_grad
    small_ref[1:2, :] = bias_grad
    if last:
        x_ref, act_ref = before[:2]
        weight_sums(x_ref[...], g_ref[...], act_ref, pre_ref, before[2:], sums)


def astern(meta, own, far, grad, spans, up, down, slope, vectors, u, before):
    half, d = own.shape
    hidden = up[0].shape[1]
    cuts = len(far)
    rows = fixed(half, d)
    wide = fixed(half, 2 * hidden)
    grads = [] if not before else [(d, hidden)] * 2 + [(hidden, d)] * 2
    extra = [] if not before else [rows, wide] + [fixed(*shape) for shape in grads[: len(before) - 2]]
    made = [like((half, d), BF), like((half, 2 * hidden), BF)]
    others = [like((half, d), F32), like((half, d), BF), like((2, d), F32)]
    shapes = [like((half, d), BF)] + ([] if before else made) + others + [like(shape, BF) for shape in grads]
    return call(
        functools.partial(astern_kernel, u, cuts),
        "astern",
        (1,),
        meta,
        (own, *far, grad, spans, *up, *down, slope, vectors, *before),
        [rows]
        + [fixed(half // cuts, d)] * cuts
        + [pl.BlockSpec((half, d), lambda i, m: (u * 2 + m[0], 0)), fixed(*spans.shape)]
        + [fixed(d, hidden)] * 2
        + [fixed(hidden, d)] * 2
        + [wide, fixed(4, d)]
        + extra,
        [fixed(*shape.shape) for shape in shapes],
        shapes,
        [pltpu.VMEM(shape.shape, shape.dtype) for shape in made] if before else (),
        limit=20 if before else VMEM,
        hold=(0, 7 + cuts, *range(9 + cuts, 9 + cuts + len(before))),
        far=(1 + cuts,),
        out=() if before else (1, 2),
        out_far=(0, 1) if before else (0, 3),
    )


def weight_kernel(meta_ref, x_ref, g_ref, act_ref, pre_ref, *refs):
    before, sums = refs[:-4], refs[-4:]
    weight_sums(x_ref[...], g_ref[...], act_ref, pre_ref, before, sums)


def weight_sums(x, g, act_ref, pre_ref, before, sums):
    hidden = act_ref.shape[1] // 2
    for i in range(2):
        for c in range(hidden // HB):
            columns = pl.ds(i * hidden + c * HB, HB)
            block = pl.ds(c * HB, HB)
            up = tn(x, pre_ref[:, columns])
            down = tn(act_ref[:, columns], g)
            if before:
                up = up + before[i][:, block].astype(F32)
                down = down + before[2 + i][block, :].astype(F32)
            sums[i][:, block] = up.astype(BF)
            sums[2 + i][block, :] = down.astype(BF)


def weight_grads(meta, x, g, act, pre, before):
    rows, d = x.shape
    hidden = act.shape[1] // 2
    shapes = [(d, hidden)] * 2 + [(hidden, d)] * 2
    return call(
        weight_kernel,
        "weight_grads",
        (1,),
        meta,
        (x, g, act, pre, *before),
        [fixed(rows, d)] * 2 + [fixed(rows, 2 * hidden)] * 2 + [fixed(*shape) for shape in shapes[: len(before)]],
        [fixed(*shape) for shape in shapes],
        [like(shape, BF) for shape in shapes],
        hold=(0, 1, 2, 3),
        out=(0, 1, 2, 3),
    )


def inner_kernel(meta_ref, own_ref, far_ref, xhat_ref, rstd_ref, vec_ref, a0, a1, w0, w1, *refs):
    last = len(refs) == 11
    out_ref, g0, g1, m0, m1, small_ref = refs[-6:]
    grad = own_ref[...] + far_ref[...].astype(F32)
    xhat = xhat_ref[...]
    gain_grad = jnp.sum(grad * xhat, axis=0, keepdims=True)
    bias_grad = jnp.sum(grad, axis=0, keepdims=True)
    gy = grad * vec_ref[0:1, :]
    mean_gy = jnp.mean(gy, axis=-1, keepdims=True)
    mean_gx = jnp.mean(gy * xhat, axis=-1, keepdims=True)
    inner = rstd_ref[:, 0:1] * (gy - mean_gy - xhat * mean_gx)
    out_ref[...] = inner
    low = inner.astype(BF)
    g0[...] = nt(w0[...], low).astype(BF)
    g1[...] = nt(w1[...], low).astype(BF)
    small = jnp.concatenate([gain_grad, bias_grad], axis=0)
    small_ref[...] = small
    if last:
        before0, before1, before_small, outer0, outer1 = refs[:5]
        below = jnp.concatenate(
            [small + before_small[...], outer0[...] + outer1[...], jnp.zeros((60, small.shape[1]), F32)], axis=0
        ).astype(BF)
        for m, a, before in ((m0, a0, before0), (m1, a1, before1)):
            m[:192, :] = (nn(a[...], low) + before[...]).astype(BF)
            m[192:, :] = below
    else:
        m0[...] = nn(a0[...], low)
        m1[...] = nn(a1[...], low)


def inner_norm(meta, own, far, xhat, rstd, vectors, att, weights, before):
    rows, d = xhat.shape
    merge = like((256, d), BF) if before else like((192, d), F32)
    return call(
        inner_kernel,
        "inner_norm",
        (1,),
        meta,
        (own, far, xhat, rstd, vectors, *att, *weights, *before),
        [fixed(rows, d)] * 3
        + [fixed(rows, 128), fixed(4, d)]
        + [fixed(192, rows)] * 2
        + [fixed(192, d)] * 2
        + ([fixed(192, d)] * 2 + [fixed(2, d)] * 3 if before else []),
        [fixed(rows, d), fixed(192, rows), fixed(192, rows), fixed(*merge.shape), fixed(*merge.shape), fixed(2, d)],
        [like((rows, d), F32), like((192, rows), BF), like((192, rows), BF), merge, merge, like((2, d), F32)],
        far=(0, 2, 3, 5, 6, 7, 8, *((9, 10) if before else ())),
        out=(1,),
        out_far=(0,) if before else (0, 3, 4),
    )


def fold_kernel(bits, meta_ref, *refs):
    for i in range(2):
        here, there = refs[2 * i : 2 * i + 2]
        if bits:
            send, keep = refs[4 + 2 * i : 6 + 2 * i]
            half = send.shape[0]
            bit = meta_ref[bits[i]]
            for part, j in ((send, 1 - bit), (keep, bit)):
                rows = pl.ds(pl.multiple_of(j * half, 16), half)
                part[...] = (here[rows, :].astype(F32) + there[rows, :].astype(F32)).astype(BF)
        else:
            refs[4 + i][...] = (here[...].astype(F32) + there[...].astype(F32)).astype(BF)


def fold(meta, pairs, bits, hold=()):
    args = [value for pair in pairs for value in pair]
    rows, d = args[0].shape
    shapes = [like((rows // 2, d), BF)] * 4 if bits else [like((rows, d), BF)] * 2
    return call(
        functools.partial(fold_kernel, bits),
        "fold",
        (1,),
        meta,
        args,
        [fixed(rows, d)] * 4,
        [fixed(*shape.shape) for shape in shapes],
        shapes,
        hold=hold,
    )


def local(groups, tokens, lengths, span_starts, wq, wk, wv, wm, wu, wd, ig, ib, og, ob, out_grad):
    rows, d = tokens.shape
    seqs = lengths.shape[0]
    frames = rows // seqs
    half = frames // 2
    core = lax.axis_index("tensor") % 2
    place_dp = lax.axis_index("dp")
    bits = groups.bit_length() - 1

    def swap(value, k):
        return lax.ppermute(value, "tensor", [(i, i ^ k) for i in range(4)])

    def swap_dp(value, k):
        return lax.ppermute(value, "dp", [(i, i ^ k) for i in range(groups)])

    def add(a, b):
        return (a.astype(F32) + b.astype(F32)).astype(BF)

    def total(pieces):
        return sum(piece.astype(F32) for piece in pieces).astype(BF) if len(pieces) > 1 else pieces[0]

    stages = [(0, 1)] + [(b, 2) for b in range(1, bits - 1, 2)] + ([(bits - 1, 1)] if bits % 2 == 0 else [])
    bit_orders = (list(range(bits)), [1, 0, *range(2, bits)])

    def spot_of(stage):
        return (place_dp >> stage[0]) & ((1 << stage[1]) - 1)

    class Chain:
        def __init__(self, part, order, cut_already=False):
            self.part = part.reshape((1,) * len(order) + part.shape) if cut_already else part
            self.order = order
            self.steps = [] if cut_already else [(True, stage) for stage in order]
            self.steps += [(False, stage) for stage in reversed(order)]

        def cut(self, stage, j):
            size = self.part.shape[0] >> stage[1]
            return lax.dynamic_slice_in_dim(self.part, (spot_of(stage) ^ j) * size, size, 0)

        def start(self):
            if self.steps:
                scatter, stage = self.steps[0]
                others = range(1, 1 << stage[1])
                self.pending = [swap_dp(self.cut(stage, j) if scatter else self.part, j << stage[0]) for j in others]

        def finish(self, *after):
            if not self.steps:
                return
            scatter, stage = self.steps.pop(0)
            got = self.pending
            if after:
                got = list(lax.optimization_barrier((*got, *after))[: len(got)])
            if scatter:
                state = total([self.cut(stage, 0)] + got)
                if not self.steps[0][0]:
                    state = state.reshape((1,) * len(self.order) + state.shape)
            else:
                axis = self.order.index(stage)
                spot = spot_of(stage)
                mine = self.part
                if len(got) == 1:
                    laid = [jnp.where(spot, got[0], mine), jnp.where(spot, mine, got[0])]
                    state = jnp.concatenate(laid, axis=axis)
                else:
                    state = jnp.zeros(mine.shape[:axis] + (1 + len(got),) + mine.shape[axis + 1 :], BF)
                    for j, piece in enumerate([mine] + got):
                        state = lax.dynamic_update_slice_in_dim(state, piece, spot ^ j, axis)
                if not self.steps:
                    state = state.reshape(-1, d)
            self.part = state

    def finish(group, *after):
        for chain in group:
            chain.finish(*after)

    def start(group):
        for chain in group:
            chain.start()

    def together(group):
        for chain, value in zip(group, lax.optimization_barrier(tuple(chain.part for chain in group))):
            chain.part = value

    all_bits = [((place_dp >> b) & 1).reshape(1) for b in range(bits)]
    scalars = jnp.concatenate([core.reshape(1), lengths, *all_bits])
    token = []

    def meta():
        return lax.optimization_barrier((scalars, *token))[0] if token else scalars

    def done(results, *others):
        token[:] = [results[0], *others]
        return results

    merge_w = (wm, swap(wm, 1), swap(wm, 2), swap(wm, 3))
    up_w = (wu, swap(wu, 1))
    down_w = (wd, swap(wd, 1))
    vectors = jnp.stack([ig, ib, og, ob])
    qkv_w = (wq.T, wk.T, wv.T)

    fwd, att, front, far = [], [], [], []
    qkv_of = [done(project(scalars, tokens, qkv_w, 0, frames))]
    for u in range(seqs):
        fwd.append(done(attend_forward(meta(), *qkv_of[u], u, frames), *(merge_w[1:] if u == 0 else far[u - 1][:1])))
        own, other = fwd[u][:2]
        att.append((own, swap(other, 1), swap(own, 2), swap(other, 3)))
        if u + 1 < seqs:
            qkv_of.append(done(project(meta(), tokens, qkv_w, u + 1, frames), up_w[1], down_w[1]))
        front.append(done(ahead(meta(), tokens, att[u], merge_w, up_w, down_w, vectors, u, 2 if u + 1 < seqs else 1)))
        far.append([swap(part, 2) for part in front[u][6:]])
    out_rows, back, far_grad, smalls, sums = [], [], [], [], ()
    for u in range(seqs):
        last = u == seqs - 1
        before = (front[u][2], front[u][3], *sums) if last else ()
        res = done(astern(meta(), front[u][5], far[u], out_grad, span_starts, up_w, down_w, front[u][4], vectors, u, before))
        out_rows.append(res[0])
        back.append(res[1 if last else 3])
        smalls.append(res[3 if last else 5])
        if last:
            sent, sums = res[2], res[4:]
        else:
            far_grad.append(swap(res[4], 2))
            sums = done(weight_grads(meta(), front[u][2], res[1], front[u][3], res[2], sums))

    def inner_step(u, before):
        res = done(inner_norm(meta(), back[u], far_grad[u], front[u][0], front[u][1], vectors, att[u][:2], merge_w[:2], before))
        return res, (res[1], swap(res[2], 1))

    def attend_step(u, grads):
        return done(attend_backward(meta(), *qkv_of[u], grads, fwd[u][:2], fwd[u][2], u, frames))

    def entry_step(u, grads, before):
        return done(entry_back(meta(), tokens, grads, qkv_w, before, u, frames))


    first_bit = 1 + seqs

    def scatter(step, pairs, after, hold=()):
        pairs = [tuple(lax.optimization_barrier((*pair, after))[:2]) for pair in pairs]
        if step == bits:
            return done(fold(meta(), pairs, (), hold))
        out = done(fold(meta(), pairs, tuple(first_bit + order[step] for order in bit_orders), hold))
        return [(out[2 * i + 1], swap_dp(out[2 * i], 1 << bit_orders[i][step])) for i in range(2)]

    inner, entry, so_far, near, crossed = [], [], (), [], []
    out_other = [swap(r, 1) for r in out_rows]

    def exchange(out):
        got = swap(out[0], 1)
        near.append((out[1], got))
        crossed.append(swap(total(near[-1]), 2))
        return got

    for u in range(seqs):
        last = u == seqs - 1
        if u == 0:
            up_own, up_other, down_own, down_other = lax.optimization_barrier((*sums, far_grad[0]))[:4]
            moving = [(down_own, swap(down_other, 1)), (up_own, swap(up_other, 1))]
            res, grads = inner_step(0, ())
            inner.append(res)
            far_grad.append(swap(lax.optimization_barrier((sent, res[0]))[0], 2))
            moving = scatter(0, moving, res[0])
        dqkv = attend_step(u, grads)
        if u == 0:
            token.extend(out_other)
        moving = scatter(1 + 2 * u, moving, dqkv[0])
        if not last:
            before = ()
            if u + 1 == seqs - 1:
                before = (inner[0][3], inner[0][4], inner[0][5], *smalls)
            res, grads = inner_step(u + 1, before)
            inner.append(res)
            moving = scatter(2, moving, res[0])
        else:
            for step in range(4, bits + 1):
                moving = scatter(step, moving, moving[0][0])
            first, second = (
                Chain(moving[i], [(b, 1) for b in order], True) for i, order in enumerate(bit_orders)
            )
            start([first, second])
            token.extend(crossed)
        out = entry_step(u, dqkv, so_far)
        entry.append(out)
        if not last:
            merge_got = swap(lax.optimization_barrier((res[4], out[0]))[0], 1)
            so_far = (out[2], res[3], merge_got)
            token.append(exchange(out))
    qkv = Chain(out[2], stages)
    qkv.start()

    got = exchange(out)
    layer_output = place(meta(), out_rows, out_other)

    finish([first, second], got)
    finish([qkv])
    together([qkv, first, second])
    start([qkv, first, second])
    finish([qkv, first, second], crossed[-1])
    together([qkv, first, second])
    start([qkv, first])
    ready = []
    for u in range(seqs):
        rest = near[u][0].astype(F32) + near[u][1].astype(F32) + crossed[u].astype(F32)
        ready.append((inner[u][0] + rest).astype(BF))
    input_grad = place(scalars, ready, [swap(r, 1) for r in ready])
    finish([qkv, first])
    together([qkv, first, second])
    start([qkv, second])
    finish([qkv, second], input_grad, layer_output)
    while qkv.steps or first.steps or second.steps:
        start([qkv, first, second])
        finish([qkv, first, second])
        together([qkv, first, second])
    down_sum, up_sum, joint = (chain.part for chain in (first, second, qkv))
    qkv_sum, merge_sum = joint[:576], joint[576:]
    small = merge_sum[192:196].astype(F32)
    query_grad, key_grad, value_grad = (qkv_sum[192 * i : 192 * (i + 1)].astype(F32).T for i in range(3))
    return (
        layer_output,
        input_grad,
        query_grad,
        key_grad,
        value_grad,
        merge_sum[:192].astype(F32),
        up_sum.astype(F32),
        down_sum.astype(F32),
        small[0],
        small[1],
        small[2],
        small[3],
    )


def solution(mesh):
    in_specs = (
        P("dp", None),
        P("dp"),
        P("dp", None),
        P(None, "tensor"),
        P(None, "tensor"),
        P(None, "tensor"),
        P("tensor", None),
        P(None, "tensor"),
        P("tensor", None),
        P(),
        P(),
        P(),
        P(),
        P("dp", None),
    )
    out_specs = (
        P("dp", None),
        P("dp", None),
        P(None, "tensor"),
        P(None, "tensor"),
        P(None, "tensor"),
        P("tensor", None),
        P(None, "tensor"),
        P("tensor", None),
        P(),
        P(),
        P(),
        P(),
    )
    body = functools.partial(local, mesh.shape["dp"])
    return jax.shard_map(body, mesh=mesh, in_specs=in_specs, out_specs=out_specs, check_vma=False)
```

```python
import functools

import jax
import jax.numpy as jnp
from jax import lax
from jax.experimental import pallas as pl
from jax.experimental.pallas import tpu as pltpu
from jax.sharding import PartitionSpec as P

HEAD_DIM = 64
SPAN = 10
EPS = 1e-05
LOG2E = 1.4426950408889634
KF = 1024
KB = 512
VMEM = 12
RB = 128
HB = 256
BF = jnp.bfloat16
F32 = jnp.float32
MIB = 1 << 20


def nn(a, b):
    return lax.dot_general(a, b, (((1,), (0,)), ((), ())), preferred_element_type=F32)


def nt(a, b):
    return lax.dot_general(a, b, (((1,), (1,)), ((), ())), preferred_element_type=F32)


def tn(a, b):
    return lax.dot_general(a, b, (((0,), (0,)), ((), ())), preferred_element_type=F32)


def params(limit):
    return pltpu.CompilerParams(vmem_limit_bytes=limit * MIB)


def cost(micros):
    return pl.CostEstimate(flops=int(micros * 1.1e9), bytes_accessed=1024, transcendentals=0)


MICROS = {"project": 3, "attend_forward": 8, "attend_backward": 12, "entry_back": 5, "place": 3, "ahead": 9, "astern": 10, "inner_norm": 3, "weight_grads": 4, "fold": 2}


def lane_parts(block):
    left = block[:, :128]
    lane = lax.broadcasted_iota(jnp.int32, left.shape, 1)
    zero = jnp.zeros_like(left)
    return (
        jnp.where(lane < HEAD_DIM, left, zero),
        jnp.where(lane >= HEAD_DIM, left, zero),
        block[:, 128:],
    )


TILE = (0, 0, 1)


def call(kernel, name, grid, meta, args, in_specs, out_specs, out_shape, scratch=(), limit=VMEM, hold=(), far=(), out=(), out_far=()):
    def place_input(i, value):
        space = pltpu.VMEM if i in hold else pltpu.HBM if i in far else None
        return value if space is None else pltpu.with_memory_space_constraint(value, space)

    def place_output(i, value):
        space = pltpu.VMEM if i in out else pltpu.HBM if i in out_far else None
        return value if space is None else space(value.shape, value.dtype)

    single = not isinstance(out_shape, list)
    return pl.pallas_call(
        kernel,
        grid_spec=pltpu.PrefetchScalarGridSpec(
            num_scalar_prefetch=1,
            grid=grid,
            in_specs=in_specs,
            out_specs=out_specs,
            scratch_shapes=scratch,
        ),
        out_shape=place_output(0, out_shape) if single else [place_output(i, o) for i, o in enumerate(out_shape)],
        compiler_params=params(limit),
        cost_estimate=cost(MICROS[name]),
        name=name,
    )(meta, *(place_input(i, value) for i, value in enumerate(args)))


def fixed(*shape):
    return pl.BlockSpec(shape, lambda *_: (0,) * len(shape))


def like(shape, dtype):
    return jax.ShapeDtypeStruct(shape, dtype)


def project_kernel(meta_ref, x_ref, wq_ref, wk_ref, wv_ref, q_ref, k_ref, v_ref):
    x = x_ref[...]
    for w_ref, o_ref in ((wq_ref, q_ref), (wk_ref, k_ref), (wv_ref, v_ref)):
        o_ref[:, :192] = nt(x, w_ref[...]).astype(BF)
        o_ref[:, 192:] = jnp.zeros((x.shape[0], HEAD_DIM), BF)


def project(meta, tokens, weights, u, frames):
    rows, d = frames, tokens.shape[1]
    block = 256
    return call(
        project_kernel,
        "project",
        (rows // block,),
        meta,
        (tokens, *weights),
        [pl.BlockSpec((block, d), lambda i, m: (u * (rows // block) + i, 0))] + [fixed(192, d)] * 3,
        [pl.BlockSpec((block, 256), lambda i, m: (i, 0))] * 3,
        [like((rows, 256), BF)] * 3,
        far=range(4),
        out=(0, 1, 2),
    )


def forward_kernel(u, meta_ref, q_ref, k_ref, v_ref, own_ref, other_ref, lse_ref, s_ref):
    length = meta_ref[1 + u]
    step = pl.program_id(0)
    blocks = lax.div(length + KF - 1, KF)
    parts = lane_parts(q_ref[...] * jnp.asarray(0.125, BF))
    width = q_ref.shape[0]

    def first(kb, highest):
        start = pl.multiple_of(kb * KF, KF)
        rows = pl.ds(start, KF)
        live = start + lax.broadcasted_iota(jnp.int32, (KF, width), 0) < length
        out = []
        for h in range(3):
            tile = pl.ds(128 * TILE[h], 128)
            s = nt(k_ref[rows, tile], parts[h])
            s = jnp.where(live, s, -1e30)
            s_ref[h, rows, :] = s
            out.append(jnp.maximum(highest[h], jnp.max(s, axis=0, keepdims=True)))
        return tuple(out)

    floor = jnp.full((1, width), -1e30, F32)
    highest = lax.fori_loop(0, blocks, first, (floor,) * 3)

    def second(kb, carry):
        rows = pl.ds(pl.multiple_of(kb * KF, KF), KF)
        out = []
        for h in range(3):
            total, result = carry[h]
            p = jnp.exp2((s_ref[h, rows, :] - highest[h]) * LOG2E)
            total = total + jnp.sum(p, axis=0, keepdims=True)
            v = v_ref[rows, pl.ds(128 * TILE[h], 128)]
            result = result + tn(v, p.astype(BF))
            out.append((total, result))
        return tuple(out)

    init = ((jnp.zeros((1, width), F32), jnp.zeros((128, width), F32)),) * 3
    done = lax.fori_loop(0, blocks, second, init)
    outs = []
    for h in range(3):
        total, result = done[h]
        lo = HEAD_DIM * (h % 2)
        o = result[lo : lo + HEAD_DIM] / total
        lse_ref[0, pl.ds(h, 1), :] = highest[h] * LOG2E + jnp.log2(total)
        outs.append(o.astype(BF))
    whole = jnp.concatenate(outs, axis=0)
    for j, o_ref in enumerate((own_ref, other_ref)):

        @pl.when(step == j)
        def _():
            o_ref[...] = whole


def attend_forward(meta, q, k, v, u, frames):
    half = frames // 2
    return call(
        functools.partial(forward_kernel, u),
        "attend_forward",
        (2,),
        meta,
        (q, k, v),
        [
            pl.BlockSpec((half, 256), lambda i, m: (i ^ m[0], 0)),
            fixed(frames, 256),
            fixed(frames, 256),
        ],
        [
            fixed(192, half),
            fixed(192, half),
            pl.BlockSpec((1, 8, half), lambda i, m: (i, 0, 0)),
        ],
        [
            like((192, half), BF),
            like((192, half), BF),
            like((2, 8, half), F32),
        ],
        [pltpu.VMEM((3, frames, half), F32)],
        hold=(0, 1, 2),
    )


def backward_kernel(
    u, meta_ref, q_ref, k_ref, v_ref, d0_ref, d1_ref, o0_ref, o1_ref, lse_ref,
    dq_ref, dk_ref, dv_ref, kt_ref, dk_acc, dv_acc, do_ref, o_ref,
):
    length = meta_ref[1 + u]
    blocks = lax.div(length + KB - 1, KB)
    step = pl.program_id(0)

    @pl.when(step == 0)
    def _():
        dk_acc[...] = jnp.zeros_like(dk_acc)
        dv_acc[...] = jnp.zeros_like(dv_acc)
        kt_ref[...] = jnp.transpose(k_ref[...])
        do_ref[...] = d0_ref[...]
        o_ref[...] = o0_ref[...]

    @pl.when(step == 1)
    def _():
        do_ref[...] = d1_ref[...]
        o_ref[...] = o1_ref[...]

    parts = lane_parts(q_ref[...] * jnp.asarray(0.125, BF))
    width = q_ref.shape[0]
    empty = jnp.zeros((HEAD_DIM, width), BF)
    head = [do_ref[pl.ds(h * HEAD_DIM, HEAD_DIM), :] for h in range(3)]
    grads = (
        jnp.concatenate([head[0], empty], axis=0),
        jnp.concatenate([empty, head[1]], axis=0),
        jnp.concatenate([head[2], empty], axis=0),
    )
    delta = [
        jnp.sum(
            head[h].astype(F32) * o_ref[pl.ds(h * HEAD_DIM, HEAD_DIM), :].astype(F32), axis=0, keepdims=True
        )
        for h in range(3)
    ]
    lse = [lse_ref[0, pl.ds(h, 1), :] for h in range(3)]

    def body(kb, carry):
        start = pl.multiple_of(kb * KB, KB)
        rows = pl.ds(start, KB)
        live = start + lax.broadcasted_iota(jnp.int32, (KB, width), 0) < length
        out = []
        for h in range(3):
            tile = pl.ds(128 * TILE[h], 128)
            s = nt(k_ref[rows, tile], parts[h])
            s = jnp.where(live, s, -1e30)
            p = jnp.exp2(s * LOG2E - lse[h])
            dp = nn(v_ref[rows, tile], grads[h])
            ds = (p * (dp - delta[h])).astype(BF)
            dv_acc[rows, tile] += nt(p.astype(BF), grads[h])
            dk_acc[rows, tile] += nn(ds, parts[h])
            kt = kt_ref[pl.ds(h * HEAD_DIM, HEAD_DIM), rows]
            out.append(carry[h] + nn(kt, ds))
        return tuple(out)

    zero = jnp.zeros((HEAD_DIM, width), F32)
    done = lax.fori_loop(0, blocks, body, (zero,) * 3)
    full = jnp.concatenate(done + (zero,), axis=0) * 0.125
    dq_ref[...] = jnp.transpose(full).astype(BF)

    @pl.when(step == 1)
    def _():
        dk_ref[...] = dk_acc[...].astype(BF)
        dv_ref[...] = dv_acc[...].astype(BF)


def attend_backward(meta, q, k, v, grads, outs, lse, u, frames):
    half = frames // 2
    return call(
        functools.partial(backward_kernel, u),
        "attend_backward",
        (2,),
        meta,
        (q, k, v, *grads, *outs, lse),
        [
            pl.BlockSpec((half, 256), lambda i, m: (i ^ m[0], 0)),
            fixed(frames, 256),
            fixed(frames, 256),
            fixed(192, half),
            fixed(192, half),
            fixed(192, half),
            fixed(192, half),
            pl.BlockSpec((1, 8, half), lambda i, m: (i, 0, 0)),
        ],
        [
            pl.BlockSpec((half, 256), lambda i, m: (i ^ m[0], 0)),
            fixed(frames, 256),
            fixed(frames, 256),
        ],
        [like((frames, 256), BF)] * 3,
        [
            pltpu.VMEM((256, frames), BF),
            pltpu.VMEM((frames, 256), F32),
            pltpu.VMEM((frames, 256), F32),
            pltpu.VMEM((192, half), BF),
            pltpu.VMEM((192, half), BF),
        ],
        hold=(3,),
        far=(0, 1, 2),
        out=(0, 1, 2),
    )


def entry_kernel(meta_ref, x_ref, dq_ref, dk_ref, dv_ref, wq_ref, wk_ref, wv_ref, *refs):
    last = len(refs) == 7
    before_ref = refs[0] if last else None
    send_ref, keep_ref, sum_ref, acc = refs[-4:]
    step = pl.program_id(0)
    x = x_ref[...]
    total = jnp.zeros(x.shape, F32)
    for i, (g_ref, w_ref) in enumerate(((dq_ref, wq_ref), (dk_ref, wk_ref), (dv_ref, wv_ref))):
        rows = pl.ds(192 * i, 192)
        g = g_ref[:, :192]
        total = total + nn(g, w_ref[...])
        product = tn(g, x)

        @pl.when(step == 0)
        def _():
            acc[rows, :] = product if before_ref is None else product + before_ref[rows, :]

        @pl.when(step == 1)
        def _():
            sum_ref[rows, :] = (product + acc[rows, :]).astype(sum_ref.dtype)

    low = total.astype(BF)

    @pl.when(step == 0)
    def _():
        send_ref[...] = low
        if last:
            merged = refs[1][...].astype(F32) + refs[2][...].astype(F32)
            sum_ref[576:, :] = merged.astype(sum_ref.dtype)

    @pl.when(step == 1)
    def _():
        keep_ref[...] = low


def entry_back(meta, tokens, grads, weights, before, u, frames):
    half = frames // 2
    d = tokens.shape[1]
    rows, dtype = (832, BF) if before else (576, F32)
    return call(
        entry_kernel,
        "entry_back",
        (2,),
        meta,
        (tokens, *grads, *weights, *before),
        [pl.BlockSpec((half, d), lambda i, m: (u * 2 + (1 - i ^ m[0]), 0))]
        + [pl.BlockSpec((half, 256), lambda i, m: (1 - i ^ m[0], 0))] * 3
        + [fixed(192, d)] * 3
        + [fixed(*value.shape) for value in before],
        [fixed(half, d), fixed(half, d), fixed(rows, d)],
        [like((half, d), BF), like((half, d), BF), like((rows, d), dtype)],
        [pltpu.VMEM((576, d), F32)],
        hold=(1, 2, 3),
        far=(0, 4, 5, 6),
    )


def place_kernel(meta_ref, *refs):
    o_ref = refs[-1]
    for j in range(2):

        @pl.when(pl.program_id(0) % 2 == j)
        def _():
            if len(refs) == 3:
                o_ref[...] = refs[j][...]
            else:
                count = (len(refs) - 1) // 2
                for u in range(count):

                    @pl.when(pl.program_id(0) // 2 == u)
                    def _():
                        o_ref[...] = refs[j * count + u][...]


def place(meta, own, other, half):
    d = own[0].shape[1]
    count = 2 * sum(block.shape[0] for block in own) // half
    one = len(own) == 1
    spec = pl.BlockSpec((half, d), lambda i, m: (i // 2 if one else 0, 0))
    return call(
        place_kernel,
        "place",
        (count,),
        meta,
        (*own, *other),
        [spec] * (2 * len(own)),
        pl.BlockSpec((half, d), lambda i, m: (i ^ m[0], 0)),
        like((count * half, d), own[0].dtype),
    )


def normalise(values):
    average = jnp.mean(values, axis=-1, keepdims=True)
    centred = values - average
    spread = jnp.mean(centred * centred, axis=-1, keepdims=True)
    rstd = lax.rsqrt(spread + EPS)
    return centred * rstd, rstd


def gelu_pair(v):
    e = jnp.exp2(v * v * (-0.5 * LOG2E))
    t = 1.0 / (1.0 + (0.3275911 * 0.7071067811865476) * jnp.abs(v))
    poly = t * (0.5 * 0.254829592 + t * (0.5 * -0.284496736 + t * (0.5 * 1.421413741 + t * (0.5 * -1.453152027 + t * (0.5 * 1.061405429)))))
    tail = poly * e
    phi_cap = jnp.where(v >= 0, 1.0 - tail, tail)
    return v * phi_cap, phi_cap + v * (e * 0.3989422804014327)


def ahead_kernel(
    meta_ref, tok_ref, a0, a1, a2, a3, w0, w1, w2, w3, ua_ref, ub_ref, da_ref, db_ref, vec_ref,
    xhat_ref, rstd_ref, low_ref, act_ref, slope_ref, own_ref, sent_ref,
):
    gain, bias = vec_ref[0:1, :], vec_ref[1:2, :]
    hidden = ua_ref.shape[1]
    for r in range(tok_ref.shape[0] // RB):
        rows = pl.ds(r * RB, RB)
        branch = jnp.zeros((RB, tok_ref.shape[1]), F32)
        for a, w in ((a0, w0), (a1, w1), (a2, w2), (a3, w3)):
            branch = branch + tn(a[:, rows], w[...]).astype(BF).astype(F32)
        xhat, rstd = normalise(tok_ref[rows, :].astype(F32) + branch)
        xhat_ref[rows, :] = xhat
        rstd_ref[rows, :] = jnp.broadcast_to(rstd, (RB, rstd_ref.shape[1]))
        normed = xhat * gain + bias
        low = normed.astype(BF)
        low_ref[rows, :] = low
        sent = jnp.zeros(normed.shape, F32)
        for g, (up, down) in enumerate(((ua_ref, da_ref), (ub_ref, db_ref))):
            acts = []
            for c in range(hidden // HB):
                act, slope = gelu_pair(nn(low, up[:, c * HB : (c + 1) * HB]))
                columns = pl.ds(g * hidden + c * HB, HB)
                acts.append(act.astype(BF))
                act_ref[rows, columns] = acts[-1]
                slope_ref[rows, columns] = slope.astype(BF)
            sent = sent + nn(jnp.concatenate(acts, axis=1), down[...]).astype(BF).astype(F32)
        own_ref[rows, :] = normed + sent
        sent_ref[rows, :] = sent.astype(BF)


def ahead(meta, tokens, att, merge_w, up, down, vectors, u):
    half = att[0].shape[1]
    d, hidden = up[0].shape
    return call(
        ahead_kernel,
        "ahead",
        (1,),
        meta,
        (tokens, *att, *merge_w, *up, *down, vectors),
        [pl.BlockSpec((half, d), lambda i, m: (u * 2 + m[0], 0))]
        + [fixed(192, half)] * 4
        + [fixed(192, d)] * 4
        + [fixed(d, hidden)] * 2
        + [fixed(hidden, d)] * 2
        + [fixed(4, d)],
        [fixed(half, d), fixed(half, 128), fixed(half, d), fixed(half, 2 * hidden), fixed(half, 2 * hidden), fixed(half, d), fixed(half, d)],
        [
            like((half, d), F32),
            like((half, 128), F32),
            like((half, d), BF),
            like((half, 2 * hidden), BF),
            like((half, 2 * hidden), BF),
            like((half, d), F32),
            like((half, d), BF),
        ],
        far=(0,),
        out=(2, 3, 4, 5),
        out_far=(0, 1),
    )


def astern_kernel(u, meta_ref, own_ref, far_ref, grad_ref, span_ref, ua_ref, ub_ref, da_ref, db_ref, slope_ref, vec_ref, *refs):
    last = len(refs) > 6
    if last:
        before = refs[:-10]
        out_ref, back_ref, sent_ref, small_ref, *sums, g_ref, pre_ref = refs[-10:]
    else:
        out_ref, g_ref, pre_ref, back_ref, sent_ref, small_ref = refs
    gain, bias = vec_ref[2:3, :], vec_ref[3:4, :]
    half, d = own_ref.shape
    hidden = ua_ref.shape[1]
    starts = span_ref[u : u + 1, :]
    gain_grad = jnp.zeros(gain.shape, F32)
    bias_grad = jnp.zeros(gain.shape, F32)
    for r in range(half // RB):
        rows = pl.ds(r * RB, RB)
        xhat, rstd = normalise(own_ref[rows, :] + far_ref[rows, :].astype(F32))
        out_ref[rows, :] = (xhat * gain + bias).astype(BF)
        frame = meta_ref[0] * half + r * RB + lax.broadcasted_iota(jnp.int32, (RB, starts.shape[1]), 0)
        inside = (frame >= starts) & (frame < starts + SPAN)
        weight = jnp.max(jnp.where(inside, 1.0, 0.0), axis=1, keepdims=True)
        cot = grad_ref[rows, :].astype(F32) * weight
        gain_grad = gain_grad + jnp.sum(cot * xhat, axis=0, keepdims=True)
        bias_grad = bias_grad + jnp.sum(cot, axis=0, keepdims=True)
        gy = cot * gain
        mean_gy = jnp.mean(gy, axis=-1, keepdims=True)
        mean_gx = jnp.mean(gy * xhat, axis=-1, keepdims=True)
        sum_grad = rstd * (gy - mean_gy - xhat * mean_gx)
        low = sum_grad.astype(BF)
        g_ref[rows, :] = low
        sent = jnp.zeros(sum_grad.shape, F32)
        for g, (up, down) in enumerate(((ua_ref, da_ref), (ub_ref, db_ref))):
            pres = []
            for c in range(hidden // HB):
                columns = pl.ds(g * hidden + c * HB, HB)
                slope = slope_ref[rows, columns].astype(F32)
                pres.append((nt(low, down[c * HB : (c + 1) * HB, :]) * slope).astype(BF))
                pre_ref[rows, columns] = pres[-1]
            sent = sent + nt(jnp.concatenate(pres, axis=1), up[...]).astype(BF).astype(F32)
        back_ref[rows, :] = sum_grad + sent
        sent_ref[rows, :] = sent.astype(BF)
    small_ref[0:1, :] = gain_grad
    small_ref[1:2, :] = bias_grad
    if last:
        x_ref, act_ref = before[:2]
        weight_sums(x_ref[...], g_ref[...], act_ref, pre_ref, before[2:], sums)


def astern(meta, own, far, grad, spans, up, down, slope, vectors, u, before):
    half, d = own.shape
    hidden = up[0].shape[1]
    rows = fixed(half, d)
    wide = fixed(half, 2 * hidden)
    grads = [] if not before else [(d, hidden)] * 2 + [(hidden, d)] * 2
    extra = [] if not before else [rows, wide] + [fixed(*shape) for shape in grads[: len(before) - 2]]
    made = [like((half, d), BF), like((half, 2 * hidden), BF)]
    others = [like((half, d), F32), like((half, d), BF), like((2, d), F32)]
    shapes = [like((half, d), BF)] + ([] if before else made) + others + [like(shape, BF) for shape in grads]
    return call(
        functools.partial(astern_kernel, u),
        "astern",
        (1,),
        meta,
        (own, far, grad, spans, *up, *down, slope, vectors, *before),
        [rows] * 2
        + [pl.BlockSpec((half, d), lambda i, m: (u * 2 + m[0], 0)), fixed(*spans.shape)]
        + [fixed(d, hidden)] * 2
        + [fixed(hidden, d)] * 2
        + [wide, fixed(4, d)]
        + extra,
        [fixed(*shape.shape) for shape in shapes],
        shapes,
        [pltpu.VMEM(shape.shape, shape.dtype) for shape in made] if before else (),
        limit=20 if before else VMEM,
        hold=(0, 8, *range(10, 10 + len(before))),
        far=(2,),
        out=() if before else (1, 2),
        out_far=(0, 1) if before else (0, 3),
    )


def weight_kernel(meta_ref, x_ref, g_ref, act_ref, pre_ref, *refs):
    before, sums = refs[:-4], refs[-4:]
    weight_sums(x_ref[...], g_ref[...], act_ref, pre_ref, before, sums)


def weight_sums(x, g, act_ref, pre_ref, before, sums):
    hidden = act_ref.shape[1] // 2
    for i in range(2):
        for c in range(hidden // HB):
            columns = pl.ds(i * hidden + c * HB, HB)
            block = pl.ds(c * HB, HB)
            up = tn(x, pre_ref[:, columns])
            down = tn(act_ref[:, columns], g)
            if before:
                up = up + before[i][:, block].astype(F32)
                down = down + before[2 + i][block, :].astype(F32)
            sums[i][:, block] = up.astype(BF)
            sums[2 + i][block, :] = down.astype(BF)


def weight_grads(meta, x, g, act, pre, before):
    rows, d = x.shape
    hidden = act.shape[1] // 2
    shapes = [(d, hidden)] * 2 + [(hidden, d)] * 2
    return call(
        weight_kernel,
        "weight_grads",
        (1,),
        meta,
        (x, g, act, pre, *before),
        [fixed(rows, d)] * 2 + [fixed(rows, 2 * hidden)] * 2 + [fixed(*shape) for shape in shapes[: len(before)]],
        [fixed(*shape) for shape in shapes],
        [like(shape, BF) for shape in shapes],
        hold=(0, 1, 2, 3),
        out=(0, 1, 2, 3),
    )


def inner_kernel(meta_ref, own_ref, far_ref, xhat_ref, rstd_ref, vec_ref, a0, a1, w0, w1, *refs):
    last = len(refs) == 11
    out_ref, g0, g1, m0, m1, small_ref = refs[-6:]
    grad = own_ref[...] + far_ref[...].astype(F32)
    xhat = xhat_ref[...]
    gain_grad = jnp.sum(grad * xhat, axis=0, keepdims=True)
    bias_grad = jnp.sum(grad, axis=0, keepdims=True)
    gy = grad * vec_ref[0:1, :]
    mean_gy = jnp.mean(gy, axis=-1, keepdims=True)
    mean_gx = jnp.mean(gy * xhat, axis=-1, keepdims=True)
    inner = rstd_ref[:, 0:1] * (gy - mean_gy - xhat * mean_gx)
    out_ref[...] = inner
    low = inner.astype(BF)
    g0[...] = nt(w0[...], low).astype(BF)
    g1[...] = nt(w1[...], low).astype(BF)
    small = jnp.concatenate([gain_grad, bias_grad], axis=0)
    small_ref[...] = small
    if last:
        before0, before1, before_small, outer0, outer1 = refs[:5]
        below = jnp.concatenate(
            [small + before_small[...], outer0[...] + outer1[...], jnp.zeros((60, small.shape[1]), F32)], axis=0
        ).astype(BF)
        for m, a, before in ((m0, a0, before0), (m1, a1, before1)):
            m[:192, :] = (nn(a[...], low) + before[...]).astype(BF)
            m[192:, :] = below
    else:
        m0[...] = nn(a0[...], low)
        m1[...] = nn(a1[...], low)


def inner_norm(meta, own, far, xhat, rstd, vectors, att, weights, before):
    rows, d = xhat.shape
    merge = like((256, d), BF) if before else like((192, d), F32)
    return call(
        inner_kernel,
        "inner_norm",
        (1,),
        meta,
        (own, far, xhat, rstd, vectors, *att, *weights, *before),
        [fixed(rows, d)] * 3
        + [fixed(rows, 128), fixed(4, d)]
        + [fixed(192, rows)] * 2
        + [fixed(192, d)] * 2
        + ([fixed(192, d)] * 2 + [fixed(2, d)] * 3 if before else []),
        [fixed(rows, d), fixed(192, rows), fixed(192, rows), fixed(*merge.shape), fixed(*merge.shape), fixed(2, d)],
        [like((rows, d), F32), like((192, rows), BF), like((192, rows), BF), merge, merge, like((2, d), F32)],
        far=(0, 2, 3, 5, 6, 7, 8, *((9, 10) if before else ())),
        out=(1,),
        out_far=(0,) if before else (0, 3, 4),
    )


def fold_kernel(bits, meta_ref, *refs):
    for i in range(2):
        here, there = refs[2 * i : 2 * i + 2]
        if bits:
            send, keep = refs[4 + 2 * i : 6 + 2 * i]
            half = send.shape[0]
            bit = meta_ref[bits[i]]
            for part, j in ((send, 1 - bit), (keep, bit)):
                rows = pl.ds(pl.multiple_of(j * half, 16), half)
                part[...] = (here[rows, :].astype(F32) + there[rows, :].astype(F32)).astype(BF)
        else:
            refs[4 + i][...] = (here[...].astype(F32) + there[...].astype(F32)).astype(BF)


def fold(meta, pairs, bits, hold=()):
    args = [value for pair in pairs for value in pair]
    rows, d = args[0].shape
    shapes = [like((rows // 2, d), BF)] * 4 if bits else [like((rows, d), BF)] * 2
    return call(
        functools.partial(fold_kernel, bits),
        "fold",
        (1,),
        meta,
        args,
        [fixed(rows, d)] * 4,
        [fixed(*shape.shape) for shape in shapes],
        shapes,
        hold=hold,
    )


def local(groups, tokens, lengths, span_starts, wq, wk, wv, wm, wu, wd, ig, ib, og, ob, out_grad):
    rows, d = tokens.shape
    seqs = lengths.shape[0]
    frames = rows // seqs
    half = frames // 2
    core = lax.axis_index("tensor") % 2
    place_dp = lax.axis_index("dp")
    bits = groups.bit_length() - 1

    def swap(value, k):
        return lax.ppermute(value, "tensor", [(i, i ^ k) for i in range(4)])

    def swap_dp(value, k):
        return lax.ppermute(value, "dp", [(i, i ^ k) for i in range(groups)])

    def add(a, b):
        return (a.astype(F32) + b.astype(F32)).astype(BF)

    def total(pieces):
        return sum(piece.astype(F32) for piece in pieces).astype(BF) if len(pieces) > 1 else pieces[0]

    stages = [(0, 1)] + [(b, 2) for b in range(1, bits - 1, 2)] + ([(bits - 1, 1)] if bits % 2 == 0 else [])
    bit_orders = (list(range(bits)), [1, 0, *range(2, bits)])

    def spot_of(stage):
        return (place_dp >> stage[0]) & ((1 << stage[1]) - 1)

    class Chain:
        def __init__(self, part, order, cut_already=False):
            self.part = part.reshape((1,) * len(order) + part.shape) if cut_already else part
            self.order = order
            self.steps = [] if cut_already else [(True, stage) for stage in order]
            self.steps += [(False, stage) for stage in reversed(order)]

        def cut(self, stage, j):
            size = self.part.shape[0] >> stage[1]
            return lax.dynamic_slice_in_dim(self.part, (spot_of(stage) ^ j) * size, size, 0)

        def start(self):
            if self.steps:
                scatter, stage = self.steps[0]
                others = range(1, 1 << stage[1])
                self.pending = [swap_dp(self.cut(stage, j) if scatter else self.part, j << stage[0]) for j in others]

        def finish(self, *after):
            if not self.steps:
                return
            scatter, stage = self.steps.pop(0)
            got = self.pending
            if after:
                got = list(lax.optimization_barrier((*got, *after))[: len(got)])
            if scatter:
                state = total([self.cut(stage, 0)] + got)
                if not self.steps[0][0]:
                    state = state.reshape((1,) * len(self.order) + state.shape)
            else:
                axis = self.order.index(stage)
                spot = spot_of(stage)
                mine = self.part
                if len(got) == 1:
                    laid = [jnp.where(spot, got[0], mine), jnp.where(spot, mine, got[0])]
                    state = jnp.concatenate(laid, axis=axis)
                else:
                    state = jnp.zeros(mine.shape[:axis] + (1 + len(got),) + mine.shape[axis + 1 :], BF)
                    for j, piece in enumerate([mine] + got):
                        state = lax.dynamic_update_slice_in_dim(state, piece, spot ^ j, axis)
                if not self.steps:
                    state = state.reshape(-1, d)
            self.part = state

    def finish(group, *after):
        for chain in group:
            chain.finish(*after)

    def start(group):
        for chain in group:
            chain.start()

    def together(group):
        for chain, value in zip(group, lax.optimization_barrier(tuple(chain.part for chain in group))):
            chain.part = value

    all_bits = [((place_dp >> b) & 1).reshape(1) for b in range(bits)]
    scalars = jnp.concatenate([core.reshape(1), lengths, *all_bits])
    token = []

    def meta():
        return lax.optimization_barrier((scalars, *token))[0] if token else scalars

    def done(results, *others):
        token[:] = [results[0], *others]
        return results

    merge_w = (wm, swap(wm, 1), swap(wm, 2), swap(wm, 3))
    up_w = (wu, swap(wu, 1))
    down_w = (wd, swap(wd, 1))
    vectors = jnp.stack([ig, ib, og, ob])
    qkv_w = (wq.T, wk.T, wv.T)

    fwd, att, front, far = [], [], [], []
    qkv_of = [done(project(scalars, tokens, qkv_w, 0, frames))]
    for u in range(seqs):
        fwd.append(done(attend_forward(meta(), *qkv_of[u], u, frames), *(merge_w[1:] if u == 0 else ())))
        own, other = fwd[u][:2]
        att.append((own, swap(other, 1), swap(own, 2), swap(other, 3)))
        if u + 1 < seqs:
            qkv_of.append(done(project(meta(), tokens, qkv_w, u + 1, frames), up_w[1], down_w[1]))
    for u in range(seqs):
        front.append(done(ahead(meta(), tokens, att[u], merge_w, up_w, down_w, vectors, u)))
        far.append(swap(front[u][6], 2))
    out_rows, back, far_grad, smalls, sums = [], [], [], [], ()
    for u in range(seqs):
        last = u == seqs - 1
        before = (front[u][2], front[u][3], *sums) if last else ()
        res = done(astern(meta(), front[u][5], far[u], out_grad, span_starts, up_w, down_w, front[u][4], vectors, u, before))
        out_rows.append(res[0])
        back.append(res[1 if last else 3])
        smalls.append(res[3 if last else 5])
        if last:
            sent, sums = res[2], res[4:]
        else:
            far_grad.append(swap(res[4], 2))
            sums = done(weight_grads(meta(), front[u][2], res[1], front[u][3], res[2], sums))

    def inner_step(u, before):
        res = done(inner_norm(meta(), back[u], far_grad[u], front[u][0], front[u][1], vectors, att[u][:2], merge_w[:2], before))
        return res, (res[1], swap(res[2], 1))

    def attend_step(u, grads):
        return done(attend_backward(meta(), *qkv_of[u], grads, fwd[u][:2], fwd[u][2], u, frames))

    def entry_step(u, grads, before):
        return done(entry_back(meta(), tokens, grads, qkv_w, before, u, frames))


    first_bit = 1 + seqs

    def scatter(step, pairs, after, hold=()):
        pairs = [tuple(lax.optimization_barrier((*pair, after))[:2]) for pair in pairs]
        if step == bits:
            return done(fold(meta(), pairs, (), hold))
        out = done(fold(meta(), pairs, tuple(first_bit + order[step] for order in bit_orders), hold))
        return [(out[2 * i + 1], swap_dp(out[2 * i], 1 << bit_orders[i][step])) for i in range(2)]

    inner, so_far, near = [], (), []
    out_other = [swap(r, 1) for r in out_rows]

    for u in range(seqs):
        last = u == seqs - 1
        if u == 0:
            up_own, up_other, down_own, down_other = lax.optimization_barrier((*sums, far_grad[0]))[:4]
            moving = [(down_own, swap(down_other, 1)), (up_own, swap(up_other, 1))]
            res, grads = inner_step(0, ())
            inner.append(res)
            far_grad.append(swap(lax.optimization_barrier((sent, res[0]))[0], 2))
            moving = scatter(0, moving, res[0])
        dqkv = attend_step(u, grads)
        moving = scatter(1 + 2 * u, moving, dqkv[0])
        if not last:
            before = ()
            if u + 1 == seqs - 1:
                before = (inner[0][3], inner[0][4], inner[0][5], *smalls)
            res, grads = inner_step(u + 1, before)
            inner.append(res)
        else:
            for step in range(4, bits + 1):
                moving = scatter(step, moving, moving[0][0])
            first, second = (
                Chain(moving[i], [(b, 1) for b in order], True) for i, order in enumerate(bit_orders)
            )
            start([first, second])
            token.extend(out_other)
        out = entry_step(u, dqkv, so_far)
        near.append((out[1], swap(out[0], 1)))
        if not last:
            merge_got = swap(lax.optimization_barrier((res[4], out[0]))[0], 1)
            so_far = (out[2], res[3], merge_got)
            moving = scatter(2, moving, out[0])
    qkv = Chain(out[2], stages)
    qkv.start()

    layer_output = place(meta(), out_rows, out_other, half)

    here = jnp.concatenate([total(pair) for pair in near], axis=0)
    crossed = swap(here, 2)
    finish([first, second], near[-1][1])
    finish([qkv])
    together([qkv, first, second])
    start([qkv, first, second])
    finish([qkv, first, second])
    together([qkv, first, second])
    start([qkv, first])
    finish([qkv, first])
    together([qkv, first, second])
    start([qkv, second])
    crossed = lax.optimization_barrier((crossed, qkv.part))[0]
    rest = jnp.concatenate([pair[0].astype(F32) + pair[1].astype(F32) for pair in near], axis=0)
    ready = (jnp.concatenate([res[0] for res in inner], axis=0) + (rest + crossed.astype(F32))).astype(BF)
    input_grad = place(scalars, [ready], [swap(ready, 1)], half)
    finish([qkv, second], input_grad, layer_output)
    while qkv.steps or first.steps or second.steps:
        start([qkv, first, second])
        finish([qkv, first, second])
        together([qkv, first, second])
    down_sum, up_sum, joint = (chain.part for chain in (first, second, qkv))
    qkv_sum, merge_sum = joint[:576], joint[576:]
    small = merge_sum[192:196].astype(F32)
    query_grad, key_grad, value_grad = (qkv_sum[192 * i : 192 * (i + 1)].astype(F32).T for i in range(3))
    return (
        layer_output,
        input_grad,
        query_grad,
        key_grad,
        value_grad,
        merge_sum[:192].astype(F32),
        up_sum.astype(F32),
        down_sum.astype(F32),
        small[0],
        small[1],
        small[2],
        small[3],
    )


def solution(mesh):
    in_specs = (
        P("dp", None),
        P("dp"),
        P("dp", None),
        P(None, "tensor"),
        P(None, "tensor"),
        P(None, "tensor"),
        P("tensor", None),
        P(None, "tensor"),
        P("tensor", None),
        P(),
        P(),
        P(),
        P(),
        P("dp", None),
    )
    out_specs = (
        P("dp", None),
        P("dp", None),
        P(None, "tensor"),
        P(None, "tensor"),
        P(None, "tensor"),
        P("tensor", None),
        P(None, "tensor"),
        P("tensor", None),
        P(),
        P(),
        P(),
        P(),
    )
    body = functools.partial(local, mesh.shape["dp"])
    return jax.shard_map(body, mesh=mesh, in_specs=in_specs, out_specs=out_specs, check_vma=False)
```

```python
import functools

import jax
import jax.numpy as jnp
from jax import lax
from jax.experimental import pallas as pl
from jax.experimental.pallas import tpu as pltpu
from jax.sharding import PartitionSpec as P

HEAD_DIM = 64
SPAN = 10
EPS = 1e-05
LOG2E = 1.4426950408889634
KF = 1024
KB = 512
VMEM = 12
RB = 128
HB = 256
BF = jnp.bfloat16
F32 = jnp.float32
MIB = 1 << 20


def nn(a, b):
    return lax.dot_general(a, b, (((1,), (0,)), ((), ())), preferred_element_type=F32)


def nt(a, b):
    return lax.dot_general(a, b, (((1,), (1,)), ((), ())), preferred_element_type=F32)


def tn(a, b):
    return lax.dot_general(a, b, (((0,), (0,)), ((), ())), preferred_element_type=F32)


def params(limit):
    return pltpu.CompilerParams(vmem_limit_bytes=limit * MIB)


def cost(micros):
    return pl.CostEstimate(flops=int(micros * 1.1e9), bytes_accessed=1024, transcendentals=0)


MICROS = {"project": 3, "attend_forward": 8, "attend_backward": 12, "entry_back": 5, "place": 3, "ahead": 9, "astern": 10, "inner_norm": 3, "weight_grads": 4, "fold": 2}


def lane_parts(block):
    left = block[:, :128]
    lane = lax.broadcasted_iota(jnp.int32, left.shape, 1)
    zero = jnp.zeros_like(left)
    return (
        jnp.where(lane < HEAD_DIM, left, zero),
        jnp.where(lane >= HEAD_DIM, left, zero),
        block[:, 128:],
    )


TILE = (0, 0, 1)


def call(kernel, name, grid, meta, args, in_specs, out_specs, out_shape, scratch=(), limit=VMEM, hold=(), far=(), out=(), out_far=()):
    def place_input(i, value):
        space = pltpu.VMEM if i in hold else pltpu.HBM if i in far else None
        return value if space is None else pltpu.with_memory_space_constraint(value, space)

    def place_output(i, value):
        space = pltpu.VMEM if i in out else pltpu.HBM if i in out_far else None
        return value if space is None else space(value.shape, value.dtype)

    single = not isinstance(out_shape, list)
    return pl.pallas_call(
        kernel,
        grid_spec=pltpu.PrefetchScalarGridSpec(
            num_scalar_prefetch=1,
            grid=grid,
            in_specs=in_specs,
            out_specs=out_specs,
            scratch_shapes=scratch,
        ),
        out_shape=place_output(0, out_shape) if single else [place_output(i, o) for i, o in enumerate(out_shape)],
        compiler_params=params(limit),
        cost_estimate=cost(MICROS[name]),
        name=name,
    )(meta, *(place_input(i, value) for i, value in enumerate(args)))


def fixed(*shape):
    return pl.BlockSpec(shape, lambda *_: (0,) * len(shape))


def like(shape, dtype):
    return jax.ShapeDtypeStruct(shape, dtype)


def project_kernel(meta_ref, x_ref, wq_ref, wk_ref, wv_ref, q_ref, k_ref, v_ref):
    x = x_ref[...]
    for w_ref, o_ref in ((wq_ref, q_ref), (wk_ref, k_ref), (wv_ref, v_ref)):
        o_ref[:, :192] = nt(x, w_ref[...]).astype(BF)
        o_ref[:, 192:] = jnp.zeros((x.shape[0], HEAD_DIM), BF)


def project(meta, tokens, weights, u, frames):
    rows, d = frames, tokens.shape[1]
    block = 256
    return call(
        project_kernel,
        "project",
        (rows // block,),
        meta,
        (tokens, *weights),
        [pl.BlockSpec((block, d), lambda i, m: (u * (rows // block) + i, 0))] + [fixed(192, d)] * 3,
        [pl.BlockSpec((block, 256), lambda i, m: (i, 0))] * 3,
        [like((rows, 256), BF)] * 3,
        far=range(4),
        out_far=(0, 1, 2),
    )


def forward_kernel(u, meta_ref, q_ref, k_ref, v_ref, own_ref, other_ref, lse_ref, s_ref):
    length = meta_ref[1 + u]
    step = pl.program_id(0)
    blocks = lax.div(length + KF - 1, KF)
    parts = lane_parts(q_ref[...] * jnp.asarray(0.125, BF))
    width = q_ref.shape[0]

    def first(kb, highest):
        start = pl.multiple_of(kb * KF, KF)
        rows = pl.ds(start, KF)
        live = start + lax.broadcasted_iota(jnp.int32, (KF, width), 0) < length
        out = []
        for h in range(3):
            tile = pl.ds(128 * TILE[h], 128)
            s = nt(k_ref[rows, tile], parts[h])
            s = jnp.where(live, s, -1e30)
            s_ref[h, rows, :] = s
            out.append(jnp.maximum(highest[h], jnp.max(s, axis=0, keepdims=True)))
        return tuple(out)

    floor = jnp.full((1, width), -1e30, F32)
    highest = lax.fori_loop(0, blocks, first, (floor,) * 3)

    def second(kb, carry):
        rows = pl.ds(pl.multiple_of(kb * KF, KF), KF)
        out = []
        for h in range(3):
            total, result = carry[h]
            p = jnp.exp2((s_ref[h, rows, :] - highest[h]) * LOG2E)
            total = total + jnp.sum(p, axis=0, keepdims=True)
            v = v_ref[rows, pl.ds(128 * TILE[h], 128)]
            result = result + tn(v, p.astype(BF))
            out.append((total, result))
        return tuple(out)

    init = ((jnp.zeros((1, width), F32), jnp.zeros((128, width), F32)),) * 3
    done = lax.fori_loop(0, blocks, second, init)
    outs = []
    for h in range(3):
        total, result = done[h]
        lo = HEAD_DIM * (h % 2)
        o = result[lo : lo + HEAD_DIM] / total
        lse_ref[0, pl.ds(h, 1), :] = highest[h] * LOG2E + jnp.log2(total)
        outs.append(o.astype(BF))
    whole = jnp.concatenate(outs, axis=0)
    for j, o_ref in enumerate((own_ref, other_ref)):

        @pl.when(step == j)
        def _():
            o_ref[...] = whole


def attend_forward(meta, q, k, v, u, frames):
    half = frames // 2
    return call(
        functools.partial(forward_kernel, u),
        "attend_forward",
        (2,),
        meta,
        (q, k, v),
        [
            pl.BlockSpec((half, 256), lambda i, m: (i ^ m[0], 0)),
            fixed(frames, 256),
            fixed(frames, 256),
        ],
        [
            fixed(192, half),
            fixed(192, half),
            pl.BlockSpec((1, 8, half), lambda i, m: (i, 0, 0)),
        ],
        [
            like((192, half), BF),
            like((192, half), BF),
            like((2, 8, half), F32),
        ],
        [pltpu.VMEM((3, frames, half), F32)],
        far=(0, 1, 2),
    )


def backward_kernel(
    u, meta_ref, q_ref, k_ref, v_ref, d0_ref, d1_ref, o0_ref, o1_ref, lse_ref,
    dq_ref, dk_ref, dv_ref, kt_ref, dk_acc, dv_acc, do_ref, o_ref,
):
    length = meta_ref[1 + u]
    blocks = lax.div(length + KB - 1, KB)
    step = pl.program_id(0)

    @pl.when(step == 0)
    def _():
        dk_acc[...] = jnp.zeros_like(dk_acc)
        dv_acc[...] = jnp.zeros_like(dv_acc)
        kt_ref[...] = jnp.transpose(k_ref[...])
        do_ref[...] = d0_ref[...]
        o_ref[...] = o0_ref[...]

    @pl.when(step == 1)
    def _():
        do_ref[...] = d1_ref[...]
        o_ref[...] = o1_ref[...]

    parts = lane_parts(q_ref[...] * jnp.asarray(0.125, BF))
    width = q_ref.shape[0]
    empty = jnp.zeros((HEAD_DIM, width), BF)
    head = [do_ref[pl.ds(h * HEAD_DIM, HEAD_DIM), :] for h in range(3)]
    grads = (
        jnp.concatenate([head[0], empty], axis=0),
        jnp.concatenate([empty, head[1]], axis=0),
        jnp.concatenate([head[2], empty], axis=0),
    )
    delta = [
        jnp.sum(
            head[h].astype(F32) * o_ref[pl.ds(h * HEAD_DIM, HEAD_DIM), :].astype(F32), axis=0, keepdims=True
        )
        for h in range(3)
    ]
    lse = [lse_ref[0, pl.ds(h, 1), :] for h in range(3)]

    def body(kb, carry):
        start = pl.multiple_of(kb * KB, KB)
        rows = pl.ds(start, KB)
        live = start + lax.broadcasted_iota(jnp.int32, (KB, width), 0) < length
        out = []
        for h in range(3):
            tile = pl.ds(128 * TILE[h], 128)
            s = nt(k_ref[rows, tile], parts[h])
            s = jnp.where(live, s, -1e30)
            p = jnp.exp2(s * LOG2E - lse[h])
            dp = nn(v_ref[rows, tile], grads[h])
            ds = (p * (dp - delta[h])).astype(BF)
            dv_acc[rows, tile] += nt(p.astype(BF), grads[h])
            dk_acc[rows, tile] += nn(ds, parts[h])
            kt = kt_ref[pl.ds(h * HEAD_DIM, HEAD_DIM), rows]
            out.append(carry[h] + nn(kt, ds))
        return tuple(out)

    zero = jnp.zeros((HEAD_DIM, width), F32)
    done = lax.fori_loop(0, blocks, body, (zero,) * 3)
    full = jnp.concatenate(done + (zero,), axis=0) * 0.125
    dq_ref[...] = jnp.transpose(full).astype(BF)

    @pl.when(step == 1)
    def _():
        dk_ref[...] = dk_acc[...].astype(BF)
        dv_ref[...] = dv_acc[...].astype(BF)


def attend_backward(meta, q, k, v, grads, outs, lse, u, frames):
    half = frames // 2
    return call(
        functools.partial(backward_kernel, u),
        "attend_backward",
        (2,),
        meta,
        (q, k, v, *grads, *outs, lse),
        [
            pl.BlockSpec((half, 256), lambda i, m: (i ^ m[0], 0)),
            fixed(frames, 256),
            fixed(frames, 256),
            fixed(192, half),
            fixed(192, half),
            fixed(192, half),
            fixed(192, half),
            pl.BlockSpec((1, 8, half), lambda i, m: (i, 0, 0)),
        ],
        [
            pl.BlockSpec((half, 256), lambda i, m: (i ^ m[0], 0)),
            fixed(frames, 256),
            fixed(frames, 256),
        ],
        [like((frames, 256), BF)] * 3,
        [
            pltpu.VMEM((256, frames), BF),
            pltpu.VMEM((frames, 256), F32),
            pltpu.VMEM((frames, 256), F32),
            pltpu.VMEM((192, half), BF),
            pltpu.VMEM((192, half), BF),
        ],
        hold=(3,),
        far=(0, 1, 2),
        out=(0, 1, 2),
    )


def entry_kernel(meta_ref, x_ref, dq_ref, dk_ref, dv_ref, wq_ref, wk_ref, wv_ref, *refs):
    last = len(refs) == 7
    before_ref = refs[0] if last else None
    send_ref, keep_ref, sum_ref, acc = refs[-4:]
    step = pl.program_id(0)
    x = x_ref[...]
    total = jnp.zeros(x.shape, F32)
    for i, (g_ref, w_ref) in enumerate(((dq_ref, wq_ref), (dk_ref, wk_ref), (dv_ref, wv_ref))):
        rows = pl.ds(192 * i, 192)
        g = g_ref[:, :192]
        total = total + nn(g, w_ref[...])
        product = tn(g, x)

        @pl.when(step == 0)
        def _():
            acc[rows, :] = product if before_ref is None else product + before_ref[rows, :]

        @pl.when(step == 1)
        def _():
            sum_ref[rows, :] = (product + acc[rows, :]).astype(sum_ref.dtype)

    low = total.astype(BF)

    @pl.when(step == 0)
    def _():
        send_ref[...] = low
        if last:
            merged = refs[1][...].astype(F32) + refs[2][...].astype(F32)
            sum_ref[576:, :] = merged.astype(sum_ref.dtype)

    @pl.when(step == 1)
    def _():
        keep_ref[...] = low


def entry_back(meta, tokens, grads, weights, before, u, frames):
    half = frames // 2
    d = tokens.shape[1]
    rows, dtype = (832, BF) if before else (576, F32)
    return call(
        entry_kernel,
        "entry_back",
        (2,),
        meta,
        (tokens, *grads, *weights, *before),
        [pl.BlockSpec((half, d), lambda i, m: (u * 2 + (1 - i ^ m[0]), 0))]
        + [pl.BlockSpec((half, 256), lambda i, m: (1 - i ^ m[0], 0))] * 3
        + [fixed(192, d)] * 3
        + [fixed(*value.shape) for value in before],
        [fixed(half, d), fixed(half, d), fixed(rows, d)],
        [like((half, d), BF), like((half, d), BF), like((rows, d), dtype)],
        [pltpu.VMEM((576, d), F32)],
        hold=(1, 2, 3),
        far=(0, 4, 5, 6),
    )


def place_kernel(meta_ref, *refs):
    o_ref = refs[-1]
    for i, r_ref in enumerate(refs[:-1]):

        @pl.when(pl.program_id(0) == i)
        def _():
            o_ref[...] = r_ref[...]


def place(meta, own, other):
    half, d = own[0].shape
    count = 2 * len(own)
    return call(
        place_kernel,
        "place",
        (count,),
        meta,
        [block for pair in zip(own, other) for block in pair],
        [fixed(half, d)] * count,
        pl.BlockSpec((half, d), lambda i, m: (i ^ m[0], 0)),
        like((count * half, d), own[0].dtype),
    )


def normalise(values):
    average = jnp.mean(values, axis=-1, keepdims=True)
    centred = values - average
    spread = jnp.mean(centred * centred, axis=-1, keepdims=True)
    rstd = lax.rsqrt(spread + EPS)
    return centred * rstd, rstd


def gelu_pair(v):
    e = jnp.exp2(v * v * (-0.5 * LOG2E))
    t = 1.0 / (1.0 + (0.3275911 * 0.7071067811865476) * jnp.abs(v))
    poly = t * (0.5 * 0.254829592 + t * (0.5 * -0.284496736 + t * (0.5 * 1.421413741 + t * (0.5 * -1.453152027 + t * (0.5 * 1.061405429)))))
    tail = poly * e
    phi_cap = jnp.where(v >= 0, 1.0 - tail, tail)
    return v * phi_cap, phi_cap + v * (e * 0.3989422804014327)


def ahead_kernel(
    meta_ref, tok_ref, a0, a1, a2, a3, w0, w1, w2, w3, ua_ref, ub_ref, da_ref, db_ref, vec_ref,
    xhat_ref, rstd_ref, low_ref, act_ref, slope_ref, own_ref, sent_ref,
):
    gain, bias = vec_ref[0:1, :], vec_ref[1:2, :]
    hidden = ua_ref.shape[1]
    for r in range(tok_ref.shape[0] // RB):
        rows = pl.ds(r * RB, RB)
        branch = jnp.zeros((RB, tok_ref.shape[1]), F32)
        for a, w in ((a0, w0), (a1, w1), (a2, w2), (a3, w3)):
            branch = branch + tn(a[:, rows], w[...]).astype(BF).astype(F32)
        xhat, rstd = normalise(tok_ref[rows, :].astype(F32) + branch)
        xhat_ref[rows, :] = xhat
        rstd_ref[rows, :] = jnp.broadcast_to(rstd, (RB, rstd_ref.shape[1]))
        normed = xhat * gain + bias
        low = normed.astype(BF)
        low_ref[rows, :] = low
        sent = jnp.zeros(normed.shape, F32)
        for g, (up, down) in enumerate(((ua_ref, da_ref), (ub_ref, db_ref))):
            acts = []
            for c in range(hidden // HB):
                act, slope = gelu_pair(nn(low, up[:, c * HB : (c + 1) * HB]))
                columns = pl.ds(g * hidden + c * HB, HB)
                acts.append(act.astype(BF))
                act_ref[rows, columns] = acts[-1]
                slope_ref[rows, columns] = slope.astype(BF)
            sent = sent + nn(jnp.concatenate(acts, axis=1), down[...]).astype(BF).astype(F32)
        own_ref[rows, :] = normed + sent
        sent_ref[rows, :] = sent.astype(BF)


def ahead(meta, tokens, att, merge_w, up, down, vectors, u):
    half = att[0].shape[1]
    d, hidden = up[0].shape
    return call(
        ahead_kernel,
        "ahead",
        (1,),
        meta,
        (tokens, *att, *merge_w, *up, *down, vectors),
        [pl.BlockSpec((half, d), lambda i, m: (u * 2 + m[0], 0))]
        + [fixed(192, half)] * 4
        + [fixed(192, d)] * 4
        + [fixed(d, hidden)] * 2
        + [fixed(hidden, d)] * 2
        + [fixed(4, d)],
        [fixed(half, d), fixed(half, 128), fixed(half, d), fixed(half, 2 * hidden), fixed(half, 2 * hidden), fixed(half, d), fixed(half, d)],
        [
            like((half, d), F32),
            like((half, 128), F32),
            like((half, d), BF),
            like((half, 2 * hidden), BF),
            like((half, 2 * hidden), BF),
            like((half, d), F32),
            like((half, d), BF),
        ],
        far=(0,),
        out=(2, 3, 4, 5),
        out_far=(0, 1),
    )


def astern_kernel(u, meta_ref, own_ref, far_ref, grad_ref, span_ref, ua_ref, ub_ref, da_ref, db_ref, slope_ref, vec_ref, *refs):
    last = len(refs) > 6
    if last:
        before = refs[:-10]
        out_ref, back_ref, sent_ref, small_ref, *sums, g_ref, pre_ref = refs[-10:]
    else:
        out_ref, g_ref, pre_ref, back_ref, sent_ref, small_ref = refs
    gain, bias = vec_ref[2:3, :], vec_ref[3:4, :]
    half, d = own_ref.shape
    hidden = ua_ref.shape[1]
    starts = span_ref[u : u + 1, :]
    gain_grad = jnp.zeros(gain.shape, F32)
    bias_grad = jnp.zeros(gain.shape, F32)
    for r in range(half // RB):
        rows = pl.ds(r * RB, RB)
        xhat, rstd = normalise(own_ref[rows, :] + far_ref[rows, :].astype(F32))
        out_ref[rows, :] = (xhat * gain + bias).astype(BF)
        frame = meta_ref[0] * half + r * RB + lax.broadcasted_iota(jnp.int32, (RB, starts.shape[1]), 0)
        inside = (frame >= starts) & (frame < starts + SPAN)
        weight = jnp.max(jnp.where(inside, 1.0, 0.0), axis=1, keepdims=True)
        cot = grad_ref[rows, :].astype(F32) * weight
        gain_grad = gain_grad + jnp.sum(cot * xhat, axis=0, keepdims=True)
        bias_grad = bias_grad + jnp.sum(cot, axis=0, keepdims=True)
        gy = cot * gain
        mean_gy = jnp.mean(gy, axis=-1, keepdims=True)
        mean_gx = jnp.mean(gy * xhat, axis=-1, keepdims=True)
        sum_grad = rstd * (gy - mean_gy - xhat * mean_gx)
        low = sum_grad.astype(BF)
        g_ref[rows, :] = low
        sent = jnp.zeros(sum_grad.shape, F32)
        for g, (up, down) in enumerate(((ua_ref, da_ref), (ub_ref, db_ref))):
            pres = []
            for c in range(hidden // HB):
                columns = pl.ds(g * hidden + c * HB, HB)
                slope = slope_ref[rows, columns].astype(F32)
                pres.append((nt(low, down[c * HB : (c + 1) * HB, :]) * slope).astype(BF))
                pre_ref[rows, columns] = pres[-1]
            sent = sent + nt(jnp.concatenate(pres, axis=1), up[...]).astype(BF).astype(F32)
        back_ref[rows, :] = sum_grad + sent
        sent_ref[rows, :] = sent.astype(BF)
    small_ref[0:1, :] = gain_grad
    small_ref[1:2, :] = bias_grad
    if last:
        x_ref, act_ref = before[:2]
        weight_sums(x_ref[...], g_ref[...], act_ref, pre_ref, before[2:], sums)


def astern(meta, own, far, grad, spans, up, down, slope, vectors, u, before):
    half, d = own.shape
    hidden = up[0].shape[1]
    rows = fixed(half, d)
    wide = fixed(half, 2 * hidden)
    grads = [] if not before else [(d, hidden)] * 2 + [(hidden, d)] * 2
    extra = [] if not before else [rows, wide] + [fixed(*shape) for shape in grads[: len(before) - 2]]
    made = [like((half, d), BF), like((half, 2 * hidden), BF)]
    others = [like((half, d), F32), like((half, d), BF), like((2, d), F32)]
    shapes = [like((half, d), BF)] + ([] if before else made) + others + [like(shape, BF) for shape in grads]
    return call(
        functools.partial(astern_kernel, u),
        "astern",
        (1,),
        meta,
        (own, far, grad, spans, *up, *down, slope, vectors, *before),
        [rows] * 2
        + [pl.BlockSpec((half, d), lambda i, m: (u * 2 + m[0], 0)), fixed(*spans.shape)]
        + [fixed(d, hidden)] * 2
        + [fixed(hidden, d)] * 2
        + [wide, fixed(4, d)]
        + extra,
        [fixed(*shape.shape) for shape in shapes],
        shapes,
        [pltpu.VMEM(shape.shape, shape.dtype) for shape in made] if before else (),
        limit=20 if before else VMEM,
        hold=(0, 8, *range(10, 10 + len(before))),
        far=(2,),
        out=() if before else (1, 2),
        out_far=(0, 1) if before else (0, 3),
    )


def weight_kernel(meta_ref, x_ref, g_ref, act_ref, pre_ref, *refs):
    before, sums = refs[:-4], refs[-4:]
    weight_sums(x_ref[...], g_ref[...], act_ref, pre_ref, before, sums)


def weight_sums(x, g, act_ref, pre_ref, before, sums):
    hidden = act_ref.shape[1] // 2
    for i in range(2):
        for c in range(hidden // HB):
            columns = pl.ds(i * hidden + c * HB, HB)
            block = pl.ds(c * HB, HB)
            up = tn(x, pre_ref[:, columns])
            down = tn(act_ref[:, columns], g)
            if before:
                up = up + before[i][:, block].astype(F32)
                down = down + before[2 + i][block, :].astype(F32)
            sums[i][:, block] = up.astype(BF)
            sums[2 + i][block, :] = down.astype(BF)


def weight_grads(meta, x, g, act, pre, before):
    rows, d = x.shape
    hidden = act.shape[1] // 2
    shapes = [(d, hidden)] * 2 + [(hidden, d)] * 2
    return call(
        weight_kernel,
        "weight_grads",
        (1,),
        meta,
        (x, g, act, pre, *before),
        [fixed(rows, d)] * 2 + [fixed(rows, 2 * hidden)] * 2 + [fixed(*shape) for shape in shapes[: len(before)]],
        [fixed(*shape) for shape in shapes],
        [like(shape, BF) for shape in shapes],
        hold=(0, 1, 2, 3),
        out=(0, 1, 2, 3),
    )


def inner_kernel(meta_ref, own_ref, far_ref, xhat_ref, rstd_ref, vec_ref, a0, a1, w0, w1, *refs):
    last = len(refs) == 11
    out_ref, g0, g1, m0, m1, small_ref = refs[-6:]
    grad = own_ref[...] + far_ref[...].astype(F32)
    xhat = xhat_ref[...]
    gain_grad = jnp.sum(grad * xhat, axis=0, keepdims=True)
    bias_grad = jnp.sum(grad, axis=0, keepdims=True)
    gy = grad * vec_ref[0:1, :]
    mean_gy = jnp.mean(gy, axis=-1, keepdims=True)
    mean_gx = jnp.mean(gy * xhat, axis=-1, keepdims=True)
    inner = rstd_ref[:, 0:1] * (gy - mean_gy - xhat * mean_gx)
    out_ref[...] = inner
    low = inner.astype(BF)
    g0[...] = nt(w0[...], low).astype(BF)
    g1[...] = nt(w1[...], low).astype(BF)
    small = jnp.concatenate([gain_grad, bias_grad], axis=0)
    small_ref[...] = small
    if last:
        before0, before1, before_small, outer0, outer1 = refs[:5]
        below = jnp.concatenate(
            [small + before_small[...], outer0[...] + outer1[...], jnp.zeros((60, small.shape[1]), F32)], axis=0
        ).astype(BF)
        for m, a, before in ((m0, a0, before0), (m1, a1, before1)):
            m[:192, :] = (nn(a[...], low) + before[...]).astype(BF)
            m[192:, :] = below
    else:
        m0[...] = nn(a0[...], low)
        m1[...] = nn(a1[...], low)


def inner_norm(meta, own, far, xhat, rstd, vectors, att, weights, before):
    rows, d = xhat.shape
    merge = like((256, d), BF) if before else like((192, d), F32)
    return call(
        inner_kernel,
        "inner_norm",
        (1,),
        meta,
        (own, far, xhat, rstd, vectors, *att, *weights, *before),
        [fixed(rows, d)] * 3
        + [fixed(rows, 128), fixed(4, d)]
        + [fixed(192, rows)] * 2
        + [fixed(192, d)] * 2
        + ([fixed(192, d)] * 2 + [fixed(2, d)] * 3 if before else []),
        [fixed(rows, d), fixed(192, rows), fixed(192, rows), fixed(*merge.shape), fixed(*merge.shape), fixed(2, d)],
        [like((rows, d), F32), like((192, rows), BF), like((192, rows), BF), merge, merge, like((2, d), F32)],
        far=(0, 2, 3, 5, 6, 7, 8, *((9, 10) if before else ())),
        out=(1,),
        out_far=(0,) if before else (0, 3, 4),
    )


def fold_kernel(bits, meta_ref, *refs):
    for i in range(2):
        here, there = refs[2 * i : 2 * i + 2]
        if bits:
            send, keep = refs[4 + 2 * i : 6 + 2 * i]
            half = send.shape[0]
            bit = meta_ref[bits[i]]
            for part, j in ((send, 1 - bit), (keep, bit)):
                rows = pl.ds(pl.multiple_of(j * half, 16), half)
                part[...] = (here[rows, :].astype(F32) + there[rows, :].astype(F32)).astype(BF)
        else:
            refs[4 + i][...] = (here[...].astype(F32) + there[...].astype(F32)).astype(BF)


def fold(meta, pairs, bits, hold=()):
    args = [value for pair in pairs for value in pair]
    rows, d = args[0].shape
    shapes = [like((rows // 2, d), BF)] * 4 if bits else [like((rows, d), BF)] * 2
    return call(
        functools.partial(fold_kernel, bits),
        "fold",
        (1,),
        meta,
        args,
        [fixed(rows, d)] * 4,
        [fixed(*shape.shape) for shape in shapes],
        shapes,
        hold=hold,
    )


def local(groups, tokens, lengths, span_starts, wq, wk, wv, wm, wu, wd, ig, ib, og, ob, out_grad):
    rows, d = tokens.shape
    seqs = lengths.shape[0]
    frames = rows // seqs
    half = frames // 2
    core = lax.axis_index("tensor") % 2
    place_dp = lax.axis_index("dp")
    bits = groups.bit_length() - 1

    def swap(value, k):
        return lax.ppermute(value, "tensor", [(i, i ^ k) for i in range(4)])

    def swap_dp(value, k):
        return lax.ppermute(value, "dp", [(i, i ^ k) for i in range(groups)])

    def add(a, b):
        return (a.astype(F32) + b.astype(F32)).astype(BF)

    def total(pieces):
        return sum(piece.astype(F32) for piece in pieces).astype(BF) if len(pieces) > 1 else pieces[0]

    stages = [(0, 1)] + [(b, 2) for b in range(1, bits - 1, 2)] + ([(bits - 1, 1)] if bits % 2 == 0 else [])
    bit_orders = (list(range(bits)), [1, 0, *range(2, bits)])

    def spot_of(stage):
        return (place_dp >> stage[0]) & ((1 << stage[1]) - 1)

    class Chain:
        def __init__(self, part, order, cut_already=False):
            self.part = part.reshape((1,) * len(order) + part.shape) if cut_already else part
            self.order = order
            self.steps = [] if cut_already else [(True, stage) for stage in order]
            self.steps += [(False, stage) for stage in reversed(order)]

        def cut(self, stage, j):
            size = self.part.shape[0] >> stage[1]
            return lax.dynamic_slice_in_dim(self.part, (spot_of(stage) ^ j) * size, size, 0)

        def start(self):
            if self.steps:
                scatter, stage = self.steps[0]
                others = range(1, 1 << stage[1])
                self.pending = [swap_dp(self.cut(stage, j) if scatter else self.part, j << stage[0]) for j in others]

        def finish(self, *after):
            if not self.steps:
                return
            scatter, stage = self.steps.pop(0)
            got = self.pending
            if after:
                got = list(lax.optimization_barrier((*got, *after))[: len(got)])
            if scatter:
                state = total([self.cut(stage, 0)] + got)
                if not self.steps[0][0]:
                    state = state.reshape((1,) * len(self.order) + state.shape)
            else:
                axis = self.order.index(stage)
                spot = spot_of(stage)
                mine = self.part
                if len(got) == 1:
                    laid = [jnp.where(spot, got[0], mine), jnp.where(spot, mine, got[0])]
                    state = jnp.concatenate(laid, axis=axis)
                else:
                    state = jnp.zeros(mine.shape[:axis] + (1 + len(got),) + mine.shape[axis + 1 :], BF)
                    for j, piece in enumerate([mine] + got):
                        state = lax.dynamic_update_slice_in_dim(state, piece, spot ^ j, axis)
                if not self.steps:
                    state = state.reshape(-1, d)
            self.part = state

    def finish(group, *after):
        for chain in group:
            chain.finish(*after)

    def start(group):
        for chain in group:
            chain.start()

    def together(group):
        for chain, value in zip(group, lax.optimization_barrier(tuple(chain.part for chain in group))):
            chain.part = value

    all_bits = [((place_dp >> b) & 1).reshape(1) for b in range(bits)]
    scalars = jnp.concatenate([core.reshape(1), lengths, *all_bits])
    token = []

    def meta():
        return lax.optimization_barrier((scalars, *token))[0] if token else scalars

    def done(results, *others):
        token[:] = [results[0], *others]
        return results

    merge_w = (wm, swap(wm, 1), swap(wm, 2), swap(wm, 3))
    up_w = (wu, swap(wu, 1))
    down_w = (wd, swap(wd, 1))
    vectors = jnp.stack([ig, ib, og, ob])
    qkv_w = (wq.T, wk.T, wv.T)

    fwd, att, front, far = [], [], [], []
    qkv_of = [done(project(scalars, tokens, qkv_w, 0, frames))]
    for u in range(seqs):
        fwd.append(done(attend_forward(meta(), *qkv_of[u], u, frames), *(merge_w[1:] if u == 0 else ())))
        own, other = fwd[u][:2]
        att.append((own, swap(other, 1), swap(own, 2), swap(other, 3)))
        if u + 1 < seqs:
            qkv_of.append(done(project(meta(), tokens, qkv_w, u + 1, frames), up_w[1], down_w[1]))
    for u in range(seqs):
        front.append(done(ahead(meta(), tokens, att[u], merge_w, up_w, down_w, vectors, u)))
        far.append(swap(front[u][6], 2))
    out_rows, back, far_grad, smalls, sums = [], [], [], [], ()
    for u in range(seqs):
        last = u == seqs - 1
        before = (front[u][2], front[u][3], *sums) if last else ()
        res = done(astern(meta(), front[u][5], far[u], out_grad, span_starts, up_w, down_w, front[u][4], vectors, u, before))
        out_rows.append(res[0])
        back.append(res[1 if last else 3])
        smalls.append(res[3 if last else 5])
        if last:
            sent, sums = res[2], res[4:]
        else:
            far_grad.append(swap(res[4], 2))
            sums = done(weight_grads(meta(), front[u][2], res[1], front[u][3], res[2], sums))

    def inner_step(u, before):
        res = done(inner_norm(meta(), back[u], far_grad[u], front[u][0], front[u][1], vectors, att[u][:2], merge_w[:2], before))
        return res, (res[1], swap(res[2], 1))

    def attend_step(u, grads):
        return done(attend_backward(meta(), *qkv_of[u], grads, fwd[u][:2], fwd[u][2], u, frames))

    def entry_step(u, grads, before):
        return done(entry_back(meta(), tokens, grads, qkv_w, before, u, frames))


    first_bit = 1 + seqs

    def scatter(step, pairs, after, hold=()):
        pairs = [tuple(lax.optimization_barrier((*pair, after))[:2]) for pair in pairs]
        if step == bits:
            return done(fold(meta(), pairs, (), hold))
        out = done(fold(meta(), pairs, tuple(first_bit + order[step] for order in bit_orders), hold))
        return [(out[2 * i + 1], swap_dp(out[2 * i], 1 << bit_orders[i][step])) for i in range(2)]

    inner, entry, so_far, near, crossed = [], [], (), [], []
    out_other = [swap(r, 1) for r in out_rows]

    def exchange(out):
        got = swap(out[0], 1)
        near.append((out[1], got))
        crossed.append(swap(total(near[-1]), 2))
        return got

    for u in range(seqs):
        last = u == seqs - 1
        if u == 0:
            up_own, up_other, down_own, down_other = lax.optimization_barrier((*sums, far_grad[0]))[:4]
            moving = [(down_own, swap(down_other, 1)), (up_own, swap(up_other, 1))]
            res, grads = inner_step(0, ())
            inner.append(res)
            far_grad.append(swap(lax.optimization_barrier((sent, res[0]))[0], 2))
            moving = scatter(0, moving, res[0])
        dqkv = attend_step(u, grads)
        moving = scatter(1 + 2 * u, moving, dqkv[0])
        if not last:
            before = ()
            if u + 1 == seqs - 1:
                before = (inner[0][3], inner[0][4], inner[0][5], *smalls)
            res, grads = inner_step(u + 1, before)
            inner.append(res)
        else:
            for step in range(4, bits + 1):
                moving = scatter(step, moving, moving[0][0])
            first, second = (
                Chain(moving[i], [(b, 1) for b in order], True) for i, order in enumerate(bit_orders)
            )
            start([first, second])
            token.extend(out_other)
        out = entry_step(u, dqkv, so_far)
        entry.append(out)
        if not last:
            merge_got = swap(lax.optimization_barrier((res[4], out[0]))[0], 1)
            so_far = (out[2], res[3], merge_got)
            moving = scatter(2, moving, out[0])
            exchange(out)
    qkv = Chain(out[2], stages)
    qkv.start()

    got = exchange(out)
    layer_output = place(meta(), out_rows, out_other)

    finish([first, second], got)
    finish([qkv])
    together([qkv, first, second])
    start([qkv, first, second])
    finish([qkv, first, second], crossed[0])
    together([qkv, first, second])
    start([qkv, first])
    finish([qkv, first], crossed[1])
    together([qkv, first, second])
    start([qkv, second])
    ready = []
    for u in range(seqs):
        rest = near[u][0].astype(F32) + near[u][1].astype(F32) + crossed[u].astype(F32)
        ready.append((inner[u][0] + rest).astype(BF))
    input_grad = place(scalars, ready, [swap(r, 1) for r in ready])
    finish([qkv, second], input_grad, layer_output)
    while qkv.steps or first.steps or second.steps:
        start([qkv, first, second])
        finish([qkv, first, second])
        together([qkv, first, second])
    down_sum, up_sum, joint = (chain.part for chain in (first, second, qkv))
    qkv_sum, merge_sum = joint[:576], joint[576:]
    small = merge_sum[192:196].astype(F32)
    query_grad, key_grad, value_grad = (qkv_sum[192 * i : 192 * (i + 1)].astype(F32).T for i in range(3))
    return (
        layer_output,
        input_grad,
        query_grad,
        key_grad,
        value_grad,
        merge_sum[:192].astype(F32),
        up_sum.astype(F32),
        down_sum.astype(F32),
        small[0],
        small[1],
        small[2],
        small[3],
    )


def solution(mesh):
    in_specs = (
        P("dp", None),
        P("dp"),
        P("dp", None),
        P(None, "tensor"),
        P(None, "tensor"),
        P(None, "tensor"),
        P("tensor", None),
        P(None, "tensor"),
        P("tensor", None),
        P(),
        P(),
        P(),
        P(),
        P("dp", None),
    )
    out_specs = (
        P("dp", None),
        P("dp", None),
        P(None, "tensor"),
        P(None, "tensor"),
        P(None, "tensor"),
        P("tensor", None),
        P(None, "tensor"),
        P("tensor", None),
        P(),
        P(),
        P(),
        P(),
    )
    body = functools.partial(local, mesh.shape["dp"])
    return jax.shard_map(body, mesh=mesh, in_specs=in_specs, out_specs=out_specs, check_vma=False)
```

```python
import functools

import jax
import jax.numpy as jnp
from jax import lax
from jax.experimental import pallas as pl
from jax.experimental.pallas import tpu as pltpu
from jax.sharding import PartitionSpec as P

HEAD_DIM = 64
SPAN = 10
EPS = 1e-05
LOG2E = 1.4426950408889634
KF = 1024
KB = 512
VMEM = 12
RB = 128
HB = 256
BF = jnp.bfloat16
F32 = jnp.float32
MIB = 1 << 20


def nn(a, b):
    return lax.dot_general(a, b, (((1,), (0,)), ((), ())), preferred_element_type=F32)


def nt(a, b):
    return lax.dot_general(a, b, (((1,), (1,)), ((), ())), preferred_element_type=F32)


def tn(a, b):
    return lax.dot_general(a, b, (((0,), (0,)), ((), ())), preferred_element_type=F32)


def params(limit):
    return pltpu.CompilerParams(vmem_limit_bytes=limit * MIB)


def cost(micros):
    return pl.CostEstimate(flops=int(micros * 1.1e9), bytes_accessed=1024, transcendentals=0)


MICROS = {"project": 3, "attend_forward": 8, "attend_backward": 12, "entry_back": 5, "place": 3, "ahead": 9, "astern": 10, "inner_norm": 3, "weight_grads": 4, "fold": 2}


def lane_parts(block):
    left = block[:, :128]
    lane = lax.broadcasted_iota(jnp.int32, left.shape, 1)
    zero = jnp.zeros_like(left)
    return (
        jnp.where(lane < HEAD_DIM, left, zero),
        jnp.where(lane >= HEAD_DIM, left, zero),
        block[:, 128:],
    )


TILE = (0, 0, 1)


def call(kernel, name, grid, meta, args, in_specs, out_specs, out_shape, scratch=(), limit=VMEM, hold=(), far=(), out=(), out_far=()):
    def place_input(i, value):
        space = pltpu.VMEM if i in hold else pltpu.HBM if i in far else None
        return value if space is None else pltpu.with_memory_space_constraint(value, space)

    def place_output(i, value):
        space = pltpu.VMEM if i in out else pltpu.HBM if i in out_far else None
        return value if space is None else space(value.shape, value.dtype)

    single = not isinstance(out_shape, list)
    return pl.pallas_call(
        kernel,
        grid_spec=pltpu.PrefetchScalarGridSpec(
            num_scalar_prefetch=1,
            grid=grid,
            in_specs=in_specs,
            out_specs=out_specs,
            scratch_shapes=scratch,
        ),
        out_shape=place_output(0, out_shape) if single else [place_output(i, o) for i, o in enumerate(out_shape)],
        compiler_params=params(limit),
        cost_estimate=cost(MICROS[name]),
        name=name,
    )(meta, *(place_input(i, value) for i, value in enumerate(args)))


def fixed(*shape):
    return pl.BlockSpec(shape, lambda *_: (0,) * len(shape))


def like(shape, dtype):
    return jax.ShapeDtypeStruct(shape, dtype)


def project_kernel(meta_ref, x_ref, wq_ref, wk_ref, wv_ref, *refs):
    x = x_ref[...]
    for i, w_ref in enumerate((wq_ref, wk_ref, wv_ref)):
        low = nt(x, w_ref[...]).astype(BF)
        for o_ref in (refs[i], refs[3 + i]):
            o_ref[:, :192] = low
            o_ref[:, 192:] = jnp.zeros((x.shape[0], HEAD_DIM), BF)


def project(meta, tokens, weights, u, frames):
    rows, d = frames, tokens.shape[1]
    block = 256
    return call(
        project_kernel,
        "project",
        (rows // block,),
        meta,
        (tokens, *weights),
        [pl.BlockSpec((block, d), lambda i, m: (u * (rows // block) + i, 0))] + [fixed(192, d)] * 3,
        [pl.BlockSpec((block, 256), lambda i, m: (i, 0))] * 6,
        [like((rows, 256), BF)] * 6,
        far=range(4),
        out=(0, 1, 2),
        out_far=(3, 4, 5),
    )


def forward_kernel(u, meta_ref, q_ref, k_ref, v_ref, own_ref, other_ref, lse_ref, s_ref):
    length = meta_ref[1 + u]
    step = pl.program_id(0)
    blocks = lax.div(length + KF - 1, KF)
    parts = lane_parts(q_ref[...] * jnp.asarray(0.125, BF))
    width = q_ref.shape[0]

    def first(kb, highest):
        start = pl.multiple_of(kb * KF, KF)
        rows = pl.ds(start, KF)
        live = start + lax.broadcasted_iota(jnp.int32, (KF, width), 0) < length
        out = []
        for h in range(3):
            tile = pl.ds(128 * TILE[h], 128)
            s = nt(k_ref[rows, tile], parts[h])
            s = jnp.where(live, s, -1e30)
            s_ref[h, rows, :] = s
            out.append(jnp.maximum(highest[h], jnp.max(s, axis=0, keepdims=True)))
        return tuple(out)

    floor = jnp.full((1, width), -1e30, F32)
    highest = lax.fori_loop(0, blocks, first, (floor,) * 3)

    def second(kb, carry):
        rows = pl.ds(pl.multiple_of(kb * KF, KF), KF)
        out = []
        for h in range(3):
            total, result = carry[h]
            p = jnp.exp2((s_ref[h, rows, :] - highest[h]) * LOG2E)
            total = total + jnp.sum(p, axis=0, keepdims=True)
            v = v_ref[rows, pl.ds(128 * TILE[h], 128)]
            result = result + tn(v, p.astype(BF))
            out.append((total, result))
        return tuple(out)

    init = ((jnp.zeros((1, width), F32), jnp.zeros((128, width), F32)),) * 3
    done = lax.fori_loop(0, blocks, second, init)
    outs = []
    for h in range(3):
        total, result = done[h]
        lo = HEAD_DIM * (h % 2)
        o = result[lo : lo + HEAD_DIM] / total
        lse_ref[0, pl.ds(h, 1), :] = highest[h] * LOG2E + jnp.log2(total)
        outs.append(o.astype(BF))
    whole = jnp.concatenate(outs, axis=0)
    for j, o_ref in enumerate((own_ref, other_ref)):

        @pl.when(step == j)
        def _():
            o_ref[...] = whole


def attend_forward(meta, q, k, v, u, frames):
    half = frames // 2
    return call(
        functools.partial(forward_kernel, u),
        "attend_forward",
        (2,),
        meta,
        (q, k, v),
        [
            pl.BlockSpec((half, 256), lambda i, m: (i ^ m[0], 0)),
            fixed(frames, 256),
            fixed(frames, 256),
        ],
        [
            fixed(192, half),
            fixed(192, half),
            pl.BlockSpec((1, 8, half), lambda i, m: (i, 0, 0)),
        ],
        [
            like((192, half), BF),
            like((192, half), BF),
            like((2, 8, half), F32),
        ],
        [pltpu.VMEM((3, frames, half), F32)],
        hold=(0, 1, 2),
        out_far=(0, 1),
    )


def backward_kernel(
    u, meta_ref, q_ref, k_ref, v_ref, d0_ref, d1_ref, o0_ref, o1_ref, lse_ref,
    dq_ref, dk_ref, dv_ref, kt_ref, dk_acc, dv_acc, do_ref, o_ref,
):
    length = meta_ref[1 + u]
    blocks = lax.div(length + KB - 1, KB)
    step = pl.program_id(0)

    @pl.when(step == 0)
    def _():
        dk_acc[...] = jnp.zeros_like(dk_acc)
        dv_acc[...] = jnp.zeros_like(dv_acc)
        kt_ref[...] = jnp.transpose(k_ref[...])
        do_ref[...] = d0_ref[...]
        o_ref[...] = o0_ref[...]

    @pl.when(step == 1)
    def _():
        do_ref[...] = d1_ref[...]
        o_ref[...] = o1_ref[...]

    parts = lane_parts(q_ref[...] * jnp.asarray(0.125, BF))
    width = q_ref.shape[0]
    empty = jnp.zeros((HEAD_DIM, width), BF)
    head = [do_ref[pl.ds(h * HEAD_DIM, HEAD_DIM), :] for h in range(3)]
    grads = (
        jnp.concatenate([head[0], empty], axis=0),
        jnp.concatenate([empty, head[1]], axis=0),
        jnp.concatenate([head[2], empty], axis=0),
    )
    delta = [
        jnp.sum(
            head[h].astype(F32) * o_ref[pl.ds(h * HEAD_DIM, HEAD_DIM), :].astype(F32), axis=0, keepdims=True
        )
        for h in range(3)
    ]
    lse = [lse_ref[0, pl.ds(h, 1), :] for h in range(3)]

    def body(kb, carry):
        start = pl.multiple_of(kb * KB, KB)
        rows = pl.ds(start, KB)
        live = start + lax.broadcasted_iota(jnp.int32, (KB, width), 0) < length
        out = []
        for h in range(3):
            tile = pl.ds(128 * TILE[h], 128)
            s = nt(k_ref[rows, tile], parts[h])
            s = jnp.where(live, s, -1e30)
            p = jnp.exp2(s * LOG2E - lse[h])
            dp = nn(v_ref[rows, tile], grads[h])
            ds = (p * (dp - delta[h])).astype(BF)
            dv_acc[rows, tile] += nt(p.astype(BF), grads[h])
            dk_acc[rows, tile] += nn(ds, parts[h])
            kt = kt_ref[pl.ds(h * HEAD_DIM, HEAD_DIM), rows]
            out.append(carry[h] + nn(kt, ds))
        return tuple(out)

    zero = jnp.zeros((HEAD_DIM, width), F32)
    done = lax.fori_loop(0, blocks, body, (zero,) * 3)
    full = jnp.concatenate(done + (zero,), axis=0) * 0.125
    dq_ref[...] = jnp.transpose(full).astype(BF)

    @pl.when(step == 1)
    def _():
        dk_ref[...] = dk_acc[...].astype(BF)
        dv_ref[...] = dv_acc[...].astype(BF)


def attend_backward(meta, q, k, v, grads, outs, lse, u, frames):
    half = frames // 2
    return call(
        functools.partial(backward_kernel, u),
        "attend_backward",
        (2,),
        meta,
        (q, k, v, *grads, *outs, lse),
        [
            pl.BlockSpec((half, 256), lambda i, m: (i ^ m[0], 0)),
            fixed(frames, 256),
            fixed(frames, 256),
            fixed(192, half),
            fixed(192, half),
            fixed(192, half),
            fixed(192, half),
            pl.BlockSpec((1, 8, half), lambda i, m: (i, 0, 0)),
        ],
        [
            pl.BlockSpec((half, 256), lambda i, m: (i ^ m[0], 0)),
            fixed(frames, 256),
            fixed(frames, 256),
        ],
        [like((frames, 256), BF)] * 3,
        [
            pltpu.VMEM((256, frames), BF),
            pltpu.VMEM((frames, 256), F32),
            pltpu.VMEM((frames, 256), F32),
            pltpu.VMEM((192, half), BF),
            pltpu.VMEM((192, half), BF),
        ],
        hold=(3, 4),
        far=(0, 1, 2, 5, 6),
        out=(0, 1, 2),
    )


def entry_kernel(meta_ref, x_ref, dq_ref, dk_ref, dv_ref, wq_ref, wk_ref, wv_ref, *refs):
    last = len(refs) == 7
    before_ref = refs[0] if last else None
    send_ref, keep_ref, sum_ref, acc = refs[-4:]
    step = pl.program_id(0)
    x = x_ref[...]
    total = jnp.zeros(x.shape, F32)
    for i, (g_ref, w_ref) in enumerate(((dq_ref, wq_ref), (dk_ref, wk_ref), (dv_ref, wv_ref))):
        rows = pl.ds(192 * i, 192)
        g = g_ref[:, :192]
        total = total + nn(g, w_ref[...])
        product = tn(g, x)

        @pl.when(step == 0)
        def _():
            acc[rows, :] = product if before_ref is None else product + before_ref[rows, :]

        @pl.when(step == 1)
        def _():
            sum_ref[rows, :] = (product + acc[rows, :]).astype(sum_ref.dtype)

    low = total.astype(BF)

    @pl.when(step == 0)
    def _():
        send_ref[...] = low
        if last:
            merged = refs[1][...].astype(F32) + refs[2][...].astype(F32)
            sum_ref[576:, :] = merged.astype(sum_ref.dtype)

    @pl.when(step == 1)
    def _():
        keep_ref[...] = low


def entry_back(meta, tokens, grads, weights, before, u, frames):
    half = frames // 2
    d = tokens.shape[1]
    rows, dtype = (832, BF) if before else (576, F32)
    return call(
        entry_kernel,
        "entry_back",
        (2,),
        meta,
        (tokens, *grads, *weights, *before),
        [pl.BlockSpec((half, d), lambda i, m: (u * 2 + (1 - i ^ m[0]), 0))]
        + [pl.BlockSpec((half, 256), lambda i, m: (1 - i ^ m[0], 0))] * 3
        + [fixed(192, d)] * 3
        + [fixed(*value.shape) for value in before],
        [fixed(half, d), fixed(half, d), fixed(rows, d)],
        [like((half, d), BF), like((half, d), BF), like((rows, d), dtype)],
        [pltpu.VMEM((576, d), F32)],
        hold=(1, 2, 3),
        far=(0, 4, 5, 6),
    )


def place_kernel(meta_ref, *refs):
    o_ref = refs[-1]
    for i, r_ref in enumerate(refs[:-1]):

        @pl.when(pl.program_id(0) == i)
        def _():
            o_ref[...] = r_ref[...]


def place(meta, own, other):
    half, d = own[0].shape
    count = 2 * len(own)
    return call(
        place_kernel,
        "place",
        (count,),
        meta,
        [block for pair in zip(own, other) for block in pair],
        [fixed(half, d)] * count,
        pl.BlockSpec((half, d), lambda i, m: (i ^ m[0], 0)),
        like((count * half, d), own[0].dtype),
    )


def normalise(values):
    average = jnp.mean(values, axis=-1, keepdims=True)
    centred = values - average
    spread = jnp.mean(centred * centred, axis=-1, keepdims=True)
    rstd = lax.rsqrt(spread + EPS)
    return centred * rstd, rstd


def gelu_pair(v):
    e = jnp.exp2(v * v * (-0.5 * LOG2E))
    t = 1.0 / (1.0 + (0.3275911 * 0.7071067811865476) * jnp.abs(v))
    poly = t * (0.5 * 0.254829592 + t * (0.5 * -0.284496736 + t * (0.5 * 1.421413741 + t * (0.5 * -1.453152027 + t * (0.5 * 1.061405429)))))
    tail = poly * e
    phi_cap = jnp.where(v >= 0, 1.0 - tail, tail)
    return v * phi_cap, phi_cap + v * (e * 0.3989422804014327)


def ahead_kernel(
    meta_ref, tok_ref, a0, a1, a2, a3, w0, w1, w2, w3, ua_ref, ub_ref, da_ref, db_ref, vec_ref,
    xhat_ref, rstd_ref, low_ref, act_ref, slope_ref, own_ref, sent_ref,
):
    gain, bias = vec_ref[0:1, :], vec_ref[1:2, :]
    hidden = ua_ref.shape[1]
    for r in range(tok_ref.shape[0] // RB):
        rows = pl.ds(r * RB, RB)
        branch = jnp.zeros((RB, tok_ref.shape[1]), F32)
        for a, w in ((a0, w0), (a1, w1), (a2, w2), (a3, w3)):
            branch = branch + tn(a[:, rows], w[...]).astype(BF).astype(F32)
        xhat, rstd = normalise(tok_ref[rows, :].astype(F32) + branch)
        xhat_ref[rows, :] = xhat
        rstd_ref[rows, :] = jnp.broadcast_to(rstd, (RB, rstd_ref.shape[1]))
        normed = xhat * gain + bias
        low = normed.astype(BF)
        low_ref[rows, :] = low
        sent = jnp.zeros(normed.shape, F32)
        for g, (up, down) in enumerate(((ua_ref, da_ref), (ub_ref, db_ref))):
            acts = []
            for c in range(hidden // HB):
                act, slope = gelu_pair(nn(low, up[:, c * HB : (c + 1) * HB]))
                columns = pl.ds(g * hidden + c * HB, HB)
                acts.append(act.astype(BF))
                act_ref[rows, columns] = acts[-1]
                slope_ref[rows, columns] = slope.astype(BF)
            sent = sent + nn(jnp.concatenate(acts, axis=1), down[...]).astype(BF).astype(F32)
        own_ref[rows, :] = normed + sent
        sent_ref[rows, :] = sent.astype(BF)


def ahead(meta, tokens, att, merge_w, up, down, vectors, u):
    half = att[0].shape[1]
    d, hidden = up[0].shape
    return call(
        ahead_kernel,
        "ahead",
        (1,),
        meta,
        (tokens, *att, *merge_w, *up, *down, vectors),
        [pl.BlockSpec((half, d), lambda i, m: (u * 2 + m[0], 0))]
        + [fixed(192, half)] * 4
        + [fixed(192, d)] * 4
        + [fixed(d, hidden)] * 2
        + [fixed(hidden, d)] * 2
        + [fixed(4, d)],
        [fixed(half, d), fixed(half, 128), fixed(half, d), fixed(half, 2 * hidden), fixed(half, 2 * hidden), fixed(half, d), fixed(half, d)],
        [
            like((half, d), F32),
            like((half, 128), F32),
            like((half, d), BF),
            like((half, 2 * hidden), BF),
            like((half, 2 * hidden), BF),
            like((half, d), F32),
            like((half, d), BF),
        ],
        hold=range(9, 13),
        far=(0, 1),
        out=(2, 3, 4, 5),
        out_far=(0, 1),
    )


def astern_kernel(u, meta_ref, own_ref, far_ref, grad_ref, span_ref, ua_ref, ub_ref, da_ref, db_ref, slope_ref, vec_ref, *refs):
    last = len(refs) > 6
    if last:
        before = refs[:-10]
        out_ref, back_ref, sent_ref, small_ref, *sums, g_ref, pre_ref = refs[-10:]
    else:
        out_ref, g_ref, pre_ref, back_ref, sent_ref, small_ref = refs
    gain, bias = vec_ref[2:3, :], vec_ref[3:4, :]
    half, d = own_ref.shape
    hidden = ua_ref.shape[1]
    starts = span_ref[u : u + 1, :]
    gain_grad = jnp.zeros(gain.shape, F32)
    bias_grad = jnp.zeros(gain.shape, F32)
    for r in range(half // RB):
        rows = pl.ds(r * RB, RB)
        xhat, rstd = normalise(own_ref[rows, :] + far_ref[rows, :].astype(F32))
        out_ref[rows, :] = (xhat * gain + bias).astype(BF)
        frame = meta_ref[0] * half + r * RB + lax.broadcasted_iota(jnp.int32, (RB, starts.shape[1]), 0)
        inside = (frame >= starts) & (frame < starts + SPAN)
        weight = jnp.max(jnp.where(inside, 1.0, 0.0), axis=1, keepdims=True)
        cot = grad_ref[rows, :].astype(F32) * weight
        gain_grad = gain_grad + jnp.sum(cot * xhat, axis=0, keepdims=True)
        bias_grad = bias_grad + jnp.sum(cot, axis=0, keepdims=True)
        gy = cot * gain
        mean_gy = jnp.mean(gy, axis=-1, keepdims=True)
        mean_gx = jnp.mean(gy * xhat, axis=-1, keepdims=True)
        sum_grad = rstd * (gy - mean_gy - xhat * mean_gx)
        low = sum_grad.astype(BF)
        g_ref[rows, :] = low
        sent = jnp.zeros(sum_grad.shape, F32)
        for g, (up, down) in enumerate(((ua_ref, da_ref), (ub_ref, db_ref))):
            pres = []
            for c in range(hidden // HB):
                columns = pl.ds(g * hidden + c * HB, HB)
                slope = slope_ref[rows, columns].astype(F32)
                pres.append((nt(low, down[c * HB : (c + 1) * HB, :]) * slope).astype(BF))
                pre_ref[rows, columns] = pres[-1]
            sent = sent + nt(jnp.concatenate(pres, axis=1), up[...]).astype(BF).astype(F32)
        back_ref[rows, :] = sum_grad + sent
        sent_ref[rows, :] = sent.astype(BF)
    small_ref[0:1, :] = gain_grad
    small_ref[1:2, :] = bias_grad
    if last:
        x_ref, act_ref = before[:2]
        weight_sums(x_ref[...], g_ref[...], act_ref, pre_ref, before[2:], sums)


def astern(meta, own, far, grad, spans, up, down, slope, vectors, u, before):
    half, d = own.shape
    hidden = up[0].shape[1]
    rows = fixed(half, d)
    wide = fixed(half, 2 * hidden)
    grads = [] if not before else [(d, hidden)] * 2 + [(hidden, d)] * 2
    extra = [] if not before else [rows, wide] + [fixed(*shape) for shape in grads[: len(before) - 2]]
    made = [like((half, d), BF), like((half, 2 * hidden), BF)]
    others = [like((half, d), F32), like((half, d), BF), like((2, d), F32)]
    shapes = [like((half, d), BF)] + ([] if before else made) + others + [like(shape, BF) for shape in grads]
    return call(
        functools.partial(astern_kernel, u),
        "astern",
        (1,),
        meta,
        (own, far, grad, spans, *up, *down, slope, vectors, *before),
        [rows] * 2
        + [pl.BlockSpec((half, d), lambda i, m: (u * 2 + m[0], 0)), fixed(*spans.shape)]
        + [fixed(d, hidden)] * 2
        + [fixed(hidden, d)] * 2
        + [wide, fixed(4, d)]
        + extra,
        [fixed(*shape.shape) for shape in shapes],
        shapes,
        [pltpu.VMEM(shape.shape, shape.dtype) for shape in made] if before else (),
        limit=20 if before else VMEM,
        hold=(0, 1, *range(4, 9), *range(10, 10 + len(before))),
        far=(2,),
        out=() if before else (1, 2),
        out_far=(1, 4, 6) if before else (3,),
    )


def weight_kernel(meta_ref, x_ref, g_ref, act_ref, pre_ref, *refs):
    before, sums = refs[:-4], refs[-4:]
    weight_sums(x_ref[...], g_ref[...], act_ref, pre_ref, before, sums)


def weight_sums(x, g, act_ref, pre_ref, before, sums):
    hidden = act_ref.shape[1] // 2
    for i in range(2):
        for c in range(hidden // HB):
            columns = pl.ds(i * hidden + c * HB, HB)
            block = pl.ds(c * HB, HB)
            up = tn(x, pre_ref[:, columns])
            down = tn(act_ref[:, columns], g)
            if before:
                up = up + before[i][:, block].astype(F32)
                down = down + before[2 + i][block, :].astype(F32)
            sums[i][:, block] = up.astype(BF)
            sums[2 + i][block, :] = down.astype(BF)


def weight_grads(meta, x, g, act, pre, before):
    rows, d = x.shape
    hidden = act.shape[1] // 2
    shapes = [(d, hidden)] * 2 + [(hidden, d)] * 2
    return call(
        weight_kernel,
        "weight_grads",
        (1,),
        meta,
        (x, g, act, pre, *before),
        [fixed(rows, d)] * 2 + [fixed(rows, 2 * hidden)] * 2 + [fixed(*shape) for shape in shapes[: len(before)]],
        [fixed(*shape) for shape in shapes],
        [like(shape, BF) for shape in shapes],
        hold=(0, 1, 2, 3),
        out=(0, 1, 2, 3),
    )


def inner_kernel(meta_ref, own_ref, far_ref, xhat_ref, rstd_ref, vec_ref, a0, a1, w0, w1, *refs):
    last = len(refs) == 11
    out_ref, g0, g1, m0, m1, small_ref = refs[-6:]
    grad = own_ref[...] + far_ref[...].astype(F32)
    xhat = xhat_ref[...]
    gain_grad = jnp.sum(grad * xhat, axis=0, keepdims=True)
    bias_grad = jnp.sum(grad, axis=0, keepdims=True)
    gy = grad * vec_ref[0:1, :]
    mean_gy = jnp.mean(gy, axis=-1, keepdims=True)
    mean_gx = jnp.mean(gy * xhat, axis=-1, keepdims=True)
    inner = rstd_ref[:, 0:1] * (gy - mean_gy - xhat * mean_gx)
    out_ref[...] = inner
    low = inner.astype(BF)
    g0[...] = nt(w0[...], low).astype(BF)
    g1[...] = nt(w1[...], low).astype(BF)
    small = jnp.concatenate([gain_grad, bias_grad], axis=0)
    small_ref[...] = small
    if last:
        before0, before1, before_small, outer0, outer1 = refs[:5]
        below = jnp.concatenate(
            [small + before_small[...], outer0[...] + outer1[...], jnp.zeros((60, small.shape[1]), F32)], axis=0
        ).astype(BF)
        for m, a, before in ((m0, a0, before0), (m1, a1, before1)):
            m[:192, :] = (nn(a[...], low) + before[...]).astype(BF)
            m[192:, :] = below
    else:
        m0[...] = nn(a0[...], low)
        m1[...] = nn(a1[...], low)


def inner_norm(meta, own, far, xhat, rstd, vectors, att, weights, before):
    rows, d = xhat.shape
    merge = like((256, d), BF) if before else like((192, d), F32)
    return call(
        inner_kernel,
        "inner_norm",
        (1,),
        meta,
        (own, far, xhat, rstd, vectors, *att, *weights, *before),
        [fixed(rows, d)] * 3
        + [fixed(rows, 128), fixed(4, d)]
        + [fixed(192, rows)] * 2
        + [fixed(192, d)] * 2
        + ([fixed(192, d)] * 2 + [fixed(2, d)] * 3 if before else []),
        [fixed(rows, d), fixed(192, rows), fixed(192, rows), fixed(*merge.shape), fixed(*merge.shape), fixed(2, d)],
        [like((rows, d), F32), like((192, rows), BF), like((192, rows), BF), merge, merge, like((2, d), F32)],
        hold=(1,),
        far=(0, 2, 3, 5, *((9, 10) if before else ())),
        out=(1,),
        out_far=(0,) if before else (0, 3, 4),
    )


def fold_kernel(bits, meta_ref, *refs):
    for i in range(2):
        here, there = refs[2 * i : 2 * i + 2]
        if bits:
            send, keep = refs[4 + 2 * i : 6 + 2 * i]
            half = send.shape[0]
            bit = meta_ref[bits[i]]
            for part, j in ((send, 1 - bit), (keep, bit)):
                rows = pl.ds(pl.multiple_of(j * half, 16), half)
                part[...] = (here[rows, :].astype(F32) + there[rows, :].astype(F32)).astype(BF)
        else:
            refs[4 + i][...] = (here[...].astype(F32) + there[...].astype(F32)).astype(BF)


def fold(meta, pairs, bits, hold=(), far=()):
    args = [value for pair in pairs for value in pair]
    rows, d = args[0].shape
    shapes = [like((rows // 2, d), BF)] * 4 if bits else [like((rows, d), BF)] * 2
    return call(
        functools.partial(fold_kernel, bits),
        "fold",
        (1,),
        meta,
        args,
        [fixed(rows, d)] * 4,
        [fixed(*shape.shape) for shape in shapes],
        shapes,
        hold=hold,
        far=far,
    )


def local(groups, tokens, lengths, span_starts, wq, wk, wv, wm, wu, wd, ig, ib, og, ob, out_grad):
    rows, d = tokens.shape
    seqs = lengths.shape[0]
    frames = rows // seqs
    half = frames // 2
    core = lax.axis_index("tensor") % 2
    place_dp = lax.axis_index("dp")
    bits = groups.bit_length() - 1

    def swap(value, k):
        return lax.ppermute(value, "tensor", [(i, i ^ k) for i in range(4)])

    def swap_dp(value, k):
        return lax.ppermute(value, "dp", [(i, i ^ k) for i in range(groups)])

    def add(a, b):
        return (a.astype(F32) + b.astype(F32)).astype(BF)

    def total(pieces):
        return sum(piece.astype(F32) for piece in pieces).astype(BF) if len(pieces) > 1 else pieces[0]

    stages = [(0, 1)] + [(b, 2) for b in range(1, bits - 1, 2)] + ([(bits - 1, 1)] if bits % 2 == 0 else [])
    bit_orders = (list(range(bits)), [1, 0, *range(2, bits)])

    def spot_of(stage):
        return (place_dp >> stage[0]) & ((1 << stage[1]) - 1)

    class Chain:
        def __init__(self, part, order, cut_already=False):
            self.part = part.reshape((1,) * len(order) + part.shape) if cut_already else part
            self.order = order
            self.steps = [] if cut_already else [(True, stage) for stage in order]
            self.steps += [(False, stage) for stage in reversed(order)]

        def cut(self, stage, j):
            size = self.part.shape[0] >> stage[1]
            return lax.dynamic_slice_in_dim(self.part, (spot_of(stage) ^ j) * size, size, 0)

        def start(self):
            if self.steps:
                scatter, stage = self.steps[0]
                others = range(1, 1 << stage[1])
                self.pending = [swap_dp(self.cut(stage, j) if scatter else self.part, j << stage[0]) for j in others]

        def finish(self, *after):
            if not self.steps:
                return
            scatter, stage = self.steps.pop(0)
            got = self.pending
            if after:
                got = list(lax.optimization_barrier((*got, *after))[: len(got)])
            if scatter:
                state = total([self.cut(stage, 0)] + got)
                if not self.steps[0][0]:
                    state = state.reshape((1,) * len(self.order) + state.shape)
            else:
                axis = self.order.index(stage)
                spot = spot_of(stage)
                mine = self.part
                if len(got) == 1:
                    laid = [jnp.where(spot, got[0], mine), jnp.where(spot, mine, got[0])]
                    state = jnp.concatenate(laid, axis=axis)
                else:
                    state = jnp.zeros(mine.shape[:axis] + (1 + len(got),) + mine.shape[axis + 1 :], BF)
                    for j, piece in enumerate([mine] + got):
                        state = lax.dynamic_update_slice_in_dim(state, piece, spot ^ j, axis)
                if not self.steps:
                    state = state.reshape(-1, d)
            self.part = state

    def finish(group, *after):
        for chain in group:
            chain.finish(*after)

    def start(group):
        for chain in group:
            chain.start()

    def together(group):
        for chain, value in zip(group, lax.optimization_barrier(tuple(chain.part for chain in group))):
            chain.part = value

    all_bits = [((place_dp >> b) & 1).reshape(1) for b in range(bits)]
    scalars = jnp.concatenate([core.reshape(1), lengths, *all_bits])
    token = []

    def meta():
        return lax.optimization_barrier((scalars, *token))[0] if token else scalars

    def done(results, *others):
        token[:] = [results[0], *others]
        return results

    merge_w = (wm, swap(wm, 1), swap(wm, 2), swap(wm, 3))
    up_w = (wu, swap(wu, 1))
    down_w = (wd, swap(wd, 1))
    vectors = jnp.stack([ig, ib, og, ob])
    qkv_w = (wq.T, wk.T, wv.T)

    fwd, att, front, far = [], [], [], []
    qkv_of = [done(project(scalars, tokens, qkv_w, 0, frames))]
    for u in range(seqs):
        fwd.append(done(attend_forward(meta(), *qkv_of[u][:3], u, frames), *(merge_w[1:] if u == 0 else ())))
        own, other = fwd[u][:2]
        att.append((own, swap(other, 1), swap(own, 2), swap(other, 3)))
        if u + 1 < seqs:
            qkv_of.append(done(project(meta(), tokens, qkv_w, u + 1, frames), up_w[1], down_w[1]))
    for u in range(seqs):
        front.append(done(ahead(meta(), tokens, att[u], merge_w, up_w, down_w, vectors, u)))
        far.append(swap(front[u][6], 2))
    out_rows, back, far_grad, smalls, sums = [], [], [], [], ()
    for u in range(seqs):
        last = u == seqs - 1
        before = (front[u][2], front[u][3], *sums) if last else ()
        res = done(astern(meta(), front[u][5], far[u], out_grad, span_starts, up_w, down_w, front[u][4], vectors, u, before))
        out_rows.append(res[0])
        back.append(res[1 if last else 3])
        smalls.append(res[3 if last else 5])
        if last:
            sent, sums = res[2], res[4:]
        else:
            far_grad.append(swap(res[4], 2))
            sums = done(weight_grads(meta(), front[u][2], res[1], front[u][3], res[2], sums))

    def inner_step(u, before):
        res = done(inner_norm(meta(), back[u], far_grad[u], front[u][0], front[u][1], vectors, att[u][:2], merge_w[:2], before))
        return res, (res[1], swap(res[2], 1))

    def attend_step(u, grads):
        return done(attend_backward(meta(), *qkv_of[u][3:], grads, fwd[u][:2], fwd[u][2], u, frames))

    def entry_step(u, grads, before):
        return done(entry_back(meta(), tokens, grads, qkv_w, before, u, frames))


    first_bit = 1 + seqs

    def scatter(step, pairs, after):
        pairs = [tuple(lax.optimization_barrier((*pair, after))[:2]) for pair in pairs]
        if step == bits:
            return done(fold(meta(), pairs, ()))
        out = done(fold(meta(), pairs, tuple(first_bit + order[step] for order in bit_orders), *(((1, 3), (0, 2)) if step == 0 else ())))
        return [(out[2 * i + 1], swap_dp(out[2 * i], 1 << bit_orders[i][step])) for i in range(2)]

    inner, entry, so_far, near, crossed = [], [], (), [], []
    out_other = [swap(r, 1) for r in out_rows]

    def exchange(out):
        got = swap(out[0], 1)
        near.append((out[1], got))
        crossed.append(swap(total(near[-1]), 2))
        return got

    for u in range(seqs):
        last = u == seqs - 1
        if u == 0:
            up_own, up_other, down_own, down_other = lax.optimization_barrier((*sums, far_grad[0]))[:4]
            moving = [(down_own, swap(down_other, 1)), (up_own, swap(up_other, 1))]
            res, grads = inner_step(0, ())
            inner.append(res)
            far_grad.append(swap(lax.optimization_barrier((sent, res[0]))[0], 2))
            moving = scatter(0, moving, res[0])
        dqkv = attend_step(u, grads)
        moving = scatter(1 + 2 * u, moving, dqkv[0])
        if not last:
            before = ()
            if u + 1 == seqs - 1:
                before = (inner[0][3], inner[0][4], inner[0][5], *smalls)
            res, grads = inner_step(u + 1, before)
            inner.append(res)
        else:
            for step in range(4, bits + 1):
                moving = scatter(step, moving, moving[0][0])
            first, second = (
                Chain(moving[i], [(b, 1) for b in order], True) for i, order in enumerate(bit_orders)
            )
            start([first, second])
            token.extend(out_other)
        out = entry_step(u, dqkv, so_far)
        entry.append(out)
        if not last:
            merge_got = swap(lax.optimization_barrier((res[4], out[0]))[0], 1)
            so_far = (out[2], res[3], merge_got)
            moving = scatter(2, moving, out[0])
            exchange(out)
    qkv = Chain(out[2], stages)
    qkv.start()

    got = exchange(out)
    layer_output = place(meta(), out_rows, out_other)

    finish([first, second], got)
    finish([qkv])
    together([qkv, first, second])
    start([qkv, first, second])
    finish([qkv, first, second], crossed[0])
    together([qkv, first, second])
    start([qkv, first])
    finish([qkv, first], crossed[1])
    together([qkv, first, second])
    start([qkv, second])
    ready = []
    for u in range(seqs):
        rest = near[u][0].astype(F32) + near[u][1].astype(F32) + crossed[u].astype(F32)
        ready.append((inner[u][0] + rest).astype(BF))
    input_grad = place(scalars, ready, [swap(r, 1) for r in ready])
    finish([qkv, second], input_grad, layer_output)
    while qkv.steps or first.steps or second.steps:
        start([qkv, first, second])
        finish([qkv, first, second])
        together([qkv, first, second])
    down_sum, up_sum, joint = (chain.part for chain in (first, second, qkv))
    qkv_sum, merge_sum = joint[:576], joint[576:]
    small = merge_sum[192:196].astype(F32)
    query_grad, key_grad, value_grad = (qkv_sum[192 * i : 192 * (i + 1)].astype(F32).T for i in range(3))
    return (
        layer_output,
        input_grad,
        query_grad,
        key_grad,
        value_grad,
        merge_sum[:192].astype(F32),
        up_sum.astype(F32),
        down_sum.astype(F32),
        small[0],
        small[1],
        small[2],
        small[3],
    )


def solution(mesh):
    in_specs = (
        P("dp", None),
        P("dp"),
        P("dp", None),
        P(None, "tensor"),
        P(None, "tensor"),
        P(None, "tensor"),
        P("tensor", None),
        P(None, "tensor"),
        P("tensor", None),
        P(),
        P(),
        P(),
        P(),
        P("dp", None),
    )
    out_specs = (
        P("dp", None),
        P("dp", None),
        P(None, "tensor"),
        P(None, "tensor"),
        P(None, "tensor"),
        P("tensor", None),
        P(None, "tensor"),
        P("tensor", None),
        P(),
        P(),
        P(),
        P(),
    )
    body = functools.partial(local, mesh.shape["dp"])
    return jax.shard_map(body, mesh=mesh, in_specs=in_specs, out_specs=out_specs, check_vma=False)
```

```python
import functools

import jax
import jax.numpy as jnp
from jax import lax
from jax.experimental import pallas as pl
from jax.experimental.pallas import tpu as pltpu
from jax.sharding import PartitionSpec as P

HEAD_DIM = 64
SPAN = 10
EPS = 1e-05
LOG2E = 1.4426950408889634
KB = 256
VMEM = 12
RB = 128
HB = 256
BF = jnp.bfloat16
F32 = jnp.float32
MIB = 1 << 20


def nn(a, b):
    return lax.dot_general(a, b, (((1,), (0,)), ((), ())), preferred_element_type=F32)


def nt(a, b):
    return lax.dot_general(a, b, (((1,), (1,)), ((), ())), preferred_element_type=F32)


def tn(a, b):
    return lax.dot_general(a, b, (((0,), (0,)), ((), ())), preferred_element_type=F32)


def params(limit):
    return pltpu.CompilerParams(vmem_limit_bytes=limit * MIB)


def cost(micros):
    return pl.CostEstimate(flops=int(micros * 1.1e9), bytes_accessed=1024, transcendentals=0)


MICROS = {"project": 3, "attend_forward": 8, "attend_backward": 12, "entry_back": 5, "place": 3, "ahead": 9, "astern": 10, "inner_norm": 3, "weight_grads": 4, "fold": 2, "joint_grads": 4, "entry_rows": 3}


def lane_parts(block):
    left = block[:, :128]
    lane = lax.broadcasted_iota(jnp.int32, left.shape, 1)
    zero = jnp.zeros_like(left)
    return (
        jnp.where(lane < HEAD_DIM, left, zero),
        jnp.where(lane >= HEAD_DIM, left, zero),
        block[:, 128:],
    )


TILE = (0, 0, 1)


def call(kernel, name, grid, meta, args, in_specs, out_specs, out_shape, scratch=(), limit=VMEM, hold=(), far=(), out=(), out_far=()):
    def place_input(i, value):
        space = pltpu.VMEM if i in hold else pltpu.HBM if i in far else None
        return value if space is None else pltpu.with_memory_space_constraint(value, space)

    def place_output(i, value):
        space = pltpu.VMEM if i in out else pltpu.HBM if i in out_far else None
        return value if space is None else space(value.shape, value.dtype)

    single = not isinstance(out_shape, list)
    return pl.pallas_call(
        kernel,
        grid_spec=pltpu.PrefetchScalarGridSpec(
            num_scalar_prefetch=1,
            grid=grid,
            in_specs=in_specs,
            out_specs=out_specs,
            scratch_shapes=scratch,
        ),
        out_shape=place_output(0, out_shape) if single else [place_output(i, o) for i, o in enumerate(out_shape)],
        compiler_params=params(limit),
        cost_estimate=cost(MICROS[name]),
        name=name,
    )(meta, *(place_input(i, value) for i, value in enumerate(args)))


def fixed(*shape):
    return pl.BlockSpec(shape, lambda *_: (0,) * len(shape))


def like(shape, dtype):
    return jax.ShapeDtypeStruct(shape, dtype)


def project_kernel(meta_ref, x_ref, wq_ref, wk_ref, wv_ref, q_ref, k_ref, v_ref):
    x = x_ref[...]
    for w_ref, o_ref in ((wq_ref, q_ref), (wk_ref, k_ref), (wv_ref, v_ref)):
        o_ref[:, :192] = nt(x, w_ref[...]).astype(BF)
        o_ref[:, 192:] = jnp.zeros((x.shape[0], HEAD_DIM), BF)


def project(meta, tokens, weights, u, frames):
    rows, d = frames, tokens.shape[1]
    block = 256
    return call(
        project_kernel,
        "project",
        (rows // block,),
        meta,
        (tokens, *weights),
        [pl.BlockSpec((block, d), lambda i, m: (u * (rows // block) + i, 0))] + [fixed(192, d)] * 3,
        [pl.BlockSpec((block, 256), lambda i, m: (i, 0))] * 3,
        [like((rows, 256), BF)] * 3,
        far=range(4),
        out=(0, 1, 2),
    )


def forward_kernel(u, meta_ref, q_ref, k_ref, v_ref, own_ref, other_ref, lse_ref, s_ref):
    length = meta_ref[1 + u]
    step = pl.program_id(0)
    blocks = lax.div(length + KB - 1, KB)
    parts = lane_parts(q_ref[...] * jnp.asarray(0.125, BF))
    width = q_ref.shape[0]

    def first(kb, highest):
        start = pl.multiple_of(kb * KB, KB)
        rows = pl.ds(start, KB)
        live = start + lax.broadcasted_iota(jnp.int32, (KB, width), 0) < length
        out = []
        for h in range(3):
            tile = pl.ds(128 * TILE[h], 128)
            s = nt(k_ref[rows, tile], parts[h])
            s = jnp.where(live, s, -1e30)
            s_ref[h, rows, :] = s
            out.append(jnp.maximum(highest[h], jnp.max(s, axis=0, keepdims=True)))
        return tuple(out)

    floor = jnp.full((1, width), -1e30, F32)
    highest = lax.fori_loop(0, blocks, first, (floor,) * 3)

    def second(kb, carry):
        rows = pl.ds(pl.multiple_of(kb * KB, KB), KB)
        out = []
        for h in range(3):
            total, result = carry[h]
            p = jnp.exp2((s_ref[h, rows, :] - highest[h]) * LOG2E)
            total = total + jnp.sum(p, axis=0, keepdims=True)
            v = v_ref[rows, pl.ds(128 * TILE[h], 128)]
            result = result + tn(v, p.astype(BF))
            out.append((total, result))
        return tuple(out)

    init = ((jnp.zeros((1, width), F32), jnp.zeros((128, width), F32)),) * 3
    done = lax.fori_loop(0, blocks, second, init)
    outs = []
    for h in range(3):
        total, result = done[h]
        lo = HEAD_DIM * (h % 2)
        o = result[lo : lo + HEAD_DIM] / total
        lse_ref[0, pl.ds(h, 1), :] = highest[h] * LOG2E + jnp.log2(total)
        outs.append(o.astype(BF))
    whole = jnp.concatenate(outs, axis=0)
    for j, o_ref in enumerate((own_ref, other_ref)):

        @pl.when(step == j)
        def _():
            o_ref[...] = whole


def attend_forward(meta, q, k, v, u, frames):
    half = frames // 2
    return call(
        functools.partial(forward_kernel, u),
        "attend_forward",
        (2,),
        meta,
        (q, k, v),
        [
            pl.BlockSpec((half, 256), lambda i, m: (i ^ m[0], 0)),
            fixed(frames, 256),
            fixed(frames, 256),
        ],
        [
            fixed(192, half),
            fixed(192, half),
            pl.BlockSpec((1, 8, half), lambda i, m: (i, 0, 0)),
        ],
        [
            like((192, half), BF),
            like((192, half), BF),
            like((2, 8, half), F32),
        ],
        [pltpu.VMEM((3, frames, half), F32)],
        hold=(0, 1, 2),
    )


def backward_kernel(
    u, meta_ref, q_ref, k_ref, v_ref, d0_ref, d1_ref, o0_ref, o1_ref, lse_ref,
    dq_ref, dk_ref, dv_ref, kt_ref, dk_acc, dv_acc, do_ref, o_ref,
):
    length = meta_ref[1 + u]
    blocks = lax.div(length + KB - 1, KB)
    step = pl.program_id(0)

    @pl.when(step == 0)
    def _():
        dk_acc[...] = jnp.zeros_like(dk_acc)
        dv_acc[...] = jnp.zeros_like(dv_acc)
        kt_ref[...] = jnp.transpose(k_ref[...])
        do_ref[...] = d0_ref[...]
        o_ref[...] = o0_ref[...]

    @pl.when(step == 1)
    def _():
        do_ref[...] = d1_ref[...]
        o_ref[...] = o1_ref[...]

    parts = lane_parts(q_ref[...] * jnp.asarray(0.125, BF))
    width = q_ref.shape[0]
    empty = jnp.zeros((HEAD_DIM, width), BF)
    head = [do_ref[pl.ds(h * HEAD_DIM, HEAD_DIM), :] for h in range(3)]
    grads = (
        jnp.concatenate([head[0], empty], axis=0),
        jnp.concatenate([empty, head[1]], axis=0),
        jnp.concatenate([head[2], empty], axis=0),
    )
    delta = [
        jnp.sum(
            head[h].astype(F32) * o_ref[pl.ds(h * HEAD_DIM, HEAD_DIM), :].astype(F32), axis=0, keepdims=True
        )
        for h in range(3)
    ]
    lse = [lse_ref[0, pl.ds(h, 1), :] for h in range(3)]

    def body(kb, carry):
        start = pl.multiple_of(kb * KB, KB)
        rows = pl.ds(start, KB)
        live = start + lax.broadcasted_iota(jnp.int32, (KB, width), 0) < length
        out = []
        for h in range(3):
            tile = pl.ds(128 * TILE[h], 128)
            s = nt(k_ref[rows, tile], parts[h])
            s = jnp.where(live, s, -1e30)
            p = jnp.exp2(s * LOG2E - lse[h])
            dp = nn(v_ref[rows, tile], grads[h])
            ds = (p * (dp - delta[h])).astype(BF)
            dv_acc[rows, tile] += nt(p.astype(BF), grads[h])
            dk_acc[rows, tile] += nn(ds, parts[h])
            kt = kt_ref[pl.ds(h * HEAD_DIM, HEAD_DIM), rows]
            out.append(carry[h] + nn(kt, ds))
        return tuple(out)

    zero = jnp.zeros((HEAD_DIM, width), F32)
    done = lax.fori_loop(0, blocks, body, (zero,) * 3)
    full = jnp.concatenate(done + (zero,), axis=0) * 0.125
    dq_ref[...] = jnp.transpose(full).astype(BF)

    @pl.when(step == 1)
    def _():
        dk_ref[...] = dk_acc[...].astype(BF)
        dv_ref[...] = dv_acc[...].astype(BF)


def attend_backward(meta, q, k, v, grads, outs, lse, u, frames):
    half = frames // 2
    return call(
        functools.partial(backward_kernel, u),
        "attend_backward",
        (2,),
        meta,
        (q, k, v, *grads, *outs, lse),
        [
            pl.BlockSpec((half, 256), lambda i, m: (i ^ m[0], 0)),
            fixed(frames, 256),
            fixed(frames, 256),
            fixed(192, half),
            fixed(192, half),
            fixed(192, half),
            fixed(192, half),
            pl.BlockSpec((1, 8, half), lambda i, m: (i, 0, 0)),
        ],
        [
            pl.BlockSpec((half, 256), lambda i, m: (i ^ m[0], 0)),
            fixed(frames, 256),
            fixed(frames, 256),
        ],
        [like((frames, 256), BF)] * 3,
        [
            pltpu.VMEM((256, frames), BF),
            pltpu.VMEM((frames, 256), F32),
            pltpu.VMEM((frames, 256), F32),
            pltpu.VMEM((192, half), BF),
            pltpu.VMEM((192, half), BF),
        ],
        hold=(3,),
        far=(0, 1, 2),
        out=(0, 1, 2),
    )


def entry_kernel(meta_ref, x_ref, dq_ref, dk_ref, dv_ref, wq_ref, wk_ref, wv_ref, send_ref, keep_ref, sum_ref, acc):
    step = pl.program_id(0)
    x = x_ref[...]
    total = jnp.zeros(x.shape, F32)
    for i, (g_ref, w_ref) in enumerate(((dq_ref, wq_ref), (dk_ref, wk_ref), (dv_ref, wv_ref))):
        rows = pl.ds(192 * i, 192)
        g = g_ref[:, :192]
        total = total + nn(g, w_ref[...])
        product = tn(g, x)

        @pl.when(step == 0)
        def _():
            acc[rows, :] = product

        @pl.when(step == 1)
        def _():
            sum_ref[rows, :] = product + acc[rows, :]

    low = total.astype(BF)

    @pl.when(step == 0)
    def _():
        send_ref[...] = low

    @pl.when(step == 1)
    def _():
        keep_ref[...] = low


def entry_back(meta, tokens, grads, weights, u, frames):
    half = frames // 2
    d = tokens.shape[1]
    return call(
        entry_kernel,
        "entry_back",
        (2,),
        meta,
        (tokens, *grads, *weights),
        [pl.BlockSpec((half, d), lambda i, m: (u * 2 + (1 - i ^ m[0]), 0))]
        + [pl.BlockSpec((half, 256), lambda i, m: (1 - i ^ m[0], 0))] * 3
        + [fixed(192, d)] * 3,
        [fixed(half, d), fixed(half, d), fixed(576, d)],
        [like((half, d), BF), like((half, d), BF), like((576, d), F32)],
        [pltpu.VMEM((576, d), F32)],
        hold=(1, 2, 3),
        far=(0, 4, 5, 6),
    )


def joint_kernel(meta_ref, x_ref, dq_ref, dk_ref, dv_ref, before_ref, m0_ref, m1_ref, sum_ref, acc):
    step = pl.program_id(0)
    x = x_ref[...]
    for i, g_ref in enumerate((dq_ref, dk_ref, dv_ref)):
        rows = pl.ds(192 * i, 192)
        product = tn(g_ref[:, :192], x)

        @pl.when(step == 0)
        def _():
            acc[rows, :] = product

        @pl.when(step == 1)
        def _():
            sum_ref[rows, :] = (product + acc[rows, :] + before_ref[rows, :]).astype(BF)

    @pl.when(step == 0)
    def _():
        sum_ref[576:, :] = (m0_ref[...].astype(F32) + m1_ref[...].astype(F32)).astype(BF)


def joint_grads(meta, tokens, grads, before, u, frames):
    half = frames // 2
    d = tokens.shape[1]
    return call(
        joint_kernel,
        "joint_grads",
        (2,),
        meta,
        (tokens, *grads, *before),
        [pl.BlockSpec((half, d), lambda i, m: (u * 2 + i, 0))]
        + [pl.BlockSpec((half, 256), lambda i, m: (i, 0))] * 3
        + [fixed(*value.shape) for value in before],
        [fixed(832, d)],
        [like((832, d), BF)],
        [pltpu.VMEM((576, d), F32)],
        hold=(1, 2, 3),
        far=(0,),
    )


def rows_kernel(meta_ref, dq_ref, dk_ref, dv_ref, wq_ref, wk_ref, wv_ref, send_ref, keep_ref):
    total = sum(nn(g[:, :192], w[...]) for g, w in ((dq_ref, wq_ref), (dk_ref, wk_ref), (dv_ref, wv_ref)))
    for j, o_ref in enumerate((send_ref, keep_ref)):

        @pl.when(pl.program_id(0) == j)
        def _():
            o_ref[...] = total.astype(BF)


def entry_rows(meta, grads, weights, frames):
    half = frames // 2
    d = weights[0].shape[1]
    return call(
        rows_kernel,
        "entry_rows",
        (2,),
        meta,
        (*grads, *weights),
        [pl.BlockSpec((half, 256), lambda i, m: (1 - i ^ m[0], 0))] * 3 + [fixed(192, d)] * 3,
        [fixed(half, d), fixed(half, d)],
        [like((half, d), BF), like((half, d), BF)],
        hold=(0, 1, 2),
        far=(3, 4, 5),
    )


def place_kernel(meta_ref, *refs):
    o_ref = refs[-1]
    for i, r_ref in enumerate(refs[:-1]):

        @pl.when(pl.program_id(0) == i)
        def _():
            o_ref[...] = r_ref[...]


def place(meta, own, other):
    half, d = own[0].shape
    count = 2 * len(own)
    return call(
        place_kernel,
        "place",
        (count,),
        meta,
        [block for pair in zip(own, other) for block in pair],
        [fixed(half, d)] * count,
        pl.BlockSpec((half, d), lambda i, m: (i ^ m[0], 0)),
        like((count * half, d), own[0].dtype),
    )


def normalise(values):
    average = jnp.mean(values, axis=-1, keepdims=True)
    centred = values - average
    spread = jnp.mean(centred * centred, axis=-1, keepdims=True)
    rstd = lax.rsqrt(spread + EPS)
    return centred * rstd, rstd


def gelu_pair(v):
    e = jnp.exp2(v * v * (-0.5 * LOG2E))
    t = 1.0 / (1.0 + (0.3275911 * 0.7071067811865476) * jnp.abs(v))
    poly = t * (0.5 * 0.254829592 + t * (0.5 * -0.284496736 + t * (0.5 * 1.421413741 + t * (0.5 * -1.453152027 + t * (0.5 * 1.061405429)))))
    tail = poly * e
    phi_cap = jnp.where(v >= 0, 1.0 - tail, tail)
    return v * phi_cap, phi_cap + v * (e * 0.3989422804014327)


def ahead_kernel(
    meta_ref, tok_ref, a0, a1, a2, a3, w0, w1, w2, w3, ua_ref, ub_ref, da_ref, db_ref, vec_ref,
    xhat_ref, rstd_ref, low_ref, act_ref, slope_ref, own_ref, sent_ref,
):
    gain, bias = vec_ref[0:1, :], vec_ref[1:2, :]
    hidden = ua_ref.shape[1]
    for r in range(tok_ref.shape[0] // RB):
        rows = pl.ds(r * RB, RB)
        branch = jnp.zeros((RB, tok_ref.shape[1]), F32)
        for a, w in ((a0, w0), (a1, w1), (a2, w2), (a3, w3)):
            branch = branch + tn(a[:, rows], w[...]).astype(BF).astype(F32)
        xhat, rstd = normalise(tok_ref[rows, :].astype(F32) + branch)
        xhat_ref[rows, :] = xhat
        rstd_ref[rows, :] = jnp.broadcast_to(rstd, (RB, rstd_ref.shape[1]))
        normed = xhat * gain + bias
        low = normed.astype(BF)
        low_ref[rows, :] = low
        sent = jnp.zeros(normed.shape, F32)
        for g, (up, down) in enumerate(((ua_ref, da_ref), (ub_ref, db_ref))):
            acts = []
            for c in range(hidden // HB):
                act, slope = gelu_pair(nn(low, up[:, c * HB : (c + 1) * HB]))
                columns = pl.ds(g * hidden + c * HB, HB)
                acts.append(act.astype(BF))
                act_ref[rows, columns] = acts[-1]
                slope_ref[rows, columns] = slope.astype(BF)
            sent = sent + nn(jnp.concatenate(acts, axis=1), down[...]).astype(BF).astype(F32)
        own_ref[rows, :] = normed + sent
        sent_ref[rows, :] = sent.astype(BF)


def ahead(meta, tokens, att, merge_w, up, down, vectors, u):
    half = att[0].shape[1]
    d, hidden = up[0].shape
    return call(
        ahead_kernel,
        "ahead",
        (1,),
        meta,
        (tokens, *att, *merge_w, *up, *down, vectors),
        [pl.BlockSpec((half, d), lambda i, m: (u * 2 + m[0], 0))]
        + [fixed(192, half)] * 4
        + [fixed(192, d)] * 4
        + [fixed(d, hidden)] * 2
        + [fixed(hidden, d)] * 2
        + [fixed(4, d)],
        [fixed(half, d), fixed(half, 128), fixed(half, d), fixed(half, 2 * hidden), fixed(half, 2 * hidden), fixed(half, d), fixed(half, d)],
        [
            like((half, d), F32),
            like((half, 128), F32),
            like((half, d), BF),
            like((half, 2 * hidden), BF),
            like((half, 2 * hidden), BF),
            like((half, d), F32),
            like((half, d), BF),
        ],
        far=(0,),
        out=(2, 3, 4, 5),
        out_far=(0, 1),
    )


def astern_kernel(u, meta_ref, own_ref, far_ref, grad_ref, span_ref, ua_ref, ub_ref, da_ref, db_ref, slope_ref, vec_ref, *refs):
    last = len(refs) > 6
    if last:
        before = refs[:-10]
        out_ref, back_ref, sent_ref, small_ref, *sums, g_ref, pre_ref = refs[-10:]
    else:
        out_ref, g_ref, pre_ref, back_ref, sent_ref, small_ref = refs
    gain, bias = vec_ref[2:3, :], vec_ref[3:4, :]
    half, d = own_ref.shape
    hidden = ua_ref.shape[1]
    starts = span_ref[u : u + 1, :]
    gain_grad = jnp.zeros(gain.shape, F32)
    bias_grad = jnp.zeros(gain.shape, F32)
    for r in range(half // RB):
        rows = pl.ds(r * RB, RB)
        xhat, rstd = normalise(own_ref[rows, :] + far_ref[rows, :].astype(F32))
        out_ref[rows, :] = (xhat * gain + bias).astype(BF)
        frame = meta_ref[0] * half + r * RB + lax.broadcasted_iota(jnp.int32, (RB, starts.shape[1]), 0)
        inside = (frame >= starts) & (frame < starts + SPAN)
        weight = jnp.max(jnp.where(inside, 1.0, 0.0), axis=1, keepdims=True)
        cot = grad_ref[rows, :].astype(F32) * weight
        gain_grad = gain_grad + jnp.sum(cot * xhat, axis=0, keepdims=True)
        bias_grad = bias_grad + jnp.sum(cot, axis=0, keepdims=True)
        gy = cot * gain
        mean_gy = jnp.mean(gy, axis=-1, keepdims=True)
        mean_gx = jnp.mean(gy * xhat, axis=-1, keepdims=True)
        sum_grad = rstd * (gy - mean_gy - xhat * mean_gx)
        low = sum_grad.astype(BF)
        g_ref[rows, :] = low
        sent = jnp.zeros(sum_grad.shape, F32)
        for g, (up, down) in enumerate(((ua_ref, da_ref), (ub_ref, db_ref))):
            pres = []
            for c in range(hidden // HB):
                columns = pl.ds(g * hidden + c * HB, HB)
                slope = slope_ref[rows, columns].astype(F32)
                pres.append((nt(low, down[c * HB : (c + 1) * HB, :]) * slope).astype(BF))
                pre_ref[rows, columns] = pres[-1]
            sent = sent + nt(jnp.concatenate(pres, axis=1), up[...]).astype(BF).astype(F32)
        back_ref[rows, :] = sum_grad + sent
        sent_ref[rows, :] = sent.astype(BF)
    small_ref[0:1, :] = gain_grad
    small_ref[1:2, :] = bias_grad
    if last:
        x_ref, act_ref = before[:2]
        weight_sums(x_ref[...], g_ref[...], act_ref, pre_ref, before[2:], sums)


def astern(meta, own, far, grad, spans, up, down, slope, vectors, u, before):
    half, d = own.shape
    hidden = up[0].shape[1]
    rows = fixed(half, d)
    wide = fixed(half, 2 * hidden)
    grads = [] if not before else [(d, hidden)] * 2 + [(hidden, d)] * 2
    extra = [] if not before else [rows, wide] + [fixed(*shape) for shape in grads[: len(before) - 2]]
    made = [like((half, d), BF), like((half, 2 * hidden), BF)]
    others = [like((half, d), F32), like((half, d), BF), like((2, d), F32)]
    shapes = [like((half, d), BF)] + ([] if before else made) + others + [like(shape, BF) for shape in grads]
    return call(
        functools.partial(astern_kernel, u),
        "astern",
        (1,),
        meta,
        (own, far, grad, spans, *up, *down, slope, vectors, *before),
        [rows] * 2
        + [pl.BlockSpec((half, d), lambda i, m: (u * 2 + m[0], 0)), fixed(*spans.shape)]
        + [fixed(d, hidden)] * 2
        + [fixed(hidden, d)] * 2
        + [wide, fixed(4, d)]
        + extra,
        [fixed(*shape.shape) for shape in shapes],
        shapes,
        [pltpu.VMEM(shape.shape, shape.dtype) for shape in made] if before else (),
        limit=20 if before else VMEM,
        hold=(0, 8, *range(10, 10 + len(before))),
        far=(2,),
        out=() if before else (1, 2),
        out_far=(0, 1) if before else (0, 3),
    )


def weight_kernel(meta_ref, x_ref, g_ref, act_ref, pre_ref, *refs):
    before, sums = refs[:-4], refs[-4:]
    weight_sums(x_ref[...], g_ref[...], act_ref, pre_ref, before, sums)


def weight_sums(x, g, act_ref, pre_ref, before, sums):
    hidden = act_ref.shape[1] // 2
    for i in range(2):
        for c in range(hidden // HB):
            columns = pl.ds(i * hidden + c * HB, HB)
            block = pl.ds(c * HB, HB)
            up = tn(x, pre_ref[:, columns])
            down = tn(act_ref[:, columns], g)
            if before:
                up = up + before[i][:, block].astype(F32)
                down = down + before[2 + i][block, :].astype(F32)
            sums[i][:, block] = up.astype(BF)
            sums[2 + i][block, :] = down.astype(BF)


def weight_grads(meta, x, g, act, pre, before):
    rows, d = x.shape
    hidden = act.shape[1] // 2
    shapes = [(d, hidden)] * 2 + [(hidden, d)] * 2
    return call(
        weight_kernel,
        "weight_grads",
        (1,),
        meta,
        (x, g, act, pre, *before),
        [fixed(rows, d)] * 2 + [fixed(rows, 2 * hidden)] * 2 + [fixed(*shape) for shape in shapes[: len(before)]],
        [fixed(*shape) for shape in shapes],
        [like(shape, BF) for shape in shapes],
        hold=(0, 1, 2, 3),
        out=(0, 1, 2, 3),
    )


def inner_kernel(meta_ref, own_ref, far_ref, xhat_ref, rstd_ref, vec_ref, a0, a1, w0, w1, *refs):
    last = len(refs) == 11
    out_ref, g0, g1, m0, m1, small_ref = refs[-6:]
    grad = own_ref[...] + far_ref[...].astype(F32)
    xhat = xhat_ref[...]
    gain_grad = jnp.sum(grad * xhat, axis=0, keepdims=True)
    bias_grad = jnp.sum(grad, axis=0, keepdims=True)
    gy = grad * vec_ref[0:1, :]
    mean_gy = jnp.mean(gy, axis=-1, keepdims=True)
    mean_gx = jnp.mean(gy * xhat, axis=-1, keepdims=True)
    inner = rstd_ref[:, 0:1] * (gy - mean_gy - xhat * mean_gx)
    out_ref[...] = inner
    low = inner.astype(BF)
    g0[...] = nt(w0[...], low).astype(BF)
    g1[...] = nt(w1[...], low).astype(BF)
    small = jnp.concatenate([gain_grad, bias_grad], axis=0)
    small_ref[...] = small
    if last:
        before0, before1, before_small, outer0, outer1 = refs[:5]
        below = jnp.concatenate(
            [small + before_small[...], outer0[...] + outer1[...], jnp.zeros((60, small.shape[1]), F32)], axis=0
        ).astype(BF)
        for m, a, before in ((m0, a0, before0), (m1, a1, before1)):
            m[:192, :] = (nn(a[...], low) + before[...]).astype(BF)
            m[192:, :] = below
    else:
        m0[...] = nn(a0[...], low)
        m1[...] = nn(a1[...], low)


def inner_norm(meta, own, far, xhat, rstd, vectors, att, weights, before):
    rows, d = xhat.shape
    merge = like((256, d), BF) if before else like((192, d), F32)
    return call(
        inner_kernel,
        "inner_norm",
        (1,),
        meta,
        (own, far, xhat, rstd, vectors, *att, *weights, *before),
        [fixed(rows, d)] * 3
        + [fixed(rows, 128), fixed(4, d)]
        + [fixed(192, rows)] * 2
        + [fixed(192, d)] * 2
        + ([fixed(192, d)] * 2 + [fixed(2, d)] * 3 if before else []),
        [fixed(rows, d), fixed(192, rows), fixed(192, rows), fixed(*merge.shape), fixed(*merge.shape), fixed(2, d)],
        [like((rows, d), F32), like((192, rows), BF), like((192, rows), BF), merge, merge, like((2, d), F32)],
        far=(0, 2, 3, 5, 6, 7, 8, *((9, 10) if before else ())),
        out=(1,),
        out_far=(0,) if before else (0, 3, 4),
    )


def fold_kernel(bits, meta_ref, *refs):
    for i in range(2):
        here, there = refs[2 * i : 2 * i + 2]
        if bits:
            send, keep = refs[4 + 2 * i : 6 + 2 * i]
            half = send.shape[0]
            bit = meta_ref[bits[i]]
            for part, j in ((send, 1 - bit), (keep, bit)):
                rows = pl.ds(pl.multiple_of(j * half, 16), half)
                part[...] = (here[rows, :].astype(F32) + there[rows, :].astype(F32)).astype(BF)
        else:
            refs[4 + i][...] = (here[...].astype(F32) + there[...].astype(F32)).astype(BF)


def fold(meta, pairs, bits, hold=()):
    args = [value for pair in pairs for value in pair]
    rows, d = args[0].shape
    shapes = [like((rows // 2, d), BF)] * 4 if bits else [like((rows, d), BF)] * 2
    return call(
        functools.partial(fold_kernel, bits),
        "fold",
        (1,),
        meta,
        args,
        [fixed(rows, d)] * 4,
        [fixed(*shape.shape) for shape in shapes],
        shapes,
        hold=hold,
    )


def local(groups, tokens, lengths, span_starts, wq, wk, wv, wm, wu, wd, ig, ib, og, ob, out_grad):
    rows, d = tokens.shape
    seqs = lengths.shape[0]
    frames = rows // seqs
    half = frames // 2
    core = lax.axis_index("tensor") % 2
    place_dp = lax.axis_index("dp")
    bits = groups.bit_length() - 1

    def swap(value, k):
        return lax.ppermute(value, "tensor", [(i, i ^ k) for i in range(4)])

    def swap_dp(value, k):
        return lax.ppermute(value, "dp", [(i, i ^ k) for i in range(groups)])

    def add(a, b):
        return (a.astype(F32) + b.astype(F32)).astype(BF)

    def total(pieces):
        return sum(piece.astype(F32) for piece in pieces).astype(BF) if len(pieces) > 1 else pieces[0]

    stages = [(0, 1)] + [(b, 2) for b in range(1, bits - 1, 2)] + ([(bits - 1, 1)] if bits % 2 == 0 else [])
    bit_orders = (list(range(bits)), [1, 0, *range(2, bits)])

    def spot_of(stage):
        return (place_dp >> stage[0]) & ((1 << stage[1]) - 1)

    class Chain:
        def __init__(self, part, order, cut_already=False):
            self.part = part.reshape((1,) * len(order) + part.shape) if cut_already else part
            self.order = order
            self.steps = [] if cut_already else [(True, stage) for stage in order]
            self.steps += [(False, stage) for stage in reversed(order)]

        def cut(self, stage, j):
            size = self.part.shape[0] >> stage[1]
            return lax.dynamic_slice_in_dim(self.part, (spot_of(stage) ^ j) * size, size, 0)

        def start(self):
            if self.steps:
                scatter, stage = self.steps[0]
                others = range(1, 1 << stage[1])
                self.pending = [swap_dp(self.cut(stage, j) if scatter else self.part, j << stage[0]) for j in others]

        def finish(self, *after):
            if not self.steps:
                return
            scatter, stage = self.steps.pop(0)
            got = self.pending
            if after:
                got = list(lax.optimization_barrier((*got, *after))[: len(got)])
            if scatter:
                state = total([self.cut(stage, 0)] + got)
                if not self.steps[0][0]:
                    state = state.reshape((1,) * len(self.order) + state.shape)
            else:
                axis = self.order.index(stage)
                spot = spot_of(stage)
                mine = self.part
                if len(got) == 1:
                    laid = [jnp.where(spot, got[0], mine), jnp.where(spot, mine, got[0])]
                    state = jnp.concatenate(laid, axis=axis)
                else:
                    state = jnp.zeros(mine.shape[:axis] + (1 + len(got),) + mine.shape[axis + 1 :], BF)
                    for j, piece in enumerate([mine] + got):
                        state = lax.dynamic_update_slice_in_dim(state, piece, spot ^ j, axis)
                if not self.steps:
                    state = state.reshape(-1, d)
            self.part = state

    def finish(group, *after):
        for chain in group:
            chain.finish(*after)

    def start(group):
        for chain in group:
            chain.start()

    def together(group):
        for chain, value in zip(group, lax.optimization_barrier(tuple(chain.part for chain in group))):
            chain.part = value

    all_bits = [((place_dp >> b) & 1).reshape(1) for b in range(bits)]
    scalars = jnp.concatenate([core.reshape(1), lengths, *all_bits])
    token = []

    def meta():
        return lax.optimization_barrier((scalars, *token))[0] if token else scalars

    def done(results, *others):
        token[:] = [results[0], *others]
        return results

    merge_w = (wm, swap(wm, 1), swap(wm, 2), swap(wm, 3))
    up_w = (wu, swap(wu, 1))
    down_w = (wd, swap(wd, 1))
    vectors = jnp.stack([ig, ib, og, ob])
    qkv_w = (wq.T, wk.T, wv.T)

    fwd, att, front, far = [], [], [], []
    qkv_of = [done(project(scalars, tokens, qkv_w, 0, frames))]
    for u in range(seqs):
        fwd.append(done(attend_forward(meta(), *qkv_of[u], u, frames), *(merge_w[1:] if u == 0 else ())))
        own, other = fwd[u][:2]
        att.append((own, swap(other, 1), swap(own, 2), swap(other, 3)))
        if u + 1 < seqs:
            qkv_of.append(done(project(meta(), tokens, qkv_w, u + 1, frames), up_w[1], down_w[1]))
    for u in range(seqs):
        front.append(done(ahead(meta(), tokens, att[u], merge_w, up_w, down_w, vectors, u)))
        far.append(swap(front[u][6], 2))
    out_rows, back, far_grad, smalls, sums = [], [], [], [], ()
    for u in range(seqs):
        last = u == seqs - 1
        before = (front[u][2], front[u][3], *sums) if last else ()
        res = done(astern(meta(), front[u][5], far[u], out_grad, span_starts, up_w, down_w, front[u][4], vectors, u, before))
        out_rows.append(res[0])
        back.append(res[1 if last else 3])
        smalls.append(res[3 if last else 5])
        if last:
            sent, sums = res[2], res[4:]
        else:
            far_grad.append(swap(res[4], 2))
            sums = done(weight_grads(meta(), front[u][2], res[1], front[u][3], res[2], sums))

    def inner_step(u, before):
        res = done(inner_norm(meta(), back[u], far_grad[u], front[u][0], front[u][1], vectors, att[u][:2], merge_w[:2], before))
        return res, (res[1], swap(res[2], 1))

    def attend_step(u, grads):
        return done(attend_backward(meta(), *qkv_of[u], grads, fwd[u][:2], fwd[u][2], u, frames))

    def entry_step(u, grads):
        return done(entry_back(meta(), tokens, grads, qkv_w, u, frames))


    first_bit = 1 + seqs

    def scatter(step, pairs, after, hold=()):
        pairs = [tuple(lax.optimization_barrier((*pair, after))[:2]) for pair in pairs]
        if step == bits:
            return done(fold(meta(), pairs, (), hold))
        out = done(fold(meta(), pairs, tuple(first_bit + order[step] for order in bit_orders), hold))
        return [(out[2 * i + 1], swap_dp(out[2 * i], 1 << bit_orders[i][step])) for i in range(2)]

    inner, so_far, near, crossed = [], (), [], []
    out_other = [swap(r, 1) for r in out_rows]

    def exchange(out):
        got = swap(out[0], 1)
        near.append((out[1], got))
        crossed.append(swap(total(near[-1]), 2))
        return got

    for u in range(seqs):
        last = u == seqs - 1
        if u == 0:
            up_own, up_other, down_own, down_other = lax.optimization_barrier((*sums, far_grad[0]))[:4]
            moving = [(down_own, swap(down_other, 1)), (up_own, swap(up_other, 1))]
            res, grads = inner_step(0, ())
            inner.append(res)
            far_grad.append(swap(lax.optimization_barrier((sent, res[0]))[0], 2))
            moving = scatter(0, moving, res[0])
        dqkv = attend_step(u, grads)
        moving = scatter(1 + 2 * u, moving, dqkv[0])
        if not last:
            before = ()
            if u + 1 == seqs - 1:
                before = (inner[0][3], inner[0][4], inner[0][5], *smalls)
            res, grads = inner_step(u + 1, before)
            inner.append(res)
        else:
            for step in range(4, bits + 1):
                moving = scatter(step, moving, moving[0][0])
            first, second = (
                Chain(moving[i], [(b, 1) for b in order], True) for i, order in enumerate(bit_orders)
            )
            start([first, second])
            token.extend(out_other)
        if last:
            qkv = Chain(done(joint_grads(meta(), tokens, dqkv, so_far, u, frames))[0], stages)
            qkv.start()
            out = done(entry_rows(meta(), dqkv, qkv_w, frames))
        else:
            out = entry_step(u, dqkv)
            merge_got = swap(lax.optimization_barrier((res[4], out[0]))[0], 1)
            so_far = (out[2], res[3], merge_got)
            moving = scatter(2, moving, out[0])
            exchange(out)

    got = exchange(out)
    layer_output = place(meta(), out_rows, out_other)

    finish([first, second], got)
    finish([qkv])
    together([qkv, first, second])
    start([qkv, first, second])
    finish([qkv, first, second], crossed[0])
    together([qkv, first, second])
    start([qkv, first])
    finish([qkv, first], crossed[1])
    together([qkv, first, second])
    start([qkv, second])
    ready = []
    for u in range(seqs):
        rest = near[u][0].astype(F32) + near[u][1].astype(F32) + crossed[u].astype(F32)
        ready.append((inner[u][0] + rest).astype(BF))
    input_grad = place(scalars, ready, [swap(r, 1) for r in ready])
    finish([qkv, second], input_grad, layer_output)
    while qkv.steps or first.steps or second.steps:
        start([qkv, first, second])
        finish([qkv, first, second])
        together([qkv, first, second])
    down_sum, up_sum, joint = (chain.part for chain in (first, second, qkv))
    qkv_sum, merge_sum = joint[:576], joint[576:]
    small = merge_sum[192:196].astype(F32)
    query_grad, key_grad, value_grad = (qkv_sum[192 * i : 192 * (i + 1)].astype(F32).T for i in range(3))
    return (
        layer_output,
        input_grad,
        query_grad,
        key_grad,
        value_grad,
        merge_sum[:192].astype(F32),
        up_sum.astype(F32),
        down_sum.astype(F32),
        small[0],
        small[1],
        small[2],
        small[3],
    )


def solution(mesh):
    in_specs = (
        P("dp", None),
        P("dp"),
        P("dp", None),
        P(None, "tensor"),
        P(None, "tensor"),
        P(None, "tensor"),
        P("tensor", None),
        P(None, "tensor"),
        P("tensor", None),
        P(),
        P(),
        P(),
        P(),
        P("dp", None),
    )
    out_specs = (
        P("dp", None),
        P("dp", None),
        P(None, "tensor"),
        P(None, "tensor"),
        P(None, "tensor"),
        P("tensor", None),
        P(None, "tensor"),
        P("tensor", None),
        P(),
        P(),
        P(),
        P(),
    )
    body = functools.partial(local, mesh.shape["dp"])
    return jax.shard_map(body, mesh=mesh, in_specs=in_specs, out_specs=out_specs, check_vma=False)
```

```python
import functools

import jax
import jax.numpy as jnp
from jax import lax
from jax.experimental import pallas as pl
from jax.experimental.pallas import tpu as pltpu
from jax.sharding import PartitionSpec as P

HEAD_DIM = 64
SPAN = 10
EPS = 1e-05
LOG2E = 1.4426950408889634
KF = 1024
KB = 512
VMEM = 12
RB = 128
HB = 256
BF = jnp.bfloat16
F32 = jnp.float32
MIB = 1 << 20


def nn(a, b):
    return lax.dot_general(a, b, (((1,), (0,)), ((), ())), preferred_element_type=F32)


def nt(a, b):
    return lax.dot_general(a, b, (((1,), (1,)), ((), ())), preferred_element_type=F32)


def tn(a, b):
    return lax.dot_general(a, b, (((0,), (0,)), ((), ())), preferred_element_type=F32)


def params(limit):
    return pltpu.CompilerParams(vmem_limit_bytes=limit * MIB)


def cost(micros):
    return pl.CostEstimate(flops=int(micros * 1.1e9), bytes_accessed=1024, transcendentals=0)


MICROS = {"project": 3, "attend_forward": 8, "attend_backward": 12, "entry_back": 5, "place": 3, "ahead": 9, "astern": 10, "inner_norm": 3, "weight_grads": 4, "fold": 2, "joint_grads": 4, "entry_rows": 3}


def lane_parts(block):
    left = block[:, :128]
    lane = lax.broadcasted_iota(jnp.int32, left.shape, 1)
    zero = jnp.zeros_like(left)
    return (
        jnp.where(lane < HEAD_DIM, left, zero),
        jnp.where(lane >= HEAD_DIM, left, zero),
        block[:, 128:],
    )


TILE = (0, 0, 1)


def call(kernel, name, grid, meta, args, in_specs, out_specs, out_shape, scratch=(), limit=VMEM, hold=(), far=(), out=(), out_far=()):
    def place_input(i, value):
        space = pltpu.VMEM if i in hold else pltpu.HBM if i in far else None
        return value if space is None else pltpu.with_memory_space_constraint(value, space)

    def place_output(i, value):
        space = pltpu.VMEM if i in out else pltpu.HBM if i in out_far else None
        return value if space is None else space(value.shape, value.dtype)

    single = not isinstance(out_shape, list)
    return pl.pallas_call(
        kernel,
        grid_spec=pltpu.PrefetchScalarGridSpec(
            num_scalar_prefetch=1,
            grid=grid,
            in_specs=in_specs,
            out_specs=out_specs,
            scratch_shapes=scratch,
        ),
        out_shape=place_output(0, out_shape) if single else [place_output(i, o) for i, o in enumerate(out_shape)],
        compiler_params=params(limit),
        cost_estimate=cost(MICROS[name]),
        name=name,
    )(meta, *(place_input(i, value) for i, value in enumerate(args)))


def fixed(*shape):
    return pl.BlockSpec(shape, lambda *_: (0,) * len(shape))


def like(shape, dtype):
    return jax.ShapeDtypeStruct(shape, dtype)


def project_kernel(meta_ref, x_ref, wq_ref, wk_ref, wv_ref, q_ref, k_ref, v_ref):
    x = x_ref[...]
    for w_ref, o_ref in ((wq_ref, q_ref), (wk_ref, k_ref), (wv_ref, v_ref)):
        o_ref[:, :192] = nt(x, w_ref[...]).astype(BF)
        o_ref[:, 192:] = jnp.zeros((x.shape[0], HEAD_DIM), BF)


def project(meta, tokens, weights, u, frames):
    rows, d = frames, tokens.shape[1]
    block = 256
    return call(
        project_kernel,
        "project",
        (rows // block,),
        meta,
        (tokens, *weights),
        [pl.BlockSpec((block, d), lambda i, m: (u * (rows // block) + i, 0))] + [fixed(192, d)] * 3,
        [pl.BlockSpec((block, 256), lambda i, m: (i, 0))] * 3,
        [like((rows, 256), BF)] * 3,
        far=range(4),
        out=(0, 1, 2),
    )


def forward_kernel(u, meta_ref, q_ref, k_ref, v_ref, own_ref, other_ref, lse_ref, s_ref):
    length = meta_ref[1 + u]
    step = pl.program_id(0)
    blocks = lax.div(length + KF - 1, KF)
    parts = lane_parts(q_ref[...] * jnp.asarray(0.125, BF))
    width = q_ref.shape[0]

    def first(kb, highest):
        start = pl.multiple_of(kb * KF, KF)
        rows = pl.ds(start, KF)
        live = start + lax.broadcasted_iota(jnp.int32, (KF, width), 0) < length
        out = []
        for h in range(3):
            tile = pl.ds(128 * TILE[h], 128)
            s = nt(k_ref[rows, tile], parts[h])
            s = jnp.where(live, s, -1e30)
            s_ref[h, rows, :] = s
            out.append(jnp.maximum(highest[h], jnp.max(s, axis=0, keepdims=True)))
        return tuple(out)

    floor = jnp.full((1, width), -1e30, F32)
    highest = lax.fori_loop(0, blocks, first, (floor,) * 3)

    def second(kb, carry):
        rows = pl.ds(pl.multiple_of(kb * KF, KF), KF)
        out = []
        for h in range(3):
            total, result = carry[h]
            p = jnp.exp2((s_ref[h, rows, :] - highest[h]) * LOG2E)
            total = total + jnp.sum(p, axis=0, keepdims=True)
            v = v_ref[rows, pl.ds(128 * TILE[h], 128)]
            result = result + tn(v, p.astype(BF))
            out.append((total, result))
        return tuple(out)

    init = ((jnp.zeros((1, width), F32), jnp.zeros((128, width), F32)),) * 3
    done = lax.fori_loop(0, blocks, second, init)
    outs = []
    for h in range(3):
        total, result = done[h]
        lo = HEAD_DIM * (h % 2)
        o = result[lo : lo + HEAD_DIM] / total
        lse_ref[0, pl.ds(h, 1), :] = highest[h] * LOG2E + jnp.log2(total)
        outs.append(o.astype(BF))
    whole = jnp.concatenate(outs, axis=0)
    for j, o_ref in enumerate((own_ref, other_ref)):

        @pl.when(step == j)
        def _():
            o_ref[...] = whole


def attend_forward(meta, q, k, v, u, frames):
    half = frames // 2
    return call(
        functools.partial(forward_kernel, u),
        "attend_forward",
        (2,),
        meta,
        (q, k, v),
        [
            pl.BlockSpec((half, 256), lambda i, m: (i ^ m[0], 0)),
            fixed(frames, 256),
            fixed(frames, 256),
        ],
        [
            fixed(192, half),
            fixed(192, half),
            pl.BlockSpec((1, 8, half), lambda i, m: (i, 0, 0)),
        ],
        [
            like((192, half), BF),
            like((192, half), BF),
            like((2, 8, half), F32),
        ],
        [pltpu.VMEM((3, frames, half), F32)],
        hold=(0, 1, 2),
    )


def backward_kernel(
    u, meta_ref, q_ref, k_ref, v_ref, d0_ref, d1_ref, o0_ref, o1_ref, lse_ref,
    dq_ref, dk_ref, dv_ref, kt_ref, dk_acc, dv_acc, do_ref, o_ref,
):
    length = meta_ref[1 + u]
    blocks = lax.div(length + KB - 1, KB)
    step = pl.program_id(0)

    @pl.when(step == 0)
    def _():
        dk_acc[...] = jnp.zeros_like(dk_acc)
        dv_acc[...] = jnp.zeros_like(dv_acc)
        kt_ref[...] = jnp.transpose(k_ref[...])
        do_ref[...] = d0_ref[...]
        o_ref[...] = o0_ref[...]

    @pl.when(step == 1)
    def _():
        do_ref[...] = d1_ref[...]
        o_ref[...] = o1_ref[...]

    parts = lane_parts(q_ref[...] * jnp.asarray(0.125, BF))
    width = q_ref.shape[0]
    empty = jnp.zeros((HEAD_DIM, width), BF)
    head = [do_ref[pl.ds(h * HEAD_DIM, HEAD_DIM), :] for h in range(3)]
    grads = (
        jnp.concatenate([head[0], empty], axis=0),
        jnp.concatenate([empty, head[1]], axis=0),
        jnp.concatenate([head[2], empty], axis=0),
    )
    delta = [
        jnp.sum(
            head[h].astype(F32) * o_ref[pl.ds(h * HEAD_DIM, HEAD_DIM), :].astype(F32), axis=0, keepdims=True
        )
        for h in range(3)
    ]
    lse = [lse_ref[0, pl.ds(h, 1), :] for h in range(3)]

    def body(kb, carry):
        start = pl.multiple_of(kb * KB, KB)
        rows = pl.ds(start, KB)
        live = start + lax.broadcasted_iota(jnp.int32, (KB, width), 0) < length
        out = []
        for h in range(3):
            tile = pl.ds(128 * TILE[h], 128)
            s = nt(k_ref[rows, tile], parts[h])
            s = jnp.where(live, s, -1e30)
            p = jnp.exp2(s * LOG2E - lse[h])
            dp = nn(v_ref[rows, tile], grads[h])
            ds = (p * (dp - delta[h])).astype(BF)
            dv_acc[rows, tile] += nt(p.astype(BF), grads[h])
            dk_acc[rows, tile] += nn(ds, parts[h])
            kt = kt_ref[pl.ds(h * HEAD_DIM, HEAD_DIM), rows]
            out.append(carry[h] + nn(kt, ds))
        return tuple(out)

    zero = jnp.zeros((HEAD_DIM, width), F32)
    done = lax.fori_loop(0, blocks, body, (zero,) * 3)
    full = jnp.concatenate(done + (zero,), axis=0) * 0.125
    dq_ref[...] = jnp.transpose(full).astype(BF)

    @pl.when(step == 1)
    def _():
        dk_ref[...] = dk_acc[...].astype(BF)
        dv_ref[...] = dv_acc[...].astype(BF)


def attend_backward(meta, q, k, v, grads, outs, lse, u, frames):
    half = frames // 2
    return call(
        functools.partial(backward_kernel, u),
        "attend_backward",
        (2,),
        meta,
        (q, k, v, *grads, *outs, lse),
        [
            pl.BlockSpec((half, 256), lambda i, m: (i ^ m[0], 0)),
            fixed(frames, 256),
            fixed(frames, 256),
            fixed(192, half),
            fixed(192, half),
            fixed(192, half),
            fixed(192, half),
            pl.BlockSpec((1, 8, half), lambda i, m: (i, 0, 0)),
        ],
        [
            pl.BlockSpec((half, 256), lambda i, m: (i ^ m[0], 0)),
            fixed(frames, 256),
            fixed(frames, 256),
        ],
        [like((frames, 256), BF)] * 3,
        [
            pltpu.VMEM((256, frames), BF),
            pltpu.VMEM((frames, 256), F32),
            pltpu.VMEM((frames, 256), F32),
            pltpu.VMEM((192, half), BF),
            pltpu.VMEM((192, half), BF),
        ],
        hold=(3,),
        far=(0, 1, 2),
        out=(0, 1, 2),
    )


def entry_kernel(meta_ref, x_ref, dq_ref, dk_ref, dv_ref, wq_ref, wk_ref, wv_ref, send_ref, keep_ref, sum_ref, acc):
    step = pl.program_id(0)
    x = x_ref[...]
    total = jnp.zeros(x.shape, F32)
    for i, (g_ref, w_ref) in enumerate(((dq_ref, wq_ref), (dk_ref, wk_ref), (dv_ref, wv_ref))):
        rows = pl.ds(192 * i, 192)
        g = g_ref[:, :192]
        total = total + nn(g, w_ref[...])
        product = tn(g, x)

        @pl.when(step == 0)
        def _():
            acc[rows, :] = product

        @pl.when(step == 1)
        def _():
            sum_ref[rows, :] = product + acc[rows, :]

    low = total.astype(BF)

    @pl.when(step == 0)
    def _():
        send_ref[...] = low

    @pl.when(step == 1)
    def _():
        keep_ref[...] = low


def entry_back(meta, tokens, grads, weights, u, frames):
    half = frames // 2
    d = tokens.shape[1]
    return call(
        entry_kernel,
        "entry_back",
        (2,),
        meta,
        (tokens, *grads, *weights),
        [pl.BlockSpec((half, d), lambda i, m: (u * 2 + (1 - i ^ m[0]), 0))]
        + [pl.BlockSpec((half, 256), lambda i, m: (1 - i ^ m[0], 0))] * 3
        + [fixed(192, d)] * 3,
        [fixed(half, d), fixed(half, d), fixed(576, d)],
        [like((half, d), BF), like((half, d), BF), like((576, d), F32)],
        [pltpu.VMEM((576, d), F32)],
        hold=(1, 2, 3),
        far=(0, 4, 5, 6),
    )


def joint_kernel(meta_ref, x_ref, dq_ref, dk_ref, dv_ref, before_ref, m0_ref, m1_ref, sum_ref, acc):
    step = pl.program_id(0)
    x = x_ref[...]
    for i, g_ref in enumerate((dq_ref, dk_ref, dv_ref)):
        rows = pl.ds(192 * i, 192)
        product = tn(g_ref[:, :192], x)

        @pl.when(step == 0)
        def _():
            acc[rows, :] = product

        @pl.when(step == 1)
        def _():
            sum_ref[rows, :] = (product + acc[rows, :] + before_ref[rows, :]).astype(BF)

    @pl.when(step == 0)
    def _():
        sum_ref[576:, :] = (m0_ref[...].astype(F32) + m1_ref[...].astype(F32)).astype(BF)


def joint_grads(meta, tokens, grads, before, u, frames):
    half = frames // 2
    d = tokens.shape[1]
    return call(
        joint_kernel,
        "joint_grads",
        (2,),
        meta,
        (tokens, *grads, *before),
        [pl.BlockSpec((half, d), lambda i, m: (u * 2 + i, 0))]
        + [pl.BlockSpec((half, 256), lambda i, m: (i, 0))] * 3
        + [fixed(*value.shape) for value in before],
        [fixed(832, d)],
        [like((832, d), BF)],
        [pltpu.VMEM((576, d), F32)],
        hold=(1, 2, 3),
        far=(0,),
    )


def rows_kernel(meta_ref, dq_ref, dk_ref, dv_ref, wq_ref, wk_ref, wv_ref, send_ref, keep_ref):
    total = sum(nn(g[:, :192], w[...]) for g, w in ((dq_ref, wq_ref), (dk_ref, wk_ref), (dv_ref, wv_ref)))
    for j, o_ref in enumerate((send_ref, keep_ref)):

        @pl.when(pl.program_id(0) == j)
        def _():
            o_ref[...] = total.astype(BF)


def entry_rows(meta, grads, weights, frames):
    half = frames // 2
    d = weights[0].shape[1]
    return call(
        rows_kernel,
        "entry_rows",
        (2,),
        meta,
        (*grads, *weights),
        [pl.BlockSpec((half, 256), lambda i, m: (1 - i ^ m[0], 0))] * 3 + [fixed(192, d)] * 3,
        [fixed(half, d), fixed(half, d)],
        [like((half, d), BF), like((half, d), BF)],
        hold=(0, 1, 2),
        far=(3, 4, 5),
    )


def place_kernel(meta_ref, *refs):
    o_ref = refs[-1]
    for i, r_ref in enumerate(refs[:-1]):

        @pl.when(pl.program_id(0) == i)
        def _():
            o_ref[...] = r_ref[...]


def place(meta, own, other):
    half, d = own[0].shape
    count = 2 * len(own)
    return call(
        place_kernel,
        "place",
        (count,),
        meta,
        [block for pair in zip(own, other) for block in pair],
        [fixed(half, d)] * count,
        pl.BlockSpec((half, d), lambda i, m: (i ^ m[0], 0)),
        like((count * half, d), own[0].dtype),
    )


def normalise(values):
    average = jnp.mean(values, axis=-1, keepdims=True)
    centred = values - average
    spread = jnp.mean(centred * centred, axis=-1, keepdims=True)
    rstd = lax.rsqrt(spread + EPS)
    return centred * rstd, rstd


def gelu_pair(v):
    e = jnp.exp2(v * v * (-0.5 * LOG2E))
    t = 1.0 / (1.0 + (0.3275911 * 0.7071067811865476) * jnp.abs(v))
    poly = t * (0.5 * 0.254829592 + t * (0.5 * -0.284496736 + t * (0.5 * 1.421413741 + t * (0.5 * -1.453152027 + t * (0.5 * 1.061405429)))))
    tail = poly * e
    phi_cap = jnp.where(v >= 0, 1.0 - tail, tail)
    return v * phi_cap, phi_cap + v * (e * 0.3989422804014327)


def ahead_kernel(
    meta_ref, tok_ref, a0, a1, a2, a3, w0, w1, w2, w3, ua_ref, ub_ref, da_ref, db_ref, vec_ref,
    xhat_ref, rstd_ref, low_ref, act_ref, slope_ref, own_ref, sent_ref,
):
    gain, bias = vec_ref[0:1, :], vec_ref[1:2, :]
    hidden = ua_ref.shape[1]
    for r in range(tok_ref.shape[0] // RB):
        rows = pl.ds(r * RB, RB)
        branch = jnp.zeros((RB, tok_ref.shape[1]), F32)
        for a, w in ((a0, w0), (a1, w1), (a2, w2), (a3, w3)):
            branch = branch + tn(a[:, rows], w[...]).astype(BF).astype(F32)
        xhat, rstd = normalise(tok_ref[rows, :].astype(F32) + branch)
        xhat_ref[rows, :] = xhat
        rstd_ref[rows, :] = jnp.broadcast_to(rstd, (RB, rstd_ref.shape[1]))
        normed = xhat * gain + bias
        low = normed.astype(BF)
        low_ref[rows, :] = low
        sent = jnp.zeros(normed.shape, F32)
        for g, (up, down) in enumerate(((ua_ref, da_ref), (ub_ref, db_ref))):
            acts = []
            for c in range(hidden // HB):
                act, slope = gelu_pair(nn(low, up[:, c * HB : (c + 1) * HB]))
                columns = pl.ds(g * hidden + c * HB, HB)
                acts.append(act.astype(BF))
                act_ref[rows, columns] = acts[-1]
                slope_ref[rows, columns] = slope.astype(BF)
            sent = sent + nn(jnp.concatenate(acts, axis=1), down[...]).astype(BF).astype(F32)
        own_ref[rows, :] = normed + sent
        sent_ref[rows, :] = sent.astype(BF)


def ahead(meta, tokens, att, merge_w, up, down, vectors, u):
    half = att[0].shape[1]
    d, hidden = up[0].shape
    return call(
        ahead_kernel,
        "ahead",
        (1,),
        meta,
        (tokens, *att, *merge_w, *up, *down, vectors),
        [pl.BlockSpec((half, d), lambda i, m: (u * 2 + m[0], 0))]
        + [fixed(192, half)] * 4
        + [fixed(192, d)] * 4
        + [fixed(d, hidden)] * 2
        + [fixed(hidden, d)] * 2
        + [fixed(4, d)],
        [fixed(half, d), fixed(half, 128), fixed(half, d), fixed(half, 2 * hidden), fixed(half, 2 * hidden), fixed(half, d), fixed(half, d)],
        [
            like((half, d), F32),
            like((half, 128), F32),
            like((half, d), BF),
            like((half, 2 * hidden), BF),
            like((half, 2 * hidden), BF),
            like((half, d), F32),
            like((half, d), BF),
        ],
        far=(0,),
        out=(2, 3, 4, 5),
        out_far=(0, 1),
    )


def astern_kernel(u, meta_ref, own_ref, far_ref, grad_ref, span_ref, ua_ref, ub_ref, da_ref, db_ref, slope_ref, vec_ref, *refs):
    last = len(refs) > 6
    if last:
        before = refs[:-10]
        out_ref, back_ref, sent_ref, small_ref, *sums, g_ref, pre_ref = refs[-10:]
    else:
        out_ref, g_ref, pre_ref, back_ref, sent_ref, small_ref = refs
    gain, bias = vec_ref[2:3, :], vec_ref[3:4, :]
    half, d = own_ref.shape
    hidden = ua_ref.shape[1]
    starts = span_ref[u : u + 1, :]
    gain_grad = jnp.zeros(gain.shape, F32)
    bias_grad = jnp.zeros(gain.shape, F32)
    for r in range(half // RB):
        rows = pl.ds(r * RB, RB)
        xhat, rstd = normalise(own_ref[rows, :] + far_ref[rows, :].astype(F32))
        out_ref[rows, :] = (xhat * gain + bias).astype(BF)
        frame = meta_ref[0] * half + r * RB + lax.broadcasted_iota(jnp.int32, (RB, starts.shape[1]), 0)
        inside = (frame >= starts) & (frame < starts + SPAN)
        weight = jnp.max(jnp.where(inside, 1.0, 0.0), axis=1, keepdims=True)
        cot = grad_ref[rows, :].astype(F32) * weight
        gain_grad = gain_grad + jnp.sum(cot * xhat, axis=0, keepdims=True)
        bias_grad = bias_grad + jnp.sum(cot, axis=0, keepdims=True)
        gy = cot * gain
        mean_gy = jnp.mean(gy, axis=-1, keepdims=True)
        mean_gx = jnp.mean(gy * xhat, axis=-1, keepdims=True)
        sum_grad = rstd * (gy - mean_gy - xhat * mean_gx)
        low = sum_grad.astype(BF)
        g_ref[rows, :] = low
        sent = jnp.zeros(sum_grad.shape, F32)
        for g, (up, down) in enumerate(((ua_ref, da_ref), (ub_ref, db_ref))):
            pres = []
            for c in range(hidden // HB):
                columns = pl.ds(g * hidden + c * HB, HB)
                slope = slope_ref[rows, columns].astype(F32)
                pres.append((nt(low, down[c * HB : (c + 1) * HB, :]) * slope).astype(BF))
                pre_ref[rows, columns] = pres[-1]
            sent = sent + nt(jnp.concatenate(pres, axis=1), up[...]).astype(BF).astype(F32)
        back_ref[rows, :] = sum_grad + sent
        sent_ref[rows, :] = sent.astype(BF)
    small_ref[0:1, :] = gain_grad
    small_ref[1:2, :] = bias_grad
    if last:
        x_ref, act_ref = before[:2]
        weight_sums(x_ref[...], g_ref[...], act_ref, pre_ref, before[2:], sums)


def astern(meta, own, far, grad, spans, up, down, slope, vectors, u, before):
    half, d = own.shape
    hidden = up[0].shape[1]
    rows = fixed(half, d)
    wide = fixed(half, 2 * hidden)
    grads = [] if not before else [(d, hidden)] * 2 + [(hidden, d)] * 2
    extra = [] if not before else [rows, wide] + [fixed(*shape) for shape in grads[: len(before) - 2]]
    made = [like((half, d), BF), like((half, 2 * hidden), BF)]
    others = [like((half, d), F32), like((half, d), BF), like((2, d), F32)]
    shapes = [like((half, d), BF)] + ([] if before else made) + others + [like(shape, BF) for shape in grads]
    return call(
        functools.partial(astern_kernel, u),
        "astern",
        (1,),
        meta,
        (own, far, grad, spans, *up, *down, slope, vectors, *before),
        [rows] * 2
        + [pl.BlockSpec((half, d), lambda i, m: (u * 2 + m[0], 0)), fixed(*spans.shape)]
        + [fixed(d, hidden)] * 2
        + [fixed(hidden, d)] * 2
        + [wide, fixed(4, d)]
        + extra,
        [fixed(*shape.shape) for shape in shapes],
        shapes,
        [pltpu.VMEM(shape.shape, shape.dtype) for shape in made] if before else (),
        limit=20 if before else VMEM,
        hold=(0, 8, *range(10, 10 + len(before))),
        far=(2,),
        out=() if before else (1, 2),
        out_far=(0, 1) if before else (0, 3),
    )


def weight_kernel(meta_ref, x_ref, g_ref, act_ref, pre_ref, *refs):
    before, sums = refs[:-4], refs[-4:]
    weight_sums(x_ref[...], g_ref[...], act_ref, pre_ref, before, sums)


def weight_sums(x, g, act_ref, pre_ref, before, sums):
    hidden = act_ref.shape[1] // 2
    for i in range(2):
        for c in range(hidden // HB):
            columns = pl.ds(i * hidden + c * HB, HB)
            block = pl.ds(c * HB, HB)
            up = tn(x, pre_ref[:, columns])
            down = tn(act_ref[:, columns], g)
            if before:
                up = up + before[i][:, block].astype(F32)
                down = down + before[2 + i][block, :].astype(F32)
            sums[i][:, block] = up.astype(BF)
            sums[2 + i][block, :] = down.astype(BF)


def weight_grads(meta, x, g, act, pre, before):
    rows, d = x.shape
    hidden = act.shape[1] // 2
    shapes = [(d, hidden)] * 2 + [(hidden, d)] * 2
    return call(
        weight_kernel,
        "weight_grads",
        (1,),
        meta,
        (x, g, act, pre, *before),
        [fixed(rows, d)] * 2 + [fixed(rows, 2 * hidden)] * 2 + [fixed(*shape) for shape in shapes[: len(before)]],
        [fixed(*shape) for shape in shapes],
        [like(shape, BF) for shape in shapes],
        hold=(0, 1, 2, 3),
        out=(0, 1, 2, 3),
    )


def inner_kernel(meta_ref, own_ref, far_ref, xhat_ref, rstd_ref, vec_ref, a0, a1, w0, w1, *refs):
    last = len(refs) == 11
    out_ref, g0, g1, m0, m1, small_ref = refs[-6:]
    grad = own_ref[...] + far_ref[...].astype(F32)
    xhat = xhat_ref[...]
    gain_grad = jnp.sum(grad * xhat, axis=0, keepdims=True)
    bias_grad = jnp.sum(grad, axis=0, keepdims=True)
    gy = grad * vec_ref[0:1, :]
    mean_gy = jnp.mean(gy, axis=-1, keepdims=True)
    mean_gx = jnp.mean(gy * xhat, axis=-1, keepdims=True)
    inner = rstd_ref[:, 0:1] * (gy - mean_gy - xhat * mean_gx)
    out_ref[...] = inner
    low = inner.astype(BF)
    g0[...] = nt(w0[...], low).astype(BF)
    g1[...] = nt(w1[...], low).astype(BF)
    small = jnp.concatenate([gain_grad, bias_grad], axis=0)
    small_ref[...] = small
    if last:
        before0, before1, before_small, outer0, outer1 = refs[:5]
        below = jnp.concatenate(
            [small + before_small[...], outer0[...] + outer1[...], jnp.zeros((60, small.shape[1]), F32)], axis=0
        ).astype(BF)
        for m, a, before in ((m0, a0, before0), (m1, a1, before1)):
            m[:192, :] = (nn(a[...], low) + before[...]).astype(BF)
            m[192:, :] = below
    else:
        m0[...] = nn(a0[...], low)
        m1[...] = nn(a1[...], low)


def inner_norm(meta, own, far, xhat, rstd, vectors, att, weights, before):
    rows, d = xhat.shape
    merge = like((256, d), BF) if before else like((192, d), F32)
    return call(
        inner_kernel,
        "inner_norm",
        (1,),
        meta,
        (own, far, xhat, rstd, vectors, *att, *weights, *before),
        [fixed(rows, d)] * 3
        + [fixed(rows, 128), fixed(4, d)]
        + [fixed(192, rows)] * 2
        + [fixed(192, d)] * 2
        + ([fixed(192, d)] * 2 + [fixed(2, d)] * 3 if before else []),
        [fixed(rows, d), fixed(192, rows), fixed(192, rows), fixed(*merge.shape), fixed(*merge.shape), fixed(2, d)],
        [like((rows, d), F32), like((192, rows), BF), like((192, rows), BF), merge, merge, like((2, d), F32)],
        far=(0, 2, 3, 5, 6, 7, 8, *((9, 10) if before else ())),
        out=(1,),
        out_far=(0,) if before else (0, 3, 4),
    )


def fold_kernel(bits, meta_ref, *refs):
    for i in range(2):
        here, there = refs[2 * i : 2 * i + 2]
        if bits:
            send, keep = refs[4 + 2 * i : 6 + 2 * i]
            half = send.shape[0]
            bit = meta_ref[bits[i]]
            for part, j in ((send, 1 - bit), (keep, bit)):
                rows = pl.ds(pl.multiple_of(j * half, 16), half)
                part[...] = (here[rows, :].astype(F32) + there[rows, :].astype(F32)).astype(BF)
        else:
            refs[4 + i][...] = (here[...].astype(F32) + there[...].astype(F32)).astype(BF)


def fold(meta, pairs, bits, hold=()):
    args = [value for pair in pairs for value in pair]
    rows, d = args[0].shape
    shapes = [like((rows // 2, d), BF)] * 4 if bits else [like((rows, d), BF)] * 2
    return call(
        functools.partial(fold_kernel, bits),
        "fold",
        (1,),
        meta,
        args,
        [fixed(rows, d)] * 4,
        [fixed(*shape.shape) for shape in shapes],
        shapes,
        hold=hold,
    )


def local(groups, tokens, lengths, span_starts, wq, wk, wv, wm, wu, wd, ig, ib, og, ob, out_grad):
    rows, d = tokens.shape
    seqs = lengths.shape[0]
    frames = rows // seqs
    half = frames // 2
    core = lax.axis_index("tensor") % 2
    place_dp = lax.axis_index("dp")
    bits = groups.bit_length() - 1

    def swap(value, k):
        return lax.ppermute(value, "tensor", [(i, i ^ k) for i in range(4)])

    def swap_dp(value, k):
        return lax.ppermute(value, "dp", [(i, i ^ k) for i in range(groups)])

    def add(a, b):
        return (a.astype(F32) + b.astype(F32)).astype(BF)

    def total(pieces):
        return sum(piece.astype(F32) for piece in pieces).astype(BF) if len(pieces) > 1 else pieces[0]

    stages = [(0, 1)] + [(b, 2) for b in range(1, bits - 1, 2)] + ([(bits - 1, 1)] if bits % 2 == 0 else [])
    bit_orders = (list(range(bits)), [1, 0, *range(2, bits)])

    def spot_of(stage):
        return (place_dp >> stage[0]) & ((1 << stage[1]) - 1)

    class Chain:
        def __init__(self, part, order, cut_already=False):
            self.part = part.reshape((1,) * len(order) + part.shape) if cut_already else part
            self.order = order
            self.steps = [] if cut_already else [(True, stage) for stage in order]
            self.steps += [(False, stage) for stage in reversed(order)]

        def cut(self, stage, j):
            size = self.part.shape[0] >> stage[1]
            return lax.dynamic_slice_in_dim(self.part, (spot_of(stage) ^ j) * size, size, 0)

        def start(self):
            if self.steps:
                scatter, stage = self.steps[0]
                others = range(1, 1 << stage[1])
                self.pending = [swap_dp(self.cut(stage, j) if scatter else self.part, j << stage[0]) for j in others]

        def finish(self, *after):
            if not self.steps:
                return
            scatter, stage = self.steps.pop(0)
            got = self.pending
            if after:
                got = list(lax.optimization_barrier((*got, *after))[: len(got)])
            if scatter:
                state = total([self.cut(stage, 0)] + got)
                if not self.steps[0][0]:
                    state = state.reshape((1,) * len(self.order) + state.shape)
            else:
                axis = self.order.index(stage)
                spot = spot_of(stage)
                mine = self.part
                if len(got) == 1:
                    laid = [jnp.where(spot, got[0], mine), jnp.where(spot, mine, got[0])]
                    state = jnp.concatenate(laid, axis=axis)
                else:
                    state = jnp.zeros(mine.shape[:axis] + (1 + len(got),) + mine.shape[axis + 1 :], BF)
                    for j, piece in enumerate([mine] + got):
                        state = lax.dynamic_update_slice_in_dim(state, piece, spot ^ j, axis)
                if not self.steps:
                    state = state.reshape(-1, d)
            self.part = state

    def finish(group, *after):
        for chain in group:
            chain.finish(*after)

    def start(group):
        for chain in group:
            chain.start()

    def together(group):
        for chain, value in zip(group, lax.optimization_barrier(tuple(chain.part for chain in group))):
            chain.part = value

    all_bits = [((place_dp >> b) & 1).reshape(1) for b in range(bits)]
    scalars = jnp.concatenate([core.reshape(1), lengths, *all_bits])
    token = []

    def meta():
        return lax.optimization_barrier((scalars, *token))[0] if token else scalars

    def done(results, *others):
        token[:] = [results[0], *others]
        return results

    merge_w = (wm, swap(wm, 1), swap(wm, 2), swap(wm, 3))
    up_w = (wu, swap(wu, 1))
    down_w = (wd, swap(wd, 1))
    vectors = jnp.stack([ig, ib, og, ob])
    qkv_w = (wq.T, wk.T, wv.T)

    fwd, att, front, far = [], [], [], []
    qkv_of = [done(project(scalars, tokens, qkv_w, 0, frames))]
    for u in range(seqs):
        fwd.append(done(attend_forward(meta(), *qkv_of[u], u, frames), *(merge_w[1:] if u == 0 else ())))
        own, other = fwd[u][:2]
        att.append((own, swap(other, 1), swap(own, 2), swap(other, 3)))
        if u + 1 < seqs:
            qkv_of.append(done(project(meta(), tokens, qkv_w, u + 1, frames), up_w[1], down_w[1]))
    for u in range(seqs):
        front.append(done(ahead(meta(), tokens, att[u], merge_w, up_w, down_w, vectors, u)))
        far.append(swap(front[u][6], 2))
    out_rows, back, far_grad, smalls, sums = [], [], [], [], ()
    for u in range(seqs):
        last = u == seqs - 1
        before = (front[u][2], front[u][3], *sums) if last else ()
        res = done(astern(meta(), front[u][5], far[u], out_grad, span_starts, up_w, down_w, front[u][4], vectors, u, before))
        out_rows.append(res[0])
        back.append(res[1 if last else 3])
        smalls.append(res[3 if last else 5])
        if last:
            sent, sums = res[2], res[4:]
        else:
            far_grad.append(swap(res[4], 2))
            sums = done(weight_grads(meta(), front[u][2], res[1], front[u][3], res[2], sums))

    def inner_step(u, before):
        res = done(inner_norm(meta(), back[u], far_grad[u], front[u][0], front[u][1], vectors, att[u][:2], merge_w[:2], before))
        return res, (res[1], swap(res[2], 1))

    def attend_step(u, grads):
        return done(attend_backward(meta(), *qkv_of[u], grads, fwd[u][:2], fwd[u][2], u, frames))

    def entry_step(u, grads):
        return done(entry_back(meta(), tokens, grads, qkv_w, u, frames))


    first_bit = 1 + seqs

    def scatter(step, pairs, after, hold=()):
        pairs = [tuple(lax.optimization_barrier((*pair, after))[:2]) for pair in pairs]
        if step == bits:
            return done(fold(meta(), pairs, (), hold))
        out = done(fold(meta(), pairs, tuple(first_bit + order[step] for order in bit_orders), hold))
        return [(out[2 * i + 1], swap_dp(out[2 * i], 1 << bit_orders[i][step])) for i in range(2)]

    inner, so_far, near, crossed = [], (), [], []
    out_other = [swap(r, 1) for r in out_rows]

    def exchange(out):
        got = swap(out[0], 1)
        near.append((out[1], got))
        crossed.append(swap(total(near[-1]), 2))
        return got

    for u in range(seqs):
        last = u == seqs - 1
        if u == 0:
            up_own, up_other, down_own, down_other = lax.optimization_barrier((*sums, far_grad[0]))[:4]
            moving = [(down_own, swap(down_other, 1)), (up_own, swap(up_other, 1))]
            res, grads = inner_step(0, ())
            inner.append(res)
            far_grad.append(swap(lax.optimization_barrier((sent, res[0]))[0], 2))
            moving = scatter(0, moving, res[0])
        dqkv = attend_step(u, grads)
        moving = scatter(1 + 2 * u, moving, dqkv[0])
        if not last:
            before = ()
            if u + 1 == seqs - 1:
                before = (inner[0][3], inner[0][4], inner[0][5], *smalls)
            res, grads = inner_step(u + 1, before)
            inner.append(res)
        else:
            for step in range(4, bits + 1):
                moving = scatter(step, moving, moving[0][0])
            first, second = (
                Chain(moving[i], [(b, 1) for b in order], True) for i, order in enumerate(bit_orders)
            )
            start([first, second])
            token.extend(out_other)
        if last:
            qkv = Chain(done(joint_grads(meta(), tokens, dqkv, so_far, u, frames))[0], stages)
            qkv.start()
            out = done(entry_rows(meta(), dqkv, qkv_w, frames))
        else:
            out = entry_step(u, dqkv)
            merge_got = swap(lax.optimization_barrier((res[4], out[0]))[0], 1)
            so_far = (out[2], res[3], merge_got)
            moving = scatter(2, moving, out[0])
            exchange(out)

    got = exchange(out)
    layer_output = place(meta(), out_rows, out_other)

    finish([first, second], got)
    finish([qkv], layer_output)
    together([qkv, first, second])
    start([qkv, first, second])
    finish([qkv, first, second], crossed[0])
    together([qkv, first, second])
    start([qkv, first])
    finish([qkv, first], crossed[1])
    together([qkv, first, second])
    start([qkv, second])
    ready = []
    for u in range(seqs):
        rest = near[u][0].astype(F32) + near[u][1].astype(F32) + crossed[u].astype(F32)
        ready.append((inner[u][0] + rest).astype(BF))
    input_grad = place(scalars, ready, [swap(r, 1) for r in ready])
    finish([qkv, second], input_grad)
    while qkv.steps or first.steps or second.steps:
        start([qkv, first, second])
        finish([qkv, first, second])
        together([qkv, first, second])
    down_sum, up_sum, joint = (chain.part for chain in (first, second, qkv))
    qkv_sum, merge_sum = joint[:576], joint[576:]
    small = merge_sum[192:196].astype(F32)
    query_grad, key_grad, value_grad = (qkv_sum[192 * i : 192 * (i + 1)].astype(F32).T for i in range(3))
    return (
        layer_output,
        input_grad,
        query_grad,
        key_grad,
        value_grad,
        merge_sum[:192].astype(F32),
        up_sum.astype(F32),
        down_sum.astype(F32),
        small[0],
        small[1],
        small[2],
        small[3],
    )


def solution(mesh):
    in_specs = (
        P("dp", None),
        P("dp"),
        P("dp", None),
        P(None, "tensor"),
        P(None, "tensor"),
        P(None, "tensor"),
        P("tensor", None),
        P(None, "tensor"),
        P("tensor", None),
        P(),
        P(),
        P(),
        P(),
        P("dp", None),
    )
    out_specs = (
        P("dp", None),
        P("dp", None),
        P(None, "tensor"),
        P(None, "tensor"),
        P(None, "tensor"),
        P("tensor", None),
        P(None, "tensor"),
        P("tensor", None),
        P(),
        P(),
        P(),
        P(),
    )
    body = functools.partial(local, mesh.shape["dp"])
    return jax.shard_map(body, mesh=mesh, in_specs=in_specs, out_specs=out_specs, check_vma=False)
```

```python
import functools

import jax
import jax.numpy as jnp
from jax import lax
from jax.experimental import pallas as pl
from jax.experimental.pallas import tpu as pltpu
from jax.sharding import PartitionSpec as P

HEAD_DIM = 64
SPAN = 10
EPS = 1e-05
LOG2E = 1.4426950408889634
KF = 1024
KB = 512
VMEM = 12
RB = 128
HB = 256
BF = jnp.bfloat16
F32 = jnp.float32
MIB = 1 << 20


def nn(a, b):
    return lax.dot_general(a, b, (((1,), (0,)), ((), ())), preferred_element_type=F32)


def nt(a, b):
    return lax.dot_general(a, b, (((1,), (1,)), ((), ())), preferred_element_type=F32)


def tn(a, b):
    return lax.dot_general(a, b, (((0,), (0,)), ((), ())), preferred_element_type=F32)


def params(limit):
    return pltpu.CompilerParams(vmem_limit_bytes=limit * MIB)


def cost(micros):
    return pl.CostEstimate(flops=int(micros * 1.1e9), bytes_accessed=1024, transcendentals=0)


MICROS = {"project": 3, "attend_forward": 8, "attend_backward": 12, "entry_back": 5, "place": 3, "ahead": 9, "astern": 10, "inner_norm": 3, "weight_grads": 4, "fold": 2, "joint_grads": 4, "entry_rows": 3}


def lane_parts(block):
    left = block[:, :128]
    lane = lax.broadcasted_iota(jnp.int32, left.shape, 1)
    zero = jnp.zeros_like(left)
    return (
        jnp.where(lane < HEAD_DIM, left, zero),
        jnp.where(lane >= HEAD_DIM, left, zero),
        block[:, 128:],
    )


TILE = (0, 0, 1)


def call(kernel, name, grid, meta, args, in_specs, out_specs, out_shape, scratch=(), limit=VMEM, hold=(), far=(), out=(), out_far=()):
    def place_input(i, value):
        space = pltpu.VMEM if i in hold else pltpu.HBM if i in far else None
        return value if space is None else pltpu.with_memory_space_constraint(value, space)

    def place_output(i, value):
        space = pltpu.VMEM if i in out else pltpu.HBM if i in out_far else None
        return value if space is None else space(value.shape, value.dtype)

    single = not isinstance(out_shape, list)
    return pl.pallas_call(
        kernel,
        grid_spec=pltpu.PrefetchScalarGridSpec(
            num_scalar_prefetch=1,
            grid=grid,
            in_specs=in_specs,
            out_specs=out_specs,
            scratch_shapes=scratch,
        ),
        out_shape=place_output(0, out_shape) if single else [place_output(i, o) for i, o in enumerate(out_shape)],
        compiler_params=params(limit),
        cost_estimate=cost(MICROS[name]),
        name=name,
    )(meta, *(place_input(i, value) for i, value in enumerate(args)))


def fixed(*shape):
    return pl.BlockSpec(shape, lambda *_: (0,) * len(shape))


def like(shape, dtype):
    return jax.ShapeDtypeStruct(shape, dtype)


def project_kernel(meta_ref, x_ref, wq_ref, wk_ref, wv_ref, q_ref, k_ref, v_ref):
    x = x_ref[...]
    for w_ref, o_ref in ((wq_ref, q_ref), (wk_ref, k_ref), (wv_ref, v_ref)):
        o_ref[:, :192] = nt(x, w_ref[...]).astype(BF)
        o_ref[:, 192:] = jnp.zeros((x.shape[0], HEAD_DIM), BF)


def project(meta, tokens, weights, u, frames):
    rows, d = frames, tokens.shape[1]
    block = 256
    return call(
        project_kernel,
        "project",
        (rows // block,),
        meta,
        (tokens, *weights),
        [pl.BlockSpec((block, d), lambda i, m: (u * (rows // block) + i, 0))] + [fixed(192, d)] * 3,
        [pl.BlockSpec((block, 256), lambda i, m: (i, 0))] * 3,
        [like((rows, 256), BF)] * 3,
        far=range(4),
        out=(0, 1, 2),
    )


def forward_kernel(u, meta_ref, q_ref, k_ref, v_ref, own_ref, other_ref, lse_ref, s_ref):
    length = meta_ref[1 + u]
    step = pl.program_id(0)
    blocks = lax.div(length + KF - 1, KF)
    parts = lane_parts(q_ref[...] * jnp.asarray(0.125, BF))
    width = q_ref.shape[0]

    def first(kb, highest):
        start = pl.multiple_of(kb * KF, KF)
        rows = pl.ds(start, KF)
        live = start + lax.broadcasted_iota(jnp.int32, (KF, width), 0) < length
        out = []
        for h in range(3):
            tile = pl.ds(128 * TILE[h], 128)
            s = nt(k_ref[rows, tile], parts[h])
            s = jnp.where(live, s, -1e30)
            s_ref[h, rows, :] = s
            out.append(jnp.maximum(highest[h], jnp.max(s, axis=0, keepdims=True)))
        return tuple(out)

    floor = jnp.full((1, width), -1e30, F32)
    highest = lax.fori_loop(0, blocks, first, (floor,) * 3)

    def second(kb, carry):
        rows = pl.ds(pl.multiple_of(kb * KF, KF), KF)
        out = []
        for h in range(3):
            total, result = carry[h]
            p = jnp.exp2((s_ref[h, rows, :] - highest[h]) * LOG2E)
            total = total + jnp.sum(p, axis=0, keepdims=True)
            v = v_ref[rows, pl.ds(128 * TILE[h], 128)]
            result = result + tn(v, p.astype(BF))
            out.append((total, result))
        return tuple(out)

    init = ((jnp.zeros((1, width), F32), jnp.zeros((128, width), F32)),) * 3
    done = lax.fori_loop(0, blocks, second, init)
    outs = []
    for h in range(3):
        total, result = done[h]
        lo = HEAD_DIM * (h % 2)
        o = result[lo : lo + HEAD_DIM] / total
        lse_ref[0, pl.ds(h, 1), :] = highest[h] * LOG2E + jnp.log2(total)
        outs.append(o.astype(BF))
    whole = jnp.concatenate(outs, axis=0)
    for j, o_ref in enumerate((own_ref, other_ref)):

        @pl.when(step == j)
        def _():
            o_ref[...] = whole


def attend_forward(meta, q, k, v, u, frames):
    half = frames // 2
    return call(
        functools.partial(forward_kernel, u),
        "attend_forward",
        (2,),
        meta,
        (q, k, v),
        [
            pl.BlockSpec((half, 256), lambda i, m: (i ^ m[0], 0)),
            fixed(frames, 256),
            fixed(frames, 256),
        ],
        [
            fixed(192, half),
            fixed(192, half),
            pl.BlockSpec((1, 8, half), lambda i, m: (i, 0, 0)),
        ],
        [
            like((192, half), BF),
            like((192, half), BF),
            like((2, 8, half), F32),
        ],
        [pltpu.VMEM((3, frames, half), F32)],
        hold=(0, 1, 2),
    )


def backward_kernel(
    u, meta_ref, q_ref, k_ref, v_ref, d0_ref, d1_ref, o0_ref, o1_ref, lse_ref,
    dq_ref, dk_ref, dv_ref, kt_ref, dk_acc, dv_acc, do_ref, o_ref,
):
    length = meta_ref[1 + u]
    blocks = lax.div(length + KB - 1, KB)
    step = pl.program_id(0)

    @pl.when(step == 0)
    def _():
        dk_acc[...] = jnp.zeros_like(dk_acc)
        dv_acc[...] = jnp.zeros_like(dv_acc)
        kt_ref[...] = jnp.transpose(k_ref[...])
        do_ref[...] = d0_ref[...]
        o_ref[...] = o0_ref[...]

    @pl.when(step == 1)
    def _():
        do_ref[...] = d1_ref[...]
        o_ref[...] = o1_ref[...]

    parts = lane_parts(q_ref[...] * jnp.asarray(0.125, BF))
    width = q_ref.shape[0]
    empty = jnp.zeros((HEAD_DIM, width), BF)
    head = [do_ref[pl.ds(h * HEAD_DIM, HEAD_DIM), :] for h in range(3)]
    grads = (
        jnp.concatenate([head[0], empty], axis=0),
        jnp.concatenate([empty, head[1]], axis=0),
        jnp.concatenate([head[2], empty], axis=0),
    )
    delta = [
        jnp.sum(
            head[h].astype(F32) * o_ref[pl.ds(h * HEAD_DIM, HEAD_DIM), :].astype(F32), axis=0, keepdims=True
        )
        for h in range(3)
    ]
    lse = [lse_ref[0, pl.ds(h, 1), :] for h in range(3)]

    def body(kb, carry):
        start = pl.multiple_of(kb * KB, KB)
        rows = pl.ds(start, KB)
        live = start + lax.broadcasted_iota(jnp.int32, (KB, width), 0) < length
        out = []
        for h in range(3):
            tile = pl.ds(128 * TILE[h], 128)
            s = nt(k_ref[rows, tile], parts[h])
            s = jnp.where(live, s, -1e30)
            p = jnp.exp2(s * LOG2E - lse[h])
            dp = nn(v_ref[rows, tile], grads[h])
            ds = (p * (dp - delta[h])).astype(BF)
            dv_acc[rows, tile] += nt(p.astype(BF), grads[h])
            dk_acc[rows, tile] += nn(ds, parts[h])
            kt = kt_ref[pl.ds(h * HEAD_DIM, HEAD_DIM), rows]
            out.append(carry[h] + nn(kt, ds))
        return tuple(out)

    zero = jnp.zeros((HEAD_DIM, width), F32)
    done = lax.fori_loop(0, blocks, body, (zero,) * 3)
    full = jnp.concatenate(done + (zero,), axis=0) * 0.125
    dq_ref[...] = jnp.transpose(full).astype(BF)

    @pl.when(step == 1)
    def _():
        dk_ref[...] = dk_acc[...].astype(BF)
        dv_ref[...] = dv_acc[...].astype(BF)


def attend_backward(meta, q, k, v, grads, outs, lse, u, frames):
    half = frames // 2
    return call(
        functools.partial(backward_kernel, u),
        "attend_backward",
        (2,),
        meta,
        (q, k, v, *grads, *outs, lse),
        [
            pl.BlockSpec((half, 256), lambda i, m: (i ^ m[0], 0)),
            fixed(frames, 256),
            fixed(frames, 256),
            fixed(192, half),
            fixed(192, half),
            fixed(192, half),
            fixed(192, half),
            pl.BlockSpec((1, 8, half), lambda i, m: (i, 0, 0)),
        ],
        [
            pl.BlockSpec((half, 256), lambda i, m: (i ^ m[0], 0)),
            fixed(frames, 256),
            fixed(frames, 256),
        ],
        [like((frames, 256), BF)] * 3,
        [
            pltpu.VMEM((256, frames), BF),
            pltpu.VMEM((frames, 256), F32),
            pltpu.VMEM((frames, 256), F32),
            pltpu.VMEM((192, half), BF),
            pltpu.VMEM((192, half), BF),
        ],
        hold=(3,),
        far=(0, 1, 2),
        out=(0, 1, 2),
    )


def entry_kernel(meta_ref, x_ref, dq_ref, dk_ref, dv_ref, wq_ref, wk_ref, wv_ref, send_ref, keep_ref, sum_ref, acc):
    step = pl.program_id(0)
    x = x_ref[...]
    total = jnp.zeros(x.shape, F32)
    for i, (g_ref, w_ref) in enumerate(((dq_ref, wq_ref), (dk_ref, wk_ref), (dv_ref, wv_ref))):
        rows = pl.ds(192 * i, 192)
        g = g_ref[:, :192]
        total = total + nn(g, w_ref[...])
        product = tn(g, x)

        @pl.when(step == 0)
        def _():
            acc[rows, :] = product

        @pl.when(step == 1)
        def _():
            sum_ref[rows, :] = product + acc[rows, :]

    low = total.astype(BF)

    @pl.when(step == 0)
    def _():
        send_ref[...] = low

    @pl.when(step == 1)
    def _():
        keep_ref[...] = low


def entry_back(meta, tokens, grads, weights, u, frames):
    half = frames // 2
    d = tokens.shape[1]
    return call(
        entry_kernel,
        "entry_back",
        (2,),
        meta,
        (tokens, *grads, *weights),
        [pl.BlockSpec((half, d), lambda i, m: (u * 2 + (1 - i ^ m[0]), 0))]
        + [pl.BlockSpec((half, 256), lambda i, m: (1 - i ^ m[0], 0))] * 3
        + [fixed(192, d)] * 3,
        [fixed(half, d), fixed(half, d), fixed(576, d)],
        [like((half, d), BF), like((half, d), BF), like((576, d), F32)],
        [pltpu.VMEM((576, d), F32)],
        hold=(1, 2, 3),
        far=(0, 4, 5, 6),
    )


def joint_kernel(meta_ref, x_ref, dq_ref, dk_ref, dv_ref, before_ref, m0_ref, m1_ref, sum_ref, acc):
    step = pl.program_id(0)
    x = x_ref[...]
    for i, g_ref in enumerate((dq_ref, dk_ref, dv_ref)):
        rows = pl.ds(192 * i, 192)
        product = tn(g_ref[:, :192], x)

        @pl.when(step == 0)
        def _():
            acc[rows, :] = product

        @pl.when(step == 1)
        def _():
            sum_ref[rows, :] = (product + acc[rows, :] + before_ref[rows, :]).astype(BF)

    @pl.when(step == 0)
    def _():
        sum_ref[576:, :] = (m0_ref[...].astype(F32) + m1_ref[...].astype(F32)).astype(BF)


def joint_grads(meta, tokens, grads, before, u, frames):
    half = frames // 2
    d = tokens.shape[1]
    return call(
        joint_kernel,
        "joint_grads",
        (2,),
        meta,
        (tokens, *grads, *before),
        [pl.BlockSpec((half, d), lambda i, m: (u * 2 + i, 0))]
        + [pl.BlockSpec((half, 256), lambda i, m: (i, 0))] * 3
        + [fixed(*value.shape) for value in before],
        [fixed(832, d)],
        [like((832, d), BF)],
        [pltpu.VMEM((576, d), F32)],
        hold=(1, 2, 3),
        far=(0,),
    )


def rows_kernel(meta_ref, dq_ref, dk_ref, dv_ref, wq_ref, wk_ref, wv_ref, send_ref, keep_ref):
    total = sum(nn(g[:, :192], w[...]) for g, w in ((dq_ref, wq_ref), (dk_ref, wk_ref), (dv_ref, wv_ref)))
    for j, o_ref in enumerate((send_ref, keep_ref)):

        @pl.when(pl.program_id(0) == j)
        def _():
            o_ref[...] = total.astype(BF)


def entry_rows(meta, grads, weights, frames):
    half = frames // 2
    d = weights[0].shape[1]
    return call(
        rows_kernel,
        "entry_rows",
        (2,),
        meta,
        (*grads, *weights),
        [pl.BlockSpec((half, 256), lambda i, m: (1 - i ^ m[0], 0))] * 3 + [fixed(192, d)] * 3,
        [fixed(half, d), fixed(half, d)],
        [like((half, d), BF), like((half, d), BF)],
        hold=(0, 1, 2),
        far=(3, 4, 5),
    )


def place_kernel(meta_ref, *refs):
    o_ref = refs[-1]
    for i, r_ref in enumerate(refs[:-1]):

        @pl.when(pl.program_id(0) == i)
        def _():
            o_ref[...] = r_ref[...]


def place(meta, own, other):
    half, d = own[0].shape
    count = 2 * len(own)
    return call(
        place_kernel,
        "place",
        (count,),
        meta,
        [block for pair in zip(own, other) for block in pair],
        [fixed(half, d)] * count,
        pl.BlockSpec((half, d), lambda i, m: (i ^ m[0], 0)),
        like((count * half, d), own[0].dtype),
    )


def normalise(values):
    average = jnp.mean(values, axis=-1, keepdims=True)
    centred = values - average
    spread = jnp.mean(centred * centred, axis=-1, keepdims=True)
    rstd = lax.rsqrt(spread + EPS)
    return centred * rstd, rstd


def gelu_pair(v):
    e = jnp.exp2(v * v * (-0.5 * LOG2E))
    t = 1.0 / (1.0 + (0.3275911 * 0.7071067811865476) * jnp.abs(v))
    poly = t * (0.5 * 0.254829592 + t * (0.5 * -0.284496736 + t * (0.5 * 1.421413741 + t * (0.5 * -1.453152027 + t * (0.5 * 1.061405429)))))
    tail = poly * e
    phi_cap = jnp.where(v >= 0, 1.0 - tail, tail)
    return v * phi_cap, phi_cap + v * (e * 0.3989422804014327)


def ahead_kernel(
    meta_ref, tok_ref, a0, a1, a2, a3, w0, w1, w2, w3, ua_ref, ub_ref, da_ref, db_ref, vec_ref,
    xhat_ref, rstd_ref, low_ref, act_ref, slope_ref, own_ref, sent_ref,
):
    gain, bias = vec_ref[0:1, :], vec_ref[1:2, :]
    hidden = ua_ref.shape[1]
    for r in range(tok_ref.shape[0] // RB):
        rows = pl.ds(r * RB, RB)
        branch = jnp.zeros((RB, tok_ref.shape[1]), F32)
        for a, w in ((a0, w0), (a1, w1), (a2, w2), (a3, w3)):
            branch = branch + tn(a[:, rows], w[...]).astype(BF).astype(F32)
        xhat, rstd = normalise(tok_ref[rows, :].astype(F32) + branch)
        xhat_ref[rows, :] = xhat
        rstd_ref[rows, :] = jnp.broadcast_to(rstd, (RB, rstd_ref.shape[1]))
        normed = xhat * gain + bias
        low = normed.astype(BF)
        low_ref[rows, :] = low
        sent = jnp.zeros(normed.shape, F32)
        for g, (up, down) in enumerate(((ua_ref, da_ref), (ub_ref, db_ref))):
            acts = []
            for c in range(hidden // HB):
                act, slope = gelu_pair(nn(low, up[:, c * HB : (c + 1) * HB]))
                columns = pl.ds(g * hidden + c * HB, HB)
                acts.append(act.astype(BF))
                act_ref[rows, columns] = acts[-1]
                slope_ref[rows, columns] = slope.astype(BF)
            sent = sent + nn(jnp.concatenate(acts, axis=1), down[...]).astype(BF).astype(F32)
        own_ref[rows, :] = normed + sent
        sent_ref[rows, :] = sent.astype(BF)


def ahead(meta, tokens, att, merge_w, up, down, vectors, u):
    half = att[0].shape[1]
    d, hidden = up[0].shape
    return call(
        ahead_kernel,
        "ahead",
        (1,),
        meta,
        (tokens, *att, *merge_w, *up, *down, vectors),
        [pl.BlockSpec((half, d), lambda i, m: (u * 2 + m[0], 0))]
        + [fixed(192, half)] * 4
        + [fixed(192, d)] * 4
        + [fixed(d, hidden)] * 2
        + [fixed(hidden, d)] * 2
        + [fixed(4, d)],
        [fixed(half, d), fixed(half, 128), fixed(half, d), fixed(half, 2 * hidden), fixed(half, 2 * hidden), fixed(half, d), fixed(half, d)],
        [
            like((half, d), F32),
            like((half, 128), F32),
            like((half, d), BF),
            like((half, 2 * hidden), BF),
            like((half, 2 * hidden), BF),
            like((half, d), F32),
            like((half, d), BF),
        ],
        far=(0,),
        out=(2, 3, 4, 5),
        out_far=(0, 1),
    )


def astern_kernel(u, meta_ref, own_ref, far_ref, grad_ref, span_ref, ua_ref, ub_ref, da_ref, db_ref, slope_ref, vec_ref, *refs):
    last = len(refs) > 6
    if last:
        before = refs[:-10]
        out_ref, back_ref, sent_ref, small_ref, *sums, g_ref, pre_ref = refs[-10:]
    else:
        out_ref, g_ref, pre_ref, back_ref, sent_ref, small_ref = refs
    gain, bias = vec_ref[2:3, :], vec_ref[3:4, :]
    half, d = own_ref.shape
    hidden = ua_ref.shape[1]
    starts = span_ref[u : u + 1, :]
    gain_grad = jnp.zeros(gain.shape, F32)
    bias_grad = jnp.zeros(gain.shape, F32)
    for r in range(half // RB):
        rows = pl.ds(r * RB, RB)
        xhat, rstd = normalise(own_ref[rows, :] + far_ref[rows, :].astype(F32))
        out_ref[rows, :] = (xhat * gain + bias).astype(BF)
        frame = meta_ref[0] * half + r * RB + lax.broadcasted_iota(jnp.int32, (RB, starts.shape[1]), 0)
        inside = (frame >= starts) & (frame < starts + SPAN)
        weight = jnp.max(jnp.where(inside, 1.0, 0.0), axis=1, keepdims=True)
        cot = grad_ref[rows, :].astype(F32) * weight
        gain_grad = gain_grad + jnp.sum(cot * xhat, axis=0, keepdims=True)
        bias_grad = bias_grad + jnp.sum(cot, axis=0, keepdims=True)
        gy = cot * gain
        mean_gy = jnp.mean(gy, axis=-1, keepdims=True)
        mean_gx = jnp.mean(gy * xhat, axis=-1, keepdims=True)
        sum_grad = rstd * (gy - mean_gy - xhat * mean_gx)
        low = sum_grad.astype(BF)
        g_ref[rows, :] = low
        sent = jnp.zeros(sum_grad.shape, F32)
        for g, (up, down) in enumerate(((ua_ref, da_ref), (ub_ref, db_ref))):
            pres = []
            for c in range(hidden // HB):
                columns = pl.ds(g * hidden + c * HB, HB)
                slope = slope_ref[rows, columns].astype(F32)
                pres.append((nt(low, down[c * HB : (c + 1) * HB, :]) * slope).astype(BF))
                pre_ref[rows, columns] = pres[-1]
            sent = sent + nt(jnp.concatenate(pres, axis=1), up[...]).astype(BF).astype(F32)
        back_ref[rows, :] = sum_grad + sent
        sent_ref[rows, :] = sent.astype(BF)
    small_ref[0:1, :] = gain_grad
    small_ref[1:2, :] = bias_grad
    if last:
        x_ref, act_ref = before[:2]
        weight_sums(x_ref[...], g_ref[...], act_ref, pre_ref, before[2:], sums)


def astern(meta, own, far, grad, spans, up, down, slope, vectors, u, before):
    half, d = own.shape
    hidden = up[0].shape[1]
    rows = fixed(half, d)
    wide = fixed(half, 2 * hidden)
    grads = [] if not before else [(d, hidden)] * 2 + [(hidden, d)] * 2
    extra = [] if not before else [rows, wide] + [fixed(*shape) for shape in grads[: len(before) - 2]]
    made = [like((half, d), BF), like((half, 2 * hidden), BF)]
    others = [like((half, d), F32), like((half, d), BF), like((2, d), F32)]
    shapes = [like((half, d), BF)] + ([] if before else made) + others + [like(shape, BF) for shape in grads]
    return call(
        functools.partial(astern_kernel, u),
        "astern",
        (1,),
        meta,
        (own, far, grad, spans, *up, *down, slope, vectors, *before),
        [rows] * 2
        + [pl.BlockSpec((half, d), lambda i, m: (u * 2 + m[0], 0)), fixed(*spans.shape)]
        + [fixed(d, hidden)] * 2
        + [fixed(hidden, d)] * 2
        + [wide, fixed(4, d)]
        + extra,
        [fixed(*shape.shape) for shape in shapes],
        shapes,
        [pltpu.VMEM(shape.shape, shape.dtype) for shape in made] if before else (),
        limit=20 if before else VMEM,
        hold=(0, 8, *range(10, 10 + len(before))),
        far=(2,),
        out=() if before else (1, 2),
        out_far=(0, 1) if before else (0, 3),
    )


def weight_kernel(meta_ref, x_ref, g_ref, act_ref, pre_ref, *refs):
    before, sums = refs[:-4], refs[-4:]
    weight_sums(x_ref[...], g_ref[...], act_ref, pre_ref, before, sums)


def weight_sums(x, g, act_ref, pre_ref, before, sums):
    hidden = act_ref.shape[1] // 2
    for i in range(2):
        for c in range(hidden // HB):
            columns = pl.ds(i * hidden + c * HB, HB)
            block = pl.ds(c * HB, HB)
            up = tn(x, pre_ref[:, columns])
            down = tn(act_ref[:, columns], g)
            if before:
                up = up + before[i][:, block].astype(F32)
                down = down + before[2 + i][block, :].astype(F32)
            sums[i][:, block] = up.astype(BF)
            sums[2 + i][block, :] = down.astype(BF)


def weight_grads(meta, x, g, act, pre, before):
    rows, d = x.shape
    hidden = act.shape[1] // 2
    shapes = [(d, hidden)] * 2 + [(hidden, d)] * 2
    return call(
        weight_kernel,
        "weight_grads",
        (1,),
        meta,
        (x, g, act, pre, *before),
        [fixed(rows, d)] * 2 + [fixed(rows, 2 * hidden)] * 2 + [fixed(*shape) for shape in shapes[: len(before)]],
        [fixed(*shape) for shape in shapes],
        [like(shape, BF) for shape in shapes],
        hold=(0, 1, 2, 3),
        out=(0, 1, 2, 3),
    )


def inner_kernel(meta_ref, own_ref, far_ref, xhat_ref, rstd_ref, vec_ref, a0, a1, w0, w1, *refs):
    last = len(refs) == 11
    out_ref, g0, g1, m0, m1, small_ref = refs[-6:]
    grad = own_ref[...] + far_ref[...].astype(F32)
    xhat = xhat_ref[...]
    gain_grad = jnp.sum(grad * xhat, axis=0, keepdims=True)
    bias_grad = jnp.sum(grad, axis=0, keepdims=True)
    gy = grad * vec_ref[0:1, :]
    mean_gy = jnp.mean(gy, axis=-1, keepdims=True)
    mean_gx = jnp.mean(gy * xhat, axis=-1, keepdims=True)
    inner = rstd_ref[:, 0:1] * (gy - mean_gy - xhat * mean_gx)
    out_ref[...] = inner
    low = inner.astype(BF)
    g0[...] = nt(w0[...], low).astype(BF)
    g1[...] = nt(w1[...], low).astype(BF)
    small = jnp.concatenate([gain_grad, bias_grad], axis=0)
    small_ref[...] = small
    if last:
        before0, before1, before_small, outer0, outer1 = refs[:5]
        below = jnp.concatenate(
            [small + before_small[...], outer0[...] + outer1[...], jnp.zeros((60, small.shape[1]), F32)], axis=0
        ).astype(BF)
        for m, a, before in ((m0, a0, before0), (m1, a1, before1)):
            m[:192, :] = (nn(a[...], low) + before[...]).astype(BF)
            m[192:, :] = below
    else:
        m0[...] = nn(a0[...], low)
        m1[...] = nn(a1[...], low)


def inner_norm(meta, own, far, xhat, rstd, vectors, att, weights, before):
    rows, d = xhat.shape
    merge = like((256, d), BF) if before else like((192, d), F32)
    return call(
        inner_kernel,
        "inner_norm",
        (1,),
        meta,
        (own, far, xhat, rstd, vectors, *att, *weights, *before),
        [fixed(rows, d)] * 3
        + [fixed(rows, 128), fixed(4, d)]
        + [fixed(192, rows)] * 2
        + [fixed(192, d)] * 2
        + ([fixed(192, d)] * 2 + [fixed(2, d)] * 3 if before else []),
        [fixed(rows, d), fixed(192, rows), fixed(192, rows), fixed(*merge.shape), fixed(*merge.shape), fixed(2, d)],
        [like((rows, d), F32), like((192, rows), BF), like((192, rows), BF), merge, merge, like((2, d), F32)],
        far=(0, 2, 3, 5, 6, 7, 8, *((9, 10) if before else ())),
        out=(1,),
        out_far=(0,) if before else (0, 3, 4),
    )


def fold_kernel(bits, meta_ref, *refs):
    for i in range(2):
        here, there = refs[2 * i : 2 * i + 2]
        if bits:
            send, keep = refs[4 + 2 * i : 6 + 2 * i]
            half = send.shape[0]
            bit = meta_ref[bits[i]]
            for part, j in ((send, 1 - bit), (keep, bit)):
                rows = pl.ds(pl.multiple_of(j * half, 16), half)
                part[...] = (here[rows, :].astype(F32) + there[rows, :].astype(F32)).astype(BF)
        else:
            refs[4 + i][...] = (here[...].astype(F32) + there[...].astype(F32)).astype(BF)


def fold(meta, pairs, bits, hold=()):
    args = [value for pair in pairs for value in pair]
    rows, d = args[0].shape
    shapes = [like((rows // 2, d), BF)] * 4 if bits else [like((rows, d), BF)] * 2
    return call(
        functools.partial(fold_kernel, bits),
        "fold",
        (1,),
        meta,
        args,
        [fixed(rows, d)] * 4,
        [fixed(*shape.shape) for shape in shapes],
        shapes,
        hold=hold,
    )


def local(groups, tokens, lengths, span_starts, wq, wk, wv, wm, wu, wd, ig, ib, og, ob, out_grad):
    rows, d = tokens.shape
    seqs = lengths.shape[0]
    frames = rows // seqs
    half = frames // 2
    core = lax.axis_index("tensor") % 2
    place_dp = lax.axis_index("dp")
    bits = groups.bit_length() - 1

    def swap(value, k):
        return lax.ppermute(value, "tensor", [(i, i ^ k) for i in range(4)])

    def swap_dp(value, k):
        return lax.ppermute(value, "dp", [(i, i ^ k) for i in range(groups)])

    def add(a, b):
        return (a.astype(F32) + b.astype(F32)).astype(BF)

    def total(pieces):
        return sum(piece.astype(F32) for piece in pieces).astype(BF) if len(pieces) > 1 else pieces[0]

    stages = [(0, 1)] + [(b, 2) for b in range(1, bits - 1, 2)] + ([(bits - 1, 1)] if bits % 2 == 0 else [])
    bit_orders = (list(range(bits)), [1, 0, *range(2, bits)])

    def spot_of(stage):
        return (place_dp >> stage[0]) & ((1 << stage[1]) - 1)

    class Chain:
        def __init__(self, part, order, cut_already=False):
            self.part = part.reshape((1,) * len(order) + part.shape) if cut_already else part
            self.order = order
            self.steps = [] if cut_already else [(True, stage) for stage in order]
            self.steps += [(False, stage) for stage in reversed(order)]

        def cut(self, stage, j):
            size = self.part.shape[0] >> stage[1]
            return lax.dynamic_slice_in_dim(self.part, (spot_of(stage) ^ j) * size, size, 0)

        def start(self):
            if self.steps:
                scatter, stage = self.steps[0]
                others = range(1, 1 << stage[1])
                self.pending = [swap_dp(self.cut(stage, j) if scatter else self.part, j << stage[0]) for j in others]

        def finish(self, *after):
            if not self.steps:
                return
            scatter, stage = self.steps.pop(0)
            got = self.pending
            if after:
                got = list(lax.optimization_barrier((*got, *after))[: len(got)])
            if scatter:
                state = total([self.cut(stage, 0)] + got)
                if not self.steps[0][0]:
                    state = state.reshape((1,) * len(self.order) + state.shape)
            else:
                axis = self.order.index(stage)
                spot = spot_of(stage)
                mine = self.part
                if len(got) == 1:
                    laid = [jnp.where(spot, got[0], mine), jnp.where(spot, mine, got[0])]
                    state = jnp.concatenate(laid, axis=axis)
                else:
                    state = jnp.zeros(mine.shape[:axis] + (1 + len(got),) + mine.shape[axis + 1 :], BF)
                    for j, piece in enumerate([mine] + got):
                        state = lax.dynamic_update_slice_in_dim(state, piece, spot ^ j, axis)
                if not self.steps:
                    state = state.reshape(-1, d)
            self.part = state

    def finish(group, *after):
        for chain in group:
            chain.finish(*after)

    def start(group):
        for chain in group:
            chain.start()

    def together(group):
        for chain, value in zip(group, lax.optimization_barrier(tuple(chain.part for chain in group))):
            chain.part = value

    all_bits = [((place_dp >> b) & 1).reshape(1) for b in range(bits)]
    scalars = jnp.concatenate([core.reshape(1), lengths, *all_bits])
    token = []

    def meta():
        return lax.optimization_barrier((scalars, *token))[0] if token else scalars

    def done(results, *others):
        token[:] = [results[0], *others]
        return results

    merge_w = (wm, swap(wm, 1), swap(wm, 2), swap(wm, 3))
    up_w = (wu, swap(wu, 1))
    down_w = (wd, swap(wd, 1))
    vectors = jnp.stack([ig, ib, og, ob])
    qkv_w = (wq.T, wk.T, wv.T)

    fwd, att, front, far = [], [], [], []
    qkv_of = [done(project(scalars, tokens, qkv_w, 0, frames))]
    for u in range(seqs):
        fwd.append(done(attend_forward(meta(), *qkv_of[u], u, frames), *(merge_w[1:] if u == 0 else ())))
        own, other = fwd[u][:2]
        att.append((own, swap(other, 1), swap(own, 2), swap(other, 3)))
        if u + 1 < seqs:
            qkv_of.append(done(project(meta(), tokens, qkv_w, u + 1, frames), up_w[1], down_w[1]))
    for u in range(seqs):
        front.append(done(ahead(meta(), tokens, att[u], merge_w, up_w, down_w, vectors, u)))
        far.append(swap(front[u][6], 2))
    out_rows, back, far_grad, smalls, sums = [], [], [], [], ()
    for u in range(seqs):
        last = u == seqs - 1
        before = (front[u][2], front[u][3], *sums) if last else ()
        res = done(astern(meta(), front[u][5], far[u], out_grad, span_starts, up_w, down_w, front[u][4], vectors, u, before))
        out_rows.append(res[0])
        back.append(res[1 if last else 3])
        smalls.append(res[3 if last else 5])
        if last:
            sent, sums = res[2], res[4:]
        else:
            far_grad.append(swap(res[4], 2))
            sums = done(weight_grads(meta(), front[u][2], res[1], front[u][3], res[2], sums))

    def inner_step(u, before):
        res = done(inner_norm(meta(), back[u], far_grad[u], front[u][0], front[u][1], vectors, att[u][:2], merge_w[:2], before))
        return res, (res[1], swap(res[2], 1))

    def attend_step(u, grads):
        return done(attend_backward(meta(), *qkv_of[u], grads, fwd[u][:2], fwd[u][2], u, frames))

    def entry_step(u, grads):
        return done(entry_back(meta(), tokens, grads, qkv_w, u, frames))


    first_bit = 1 + seqs

    def scatter(step, pairs, after, hold=()):
        pairs = [tuple(lax.optimization_barrier((*pair, after))[:2]) for pair in pairs]
        if step == bits:
            return done(fold(meta(), pairs, (), hold))
        out = done(fold(meta(), pairs, tuple(first_bit + order[step] for order in bit_orders), hold))
        return [(out[2 * i + 1], swap_dp(out[2 * i], 1 << bit_orders[i][step])) for i in range(2)]

    inner, so_far, near, crossed = [], (), [], []
    out_other = [swap(r, 1) for r in out_rows]

    def exchange(out):
        got = swap(out[0], 1)
        near.append((out[1], got))
        crossed.append(swap(total(near[-1]), 2))
        return got

    for u in range(seqs):
        last = u == seqs - 1
        if u == 0:
            up_own, up_other, down_own, down_other = lax.optimization_barrier((*sums, far_grad[0]))[:4]
            moving = [(down_own, swap(down_other, 1)), (up_own, swap(up_other, 1))]
            res, grads = inner_step(0, ())
            inner.append(res)
            far_grad.append(swap(lax.optimization_barrier((sent, res[0]))[0], 2))
            moving = scatter(0, moving, res[0])
        dqkv = attend_step(u, grads)
        moving = scatter(1 + 2 * u, moving, dqkv[0])
        if not last:
            before = ()
            if u + 1 == seqs - 1:
                before = (inner[0][3], inner[0][4], inner[0][5], *smalls)
            res, grads = inner_step(u + 1, before)
            inner.append(res)
        else:
            for step in range(4, bits + 1):
                moving = scatter(step, moving, moving[0][0])
            first, second = (
                Chain(moving[i], [(b, 1) for b in order], True) for i, order in enumerate(bit_orders)
            )
            start([first, second])
            token.extend(out_other)
        if last:
            qkv = Chain(done(joint_grads(meta(), tokens, dqkv, so_far, u, frames))[0], stages)
            qkv.start()
            out = done(entry_rows(meta(), dqkv, qkv_w, frames))
        else:
            out = entry_step(u, dqkv)
            merge_got = swap(lax.optimization_barrier((res[4], out[0]))[0], 1)
            so_far = (out[2], res[3], merge_got)
            moving = scatter(2, moving, out[0])
            exchange(out)

    got = exchange(out)
    layer_output = place(meta(), out_rows, out_other)

    finish([first, second], got)
    finish([qkv], crossed[0])
    together([qkv, first, second])
    start([qkv, first, second])
    finish([qkv, first, second], crossed[-1])
    together([qkv, first, second])
    start([qkv, first])
    ready = []
    for u in range(seqs):
        rest = near[u][0].astype(F32) + near[u][1].astype(F32) + crossed[u].astype(F32)
        ready.append((inner[u][0] + rest).astype(BF))
    input_grad = place(scalars, ready, [swap(r, 1) for r in ready])
    finish([qkv, first], layer_output)
    together([qkv, first, second])
    start([qkv, second])
    finish([qkv, second], input_grad)
    while qkv.steps or first.steps or second.steps:
        start([qkv, first, second])
        finish([qkv, first, second])
        together([qkv, first, second])
    down_sum, up_sum, joint = (chain.part for chain in (first, second, qkv))
    qkv_sum, merge_sum = joint[:576], joint[576:]
    small = merge_sum[192:196].astype(F32)
    query_grad, key_grad, value_grad = (qkv_sum[192 * i : 192 * (i + 1)].astype(F32).T for i in range(3))
    return (
        layer_output,
        input_grad,
        query_grad,
        key_grad,
        value_grad,
        merge_sum[:192].astype(F32),
        up_sum.astype(F32),
        down_sum.astype(F32),
        small[0],
        small[1],
        small[2],
        small[3],
    )


def solution(mesh):
    in_specs = (
        P("dp", None),
        P("dp"),
        P("dp", None),
        P(None, "tensor"),
        P(None, "tensor"),
        P(None, "tensor"),
        P("tensor", None),
        P(None, "tensor"),
        P("tensor", None),
        P(),
        P(),
        P(),
        P(),
        P("dp", None),
    )
    out_specs = (
        P("dp", None),
        P("dp", None),
        P(None, "tensor"),
        P(None, "tensor"),
        P(None, "tensor"),
        P("tensor", None),
        P(None, "tensor"),
        P("tensor", None),
        P(),
        P(),
        P(),
        P(),
    )
    body = functools.partial(local, mesh.shape["dp"])
    return jax.shard_map(body, mesh=mesh, in_specs=in_specs, out_specs=out_specs, check_vma=False)
```

```python
import functools

import jax
import jax.numpy as jnp
from jax import lax
from jax.experimental import pallas as pl
from jax.experimental.pallas import tpu as pltpu
from jax.sharding import PartitionSpec as P

HEAD_DIM = 64
SPAN = 10
EPS = 1e-05
LOG2E = 1.4426950408889634
KF = 1024
KB = 512
VMEM = 12
RB = 128
HB = 256
BF = jnp.bfloat16
F32 = jnp.float32
MIB = 1 << 20


def nn(a, b):
    return lax.dot_general(a, b, (((1,), (0,)), ((), ())), preferred_element_type=F32)


def nt(a, b):
    return lax.dot_general(a, b, (((1,), (1,)), ((), ())), preferred_element_type=F32)


def tn(a, b):
    return lax.dot_general(a, b, (((0,), (0,)), ((), ())), preferred_element_type=F32)


def params(limit):
    return pltpu.CompilerParams(vmem_limit_bytes=limit * MIB)


def cost(micros):
    return pl.CostEstimate(flops=int(micros * 1.1e9), bytes_accessed=1024, transcendentals=0)


MICROS = {"project": 3, "attend_forward": 8, "attend_backward": 12, "entry_back": 5, "place": 3, "ahead": 9, "astern": 10, "inner_norm": 3, "weight_grads": 4, "fold": 2, "joint_grads": 4, "entry_rows": 3}


def lane_parts(block):
    left = block[:, :128]
    lane = lax.broadcasted_iota(jnp.int32, left.shape, 1)
    zero = jnp.zeros_like(left)
    return (
        jnp.where(lane < HEAD_DIM, left, zero),
        jnp.where(lane >= HEAD_DIM, left, zero),
        block[:, 128:],
    )


TILE = (0, 0, 1)


def call(kernel, name, grid, meta, args, in_specs, out_specs, out_shape, scratch=(), limit=VMEM, hold=(), far=(), out=(), out_far=()):
    def place_input(i, value):
        space = pltpu.VMEM if i in hold else pltpu.HBM if i in far else None
        return value if space is None else pltpu.with_memory_space_constraint(value, space)

    def place_output(i, value):
        space = pltpu.VMEM if i in out else pltpu.HBM if i in out_far else None
        return value if space is None else space(value.shape, value.dtype)

    single = not isinstance(out_shape, list)
    return pl.pallas_call(
        kernel,
        grid_spec=pltpu.PrefetchScalarGridSpec(
            num_scalar_prefetch=1,
            grid=grid,
            in_specs=in_specs,
            out_specs=out_specs,
            scratch_shapes=scratch,
        ),
        out_shape=place_output(0, out_shape) if single else [place_output(i, o) for i, o in enumerate(out_shape)],
        compiler_params=params(limit),
        cost_estimate=cost(MICROS[name]),
        name=name,
    )(meta, *(place_input(i, value) for i, value in enumerate(args)))


def fixed(*shape):
    return pl.BlockSpec(shape, lambda *_: (0,) * len(shape))


def like(shape, dtype):
    return jax.ShapeDtypeStruct(shape, dtype)


def project_kernel(meta_ref, x_ref, wq_ref, wk_ref, wv_ref, q_ref, k_ref, v_ref):
    x = x_ref[...]
    for w_ref, o_ref in ((wq_ref, q_ref), (wk_ref, k_ref), (wv_ref, v_ref)):
        o_ref[:, :192] = nt(x, w_ref[...]).astype(BF)
        o_ref[:, 192:] = jnp.zeros((x.shape[0], HEAD_DIM), BF)


def project(meta, tokens, weights, u, frames):
    rows, d = frames, tokens.shape[1]
    block = 256
    return call(
        project_kernel,
        "project",
        (rows // block,),
        meta,
        (tokens, *weights),
        [pl.BlockSpec((block, d), lambda i, m: (u * (rows // block) + i, 0))] + [fixed(192, d)] * 3,
        [pl.BlockSpec((block, 256), lambda i, m: (i, 0))] * 3,
        [like((rows, 256), BF)] * 3,
        far=range(4),
        out=(0, 1, 2),
    )


def forward_kernel(u, meta_ref, q_ref, k_ref, v_ref, own_ref, other_ref, lse_ref, s_ref):
    length = meta_ref[1 + u]
    step = pl.program_id(0)
    blocks = lax.div(length + KF - 1, KF)
    parts = lane_parts(q_ref[...] * jnp.asarray(0.125, BF))
    width = q_ref.shape[0]

    def first(kb, highest):
        start = pl.multiple_of(kb * KF, KF)
        rows = pl.ds(start, KF)
        live = start + lax.broadcasted_iota(jnp.int32, (KF, width), 0) < length
        out = []
        for h in range(3):
            tile = pl.ds(128 * TILE[h], 128)
            s = nt(k_ref[rows, tile], parts[h])
            s = jnp.where(live, s, -1e30)
            s_ref[h, rows, :] = s
            out.append(jnp.maximum(highest[h], jnp.max(s, axis=0, keepdims=True)))
        return tuple(out)

    floor = jnp.full((1, width), -1e30, F32)
    highest = lax.fori_loop(0, blocks, first, (floor,) * 3)

    def second(kb, carry):
        rows = pl.ds(pl.multiple_of(kb * KF, KF), KF)
        out = []
        for h in range(3):
            total, result = carry[h]
            p = jnp.exp2((s_ref[h, rows, :] - highest[h]) * LOG2E)
            total = total + jnp.sum(p, axis=0, keepdims=True)
            v = v_ref[rows, pl.ds(128 * TILE[h], 128)]
            result = result + tn(v, p.astype(BF))
            out.append((total, result))
        return tuple(out)

    init = ((jnp.zeros((1, width), F32), jnp.zeros((128, width), F32)),) * 3
    done = lax.fori_loop(0, blocks, second, init)
    outs = []
    for h in range(3):
        total, result = done[h]
        lo = HEAD_DIM * (h % 2)
        o = result[lo : lo + HEAD_DIM] / total
        lse_ref[0, pl.ds(h, 1), :] = highest[h] * LOG2E + jnp.log2(total)
        outs.append(o.astype(BF))
    whole = jnp.concatenate(outs, axis=0)
    for j, o_ref in enumerate((own_ref, other_ref)):

        @pl.when(step == j)
        def _():
            o_ref[...] = whole


def attend_forward(meta, q, k, v, u, frames):
    half = frames // 2
    return call(
        functools.partial(forward_kernel, u),
        "attend_forward",
        (2,),
        meta,
        (q, k, v),
        [
            pl.BlockSpec((half, 256), lambda i, m: (i ^ m[0], 0)),
            fixed(frames, 256),
            fixed(frames, 256),
        ],
        [
            fixed(192, half),
            fixed(192, half),
            pl.BlockSpec((1, 8, half), lambda i, m: (i, 0, 0)),
        ],
        [
            like((192, half), BF),
            like((192, half), BF),
            like((2, 8, half), F32),
        ],
        [pltpu.VMEM((3, frames, half), F32)],
        hold=(0, 1, 2),
    )


def backward_kernel(
    u, meta_ref, q_ref, k_ref, v_ref, d0_ref, d1_ref, o0_ref, o1_ref, lse_ref,
    dq_ref, dk_ref, dv_ref, kt_ref, dk_acc, dv_acc, do_ref, o_ref,
):
    length = meta_ref[1 + u]
    blocks = lax.div(length + KB - 1, KB)
    step = pl.program_id(0)

    @pl.when(step == 0)
    def _():
        dk_acc[...] = jnp.zeros_like(dk_acc)
        dv_acc[...] = jnp.zeros_like(dv_acc)
        kt_ref[...] = jnp.transpose(k_ref[...])
        do_ref[...] = d0_ref[...]
        o_ref[...] = o0_ref[...]

    @pl.when(step == 1)
    def _():
        do_ref[...] = d1_ref[...]
        o_ref[...] = o1_ref[...]

    parts = lane_parts(q_ref[...] * jnp.asarray(0.125, BF))
    width = q_ref.shape[0]
    empty = jnp.zeros((HEAD_DIM, width), BF)
    head = [do_ref[pl.ds(h * HEAD_DIM, HEAD_DIM), :] for h in range(3)]
    grads = (
        jnp.concatenate([head[0], empty], axis=0),
        jnp.concatenate([empty, head[1]], axis=0),
        jnp.concatenate([head[2], empty], axis=0),
    )
    delta = [
        jnp.sum(
            head[h].astype(F32) * o_ref[pl.ds(h * HEAD_DIM, HEAD_DIM), :].astype(F32), axis=0, keepdims=True
        )
        for h in range(3)
    ]
    lse = [lse_ref[0, pl.ds(h, 1), :] for h in range(3)]

    def body(kb, carry):
        start = pl.multiple_of(kb * KB, KB)
        rows = pl.ds(start, KB)
        live = start + lax.broadcasted_iota(jnp.int32, (KB, width), 0) < length
        out = []
        for h in range(3):
            tile = pl.ds(128 * TILE[h], 128)
            s = nt(k_ref[rows, tile], parts[h])
            s = jnp.where(live, s, -1e30)
            p = jnp.exp2(s * LOG2E - lse[h])
            dp = nn(v_ref[rows, tile], grads[h])
            ds = (p * (dp - delta[h])).astype(BF)
            dv_acc[rows, tile] += nt(p.astype(BF), grads[h])
            dk_acc[rows, tile] += nn(ds, parts[h])
            kt = kt_ref[pl.ds(h * HEAD_DIM, HEAD_DIM), rows]
            out.append(carry[h] + nn(kt, ds))
        return tuple(out)

    zero = jnp.zeros((HEAD_DIM, width), F32)
    done = lax.fori_loop(0, blocks, body, (zero,) * 3)
    full = jnp.concatenate(done + (zero,), axis=0) * 0.125
    dq_ref[...] = jnp.transpose(full).astype(BF)

    @pl.when(step == 1)
    def _():
        dk_ref[...] = dk_acc[...].astype(BF)
        dv_ref[...] = dv_acc[...].astype(BF)


def attend_backward(meta, q, k, v, grads, outs, lse, u, frames):
    half = frames // 2
    return call(
        functools.partial(backward_kernel, u),
        "attend_backward",
        (2,),
        meta,
        (q, k, v, *grads, *outs, lse),
        [
            pl.BlockSpec((half, 256), lambda i, m: (i ^ m[0], 0)),
            fixed(frames, 256),
            fixed(frames, 256),
            fixed(192, half),
            fixed(192, half),
            fixed(192, half),
            fixed(192, half),
            pl.BlockSpec((1, 8, half), lambda i, m: (i, 0, 0)),
        ],
        [
            pl.BlockSpec((half, 256), lambda i, m: (i ^ m[0], 0)),
            fixed(frames, 256),
            fixed(frames, 256),
        ],
        [like((frames, 256), BF)] * 3,
        [
            pltpu.VMEM((256, frames), BF),
            pltpu.VMEM((frames, 256), F32),
            pltpu.VMEM((frames, 256), F32),
            pltpu.VMEM((192, half), BF),
            pltpu.VMEM((192, half), BF),
        ],
        hold=(3,),
        far=(0, 1, 2),
        out=(0, 1, 2),
    )


def entry_kernel(meta_ref, x_ref, dq_ref, dk_ref, dv_ref, wq_ref, wk_ref, wv_ref, send_ref, keep_ref, sum_ref, acc):
    step = pl.program_id(0)
    x = x_ref[...]
    total = jnp.zeros(x.shape, F32)
    for i, (g_ref, w_ref) in enumerate(((dq_ref, wq_ref), (dk_ref, wk_ref), (dv_ref, wv_ref))):
        rows = pl.ds(192 * i, 192)
        g = g_ref[:, :192]
        total = total + nn(g, w_ref[...])
        product = tn(g, x)

        @pl.when(step == 0)
        def _():
            acc[rows, :] = product

        @pl.when(step == 1)
        def _():
            sum_ref[rows, :] = product + acc[rows, :]

    low = total.astype(BF)

    @pl.when(step == 0)
    def _():
        send_ref[...] = low

    @pl.when(step == 1)
    def _():
        keep_ref[...] = low


def entry_back(meta, tokens, grads, weights, u, frames):
    half = frames // 2
    d = tokens.shape[1]
    return call(
        entry_kernel,
        "entry_back",
        (2,),
        meta,
        (tokens, *grads, *weights),
        [pl.BlockSpec((half, d), lambda i, m: (u * 2 + (1 - i ^ m[0]), 0))]
        + [pl.BlockSpec((half, 256), lambda i, m: (1 - i ^ m[0], 0))] * 3
        + [fixed(192, d)] * 3,
        [fixed(half, d), fixed(half, d), fixed(576, d)],
        [like((half, d), BF), like((half, d), BF), like((576, d), F32)],
        [pltpu.VMEM((576, d), F32)],
        hold=(1, 2, 3),
        far=(0, 4, 5, 6),
    )


def joint_kernel(meta_ref, x_ref, dq_ref, dk_ref, dv_ref, before_ref, m0_ref, m1_ref, sum_ref, acc):
    step = pl.program_id(0)
    x = x_ref[...]
    for i, g_ref in enumerate((dq_ref, dk_ref, dv_ref)):
        rows = pl.ds(192 * i, 192)
        product = tn(g_ref[:, :192], x)

        @pl.when(step == 0)
        def _():
            acc[rows, :] = product

        @pl.when(step == 1)
        def _():
            sum_ref[rows, :] = (product + acc[rows, :] + before_ref[rows, :]).astype(BF)

    @pl.when(step == 0)
    def _():
        sum_ref[576:, :] = (m0_ref[...].astype(F32) + m1_ref[...].astype(F32)).astype(BF)


def joint_grads(meta, tokens, grads, before, u, frames):
    half = frames // 2
    d = tokens.shape[1]
    return call(
        joint_kernel,
        "joint_grads",
        (2,),
        meta,
        (tokens, *grads, *before),
        [pl.BlockSpec((half, d), lambda i, m: (u * 2 + i, 0))]
        + [pl.BlockSpec((half, 256), lambda i, m: (i, 0))] * 3
        + [fixed(*value.shape) for value in before],
        [fixed(832, d)],
        [like((832, d), BF)],
        [pltpu.VMEM((576, d), F32)],
        hold=(1, 2, 3),
        far=(0,),
    )


def rows_kernel(meta_ref, dq_ref, dk_ref, dv_ref, wq_ref, wk_ref, wv_ref, send_ref, keep_ref):
    total = sum(nn(g[:, :192], w[...]) for g, w in ((dq_ref, wq_ref), (dk_ref, wk_ref), (dv_ref, wv_ref)))
    for j, o_ref in enumerate((send_ref, keep_ref)):

        @pl.when(pl.program_id(0) == j)
        def _():
            o_ref[...] = total.astype(BF)


def entry_rows(meta, grads, weights, frames):
    half = frames // 2
    d = weights[0].shape[1]
    return call(
        rows_kernel,
        "entry_rows",
        (2,),
        meta,
        (*grads, *weights),
        [pl.BlockSpec((half, 256), lambda i, m: (1 - i ^ m[0], 0))] * 3 + [fixed(192, d)] * 3,
        [fixed(half, d), fixed(half, d)],
        [like((half, d), BF), like((half, d), BF)],
        hold=(0, 1, 2),
        far=(3, 4, 5),
    )


def place_kernel(meta_ref, *refs):
    o_ref = refs[-1]
    for i, r_ref in enumerate(refs[:-1]):

        @pl.when(pl.program_id(0) == i)
        def _():
            o_ref[...] = r_ref[...]


def place(meta, own, other):
    half, d = own[0].shape
    count = 2 * len(own)
    return call(
        place_kernel,
        "place",
        (count,),
        meta,
        [block for pair in zip(own, other) for block in pair],
        [fixed(half, d)] * count,
        pl.BlockSpec((half, d), lambda i, m: (i ^ m[0], 0)),
        like((count * half, d), own[0].dtype),
    )


def normalise(values):
    average = jnp.mean(values, axis=-1, keepdims=True)
    centred = values - average
    spread = jnp.mean(centred * centred, axis=-1, keepdims=True)
    rstd = lax.rsqrt(spread + EPS)
    return centred * rstd, rstd


def gelu_pair(v):
    e = jnp.exp2(v * v * (-0.5 * LOG2E))
    t = 1.0 / (1.0 + (0.3275911 * 0.7071067811865476) * jnp.abs(v))
    poly = t * (0.5 * 0.254829592 + t * (0.5 * -0.284496736 + t * (0.5 * 1.421413741 + t * (0.5 * -1.453152027 + t * (0.5 * 1.061405429)))))
    tail = poly * e
    phi_cap = jnp.where(v >= 0, 1.0 - tail, tail)
    return v * phi_cap, phi_cap + v * (e * 0.3989422804014327)


def ahead_kernel(
    meta_ref, tok_ref, a0, a1, a2, a3, w0, w1, w2, w3, ua_ref, ub_ref, da_ref, db_ref, vec_ref,
    xhat_ref, rstd_ref, low_ref, act_ref, slope_ref, own_ref, sent_ref,
):
    gain, bias = vec_ref[0:1, :], vec_ref[1:2, :]
    hidden = ua_ref.shape[1]
    for r in range(tok_ref.shape[0] // RB):
        rows = pl.ds(r * RB, RB)
        branch = jnp.zeros((RB, tok_ref.shape[1]), F32)
        for a, w in ((a0, w0), (a1, w1), (a2, w2), (a3, w3)):
            branch = branch + tn(a[:, rows], w[...]).astype(BF).astype(F32)
        xhat, rstd = normalise(tok_ref[rows, :].astype(F32) + branch)
        xhat_ref[rows, :] = xhat
        rstd_ref[rows, :] = jnp.broadcast_to(rstd, (RB, rstd_ref.shape[1]))
        normed = xhat * gain + bias
        low = normed.astype(BF)
        low_ref[rows, :] = low
        sent = jnp.zeros(normed.shape, F32)
        for g, (up, down) in enumerate(((ua_ref, da_ref), (ub_ref, db_ref))):
            acts = []
            for c in range(hidden // HB):
                act, slope = gelu_pair(nn(low, up[:, c * HB : (c + 1) * HB]))
                columns = pl.ds(g * hidden + c * HB, HB)
                acts.append(act.astype(BF))
                act_ref[rows, columns] = acts[-1]
                slope_ref[rows, columns] = slope.astype(BF)
            sent = sent + nn(jnp.concatenate(acts, axis=1), down[...]).astype(BF).astype(F32)
        own_ref[rows, :] = normed + sent
        sent_ref[rows, :] = sent.astype(BF)


def ahead(meta, tokens, att, merge_w, up, down, vectors, u):
    half = att[0].shape[1]
    d, hidden = up[0].shape
    return call(
        ahead_kernel,
        "ahead",
        (1,),
        meta,
        (tokens, *att, *merge_w, *up, *down, vectors),
        [pl.BlockSpec((half, d), lambda i, m: (u * 2 + m[0], 0))]
        + [fixed(192, half)] * 4
        + [fixed(192, d)] * 4
        + [fixed(d, hidden)] * 2
        + [fixed(hidden, d)] * 2
        + [fixed(4, d)],
        [fixed(half, d), fixed(half, 128), fixed(half, d), fixed(half, 2 * hidden), fixed(half, 2 * hidden), fixed(half, d), fixed(half, d)],
        [
            like((half, d), F32),
            like((half, 128), F32),
            like((half, d), BF),
            like((half, 2 * hidden), BF),
            like((half, 2 * hidden), BF),
            like((half, d), F32),
            like((half, d), BF),
        ],
        far=(0,),
        out=(2, 3, 4, 5),
        out_far=(0, 1),
    )


def astern_kernel(u, meta_ref, own_ref, far_ref, grad_ref, span_ref, ua_ref, ub_ref, da_ref, db_ref, slope_ref, vec_ref, *refs):
    last = len(refs) > 6
    if last:
        before = refs[:-10]
        out_ref, back_ref, sent_ref, small_ref, *sums, g_ref, pre_ref = refs[-10:]
    else:
        out_ref, g_ref, pre_ref, back_ref, sent_ref, small_ref = refs
    gain, bias = vec_ref[2:3, :], vec_ref[3:4, :]
    half, d = own_ref.shape
    hidden = ua_ref.shape[1]
    starts = span_ref[u : u + 1, :]
    gain_grad = jnp.zeros(gain.shape, F32)
    bias_grad = jnp.zeros(gain.shape, F32)
    for r in range(half // RB):
        rows = pl.ds(r * RB, RB)
        xhat, rstd = normalise(own_ref[rows, :] + far_ref[rows, :].astype(F32))
        out_ref[rows, :] = (xhat * gain + bias).astype(BF)
        frame = meta_ref[0] * half + r * RB + lax.broadcasted_iota(jnp.int32, (RB, starts.shape[1]), 0)
        inside = (frame >= starts) & (frame < starts + SPAN)
        weight = jnp.max(jnp.where(inside, 1.0, 0.0), axis=1, keepdims=True)
        cot = grad_ref[rows, :].astype(F32) * weight
        gain_grad = gain_grad + jnp.sum(cot * xhat, axis=0, keepdims=True)
        bias_grad = bias_grad + jnp.sum(cot, axis=0, keepdims=True)
        gy = cot * gain
        mean_gy = jnp.mean(gy, axis=-1, keepdims=True)
        mean_gx = jnp.mean(gy * xhat, axis=-1, keepdims=True)
        sum_grad = rstd * (gy - mean_gy - xhat * mean_gx)
        low = sum_grad.astype(BF)
        g_ref[rows, :] = low
        sent = jnp.zeros(sum_grad.shape, F32)
        for g, (up, down) in enumerate(((ua_ref, da_ref), (ub_ref, db_ref))):
            pres = []
            for c in range(hidden // HB):
                columns = pl.ds(g * hidden + c * HB, HB)
                slope = slope_ref[rows, columns].astype(F32)
                pres.append((nt(low, down[c * HB : (c + 1) * HB, :]) * slope).astype(BF))
                pre_ref[rows, columns] = pres[-1]
            sent = sent + nt(jnp.concatenate(pres, axis=1), up[...]).astype(BF).astype(F32)
        back_ref[rows, :] = sum_grad + sent
        sent_ref[rows, :] = sent.astype(BF)
    small_ref[0:1, :] = gain_grad
    small_ref[1:2, :] = bias_grad
    if last:
        x_ref, act_ref = before[:2]
        weight_sums(x_ref[...], g_ref[...], act_ref, pre_ref, before[2:], sums)


def astern(meta, own, far, grad, spans, up, down, slope, vectors, u, before):
    half, d = own.shape
    hidden = up[0].shape[1]
    rows = fixed(half, d)
    wide = fixed(half, 2 * hidden)
    grads = [] if not before else [(d, hidden)] * 2 + [(hidden, d)] * 2
    extra = [] if not before else [rows, wide] + [fixed(*shape) for shape in grads[: len(before) - 2]]
    made = [like((half, d), BF), like((half, 2 * hidden), BF)]
    others = [like((half, d), F32), like((half, d), BF), like((2, d), F32)]
    shapes = [like((half, d), BF)] + ([] if before else made) + others + [like(shape, BF) for shape in grads]
    return call(
        functools.partial(astern_kernel, u),
        "astern",
        (1,),
        meta,
        (own, far, grad, spans, *up, *down, slope, vectors, *before),
        [rows] * 2
        + [pl.BlockSpec((half, d), lambda i, m: (u * 2 + m[0], 0)), fixed(*spans.shape)]
        + [fixed(d, hidden)] * 2
        + [fixed(hidden, d)] * 2
        + [wide, fixed(4, d)]
        + extra,
        [fixed(*shape.shape) for shape in shapes],
        shapes,
        [pltpu.VMEM(shape.shape, shape.dtype) for shape in made] if before else (),
        limit=20 if before else VMEM,
        hold=(0, 8, *range(10, 10 + len(before))),
        far=(2,),
        out=() if before else (1, 2),
        out_far=(0, 1) if before else (0, 3),
    )


def weight_kernel(meta_ref, x_ref, g_ref, act_ref, pre_ref, *refs):
    before, sums = refs[:-4], refs[-4:]
    weight_sums(x_ref[...], g_ref[...], act_ref, pre_ref, before, sums)


def weight_sums(x, g, act_ref, pre_ref, before, sums):
    hidden = act_ref.shape[1] // 2
    for i in range(2):
        for c in range(hidden // HB):
            columns = pl.ds(i * hidden + c * HB, HB)
            block = pl.ds(c * HB, HB)
            up = tn(x, pre_ref[:, columns])
            down = tn(act_ref[:, columns], g)
            if before:
                up = up + before[i][:, block].astype(F32)
                down = down + before[2 + i][block, :].astype(F32)
            sums[i][:, block] = up.astype(BF)
            sums[2 + i][block, :] = down.astype(BF)


def weight_grads(meta, x, g, act, pre, before):
    rows, d = x.shape
    hidden = act.shape[1] // 2
    shapes = [(d, hidden)] * 2 + [(hidden, d)] * 2
    return call(
        weight_kernel,
        "weight_grads",
        (1,),
        meta,
        (x, g, act, pre, *before),
        [fixed(rows, d)] * 2 + [fixed(rows, 2 * hidden)] * 2 + [fixed(*shape) for shape in shapes[: len(before)]],
        [fixed(*shape) for shape in shapes],
        [like(shape, BF) for shape in shapes],
        hold=(0, 1, 2, 3),
        out=(0, 1, 2, 3),
    )


def inner_kernel(meta_ref, own_ref, far_ref, xhat_ref, rstd_ref, vec_ref, a0, a1, w0, w1, *refs):
    last = len(refs) == 11
    out_ref, g0, g1, m0, m1, small_ref = refs[-6:]
    grad = own_ref[...] + far_ref[...].astype(F32)
    xhat = xhat_ref[...]
    gain_grad = jnp.sum(grad * xhat, axis=0, keepdims=True)
    bias_grad = jnp.sum(grad, axis=0, keepdims=True)
    gy = grad * vec_ref[0:1, :]
    mean_gy = jnp.mean(gy, axis=-1, keepdims=True)
    mean_gx = jnp.mean(gy * xhat, axis=-1, keepdims=True)
    inner = rstd_ref[:, 0:1] * (gy - mean_gy - xhat * mean_gx)
    out_ref[...] = inner
    low = inner.astype(BF)
    g0[...] = nt(w0[...], low).astype(BF)
    g1[...] = nt(w1[...], low).astype(BF)
    small = jnp.concatenate([gain_grad, bias_grad], axis=0)
    small_ref[...] = small
    if last:
        before0, before1, before_small, outer0, outer1 = refs[:5]
        below = jnp.concatenate(
            [small + before_small[...], outer0[...] + outer1[...], jnp.zeros((60, small.shape[1]), F32)], axis=0
        ).astype(BF)
        for m, a, before in ((m0, a0, before0), (m1, a1, before1)):
            m[:192, :] = (nn(a[...], low) + before[...]).astype(BF)
            m[192:, :] = below
    else:
        m0[...] = nn(a0[...], low)
        m1[...] = nn(a1[...], low)


def inner_norm(meta, own, far, xhat, rstd, vectors, att, weights, before):
    rows, d = xhat.shape
    merge = like((256, d), BF) if before else like((192, d), F32)
    return call(
        inner_kernel,
        "inner_norm",
        (1,),
        meta,
        (own, far, xhat, rstd, vectors, *att, *weights, *before),
        [fixed(rows, d)] * 3
        + [fixed(rows, 128), fixed(4, d)]
        + [fixed(192, rows)] * 2
        + [fixed(192, d)] * 2
        + ([fixed(192, d)] * 2 + [fixed(2, d)] * 3 if before else []),
        [fixed(rows, d), fixed(192, rows), fixed(192, rows), fixed(*merge.shape), fixed(*merge.shape), fixed(2, d)],
        [like((rows, d), F32), like((192, rows), BF), like((192, rows), BF), merge, merge, like((2, d), F32)],
        far=(0, 2, 3, 5, 6, 7, 8, *((9, 10) if before else ())),
        out=(1,),
        out_far=(0,) if before else (0, 3, 4),
    )


def fold_kernel(bits, meta_ref, *refs):
    for i in range(2):
        here, there = refs[2 * i : 2 * i + 2]
        if bits:
            send, keep = refs[4 + 2 * i : 6 + 2 * i]
            half = send.shape[0]
            bit = meta_ref[bits[i]]
            for part, j in ((send, 1 - bit), (keep, bit)):
                rows = pl.ds(pl.multiple_of(j * half, 16), half)
                part[...] = (here[rows, :].astype(F32) + there[rows, :].astype(F32)).astype(BF)
        else:
            refs[4 + i][...] = (here[...].astype(F32) + there[...].astype(F32)).astype(BF)


def fold(meta, pairs, bits, hold=()):
    args = [value for pair in pairs for value in pair]
    rows, d = args[0].shape
    shapes = [like((rows // 2, d), BF)] * 4 if bits else [like((rows, d), BF)] * 2
    return call(
        functools.partial(fold_kernel, bits),
        "fold",
        (1,),
        meta,
        args,
        [fixed(rows, d)] * 4,
        [fixed(*shape.shape) for shape in shapes],
        shapes,
        hold=hold,
    )


def local(groups, tokens, lengths, span_starts, wq, wk, wv, wm, wu, wd, ig, ib, og, ob, out_grad):
    rows, d = tokens.shape
    seqs = lengths.shape[0]
    frames = rows // seqs
    half = frames // 2
    core = lax.axis_index("tensor") % 2
    place_dp = lax.axis_index("dp")
    bits = groups.bit_length() - 1

    def swap(value, k):
        return lax.ppermute(value, "tensor", [(i, i ^ k) for i in range(4)])

    def swap_dp(value, k):
        return lax.ppermute(value, "dp", [(i, i ^ k) for i in range(groups)])

    def add(a, b):
        return (a.astype(F32) + b.astype(F32)).astype(BF)

    def total(pieces):
        return sum(piece.astype(F32) for piece in pieces).astype(BF) if len(pieces) > 1 else pieces[0]

    stages = [(0, 1)] + [(b, 2) for b in range(1, bits - 1, 2)] + ([(bits - 1, 1)] if bits % 2 == 0 else [])
    bit_orders = (list(range(bits)), [1, 0, *range(2, bits)])

    def spot_of(stage):
        return (place_dp >> stage[0]) & ((1 << stage[1]) - 1)

    class Chain:
        def __init__(self, part, order, cut_already=False):
            self.part = part.reshape((1,) * len(order) + part.shape) if cut_already else part
            self.order = order
            self.steps = [] if cut_already else [(True, stage) for stage in order]
            self.steps += [(False, stage) for stage in reversed(order)]

        def cut(self, stage, j):
            size = self.part.shape[0] >> stage[1]
            return lax.dynamic_slice_in_dim(self.part, (spot_of(stage) ^ j) * size, size, 0)

        def start(self):
            if self.steps:
                scatter, stage = self.steps[0]
                others = range(1, 1 << stage[1])
                self.pending = [swap_dp(self.cut(stage, j) if scatter else self.part, j << stage[0]) for j in others]

        def finish(self, *after):
            if not self.steps:
                return
            scatter, stage = self.steps.pop(0)
            got = self.pending
            if after:
                got = list(lax.optimization_barrier((*got, *after))[: len(got)])
            if scatter:
                state = total([self.cut(stage, 0)] + got)
                if not self.steps[0][0]:
                    state = state.reshape((1,) * len(self.order) + state.shape)
            else:
                axis = self.order.index(stage)
                spot = spot_of(stage)
                mine = self.part
                if len(got) == 1:
                    laid = [jnp.where(spot, got[0], mine), jnp.where(spot, mine, got[0])]
                    state = jnp.concatenate(laid, axis=axis)
                else:
                    state = jnp.zeros(mine.shape[:axis] + (1 + len(got),) + mine.shape[axis + 1 :], BF)
                    for j, piece in enumerate([mine] + got):
                        state = lax.dynamic_update_slice_in_dim(state, piece, spot ^ j, axis)
                if not self.steps:
                    state = state.reshape(-1, d)
            self.part = state

    def finish(group, *after):
        for chain in group:
            chain.finish(*after)

    def start(group):
        for chain in group:
            chain.start()

    def together(group):
        for chain, value in zip(group, lax.optimization_barrier(tuple(chain.part for chain in group))):
            chain.part = value

    all_bits = [((place_dp >> b) & 1).reshape(1) for b in range(bits)]
    scalars = jnp.concatenate([core.reshape(1), lengths, *all_bits])
    token = []

    def meta():
        return lax.optimization_barrier((scalars, *token))[0] if token else scalars

    def done(results, *others):
        token[:] = [results[0], *others]
        return results

    merge_w = (wm, swap(wm, 1), swap(wm, 2), swap(wm, 3))
    up_w = (wu, swap(wu, 1))
    down_w = (wd, swap(wd, 1))
    vectors = jnp.stack([ig, ib, og, ob])
    qkv_w = (wq.T, wk.T, wv.T)

    fwd, att, front, far = [], [], [], []
    qkv_of = [done(project(scalars, tokens, qkv_w, 0, frames))]
    for u in range(seqs):
        fwd.append(done(attend_forward(meta(), *qkv_of[u], u, frames), *(merge_w[1:] if u == 0 else ())))
        own, other = fwd[u][:2]
        att.append((own, swap(other, 1), swap(own, 2), swap(other, 3)))
        if u + 1 < seqs:
            qkv_of.append(done(project(meta(), tokens, qkv_w, u + 1, frames), up_w[1], down_w[1]))
    for u in range(seqs):
        front.append(done(ahead(meta(), tokens, att[u], merge_w, up_w, down_w, vectors, u)))
        far.append(swap(front[u][6], 2))
    out_rows, back, far_grad, smalls, sums = [], [], [], [], ()
    for u in range(seqs):
        last = u == seqs - 1
        before = (front[u][2], front[u][3], *sums) if last else ()
        res = done(astern(meta(), front[u][5], far[u], out_grad, span_starts, up_w, down_w, front[u][4], vectors, u, before))
        out_rows.append(res[0])
        back.append(res[1 if last else 3])
        smalls.append(res[3 if last else 5])
        if last:
            sent, sums = res[2], res[4:]
        else:
            far_grad.append(swap(res[4], 2))
            sums = done(weight_grads(meta(), front[u][2], res[1], front[u][3], res[2], sums))

    def inner_step(u, before):
        res = done(inner_norm(meta(), back[u], far_grad[u], front[u][0], front[u][1], vectors, att[u][:2], merge_w[:2], before))
        return res, (res[1], swap(res[2], 1))

    def attend_step(u, grads):
        return done(attend_backward(meta(), *qkv_of[u], grads, fwd[u][:2], fwd[u][2], u, frames))

    def entry_step(u, grads):
        return done(entry_back(meta(), tokens, grads, qkv_w, u, frames))


    first_bit = 1 + seqs

    def scatter(step, pairs, after, hold=()):
        pairs = [tuple(lax.optimization_barrier((*pair, after))[:2]) for pair in pairs]
        if step == bits:
            return done(fold(meta(), pairs, (), hold))
        out = done(fold(meta(), pairs, tuple(first_bit + order[step] for order in bit_orders), hold))
        return [(out[2 * i + 1], swap_dp(out[2 * i], 1 << bit_orders[i][step])) for i in range(2)]

    inner, so_far, near, crossed = [], (), [], []
    out_other = [swap(r, 1) for r in out_rows]

    def exchange(out):
        got = swap(out[0], 1)
        near.append((out[1], got))
        crossed.append(swap(total(near[-1]), 2))
        return got

    for u in range(seqs):
        last = u == seqs - 1
        if u == 0:
            up_own, up_other, down_own, down_other = lax.optimization_barrier((*sums, far_grad[0]))[:4]
            moving = [(down_own, swap(down_other, 1)), (up_own, swap(up_other, 1))]
            res, grads = inner_step(0, ())
            inner.append(res)
            far_grad.append(swap(lax.optimization_barrier((sent, res[0]))[0], 2))
            moving = scatter(0, moving, res[0])
        dqkv = attend_step(u, grads)
        moving = scatter(1 + 2 * u, moving, dqkv[0])
        if not last:
            before = ()
            if u + 1 == seqs - 1:
                before = (inner[0][3], inner[0][4], inner[0][5], *smalls)
            res, grads = inner_step(u + 1, before)
            inner.append(res)
        else:
            for step in range(4, bits + 1):
                moving = scatter(step, moving, moving[0][0])
            first, second = (
                Chain(moving[i], [(b, 1) for b in order], True) for i, order in enumerate(bit_orders)
            )
            start([first, second])
            token.extend(out_other)
        if last:
            qkv = Chain(done(joint_grads(meta(), tokens, dqkv, so_far, u, frames))[0], stages)
            qkv.start()
            out = done(entry_rows(meta(), dqkv, qkv_w, frames))
        else:
            out = entry_step(u, dqkv)
            merge_got = swap(lax.optimization_barrier((res[4], out[0]))[0], 1)
            so_far = (out[2], res[3], merge_got)
            moving = scatter(2, moving, out[0])
            exchange(out)

    got = exchange(out)
    layer_output = place(meta(), out_rows, out_other)

    finish([first, second], got)
    finish([qkv], layer_output)
    together([qkv, first, second])
    start([qkv, first, second])
    finish([qkv, first, second], *crossed)
    together([qkv, first, second])
    start([qkv, first])
    ready = []
    for u in range(seqs):
        rest = near[u][0].astype(F32) + near[u][1].astype(F32) + crossed[u].astype(F32)
        ready.append((inner[u][0] + rest).astype(BF))
    input_grad = place(scalars, ready, [swap(r, 1) for r in ready])
    finish([qkv, first])
    together([qkv, first, second])
    start([qkv, second])
    finish([qkv, second], input_grad)
    while qkv.steps or first.steps or second.steps:
        start([qkv, first, second])
        finish([qkv, first, second])
        together([qkv, first, second])
    down_sum, up_sum, joint = (chain.part for chain in (first, second, qkv))
    qkv_sum, merge_sum = joint[:576], joint[576:]
    small = merge_sum[192:196].astype(F32)
    query_grad, key_grad, value_grad = (qkv_sum[192 * i : 192 * (i + 1)].astype(F32).T for i in range(3))
    return (
        layer_output,
        input_grad,
        query_grad,
        key_grad,
        value_grad,
        merge_sum[:192].astype(F32),
        up_sum.astype(F32),
        down_sum.astype(F32),
        small[0],
        small[1],
        small[2],
        small[3],
    )


def solution(mesh):
    in_specs = (
        P("dp", None),
        P("dp"),
        P("dp", None),
        P(None, "tensor"),
        P(None, "tensor"),
        P(None, "tensor"),
        P("tensor", None),
        P(None, "tensor"),
        P("tensor", None),
        P(),
        P(),
        P(),
        P(),
        P("dp", None),
    )
    out_specs = (
        P("dp", None),
        P("dp", None),
        P(None, "tensor"),
        P(None, "tensor"),
        P(None, "tensor"),
        P("tensor", None),
        P(None, "tensor"),
        P("tensor", None),
        P(),
        P(),
        P(),
        P(),
    )
    body = functools.partial(local, mesh.shape["dp"])
    return jax.shard_map(body, mesh=mesh, in_specs=in_specs, out_specs=out_specs, check_vma=False)
```

```python
import functools

import jax
import jax.numpy as jnp
from jax import lax
from jax.experimental import pallas as pl
from jax.experimental.pallas import tpu as pltpu
from jax.sharding import PartitionSpec as P

HEAD_DIM = 64
SPAN = 10
EPS = 1e-05
LOG2E = 1.4426950408889634
KF = 1024
KB = 512
VMEM = 12
RB = 128
HB = 256
BF = jnp.bfloat16
F32 = jnp.float32
MIB = 1 << 20


def nn(a, b):
    return lax.dot_general(a, b, (((1,), (0,)), ((), ())), preferred_element_type=F32)


def nt(a, b):
    return lax.dot_general(a, b, (((1,), (1,)), ((), ())), preferred_element_type=F32)


def tn(a, b):
    return lax.dot_general(a, b, (((0,), (0,)), ((), ())), preferred_element_type=F32)


def params(limit):
    return pltpu.CompilerParams(vmem_limit_bytes=limit * MIB)


def cost(micros):
    return pl.CostEstimate(flops=int(micros * 1.1e9), bytes_accessed=1024, transcendentals=0)


MICROS = {"project": 3, "attend_forward": 8, "attend_backward": 12, "entry_back": 5, "place": 3, "ahead": 9, "astern": 10, "inner_norm": 3, "weight_grads": 4, "fold": 2, "joint_grads": 4, "entry_rows": 3}


def lane_parts(block):
    left = block[:, :128]
    lane = lax.broadcasted_iota(jnp.int32, left.shape, 1)
    zero = jnp.zeros_like(left)
    return (
        jnp.where(lane < HEAD_DIM, left, zero),
        jnp.where(lane >= HEAD_DIM, left, zero),
        block[:, 128:],
    )


TILE = (0, 0, 1)


def call(kernel, name, grid, meta, args, in_specs, out_specs, out_shape, scratch=(), limit=VMEM, hold=(), far=(), out=(), out_far=()):
    def place_input(i, value):
        space = pltpu.VMEM if i in hold else pltpu.HBM if i in far else None
        return value if space is None else pltpu.with_memory_space_constraint(value, space)

    def place_output(i, value):
        space = pltpu.VMEM if i in out else pltpu.HBM if i in out_far else None
        return value if space is None else space(value.shape, value.dtype)

    single = not isinstance(out_shape, list)
    return pl.pallas_call(
        kernel,
        grid_spec=pltpu.PrefetchScalarGridSpec(
            num_scalar_prefetch=1,
            grid=grid,
            in_specs=in_specs,
            out_specs=out_specs,
            scratch_shapes=scratch,
        ),
        out_shape=place_output(0, out_shape) if single else [place_output(i, o) for i, o in enumerate(out_shape)],
        compiler_params=params(limit),
        cost_estimate=cost(MICROS[name]),
        name=name,
    )(meta, *(place_input(i, value) for i, value in enumerate(args)))


def fixed(*shape):
    return pl.BlockSpec(shape, lambda *_: (0,) * len(shape))


def like(shape, dtype):
    return jax.ShapeDtypeStruct(shape, dtype)


def project_kernel(meta_ref, x_ref, wq_ref, wk_ref, wv_ref, q_ref, k_ref, v_ref):
    x = x_ref[...]
    for w_ref, o_ref in ((wq_ref, q_ref), (wk_ref, k_ref), (wv_ref, v_ref)):
        o_ref[:, :192] = nt(x, w_ref[...]).astype(BF)
        o_ref[:, 192:] = jnp.zeros((x.shape[0], HEAD_DIM), BF)


def project(meta, tokens, weights, u, frames):
    rows, d = frames, tokens.shape[1]
    block = 256
    return call(
        project_kernel,
        "project",
        (rows // block,),
        meta,
        (tokens, *weights),
        [pl.BlockSpec((block, d), lambda i, m: (u * (rows // block) + i, 0))] + [fixed(192, d)] * 3,
        [pl.BlockSpec((block, 256), lambda i, m: (i, 0))] * 3,
        [like((rows, 256), BF)] * 3,
        far=range(4),
        out=(0, 1, 2),
    )


def forward_kernel(u, meta_ref, q_ref, k_ref, v_ref, own_ref, other_ref, lse_ref, s_ref):
    length = meta_ref[1 + u]
    step = pl.program_id(0)
    blocks = lax.div(length + KF - 1, KF)
    parts = lane_parts(q_ref[...] * jnp.asarray(0.125, BF))
    width = q_ref.shape[0]

    def first(kb, highest):
        start = pl.multiple_of(kb * KF, KF)
        rows = pl.ds(start, KF)
        live = start + lax.broadcasted_iota(jnp.int32, (KF, width), 0) < length
        out = []
        for h in range(3):
            tile = pl.ds(128 * TILE[h], 128)
            s = nt(k_ref[rows, tile], parts[h])
            s = jnp.where(live, s, -1e30)
            s_ref[h, rows, :] = s
            out.append(jnp.maximum(highest[h], jnp.max(s, axis=0, keepdims=True)))
        return tuple(out)

    floor = jnp.full((1, width), -1e30, F32)
    highest = lax.fori_loop(0, blocks, first, (floor,) * 3)

    def second(kb, carry):
        rows = pl.ds(pl.multiple_of(kb * KF, KF), KF)
        out = []
        for h in range(3):
            total, result = carry[h]
            p = jnp.exp2((s_ref[h, rows, :] - highest[h]) * LOG2E)
            total = total + jnp.sum(p, axis=0, keepdims=True)
            v = v_ref[rows, pl.ds(128 * TILE[h], 128)]
            result = result + tn(v, p.astype(BF))
            out.append((total, result))
        return tuple(out)

    init = ((jnp.zeros((1, width), F32), jnp.zeros((128, width), F32)),) * 3
    done = lax.fori_loop(0, blocks, second, init)
    outs = []
    for h in range(3):
        total, result = done[h]
        lo = HEAD_DIM * (h % 2)
        o = result[lo : lo + HEAD_DIM] / total
        lse_ref[0, pl.ds(h, 1), :] = highest[h] * LOG2E + jnp.log2(total)
        outs.append(o.astype(BF))
    whole = jnp.concatenate(outs, axis=0)
    for j, o_ref in enumerate((own_ref, other_ref)):

        @pl.when(step == j)
        def _():
            o_ref[...] = whole


def attend_forward(meta, q, k, v, u, frames):
    half = frames // 2
    return call(
        functools.partial(forward_kernel, u),
        "attend_forward",
        (2,),
        meta,
        (q, k, v),
        [
            pl.BlockSpec((half, 256), lambda i, m: (i ^ m[0], 0)),
            fixed(frames, 256),
            fixed(frames, 256),
        ],
        [
            fixed(192, half),
            fixed(192, half),
            pl.BlockSpec((1, 8, half), lambda i, m: (i, 0, 0)),
        ],
        [
            like((192, half), BF),
            like((192, half), BF),
            like((2, 8, half), F32),
        ],
        [pltpu.VMEM((3, frames, half), F32)],
        hold=(0, 1, 2),
    )


def backward_kernel(
    u, meta_ref, q_ref, k_ref, v_ref, d0_ref, d1_ref, o0_ref, o1_ref, lse_ref,
    dq_ref, dk_ref, dv_ref, kt_ref, dk_acc, dv_acc, do_ref, o_ref,
):
    length = meta_ref[1 + u]
    blocks = lax.div(length + KB - 1, KB)
    step = pl.program_id(0)

    @pl.when(step == 0)
    def _():
        dk_acc[...] = jnp.zeros_like(dk_acc)
        dv_acc[...] = jnp.zeros_like(dv_acc)
        kt_ref[...] = jnp.transpose(k_ref[...])
        do_ref[...] = d0_ref[...]
        o_ref[...] = o0_ref[...]

    @pl.when(step == 1)
    def _():
        do_ref[...] = d1_ref[...]
        o_ref[...] = o1_ref[...]

    parts = lane_parts(q_ref[...] * jnp.asarray(0.125, BF))
    width = q_ref.shape[0]
    empty = jnp.zeros((HEAD_DIM, width), BF)
    head = [do_ref[pl.ds(h * HEAD_DIM, HEAD_DIM), :] for h in range(3)]
    grads = (
        jnp.concatenate([head[0], empty], axis=0),
        jnp.concatenate([empty, head[1]], axis=0),
        jnp.concatenate([head[2], empty], axis=0),
    )
    delta = [
        jnp.sum(
            head[h].astype(F32) * o_ref[pl.ds(h * HEAD_DIM, HEAD_DIM), :].astype(F32), axis=0, keepdims=True
        )
        for h in range(3)
    ]
    lse = [lse_ref[0, pl.ds(h, 1), :] for h in range(3)]

    def body(kb, carry):
        start = pl.multiple_of(kb * KB, KB)
        rows = pl.ds(start, KB)
        live = start + lax.broadcasted_iota(jnp.int32, (KB, width), 0) < length
        out = []
        for h in range(3):
            tile = pl.ds(128 * TILE[h], 128)
            s = nt(k_ref[rows, tile], parts[h])
            s = jnp.where(live, s, -1e30)
            p = jnp.exp2(s * LOG2E - lse[h])
            dp = nn(v_ref[rows, tile], grads[h])
            ds = (p * (dp - delta[h])).astype(BF)
            dv_acc[rows, tile] += nt(p.astype(BF), grads[h])
            dk_acc[rows, tile] += nn(ds, parts[h])
            kt = kt_ref[pl.ds(h * HEAD_DIM, HEAD_DIM), rows]
            out.append(carry[h] + nn(kt, ds))
        return tuple(out)

    zero = jnp.zeros((HEAD_DIM, width), F32)
    done = lax.fori_loop(0, blocks, body, (zero,) * 3)
    full = jnp.concatenate(done + (zero,), axis=0) * 0.125
    dq_ref[...] = jnp.transpose(full).astype(BF)

    @pl.when(step == 1)
    def _():
        dk_ref[...] = dk_acc[...].astype(BF)
        dv_ref[...] = dv_acc[...].astype(BF)


def attend_backward(meta, q, k, v, grads, outs, lse, u, frames):
    half = frames // 2
    return call(
        functools.partial(backward_kernel, u),
        "attend_backward",
        (2,),
        meta,
        (q, k, v, *grads, *outs, lse),
        [
            pl.BlockSpec((half, 256), lambda i, m: (i ^ m[0], 0)),
            fixed(frames, 256),
            fixed(frames, 256),
            fixed(192, half),
            fixed(192, half),
            fixed(192, half),
            fixed(192, half),
            pl.BlockSpec((1, 8, half), lambda i, m: (i, 0, 0)),
        ],
        [
            pl.BlockSpec((half, 256), lambda i, m: (i ^ m[0], 0)),
            fixed(frames, 256),
            fixed(frames, 256),
        ],
        [like((frames, 256), BF)] * 3,
        [
            pltpu.VMEM((256, frames), BF),
            pltpu.VMEM((frames, 256), F32),
            pltpu.VMEM((frames, 256), F32),
            pltpu.VMEM((192, half), BF),
            pltpu.VMEM((192, half), BF),
        ],
        hold=(3,),
        far=(0, 1, 2),
        out=(0, 1, 2),
    )


def entry_kernel(meta_ref, x_ref, dq_ref, dk_ref, dv_ref, wq_ref, wk_ref, wv_ref, send_ref, keep_ref, sum_ref, acc):
    step = pl.program_id(0)
    x = x_ref[...]
    total = jnp.zeros(x.shape, F32)
    for i, (g_ref, w_ref) in enumerate(((dq_ref, wq_ref), (dk_ref, wk_ref), (dv_ref, wv_ref))):
        rows = pl.ds(192 * i, 192)
        g = g_ref[:, :192]
        total = total + nn(g, w_ref[...])
        product = tn(g, x)

        @pl.when(step == 0)
        def _():
            acc[rows, :] = product

        @pl.when(step == 1)
        def _():
            sum_ref[rows, :] = product + acc[rows, :]

    low = total.astype(BF)

    @pl.when(step == 0)
    def _():
        send_ref[...] = low

    @pl.when(step == 1)
    def _():
        keep_ref[...] = low


def entry_back(meta, tokens, grads, weights, u, frames):
    half = frames // 2
    d = tokens.shape[1]
    return call(
        entry_kernel,
        "entry_back",
        (2,),
        meta,
        (tokens, *grads, *weights),
        [pl.BlockSpec((half, d), lambda i, m: (u * 2 + (1 - i ^ m[0]), 0))]
        + [pl.BlockSpec((half, 256), lambda i, m: (1 - i ^ m[0], 0))] * 3
        + [fixed(192, d)] * 3,
        [fixed(half, d), fixed(half, d), fixed(576, d)],
        [like((half, d), BF), like((half, d), BF), like((576, d), F32)],
        [pltpu.VMEM((576, d), F32)],
        hold=(1, 2, 3),
        far=(0, 4, 5, 6),
    )


def joint_kernel(meta_ref, x_ref, dq_ref, dk_ref, dv_ref, before_ref, m0_ref, m1_ref, sum_ref, acc):
    step = pl.program_id(0)
    x = x_ref[...]
    for i, g_ref in enumerate((dq_ref, dk_ref, dv_ref)):
        rows = pl.ds(192 * i, 192)
        product = tn(g_ref[:, :192], x)

        @pl.when(step == 0)
        def _():
            acc[rows, :] = product

        @pl.when(step == 1)
        def _():
            sum_ref[rows, :] = (product + acc[rows, :] + before_ref[rows, :]).astype(BF)

    @pl.when(step == 0)
    def _():
        sum_ref[576:, :] = (m0_ref[...].astype(F32) + m1_ref[...].astype(F32)).astype(BF)


def joint_grads(meta, tokens, grads, before, u, frames):
    half = frames // 2
    d = tokens.shape[1]
    return call(
        joint_kernel,
        "joint_grads",
        (2,),
        meta,
        (tokens, *grads, *before),
        [pl.BlockSpec((half, d), lambda i, m: (u * 2 + i, 0))]
        + [pl.BlockSpec((half, 256), lambda i, m: (i, 0))] * 3
        + [fixed(*value.shape) for value in before],
        [fixed(832, d)],
        [like((832, d), BF)],
        [pltpu.VMEM((576, d), F32)],
        hold=(1, 2, 3),
        far=(0,),
    )


def rows_kernel(meta_ref, dq_ref, dk_ref, dv_ref, wq_ref, wk_ref, wv_ref, send_ref, keep_ref):
    total = sum(nn(g[:, :192], w[...]) for g, w in ((dq_ref, wq_ref), (dk_ref, wk_ref), (dv_ref, wv_ref)))
    for j, o_ref in enumerate((send_ref, keep_ref)):

        @pl.when(pl.program_id(0) == j)
        def _():
            o_ref[...] = total.astype(BF)


def entry_rows(meta, grads, weights, frames):
    half = frames // 2
    d = weights[0].shape[1]
    return call(
        rows_kernel,
        "entry_rows",
        (2,),
        meta,
        (*grads, *weights),
        [pl.BlockSpec((half, 256), lambda i, m: (1 - i ^ m[0], 0))] * 3 + [fixed(192, d)] * 3,
        [fixed(half, d), fixed(half, d)],
        [like((half, d), BF), like((half, d), BF)],
        hold=(0, 1, 2),
        far=(3, 4, 5),
    )


def place_kernel(meta_ref, *refs):
    o_ref = refs[-1]
    for i, r_ref in enumerate(refs[:-1]):

        @pl.when(pl.program_id(0) == i)
        def _():
            o_ref[...] = r_ref[...]


def place(meta, own, other):
    half, d = own[0].shape
    count = 2 * len(own)
    return call(
        place_kernel,
        "place",
        (count,),
        meta,
        [block for pair in zip(own, other) for block in pair],
        [fixed(half, d)] * count,
        pl.BlockSpec((half, d), lambda i, m: (i ^ m[0], 0)),
        like((count * half, d), own[0].dtype),
    )


def normalise(values):
    average = jnp.mean(values, axis=-1, keepdims=True)
    centred = values - average
    spread = jnp.mean(centred * centred, axis=-1, keepdims=True)
    rstd = lax.rsqrt(spread + EPS)
    return centred * rstd, rstd


def gelu_pair(v):
    e = jnp.exp2(v * v * (-0.5 * LOG2E))
    t = 1.0 / (1.0 + (0.3275911 * 0.7071067811865476) * jnp.abs(v))
    poly = t * (0.5 * 0.254829592 + t * (0.5 * -0.284496736 + t * (0.5 * 1.421413741 + t * (0.5 * -1.453152027 + t * (0.5 * 1.061405429)))))
    tail = poly * e
    phi_cap = jnp.where(v >= 0, 1.0 - tail, tail)
    return v * phi_cap, phi_cap + v * (e * 0.3989422804014327)


def ahead_kernel(
    meta_ref, tok_ref, a0, a1, a2, a3, w0, w1, w2, w3, ua_ref, ub_ref, da_ref, db_ref, vec_ref,
    xhat_ref, rstd_ref, low_ref, act_ref, slope_ref, own_ref, sent_ref,
):
    gain, bias = vec_ref[0:1, :], vec_ref[1:2, :]
    hidden = ua_ref.shape[1]
    for r in range(tok_ref.shape[0] // RB):
        rows = pl.ds(r * RB, RB)
        branch = jnp.zeros((RB, tok_ref.shape[1]), F32)
        for a, w in ((a0, w0), (a1, w1), (a2, w2), (a3, w3)):
            branch = branch + tn(a[:, rows], w[...]).astype(BF).astype(F32)
        xhat, rstd = normalise(tok_ref[rows, :].astype(F32) + branch)
        xhat_ref[rows, :] = xhat
        rstd_ref[rows, :] = jnp.broadcast_to(rstd, (RB, rstd_ref.shape[1]))
        normed = xhat * gain + bias
        low = normed.astype(BF)
        low_ref[rows, :] = low
        sent = jnp.zeros(normed.shape, F32)
        for g, (up, down) in enumerate(((ua_ref, da_ref), (ub_ref, db_ref))):
            acts = []
            for c in range(hidden // HB):
                act, slope = gelu_pair(nn(low, up[:, c * HB : (c + 1) * HB]))
                columns = pl.ds(g * hidden + c * HB, HB)
                acts.append(act.astype(BF))
                act_ref[rows, columns] = acts[-1]
                slope_ref[rows, columns] = slope.astype(BF)
            sent = sent + nn(jnp.concatenate(acts, axis=1), down[...]).astype(BF).astype(F32)
        own_ref[rows, :] = normed + sent
        sent_ref[rows, :] = sent.astype(BF)


def ahead(meta, tokens, att, merge_w, up, down, vectors, u):
    half = att[0].shape[1]
    d, hidden = up[0].shape
    return call(
        ahead_kernel,
        "ahead",
        (1,),
        meta,
        (tokens, *att, *merge_w, *up, *down, vectors),
        [pl.BlockSpec((half, d), lambda i, m: (u * 2 + m[0], 0))]
        + [fixed(192, half)] * 4
        + [fixed(192, d)] * 4
        + [fixed(d, hidden)] * 2
        + [fixed(hidden, d)] * 2
        + [fixed(4, d)],
        [fixed(half, d), fixed(half, 128), fixed(half, d), fixed(half, 2 * hidden), fixed(half, 2 * hidden), fixed(half, d), fixed(half, d)],
        [
            like((half, d), F32),
            like((half, 128), F32),
            like((half, d), BF),
            like((half, 2 * hidden), BF),
            like((half, 2 * hidden), BF),
            like((half, d), F32),
            like((half, d), BF),
        ],
        far=(0,),
        out=(2, 3, 4, 5),
        out_far=(0, 1),
    )


def astern_kernel(u, meta_ref, own_ref, far_ref, grad_ref, span_ref, ua_ref, ub_ref, da_ref, db_ref, slope_ref, vec_ref, *refs):
    last = len(refs) > 6
    if last:
        before = refs[:-10]
        out_ref, back_ref, sent_ref, small_ref, *sums, g_ref, pre_ref = refs[-10:]
    else:
        out_ref, g_ref, pre_ref, back_ref, sent_ref, small_ref = refs
    gain, bias = vec_ref[2:3, :], vec_ref[3:4, :]
    half, d = own_ref.shape
    hidden = ua_ref.shape[1]
    starts = span_ref[u : u + 1, :]
    gain_grad = jnp.zeros(gain.shape, F32)
    bias_grad = jnp.zeros(gain.shape, F32)
    for r in range(half // RB):
        rows = pl.ds(r * RB, RB)
        xhat, rstd = normalise(own_ref[rows, :] + far_ref[rows, :].astype(F32))
        out_ref[rows, :] = (xhat * gain + bias).astype(BF)
        frame = meta_ref[0] * half + r * RB + lax.broadcasted_iota(jnp.int32, (RB, starts.shape[1]), 0)
        inside = (frame >= starts) & (frame < starts + SPAN)
        weight = jnp.max(jnp.where(inside, 1.0, 0.0), axis=1, keepdims=True)
        cot = grad_ref[rows, :].astype(F32) * weight
        gain_grad = gain_grad + jnp.sum(cot * xhat, axis=0, keepdims=True)
        bias_grad = bias_grad + jnp.sum(cot, axis=0, keepdims=True)
        gy = cot * gain
        mean_gy = jnp.mean(gy, axis=-1, keepdims=True)
        mean_gx = jnp.mean(gy * xhat, axis=-1, keepdims=True)
        sum_grad = rstd * (gy - mean_gy - xhat * mean_gx)
        low = sum_grad.astype(BF)
        g_ref[rows, :] = low
        sent = jnp.zeros(sum_grad.shape, F32)
        for g, (up, down) in enumerate(((ua_ref, da_ref), (ub_ref, db_ref))):
            pres = []
            for c in range(hidden // HB):
                columns = pl.ds(g * hidden + c * HB, HB)
                slope = slope_ref[rows, columns].astype(F32)
                pres.append((nt(low, down[c * HB : (c + 1) * HB, :]) * slope).astype(BF))
                pre_ref[rows, columns] = pres[-1]
            sent = sent + nt(jnp.concatenate(pres, axis=1), up[...]).astype(BF).astype(F32)
        back_ref[rows, :] = sum_grad + sent
        sent_ref[rows, :] = sent.astype(BF)
    small_ref[0:1, :] = gain_grad
    small_ref[1:2, :] = bias_grad
    if last:
        x_ref, act_ref = before[:2]
        weight_sums(x_ref[...], g_ref[...], act_ref, pre_ref, before[2:], sums)


def astern(meta, own, far, grad, spans, up, down, slope, vectors, u, before):
    half, d = own.shape
    hidden = up[0].shape[1]
    rows = fixed(half, d)
    wide = fixed(half, 2 * hidden)
    grads = [] if not before else [(d, hidden)] * 2 + [(hidden, d)] * 2
    extra = [] if not before else [rows, wide] + [fixed(*shape) for shape in grads[: len(before) - 2]]
    made = [like((half, d), BF), like((half, 2 * hidden), BF)]
    others = [like((half, d), F32), like((half, d), BF), like((2, d), F32)]
    shapes = [like((half, d), BF)] + ([] if before else made) + others + [like(shape, BF) for shape in grads]
    return call(
        functools.partial(astern_kernel, u),
        "astern",
        (1,),
        meta,
        (own, far, grad, spans, *up, *down, slope, vectors, *before),
        [rows] * 2
        + [pl.BlockSpec((half, d), lambda i, m: (u * 2 + m[0], 0)), fixed(*spans.shape)]
        + [fixed(d, hidden)] * 2
        + [fixed(hidden, d)] * 2
        + [wide, fixed(4, d)]
        + extra,
        [fixed(*shape.shape) for shape in shapes],
        shapes,
        [pltpu.VMEM(shape.shape, shape.dtype) for shape in made] if before else (),
        limit=20 if before else VMEM,
        hold=(0, 8, *range(10, 10 + len(before))),
        far=(2,),
        out=() if before else (1, 2),
        out_far=(0, 1) if before else (0, 3),
    )


def weight_kernel(meta_ref, x_ref, g_ref, act_ref, pre_ref, *refs):
    before, sums = refs[:-4], refs[-4:]
    weight_sums(x_ref[...], g_ref[...], act_ref, pre_ref, before, sums)


def weight_sums(x, g, act_ref, pre_ref, before, sums):
    hidden = act_ref.shape[1] // 2
    for i in range(2):
        for c in range(hidden // HB):
            columns = pl.ds(i * hidden + c * HB, HB)
            block = pl.ds(c * HB, HB)
            up = tn(x, pre_ref[:, columns])
            down = tn(act_ref[:, columns], g)
            if before:
                up = up + before[i][:, block].astype(F32)
                down = down + before[2 + i][block, :].astype(F32)
            sums[i][:, block] = up.astype(BF)
            sums[2 + i][block, :] = down.astype(BF)


def weight_grads(meta, x, g, act, pre, before):
    rows, d = x.shape
    hidden = act.shape[1] // 2
    shapes = [(d, hidden)] * 2 + [(hidden, d)] * 2
    return call(
        weight_kernel,
        "weight_grads",
        (1,),
        meta,
        (x, g, act, pre, *before),
        [fixed(rows, d)] * 2 + [fixed(rows, 2 * hidden)] * 2 + [fixed(*shape) for shape in shapes[: len(before)]],
        [fixed(*shape) for shape in shapes],
        [like(shape, BF) for shape in shapes],
        hold=(0, 1, 2, 3),
        out=(0, 1, 2, 3),
    )


def inner_kernel(meta_ref, own_ref, far_ref, xhat_ref, rstd_ref, vec_ref, a0, a1, w0, w1, *refs):
    last = len(refs) == 11
    out_ref, g0, g1, m0, m1, small_ref = refs[-6:]
    grad = own_ref[...] + far_ref[...].astype(F32)
    xhat = xhat_ref[...]
    gain_grad = jnp.sum(grad * xhat, axis=0, keepdims=True)
    bias_grad = jnp.sum(grad, axis=0, keepdims=True)
    gy = grad * vec_ref[0:1, :]
    mean_gy = jnp.mean(gy, axis=-1, keepdims=True)
    mean_gx = jnp.mean(gy * xhat, axis=-1, keepdims=True)
    inner = rstd_ref[:, 0:1] * (gy - mean_gy - xhat * mean_gx)
    out_ref[...] = inner
    low = inner.astype(BF)
    g0[...] = nt(w0[...], low).astype(BF)
    g1[...] = nt(w1[...], low).astype(BF)
    small = jnp.concatenate([gain_grad, bias_grad], axis=0)
    small_ref[...] = small
    if last:
        before0, before1, before_small, outer0, outer1 = refs[:5]
        below = jnp.concatenate(
            [small + before_small[...], outer0[...] + outer1[...], jnp.zeros((60, small.shape[1]), F32)], axis=0
        ).astype(BF)
        for m, a, before in ((m0, a0, before0), (m1, a1, before1)):
            m[:192, :] = (nn(a[...], low) + before[...]).astype(BF)
            m[192:, :] = below
    else:
        m0[...] = nn(a0[...], low)
        m1[...] = nn(a1[...], low)


def inner_norm(meta, own, far, xhat, rstd, vectors, att, weights, before):
    rows, d = xhat.shape
    merge = like((256, d), BF) if before else like((192, d), F32)
    return call(
        inner_kernel,
        "inner_norm",
        (1,),
        meta,
        (own, far, xhat, rstd, vectors, *att, *weights, *before),
        [fixed(rows, d)] * 3
        + [fixed(rows, 128), fixed(4, d)]
        + [fixed(192, rows)] * 2
        + [fixed(192, d)] * 2
        + ([fixed(192, d)] * 2 + [fixed(2, d)] * 3 if before else []),
        [fixed(rows, d), fixed(192, rows), fixed(192, rows), fixed(*merge.shape), fixed(*merge.shape), fixed(2, d)],
        [like((rows, d), F32), like((192, rows), BF), like((192, rows), BF), merge, merge, like((2, d), F32)],
        far=(0, 2, 3, 5, 6, 7, 8, *((9, 10) if before else ())),
        out=(1,),
        out_far=(0,) if before else (0, 3, 4),
    )


def fold_kernel(bits, meta_ref, *refs):
    for i in range(2):
        here, there = refs[2 * i : 2 * i + 2]
        if bits:
            send, keep = refs[4 + 2 * i : 6 + 2 * i]
            half = send.shape[0]
            bit = meta_ref[bits[i]]
            for part, j in ((send, 1 - bit), (keep, bit)):
                rows = pl.ds(pl.multiple_of(j * half, 16), half)
                part[...] = (here[rows, :].astype(F32) + there[rows, :].astype(F32)).astype(BF)
        else:
            refs[4 + i][...] = (here[...].astype(F32) + there[...].astype(F32)).astype(BF)


def fold(meta, pairs, bits, hold=()):
    args = [value for pair in pairs for value in pair]
    rows, d = args[0].shape
    shapes = [like((rows // 2, d), BF)] * 4 if bits else [like((rows, d), BF)] * 2
    return call(
        functools.partial(fold_kernel, bits),
        "fold",
        (1,),
        meta,
        args,
        [fixed(rows, d)] * 4,
        [fixed(*shape.shape) for shape in shapes],
        shapes,
        hold=hold,
    )


def local(groups, tokens, lengths, span_starts, wq, wk, wv, wm, wu, wd, ig, ib, og, ob, out_grad):
    rows, d = tokens.shape
    seqs = lengths.shape[0]
    frames = rows // seqs
    half = frames // 2
    core = lax.axis_index("tensor") % 2
    place_dp = lax.axis_index("dp")
    bits = groups.bit_length() - 1

    def swap(value, k):
        return lax.ppermute(value, "tensor", [(i, i ^ k) for i in range(4)])

    def swap_dp(value, k):
        return lax.ppermute(value, "dp", [(i, i ^ k) for i in range(groups)])

    def add(a, b):
        return (a.astype(F32) + b.astype(F32)).astype(BF)

    def total(pieces):
        return sum(piece.astype(F32) for piece in pieces).astype(BF) if len(pieces) > 1 else pieces[0]

    stages = [(0, 1)] + [(b, 2) for b in range(1, bits - 1, 2)] + ([(bits - 1, 1)] if bits % 2 == 0 else [])
    bit_orders = (list(range(bits)), [1, 0, *range(2, bits)])

    def spot_of(stage):
        return (place_dp >> stage[0]) & ((1 << stage[1]) - 1)

    class Chain:
        def __init__(self, part, order, cut_already=False):
            self.part = part.reshape((1,) * len(order) + part.shape) if cut_already else part
            self.order = order
            self.steps = [] if cut_already else [(True, stage) for stage in order]
            self.steps += [(False, stage) for stage in reversed(order)]

        def cut(self, stage, j):
            size = self.part.shape[0] >> stage[1]
            return lax.dynamic_slice_in_dim(self.part, (spot_of(stage) ^ j) * size, size, 0)

        def start(self):
            if self.steps:
                scatter, stage = self.steps[0]
                others = range(1, 1 << stage[1])
                self.pending = [swap_dp(self.cut(stage, j) if scatter else self.part, j << stage[0]) for j in others]

        def finish(self, *after):
            if not self.steps:
                return
            scatter, stage = self.steps.pop(0)
            got = self.pending
            if after:
                got = list(lax.optimization_barrier((*got, *after))[: len(got)])
            if scatter:
                state = total([self.cut(stage, 0)] + got)
                if not self.steps[0][0]:
                    state = state.reshape((1,) * len(self.order) + state.shape)
            else:
                axis = self.order.index(stage)
                spot = spot_of(stage)
                mine = self.part
                if len(got) == 1:
                    laid = [jnp.where(spot, got[0], mine), jnp.where(spot, mine, got[0])]
                    state = jnp.concatenate(laid, axis=axis)
                else:
                    state = jnp.zeros(mine.shape[:axis] + (1 + len(got),) + mine.shape[axis + 1 :], BF)
                    for j, piece in enumerate([mine] + got):
                        state = lax.dynamic_update_slice_in_dim(state, piece, spot ^ j, axis)
                if not self.steps:
                    state = state.reshape(-1, d)
            self.part = state

    def finish(group, *after):
        for chain in group:
            chain.finish(*after)

    def start(group):
        for chain in group:
            chain.start()

    def together(group):
        for chain, value in zip(group, lax.optimization_barrier(tuple(chain.part for chain in group))):
            chain.part = value

    all_bits = [((place_dp >> b) & 1).reshape(1) for b in range(bits)]
    scalars = jnp.concatenate([core.reshape(1), lengths, *all_bits])
    token = []

    def meta():
        return lax.optimization_barrier((scalars, *token))[0] if token else scalars

    def done(results, *others):
        token[:] = [results[0], *others]
        return results

    merge_w = (wm, swap(wm, 1), swap(wm, 2), swap(wm, 3))
    up_w = (wu, swap(wu, 1))
    down_w = (wd, swap(wd, 1))
    vectors = jnp.stack([ig, ib, og, ob])
    qkv_w = (wq.T, wk.T, wv.T)

    fwd, att, front, far = [], [], [], []
    qkv_of = [done(project(scalars, tokens, qkv_w, 0, frames))]
    for u in range(seqs):
        fwd.append(done(attend_forward(meta(), *qkv_of[u], u, frames), *(merge_w[1:] if u == 0 else ())))
        own, other = fwd[u][:2]
        att.append((own, swap(other, 1), swap(own, 2), swap(other, 3)))
        if u + 1 < seqs:
            qkv_of.append(done(project(meta(), tokens, qkv_w, u + 1, frames), up_w[1], down_w[1]))
    for u in range(seqs):
        front.append(done(ahead(meta(), tokens, att[u], merge_w, up_w, down_w, vectors, u)))
        far.append(swap(front[u][6], 2))
    out_rows, back, far_grad, smalls, sums = [], [], [], [], ()
    for u in range(seqs):
        last = u == seqs - 1
        before = (front[u][2], front[u][3], *sums) if last else ()
        res = done(astern(meta(), front[u][5], far[u], out_grad, span_starts, up_w, down_w, front[u][4], vectors, u, before))
        out_rows.append(res[0])
        back.append(res[1 if last else 3])
        smalls.append(res[3 if last else 5])
        if last:
            sent, sums = res[2], res[4:]
        else:
            far_grad.append(swap(res[4], 2))
            sums = done(weight_grads(meta(), front[u][2], res[1], front[u][3], res[2], sums))

    def inner_step(u, before):
        res = done(inner_norm(meta(), back[u], far_grad[u], front[u][0], front[u][1], vectors, att[u][:2], merge_w[:2], before))
        return res, (res[1], swap(res[2], 1))

    def attend_step(u, grads):
        return done(attend_backward(meta(), *qkv_of[u], grads, fwd[u][:2], fwd[u][2], u, frames))

    def entry_step(u, grads):
        return done(entry_back(meta(), tokens, grads, qkv_w, u, frames))


    first_bit = 1 + seqs

    def scatter(step, pairs, after, hold=()):
        pairs = [tuple(lax.optimization_barrier((*pair, after))[:2]) for pair in pairs]
        if step == bits:
            return done(fold(meta(), pairs, (), hold))
        out = done(fold(meta(), pairs, tuple(first_bit + order[step] for order in bit_orders), hold))
        return [(out[2 * i + 1], swap_dp(out[2 * i], 1 << bit_orders[i][step])) for i in range(2)]

    inner, so_far, near, crossed = [], (), [], []
    out_other = [swap(r, 1) for r in out_rows]

    def exchange(out):
        got = swap(out[0], 1)
        near.append((out[1], got))
        crossed.append(swap(total(near[-1]), 2))
        return got

    for u in range(seqs):
        last = u == seqs - 1
        if u == 0:
            up_own, up_other, down_own, down_other = lax.optimization_barrier((*sums, far_grad[0]))[:4]
            moving = [(down_own, swap(down_other, 1)), (up_own, swap(up_other, 1))]
            res, grads = inner_step(0, ())
            inner.append(res)
            far_grad.append(swap(lax.optimization_barrier((sent, res[0]))[0], 2))
            moving = scatter(0, moving, res[0])
        dqkv = attend_step(u, grads)
        moving = scatter(1 + 2 * u, moving, dqkv[0])
        if not last:
            before = ()
            if u + 1 == seqs - 1:
                before = (inner[0][3], inner[0][4], inner[0][5], *smalls)
            res, grads = inner_step(u + 1, before)
            inner.append(res)
        else:
            for step in range(4, bits + 1):
                moving = scatter(step, moving, moving[0][0])
            first, second = (
                Chain(moving[i], [(b, 1) for b in order], True) for i, order in enumerate(bit_orders)
            )
            start([first, second])
            token.extend(out_other)
        if last:
            qkv = Chain(done(joint_grads(meta(), tokens, dqkv, so_far, u, frames))[0], stages)
            qkv.start()
            out = done(entry_rows(meta(), dqkv, qkv_w, frames))
        else:
            out = entry_step(u, dqkv)
            merge_got = swap(lax.optimization_barrier((res[4], out[0]))[0], 1)
            so_far = (out[2], res[3], merge_got)
            moving = scatter(2, moving, out[0])
            exchange(out)

    got = exchange(out)
    layer_output = place(meta(), out_rows, out_other)

    finish([first, second], got)
    finish([qkv])
    together([qkv, first, second])
    start([qkv, first, second])
    finish([qkv, first, second], crossed[0])
    together([qkv, first, second])
    start([qkv, first])
    finish([qkv, first], crossed[1], layer_output)
    together([qkv, first, second])
    start([qkv, second])
    ready = []
    for u in range(seqs):
        rest = near[u][0].astype(F32) + near[u][1].astype(F32) + crossed[u].astype(F32)
        ready.append((inner[u][0] + rest).astype(BF))
    input_grad = place(scalars, ready, [swap(r, 1) for r in ready])
    finish([qkv, second], input_grad)
    while qkv.steps or first.steps or second.steps:
        start([qkv, first, second])
        finish([qkv, first, second])
        together([qkv, first, second])
    down_sum, up_sum, joint = (chain.part for chain in (first, second, qkv))
    qkv_sum, merge_sum = joint[:576], joint[576:]
    small = merge_sum[192:196].astype(F32)
    query_grad, key_grad, value_grad = (qkv_sum[192 * i : 192 * (i + 1)].astype(F32).T for i in range(3))
    return (
        layer_output,
        input_grad,
        query_grad,
        key_grad,
        value_grad,
        merge_sum[:192].astype(F32),
        up_sum.astype(F32),
        down_sum.astype(F32),
        small[0],
        small[1],
        small[2],
        small[3],
    )


def solution(mesh):
    in_specs = (
        P("dp", None),
        P("dp"),
        P("dp", None),
        P(None, "tensor"),
        P(None, "tensor"),
        P(None, "tensor"),
        P("tensor", None),
        P(None, "tensor"),
        P("tensor", None),
        P(),
        P(),
        P(),
        P(),
        P("dp", None),
    )
    out_specs = (
        P("dp", None),
        P("dp", None),
        P(None, "tensor"),
        P(None, "tensor"),
        P(None, "tensor"),
        P("tensor", None),
        P(None, "tensor"),
        P("tensor", None),
        P(),
        P(),
        P(),
        P(),
    )
    body = functools.partial(local, mesh.shape["dp"])
    return jax.shard_map(body, mesh=mesh, in_specs=in_specs, out_specs=out_specs, check_vma=False)
```

```python
import functools

import jax
import jax.numpy as jnp
from jax import lax
from jax.experimental import pallas as pl
from jax.experimental.pallas import tpu as pltpu
from jax.sharding import PartitionSpec as P

HEAD_DIM = 64
SPAN = 10
EPS = 1e-05
LOG2E = 1.4426950408889634
KF = 1024
KB = 512
VMEM = 12
RB = 128
HB = 256
BF = jnp.bfloat16
F32 = jnp.float32
MIB = 1 << 20


def nn(a, b):
    return lax.dot_general(a, b, (((1,), (0,)), ((), ())), preferred_element_type=F32)


def nt(a, b):
    return lax.dot_general(a, b, (((1,), (1,)), ((), ())), preferred_element_type=F32)


def tn(a, b):
    return lax.dot_general(a, b, (((0,), (0,)), ((), ())), preferred_element_type=F32)


def params(limit):
    return pltpu.CompilerParams(vmem_limit_bytes=limit * MIB)


def cost(micros):
    return pl.CostEstimate(flops=int(micros * 1.1e9), bytes_accessed=1024, transcendentals=0)


MICROS = {"project": 3, "attend_forward": 8, "attend_backward": 12, "entry_back": 5, "place": 3, "ahead": 9, "astern": 10, "inner_norm": 3, "weight_grads": 4, "fold": 2}


def lane_parts(block):
    left = block[:, :128]
    lane = lax.broadcasted_iota(jnp.int32, left.shape, 1)
    zero = jnp.zeros_like(left)
    return (
        jnp.where(lane < HEAD_DIM, left, zero),
        jnp.where(lane >= HEAD_DIM, left, zero),
        block[:, 128:],
    )


TILE = (0, 0, 1)


def call(kernel, name, grid, meta, args, in_specs, out_specs, out_shape, scratch=(), limit=VMEM, hold=(), far=(), out=(), out_far=()):
    def place_input(i, value):
        space = pltpu.VMEM if i in hold else pltpu.HBM if i in far else None
        return value if space is None else pltpu.with_memory_space_constraint(value, space)

    def place_output(i, value):
        space = pltpu.VMEM if i in out else pltpu.HBM if i in out_far else None
        return value if space is None else space(value.shape, value.dtype)

    single = not isinstance(out_shape, list)
    return pl.pallas_call(
        kernel,
        grid_spec=pltpu.PrefetchScalarGridSpec(
            num_scalar_prefetch=1,
            grid=grid,
            in_specs=in_specs,
            out_specs=out_specs,
            scratch_shapes=scratch,
        ),
        out_shape=place_output(0, out_shape) if single else [place_output(i, o) for i, o in enumerate(out_shape)],
        compiler_params=params(limit),
        cost_estimate=cost(MICROS[name]),
        name=name,
    )(meta, *(place_input(i, value) for i, value in enumerate(args)))


def fixed(*shape):
    return pl.BlockSpec(shape, lambda *_: (0,) * len(shape))


def like(shape, dtype):
    return jax.ShapeDtypeStruct(shape, dtype)


def project_kernel(meta_ref, x_ref, wq_ref, wk_ref, wv_ref, q_ref, k_ref, v_ref):
    x = x_ref[...]
    for w_ref, o_ref in ((wq_ref, q_ref), (wk_ref, k_ref), (wv_ref, v_ref)):
        o_ref[:, :192] = nt(x, w_ref[...]).astype(BF)
        o_ref[:, 192:] = jnp.zeros((x.shape[0], HEAD_DIM), BF)


def project(meta, tokens, weights, u, frames):
    rows, d = frames, tokens.shape[1]
    block = 256
    return call(
        project_kernel,
        "project",
        (rows // block,),
        meta,
        (tokens, *weights),
        [pl.BlockSpec((block, d), lambda i, m: (u * (rows // block) + i, 0))] + [fixed(192, d)] * 3,
        [pl.BlockSpec((block, 256), lambda i, m: (i, 0))] * 3,
        [like((rows, 256), BF)] * 3,
        far=range(4),
        out=(0, 1, 2),
    )


def forward_kernel(u, meta_ref, q_ref, k_ref, v_ref, own_ref, other_ref, lse_ref, s_ref):
    length = meta_ref[1 + u]
    step = pl.program_id(0)
    blocks = lax.div(length + KF - 1, KF)
    parts = lane_parts(q_ref[...] * jnp.asarray(0.125, BF))
    width = q_ref.shape[0]

    def first(kb, highest):
        start = pl.multiple_of(kb * KF, KF)
        rows = pl.ds(start, KF)
        live = start + lax.broadcasted_iota(jnp.int32, (KF, width), 0) < length
        out = []
        for h in range(3):
            tile = pl.ds(128 * TILE[h], 128)
            s = nt(k_ref[rows, tile], parts[h])
            s = jnp.where(live, s, -1e30)
            s_ref[h, rows, :] = s
            out.append(jnp.maximum(highest[h], jnp.max(s, axis=0, keepdims=True)))
        return tuple(out)

    floor = jnp.full((1, width), -1e30, F32)
    highest = lax.fori_loop(0, blocks, first, (floor,) * 3)

    def second(kb, carry):
        rows = pl.ds(pl.multiple_of(kb * KF, KF), KF)
        out = []
        for h in range(3):
            total, result = carry[h]
            p = jnp.exp2((s_ref[h, rows, :] - highest[h]) * LOG2E)
            total = total + jnp.sum(p, axis=0, keepdims=True)
            v = v_ref[rows, pl.ds(128 * TILE[h], 128)]
            result = result + tn(v, p.astype(BF))
            out.append((total, result))
        return tuple(out)

    init = ((jnp.zeros((1, width), F32), jnp.zeros((128, width), F32)),) * 3
    done = lax.fori_loop(0, blocks, second, init)
    outs = []
    for h in range(3):
        total, result = done[h]
        lo = HEAD_DIM * (h % 2)
        o = result[lo : lo + HEAD_DIM] / total
        lse_ref[0, pl.ds(h, 1), :] = highest[h] * LOG2E + jnp.log2(total)
        outs.append(o.astype(BF))
    whole = jnp.concatenate(outs, axis=0)
    for j, o_ref in enumerate((own_ref, other_ref)):

        @pl.when(step == j)
        def _():
            o_ref[...] = whole


def attend_forward(meta, q, k, v, u, frames):
    half = frames // 2
    return call(
        functools.partial(forward_kernel, u),
        "attend_forward",
        (2,),
        meta,
        (q, k, v),
        [
            pl.BlockSpec((half, 256), lambda i, m: (i ^ m[0], 0)),
            fixed(frames, 256),
            fixed(frames, 256),
        ],
        [
            fixed(192, half),
            fixed(192, half),
            pl.BlockSpec((1, 8, half), lambda i, m: (i, 0, 0)),
        ],
        [
            like((192, half), BF),
            like((192, half), BF),
            like((2, 8, half), F32),
        ],
        [pltpu.VMEM((3, frames, half), F32)],
        hold=(0, 1, 2),
    )


def backward_kernel(
    u, meta_ref, q_ref, k_ref, v_ref, d0_ref, d1_ref, o0_ref, o1_ref, lse_ref,
    dq_ref, dk_ref, dv_ref, kt_ref, dk_acc, dv_acc, do_ref, o_ref,
):
    length = meta_ref[1 + u]
    blocks = lax.div(length + KB - 1, KB)
    step = pl.program_id(0)

    @pl.when(step == 0)
    def _():
        dk_acc[...] = jnp.zeros_like(dk_acc)
        dv_acc[...] = jnp.zeros_like(dv_acc)
        kt_ref[...] = jnp.transpose(k_ref[...])
        do_ref[...] = d0_ref[...]
        o_ref[...] = o0_ref[...]

    @pl.when(step == 1)
    def _():
        do_ref[...] = d1_ref[...]
        o_ref[...] = o1_ref[...]

    parts = lane_parts(q_ref[...] * jnp.asarray(0.125, BF))
    width = q_ref.shape[0]
    empty = jnp.zeros((HEAD_DIM, width), BF)
    head = [do_ref[pl.ds(h * HEAD_DIM, HEAD_DIM), :] for h in range(3)]
    grads = (
        jnp.concatenate([head[0], empty], axis=0),
        jnp.concatenate([empty, head[1]], axis=0),
        jnp.concatenate([head[2], empty], axis=0),
    )
    delta = [
        jnp.sum(
            head[h].astype(F32) * o_ref[pl.ds(h * HEAD_DIM, HEAD_DIM), :].astype(F32), axis=0, keepdims=True
        )
        for h in range(3)
    ]
    lse = [lse_ref[0, pl.ds(h, 1), :] for h in range(3)]

    def body(kb, carry):
        start = pl.multiple_of(kb * KB, KB)
        rows = pl.ds(start, KB)
        live = start + lax.broadcasted_iota(jnp.int32, (KB, width), 0) < length
        out = []
        for h in range(3):
            tile = pl.ds(128 * TILE[h], 128)
            s = nt(k_ref[rows, tile], parts[h])
            s = jnp.where(live, s, -1e30)
            p = jnp.exp2(s * LOG2E - lse[h])
            dp = nn(v_ref[rows, tile], grads[h])
            ds = (p * (dp - delta[h])).astype(BF)
            dv_acc[rows, tile] += nt(p.astype(BF), grads[h])
            dk_acc[rows, tile] += nn(ds, parts[h])
            kt = kt_ref[pl.ds(h * HEAD_DIM, HEAD_DIM), rows]
            out.append(carry[h] + nn(kt, ds))
        return tuple(out)

    zero = jnp.zeros((HEAD_DIM, width), F32)
    done = lax.fori_loop(0, blocks, body, (zero,) * 3)
    full = jnp.concatenate(done + (zero,), axis=0) * 0.125
    dq_ref[...] = jnp.transpose(full).astype(BF)

    @pl.when(step == 1)
    def _():
        dk_ref[...] = dk_acc[...].astype(BF)
        dv_ref[...] = dv_acc[...].astype(BF)


def attend_backward(meta, q, k, v, grads, outs, lse, u, frames):
    half = frames // 2
    return call(
        functools.partial(backward_kernel, u),
        "attend_backward",
        (2,),
        meta,
        (q, k, v, *grads, *outs, lse),
        [
            pl.BlockSpec((half, 256), lambda i, m: (i ^ m[0], 0)),
            fixed(frames, 256),
            fixed(frames, 256),
            fixed(192, half),
            fixed(192, half),
            fixed(192, half),
            fixed(192, half),
            pl.BlockSpec((1, 8, half), lambda i, m: (i, 0, 0)),
        ],
        [
            pl.BlockSpec((half, 256), lambda i, m: (i ^ m[0], 0)),
            fixed(frames, 256),
            fixed(frames, 256),
        ],
        [like((frames, 256), BF)] * 3,
        [
            pltpu.VMEM((256, frames), BF),
            pltpu.VMEM((frames, 256), F32),
            pltpu.VMEM((frames, 256), F32),
            pltpu.VMEM((192, half), BF),
            pltpu.VMEM((192, half), BF),
        ],
        hold=(3,),
        far=(0, 1, 2),
        out=(0, 1, 2),
    )


def entry_kernel(meta_ref, x_ref, dq_ref, dk_ref, dv_ref, wq_ref, wk_ref, wv_ref, *refs):
    last = len(refs) == 7
    before_ref = refs[0] if last else None
    send_ref, keep_ref, sum_ref, acc = refs[-4:]
    step = pl.program_id(0)
    x = x_ref[...]
    total = jnp.zeros(x.shape, F32)
    for i, (g_ref, w_ref) in enumerate(((dq_ref, wq_ref), (dk_ref, wk_ref), (dv_ref, wv_ref))):
        rows = pl.ds(192 * i, 192)
        g = g_ref[:, :192]
        total = total + nn(g, w_ref[...])
        product = tn(g, x)

        @pl.when(step == 0)
        def _():
            acc[rows, :] = product if before_ref is None else product + before_ref[rows, :]

        @pl.when(step == 1)
        def _():
            sum_ref[rows, :] = (product + acc[rows, :]).astype(sum_ref.dtype)

    low = total.astype(BF)

    @pl.when(step == 0)
    def _():
        send_ref[...] = low
        if last:
            merged = refs[1][...].astype(F32) + refs[2][...].astype(F32)
            sum_ref[576:, :] = merged.astype(sum_ref.dtype)

    @pl.when(step == 1)
    def _():
        keep_ref[...] = low


def entry_back(meta, tokens, grads, weights, before, u, frames):
    half = frames // 2
    d = tokens.shape[1]
    rows, dtype = (832, BF) if before else (576, F32)
    return call(
        entry_kernel,
        "entry_back",
        (2,),
        meta,
        (tokens, *grads, *weights, *before),
        [pl.BlockSpec((half, d), lambda i, m: (u * 2 + (1 - i ^ m[0]), 0))]
        + [pl.BlockSpec((half, 256), lambda i, m: (1 - i ^ m[0], 0))] * 3
        + [fixed(192, d)] * 3
        + [fixed(*value.shape) for value in before],
        [fixed(half, d), fixed(half, d), fixed(rows, d)],
        [like((half, d), BF), like((half, d), BF), like((rows, d), dtype)],
        [pltpu.VMEM((576, d), F32)],
        hold=(1, 2, 3),
        far=(0, 4, 5, 6),
    )


def place_kernel(meta_ref, *refs):
    o_ref = refs[-1]
    for i, r_ref in enumerate(refs[:-1]):

        @pl.when(pl.program_id(0) == i)
        def _():
            o_ref[...] = r_ref[...]


def place(meta, own, other):
    half, d = own[0].shape
    count = 2 * len(own)
    return call(
        place_kernel,
        "place",
        (count,),
        meta,
        [block for pair in zip(own, other) for block in pair],
        [fixed(half, d)] * count,
        pl.BlockSpec((half, d), lambda i, m: (i ^ m[0], 0)),
        like((count * half, d), own[0].dtype),
    )


def normalise(values):
    average = jnp.mean(values, axis=-1, keepdims=True)
    centred = values - average
    spread = jnp.mean(centred * centred, axis=-1, keepdims=True)
    rstd = lax.rsqrt(spread + EPS)
    return centred * rstd, rstd


def gelu_pair(v):
    e = jnp.exp2(v * v * (-0.5 * LOG2E))
    t = 1.0 / (1.0 + (0.3275911 * 0.7071067811865476) * jnp.abs(v))
    poly = t * (0.5 * 0.254829592 + t * (0.5 * -0.284496736 + t * (0.5 * 1.421413741 + t * (0.5 * -1.453152027 + t * (0.5 * 1.061405429)))))
    tail = poly * e
    phi_cap = jnp.where(v >= 0, 1.0 - tail, tail)
    return v * phi_cap, phi_cap + v * (e * 0.3989422804014327)


def ahead_kernel(
    meta_ref, tok_ref, a0, a1, a2, a3, w0, w1, w2, w3, ua_ref, ub_ref, da_ref, db_ref, vec_ref,
    xhat_ref, rstd_ref, low_ref, act_ref, slope_ref, own_ref, sent_ref,
):
    gain, bias = vec_ref[0:1, :], vec_ref[1:2, :]
    hidden = ua_ref.shape[1]
    for r in range(tok_ref.shape[0] // RB):
        rows = pl.ds(r * RB, RB)
        branch = jnp.zeros((RB, tok_ref.shape[1]), F32)
        for a, w in ((a0, w0), (a1, w1), (a2, w2), (a3, w3)):
            branch = branch + tn(a[:, rows], w[...]).astype(BF).astype(F32)
        xhat, rstd = normalise(tok_ref[rows, :].astype(F32) + branch)
        xhat_ref[rows, :] = xhat
        rstd_ref[rows, :] = jnp.broadcast_to(rstd, (RB, rstd_ref.shape[1]))
        normed = xhat * gain + bias
        low = normed.astype(BF)
        low_ref[rows, :] = low
        sent = jnp.zeros(normed.shape, F32)
        for g, (up, down) in enumerate(((ua_ref, da_ref), (ub_ref, db_ref))):
            acts = []
            for c in range(hidden // HB):
                act, slope = gelu_pair(nn(low, up[:, c * HB : (c + 1) * HB]))
                columns = pl.ds(g * hidden + c * HB, HB)
                acts.append(act.astype(BF))
                act_ref[rows, columns] = acts[-1]
                slope_ref[rows, columns] = slope.astype(BF)
            sent = sent + nn(jnp.concatenate(acts, axis=1), down[...]).astype(BF).astype(F32)
        own_ref[rows, :] = normed + sent
        sent_ref[rows, :] = sent.astype(BF)


def ahead(meta, tokens, att, merge_w, up, down, vectors, u):
    half = att[0].shape[1]
    d, hidden = up[0].shape
    return call(
        ahead_kernel,
        "ahead",
        (1,),
        meta,
        (tokens, *att, *merge_w, *up, *down, vectors),
        [pl.BlockSpec((half, d), lambda i, m: (u * 2 + m[0], 0))]
        + [fixed(192, half)] * 4
        + [fixed(192, d)] * 4
        + [fixed(d, hidden)] * 2
        + [fixed(hidden, d)] * 2
        + [fixed(4, d)],
        [fixed(half, d), fixed(half, 128), fixed(half, d), fixed(half, 2 * hidden), fixed(half, 2 * hidden), fixed(half, d), fixed(half, d)],
        [
            like((half, d), F32),
            like((half, 128), F32),
            like((half, d), BF),
            like((half, 2 * hidden), BF),
            like((half, 2 * hidden), BF),
            like((half, d), F32),
            like((half, d), BF),
        ],
        far=(0,),
        out=(2, 3, 4, 5),
        out_far=(0, 1),
    )


def astern_kernel(u, meta_ref, own_ref, far_ref, grad_ref, span_ref, ua_ref, ub_ref, da_ref, db_ref, slope_ref, vec_ref, *refs):
    last = len(refs) > 6
    if last:
        before = refs[:-10]
        out_ref, back_ref, sent_ref, small_ref, *sums, g_ref, pre_ref = refs[-10:]
    else:
        out_ref, g_ref, pre_ref, back_ref, sent_ref, small_ref = refs
    gain, bias = vec_ref[2:3, :], vec_ref[3:4, :]
    half, d = own_ref.shape
    hidden = ua_ref.shape[1]
    starts = span_ref[u : u + 1, :]
    gain_grad = jnp.zeros(gain.shape, F32)
    bias_grad = jnp.zeros(gain.shape, F32)
    for r in range(half // RB):
        rows = pl.ds(r * RB, RB)
        xhat, rstd = normalise(own_ref[rows, :] + far_ref[rows, :].astype(F32))
        out_ref[rows, :] = (xhat * gain + bias).astype(BF)
        frame = meta_ref[0] * half + r * RB + lax.broadcasted_iota(jnp.int32, (RB, starts.shape[1]), 0)
        inside = (frame >= starts) & (frame < starts + SPAN)
        weight = jnp.max(jnp.where(inside, 1.0, 0.0), axis=1, keepdims=True)
        cot = grad_ref[rows, :].astype(F32) * weight
        gain_grad = gain_grad + jnp.sum(cot * xhat, axis=0, keepdims=True)
        bias_grad = bias_grad + jnp.sum(cot, axis=0, keepdims=True)
        gy = cot * gain
        mean_gy = jnp.mean(gy, axis=-1, keepdims=True)
        mean_gx = jnp.mean(gy * xhat, axis=-1, keepdims=True)
        sum_grad = rstd * (gy - mean_gy - xhat * mean_gx)
        low = sum_grad.astype(BF)
        g_ref[rows, :] = low
        sent = jnp.zeros(sum_grad.shape, F32)
        for g, (up, down) in enumerate(((ua_ref, da_ref), (ub_ref, db_ref))):
            pres = []
            for c in range(hidden // HB):
                columns = pl.ds(g * hidden + c * HB, HB)
                slope = slope_ref[rows, columns].astype(F32)
                pres.append((nt(low, down[c * HB : (c + 1) * HB, :]) * slope).astype(BF))
                pre_ref[rows, columns] = pres[-1]
            sent = sent + nt(jnp.concatenate(pres, axis=1), up[...]).astype(BF).astype(F32)
        back_ref[rows, :] = sum_grad + sent
        sent_ref[rows, :] = sent.astype(BF)
    small_ref[0:1, :] = gain_grad
    small_ref[1:2, :] = bias_grad
    if last:
        x_ref, act_ref = before[:2]
        weight_sums(x_ref[...], g_ref[...], act_ref, pre_ref, before[2:], sums)


def astern(meta, own, far, grad, spans, up, down, slope, vectors, u, before):
    half, d = own.shape
    hidden = up[0].shape[1]
    rows = fixed(half, d)
    wide = fixed(half, 2 * hidden)
    grads = [] if not before else [(d, hidden)] * 2 + [(hidden, d)] * 2
    extra = [] if not before else [rows, wide] + [fixed(*shape) for shape in grads[: len(before) - 2]]
    made = [like((half, d), BF), like((half, 2 * hidden), BF)]
    others = [like((half, d), F32), like((half, d), BF), like((2, d), F32)]
    shapes = [like((half, d), BF)] + ([] if before else made) + others + [like(shape, BF) for shape in grads]
    return call(
        functools.partial(astern_kernel, u),
        "astern",
        (1,),
        meta,
        (own, far, grad, spans, *up, *down, slope, vectors, *before),
        [rows] * 2
        + [pl.BlockSpec((half, d), lambda i, m: (u * 2 + m[0], 0)), fixed(*spans.shape)]
        + [fixed(d, hidden)] * 2
        + [fixed(hidden, d)] * 2
        + [wide, fixed(4, d)]
        + extra,
        [fixed(*shape.shape) for shape in shapes],
        shapes,
        [pltpu.VMEM(shape.shape, shape.dtype) for shape in made] if before else (),
        limit=20 if before else VMEM,
        hold=(0, 8, *range(10, 10 + len(before))),
        far=(2,),
        out=() if before else (1, 2),
        out_far=(0, 1) if before else (0, 3),
    )


def weight_kernel(meta_ref, x_ref, g_ref, act_ref, pre_ref, *refs):
    before, sums = refs[:-4], refs[-4:]
    weight_sums(x_ref[...], g_ref[...], act_ref, pre_ref, before, sums)


def weight_sums(x, g, act_ref, pre_ref, before, sums):
    hidden = act_ref.shape[1] // 2
    for i in range(2):
        for c in range(hidden // HB):
            columns = pl.ds(i * hidden + c * HB, HB)
            block = pl.ds(c * HB, HB)
            up = tn(x, pre_ref[:, columns])
            down = tn(act_ref[:, columns], g)
            if before:
                up = up + before[i][:, block].astype(F32)
                down = down + before[2 + i][block, :].astype(F32)
            sums[i][:, block] = up.astype(BF)
            sums[2 + i][block, :] = down.astype(BF)


def weight_grads(meta, x, g, act, pre, before):
    rows, d = x.shape
    hidden = act.shape[1] // 2
    shapes = [(d, hidden)] * 2 + [(hidden, d)] * 2
    return call(
        weight_kernel,
        "weight_grads",
        (1,),
        meta,
        (x, g, act, pre, *before),
        [fixed(rows, d)] * 2 + [fixed(rows, 2 * hidden)] * 2 + [fixed(*shape) for shape in shapes[: len(before)]],
        [fixed(*shape) for shape in shapes],
        [like(shape, BF) for shape in shapes],
        hold=(0, 1, 2, 3),
        out=(0, 1, 2, 3),
    )


def inner_kernel(meta_ref, own_ref, far_ref, xhat_ref, rstd_ref, vec_ref, a0, a1, w0, w1, *refs):
    last = len(refs) == 11
    out_ref, g0, g1, m0, m1, small_ref = refs[-6:]
    grad = own_ref[...] + far_ref[...].astype(F32)
    xhat = xhat_ref[...]
    gain_grad = jnp.sum(grad * xhat, axis=0, keepdims=True)
    bias_grad = jnp.sum(grad, axis=0, keepdims=True)
    gy = grad * vec_ref[0:1, :]
    mean_gy = jnp.mean(gy, axis=-1, keepdims=True)
    mean_gx = jnp.mean(gy * xhat, axis=-1, keepdims=True)
    inner = rstd_ref[:, 0:1] * (gy - mean_gy - xhat * mean_gx)
    out_ref[...] = inner
    low = inner.astype(BF)
    g0[...] = nt(w0[...], low).astype(BF)
    g1[...] = nt(w1[...], low).astype(BF)
    small = jnp.concatenate([gain_grad, bias_grad], axis=0)
    small_ref[...] = small
    if last:
        before0, before1, before_small, outer0, outer1 = refs[:5]
        below = jnp.concatenate(
            [small + before_small[...], outer0[...] + outer1[...], jnp.zeros((60, small.shape[1]), F32)], axis=0
        ).astype(BF)
        for m, a, before in ((m0, a0, before0), (m1, a1, before1)):
            m[:192, :] = (nn(a[...], low) + before[...]).astype(BF)
            m[192:, :] = below
    else:
        m0[...] = nn(a0[...], low)
        m1[...] = nn(a1[...], low)


def inner_norm(meta, own, far, xhat, rstd, vectors, att, weights, before):
    rows, d = xhat.shape
    merge = like((256, d), BF) if before else like((192, d), F32)
    return call(
        inner_kernel,
        "inner_norm",
        (1,),
        meta,
        (own, far, xhat, rstd, vectors, *att, *weights, *before),
        [fixed(rows, d)] * 3
        + [fixed(rows, 128), fixed(4, d)]
        + [fixed(192, rows)] * 2
        + [fixed(192, d)] * 2
        + ([fixed(192, d)] * 2 + [fixed(2, d)] * 3 if before else []),
        [fixed(rows, d), fixed(192, rows), fixed(192, rows), fixed(*merge.shape), fixed(*merge.shape), fixed(2, d)],
        [like((rows, d), F32), like((192, rows), BF), like((192, rows), BF), merge, merge, like((2, d), F32)],
        far=(0, 2, 3, 5, 6, 7, 8, *((9, 10) if before else ())),
        out=(1,),
        out_far=(0,) if before else (0, 3, 4),
    )


def fold_kernel(bits, meta_ref, *refs):
    for i in range(2):
        here, there = refs[2 * i : 2 * i + 2]
        if bits:
            send, keep = refs[4 + 2 * i : 6 + 2 * i]
            half = send.shape[0]
            bit = meta_ref[bits[i]]
            for part, j in ((send, 1 - bit), (keep, bit)):
                rows = pl.ds(pl.multiple_of(j * half, 16), half)
                part[...] = (here[rows, :].astype(F32) + there[rows, :].astype(F32)).astype(BF)
        else:
            refs[4 + i][...] = (here[...].astype(F32) + there[...].astype(F32)).astype(BF)


def fold(meta, pairs, bits, hold=()):
    args = [value for pair in pairs for value in pair]
    rows, d = args[0].shape
    shapes = [like((rows // 2, d), BF)] * 4 if bits else [like((rows, d), BF)] * 2
    return call(
        functools.partial(fold_kernel, bits),
        "fold",
        (1,),
        meta,
        args,
        [fixed(rows, d)] * 4,
        [fixed(*shape.shape) for shape in shapes],
        shapes,
        hold=hold,
    )


def local(groups, tokens, lengths, span_starts, wq, wk, wv, wm, wu, wd, ig, ib, og, ob, out_grad):
    rows, d = tokens.shape
    seqs = lengths.shape[0]
    frames = rows // seqs
    half = frames // 2
    core = lax.axis_index("tensor") % 2
    place_dp = lax.axis_index("dp")
    bits = groups.bit_length() - 1

    def swap(value, k):
        return lax.ppermute(value, "tensor", [(i, i ^ k) for i in range(4)])

    def swap_dp(value, k):
        return lax.ppermute(value, "dp", [(i, i ^ k) for i in range(groups)])

    def add(a, b):
        return (a.astype(F32) + b.astype(F32)).astype(BF)

    def total(pieces):
        return sum(piece.astype(F32) for piece in pieces).astype(BF) if len(pieces) > 1 else pieces[0]

    stages = [(0, 1)] + [(b, 2) for b in range(1, bits - 1, 2)] + ([(bits - 1, 1)] if bits % 2 == 0 else [])
    bit_orders = (list(range(bits)), [1, 0, *range(2, bits)])

    def spot_of(stage):
        return (place_dp >> stage[0]) & ((1 << stage[1]) - 1)

    class Chain:
        def __init__(self, part, order, cut_already=False):
            self.part = part.reshape((1,) * len(order) + part.shape) if cut_already else part
            self.order = order
            self.steps = [] if cut_already else [(True, stage) for stage in order]
            self.steps += [(False, stage) for stage in reversed(order)]

        def cut(self, stage, j):
            size = self.part.shape[0] >> stage[1]
            return lax.dynamic_slice_in_dim(self.part, (spot_of(stage) ^ j) * size, size, 0)

        def start(self):
            if self.steps:
                scatter, stage = self.steps[0]
                others = range(1, 1 << stage[1])
                self.pending = [swap_dp(self.cut(stage, j) if scatter else self.part, j << stage[0]) for j in others]

        def finish(self, *after):
            if not self.steps:
                return
            scatter, stage = self.steps.pop(0)
            got = self.pending
            if after:
                got = list(lax.optimization_barrier((*got, *after))[: len(got)])
            if scatter:
                state = total([self.cut(stage, 0)] + got)
                if not self.steps[0][0]:
                    state = state.reshape((1,) * len(self.order) + state.shape)
            else:
                axis = self.order.index(stage)
                spot = spot_of(stage)
                mine = self.part
                if len(got) == 1:
                    laid = [jnp.where(spot, got[0], mine), jnp.where(spot, mine, got[0])]
                    state = jnp.concatenate(laid, axis=axis)
                else:
                    state = jnp.zeros(mine.shape[:axis] + (1 + len(got),) + mine.shape[axis + 1 :], BF)
                    for j, piece in enumerate([mine] + got):
                        state = lax.dynamic_update_slice_in_dim(state, piece, spot ^ j, axis)
                if not self.steps:
                    state = state.reshape(-1, d)
            self.part = state

    def finish(group, *after):
        for chain in group:
            chain.finish(*after)

    def start(group):
        for chain in group:
            chain.start()

    def together(group):
        for chain, value in zip(group, lax.optimization_barrier(tuple(chain.part for chain in group))):
            chain.part = value

    all_bits = [((place_dp >> b) & 1).reshape(1) for b in range(bits)]
    scalars = jnp.concatenate([core.reshape(1), lengths, *all_bits])
    token = []

    def meta():
        return lax.optimization_barrier((scalars, *token))[0] if token else scalars

    def done(results, *others):
        token[:] = [results[0], *others]
        return results

    merge_w = (wm, swap(wm, 1), swap(wm, 2), swap(wm, 3))
    up_w = (wu, swap(wu, 1))
    down_w = (wd, swap(wd, 1))
    vectors = jnp.stack([ig, ib, og, ob])
    qkv_w = (wq.T, wk.T, wv.T)

    fwd, att, front, far = [], [], [], []
    qkv_of = [done(project(scalars, tokens, qkv_w, 0, frames))]
    for u in range(seqs):
        fwd.append(done(attend_forward(meta(), *qkv_of[u], u, frames), *(merge_w[1:] if u == 0 else ())))
        own, other = fwd[u][:2]
        att.append((own, swap(other, 1), swap(own, 2), swap(other, 3)))
        if u + 1 < seqs:
            qkv_of.append(done(project(meta(), tokens, qkv_w, u + 1, frames), up_w[1], down_w[1]))
    for u in range(seqs):
        front.append(done(ahead(meta(), tokens, att[u], merge_w, up_w, down_w, vectors, u)))
        far.append(swap(front[u][6], 2))
    out_rows, back, far_grad, smalls, sums = [], [], [], [], ()
    for u in range(seqs):
        last = u == seqs - 1
        before = (front[u][2], front[u][3], *sums) if last else ()
        res = done(astern(meta(), front[u][5], far[u], out_grad, span_starts, up_w, down_w, front[u][4], vectors, u, before))
        out_rows.append(res[0])
        back.append(res[1 if last else 3])
        smalls.append(res[3 if last else 5])
        if last:
            sent, sums = res[2], res[4:]
        else:
            far_grad.append(swap(res[4], 2))
            sums = done(weight_grads(meta(), front[u][2], res[1], front[u][3], res[2], sums))

    def inner_step(u, before):
        res = done(inner_norm(meta(), back[u], far_grad[u], front[u][0], front[u][1], vectors, att[u][:2], merge_w[:2], before))
        return res, (res[1], swap(res[2], 1))

    def attend_step(u, grads):
        return done(attend_backward(meta(), *qkv_of[u], grads, fwd[u][:2], fwd[u][2], u, frames))

    def entry_step(u, grads, before):
        return done(entry_back(meta(), tokens, grads, qkv_w, before, u, frames))


    first_bit = 1 + seqs

    def scatter(step, pairs, after, hold=()):
        pairs = [tuple(lax.optimization_barrier((*pair, after))[:2]) for pair in pairs]
        if step == bits:
            return done(fold(meta(), pairs, (), hold))
        out = done(fold(meta(), pairs, tuple(first_bit + order[step] for order in bit_orders), hold))
        return [(out[2 * i + 1], swap_dp(out[2 * i], 1 << bit_orders[i][step])) for i in range(2)]

    inner, entry, so_far, near, crossed = [], [], (), [], []
    out_other = [swap(r, 1) for r in out_rows]

    def exchange(out):
        got = swap(out[0], 1)
        near.append((out[1], got))
        crossed.append(swap(total(near[-1]), 2))
        return got

    for u in range(seqs):
        last = u == seqs - 1
        if u == 0:
            up_own, up_other, down_own, down_other = lax.optimization_barrier((*sums, far_grad[0]))[:4]
            moving = [(down_own, swap(down_other, 1)), (up_own, swap(up_other, 1))]
            res, grads = inner_step(0, ())
            inner.append(res)
            far_grad.append(swap(lax.optimization_barrier((sent, res[0]))[0], 2))
            moving = scatter(0, moving, res[0])
        dqkv = attend_step(u, grads)
        moving = scatter(1 + 2 * u, moving, dqkv[0])
        if not last:
            before = ()
            if u + 1 == seqs - 1:
                before = (inner[0][3], inner[0][4], inner[0][5], *smalls)
            res, grads = inner_step(u + 1, before)
            inner.append(res)
        else:
            for step in range(4, bits + 1):
                moving = scatter(step, moving, moving[0][0])
            first, second = (
                Chain(moving[i], [(b, 1) for b in order], True) for i, order in enumerate(bit_orders)
            )
            start([first, second])
            token.extend(out_other)
        out = entry_step(u, dqkv, so_far)
        entry.append(out)
        if not last:
            merge_got = swap(lax.optimization_barrier((res[4], out[0]))[0], 1)
            so_far = (out[2], res[3], merge_got)
            moving = scatter(2, moving, out[0])
            exchange(out)
    qkv = Chain(out[2], stages)
    qkv.start()

    got = exchange(out)
    layer_output = place(meta(), out_rows, out_other)

    finish([first, second], got)
    finish([qkv], crossed[0])
    together([qkv, first, second])
    start([qkv, first, second])
    finish([qkv, first, second], crossed[-1])
    together([qkv, first, second])
    start([qkv, first])
    ready = []
    for u in range(seqs):
        rest = near[u][0].astype(F32) + near[u][1].astype(F32) + crossed[u].astype(F32)
        ready.append((inner[u][0] + rest).astype(BF))
    input_grad = place(scalars, ready, [swap(r, 1) for r in ready])
    finish([qkv, first], layer_output)
    together([qkv, first, second])
    start([qkv, second])
    finish([qkv, second], input_grad)
    while qkv.steps or first.steps or second.steps:
        start([qkv, first, second])
        finish([qkv, first, second])
        together([qkv, first, second])
    down_sum, up_sum, joint = (chain.part for chain in (first, second, qkv))
    qkv_sum, merge_sum = joint[:576], joint[576:]
    small = merge_sum[192:196].astype(F32)
    query_grad, key_grad, value_grad = (qkv_sum[192 * i : 192 * (i + 1)].astype(F32).T for i in range(3))
    return (
        layer_output,
        input_grad,
        query_grad,
        key_grad,
        value_grad,
        merge_sum[:192].astype(F32),
        up_sum.astype(F32),
        down_sum.astype(F32),
        small[0],
        small[1],
        small[2],
        small[3],
    )


def solution(mesh):
    in_specs = (
        P("dp", None),
        P("dp"),
        P("dp", None),
        P(None, "tensor"),
        P(None, "tensor"),
        P(None, "tensor"),
        P("tensor", None),
        P(None, "tensor"),
        P("tensor", None),
        P(),
        P(),
        P(),
        P(),
        P("dp", None),
    )
    out_specs = (
        P("dp", None),
        P("dp", None),
        P(None, "tensor"),
        P(None, "tensor"),
        P(None, "tensor"),
        P("tensor", None),
        P(None, "tensor"),
        P("tensor", None),
        P(),
        P(),
        P(),
        P(),
    )
    body = functools.partial(local, mesh.shape["dp"])
    return jax.shard_map(body, mesh=mesh, in_specs=in_specs, out_specs=out_specs, check_vma=False)
```

```python
import functools

import jax
import jax.numpy as jnp
from jax import lax
from jax.experimental import pallas as pl
from jax.experimental.pallas import tpu as pltpu
from jax.sharding import PartitionSpec as P

HEAD_DIM = 64
SPAN = 10
EPS = 1e-05
LOG2E = 1.4426950408889634
KF = 1024
KB = 512
VMEM = 12
RB = 128
HB = 256
BF = jnp.bfloat16
F32 = jnp.float32
MIB = 1 << 20


def nn(a, b):
    return lax.dot_general(a, b, (((1,), (0,)), ((), ())), preferred_element_type=F32)


def nt(a, b):
    return lax.dot_general(a, b, (((1,), (1,)), ((), ())), preferred_element_type=F32)


def tn(a, b):
    return lax.dot_general(a, b, (((0,), (0,)), ((), ())), preferred_element_type=F32)


def params(limit):
    return pltpu.CompilerParams(vmem_limit_bytes=limit * MIB)


def cost(micros):
    return pl.CostEstimate(flops=int(micros * 1.1e9), bytes_accessed=1024, transcendentals=0)


MICROS = {"project": 3, "attend_forward": 8, "attend_backward": 12, "entry_back": 5, "place": 3, "ahead": 9, "astern": 10, "inner_norm": 3, "weight_grads": 4, "fold": 2}


def lane_parts(block):
    left = block[:, :128]
    lane = lax.broadcasted_iota(jnp.int32, left.shape, 1)
    zero = jnp.zeros_like(left)
    return (
        jnp.where(lane < HEAD_DIM, left, zero),
        jnp.where(lane >= HEAD_DIM, left, zero),
        block[:, 128:],
    )


TILE = (0, 0, 1)


def call(kernel, name, grid, meta, args, in_specs, out_specs, out_shape, scratch=(), limit=VMEM, hold=(), far=(), out=(), out_far=()):
    def place_input(i, value):
        space = pltpu.VMEM if i in hold else pltpu.HBM if i in far else None
        return value if space is None else pltpu.with_memory_space_constraint(value, space)

    def place_output(i, value):
        space = pltpu.VMEM if i in out else pltpu.HBM if i in out_far else None
        return value if space is None else space(value.shape, value.dtype)

    single = not isinstance(out_shape, list)
    return pl.pallas_call(
        kernel,
        grid_spec=pltpu.PrefetchScalarGridSpec(
            num_scalar_prefetch=1,
            grid=grid,
            in_specs=in_specs,
            out_specs=out_specs,
            scratch_shapes=scratch,
        ),
        out_shape=place_output(0, out_shape) if single else [place_output(i, o) for i, o in enumerate(out_shape)],
        compiler_params=params(limit),
        cost_estimate=cost(MICROS[name]),
        name=name,
    )(meta, *(place_input(i, value) for i, value in enumerate(args)))


def fixed(*shape):
    return pl.BlockSpec(shape, lambda *_: (0,) * len(shape))


def like(shape, dtype):
    return jax.ShapeDtypeStruct(shape, dtype)


def project_kernel(meta_ref, x_ref, wq_ref, wk_ref, wv_ref, q_ref, k_ref, v_ref):
    x = x_ref[...]
    for w_ref, o_ref in ((wq_ref, q_ref), (wk_ref, k_ref), (wv_ref, v_ref)):
        o_ref[:, :192] = nt(x, w_ref[...]).astype(BF)
        o_ref[:, 192:] = jnp.zeros((x.shape[0], HEAD_DIM), BF)


def project(meta, tokens, weights, u, frames):
    rows, d = frames, tokens.shape[1]
    block = 256
    return call(
        project_kernel,
        "project",
        (rows // block,),
        meta,
        (tokens, *weights),
        [pl.BlockSpec((block, d), lambda i, m: (u * (rows // block) + i, 0))] + [fixed(192, d)] * 3,
        [pl.BlockSpec((block, 256), lambda i, m: (i, 0))] * 3,
        [like((rows, 256), BF)] * 3,
        far=range(4),
        out=(0, 1, 2),
    )


def forward_kernel(u, meta_ref, q_ref, k_ref, v_ref, own_ref, other_ref, lse_ref, s_ref):
    length = meta_ref[1 + u]
    step = pl.program_id(0)
    blocks = lax.div(length + KF - 1, KF)
    parts = lane_parts(q_ref[...] * jnp.asarray(0.125, BF))
    width = q_ref.shape[0]

    def first(kb, highest):
        start = pl.multiple_of(kb * KF, KF)
        rows = pl.ds(start, KF)
        live = start + lax.broadcasted_iota(jnp.int32, (KF, width), 0) < length
        out = []
        for h in range(3):
            tile = pl.ds(128 * TILE[h], 128)
            s = nt(k_ref[rows, tile], parts[h])
            s = jnp.where(live, s, -1e30)
            s_ref[h, rows, :] = s
            out.append(jnp.maximum(highest[h], jnp.max(s, axis=0, keepdims=True)))
        return tuple(out)

    floor = jnp.full((1, width), -1e30, F32)
    highest = lax.fori_loop(0, blocks, first, (floor,) * 3)

    def second(kb, carry):
        rows = pl.ds(pl.multiple_of(kb * KF, KF), KF)
        out = []
        for h in range(3):
            total, result = carry[h]
            p = jnp.exp2((s_ref[h, rows, :] - highest[h]) * LOG2E)
            total = total + jnp.sum(p, axis=0, keepdims=True)
            v = v_ref[rows, pl.ds(128 * TILE[h], 128)]
            result = result + tn(v, p.astype(BF))
            out.append((total, result))
        return tuple(out)

    init = ((jnp.zeros((1, width), F32), jnp.zeros((128, width), F32)),) * 3
    done = lax.fori_loop(0, blocks, second, init)
    outs = []
    for h in range(3):
        total, result = done[h]
        lo = HEAD_DIM * (h % 2)
        o = result[lo : lo + HEAD_DIM] / total
        lse_ref[0, pl.ds(h, 1), :] = highest[h] * LOG2E + jnp.log2(total)
        outs.append(o.astype(BF))
    whole = jnp.concatenate(outs, axis=0)
    for j, o_ref in enumerate((own_ref, other_ref)):

        @pl.when(step == j)
        def _():
            o_ref[...] = whole


def attend_forward(meta, q, k, v, u, frames):
    half = frames // 2
    return call(
        functools.partial(forward_kernel, u),
        "attend_forward",
        (2,),
        meta,
        (q, k, v),
        [
            pl.BlockSpec((half, 256), lambda i, m: (i ^ m[0], 0)),
            fixed(frames, 256),
            fixed(frames, 256),
        ],
        [
            fixed(192, half),
            fixed(192, half),
            pl.BlockSpec((1, 8, half), lambda i, m: (i, 0, 0)),
        ],
        [
            like((192, half), BF),
            like((192, half), BF),
            like((2, 8, half), F32),
        ],
        [pltpu.VMEM((3, frames, half), F32)],
        hold=(0, 1, 2),
    )


def backward_kernel(
    u, meta_ref, q_ref, k_ref, v_ref, d0_ref, d1_ref, o0_ref, o1_ref, lse_ref,
    dq_ref, dk_ref, dv_ref, kt_ref, dk_acc, dv_acc, do_ref, o_ref,
):
    length = meta_ref[1 + u]
    blocks = lax.div(length + KB - 1, KB)
    step = pl.program_id(0)

    @pl.when(step == 0)
    def _():
        dk_acc[...] = jnp.zeros_like(dk_acc)
        dv_acc[...] = jnp.zeros_like(dv_acc)
        kt_ref[...] = jnp.transpose(k_ref[...])
        do_ref[...] = d0_ref[...]
        o_ref[...] = o0_ref[...]

    @pl.when(step == 1)
    def _():
        do_ref[...] = d1_ref[...]
        o_ref[...] = o1_ref[...]

    parts = lane_parts(q_ref[...] * jnp.asarray(0.125, BF))
    width = q_ref.shape[0]
    empty = jnp.zeros((HEAD_DIM, width), BF)
    head = [do_ref[pl.ds(h * HEAD_DIM, HEAD_DIM), :] for h in range(3)]
    grads = (
        jnp.concatenate([head[0], empty], axis=0),
        jnp.concatenate([empty, head[1]], axis=0),
        jnp.concatenate([head[2], empty], axis=0),
    )
    delta = [
        jnp.sum(
            head[h].astype(F32) * o_ref[pl.ds(h * HEAD_DIM, HEAD_DIM), :].astype(F32), axis=0, keepdims=True
        )
        for h in range(3)
    ]
    lse = [lse_ref[0, pl.ds(h, 1), :] for h in range(3)]

    def body(kb, carry):
        start = pl.multiple_of(kb * KB, KB)
        rows = pl.ds(start, KB)
        live = start + lax.broadcasted_iota(jnp.int32, (KB, width), 0) < length
        out = []
        for h in range(3):
            tile = pl.ds(128 * TILE[h], 128)
            s = nt(k_ref[rows, tile], parts[h])
            s = jnp.where(live, s, -1e30)
            p = jnp.exp2(s * LOG2E - lse[h])
            dp = nn(v_ref[rows, tile], grads[h])
            ds = (p * (dp - delta[h])).astype(BF)
            dv_acc[rows, tile] += nt(p.astype(BF), grads[h])
            dk_acc[rows, tile] += nn(ds, parts[h])
            kt = kt_ref[pl.ds(h * HEAD_DIM, HEAD_DIM), rows]
            out.append(carry[h] + nn(kt, ds))
        return tuple(out)

    zero = jnp.zeros((HEAD_DIM, width), F32)
    done = lax.fori_loop(0, blocks, body, (zero,) * 3)
    full = jnp.concatenate(done + (zero,), axis=0) * 0.125
    dq_ref[...] = jnp.transpose(full).astype(BF)

    @pl.when(step == 1)
    def _():
        dk_ref[...] = dk_acc[...].astype(BF)
        dv_ref[...] = dv_acc[...].astype(BF)


def attend_backward(meta, q, k, v, grads, outs, lse, u, frames):
    half = frames // 2
    return call(
        functools.partial(backward_kernel, u),
        "attend_backward",
        (2,),
        meta,
        (q, k, v, *grads, *outs, lse),
        [
            pl.BlockSpec((half, 256), lambda i, m: (i ^ m[0], 0)),
            fixed(frames, 256),
            fixed(frames, 256),
            fixed(192, half),
            fixed(192, half),
            fixed(192, half),
            fixed(192, half),
            pl.BlockSpec((1, 8, half), lambda i, m: (i, 0, 0)),
        ],
        [
            pl.BlockSpec((half, 256), lambda i, m: (i ^ m[0], 0)),
            fixed(frames, 256),
            fixed(frames, 256),
        ],
        [like((frames, 256), BF)] * 3,
        [
            pltpu.VMEM((256, frames), BF),
            pltpu.VMEM((frames, 256), F32),
            pltpu.VMEM((frames, 256), F32),
            pltpu.VMEM((192, half), BF),
            pltpu.VMEM((192, half), BF),
        ],
        hold=(3,),
        far=(0, 1, 2),
        out=(0, 1, 2),
    )


def entry_kernel(meta_ref, x_ref, dq_ref, dk_ref, dv_ref, wq_ref, wk_ref, wv_ref, *refs):
    last = len(refs) == 7
    before_ref = refs[0] if last else None
    send_ref, keep_ref, sum_ref, acc = refs[-4:]
    step = pl.program_id(0)
    x = x_ref[...]
    total = jnp.zeros(x.shape, F32)
    for i, (g_ref, w_ref) in enumerate(((dq_ref, wq_ref), (dk_ref, wk_ref), (dv_ref, wv_ref))):
        rows = pl.ds(192 * i, 192)
        g = g_ref[:, :192]
        total = total + nn(g, w_ref[...])
        product = tn(g, x)

        @pl.when(step == 0)
        def _():
            acc[rows, :] = product if before_ref is None else product + before_ref[rows, :]

        @pl.when(step == 1)
        def _():
            sum_ref[rows, :] = (product + acc[rows, :]).astype(sum_ref.dtype)

    low = total.astype(BF)

    @pl.when(step == 0)
    def _():
        send_ref[...] = low
        if last:
            merged = refs[1][...].astype(F32) + refs[2][...].astype(F32)
            sum_ref[576:, :] = merged.astype(sum_ref.dtype)

    @pl.when(step == 1)
    def _():
        keep_ref[...] = low


def entry_back(meta, tokens, grads, weights, before, u, frames):
    half = frames // 2
    d = tokens.shape[1]
    rows, dtype = (832, BF) if before else (576, F32)
    return call(
        entry_kernel,
        "entry_back",
        (2,),
        meta,
        (tokens, *grads, *weights, *before),
        [pl.BlockSpec((half, d), lambda i, m: (u * 2 + (1 - i ^ m[0]), 0))]
        + [pl.BlockSpec((half, 256), lambda i, m: (1 - i ^ m[0], 0))] * 3
        + [fixed(192, d)] * 3
        + [fixed(*value.shape) for value in before],
        [fixed(half, d), fixed(half, d), fixed(rows, d)],
        [like((half, d), BF), like((half, d), BF), like((rows, d), dtype)],
        [pltpu.VMEM((576, d), F32)],
        hold=(1, 2, 3),
        far=(0, 4, 5, 6),
    )


def place_kernel(meta_ref, *refs):
    o_ref = refs[-1]
    for i, r_ref in enumerate(refs[:-1]):

        @pl.when(pl.program_id(0) == i)
        def _():
            o_ref[...] = r_ref[...]


def place(meta, own, other):
    half, d = own[0].shape
    count = 2 * len(own)
    return call(
        place_kernel,
        "place",
        (count,),
        meta,
        [block for pair in zip(own, other) for block in pair],
        [fixed(half, d)] * count,
        pl.BlockSpec((half, d), lambda i, m: (i ^ m[0], 0)),
        like((count * half, d), own[0].dtype),
    )


def normalise(values):
    average = jnp.mean(values, axis=-1, keepdims=True)
    centred = values - average
    spread = jnp.mean(centred * centred, axis=-1, keepdims=True)
    rstd = lax.rsqrt(spread + EPS)
    return centred * rstd, rstd


def gelu_pair(v):
    e = jnp.exp2(v * v * (-0.5 * LOG2E))
    t = 1.0 / (1.0 + (0.3275911 * 0.7071067811865476) * jnp.abs(v))
    poly = t * (0.5 * 0.254829592 + t * (0.5 * -0.284496736 + t * (0.5 * 1.421413741 + t * (0.5 * -1.453152027 + t * (0.5 * 1.061405429)))))
    tail = poly * e
    phi_cap = jnp.where(v >= 0, 1.0 - tail, tail)
    return v * phi_cap, phi_cap + v * (e * 0.3989422804014327)


def ahead_kernel(
    meta_ref, tok_ref, a0, a1, a2, a3, w0, w1, w2, w3, ua_ref, ub_ref, da_ref, db_ref, vec_ref,
    xhat_ref, rstd_ref, low_ref, act_ref, slope_ref, own_ref, sent_ref,
):
    gain, bias = vec_ref[0:1, :], vec_ref[1:2, :]
    hidden = ua_ref.shape[1]
    for r in range(tok_ref.shape[0] // RB):
        rows = pl.ds(r * RB, RB)
        branch = jnp.zeros((RB, tok_ref.shape[1]), F32)
        for a, w in ((a0, w0), (a1, w1), (a2, w2), (a3, w3)):
            branch = branch + tn(a[:, rows], w[...]).astype(BF).astype(F32)
        xhat, rstd = normalise(tok_ref[rows, :].astype(F32) + branch)
        xhat_ref[rows, :] = xhat
        rstd_ref[rows, :] = jnp.broadcast_to(rstd, (RB, rstd_ref.shape[1]))
        normed = xhat * gain + bias
        low = normed.astype(BF)
        low_ref[rows, :] = low
        sent = jnp.zeros(normed.shape, F32)
        for g, (up, down) in enumerate(((ua_ref, da_ref), (ub_ref, db_ref))):
            acts = []
            for c in range(hidden // HB):
                act, slope = gelu_pair(nn(low, up[:, c * HB : (c + 1) * HB]))
                columns = pl.ds(g * hidden + c * HB, HB)
                acts.append(act.astype(BF))
                act_ref[rows, columns] = acts[-1]
                slope_ref[rows, columns] = slope.astype(BF)
            sent = sent + nn(jnp.concatenate(acts, axis=1), down[...]).astype(BF).astype(F32)
        own_ref[rows, :] = normed + sent
        sent_ref[rows, :] = sent.astype(BF)


def ahead(meta, tokens, att, merge_w, up, down, vectors, u):
    half = att[0].shape[1]
    d, hidden = up[0].shape
    return call(
        ahead_kernel,
        "ahead",
        (1,),
        meta,
        (tokens, *att, *merge_w, *up, *down, vectors),
        [pl.BlockSpec((half, d), lambda i, m: (u * 2 + m[0], 0))]
        + [fixed(192, half)] * 4
        + [fixed(192, d)] * 4
        + [fixed(d, hidden)] * 2
        + [fixed(hidden, d)] * 2
        + [fixed(4, d)],
        [fixed(half, d), fixed(half, 128), fixed(half, d), fixed(half, 2 * hidden), fixed(half, 2 * hidden), fixed(half, d), fixed(half, d)],
        [
            like((half, d), F32),
            like((half, 128), F32),
            like((half, d), BF),
            like((half, 2 * hidden), BF),
            like((half, 2 * hidden), BF),
            like((half, d), F32),
            like((half, d), BF),
        ],
        far=(0,),
        out=(2, 3, 4, 5),
        out_far=(0, 1),
    )


def astern_kernel(u, meta_ref, own_ref, far_ref, grad_ref, span_ref, ua_ref, ub_ref, da_ref, db_ref, slope_ref, vec_ref, *refs):
    last = len(refs) > 6
    if last:
        before = refs[:-10]
        out_ref, back_ref, sent_ref, small_ref, *sums, g_ref, pre_ref = refs[-10:]
    else:
        out_ref, g_ref, pre_ref, back_ref, sent_ref, small_ref = refs
    gain, bias = vec_ref[2:3, :], vec_ref[3:4, :]
    half, d = own_ref.shape
    hidden = ua_ref.shape[1]
    starts = span_ref[u : u + 1, :]
    gain_grad = jnp.zeros(gain.shape, F32)
    bias_grad = jnp.zeros(gain.shape, F32)
    for r in range(half // RB):
        rows = pl.ds(r * RB, RB)
        xhat, rstd = normalise(own_ref[rows, :] + far_ref[rows, :].astype(F32))
        out_ref[rows, :] = (xhat * gain + bias).astype(BF)
        frame = meta_ref[0] * half + r * RB + lax.broadcasted_iota(jnp.int32, (RB, starts.shape[1]), 0)
        inside = (frame >= starts) & (frame < starts + SPAN)
        weight = jnp.max(jnp.where(inside, 1.0, 0.0), axis=1, keepdims=True)
        cot = grad_ref[rows, :].astype(F32) * weight
        gain_grad = gain_grad + jnp.sum(cot * xhat, axis=0, keepdims=True)
        bias_grad = bias_grad + jnp.sum(cot, axis=0, keepdims=True)
        gy = cot * gain
        mean_gy = jnp.mean(gy, axis=-1, keepdims=True)
        mean_gx = jnp.mean(gy * xhat, axis=-1, keepdims=True)
        sum_grad = rstd * (gy - mean_gy - xhat * mean_gx)
        low = sum_grad.astype(BF)
        g_ref[rows, :] = low
        sent = jnp.zeros(sum_grad.shape, F32)
        for g, (up, down) in enumerate(((ua_ref, da_ref), (ub_ref, db_ref))):
            pres = []
            for c in range(hidden // HB):
                columns = pl.ds(g * hidden + c * HB, HB)
                slope = slope_ref[rows, columns].astype(F32)
                pres.append((nt(low, down[c * HB : (c + 1) * HB, :]) * slope).astype(BF))
                pre_ref[rows, columns] = pres[-1]
            sent = sent + nt(jnp.concatenate(pres, axis=1), up[...]).astype(BF).astype(F32)
        back_ref[rows, :] = sum_grad + sent
        sent_ref[rows, :] = sent.astype(BF)
    small_ref[0:1, :] = gain_grad
    small_ref[1:2, :] = bias_grad
    if last:
        x_ref, act_ref = before[:2]
        weight_sums(x_ref[...], g_ref[...], act_ref, pre_ref, before[2:], sums)


def astern(meta, own, far, grad, spans, up, down, slope, vectors, u, before):
    half, d = own.shape
    hidden = up[0].shape[1]
    rows = fixed(half, d)
    wide = fixed(half, 2 * hidden)
    grads = [] if not before else [(d, hidden)] * 2 + [(hidden, d)] * 2
    extra = [] if not before else [rows, wide] + [fixed(*shape) for shape in grads[: len(before) - 2]]
    made = [like((half, d), BF), like((half, 2 * hidden), BF)]
    others = [like((half, d), F32), like((half, d), BF), like((2, d), F32)]
    shapes = [like((half, d), BF)] + ([] if before else made) + others + [like(shape, BF) for shape in grads]
    return call(
        functools.partial(astern_kernel, u),
        "astern",
        (1,),
        meta,
        (own, far, grad, spans, *up, *down, slope, vectors, *before),
        [rows] * 2
        + [pl.BlockSpec((half, d), lambda i, m: (u * 2 + m[0], 0)), fixed(*spans.shape)]
        + [fixed(d, hidden)] * 2
        + [fixed(hidden, d)] * 2
        + [wide, fixed(4, d)]
        + extra,
        [fixed(*shape.shape) for shape in shapes],
        shapes,
        [pltpu.VMEM(shape.shape, shape.dtype) for shape in made] if before else (),
        limit=20 if before else VMEM,
        hold=(0, 8, *range(10, 10 + len(before))),
        far=(2,),
        out=() if before else (1, 2),
        out_far=(0, 1) if before else (0, 3),
    )


def weight_kernel(meta_ref, x_ref, g_ref, act_ref, pre_ref, *refs):
    before, sums = refs[:-4], refs[-4:]
    weight_sums(x_ref[...], g_ref[...], act_ref, pre_ref, before, sums)


def weight_sums(x, g, act_ref, pre_ref, before, sums):
    hidden = act_ref.shape[1] // 2
    for i in range(2):
        for c in range(hidden // HB):
            columns = pl.ds(i * hidden + c * HB, HB)
            block = pl.ds(c * HB, HB)
            up = tn(x, pre_ref[:, columns])
            down = tn(act_ref[:, columns], g)
            if before:
                up = up + before[i][:, block].astype(F32)
                down = down + before[2 + i][block, :].astype(F32)
            sums[i][:, block] = up.astype(BF)
            sums[2 + i][block, :] = down.astype(BF)


def weight_grads(meta, x, g, act, pre, before):
    rows, d = x.shape
    hidden = act.shape[1] // 2
    shapes = [(d, hidden)] * 2 + [(hidden, d)] * 2
    return call(
        weight_kernel,
        "weight_grads",
        (1,),
        meta,
        (x, g, act, pre, *before),
        [fixed(rows, d)] * 2 + [fixed(rows, 2 * hidden)] * 2 + [fixed(*shape) for shape in shapes[: len(before)]],
        [fixed(*shape) for shape in shapes],
        [like(shape, BF) for shape in shapes],
        hold=(0, 1, 2, 3),
        out=(0, 1, 2, 3),
    )


def inner_kernel(meta_ref, own_ref, far_ref, xhat_ref, rstd_ref, vec_ref, a0, a1, w0, w1, *refs):
    last = len(refs) == 11
    out_ref, g0, g1, m0, m1, small_ref = refs[-6:]
    grad = own_ref[...] + far_ref[...].astype(F32)
    xhat = xhat_ref[...]
    gain_grad = jnp.sum(grad * xhat, axis=0, keepdims=True)
    bias_grad = jnp.sum(grad, axis=0, keepdims=True)
    gy = grad * vec_ref[0:1, :]
    mean_gy = jnp.mean(gy, axis=-1, keepdims=True)
    mean_gx = jnp.mean(gy * xhat, axis=-1, keepdims=True)
    inner = rstd_ref[:, 0:1] * (gy - mean_gy - xhat * mean_gx)
    out_ref[...] = inner
    low = inner.astype(BF)
    g0[...] = nt(w0[...], low).astype(BF)
    g1[...] = nt(w1[...], low).astype(BF)
    small = jnp.concatenate([gain_grad, bias_grad], axis=0)
    small_ref[...] = small
    if last:
        before0, before1, before_small, outer0, outer1 = refs[:5]
        below = jnp.concatenate(
            [small + before_small[...], outer0[...] + outer1[...], jnp.zeros((60, small.shape[1]), F32)], axis=0
        ).astype(BF)
        for m, a, before in ((m0, a0, before0), (m1, a1, before1)):
            m[:192, :] = (nn(a[...], low) + before[...]).astype(BF)
            m[192:, :] = below
    else:
        m0[...] = nn(a0[...], low)
        m1[...] = nn(a1[...], low)


def inner_norm(meta, own, far, xhat, rstd, vectors, att, weights, before):
    rows, d = xhat.shape
    merge = like((256, d), BF) if before else like((192, d), F32)
    return call(
        inner_kernel,
        "inner_norm",
        (1,),
        meta,
        (own, far, xhat, rstd, vectors, *att, *weights, *before),
        [fixed(rows, d)] * 3
        + [fixed(rows, 128), fixed(4, d)]
        + [fixed(192, rows)] * 2
        + [fixed(192, d)] * 2
        + ([fixed(192, d)] * 2 + [fixed(2, d)] * 3 if before else []),
        [fixed(rows, d), fixed(192, rows), fixed(192, rows), fixed(*merge.shape), fixed(*merge.shape), fixed(2, d)],
        [like((rows, d), F32), like((192, rows), BF), like((192, rows), BF), merge, merge, like((2, d), F32)],
        far=(0, 2, 3, 5, 6, 7, 8, *((9, 10) if before else ())),
        out=(1,),
        out_far=(0,) if before else (0, 3, 4),
    )


def fold_kernel(bits, meta_ref, *refs):
    for i in range(2):
        here, there = refs[2 * i : 2 * i + 2]
        if bits:
            send, keep = refs[4 + 2 * i : 6 + 2 * i]
            half = send.shape[0]
            bit = meta_ref[bits[i]]
            for part, j in ((send, 1 - bit), (keep, bit)):
                rows = pl.ds(pl.multiple_of(j * half, 16), half)
                part[...] = (here[rows, :].astype(F32) + there[rows, :].astype(F32)).astype(BF)
        else:
            refs[4 + i][...] = (here[...].astype(F32) + there[...].astype(F32)).astype(BF)


def fold(meta, pairs, bits, hold=()):
    args = [value for pair in pairs for value in pair]
    rows, d = args[0].shape
    shapes = [like((rows // 2, d), BF)] * 4 if bits else [like((rows, d), BF)] * 2
    return call(
        functools.partial(fold_kernel, bits),
        "fold",
        (1,),
        meta,
        args,
        [fixed(rows, d)] * 4,
        [fixed(*shape.shape) for shape in shapes],
        shapes,
        hold=hold,
    )


def local(groups, tokens, lengths, span_starts, wq, wk, wv, wm, wu, wd, ig, ib, og, ob, out_grad):
    rows, d = tokens.shape
    seqs = lengths.shape[0]
    frames = rows // seqs
    half = frames // 2
    core = lax.axis_index("tensor") % 2
    place_dp = lax.axis_index("dp")
    bits = groups.bit_length() - 1

    def swap(value, k):
        return lax.ppermute(value, "tensor", [(i, i ^ k) for i in range(4)])

    def swap_dp(value, k):
        return lax.ppermute(value, "dp", [(i, i ^ k) for i in range(groups)])

    def add(a, b):
        return (a.astype(F32) + b.astype(F32)).astype(BF)

    def total(pieces):
        return sum(piece.astype(F32) for piece in pieces).astype(BF) if len(pieces) > 1 else pieces[0]

    stages = [(0, 1)] + [(b, 2) for b in range(1, bits - 1, 2)] + ([(bits - 1, 1)] if bits % 2 == 0 else [])
    bit_orders = (list(range(bits)), [1, 0, *range(2, bits)])

    def spot_of(stage):
        return (place_dp >> stage[0]) & ((1 << stage[1]) - 1)

    class Chain:
        def __init__(self, part, order, cut_already=False):
            self.part = part.reshape((1,) * len(order) + part.shape) if cut_already else part
            self.order = order
            self.steps = [] if cut_already else [(True, stage) for stage in order]
            self.steps += [(False, stage) for stage in reversed(order)]

        def cut(self, stage, j):
            size = self.part.shape[0] >> stage[1]
            return lax.dynamic_slice_in_dim(self.part, (spot_of(stage) ^ j) * size, size, 0)

        def start(self):
            if self.steps:
                scatter, stage = self.steps[0]
                others = range(1, 1 << stage[1])
                self.pending = [swap_dp(self.cut(stage, j) if scatter else self.part, j << stage[0]) for j in others]

        def finish(self, *after):
            if not self.steps:
                return
            scatter, stage = self.steps.pop(0)
            got = self.pending
            if after:
                got = list(lax.optimization_barrier((*got, *after))[: len(got)])
            if scatter:
                state = total([self.cut(stage, 0)] + got)
                if not self.steps[0][0]:
                    state = state.reshape((1,) * len(self.order) + state.shape)
            else:
                axis = self.order.index(stage)
                spot = spot_of(stage)
                mine = self.part
                if len(got) == 1:
                    laid = [jnp.where(spot, got[0], mine), jnp.where(spot, mine, got[0])]
                    state = jnp.concatenate(laid, axis=axis)
                else:
                    state = jnp.zeros(mine.shape[:axis] + (1 + len(got),) + mine.shape[axis + 1 :], BF)
                    for j, piece in enumerate([mine] + got):
                        state = lax.dynamic_update_slice_in_dim(state, piece, spot ^ j, axis)
                if not self.steps:
                    state = state.reshape(-1, d)
            self.part = state

    def finish(group, *after):
        for chain in group:
            chain.finish(*after)

    def start(group):
        for chain in group:
            chain.start()

    def together(group):
        for chain, value in zip(group, lax.optimization_barrier(tuple(chain.part for chain in group))):
            chain.part = value

    all_bits = [((place_dp >> b) & 1).reshape(1) for b in range(bits)]
    scalars = jnp.concatenate([core.reshape(1), lengths, *all_bits])
    token = []

    def meta():
        return lax.optimization_barrier((scalars, *token))[0] if token else scalars

    def done(results, *others):
        token[:] = [results[0], *others]
        return results

    merge_w = (wm, swap(wm, 1), swap(wm, 2), swap(wm, 3))
    up_w = (wu, swap(wu, 1))
    down_w = (wd, swap(wd, 1))
    vectors = jnp.stack([ig, ib, og, ob])
    qkv_w = (wq.T, wk.T, wv.T)

    fwd, att, front, far = [], [], [], []
    qkv_of = [done(project(scalars, tokens, qkv_w, 0, frames))]
    for u in range(seqs):
        fwd.append(done(attend_forward(meta(), *qkv_of[u], u, frames), *(merge_w[1:] if u == 0 else ())))
        own, other = fwd[u][:2]
        att.append((own, swap(other, 1), swap(own, 2), swap(other, 3)))
        if u + 1 < seqs:
            qkv_of.append(done(project(meta(), tokens, qkv_w, u + 1, frames), up_w[1], down_w[1]))
    for u in range(seqs):
        front.append(done(ahead(meta(), tokens, att[u], merge_w, up_w, down_w, vectors, u)))
        far.append(swap(front[u][6], 2))
    out_rows, back, far_grad, smalls, sums = [], [], [], [], ()
    for u in range(seqs):
        last = u == seqs - 1
        before = (front[u][2], front[u][3], *sums) if last else ()
        res = done(astern(meta(), front[u][5], far[u], out_grad, span_starts, up_w, down_w, front[u][4], vectors, u, before))
        out_rows.append(res[0])
        back.append(res[1 if last else 3])
        smalls.append(res[3 if last else 5])
        if last:
            sent, sums = res[2], res[4:]
        else:
            far_grad.append(swap(res[4], 2))
            sums = done(weight_grads(meta(), front[u][2], res[1], front[u][3], res[2], sums))

    def inner_step(u, before):
        res = done(inner_norm(meta(), back[u], far_grad[u], front[u][0], front[u][1], vectors, att[u][:2], merge_w[:2], before))
        return res, (res[1], swap(res[2], 1))

    def attend_step(u, grads):
        return done(attend_backward(meta(), *qkv_of[u], grads, fwd[u][:2], fwd[u][2], u, frames))

    def entry_step(u, grads, before):
        return done(entry_back(meta(), tokens, grads, qkv_w, before, u, frames))


    first_bit = 1 + seqs

    def scatter(step, pairs, after, hold=()):
        pairs = [tuple(lax.optimization_barrier((*pair, after))[:2]) for pair in pairs]
        if step == bits:
            return done(fold(meta(), pairs, (), hold))
        out = done(fold(meta(), pairs, tuple(first_bit + order[step] for order in bit_orders), hold))
        return [(out[2 * i + 1], swap_dp(out[2 * i], 1 << bit_orders[i][step])) for i in range(2)]

    inner, entry, so_far, near, crossed = [], [], (), [], []
    out_other = [swap(r, 1) for r in out_rows]

    def exchange(out):
        got = swap(out[0], 1)
        near.append((out[1], got))
        crossed.append(swap(total(near[-1]), 2))
        return got

    for u in range(seqs):
        last = u == seqs - 1
        if u == 0:
            up_own, up_other, down_own, down_other = lax.optimization_barrier((*sums, far_grad[0]))[:4]
            moving = [(down_own, swap(down_other, 1)), (up_own, swap(up_other, 1))]
            res, grads = inner_step(0, ())
            inner.append(res)
            far_grad.append(swap(lax.optimization_barrier((sent, res[0]))[0], 2))
            moving = scatter(0, moving, res[0])
        dqkv = attend_step(u, grads)
        if u == 0:
            token.extend(out_other)
        moving = scatter(1 + 2 * u, moving, dqkv[0])
        if not last:
            before = ()
            if u + 1 == seqs - 1:
                before = (inner[0][3], inner[0][4], inner[0][5], *smalls)
            res, grads = inner_step(u + 1, before)
            inner.append(res)
        else:
            for step in range(4, bits + 1):
                moving = scatter(step, moving, moving[0][0])
            first, second = (
                Chain(moving[i], [(b, 1) for b in order], True) for i, order in enumerate(bit_orders)
            )
            start([first, second])
            token.append(arrived)
        out = entry_step(u, dqkv, so_far)
        entry.append(out)
        if not last:
            merge_got = swap(lax.optimization_barrier((res[4], out[0]))[0], 1)
            so_far = (out[2], res[3], merge_got)
            moving = scatter(2, moving, out[0])
            arrived = exchange(out)
    qkv = Chain(out[2], stages)
    qkv.start()

    got = exchange(out)
    layer_output = place(meta(), out_rows, out_other)

    finish([first, second], got)
    finish([qkv], crossed[0])
    together([qkv, first, second])
    start([qkv, first, second])
    finish([qkv, first, second], crossed[-1])
    together([qkv, first, second])
    start([qkv, first])
    ready = []
    for u in range(seqs):
        rest = near[u][0].astype(F32) + near[u][1].astype(F32) + crossed[u].astype(F32)
        ready.append((inner[u][0] + rest).astype(BF))
    input_grad = place(scalars, ready, [swap(r, 1) for r in ready])
    finish([qkv, first], layer_output)
    together([qkv, first, second])
    start([qkv, second])
    finish([qkv, second], input_grad)
    while qkv.steps or first.steps or second.steps:
        start([qkv, first, second])
        finish([qkv, first, second])
        together([qkv, first, second])
    down_sum, up_sum, joint = (chain.part for chain in (first, second, qkv))
    qkv_sum, merge_sum = joint[:576], joint[576:]
    small = merge_sum[192:196].astype(F32)
    query_grad, key_grad, value_grad = (qkv_sum[192 * i : 192 * (i + 1)].astype(F32).T for i in range(3))
    return (
        layer_output,
        input_grad,
        query_grad,
        key_grad,
        value_grad,
        merge_sum[:192].astype(F32),
        up_sum.astype(F32),
        down_sum.astype(F32),
        small[0],
        small[1],
        small[2],
        small[3],
    )


def solution(mesh):
    in_specs = (
        P("dp", None),
        P("dp"),
        P("dp", None),
        P(None, "tensor"),
        P(None, "tensor"),
        P(None, "tensor"),
        P("tensor", None),
        P(None, "tensor"),
        P("tensor", None),
        P(),
        P(),
        P(),
        P(),
        P("dp", None),
    )
    out_specs = (
        P("dp", None),
        P("dp", None),
        P(None, "tensor"),
        P(None, "tensor"),
        P(None, "tensor"),
        P("tensor", None),
        P(None, "tensor"),
        P("tensor", None),
        P(),
        P(),
        P(),
        P(),
    )
    body = functools.partial(local, mesh.shape["dp"])
    return jax.shard_map(body, mesh=mesh, in_specs=in_specs, out_specs=out_specs, check_vma=False)
```
